32 devices in a mesh: dp: 8 (over z, y), mp: 4 (over x, core).
Axes of the slice: x: 2, y: 2, z: 4, core: 2. Of those that a mesh axis runs over, the one named last changes fastest.
Arguments:
- decoder_rows: bfloat16 [16384, 768], P(('dp', 'mp')), may hold values from -6 to 6
- memory_rows: bfloat16 [49152, 768], P(('dp', 'mp')), may hold values from -6 to 6
- decoder_token_length: int32 [32], P('dp'), may hold values from 1 to 512, 12288 in all
- memory_length: int32 [32], P('dp'), may hold values from 1 to 1536, 36864 in all
- bucket_ids: int32 [512, 512], replicated, may hold values from 0 to 31
- relative_bucket_bias: bfloat16 [32, 12], P(None, 'mp'), may hold values from -4 to 4
- self_gain: bfloat16 [768], replicated, may hold values from 0.5 to 1.5
- self_query: bfloat16 [768, 768], P(None, 'mp'), may hold values from -0.21875 to 0.21875
- self_key: bfloat16 [768, 768], P(None, 'mp'), may hold values from -0.21875 to 0.21875
- self_value: bfloat16 [768, 768], P(None, 'mp'), may hold values from -0.21875 to 0.21875
- self_out: bfloat16 [768, 768], P('mp'), may hold values from -1.25 to 1.25
- cross_gain: bfloat16 [768], replicated, may hold values from 0.5 to 1.5
- cross_query: bfloat16 [768, 768], P(None, 'mp'), may hold values from -0.21875 to 0.21875
- cross_key: bfloat16 [768, 768], P(None, 'mp'), may hold values from -0.21875 to 0.21875
- cross_value: bfloat16 [768, 768], P(None, 'mp'), may hold values from -0.21875 to 0.21875
- cross_out: bfloat16 [768, 768], P('mp'), may hold values from -1.75 to 1.75
- hidden_gain: bfloat16 [768], replicated, may hold values from 0.5 to 1.5
- widen_weight: bfloat16 [768, 3072], P(None, 'mp'), may hold values from -0.21875 to 0.21875
- narrow_weight: bfloat16 [3072, 768], P('mp'), may hold values from -0.109375 to 0.109375
- layer_cotangent: bfloat16 [16384, 768], P(('dp', 'mp')), may hold values from -6 to 6
Outputs:
- layer_output: bfloat16 [16384, 768], P(('dp', 'mp'))
- input_grad: float32 [16384, 768], P(('dp', 'mp'))
- memory_grad: bfloat16 [49152, 768], P(('dp', 'mp'))
- position_grad: float32 [32, 12], P(None, 'mp')
- self_gain_grad: float32 [768], replicated
- self_query_grad: float32 [768, 768], P(None, 'mp')
- self_key_grad: float32 [768, 768], P(None, 'mp')
- self_value_grad: float32 [768, 768], P(None, 'mp')
- self_out_grad: float32 [768, 768], P('mp')
- cross_gain_grad: float32 [768], replicated
- cross_query_grad: float32 [768, 768], P(None, 'mp')
- cross_key_grad: float32 [768, 768], P(None, 'mp')
- cross_value_grad: float32 [768, 768], P(None, 'mp')
- cross_out_grad: float32 [768, 768], P('mp')
- hidden_gain_grad: float32 [768], replicated
- widen_grad: float32 [768, 3072], P(None, 'mp')
- narrow_grad: float32 [3072, 768], P('mp')
The draws below stay inside these ranges and needn't reach their ends.
Inputs may be any that keep to these rules, and one draw needn't show every extreme that they name: decoder_token_length[j] counts document j's real decoder tokens; some document has 512. memory_length[j] counts document j's real memory tokens; some document has 1536.
All inputs are finite; a program needn't handle non-finite values. No bound on the sum of `decoder_token_length` or of `memory_length` on one device may be relied on, other than what follows from the above.
Results may differ from the reference program's by a relative error of at most 0.024.
Values may be sent and summed in bfloat16 or wider, within the bound.
A program may use at most 192 MiB of HBM per device.

```python
import math
import jax
import jax.numpy as jnp
import numpy as np
from jax import lax

D = 768
HEADS = 12
HEAD_DIM = 64
FF = 3072
BUCKETS = 32
DOC_DEV = 4
DEC = 512
MEM_DOC = 1536
INNER = 768
MEM_PART = 192
DOCS = 32
TOKENS = 16384
MEM_TOKENS = 49152
N_DP = 8


def set_ends(values, rng, least, largest):
    index_at = [jax.random.randint(jax.random.fold_in(rng, axis), (), 0, length) for axis, length in enumerate(values.shape)]
    longest = values.shape.index(max(values.shape))
    next_to = index_at[:longest] + [(index_at[longest] + 1) % values.shape[longest]] + index_at[longest + 1:]
    return values.at[tuple(index_at)].set(least).at[tuple(next_to)].set(largest)


def block_levels(key, dims, pieces, low, high):
    factor_of, own = 1.0, jax.random.fold_in(key, 6)
    for position, blocks in pieces:
        steps = jnp.exp(jax.random.uniform(jax.random.fold_in(own, position), (blocks,), jnp.float32, low / len(pieces), high / len(pieces)))
        factor_of = factor_of * jnp.repeat(steps, dims[position] // blocks).reshape([-1 if axis == position else 1 for axis in range(len(dims))])
    return factor_of


def length_profile(number_of, total, most, lean):
    loads = [(1 << 20) // math.isqrt(rank ** lean) + 1 for rank in range(2, number_of + 1)]
    rest, holding = total - most - (number_of - 1), [1] * (number_of - 1)
    while rest > 0:
        candidates = [i for i in range(number_of - 1) if holding[i] < most]
        pool, budget = sum([loads[i] for i in candidates]), rest
        for i in candidates:
            more = min(most - holding[i], max(1, budget * loads[i] // pool), rest)
            holding[i] = holding[i] + more
            rest = rest - more
    return np.array([most] + holding)


def ragged(own_key, amount, total, most, slope):
    if amount == 2:
        one = jax.random.randint(own_key, (), max(1, total - most), min(most, total - 1) + 1)
        return jnp.stack([one, total - one])
    tallies = jnp.asarray(length_profile(amount, total, most, slope), jnp.int32)
    twos = (amount - 1) // 2
    donor, receiver = tallies[1:1 + 2 * twos:2], tallies[2:2 + 2 * twos:2]
    room = jnp.minimum(donor - 1, most - receiver)
    shifted = jax.random.randint(jax.random.fold_in(own_key, 1), (twos,), 0, 1 << 20) % (room + 1)
    tallies = tallies.at[1:1 + 2 * twos:2].set(donor - shifted).at[2:2 + 2 * twos:2].set(receiver + shifted)
    return tallies[jax.random.permutation(jax.random.fold_in(own_key, 2), amount)]


def normal_values(stream_key, extent, scale, limit, cuts=(), kind=jnp.bfloat16):
    drawn = jax.random.normal(stream_key, extent, jnp.float32) * scale
    if len(cuts) > 0:
        drawn = block_levels(stream_key, extent, cuts, -0.22, 0.18) * drawn
    return jnp.clip(drawn, min=-limit, max=limit).astype(kind)


def setup_inputs(seed: int = 0) -> dict:
    key_of = jax.random.split(jax.random.key(seed), 21)
    decoder_rows = normal_values(key_of[0], (TOKENS, D), 1.0, 6.0, ((0, 32),))
    memory_rows = normal_values(key_of[1], (MEM_TOKENS, D), 1.0, 6.0, ((0, 32),))
    decoder_token_length = ragged(key_of[2], DOCS, DOCS * DEC * 3 // 4, DEC, 1).astype(jnp.int32)
    memory_length = ragged(key_of[3], DOCS, DOCS * MEM_DOC * 3 // 4, MEM_DOC, 1).astype(jnp.int32)
    bucket_ids = set_ends(jax.random.randint(key_of[4], (DEC, DEC), 0, BUCKETS), jax.random.fold_in(key_of[4], 1), 0, BUCKETS - 1).astype(jnp.int32)
    relative_bucket_bias = normal_values(key_of[5], (BUCKETS, HEADS), 1.0, 4.0, ((1, 4),))
    self_gain = jnp.clip(1.0 + 0.1 * jax.random.normal(key_of[6], (D,), jnp.float32), 0.5, 1.5).astype(jnp.bfloat16)
    self_query = normal_values(key_of[7], (D, INNER), D ** -0.5, 0.21875, ((1, 4),))
    self_key = normal_values(key_of[8], (D, INNER), D ** -0.5, 0.21875, ((1, 4),))
    self_value = normal_values(key_of[9], (D, INNER), D ** -0.5, 0.21875, ((1, 4),))
    self_out = normal_values(key_of[10], (INNER, D), (INNER // 32) ** -0.5, 1.25, ((0, 4),))
    cross_gain = jnp.clip(1.0 + 0.1 * jax.random.normal(key_of[11], (D,), jnp.float32), 0.5, 1.5).astype(jnp.bfloat16)
    cross_query = normal_values(key_of[12], (D, INNER), D ** -0.5, 0.21875, ((1, 4),))
    cross_key = normal_values(key_of[13], (D, INNER), D ** -0.5, 0.21875, ((1, 4),))
    cross_value = normal_values(key_of[14], (D, INNER), D ** -0.5, 0.21875, ((1, 4),))
    cross_out = normal_values(key_of[15], (INNER, D), (INNER // 64) ** -0.5, 1.75, ((0, 4),))
    hidden_gain = jnp.clip(1.0 + 0.1 * jax.random.normal(key_of[16], (D,), jnp.float32), 0.5, 1.5).astype(jnp.bfloat16)
    widen_weight = normal_values(key_of[17], (D, FF), D ** -0.5, 0.21875, ((1, 4),))
    narrow_weight = normal_values(key_of[18], (FF, D), FF ** -0.5, 0.109375, ((0, 4),))
    layer_cotangent = normal_values(key_of[19], (TOKENS, D), 1.0, 6.0, ((0, 32),))
    return dict(decoder_rows=decoder_rows, memory_rows=memory_rows, decoder_token_length=decoder_token_length, memory_length=memory_length, bucket_ids=bucket_ids, relative_bucket_bias=relative_bucket_bias, self_gain=self_gain, self_query=self_query, self_key=self_key, self_value=self_value, self_out=self_out, cross_gain=cross_gain, cross_query=cross_query, cross_key=cross_key, cross_value=cross_value, cross_out=cross_out, hidden_gain=hidden_gain, widen_weight=widen_weight, narrow_weight=narrow_weight, layer_cotangent=layer_cotangent)


norm_eps = 1e-06
masked_fill = -1e+30
highest_precision_mode = lax.Precision.HIGHEST

@jax.custom_vjp
def low(v):
    return lax.optimization_barrier(v.astype(jnp.bfloat16)).astype(jnp.float32)

@jax.custom_vjp
def low_back(v):
    return v

def low_keep(v):
    return (low(v), None)

def reduced_precision_pass(kept, grad):
    return (grad,)

def back_keep(v):
    return (v, None)

def back_low(kept, grad):
    return (low(grad),)
low.defvjp(low_keep, reduced_precision_pass)
low_back.defvjp(back_keep, back_low)

def matmul(first_op, second_op):
    return jnp.dot(first_op, second_op, precision=highest_precision_mode, preferred_element_type=jnp.float32)

def rms_scale(hidden_rows, norm_gain):
    return hidden_rows * lax.rsqrt(lax.optimization_barrier(jnp.mean(hidden_rows * hidden_rows, axis=-1, keepdims=True)) + norm_eps) * norm_gain

def doc_attend(doc_query, doc_key, doc_value, attention_score_bias, allowed):
    scores = jnp.einsum('qhd,khd->hqk', doc_query, doc_key, precision=highest_precision_mode) * HEAD_DIM ** (-0.5) + attention_score_bias
    scores = low_back(scores)
    scores = jnp.where(allowed[None], scores, masked_fill)
    row_top = lax.optimization_barrier(jnp.max(scores, axis=2, keepdims=True))
    unscaled_weight_matrix = jnp.exp(scores - row_top)
    softmax_low = low(unscaled_weight_matrix / lax.optimization_barrier(jnp.sum(unscaled_weight_matrix, axis=2, keepdims=True)))
    mixed_rows = jnp.einsum('hqk,khd->qhd', softmax_low, doc_value, precision=highest_precision_mode)
    return low(low_back(mixed_rows))

def split_heads(flat_rows, doc_len):
    return flat_rows.reshape(DOCS, doc_len, HEADS, HEAD_DIM)

def memory_to_docs(flat_rows):
    shaped = flat_rows.reshape(N_DP, DOC_DEV, N_DP, MEM_PART, INNER)
    return shaped.transpose(2, 1, 0, 3, 4).reshape(DOCS, MEM_DOC, HEADS, HEAD_DIM)

def layer(hidden_rows, memory_rows, relative_bucket_bias, self_gain, self_query, self_key, self_value, self_out, cross_gain, cross_query, cross_key, cross_value, cross_out, hidden_gain, widen_weight, narrow_weight, decoder_token_length, memory_length, bucket_lookup_grid):
    attention_score_bias = jnp.einsum('pui,pf->fui', bucket_lookup_grid, relative_bucket_bias, precision=highest_precision_mode)
    positions = jnp.arange(DEC, dtype=jnp.int32)
    causal = positions[None, :] <= positions[:, None]
    slot_pos = jnp.arange(MEM_DOC, dtype=jnp.int32)
    normed = low(rms_scale(hidden_rows, self_gain))
    queries = split_heads(low(low_back(matmul(normed, self_query))), DEC)
    keys_all = split_heads(low(low_back(matmul(normed, self_key))), DEC)
    values_all = split_heads(low(low_back(matmul(normed, self_value))), DEC)

    def self_doc(entries):
        doc_query, doc_key, doc_value, doc_length = entries
        return doc_attend(doc_query, doc_key, doc_value, attention_score_bias, causal & (positions[None, :] < doc_length))
    mixed_self = lax.map(jax.checkpoint(self_doc), (queries, keys_all, values_all, decoder_token_length))
    hidden_rows = hidden_rows + low_back(matmul(mixed_self.reshape(TOKENS, INNER), self_out))
    normed = low(rms_scale(hidden_rows, cross_gain))
    queries = split_heads(low(low_back(matmul(normed, cross_query))), DEC)
    keys_all = memory_to_docs(low(low_back(matmul(memory_rows, cross_key))))
    values_all = memory_to_docs(low(low_back(matmul(memory_rows, cross_value))))

    def cross_doc(entries):
        doc_query, doc_key, doc_value, doc_length = entries
        return doc_attend(doc_query, doc_key, doc_value, 0.0, (slot_pos < doc_length)[None, :])
    mixed_cross = lax.map(jax.checkpoint(cross_doc), (queries, keys_all, values_all, memory_length))
    hidden_rows = hidden_rows + low_back(matmul(mixed_cross.reshape(TOKENS, INNER), cross_out))
    normed = low(rms_scale(hidden_rows, hidden_gain))
    widened = low_back(matmul(normed, widen_weight))
    activated = low(jax.nn.gelu(widened, approximate=True))
    return hidden_rows + low_back(matmul(activated, narrow_weight))

def reference(decoder_rows, memory_rows, decoder_token_length, memory_length, bucket_ids, relative_bucket_bias, self_gain, self_query, self_key, self_value, self_out, cross_gain, cross_query, cross_key, cross_value, cross_out, hidden_gain, widen_weight, narrow_weight, layer_cotangent):
    bucket_lookup_grid = (bucket_ids[None] == jnp.arange(BUCKETS, dtype=jnp.int32)[:, None, None]).astype(jnp.float32)
    floats = tuple((tensor.astype(jnp.float32) for tensor in (decoder_rows, memory_rows, relative_bucket_bias, self_gain, self_query, self_key, self_value, self_out, cross_gain, cross_query, cross_key, cross_value, cross_out, hidden_gain, widen_weight, narrow_weight)))

    def forward(*values_in):
        return layer(*values_in, decoder_token_length, memory_length, bucket_lookup_grid)
    result, pull_back = jax.vjp(forward, *floats)
    grads = pull_back(layer_cotangent.astype(jnp.float32))
    return (result.astype(jnp.bfloat16), grads[0], grads[1].astype(jnp.bfloat16), grads[2], grads[3], grads[4], grads[5], grads[6], grads[7], grads[8], grads[9], grads[10], grads[11], grads[12], grads[13], grads[14], grads[15])
```

```python
import functools

import jax
import jax.numpy as jnp
from jax import lax
from jax.experimental import pallas as pl
from jax.experimental.pallas import tpu as pltpu
from jax.sharding import PartitionSpec as P

HEAD_DIM = 64
NORM_EPS = 1e-06
MASKED = -1e30
SCALE = HEAD_DIM**-0.5
BF16 = jnp.bfloat16
F32 = jnp.float32
LANES = 128
Q_BLOCK = 256
K_BLOCK = 512
VMEM_BYTES = 48 * 1024 * 1024


def dot_nn(a, b):
    return lax.dot_general(a, b, (((1,), (0,)), ((), ())), preferred_element_type=F32)


def dot_nt(a, b):
    return lax.dot_general(a, b, (((1,), (1,)), ((), ())), preferred_element_type=F32)


def dot_tn(a, b):
    return lax.dot_general(a, b, (((0,), (0,)), ((), ())), preferred_element_type=F32)


def flip(a):
    return a.astype(F32).T.astype(BF16)


def head(h):
    return slice(h * HEAD_DIM, (h + 1) * HEAD_DIM)


def bias_block(tab_ref, ids_ref, h, rows, start):
    row = jnp.broadcast_to(tab_ref[h : h + 1, :], (rows, LANES))
    return jnp.concatenate(
        [
            jnp.take_along_axis(row, ids_ref[:rows, c : c + LANES], axis=1)
            for c in range(start, start + Q_BLOCK, LANES)
        ],
        axis=1,
    )


def self_forward_kernel(heads, qkv_ref, ids_ref, tab_ref, out_ref, lse_ref):
    width = heads * HEAD_DIM
    doc = qkv_ref.shape[0]
    for h in range(heads):
        cols = head(h)
        k = qkv_ref[:, width + cols.start : width + cols.stop]
        q_t = flip(qkv_ref[:, cols].astype(F32) * SCALE)
        v_t = flip(qkv_ref[:, 2 * width + cols.start : 2 * width + cols.stop])
        for start in range(0, doc, Q_BLOCK):
            rows = start + Q_BLOCK
            span = slice(start, rows)
            s = dot_nn(k[:rows], q_t[:, span]) + bias_block(tab_ref, ids_ref, h, rows, start)
            top = jnp.max(s, axis=0, keepdims=True)
            p = jnp.exp(s - top)
            total = jnp.sum(p, axis=0, keepdims=True)
            mixed_t = dot_nn(v_t[:, :rows], p.astype(BF16)) / total
            out_ref[span, cols] = mixed_t.T.astype(BF16)
            lse_ref[h : h + 1, span] = top + jnp.log(total)


def self_backward_kernel(
    heads, qkv_ref, ids_ref, tab_ref, lse_ref, mixed_ref, g_ref, grad_ref, ds_ref
):
    width = heads * HEAD_DIM
    doc = qkv_ref.shape[0]
    for h in range(heads):
        cols = head(h)
        k_cols = slice(width + cols.start, width + cols.stop)
        v_cols = slice(2 * width + cols.start, 2 * width + cols.stop)
        q = qkv_ref[:, cols]
        k = qkv_ref[:, k_cols]
        v = qkv_ref[:, v_cols]
        g = g_ref[:, cols]
        q_t = flip(q.astype(F32) * SCALE)
        k_t = flip(k)
        g_t = g.astype(F32).T
        inner = jnp.sum(g_t * mixed_ref[:, cols].astype(F32).T, axis=0, keepdims=True)
        g_t = g_t.astype(BF16)
        grad_k = grad_v = None
        for start in range(0, doc, Q_BLOCK):
            rows = start + Q_BLOCK
            span = slice(start, rows)
            s = dot_nn(k[:rows], q_t[:, span]) + bias_block(tab_ref, ids_ref, h, rows, start)
            p = jnp.exp(s - lse_ref[h : h + 1, span])
            grad_p = dot_nn(v[:rows], g_t[:, span])
            ds = (p * (grad_p - inner[:, span])).astype(BF16)
            ds_ref[h, :rows, span] = ds
            grad_q = dot_nn(k_t[:, :rows], ds) * SCALE
            grad_ref[span, cols] = grad_q.T.astype(BF16)
            part_v = dot_nn(p.astype(BF16), g[span])
            part_k = dot_nn(ds, q[span])
            if grad_v is not None:
                part_v = jnp.concatenate([part_v[:start] + grad_v, part_v[start:]], axis=0)
                part_k = jnp.concatenate([part_k[:start] + grad_k, part_k[start:]], axis=0)
            grad_v, grad_k = part_v, part_k
        grad_ref[:, k_cols] = (grad_k * SCALE).astype(BF16)
        grad_ref[:, v_cols] = grad_v.astype(BF16)


def bucket_sum_kernel(heads, buckets, ids_ref, ds_ref, out_ref, wide_ref):
    doc = ids_ref.shape[0]
    wide_ref[...] = ds_ref[...].astype(F32)

    def one_bucket(b, carry):
        sums = [jnp.zeros((8, LANES), F32) for _ in range(heads)]
        for c in range(0, doc, LANES):
            rows = c + LANES
            hit = ids_ref[:rows, c : c + LANES] == b
            for h in range(heads):
                kept = jnp.where(hit, wide_ref[h, :rows, c : c + LANES], 0.0)
                sums[h] = sums[h] + jnp.sum(kept.reshape(rows // 8, 8, LANES), axis=0)
        for h in range(heads):
            out_ref[h, pl.ds(b, 1), :] = jnp.sum(sums[h], axis=0, keepdims=True)
        return carry

    lax.fori_loop(0, buckets, one_bucket, 0)


def cross_forward_kernel(
    heads, q_ref, k_ref, v_ref, mask_ref, out_ref, lse_ref, q_t, top_ref, sum_ref, acc_ref
):
    step = pl.program_id(0)
    doc = q_ref.shape[0]

    @pl.when(step == 0)
    def _():
        for h in range(heads):
            q_t[head(h), :] = flip(q_ref[:, head(h)].astype(F32) * SCALE)
        top_ref[...] = jnp.full_like(top_ref, MASKED)
        sum_ref[...] = jnp.zeros_like(sum_ref)
        acc_ref[...] = jnp.zeros_like(acc_ref)

    for h in range(heads):
        k = k_ref[:, head(h)]
        v_t = flip(v_ref[:, head(h)])
        for start in range(0, doc, Q_BLOCK):
            span = slice(start, start + Q_BLOCK)
            s = dot_nn(k, q_t[head(h), span]) + mask_ref[...]
            old = top_ref[h : h + 1, span]
            top = jnp.maximum(old, jnp.max(s, axis=0, keepdims=True))
            p = jnp.exp(s - top)
            decay = jnp.exp(old - top)
            top_ref[h : h + 1, span] = top
            sum_ref[h : h + 1, span] = sum_ref[h : h + 1, span] * decay + jnp.sum(
                p, axis=0, keepdims=True
            )
            acc_ref[head(h), span] = acc_ref[head(h), span] * decay + dot_nn(v_t, p.astype(BF16))

    @pl.when(step == pl.num_programs(0) - 1)
    def _():
        for h in range(heads):
            mixed_t = acc_ref[head(h), :] / sum_ref[h : h + 1, :]
            out_ref[:, head(h)] = mixed_t.T.astype(BF16)
        lse_ref[...] = top_ref[...] + jnp.log(sum_ref[...])


def cross_backward_kernel(
    heads,
    q_ref,
    k_ref,
    v_ref,
    mask_ref,
    lse_ref,
    mixed_ref,
    g_ref,
    grad_q_ref,
    grad_k_ref,
    grad_v_ref,
    q_t,
    g_t,
    inner_ref,
    acc_ref,
):
    step = pl.program_id(0)
    doc = q_ref.shape[0]

    @pl.when(step == 0)
    def _():
        for h in range(heads):
            q_t[head(h), :] = flip(q_ref[:, head(h)].astype(F32) * SCALE)
            wide = g_ref[:, head(h)].astype(F32).T
            g_t[head(h), :] = wide.astype(BF16)
            inner_ref[h : h + 1, :] = jnp.sum(
                wide * mixed_ref[:, head(h)].astype(F32).T, axis=0, keepdims=True
            )
        acc_ref[...] = jnp.zeros_like(acc_ref)

    for h in range(heads):
        k = k_ref[:, head(h)]
        v = v_ref[:, head(h)]
        k_t = flip(k)
        grad_k = grad_v = None
        for start in range(0, doc, Q_BLOCK):
            span = slice(start, start + Q_BLOCK)
            s = dot_nn(k, q_t[head(h), span]) + mask_ref[...]
            p = jnp.exp(s - lse_ref[h : h + 1, span])
            grad_p = dot_nn(v, g_t[head(h), span])
            ds = (p * (grad_p - inner_ref[h : h + 1, span])).astype(BF16)
            part_v = dot_nn(p.astype(BF16), g_ref[span, head(h)])
            part_k = dot_nn(ds, q_ref[span, head(h)])
            acc_ref[head(h), span] += dot_nn(k_t, ds)
            grad_v = part_v if grad_v is None else grad_v + part_v
            grad_k = part_k if grad_k is None else grad_k + part_k
        grad_k_ref[:, head(h)] = (grad_k * SCALE).astype(BF16)
        grad_v_ref[:, head(h)] = grad_v.astype(BF16)

    @pl.when(step == pl.num_programs(0) - 1)
    def _():
        for h in range(heads):
            grad_q_ref[:, head(h)] = (acc_ref[head(h), :] * SCALE).T.astype(BF16)


def params():
    return pltpu.CompilerParams(vmem_limit_bytes=VMEM_BYTES)


def cost(flops, size, exps):
    return pl.CostEstimate(flops=flops, bytes_accessed=size, transcendentals=exps)


def self_forward(qkv, ids, table):
    doc, heads = qkv.shape[0], qkv.shape[1] // (3 * HEAD_DIM)
    area = heads * doc * doc
    return pl.pallas_call(
        functools.partial(self_forward_kernel, heads),
        out_shape=(
            jax.ShapeDtypeStruct((doc, heads * HEAD_DIM), BF16),
            jax.ShapeDtypeStruct((8, doc), F32),
        ),
        compiler_params=params(),
        cost_estimate=cost(16 * area * HEAD_DIM, 4 << 20, area),
        name="self_forward",
    )(qkv, ids, table)


def self_backward(qkv, ids, table, lse, mixed, g):
    doc, heads = qkv.shape[0], qkv.shape[1] // (3 * HEAD_DIM)
    area = heads * doc * doc
    return pl.pallas_call(
        functools.partial(self_backward_kernel, heads),
        out_shape=(
            jax.ShapeDtypeStruct(qkv.shape, BF16),
            jax.ShapeDtypeStruct((heads, doc, doc), BF16),
        ),
        compiler_params=params(),
        cost_estimate=cost(40 * area * HEAD_DIM, 8 << 20, area),
        name="self_backward",
    )(qkv, ids, table, lse, mixed, g)


def bucket_sums(ids, ds, buckets):
    heads, doc, _ = ds.shape
    sums = pl.pallas_call(
        functools.partial(bucket_sum_kernel, heads, buckets),
        out_shape=jax.ShapeDtypeStruct((heads, buckets, LANES), F32),
        scratch_shapes=[pltpu.VMEM(ds.shape, F32)],
        compiler_params=params(),
        cost_estimate=cost(64 * ds.size, 4 << 20, 0),
        name="bucket_sums",
    )(ids, ds)
    return jnp.sum(sums, axis=2)


def cross_specs(doc, slots, width, block):
    whole = pl.BlockSpec((doc, width), lambda i: (0, 0))
    part = pl.BlockSpec((block, width), lambda i: (i, 0))
    mask = pl.BlockSpec((block, Q_BLOCK), lambda i: (i, 0))
    rows = pl.BlockSpec((8, doc), lambda i: (0, 0))
    return whole, part, mask, rows


def cross_forward(q, k, v, mask):
    (doc, width), slots = q.shape, k.shape[0]
    heads = width // HEAD_DIM
    area = heads * doc * slots
    whole, part, mask_spec, rows = cross_specs(doc, slots, width, K_BLOCK)
    return pl.pallas_call(
        functools.partial(cross_forward_kernel, heads),
        grid=(slots // K_BLOCK,),
        in_specs=[whole, part, part, mask_spec],
        out_specs=(whole, rows),
        out_shape=(
            jax.ShapeDtypeStruct((doc, width), BF16),
            jax.ShapeDtypeStruct((8, doc), F32),
        ),
        scratch_shapes=[
            pltpu.VMEM((width, doc), BF16),
            pltpu.VMEM((8, doc), F32),
            pltpu.VMEM((8, doc), F32),
            pltpu.VMEM((width, doc), F32),
        ],
        compiler_params=params(),
        cost_estimate=cost(16 * area * HEAD_DIM, 4 << 20, area),
        name="cross_forward",
    )(q, k, v, mask)


def cross_backward(q, k, v, mask, lse, mixed, g):
    (doc, width), slots = q.shape, k.shape[0]
    heads = width // HEAD_DIM
    area = heads * doc * slots
    whole, part, mask_spec, rows = cross_specs(doc, slots, width, K_BLOCK)
    return pl.pallas_call(
        functools.partial(cross_backward_kernel, heads),
        grid=(slots // K_BLOCK,),
        in_specs=[whole, part, part, mask_spec, rows, whole, whole],
        out_specs=(whole, part, part),
        out_shape=(
            jax.ShapeDtypeStruct((doc, width), BF16),
            jax.ShapeDtypeStruct((slots, width), BF16),
            jax.ShapeDtypeStruct((slots, width), BF16),
        ),
        scratch_shapes=[
            pltpu.VMEM((width, doc), BF16),
            pltpu.VMEM((width, doc), BF16),
            pltpu.VMEM((8, doc), F32),
            pltpu.VMEM((width, doc), F32),
        ],
        compiler_params=params(),
        cost_estimate=cost(40 * area * HEAD_DIM, 8 << 20, area),
        name="cross_backward",
    )(q, k, v, mask, lse, mixed, g)


def norm_scale(rows):
    return lax.rsqrt(jnp.mean(rows * rows, axis=-1, keepdims=True) + NORM_EPS)


def norm(rows, gain):
    return (rows * norm_scale(rows) * gain).astype(BF16)


def norm_back(rows, gain, grad):
    scale = norm_scale(rows)
    unit = rows * scale
    grad_unit = grad * gain
    return (
        scale * (grad_unit - unit * jnp.mean(grad_unit * unit, axis=-1, keepdims=True)),
        jnp.sum(grad * unit, axis=0),
    )


GELU_ROOT = 0.7978845608028654
GELU_CUBE = 0.044715


def gelu_and_slope(v):
    square = v * v
    bend = jnp.tanh(GELU_ROOT * (v + GELU_CUBE * v * square))
    half = 0.5 * (1.0 + bend)
    slope = half + 0.5 * v * (1.0 - bend * bend) * GELU_ROOT * (1.0 + 3.0 * GELU_CUBE * square)
    return v * half, slope


def swap(array, bit, size):
    return lax.ppermute(array, "mp", [(i, i ^ bit) for i in range(size)])


def gather_pieces(own, size):
    pieces = {0: own}
    bit = size // 2
    while bit:
        for j in list(pieces):
            pieces[j | bit] = swap(pieces[j], bit, size)
        bit //= 2
    return pieces


def sum_pieces(pieces, size):
    bit = 1
    while bit < size:
        for j in [j for j in pieces if j & bit]:
            came = swap(pieces.pop(j), bit, size)
            pieces[j ^ bit] = (pieces[j ^ bit].astype(F32) + came.astype(F32)).astype(BF16)
        bit *= 2
    return pieces[0]


def shards(
    decoder_rows,
    memory_rows,
    decoder_token_length,
    memory_length,
    bucket_ids,
    relative_bucket_bias,
    self_gain,
    self_query,
    self_key,
    self_value,
    self_out,
    cross_gain,
    cross_query,
    cross_key,
    cross_value,
    cross_out,
    hidden_gain,
    widen_weight,
    narrow_weight,
    layer_cotangent,
):
    dp_size = lax.axis_size("dp")
    mp_size = lax.axis_size("mp")
    me = lax.axis_index("mp")
    doc, features = decoder_rows.shape
    slots = memory_rows.shape[0]
    cols = self_query.shape[1]
    heads = cols // HEAD_DIM
    buckets = relative_bucket_bias.shape[0]
    order = range(mp_size)

    memory_seen = lax.all_to_all(
        memory_rows.reshape(dp_size, slots // dp_size, features), "dp", 0, 0
    ).reshape(slots, features)
    table_rows = jnp.zeros((16, features), BF16)
    table_rows = table_rows.at[:heads, :buckets].set(relative_bucket_bias.T)
    weights_self = gather_pieces(
        jnp.concatenate([self_query.T, self_key.T, self_value.T, table_rows], axis=0), mp_size
    )
    weights_cross = gather_pieces(
        jnp.concatenate([self_out, cross_query.T, cross_key.T, cross_value.T, cross_out], axis=0),
        mp_size,
    )
    weights_wide = gather_pieces(widen_weight.T, mp_size)
    weights_narrow = gather_pieces(narrow_weight, mp_size)

    doc_length = lax.dynamic_index_in_dim(decoder_token_length, me, keepdims=False)
    doc_memory = lax.dynamic_index_in_dim(memory_length, me, keepdims=False)
    position = jnp.arange(doc, dtype=jnp.int32)
    allowed = (position[:, None] <= position[None, :]) & (position[:, None] < doc_length)
    ids = jnp.where(allowed, bucket_ids.T, buckets)
    mask = jnp.where(jnp.arange(slots, dtype=jnp.int32) < doc_memory, 0.0, MASKED)
    mask = jnp.broadcast_to(mask[:, None].astype(F32), (slots, Q_BLOCK))

    gain_self = self_gain.astype(F32)
    gain_cross = cross_gain.astype(F32)
    gain_hidden = hidden_gain.astype(F32)
    rows_in = decoder_rows.astype(F32)
    normed_self = norm(rows_in, gain_self)

    def table_of(piece):
        table = jnp.full((8, LANES), MASKED, F32)
        return table.at[:heads, :buckets].set(
            piece[3 * cols : 3 * cols + heads, :buckets].astype(F32)
        )

    tables = [table_of(weights_self[j]) for j in order]
    w_qkv = [weights_self[j][: 3 * cols] for j in order]
    w_self_out = [weights_cross[j][:cols] for j in order]
    w_query = [weights_cross[j][cols : 2 * cols] for j in order]
    w_key = [weights_cross[j][2 * cols : 3 * cols] for j in order]
    w_value = [weights_cross[j][3 * cols : 4 * cols] for j in order]
    w_cross_out = [weights_cross[j][4 * cols : 5 * cols] for j in order]
    w_wide = [weights_wide[j] for j in order]
    w_narrow = [weights_narrow[j] for j in order]

    qkv = [dot_nt(normed_self, w).astype(BF16) for w in w_qkv]
    mixed_self, lse_self = zip(*[self_forward(qkv[j], ids, tables[j]) for j in order])
    after_self = rows_in + sum(dot_nn(mixed_self[j], w_self_out[j]) for j in order)
    normed_cross = norm(after_self, gain_cross)
    query = [dot_nt(normed_cross, w).astype(BF16) for w in w_query]
    key = [dot_nt(memory_seen, w).astype(BF16) for w in w_key]
    value = [dot_nt(memory_seen, w).astype(BF16) for w in w_value]
    mixed_cross, lse_cross = zip(
        *[cross_forward(query[j], key[j], value[j], mask) for j in order]
    )
    after_cross = after_self + sum(dot_nn(mixed_cross[j], w_cross_out[j]) for j in order)
    normed_hidden = norm(after_cross, gain_hidden)

    cotangent = layer_cotangent.astype(F32)
    output = after_cross
    grad_normed = jnp.zeros_like(after_cross)
    grad_wide, grad_narrow = {}, {}
    for j in reversed(order):
        activated, slope = gelu_and_slope(dot_nt(normed_hidden, w_wide[j]))
        activated = activated.astype(BF16)
        output = output + dot_nn(activated, w_narrow[j])
        grad_widened = (dot_nt(layer_cotangent, w_narrow[j]) * slope).astype(BF16)
        grad_normed = grad_normed + dot_nn(grad_widened, w_wide[j])
        grad_narrow[j] = dot_tn(activated, layer_cotangent).astype(BF16)
        grad_wide[j] = dot_tn(grad_widened, normed_hidden).astype(BF16)
    layer_output = output.astype(BF16)
    sum_wide, sum_narrow = lax.psum(
        (sum_pieces(grad_wide, mp_size), sum_pieces(grad_narrow, mp_size)), "dp"
    )

    step, hidden_gain_grad = norm_back(after_cross, gain_hidden, grad_normed)
    grad_after_cross = cotangent + step
    branch = grad_after_cross.astype(BF16)

    grad_cross = {}
    grad_normed = jnp.zeros_like(after_cross)
    grad_memory = jnp.zeros((slots, features), F32)
    grad_queries, grad_keys, grad_values = {}, {}, {}
    for j in reversed(order):
        g = dot_nt(branch, w_cross_out[j]).astype(BF16)
        grad_q, grad_k, grad_v = cross_backward(
            query[j], key[j], value[j], mask, lse_cross[j], mixed_cross[j], g
        )
        grad_cross[j] = jnp.concatenate(
            [
                dot_tn(grad_q, normed_cross).astype(BF16),
                dot_tn(grad_k, memory_seen).astype(BF16),
                dot_tn(grad_v, memory_seen).astype(BF16),
                dot_tn(mixed_cross[j], branch).astype(BF16),
            ],
            axis=0,
        )
        grad_normed = grad_normed + dot_nn(grad_q, w_query[j])
        grad_memory = grad_memory + dot_nn(grad_k, w_key[j]) + dot_nn(grad_v, w_value[j])
    memory_grad = lax.all_to_all(
        grad_memory.astype(BF16).reshape(dp_size, slots // dp_size, features), "dp", 0, 0
    ).reshape(slots, features)
    part_cross = sum_pieces(grad_cross, mp_size)
    part_cross, sum_wide, sum_narrow = lax.optimization_barrier(
        (part_cross, sum_wide, sum_narrow)
    )
    sum_cross = lax.psum(part_cross, "dp")

    step, cross_gain_grad = norm_back(after_self, gain_cross, grad_normed)
    grad_after_self = grad_after_cross + step
    branch = grad_after_self.astype(BF16)

    grad_self, score_grads = {}, {}
    grad_normed = jnp.zeros_like(after_cross)
    for j in reversed(order):
        g = dot_nt(branch, w_self_out[j]).astype(BF16)
        grad_qkv, score_grads[j] = self_backward(
            qkv[j], ids, tables[j], lse_self[j], mixed_self[j], g
        )
        grad_self[j] = jnp.concatenate(
            [
                dot_tn(grad_qkv, normed_self).astype(BF16),
                dot_tn(mixed_self[j], branch).astype(BF16),
            ],
            axis=0,
        )
        grad_normed = grad_normed + dot_nn(grad_qkv, w_qkv[j])
    part_self = sum_pieces(grad_self, mp_size)
    part_self, sum_cross = lax.optimization_barrier((part_self, sum_cross))
    sum_self = lax.psum(part_self, "dp")

    step, self_gain_grad = norm_back(rows_in, gain_self, grad_normed)
    input_grad = grad_after_self + step

    sums = jnp.stack([bucket_sums(ids, score_grads[j], buckets) for j in order])
    sums = jnp.take(sums, me ^ jnp.arange(mp_size), axis=0)
    small = jnp.concatenate(
        [self_gain_grad, cross_gain_grad, hidden_gain_grad, sums.reshape(-1)]
    )
    small = lax.psum(small, ("dp", "mp"))
    sums = small[3 * features :].reshape(mp_size, heads, buckets)
    position_grad = lax.dynamic_index_in_dim(sums, me, keepdims=False).T

    sum_self = sum_self.astype(F32)
    sum_cross = sum_cross.astype(F32)
    return (
        layer_output,
        input_grad,
        memory_grad,
        position_grad,
        small[:features],
        sum_self[:cols].T,
        sum_self[cols : 2 * cols].T,
        sum_self[2 * cols : 3 * cols].T,
        sum_self[3 * cols :],
        small[features : 2 * features],
        sum_cross[:cols].T,
        sum_cross[cols : 2 * cols].T,
        sum_cross[2 * cols : 3 * cols].T,
        sum_cross[3 * cols :],
        small[2 * features : 3 * features],
        sum_wide.astype(F32).T,
        sum_narrow.astype(F32),
    )


def solution(mesh):
    return jax.shard_map(
        shards,
        mesh=mesh,
        in_specs=(
            P(("dp", "mp"), None),
            P(("dp", "mp"), None),
            P("dp"),
            P("dp"),
            P(),
            P(None, "mp"),
            P(),
            P(None, "mp"),
            P(None, "mp"),
            P(None, "mp"),
            P("mp", None),
            P(),
            P(None, "mp"),
            P(None, "mp"),
            P(None, "mp"),
            P("mp", None),
            P(),
            P(None, "mp"),
            P("mp", None),
            P(("dp", "mp"), None),
        ),
        out_specs=(
            P(("dp", "mp"), None),
            P(("dp", "mp"), None),
            P(("dp", "mp"), None),
            P(None, "mp"),
            P(),
            P(None, "mp"),
            P(None, "mp"),
            P(None, "mp"),
            P("mp", None),
            P(),
            P(None, "mp"),
            P(None, "mp"),
            P(None, "mp"),
            P("mp", None),
            P(),
            P(None, "mp"),
            P("mp", None),
        ),
        check_vma=False,
    )
```

```python
import functools

import jax
import jax.numpy as jnp
from jax import lax
from jax.experimental import pallas as pl
from jax.experimental.pallas import tpu as pltpu
from jax.sharding import PartitionSpec as P

HEAD_DIM = 64
NORM_EPS = 1e-06
MASKED = -1e30
SCALE = HEAD_DIM**-0.5
BF16 = jnp.bfloat16
F32 = jnp.float32
LANES = 128
TABLE_ROWS = 16
Q_BLOCK = 256
K_BLOCK = 512
HIDDEN_BLOCK = 256
ROW_BLOCK = 128
VMEM_BYTES = 48 * 1024 * 1024
GELU_ROOT = 0.7978845608028654
GELU_CUBE = 0.044715


def dot_nn(a, b):
    return lax.dot_general(a, b, (((1,), (0,)), ((), ())), preferred_element_type=F32)


def dot_nt(a, b):
    return lax.dot_general(a, b, (((1,), (1,)), ((), ())), preferred_element_type=F32)


def dot_tn(a, b):
    return lax.dot_general(a, b, (((0,), (0,)), ((), ())), preferred_element_type=F32)


def flip(a):
    return a.astype(F32).T.astype(BF16)


def head(h):
    return slice(h * HEAD_DIM, (h + 1) * HEAD_DIM)


def norm_scale(rows):
    return lax.rsqrt(jnp.mean(rows * rows, axis=-1, keepdims=True) + NORM_EPS)


def norm(rows, gain):
    return (rows * norm_scale(rows) * gain).astype(BF16)


def gelu_and_slope(v):
    square = v * v
    bend = jnp.tanh(GELU_ROOT * (v + GELU_CUBE * v * square))
    half = 0.5 * (1.0 + bend)
    slope = half + 0.5 * v * (1.0 - bend * bend) * GELU_ROOT * (1.0 + 3.0 * GELU_CUBE * square)
    return v * half, slope


def bias_block(table, ids_ref, h, rows, start):
    row = jnp.broadcast_to(table[h : h + 1, :], (rows, LANES))
    return jnp.concatenate(
        [
            jnp.take_along_axis(row, ids_ref[:rows, c : c + LANES], axis=1)
            for c in range(start, start + Q_BLOCK, LANES)
        ],
        axis=1,
    )


def bias_table(w_ref, buckets):
    rows = w_ref.shape[0]
    table = w_ref[rows - TABLE_ROWS :, :LANES].astype(F32)
    lane = lax.broadcasted_iota(jnp.int32, table.shape, 1)
    return jnp.where(lane < buckets, table, MASKED)


def self_forward_kernel(
    heads, buckets, rows_ref, gain_ref, w_ref, ids_ref, acc_ref, qkv_ref, mixed_ref, lse_ref, out_ref
):
    width = heads * HEAD_DIM
    doc = rows_ref.shape[0]
    normed = norm(rows_ref[...].astype(F32), gain_ref[...])
    qkv_ref[...] = dot_nt(normed, w_ref[: 3 * width]).astype(BF16)
    table = bias_table(w_ref, buckets)
    for h in range(heads):
        cols = head(h)
        k = qkv_ref[:, width + cols.start : width + cols.stop]
        q_t = flip(qkv_ref[:, cols].astype(F32) * SCALE)
        v_t = flip(qkv_ref[:, 2 * width + cols.start : 2 * width + cols.stop])
        for start in range(0, doc, Q_BLOCK):
            rows = start + Q_BLOCK
            span = slice(start, rows)
            s = dot_nn(k[:rows], q_t[:, span]) + bias_block(table, ids_ref, h, rows, start)
            top = jnp.max(s, axis=0, keepdims=True)
            p = jnp.exp(s - top)
            total = jnp.sum(p, axis=0, keepdims=True)
            mixed_t = dot_nn(v_t[:, :rows], p.astype(BF16)) / total
            mixed_ref[span, cols] = mixed_t.T.astype(BF16)
            lse_ref[h : h + 1, span] = top + jnp.log(total)
    out_ref[...] = acc_ref[...] + dot_nn(mixed_ref[...], w_ref[3 * width : 4 * width])


def self_backward_kernel(
    heads,
    buckets,
    rows_ref,
    gain_ref,
    w_ref,
    ids_ref,
    branch_ref,
    qkv_ref,
    mixed_ref,
    lse_ref,
    acc_ref,
    pack_ref,
    ds_ref,
    out_ref,
    g_ref,
    grad_ref,
):
    width = heads * HEAD_DIM
    doc = qkv_ref.shape[0]
    table = bias_table(w_ref, buckets)
    w_out = slice(3 * width, 4 * width)
    g_ref[...] = dot_nt(branch_ref[...], w_ref[w_out]).astype(BF16)
    for h in range(heads):
        cols = head(h)
        k_cols = slice(width + cols.start, width + cols.stop)
        v_cols = slice(2 * width + cols.start, 2 * width + cols.stop)
        q = qkv_ref[:, cols]
        k = qkv_ref[:, k_cols]
        v = qkv_ref[:, v_cols]
        g = g_ref[:, cols]
        q_t = flip(q.astype(F32) * SCALE)
        k_t = flip(k)
        g_t = g.astype(F32).T
        inner = jnp.sum(g_t * mixed_ref[:, cols].astype(F32).T, axis=0, keepdims=True)
        g_t = g_t.astype(BF16)
        grad_k = grad_v = None
        for start in range(0, doc, Q_BLOCK):
            rows = start + Q_BLOCK
            span = slice(start, rows)
            s = dot_nn(k[:rows], q_t[:, span]) + bias_block(table, ids_ref, h, rows, start)
            p = jnp.exp(s - lse_ref[h : h + 1, span])
            grad_p = dot_nn(v[:rows], g_t[:, span])
            ds = (p * (grad_p - inner[:, span])).astype(BF16)
            ds_ref[h, :rows, span] = ds
            grad_q = dot_nn(k_t[:, :rows], ds) * SCALE
            grad_ref[span, cols] = grad_q.T.astype(BF16)
            part_v = dot_nn(p.astype(BF16), g[span])
            part_k = dot_nn(ds, q[span])
            if grad_v is not None:
                part_v = jnp.concatenate([part_v[:start] + grad_v, part_v[start:]], axis=0)
                part_k = jnp.concatenate([part_k[:start] + grad_k, part_k[start:]], axis=0)
            grad_v, grad_k = part_v, part_k
        grad_ref[:, k_cols] = (grad_k * SCALE).astype(BF16)
        grad_ref[:, v_cols] = grad_v.astype(BF16)
    normed = norm(rows_ref[...].astype(F32), gain_ref[...])
    pack_ref[: 3 * width] = dot_tn(grad_ref[...], normed).astype(BF16)
    pack_ref[w_out] = dot_tn(mixed_ref[...], branch_ref[...]).astype(BF16)
    out_ref[...] = acc_ref[...] + dot_nn(grad_ref[...], w_ref[: 3 * width])


def bucket_sum_kernel(heads, buckets, ids_ref, ds_ref, out_ref, wide_ref):
    doc = ids_ref.shape[0]
    wide_ref[...] = ds_ref[...].astype(F32)

    def one_bucket(b, carry):
        sums = [jnp.zeros((8, LANES), F32) for _ in range(heads)]
        for c in range(0, doc, LANES):
            rows = c + LANES
            hit = ids_ref[:rows, c : c + LANES] == b
            for h in range(heads):
                kept = jnp.where(hit, wide_ref[h, :rows, c : c + LANES], 0.0)
                sums[h] = sums[h] + jnp.sum(kept.reshape(rows // 8, 8, LANES), axis=0)
        for h in range(heads):
            out_ref[h, pl.ds(b, 1), :] = jnp.sum(sums[h], axis=0, keepdims=True)
        return carry

    lax.fori_loop(0, buckets, one_bucket, 0)


def cross_forward_kernel(
    heads,
    rows_ref,
    gain_ref,
    w_ref,
    memory_ref,
    mask_ref,
    acc_ref,
    q_ref,
    k_ref,
    v_ref,
    mixed_ref,
    lse_ref,
    out_ref,
    q_t,
    top_ref,
    sum_ref,
    mix_t,
):
    step = pl.program_id(0)
    width = heads * HEAD_DIM
    doc = rows_ref.shape[0]

    @pl.when(step == 0)
    def _():
        normed = norm(rows_ref[...], gain_ref[...])
        q_ref[...] = dot_nt(normed, w_ref[:width]).astype(BF16)
        for h in range(heads):
            q_t[head(h), :] = flip(q_ref[:, head(h)].astype(F32) * SCALE)
        top_ref[...] = jnp.full_like(top_ref, MASKED)
        sum_ref[...] = jnp.zeros_like(sum_ref)
        mix_t[...] = jnp.zeros_like(mix_t)

    k_ref[...] = dot_nt(memory_ref[...], w_ref[width : 2 * width]).astype(BF16)
    v_ref[...] = dot_nt(memory_ref[...], w_ref[2 * width : 3 * width]).astype(BF16)
    for h in range(heads):
        k = k_ref[:, head(h)]
        v_t = flip(v_ref[:, head(h)])
        for start in range(0, doc, Q_BLOCK):
            span = slice(start, start + Q_BLOCK)
            s = dot_nn(k, q_t[head(h), span]) + mask_ref[...]
            old = top_ref[h : h + 1, span]
            top = jnp.maximum(old, jnp.max(s, axis=0, keepdims=True))
            p = jnp.exp(s - top)
            decay = jnp.exp(old - top)
            top_ref[h : h + 1, span] = top
            sum_ref[h : h + 1, span] = sum_ref[h : h + 1, span] * decay + jnp.sum(
                p, axis=0, keepdims=True
            )
            mix_t[head(h), span] = mix_t[head(h), span] * decay + dot_nn(v_t, p.astype(BF16))

    @pl.when(step == pl.num_programs(0) - 1)
    def _():
        for h in range(heads):
            mixed = mix_t[head(h), :] / sum_ref[h : h + 1, :]
            mixed_ref[:, head(h)] = mixed.T.astype(BF16)
        lse_ref[...] = top_ref[...] + jnp.log(sum_ref[...])
        out_ref[...] = acc_ref[...] + dot_nn(mixed_ref[...], w_ref[3 * width : 4 * width])


def cross_backward_kernel(
    heads,
    rows_ref,
    gain_ref,
    w_ref,
    memory_ref,
    mask_ref,
    branch_ref,
    q_ref,
    k_ref,
    v_ref,
    mixed_ref,
    lse_ref,
    acc_ref,
    memory_acc_ref,
    pack_ref,
    out_ref,
    memory_out_ref,
    g_ref,
    q_t,
    g_t,
    inner_ref,
    grad_q_t,
    grad_q_ref,
    grad_k_ref,
    grad_v_ref,
    sum_k_ref,
    sum_v_ref,
):
    step = pl.program_id(0)
    width = heads * HEAD_DIM
    doc = q_ref.shape[0]
    w_out = slice(3 * width, 4 * width)

    @pl.when(step == 0)
    def _():
        g_ref[...] = dot_nt(branch_ref[...], w_ref[w_out]).astype(BF16)
        for h in range(heads):
            q_t[head(h), :] = flip(q_ref[:, head(h)].astype(F32) * SCALE)
            wide = g_ref[:, head(h)].astype(F32).T
            g_t[head(h), :] = wide.astype(BF16)
            inner_ref[h : h + 1, :] = jnp.sum(
                wide * mixed_ref[:, head(h)].astype(F32).T, axis=0, keepdims=True
            )
        grad_q_t[...] = jnp.zeros_like(grad_q_t)
        sum_k_ref[...] = jnp.zeros_like(sum_k_ref)
        sum_v_ref[...] = jnp.zeros_like(sum_v_ref)

    for h in range(heads):
        k = k_ref[:, head(h)]
        v = v_ref[:, head(h)]
        k_t = flip(k)
        grad_k = grad_v = None
        for start in range(0, doc, Q_BLOCK):
            span = slice(start, start + Q_BLOCK)
            s = dot_nn(k, q_t[head(h), span]) + mask_ref[...]
            p = jnp.exp(s - lse_ref[h : h + 1, span])
            grad_p = dot_nn(v, g_t[head(h), span])
            ds = (p * (grad_p - inner_ref[h : h + 1, span])).astype(BF16)
            part_v = dot_nn(p.astype(BF16), g_ref[span, head(h)])
            part_k = dot_nn(ds, q_ref[span, head(h)])
            grad_q_t[head(h), span] += dot_nn(k_t, ds)
            grad_v = part_v if grad_v is None else grad_v + part_v
            grad_k = part_k if grad_k is None else grad_k + part_k
        grad_k_ref[:, head(h)] = (grad_k * SCALE).astype(BF16)
        grad_v_ref[:, head(h)] = grad_v.astype(BF16)
    memory = memory_ref[...]
    sum_k_ref[...] += dot_tn(grad_k_ref[...], memory)
    sum_v_ref[...] += dot_tn(grad_v_ref[...], memory)
    grad_memory = dot_nn(grad_k_ref[...], w_ref[width : 2 * width])
    grad_memory = grad_memory + dot_nn(grad_v_ref[...], w_ref[2 * width : 3 * width])
    memory_out_ref[...] = (memory_acc_ref[...] + grad_memory).astype(memory_out_ref.dtype)

    @pl.when(step == pl.num_programs(0) - 1)
    def _():
        for h in range(heads):
            grad_q_ref[:, head(h)] = (grad_q_t[head(h), :] * SCALE).T.astype(BF16)
        normed = norm(rows_ref[...], gain_ref[...])
        pack_ref[:width] = dot_tn(grad_q_ref[...], normed).astype(BF16)
        pack_ref[width : 2 * width] = sum_k_ref[...].astype(BF16)
        pack_ref[2 * width : 3 * width] = sum_v_ref[...].astype(BF16)
        pack_ref[w_out] = dot_tn(mixed_ref[...], branch_ref[...]).astype(BF16)
        out_ref[...] = acc_ref[...] + dot_nn(grad_q_ref[...], w_ref[:width])


def feed_forward_kernel(
    rows_ref,
    gain_ref,
    cotangent_ref,
    wide_ref,
    narrow_ref,
    acc_ref,
    back_acc_ref,
    grad_wide_ref,
    grad_narrow_ref,
    out_ref,
    back_ref,
    normed_ref,
):
    @pl.when(pl.program_id(0) == 0)
    def _():
        normed_ref[...] = norm(rows_ref[...], gain_ref[...])
        out_ref[...] = acc_ref[...]
        back_ref[...] = back_acc_ref[...]

    normed, cotangent = normed_ref[...], cotangent_ref[...]
    wide, narrow = wide_ref[...], narrow_ref[...]
    activated, slope = gelu_and_slope(dot_nt(normed, wide))
    activated = activated.astype(BF16)
    out_ref[...] += dot_nn(activated, narrow)
    grad_narrow_ref[...] = dot_tn(activated, cotangent).astype(BF16)
    grad_widened = (dot_nt(cotangent, narrow) * slope).astype(BF16)
    back_ref[...] += dot_nn(grad_widened, wide)
    grad_wide_ref[...] = dot_tn(grad_widened, normed).astype(BF16)


def norm_back_kernel(rows_ref, gain_ref, grad_ref, add_ref, out_ref, low_ref, gain_grad_ref):
    rows, grad, gain = rows_ref[...].astype(F32), grad_ref[...], gain_ref[...]
    scale = norm_scale(rows)
    unit = rows * scale
    grad_unit = grad * gain
    mean = jnp.mean(grad_unit * unit, axis=-1, keepdims=True)
    out = add_ref[...].astype(F32) + scale * (grad_unit - unit * mean)
    out_ref[...] = out
    low_ref[...] = out.astype(BF16)
    part = jnp.sum((grad * unit).reshape(-1, 8, rows.shape[1]), axis=0)

    @pl.when(pl.program_id(0) == 0)
    def _():
        gain_grad_ref[...] = part

    @pl.when(pl.program_id(0) > 0)
    def _():
        gain_grad_ref[...] += part


def params():
    return pltpu.CompilerParams(vmem_limit_bytes=VMEM_BYTES)


def cost(flops, size, exps):
    return pl.CostEstimate(flops=flops, bytes_accessed=size, transcendentals=exps)


def shape(dims, dtype):
    return jax.ShapeDtypeStruct(dims, dtype)


def self_forward(heads, buckets, rows, gain, weights, ids, acc):
    doc, features = rows.shape
    width = heads * HEAD_DIM
    area = heads * doc * doc
    return pl.pallas_call(
        functools.partial(self_forward_kernel, heads, buckets),
        out_shape=(
            shape((doc, 3 * width), BF16),
            shape((doc, width), BF16),
            shape((8, doc), F32),
            shape((doc, features), F32),
        ),
        compiler_params=params(),
        cost_estimate=cost(16 * area * HEAD_DIM, 8 << 20, area),
        name="self_forward",
    )(rows, gain, weights, ids, acc)


def self_backward(heads, buckets, rows, gain, weights, ids, branch, saved, acc):
    doc, features = rows.shape
    width = heads * HEAD_DIM
    area = heads * doc * doc
    return pl.pallas_call(
        functools.partial(self_backward_kernel, heads, buckets),
        out_shape=(
            shape((4 * width, features), BF16),
            shape((heads, doc, doc), BF16),
            shape((doc, features), F32),
        ),
        scratch_shapes=[pltpu.VMEM((doc, width), BF16), pltpu.VMEM((doc, 3 * width), BF16)],
        compiler_params=params(),
        cost_estimate=cost(40 * area * HEAD_DIM, 8 << 20, area),
        name="self_backward",
    )(rows, gain, weights, ids, branch, *saved, acc)


def bucket_sums(ids, ds, buckets):
    heads, doc, _ = ds.shape
    sums = pl.pallas_call(
        functools.partial(bucket_sum_kernel, heads, buckets),
        out_shape=shape((heads, buckets, LANES), F32),
        scratch_shapes=[pltpu.VMEM(ds.shape, F32)],
        compiler_params=params(),
        cost_estimate=cost(64 * ds.size, 4 << 20, 0),
        name="bucket_sums",
    )(ids, ds)
    return jnp.sum(sums, axis=2)


def whole(array):
    return pl.BlockSpec(array.shape, lambda i: (0,) * len(array.shape))


def tall(rows, columns):
    return pl.BlockSpec((rows, columns), lambda i: (i, 0))


def cross_forward(heads, rows, gain, weights, memory, mask, acc):
    (doc, features), slots = rows.shape, memory.shape[0]
    width = heads * HEAD_DIM
    area = heads * doc * slots
    out_shape = (
        shape((doc, width), BF16),
        shape((slots, width), BF16),
        shape((slots, width), BF16),
        shape((doc, width), BF16),
        shape((8, doc), F32),
        shape((doc, features), F32),
    )
    key = tall(K_BLOCK, width)
    return pl.pallas_call(
        functools.partial(cross_forward_kernel, heads),
        grid=(slots // K_BLOCK,),
        in_specs=[
            whole(rows),
            whole(gain),
            whole(weights),
            tall(K_BLOCK, features),
            tall(K_BLOCK, Q_BLOCK),
            whole(acc),
        ],
        out_specs=(whole(out_shape[0]), key, key, *[whole(out_shape[i]) for i in (3, 4, 5)]),
        out_shape=out_shape,
        scratch_shapes=[
            pltpu.VMEM((width, doc), BF16),
            pltpu.VMEM((8, doc), F32),
            pltpu.VMEM((8, doc), F32),
            pltpu.VMEM((width, doc), F32),
        ],
        compiler_params=params(),
        cost_estimate=cost(16 * area * HEAD_DIM, 8 << 20, area),
        name="cross_forward",
    )(rows, gain, weights, memory, mask, acc)


def cross_backward(
    heads, rows, gain, weights, memory, mask, branch, saved, acc, memory_acc, memory_type
):
    (doc, features), slots = rows.shape, memory.shape[0]
    width = heads * HEAD_DIM
    area = heads * doc * slots
    out_shape = (
        shape((4 * width, features), BF16),
        shape((doc, features), F32),
        shape((slots, features), memory_type),
    )
    key = tall(K_BLOCK, width)
    block = tall(K_BLOCK, features)
    query, _, _, mixed, lse = saved
    return pl.pallas_call(
        functools.partial(cross_backward_kernel, heads),
        grid=(slots // K_BLOCK,),
        in_specs=[
            whole(rows),
            whole(gain),
            whole(weights),
            block,
            tall(K_BLOCK, Q_BLOCK),
            whole(branch),
            whole(query),
            key,
            key,
            whole(mixed),
            whole(lse),
            whole(acc),
            block,
        ],
        out_specs=(whole(out_shape[0]), whole(out_shape[1]), block),
        out_shape=out_shape,
        scratch_shapes=[
            pltpu.VMEM((doc, width), BF16),
            pltpu.VMEM((width, doc), BF16),
            pltpu.VMEM((width, doc), BF16),
            pltpu.VMEM((8, doc), F32),
            pltpu.VMEM((width, doc), F32),
            pltpu.VMEM((doc, width), BF16),
            pltpu.VMEM((K_BLOCK, width), BF16),
            pltpu.VMEM((K_BLOCK, width), BF16),
            pltpu.VMEM((width, features), F32),
            pltpu.VMEM((width, features), F32),
        ],
        compiler_params=params(),
        cost_estimate=cost(40 * area * HEAD_DIM, 8 << 20, area),
        name="cross_backward",
    )(rows, gain, weights, memory, mask, branch, *saved, acc, memory_acc)


def feed_forward(rows, gain, cotangent, wide, narrow, acc, back_acc):
    (doc, features), hidden = rows.shape, wide.shape[0]
    out_shape = (
        shape((hidden, features), BF16),
        shape((hidden, features), BF16),
        shape((doc, features), F32),
        shape((doc, features), F32),
    )
    block = tall(HIDDEN_BLOCK, features)
    return pl.pallas_call(
        feed_forward_kernel,
        grid=(hidden // HIDDEN_BLOCK,),
        in_specs=[
            whole(rows),
            whole(gain),
            whole(cotangent),
            block,
            block,
            whole(acc),
            whole(back_acc),
        ],
        out_specs=(block, block, whole(out_shape[2]), whole(out_shape[3])),
        out_shape=out_shape,
        scratch_shapes=[pltpu.VMEM((doc, features), BF16)],
        compiler_params=params(),
        cost_estimate=cost(12 * doc * features * hidden, 12 << 20, doc * hidden),
        name="feed_forward",
    )(rows, gain, cotangent, wide, narrow, acc, back_acc)


def norm_back(rows, gain, grad, add):
    doc, features = rows.shape
    block = tall(ROW_BLOCK, features)
    out_shape = (
        shape((doc, features), F32),
        shape((doc, features), BF16),
        shape((8, features), F32),
    )
    return pl.pallas_call(
        norm_back_kernel,
        grid=(doc // ROW_BLOCK,),
        in_specs=[block, whole(gain), block, block],
        out_specs=(block, block, whole(out_shape[2])),
        out_shape=out_shape,
        compiler_params=params(),
        cost_estimate=cost(12 * doc * features, 6 << 20, doc),
        name="norm_back",
    )(rows, gain, grad, add)


def swap(array, bit, size):
    return lax.ppermute(array, "mp", [(i, i ^ bit) for i in range(size)])


def gather_pieces(own, size):
    pieces = {0: own}
    bit = size // 2
    while bit:
        for j in list(pieces):
            pieces[j | bit] = swap(pieces[j], bit, size)
        bit //= 2
    return pieces


def fold(pieces, bit, size):
    kept = {}
    for j in pieces:
        if not j & bit:
            came = swap(pieces[j | bit], bit, size)
            kept[j] = (pieces[j].astype(F32) + came.astype(F32)).astype(BF16)
    return kept


def fold_rest(pieces, bit, size):
    while bit < size:
        pieces = fold(pieces, bit, size)
        bit *= 2
    return pieces[0]


def shards(
    decoder_rows,
    memory_rows,
    decoder_token_length,
    memory_length,
    bucket_ids,
    relative_bucket_bias,
    self_gain,
    self_query,
    self_key,
    self_value,
    self_out,
    cross_gain,
    cross_query,
    cross_key,
    cross_value,
    cross_out,
    hidden_gain,
    widen_weight,
    narrow_weight,
    layer_cotangent,
):
    dp_size = lax.axis_size("dp")
    mp_size = lax.axis_size("mp")
    me = lax.axis_index("mp")
    doc, features = decoder_rows.shape
    slots = memory_rows.shape[0]
    cols = self_query.shape[1]
    heads = cols // HEAD_DIM
    buckets = relative_bucket_bias.shape[0]
    order = list(range(mp_size))
    backward = order[::-1]

    memory_seen = lax.all_to_all(
        memory_rows.reshape(dp_size, slots // dp_size, features), "dp", 0, 0
    ).reshape(slots, features)
    bias_rows = jnp.zeros((TABLE_ROWS, features), BF16)
    bias_rows = bias_rows.at[:heads, :buckets].set(relative_bucket_bias.T)
    w_self = gather_pieces(
        jnp.concatenate([self_query.T, self_key.T, self_value.T, self_out, bias_rows], axis=0),
        mp_size,
    )
    w_cross = gather_pieces(
        jnp.concatenate([cross_query.T, cross_key.T, cross_value.T, cross_out], axis=0), mp_size
    )
    w_wide = gather_pieces(widen_weight.T, mp_size)
    w_narrow = gather_pieces(narrow_weight, mp_size)

    doc_length = lax.dynamic_index_in_dim(decoder_token_length, me, keepdims=False)
    doc_memory = lax.dynamic_index_in_dim(memory_length, me, keepdims=False)
    position = jnp.arange(doc, dtype=jnp.int32)
    allowed = (position[:, None] <= position[None, :]) & (position[:, None] < doc_length)
    ids = jnp.where(allowed, bucket_ids.T, buckets)
    mask = jnp.where(jnp.arange(slots, dtype=jnp.int32) < doc_memory, 0.0, MASKED)
    mask = jnp.broadcast_to(mask[:, None].astype(F32), (slots, Q_BLOCK))

    gain_self = self_gain.astype(F32)[None]
    gain_cross = cross_gain.astype(F32)[None]
    gain_hidden = hidden_gain.astype(F32)[None]

    acc = decoder_rows.astype(F32)
    saved_self, saved_cross = {}, {}
    for j in order:
        *saved_self[j], acc = self_forward(
            heads, buckets, decoder_rows, gain_self, w_self[j], ids, acc
        )
    after_self = acc
    for j in order:
        *saved_cross[j], acc = cross_forward(
            heads, after_self, gain_cross, w_cross[j], memory_seen, mask, acc
        )
    after_cross = acc

    grad_wide, grad_narrow = {}, {}
    back = jnp.zeros((doc, features), F32)
    for j in order[: mp_size // 2] + order[: mp_size // 2 - 1 : -1]:
        grad_wide[j], grad_narrow[j], acc, back = feed_forward(
            after_cross, gain_hidden, layer_cotangent, w_wide[j], w_narrow[j], acc, back
        )
    layer_output = acc.astype(BF16)
    grad_after_cross, branch, hidden_gain_grad = norm_back(
        after_cross, gain_hidden, back, layer_cotangent
    )
    grad_wide = fold(grad_wide, 1, mp_size)
    grad_narrow = fold(grad_narrow, 1, mp_size)
    branch, grad_wide, grad_narrow = lax.optimization_barrier((branch, grad_wide, grad_narrow))

    grad_cross = {}
    back = jnp.zeros((doc, features), F32)
    grad_memory = jnp.zeros((slots, features), F32)
    for j in backward:
        grad_cross[j], back, grad_memory = cross_backward(
            heads,
            after_self,
            gain_cross,
            w_cross[j],
            memory_seen,
            mask,
            branch,
            saved_cross[j],
            back,
            grad_memory,
            F32 if j else BF16,
        )
    memory_grad = lax.all_to_all(
        grad_memory.reshape(dp_size, slots // dp_size, features), "dp", 0, 0
    ).reshape(slots, features)
    grad_after_self, branch, cross_gain_grad = norm_back(
        after_self, gain_cross, back, grad_after_cross
    )
    grad_wide = fold_rest(grad_wide, 2, mp_size)
    grad_narrow = fold_rest(grad_narrow, 2, mp_size)
    branch, grad_wide, grad_narrow = lax.optimization_barrier((branch, grad_wide, grad_narrow))
    sum_wide, sum_narrow = lax.psum((grad_wide, grad_narrow), "dp")

    grad_self, score_grads = {}, {}
    back = jnp.zeros((doc, features), F32)
    for j in backward:
        grad_self[j], score_grads[j], back = self_backward(
            heads,
            buckets,
            decoder_rows,
            gain_self,
            w_self[j],
            ids,
            branch,
            saved_self[j],
            back,
        )
        if j == mp_size - 1:
            grad_cross = fold(grad_cross, 1, mp_size)
            back, grad_cross = lax.optimization_barrier((back, grad_cross))
    input_grad, _, self_gain_grad = norm_back(decoder_rows, gain_self, back, grad_after_self)
    grad_cross = fold_rest(grad_cross, 2, mp_size)
    grad_self = fold_rest(grad_self, 1, mp_size)
    grad_cross, grad_self, sum_wide, sum_narrow = lax.optimization_barrier(
        (grad_cross, grad_self, sum_wide, sum_narrow)
    )
    sum_cross, sum_self = lax.psum((grad_cross, grad_self), "dp")

    sums = jnp.stack([bucket_sums(ids, score_grads[j], buckets) for j in order])
    sums = jnp.take(sums, me ^ jnp.arange(mp_size), axis=0)
    gains = jnp.stack([self_gain_grad, cross_gain_grad, hidden_gain_grad]).sum(axis=1)
    small = lax.psum(jnp.concatenate([gains.reshape(-1), sums.reshape(-1)]), ("dp", "mp"))
    gains = small[: 3 * features].reshape(3, features)
    sums = small[3 * features :].reshape(mp_size, heads, buckets)
    position_grad = lax.dynamic_index_in_dim(sums, me, keepdims=False).T

    sum_self = sum_self.astype(F32)
    sum_cross = sum_cross.astype(F32)
    return (
        layer_output,
        input_grad,
        memory_grad,
        position_grad,
        gains[0],
        sum_self[:cols].T,
        sum_self[cols : 2 * cols].T,
        sum_self[2 * cols : 3 * cols].T,
        sum_self[3 * cols :],
        gains[1],
        sum_cross[:cols].T,
        sum_cross[cols : 2 * cols].T,
        sum_cross[2 * cols : 3 * cols].T,
        sum_cross[3 * cols :],
        gains[2],
        sum_wide.astype(F32).T,
        sum_narrow.astype(F32),
    )


def solution(mesh):
    return jax.shard_map(
        shards,
        mesh=mesh,
        in_specs=(
            P(("dp", "mp"), None),
            P(("dp", "mp"), None),
            P("dp"),
            P("dp"),
            P(),
            P(None, "mp"),
            P(),
            P(None, "mp"),
            P(None, "mp"),
            P(None, "mp"),
            P("mp", None),
            P(),
            P(None, "mp"),
            P(None, "mp"),
            P(None, "mp"),
            P("mp", None),
            P(),
            P(None, "mp"),
            P("mp", None),
            P(("dp", "mp"), None),
        ),
        out_specs=(
            P(("dp", "mp"), None),
            P(("dp", "mp"), None),
            P(("dp", "mp"), None),
            P(None, "mp"),
            P(),
            P(None, "mp"),
            P(None, "mp"),
            P(None, "mp"),
            P("mp", None),
            P(),
            P(None, "mp"),
            P(None, "mp"),
            P(None, "mp"),
            P("mp", None),
            P(),
            P(None, "mp"),
            P("mp", None),
        ),
        check_vma=False,
    )
```

```python
import functools

import jax
import jax.numpy as jnp
from jax import lax
from jax.experimental import pallas as pl
from jax.experimental.pallas import tpu as pltpu
from jax.sharding import PartitionSpec as P

HEAD_DIM = 64
NORM_EPS = 1e-06
MASKED = -1e30
SCALE = HEAD_DIM**-0.5
BF16 = jnp.bfloat16
F32 = jnp.float32
LANES = 128
TABLE_ROWS = 16
Q_BLOCK = 256
K_BLOCK = 512
HIDDEN_BLOCK = 256
ROW_BLOCK = 128
VMEM_BYTES = 56 * 1024 * 1024
GELU_ROOT = 0.7978845608028654
GELU_CUBE = 0.044715


def dot_nn(a, b):
    return lax.dot_general(a, b, (((1,), (0,)), ((), ())), preferred_element_type=F32)


def dot_nt(a, b):
    return lax.dot_general(a, b, (((1,), (1,)), ((), ())), preferred_element_type=F32)


def dot_tn(a, b):
    return lax.dot_general(a, b, (((0,), (0,)), ((), ())), preferred_element_type=F32)


def flip(a):
    return a.astype(F32).T.astype(BF16)


def head(h):
    return slice(h * HEAD_DIM, (h + 1) * HEAD_DIM)


def row_blocks(ref):
    return [slice(i, i + ROW_BLOCK) for i in range(0, ref.shape[0], ROW_BLOCK)]


def norm_scale(rows):
    return lax.rsqrt(jnp.mean(rows * rows, axis=-1, keepdims=True) + NORM_EPS)


def norm_into(normed_ref, rows_ref, gain_ref):
    for span in row_blocks(rows_ref):
        rows = rows_ref[span].astype(F32)
        normed_ref[span] = (rows * norm_scale(rows) * gain_ref[...]).astype(BF16)


def norm_back_into(out_ref, low_ref, gain_grad_ref, rows_ref, gain_ref, grad_ref, add_ref):
    gain_grad_ref[...] = jnp.zeros_like(gain_grad_ref)
    for span in row_blocks(rows_ref):
        rows, grad = rows_ref[span].astype(F32), grad_ref[span]
        scale = norm_scale(rows)
        unit = rows * scale
        grad_unit = grad * gain_ref[...]
        mean = jnp.mean(grad_unit * unit, axis=-1, keepdims=True)
        out = add_ref[span].astype(F32) + scale * (grad_unit - unit * mean)
        out_ref[span] = out
        if low_ref is not None:
            low_ref[span] = out.astype(BF16)
        gain_grad_ref[...] += jnp.sum((grad * unit).reshape(-1, 8, rows.shape[1]), axis=0)


def gelu_and_slope(v):
    square = v * v
    bend = jnp.tanh(GELU_ROOT * (v + GELU_CUBE * v * square))
    half = 0.5 * (1.0 + bend)
    slope = half + 0.5 * v * (1.0 - bend * bend) * GELU_ROOT * (1.0 + 3.0 * GELU_CUBE * square)
    return v * half, slope


def bias_block(table, ids_ref, h, rows, start):
    row = jnp.broadcast_to(table[h : h + 1, :], (rows, LANES))
    return jnp.concatenate(
        [
            jnp.take_along_axis(row, ids_ref[:rows, c : c + LANES], axis=1)
            for c in range(start, start + Q_BLOCK, LANES)
        ],
        axis=1,
    )


def bias_table(weights, buckets):
    table = weights[-TABLE_ROWS:, :LANES].astype(F32)
    lane = lax.broadcasted_iota(jnp.int32, table.shape, 1)
    return jnp.where(lane < buckets, table, MASKED)


def fetch(first, share, sources, stack, sems):
    @pl.when(first & (share == 0))
    def _():
        for p, source in enumerate(sources):
            pltpu.make_async_copy(source, stack.at[p], sems.at[p]).start()

    for p, source in enumerate(sources):

        @pl.when(first & (share == p))
        def _(p=p, source=source):
            pltpu.make_async_copy(source, stack.at[p], sems.at[p]).wait()


def store_share(share, half, give_ref, keep_ref, rows, value):
    value = value.astype(BF16)

    @pl.when(share < half)
    def _():
        give_ref[0, rows] = value

    @pl.when(share >= half)
    def _():
        keep_ref[0, rows] = value


def self_forward_kernel(heads, buckets, shares, rows_ref, gain_ref, ids_ref, *refs):
    sources, (qkv_ref, mixed_ref, lse_ref, out_ref, w_ref, normed_ref, sems) = (
        refs[:shares],
        refs[shares:],
    )
    share = pl.program_id(0)
    width = heads * HEAD_DIM
    doc = rows_ref.shape[0]
    fetch(True, share, sources, w_ref, sems)

    @pl.when(share == 0)
    def _():
        norm_into(normed_ref, rows_ref, gain_ref)
        out_ref[...] = rows_ref[...].astype(F32)

    weights = w_ref.at[share]
    qkv_ref[0] = dot_nt(normed_ref[...], weights[: 3 * width]).astype(BF16)
    table = bias_table(weights, buckets)
    for h in range(heads):
        cols = head(h)
        k = qkv_ref[0, :, width + cols.start : width + cols.stop]
        q_t = flip(qkv_ref[0, :, cols].astype(F32) * SCALE)
        v_t = flip(qkv_ref[0, :, 2 * width + cols.start : 2 * width + cols.stop])
        for start in range(0, doc, Q_BLOCK):
            rows = start + Q_BLOCK
            span = slice(start, rows)
            s = dot_nn(k[:rows], q_t[:, span]) + bias_block(table, ids_ref, h, rows, start)
            top = jnp.max(s, axis=0, keepdims=True)
            p = jnp.exp(s - top)
            total = jnp.sum(p, axis=0, keepdims=True)
            mixed_t = dot_nn(v_t[:, :rows], p.astype(BF16)) / total
            mixed_ref[0, span, cols] = mixed_t.T.astype(BF16)
            lse_ref[0, h : h + 1, span] = top + jnp.log(total)
    out_ref[...] += dot_nn(mixed_ref[0], weights[3 * width : 4 * width])


def self_backward_kernel(heads, buckets, shares, *refs):
    rows_ref, gain_ref, ids_ref, branch_ref, add_ref, qkv_ref, mixed_ref, lse_ref = refs[:8]
    sources = refs[8 : 8 + shares]
    give_ref, keep_ref, ds_ref, out_ref, gain_grad_ref = refs[8 + shares : 13 + shares]
    w_ref, normed_ref, back_ref, g_ref, grad_ref, sems = refs[13 + shares :]
    share, half = pl.program_id(0), shares // 2
    width = heads * HEAD_DIM
    doc = rows_ref.shape[0]
    fetch(True, share, sources, w_ref, sems)

    @pl.when(share == 0)
    def _():
        norm_into(normed_ref, rows_ref, gain_ref)
        back_ref[...] = jnp.zeros_like(back_ref)

    weights = w_ref.at[share]
    w_out = slice(3 * width, 4 * width)
    table = bias_table(weights, buckets)
    g_ref[...] = dot_nt(branch_ref[...], weights[w_out]).astype(BF16)
    for h in range(heads):
        cols = head(h)
        k_cols = slice(width + cols.start, width + cols.stop)
        v_cols = slice(2 * width + cols.start, 2 * width + cols.stop)
        q = qkv_ref[0, :, cols]
        k = qkv_ref[0, :, k_cols]
        v = qkv_ref[0, :, v_cols]
        g = g_ref[:, cols]
        q_t = flip(q.astype(F32) * SCALE)
        k_t = flip(k)
        g_t = g.astype(F32).T
        inner = jnp.sum(g_t * mixed_ref[0, :, cols].astype(F32).T, axis=0, keepdims=True)
        g_t = g_t.astype(BF16)
        grad_k = grad_v = None
        for start in range(0, doc, Q_BLOCK):
            rows = start + Q_BLOCK
            span = slice(start, rows)
            s = dot_nn(k[:rows], q_t[:, span]) + bias_block(table, ids_ref, h, rows, start)
            p = jnp.exp(s - lse_ref[0, h : h + 1, span])
            grad_p = dot_nn(v[:rows], g_t[:, span])
            ds = (p * (grad_p - inner[:, span])).astype(BF16)
            ds_ref[0, h, :rows, span] = ds
            grad_q = dot_nn(k_t[:, :rows], ds) * SCALE
            grad_ref[span, cols] = grad_q.T.astype(BF16)
            part_v = dot_nn(p.astype(BF16), g[span])
            part_k = dot_nn(ds, q[span])
            if grad_v is not None:
                part_v = jnp.concatenate([part_v[:start] + grad_v, part_v[start:]], axis=0)
                part_k = jnp.concatenate([part_k[:start] + grad_k, part_k[start:]], axis=0)
            grad_v, grad_k = part_v, part_k
        grad_ref[:, k_cols] = (grad_k * SCALE).astype(BF16)
        grad_ref[:, v_cols] = grad_v.astype(BF16)
    store_share(
        share,
        half,
        give_ref,
        keep_ref,
        slice(0, 3 * width),
        dot_tn(grad_ref[...], normed_ref[...]),
    )
    store_share(
        share, half, give_ref, keep_ref, w_out, dot_tn(mixed_ref[0], branch_ref[...])
    )
    back_ref[...] += dot_nn(grad_ref[...], weights[: 3 * width])

    @pl.when(share == shares - 1)
    def _():
        norm_back_into(out_ref, None, gain_grad_ref, rows_ref, gain_ref, back_ref, add_ref)


def bucket_sum_kernel(heads, buckets, ids_ref, ds_ref, out_ref, wide_ref):
    doc = ids_ref.shape[0]
    wide_ref[...] = ds_ref[0].astype(F32)

    def one_bucket(b, carry):
        sums = [jnp.zeros((8, LANES), F32) for _ in range(heads)]
        for c in range(0, doc, LANES):
            rows = c + LANES
            hit = ids_ref[:rows, c : c + LANES] == b
            for h in range(heads):
                kept = jnp.where(hit, wide_ref[h, :rows, c : c + LANES], 0.0)
                sums[h] = sums[h] + jnp.sum(kept.reshape(rows // 8, 8, LANES), axis=0)
        for h in range(heads):
            out_ref[0, h, pl.ds(b, 1), :] = jnp.sum(sums[h], axis=0, keepdims=True)
        return carry

    lax.fori_loop(0, buckets, one_bucket, 0)


def cross_forward_kernel(heads, shares, rows_ref, gain_ref, memory_ref, mask_ref, *refs):
    sources = refs[:shares]
    q_ref, k_ref, v_ref, mixed_ref, lse_ref, out_ref = refs[shares : shares + 6]
    w_ref, normed_ref, q_t, top_ref, sum_ref, mix_t, sems = refs[shares + 6 :]
    share, step = pl.program_id(0), pl.program_id(1)
    width = heads * HEAD_DIM
    doc = rows_ref.shape[0]
    fetch(step == 0, share, sources, w_ref, sems)
    weights = w_ref.at[share]

    @pl.when((share == 0) & (step == 0))
    def _():
        norm_into(normed_ref, rows_ref, gain_ref)
        out_ref[...] = rows_ref[...]

    @pl.when(step == 0)
    def _():
        q_ref[0] = dot_nt(normed_ref[...], weights[:width]).astype(BF16)
        for h in range(heads):
            q_t[head(h), :] = flip(q_ref[0, :, head(h)].astype(F32) * SCALE)
        top_ref[...] = jnp.full_like(top_ref, MASKED)
        sum_ref[...] = jnp.zeros_like(sum_ref)
        mix_t[...] = jnp.zeros_like(mix_t)

    k_ref[0] = dot_nt(memory_ref[...], weights[width : 2 * width]).astype(BF16)
    v_ref[0] = dot_nt(memory_ref[...], weights[2 * width : 3 * width]).astype(BF16)
    for h in range(heads):
        k = k_ref[0, :, head(h)]
        v_t = flip(v_ref[0, :, head(h)])
        for start in range(0, doc, Q_BLOCK):
            span = slice(start, start + Q_BLOCK)
            s = dot_nn(k, q_t[head(h), span]) + mask_ref[...]
            old = top_ref[h : h + 1, span]
            top = jnp.maximum(old, jnp.max(s, axis=0, keepdims=True))
            p = jnp.exp(s - top)
            decay = jnp.exp(old - top)
            top_ref[h : h + 1, span] = top
            sum_ref[h : h + 1, span] = sum_ref[h : h + 1, span] * decay + jnp.sum(
                p, axis=0, keepdims=True
            )
            mix_t[head(h), span] = mix_t[head(h), span] * decay + dot_nn(v_t, p.astype(BF16))

    @pl.when(step == pl.num_programs(1) - 1)
    def _():
        for h in range(heads):
            mixed = mix_t[head(h), :] / sum_ref[h : h + 1, :]
            mixed_ref[0, :, head(h)] = mixed.T.astype(BF16)
        lse_ref[0] = top_ref[...] + jnp.log(sum_ref[...])
        out_ref[...] += dot_nn(mixed_ref[0], weights[3 * width : 4 * width])


def cross_backward_kernel(heads, shares, *refs):
    rows_ref, gain_ref, memory_ref, mask_ref, branch_ref, add_ref = refs[:6]
    q_ref, k_ref, v_ref, mixed_ref, lse_ref = refs[6:11]
    sources = refs[11 : 11 + shares]
    give_ref, keep_ref, memory_out_ref, out_ref, low_ref, gain_grad_ref = refs[
        11 + shares : 17 + shares
    ]
    (
        w_ref,
        normed_ref,
        back_ref,
        memory_acc,
        g_ref,
        q_t,
        g_t,
        inner_ref,
        grad_q_t,
        grad_q_ref,
        grad_k_ref,
        grad_v_ref,
        sum_k_ref,
        sum_v_ref,
        sems,
    ) = refs[17 + shares :]
    step, share, half = pl.program_id(0), pl.program_id(1), shares // 2
    last = pl.num_programs(0) - 1
    width = heads * HEAD_DIM
    doc = rows_ref.shape[0]
    w_out = slice(3 * width, 4 * width)
    fetch(step == 0, share, sources, w_ref, sems)
    weights = w_ref.at[share]

    @pl.when((step == 0) & (share == 0))
    def _():
        norm_into(normed_ref, rows_ref, gain_ref)
        back_ref[...] = jnp.zeros_like(back_ref)

    @pl.when(step == 0)
    def _():
        g_ref[share] = dot_nt(branch_ref[...], weights[w_out]).astype(BF16)
        for h in range(heads):
            q_t[share, head(h), :] = flip(q_ref[share, :, head(h)].astype(F32) * SCALE)
            wide = g_ref[share, :, head(h)].astype(F32).T
            g_t[share, head(h), :] = wide.astype(BF16)
            inner_ref[share, h : h + 1, :] = jnp.sum(
                wide * mixed_ref[share, :, head(h)].astype(F32).T, axis=0, keepdims=True
            )
        grad_q_t[share] = jnp.zeros(grad_q_t.shape[1:], F32)
        sum_k_ref[share] = jnp.zeros(sum_k_ref.shape[1:], F32)
        sum_v_ref[share] = jnp.zeros(sum_v_ref.shape[1:], F32)

    @pl.when(share == 0)
    def _():
        memory_acc[...] = jnp.zeros_like(memory_acc)

    for h in range(heads):
        k = k_ref[0, :, head(h)]
        v = v_ref[0, :, head(h)]
        k_t = flip(k)
        grad_k = grad_v = None
        for start in range(0, doc, Q_BLOCK):
            span = slice(start, start + Q_BLOCK)
            s = dot_nn(k, q_t[share, head(h), span]) + mask_ref[...]
            p = jnp.exp(s - lse_ref[share, h : h + 1, span])
            grad_p = dot_nn(v, g_t[share, head(h), span])
            ds = (p * (grad_p - inner_ref[share, h : h + 1, span])).astype(BF16)
            part_v = dot_nn(p.astype(BF16), g_ref[share, span, head(h)])
            part_k = dot_nn(ds, q_ref[share, span, head(h)])
            grad_q_t[share, head(h), span] += dot_nn(k_t, ds)
            grad_v = part_v if grad_v is None else grad_v + part_v
            grad_k = part_k if grad_k is None else grad_k + part_k
        grad_k_ref[:, head(h)] = (grad_k * SCALE).astype(BF16)
        grad_v_ref[:, head(h)] = grad_v.astype(BF16)
    memory = memory_ref[...]
    sum_k_ref[share] += dot_tn(grad_k_ref[...], memory)
    sum_v_ref[share] += dot_tn(grad_v_ref[...], memory)
    memory_acc[...] += dot_nn(grad_k_ref[...], weights[width : 2 * width]) + dot_nn(
        grad_v_ref[...], weights[2 * width : 3 * width]
    )

    @pl.when(share == shares - 1)
    def _():
        memory_out_ref[...] = memory_acc[...].astype(BF16)

    @pl.when(step == last)
    def _():
        for h in range(heads):
            grad_q_ref[:, head(h)] = (grad_q_t[share, head(h), :] * SCALE).T.astype(BF16)
        parts = (
            (slice(0, width), dot_tn(grad_q_ref[...], normed_ref[...])),
            (slice(width, 2 * width), sum_k_ref[share]),
            (slice(2 * width, 3 * width), sum_v_ref[share]),
            (w_out, dot_tn(mixed_ref[share], branch_ref[...])),
        )
        for rows, value in parts:
            store_share(share, half, give_ref, keep_ref, rows, value)
        back_ref[...] += dot_nn(grad_q_ref[...], weights[:width])

    @pl.when((step == last) & (share == shares - 1))
    def _():
        norm_back_into(out_ref, low_ref, gain_grad_ref, rows_ref, gain_ref, back_ref, add_ref)


def feed_forward_kernel(shares, rows_ref, gain_ref, cotangent_ref, *refs):
    wide_sources, narrow_sources = refs[:shares], refs[shares : 2 * shares]
    give_ref, keep_ref, layer_ref, out_ref, low_ref, gain_grad_ref = refs[
        2 * shares : 2 * shares + 6
    ]
    wide_ref, narrow_ref, normed_ref, acc_ref, back_ref, wide_sems, narrow_sems = refs[
        2 * shares + 6 :
    ]
    share, step, half = pl.program_id(0), pl.program_id(1), shares // 2
    fetch(step == 0, share, wide_sources, wide_ref, wide_sems)
    fetch(step == 0, share, narrow_sources, narrow_ref, narrow_sems)

    @pl.when((share == 0) & (step == 0))
    def _():
        norm_into(normed_ref, rows_ref, gain_ref)
        acc_ref[...] = rows_ref[...]
        back_ref[...] = jnp.zeros_like(back_ref)

    normed, cotangent = normed_ref[...], cotangent_ref[...]
    hidden = pl.ds(pl.multiple_of(step * HIDDEN_BLOCK, HIDDEN_BLOCK), HIDDEN_BLOCK)
    wide, narrow = wide_ref[share, hidden], narrow_ref[share, hidden]
    activated, slope = gelu_and_slope(dot_nt(normed, wide))
    activated = activated.astype(BF16)
    acc_ref[...] += dot_nn(activated, narrow)
    store_share(share, half, give_ref, keep_ref, 1, dot_tn(activated, cotangent))
    grad_widened = (dot_nt(cotangent, narrow) * slope).astype(BF16)
    back_ref[...] += dot_nn(grad_widened, wide)
    store_share(share, half, give_ref, keep_ref, 0, dot_tn(grad_widened, normed))

    @pl.when((share == shares - 1) & (step == pl.num_programs(1) - 1))
    def _():
        layer_ref[...] = acc_ref[...].astype(BF16)
        norm_back_into(
            out_ref, low_ref, gain_grad_ref, rows_ref, gain_ref, back_ref, cotangent_ref
        )


def params():
    return pltpu.CompilerParams(vmem_limit_bytes=VMEM_BYTES)


def cost(flops, size, exps):
    return pl.CostEstimate(flops=flops, bytes_accessed=size, transcendentals=exps)


def shape(dims, dtype):
    return jax.ShapeDtypeStruct(dims, dtype)


def whole(array):
    return pl.BlockSpec(array.shape, lambda *_: (0,) * len(array.shape))


def anywhere(arrays):
    return [pl.BlockSpec(memory_space=pl.ANY) for _ in arrays]


def self_forward(heads, buckets, rows, gain, weights, ids):
    doc, features = rows.shape
    width, shares = heads * HEAD_DIM, len(weights)
    area = shares * heads * doc * doc
    out_shape = (
        shape((shares, doc, 3 * width), BF16),
        shape((shares, doc, width), BF16),
        shape((shares, 8, doc), F32),
        shape((doc, features), F32),
    )
    return pl.pallas_call(
        functools.partial(self_forward_kernel, heads, buckets, shares),
        grid=(shares,),
        in_specs=[whole(rows), whole(gain), whole(ids), *anywhere(weights)],
        out_specs=(
            *[pl.BlockSpec((1, *o.shape[1:]), lambda i: (i, 0, 0)) for o in out_shape[:3]],
            whole(out_shape[3]),
        ),
        out_shape=out_shape,
        scratch_shapes=[
            pltpu.VMEM((shares, *weights[0].shape), BF16),
            pltpu.VMEM((doc, features), BF16),
            pltpu.SemaphoreType.DMA((shares,)),
        ],
        compiler_params=params(),
        cost_estimate=cost(16 * area * HEAD_DIM, 8 << 20, area),
        name="self_forward",
    )(rows, gain, ids, *weights)


def self_backward(heads, buckets, rows, gain, ids, branch, add, saved, weights):
    doc, features = rows.shape
    width, shares = heads * HEAD_DIM, len(weights)
    half = shares // 2
    area = shares * heads * doc * doc
    packed = shape((half, 4 * width, features), BF16)
    out_shape = (
        packed,
        packed,
        shape((shares, heads, doc, doc), BF16),
        shape((doc, features), F32),
        shape((8, features), F32),
    )
    return pl.pallas_call(
        functools.partial(self_backward_kernel, heads, buckets, shares),
        grid=(shares,),
        in_specs=[
            whole(rows),
            whole(gain),
            whole(ids),
            whole(branch),
            whole(add),
            *[pl.BlockSpec((1, *s.shape[1:]), lambda i: (i, 0, 0)) for s in saved],
            *anywhere(weights),
        ],
        out_specs=(
            pl.BlockSpec((1, *packed.shape[1:]), lambda i: (jnp.minimum(i, half - 1), 0, 0)),
            pl.BlockSpec((1, *packed.shape[1:]), lambda i: (jnp.maximum(i - half, 0), 0, 0)),
            pl.BlockSpec((1, heads, doc, doc), lambda i: (i, 0, 0, 0)),
            whole(out_shape[3]),
            whole(out_shape[4]),
        ),
        out_shape=out_shape,
        scratch_shapes=[
            pltpu.VMEM((shares, *weights[0].shape), BF16),
            pltpu.VMEM((doc, features), BF16),
            pltpu.VMEM((doc, features), F32),
            pltpu.VMEM((doc, width), BF16),
            pltpu.VMEM((doc, 3 * width), BF16),
            pltpu.SemaphoreType.DMA((shares,)),
        ],
        compiler_params=params(),
        cost_estimate=cost(40 * area * HEAD_DIM, 16 << 20, area),
        name="self_backward",
    )(rows, gain, ids, branch, add, *saved, *weights)


def bucket_sums(ids, ds, buckets):
    shares, heads, doc, _ = ds.shape
    sums = pl.pallas_call(
        functools.partial(bucket_sum_kernel, heads, buckets),
        grid=(shares,),
        in_specs=[whole(ids), pl.BlockSpec((1, heads, doc, doc), lambda i: (i, 0, 0, 0))],
        out_specs=pl.BlockSpec((1, heads, buckets, LANES), lambda i: (i, 0, 0, 0)),
        out_shape=shape((shares, heads, buckets, LANES), F32),
        scratch_shapes=[pltpu.VMEM(ds.shape[1:], F32)],
        compiler_params=params(),
        cost_estimate=cost(64 * ds.size, 16 << 20, 0),
        name="bucket_sums",
    )(ids, ds)
    return jnp.sum(sums, axis=3)


def cross_forward(heads, rows, gain, memory, mask, weights):
    (doc, features), slots = rows.shape, memory.shape[0]
    width, shares = heads * HEAD_DIM, len(weights)
    area = shares * heads * doc * slots
    out_shape = (
        shape((shares, doc, width), BF16),
        shape((shares, slots, width), BF16),
        shape((shares, slots, width), BF16),
        shape((shares, doc, width), BF16),
        shape((shares, 8, doc), F32),
        shape((doc, features), F32),
    )
    key = pl.BlockSpec((1, K_BLOCK, width), lambda i, j: (i, j, 0))
    query = pl.BlockSpec((1, doc, width), lambda i, j: (i, 0, 0))
    return pl.pallas_call(
        functools.partial(cross_forward_kernel, heads, shares),
        grid=(shares, slots // K_BLOCK),
        in_specs=[
            whole(rows),
            whole(gain),
            pl.BlockSpec((K_BLOCK, features), lambda i, j: (j, 0)),
            pl.BlockSpec((K_BLOCK, Q_BLOCK), lambda i, j: (j, 0)),
            *anywhere(weights),
        ],
        out_specs=(
            query,
            key,
            key,
            query,
            pl.BlockSpec((1, 8, doc), lambda i, j: (i, 0, 0)),
            whole(out_shape[5]),
        ),
        out_shape=out_shape,
        scratch_shapes=[
            pltpu.VMEM((shares, *weights[0].shape), BF16),
            pltpu.VMEM((doc, features), BF16),
            pltpu.VMEM((width, doc), BF16),
            pltpu.VMEM((8, doc), F32),
            pltpu.VMEM((8, doc), F32),
            pltpu.VMEM((width, doc), F32),
            pltpu.SemaphoreType.DMA((shares,)),
        ],
        compiler_params=params(),
        cost_estimate=cost(16 * area * HEAD_DIM, 16 << 20, area),
        name="cross_forward",
    )(rows, gain, memory, mask, *weights)


def cross_backward(heads, rows, gain, memory, mask, branch, add, saved, weights):
    (doc, features), slots = rows.shape, memory.shape[0]
    width, shares = heads * HEAD_DIM, len(weights)
    half, steps = shares // 2, slots // K_BLOCK
    area = shares * heads * doc * slots
    packed = shape((half, 4 * width, features), BF16)
    out_shape = (
        packed,
        packed,
        shape((slots, features), BF16),
        shape((doc, features), F32),
        shape((doc, features), BF16),
        shape((8, features), F32),
    )
    key = pl.BlockSpec((1, K_BLOCK, width), lambda i, j: (j, i, 0))
    block = pl.BlockSpec((K_BLOCK, features), lambda i, j: (i, 0))

    def give_index(i, j):
        return (jnp.where(i == steps - 1, jnp.minimum(j, half - 1), 0), 0, 0)

    def keep_index(i, j):
        return (jnp.where(i == steps - 1, jnp.maximum(j - half, 0), 0), 0, 0)

    query, _, _, mixed, lse = saved
    return pl.pallas_call(
        functools.partial(cross_backward_kernel, heads, shares),
        grid=(steps, shares),
        in_specs=[
            whole(rows),
            whole(gain),
            block,
            pl.BlockSpec((K_BLOCK, Q_BLOCK), lambda i, j: (i, 0)),
            whole(branch),
            whole(add),
            whole(query),
            key,
            key,
            whole(mixed),
            whole(lse),
            *anywhere(weights),
        ],
        out_specs=(
            pl.BlockSpec((1, *packed.shape[1:]), give_index),
            pl.BlockSpec((1, *packed.shape[1:]), keep_index),
            block,
            *[whole(o) for o in out_shape[3:]],
        ),
        out_shape=out_shape,
        scratch_shapes=[
            pltpu.VMEM((shares, *weights[0].shape), BF16),
            pltpu.VMEM((doc, features), BF16),
            pltpu.VMEM((doc, features), F32),
            pltpu.VMEM((K_BLOCK, features), F32),
            pltpu.VMEM((shares, doc, width), BF16),
            pltpu.VMEM((shares, width, doc), BF16),
            pltpu.VMEM((shares, width, doc), BF16),
            pltpu.VMEM((shares, 8, doc), F32),
            pltpu.VMEM((shares, width, doc), F32),
            pltpu.VMEM((doc, width), BF16),
            pltpu.VMEM((K_BLOCK, width), BF16),
            pltpu.VMEM((K_BLOCK, width), BF16),
            pltpu.VMEM((shares, width, features), F32),
            pltpu.VMEM((shares, width, features), F32),
            pltpu.SemaphoreType.DMA((shares,)),
        ],
        compiler_params=params(),
        cost_estimate=cost(40 * area * HEAD_DIM, 24 << 20, area),
        name="cross_backward",
    )(rows, gain, memory, mask, branch, add, *saved, *weights)


def feed_forward(rows, gain, cotangent, wide, narrow):
    (doc, features), hidden = rows.shape, wide[0].shape[0]
    shares = len(wide)
    half, steps = shares // 2, hidden // HIDDEN_BLOCK
    packed = shape((half, 2, hidden, features), BF16)
    out_shape = (
        packed,
        packed,
        shape((doc, features), BF16),
        shape((doc, features), F32),
        shape((doc, features), BF16),
        shape((8, features), F32),
    )

    def give_index(i, j):
        late = i >= half
        return (jnp.minimum(i, half - 1), 0, jnp.where(late, steps - 1, j), 0)

    def keep_index(i, j):
        return (jnp.maximum(i - half, 0), 0, jnp.where(i < half, 0, j), 0)

    return pl.pallas_call(
        functools.partial(feed_forward_kernel, shares),
        grid=(shares, steps),
        in_specs=[
            whole(rows),
            whole(gain),
            whole(cotangent),
            *anywhere(wide),
            *anywhere(narrow),
        ],
        out_specs=(
            pl.BlockSpec((1, 2, HIDDEN_BLOCK, features), give_index),
            pl.BlockSpec((1, 2, HIDDEN_BLOCK, features), keep_index),
            *[whole(o) for o in out_shape[2:]],
        ),
        out_shape=out_shape,
        scratch_shapes=[
            pltpu.VMEM((shares, hidden, features), BF16),
            pltpu.VMEM((shares, hidden, features), BF16),
            pltpu.VMEM((doc, features), BF16),
            pltpu.VMEM((doc, features), F32),
            pltpu.VMEM((doc, features), F32),
            pltpu.SemaphoreType.DMA((shares,)),
            pltpu.SemaphoreType.DMA((shares,)),
        ],
        compiler_params=params(),
        cost_estimate=cost(12 * shares * doc * features * hidden, 40 << 20, shares * doc * hidden),
        name="feed_forward",
    )(rows, gain, cotangent, *wide, *narrow)


def swap(array, bit, size):
    return lax.ppermute(array, "mp", [(i, i ^ bit) for i in range(size)])


def add_low(a, b):
    return (a.astype(F32) + b.astype(F32)).astype(BF16)


def fold_rest(stack, size):
    shares, bit = {2 * i: stack[i] for i in range(stack.shape[0])}, 2
    while bit < size:
        shares = {
            j: add_low(shares[j], swap(shares[j | bit], bit, size)) for j in shares if not j & bit
        }
        bit *= 2
    return shares[0]


def shards(
    decoder_rows,
    memory_rows,
    decoder_token_length,
    memory_length,
    bucket_ids,
    relative_bucket_bias,
    self_gain,
    self_query,
    self_key,
    self_value,
    self_out,
    cross_gain,
    cross_query,
    cross_key,
    cross_value,
    cross_out,
    hidden_gain,
    widen_weight,
    narrow_weight,
    layer_cotangent,
):
    dp_size = lax.axis_size("dp")
    mp_size = lax.axis_size("mp")
    me = lax.axis_index("mp")
    doc, features = decoder_rows.shape
    slots = memory_rows.shape[0]
    cols = self_query.shape[1]
    heads = cols // HEAD_DIM
    buckets = relative_bucket_bias.shape[0]
    order = [*range(1, mp_size, 2), *range(0, mp_size, 2)]

    bias_rows = jnp.zeros((TABLE_ROWS, features), BF16)
    bias_rows = bias_rows.at[:heads, :buckets].set(relative_bucket_bias.T)
    own_self = jnp.concatenate(
        [self_query.T, self_key.T, self_value.T, self_out, bias_rows], axis=0
    )
    own_cross = jnp.concatenate([cross_query.T, cross_key.T, cross_value.T, cross_out], axis=0)
    own_self, memory_rows = lax.optimization_barrier((own_self, memory_rows))
    memory_seen = lax.all_to_all(
        memory_rows.reshape(dp_size, slots // dp_size, features), "dp", 0, 0
    ).reshape(slots, features)

    def gather(own):
        shares, bit = {0: own}, mp_size // 2
        while bit:
            for j in list(shares):
                shares[j | bit] = swap(shares[j], bit, mp_size)
            bit //= 2
        return [shares[j] for j in order]

    w_self = gather(own_self)
    w_cross = gather(own_cross)
    w_wide = gather(widen_weight.T)
    w_narrow = gather(narrow_weight)

    doc_length = lax.dynamic_index_in_dim(decoder_token_length, me, keepdims=False)
    doc_memory = lax.dynamic_index_in_dim(memory_length, me, keepdims=False)
    position = jnp.arange(doc, dtype=jnp.int32)
    allowed = (position[:, None] <= position[None, :]) & (position[:, None] < doc_length)
    ids = jnp.where(allowed, bucket_ids.T, buckets)
    mask = jnp.where(jnp.arange(slots, dtype=jnp.int32) < doc_memory, 0.0, MASKED)
    mask = jnp.broadcast_to(mask[:, None].astype(F32), (slots, Q_BLOCK))

    gain_self = self_gain.astype(F32)[None]
    gain_cross = cross_gain.astype(F32)[None]
    gain_hidden = hidden_gain.astype(F32)[None]

    *saved_self, after_self = self_forward(heads, buckets, decoder_rows, gain_self, w_self, ids)
    *saved_cross, after_cross = cross_forward(
        heads, after_self, gain_cross, memory_seen, mask, w_cross
    )

    give, keep, layer_output, grad_after_cross, branch, hidden_gain_grad = feed_forward(
        after_cross, gain_hidden, layer_cotangent, w_wide, w_narrow
    )
    part_hidden = add_low(keep, swap(give, 1, mp_size))
    branch, part_hidden = lax.optimization_barrier((branch, part_hidden))

    give, keep, grad_memory, grad_after_self, branch, cross_gain_grad = cross_backward(
        heads,
        after_self,
        gain_cross,
        memory_seen,
        mask,
        branch,
        grad_after_cross,
        saved_cross,
        w_cross,
    )
    memory_grad = lax.all_to_all(
        grad_memory.reshape(dp_size, slots // dp_size, features), "dp", 0, 0
    ).reshape(slots, features)
    part_hidden = fold_rest(part_hidden, mp_size)
    branch, part_hidden = lax.optimization_barrier((branch, part_hidden))
    sum_hidden = lax.psum(part_hidden, "dp")
    part_cross = add_low(keep, swap(give, 1, mp_size))

    give, keep, score_grads, input_grad, self_gain_grad = self_backward(
        heads,
        buckets,
        decoder_rows,
        gain_self,
        ids,
        branch,
        grad_after_self,
        saved_self,
        w_self,
    )
    part_self = add_low(keep, swap(give, 1, mp_size))
    part_cross = fold_rest(part_cross, mp_size)
    part_self = fold_rest(part_self, mp_size)
    part_cross, part_self, sum_hidden = lax.optimization_barrier(
        (part_cross, part_self, sum_hidden)
    )
    sum_cross, sum_self = lax.psum((part_cross, part_self), "dp")

    sums = bucket_sums(ids, score_grads, buckets)
    back_to = [order.index(j) for j in range(mp_size)]
    sums = jnp.stack([sums[i] for i in back_to])
    sums = jnp.take(sums, me ^ jnp.arange(mp_size), axis=0)
    gains = jnp.stack([self_gain_grad, cross_gain_grad, hidden_gain_grad]).sum(axis=1)
    small = lax.psum(jnp.concatenate([gains.reshape(-1), sums.reshape(-1)]), ("dp", "mp"))
    gains = small[: 3 * features].reshape(3, features)
    sums = small[3 * features :].reshape(mp_size, heads, buckets)
    position_grad = lax.dynamic_index_in_dim(sums, me, keepdims=False).T

    sum_self = sum_self.astype(F32)
    sum_cross = sum_cross.astype(F32)
    sum_hidden = sum_hidden.astype(F32)
    return (
        layer_output,
        input_grad,
        memory_grad,
        position_grad,
        gains[0],
        sum_self[:cols].T,
        sum_self[cols : 2 * cols].T,
        sum_self[2 * cols : 3 * cols].T,
        sum_self[3 * cols :],
        gains[1],
        sum_cross[:cols].T,
        sum_cross[cols : 2 * cols].T,
        sum_cross[2 * cols : 3 * cols].T,
        sum_cross[3 * cols :],
        gains[2],
        sum_hidden[0].T,
        sum_hidden[1],
    )


def solution(mesh):
    return jax.shard_map(
        shards,
        mesh=mesh,
        in_specs=(
            P(("dp", "mp"), None),
            P(("dp", "mp"), None),
            P("dp"),
            P("dp"),
            P(),
            P(None, "mp"),
            P(),
            P(None, "mp"),
            P(None, "mp"),
            P(None, "mp"),
            P("mp", None),
            P(),
            P(None, "mp"),
            P(None, "mp"),
            P(None, "mp"),
            P("mp", None),
            P(),
            P(None, "mp"),
            P("mp", None),
            P(("dp", "mp"), None),
        ),
        out_specs=(
            P(("dp", "mp"), None),
            P(("dp", "mp"), None),
            P(("dp", "mp"), None),
            P(None, "mp"),
            P(),
            P(None, "mp"),
            P(None, "mp"),
            P(None, "mp"),
            P("mp", None),
            P(),
            P(None, "mp"),
            P(None, "mp"),
            P(None, "mp"),
            P("mp", None),
            P(),
            P(None, "mp"),
            P("mp", None),
        ),
        check_vma=False,
    )
```

```python
import functools

import jax
import jax.numpy as jnp
from jax import lax
from jax.experimental import pallas as pl
from jax.experimental.pallas import tpu as pltpu
from jax.sharding import PartitionSpec as P

HEAD_DIM = 64
NORM_EPS = 1e-06
MASKED = -1e30
SCALE = HEAD_DIM**-0.5
BF16 = jnp.bfloat16
F32 = jnp.float32
LANES = 128
TABLE_ROWS = 16
Q_BLOCK = 256
K_BLOCK = 512
HIDDEN_BLOCK = 256
ROW_BLOCK = 128
VMEM_BYTES = 56 * 1024 * 1024
GELU_ROOT = 0.7978845608028654
GELU_CUBE = 0.044715


def dot_nn(a, b):
    return lax.dot_general(a, b, (((1,), (0,)), ((), ())), preferred_element_type=F32)


def dot_nt(a, b):
    return lax.dot_general(a, b, (((1,), (1,)), ((), ())), preferred_element_type=F32)


def dot_tn(a, b):
    return lax.dot_general(a, b, (((0,), (0,)), ((), ())), preferred_element_type=F32)


def flip(a):
    return a.astype(F32).T.astype(BF16)


def head(h):
    return slice(h * HEAD_DIM, (h + 1) * HEAD_DIM)


def row_blocks(ref):
    return [slice(i, i + ROW_BLOCK) for i in range(0, ref.shape[0], ROW_BLOCK)]


def norm_scale(rows):
    return lax.rsqrt(jnp.mean(rows * rows, axis=-1, keepdims=True) + NORM_EPS)


def norm_into(normed_ref, rows_ref, gain_ref):
    for span in row_blocks(rows_ref):
        rows = rows_ref[span].astype(F32)
        normed_ref[span] = (rows * norm_scale(rows) * gain_ref[...]).astype(BF16)


def norm_back_into(out_ref, low_ref, gain_grad_ref, rows_ref, gain_ref, grad_ref, add_ref):
    gain_grad_ref[...] = jnp.zeros_like(gain_grad_ref)
    for span in row_blocks(rows_ref):
        rows, grad = rows_ref[span].astype(F32), grad_ref[span]
        scale = norm_scale(rows)
        unit = rows * scale
        grad_unit = grad * gain_ref[...]
        mean = jnp.mean(grad_unit * unit, axis=-1, keepdims=True)
        out = add_ref[span].astype(F32) + scale * (grad_unit - unit * mean)
        out_ref[span] = out
        if low_ref is not None:
            low_ref[span] = out.astype(BF16)
        gain_grad_ref[...] += jnp.sum((grad * unit).reshape(-1, 8, rows.shape[1]), axis=0)


def gelu_and_slope(v):
    square = v * v
    bend = jnp.tanh(GELU_ROOT * (v + GELU_CUBE * v * square))
    half = 0.5 * (1.0 + bend)
    slope = half + 0.5 * v * (1.0 - bend * bend) * GELU_ROOT * (1.0 + 3.0 * GELU_CUBE * square)
    return v * half, slope


def bias_block(table, ids_ref, h, rows, start):
    row = jnp.broadcast_to(table[h : h + 1, :], (rows, LANES))
    return jnp.concatenate(
        [
            jnp.take_along_axis(row, ids_ref[:rows, c : c + LANES], axis=1)
            for c in range(start, start + Q_BLOCK, LANES)
        ],
        axis=1,
    )


def bias_table(weights, buckets):
    table = weights[-TABLE_ROWS:, :LANES].astype(F32)
    lane = lax.broadcasted_iota(jnp.int32, table.shape, 1)
    return jnp.where(lane < buckets, table, MASKED)


def fetch(first, share, sources, stack, sems):
    @pl.when(first & (share == 0))
    def _():
        for p, source in enumerate(sources):
            pltpu.make_async_copy(source, stack.at[p], sems.at[p]).start()

    for p, source in enumerate(sources):

        @pl.when(first & (share == p))
        def _(p=p, source=source):
            pltpu.make_async_copy(source, stack.at[p], sems.at[p]).wait()


def store_share(share, half, give_ref, keep_ref, rows, value):
    value = value.astype(BF16)

    @pl.when(share < half)
    def _():
        give_ref[0, rows] = value

    @pl.when(share >= half)
    def _():
        keep_ref[0, rows] = value


def self_forward_kernel(heads, buckets, shares, rows_ref, gain_ref, ids_ref, *refs):
    sources, (qkv_ref, mixed_ref, lse_ref, out_ref, w_ref, normed_ref, sems) = (
        refs[:shares],
        refs[shares:],
    )
    share = pl.program_id(0)
    width = heads * HEAD_DIM
    doc = rows_ref.shape[0]
    fetch(True, share, sources, w_ref, sems)

    @pl.when(share == 0)
    def _():
        norm_into(normed_ref, rows_ref, gain_ref)
        out_ref[...] = rows_ref[...].astype(F32)

    weights = w_ref.at[share]
    qkv_ref[0] = dot_nt(normed_ref[...], weights[: 3 * width]).astype(BF16)
    table = bias_table(weights, buckets)
    for h in range(heads):
        cols = head(h)
        k = qkv_ref[0, :, width + cols.start : width + cols.stop]
        q_t = flip(qkv_ref[0, :, cols].astype(F32) * SCALE)
        v_t = flip(qkv_ref[0, :, 2 * width + cols.start : 2 * width + cols.stop])
        for start in range(0, doc, Q_BLOCK):
            rows = start + Q_BLOCK
            span = slice(start, rows)
            s = dot_nn(k[:rows], q_t[:, span]) + bias_block(table, ids_ref, h, rows, start)
            top = jnp.max(s, axis=0, keepdims=True)
            p = jnp.exp(s - top)
            total = jnp.sum(p, axis=0, keepdims=True)
            mixed_t = dot_nn(v_t[:, :rows], p.astype(BF16)) / total
            mixed_ref[0, span, cols] = mixed_t.T.astype(BF16)
            lse_ref[0, h : h + 1, span] = top + jnp.log(total)
    out_ref[...] += dot_nn(mixed_ref[0], weights[3 * width : 4 * width])


def self_backward_kernel(heads, buckets, shares, *refs):
    rows_ref, gain_ref, ids_ref, branch_ref, add_ref, qkv_ref, mixed_ref, lse_ref = refs[:8]
    sources = refs[8 : 8 + shares]
    give_ref, keep_ref, ds_ref, out_ref, gain_grad_ref = refs[8 + shares : 13 + shares]
    w_ref, normed_ref, back_ref, g_ref, grad_ref, sems = refs[13 + shares :]
    share, half = pl.program_id(0), shares // 2
    width = heads * HEAD_DIM
    doc = rows_ref.shape[0]
    fetch(True, share, sources, w_ref, sems)

    @pl.when(share == 0)
    def _():
        norm_into(normed_ref, rows_ref, gain_ref)
        back_ref[...] = jnp.zeros_like(back_ref)

    weights = w_ref.at[share]
    w_out = slice(3 * width, 4 * width)
    table = bias_table(weights, buckets)
    g_ref[...] = dot_nt(branch_ref[...], weights[w_out]).astype(BF16)
    for h in range(heads):
        cols = head(h)
        k_cols = slice(width + cols.start, width + cols.stop)
        v_cols = slice(2 * width + cols.start, 2 * width + cols.stop)
        q = qkv_ref[0, :, cols]
        k = qkv_ref[0, :, k_cols]
        v = qkv_ref[0, :, v_cols]
        g = g_ref[:, cols]
        q_t = flip(q.astype(F32) * SCALE)
        k_t = flip(k)
        g_t = g.astype(F32).T
        inner = jnp.sum(g_t * mixed_ref[0, :, cols].astype(F32).T, axis=0, keepdims=True)
        g_t = g_t.astype(BF16)
        grad_k = grad_v = None
        for start in range(0, doc, Q_BLOCK):
            rows = start + Q_BLOCK
            span = slice(start, rows)
            s = dot_nn(k[:rows], q_t[:, span]) + bias_block(table, ids_ref, h, rows, start)
            p = jnp.exp(s - lse_ref[0, h : h + 1, span])
            grad_p = dot_nn(v[:rows], g_t[:, span])
            ds = (p * (grad_p - inner[:, span])).astype(BF16)
            ds_ref[0, h, :rows, span] = ds
            grad_q = dot_nn(k_t[:, :rows], ds) * SCALE
            grad_ref[span, cols] = grad_q.T.astype(BF16)
            part_v = dot_nn(p.astype(BF16), g[span])
            part_k = dot_nn(ds, q[span])
            if grad_v is not None:
                part_v = jnp.concatenate([part_v[:start] + grad_v, part_v[start:]], axis=0)
                part_k = jnp.concatenate([part_k[:start] + grad_k, part_k[start:]], axis=0)
            grad_v, grad_k = part_v, part_k
        grad_ref[:, k_cols] = (grad_k * SCALE).astype(BF16)
        grad_ref[:, v_cols] = grad_v.astype(BF16)
    store_share(
        share,
        half,
        give_ref,
        keep_ref,
        slice(0, 3 * width),
        dot_tn(grad_ref[...], normed_ref[...]),
    )
    store_share(
        share, half, give_ref, keep_ref, w_out, dot_tn(mixed_ref[0], branch_ref[...])
    )
    back_ref[...] += dot_nn(grad_ref[...], weights[: 3 * width])

    @pl.when(share == shares - 1)
    def _():
        norm_back_into(out_ref, None, gain_grad_ref, rows_ref, gain_ref, back_ref, add_ref)


def bucket_sum_kernel(heads, buckets, ids_ref, ds_ref, out_ref, wide_ref):
    doc = ids_ref.shape[0]
    wide_ref[...] = ds_ref[0].astype(F32)

    def one_bucket(b, carry):
        sums = [jnp.zeros((8, LANES), F32) for _ in range(heads)]
        for c in range(0, doc, LANES):
            rows = c + LANES
            hit = ids_ref[:rows, c : c + LANES] == b
            for h in range(heads):
                kept = jnp.where(hit, wide_ref[h, :rows, c : c + LANES], 0.0)
                sums[h] = sums[h] + jnp.sum(kept.reshape(rows // 8, 8, LANES), axis=0)
        for h in range(heads):
            out_ref[0, h, pl.ds(b, 1), :] = jnp.sum(sums[h], axis=0, keepdims=True)
        return carry

    lax.fori_loop(0, buckets, one_bucket, 0)


def cross_forward_kernel(heads, shares, rows_ref, gain_ref, memory_ref, mask_ref, *refs):
    sources = refs[:shares]
    q_ref, k_ref, v_ref, mixed_ref, lse_ref, out_ref = refs[shares : shares + 6]
    w_ref, normed_ref, q_t, top_ref, sum_ref, mix_t, sems = refs[shares + 6 :]
    share, step = pl.program_id(0), pl.program_id(1)
    width = heads * HEAD_DIM
    doc = rows_ref.shape[0]
    fetch(step == 0, share, sources, w_ref, sems)
    weights = w_ref.at[share]

    @pl.when((share == 0) & (step == 0))
    def _():
        norm_into(normed_ref, rows_ref, gain_ref)
        out_ref[...] = rows_ref[...]

    @pl.when(step == 0)
    def _():
        q_ref[0] = dot_nt(normed_ref[...], weights[:width]).astype(BF16)
        for h in range(heads):
            q_t[head(h), :] = flip(q_ref[0, :, head(h)].astype(F32) * SCALE)
        top_ref[...] = jnp.full_like(top_ref, MASKED)
        sum_ref[...] = jnp.zeros_like(sum_ref)
        mix_t[...] = jnp.zeros_like(mix_t)

    k_ref[0] = dot_nt(memory_ref[...], weights[width : 2 * width]).astype(BF16)
    v_ref[0] = dot_nt(memory_ref[...], weights[2 * width : 3 * width]).astype(BF16)
    for h in range(heads):
        k = k_ref[0, :, head(h)]
        v_t = flip(v_ref[0, :, head(h)])
        for start in range(0, doc, Q_BLOCK):
            span = slice(start, start + Q_BLOCK)
            s = dot_nn(k, q_t[head(h), span]) + mask_ref[...]
            old = top_ref[h : h + 1, span]
            top = jnp.maximum(old, jnp.max(s, axis=0, keepdims=True))
            p = jnp.exp(s - top)
            decay = jnp.exp(old - top)
            top_ref[h : h + 1, span] = top
            sum_ref[h : h + 1, span] = sum_ref[h : h + 1, span] * decay + jnp.sum(
                p, axis=0, keepdims=True
            )
            mix_t[head(h), span] = mix_t[head(h), span] * decay + dot_nn(v_t, p.astype(BF16))

    @pl.when(step == pl.num_programs(1) - 1)
    def _():
        for h in range(heads):
            mixed = mix_t[head(h), :] / sum_ref[h : h + 1, :]
            mixed_ref[0, :, head(h)] = mixed.T.astype(BF16)
        lse_ref[0] = top_ref[...] + jnp.log(sum_ref[...])
        out_ref[...] += dot_nn(mixed_ref[0], weights[3 * width : 4 * width])


def cross_backward_kernel(heads, shares, *refs):
    rows_ref, gain_ref, memory_ref, mask_ref, branch_ref, add_ref = refs[:6]
    q_ref, k_ref, v_ref, mixed_ref, lse_ref = refs[6:11]
    sources = refs[11 : 11 + shares]
    give_ref, keep_ref, memory_out_ref, out_ref, low_ref, gain_grad_ref = refs[
        11 + shares : 17 + shares
    ]
    (
        w_ref,
        normed_ref,
        back_ref,
        memory_acc,
        g_ref,
        q_t,
        g_t,
        inner_ref,
        grad_q_t,
        grad_q_ref,
        grad_k_ref,
        grad_v_ref,
        sum_k_ref,
        sum_v_ref,
        sems,
    ) = refs[17 + shares :]
    step, share, half = pl.program_id(0), pl.program_id(1), shares // 2
    last = pl.num_programs(0) - 1
    width = heads * HEAD_DIM
    doc = rows_ref.shape[0]
    w_out = slice(3 * width, 4 * width)
    fetch(step == 0, share, sources, w_ref, sems)
    weights = w_ref.at[share]

    @pl.when((step == 0) & (share == 0))
    def _():
        norm_into(normed_ref, rows_ref, gain_ref)
        back_ref[...] = jnp.zeros_like(back_ref)

    @pl.when(step == 0)
    def _():
        g_ref[share] = dot_nt(branch_ref[...], weights[w_out]).astype(BF16)
        for h in range(heads):
            q_t[share, head(h), :] = flip(q_ref[share, :, head(h)].astype(F32) * SCALE)
            wide = g_ref[share, :, head(h)].astype(F32).T
            g_t[share, head(h), :] = wide.astype(BF16)
            inner_ref[share, h : h + 1, :] = jnp.sum(
                wide * mixed_ref[share, :, head(h)].astype(F32).T, axis=0, keepdims=True
            )
        grad_q_t[share] = jnp.zeros(grad_q_t.shape[1:], F32)
        sum_k_ref[share] = jnp.zeros(sum_k_ref.shape[1:], F32)
        sum_v_ref[share] = jnp.zeros(sum_v_ref.shape[1:], F32)

    @pl.when(share == 0)
    def _():
        memory_acc[...] = jnp.zeros_like(memory_acc)

    for h in range(heads):
        k = k_ref[0, :, head(h)]
        v = v_ref[0, :, head(h)]
        k_t = flip(k)
        grad_k = grad_v = None
        for start in range(0, doc, Q_BLOCK):
            span = slice(start, start + Q_BLOCK)
            s = dot_nn(k, q_t[share, head(h), span]) + mask_ref[...]
            p = jnp.exp(s - lse_ref[share, h : h + 1, span])
            grad_p = dot_nn(v, g_t[share, head(h), span])
            ds = (p * (grad_p - inner_ref[share, h : h + 1, span])).astype(BF16)
            part_v = dot_nn(p.astype(BF16), g_ref[share, span, head(h)])
            part_k = dot_nn(ds, q_ref[share, span, head(h)])
            grad_q_t[share, head(h), span] += dot_nn(k_t, ds)
            grad_v = part_v if grad_v is None else grad_v + part_v
            grad_k = part_k if grad_k is None else grad_k + part_k
        grad_k_ref[:, head(h)] = (grad_k * SCALE).astype(BF16)
        grad_v_ref[:, head(h)] = grad_v.astype(BF16)
    memory = memory_ref[...]
    sum_k_ref[share] += dot_tn(grad_k_ref[...], memory)
    sum_v_ref[share] += dot_tn(grad_v_ref[...], memory)
    memory_acc[...] += dot_nn(grad_k_ref[...], weights[width : 2 * width]) + dot_nn(
        grad_v_ref[...], weights[2 * width : 3 * width]
    )

    @pl.when(share == shares - 1)
    def _():
        memory_out_ref[...] = memory_acc[...].astype(BF16)

    @pl.when(step == last)
    def _():
        for h in range(heads):
            grad_q_ref[:, head(h)] = (grad_q_t[share, head(h), :] * SCALE).T.astype(BF16)
        parts = (
            (slice(0, width), dot_tn(grad_q_ref[...], normed_ref[...])),
            (slice(width, 2 * width), sum_k_ref[share]),
            (slice(2 * width, 3 * width), sum_v_ref[share]),
            (w_out, dot_tn(mixed_ref[share], branch_ref[...])),
        )
        for rows, value in parts:
            store_share(share, half, give_ref, keep_ref, rows, value)
        back_ref[...] += dot_nn(grad_q_ref[...], weights[:width])

    @pl.when((step == last) & (share == shares - 1))
    def _():
        norm_back_into(out_ref, low_ref, gain_grad_ref, rows_ref, gain_ref, back_ref, add_ref)


def feed_forward_kernel(shares, rows_ref, gain_ref, cotangent_ref, *refs):
    wide_sources, narrow_sources = refs[:shares], refs[shares : 2 * shares]
    give_ref, keep_ref, layer_ref, out_ref, low_ref, gain_grad_ref = refs[
        2 * shares : 2 * shares + 6
    ]
    wide_ref, narrow_ref, normed_ref, acc_ref, back_ref, wide_sems, narrow_sems = refs[
        2 * shares + 6 :
    ]
    share, step, half = pl.program_id(0), pl.program_id(1), shares // 2
    fetch(step == 0, share, wide_sources, wide_ref, wide_sems)
    fetch(step == 0, share, narrow_sources, narrow_ref, narrow_sems)

    @pl.when((share == 0) & (step == 0))
    def _():
        norm_into(normed_ref, rows_ref, gain_ref)
        acc_ref[...] = rows_ref[...]
        back_ref[...] = jnp.zeros_like(back_ref)

    normed, cotangent = normed_ref[...], cotangent_ref[...]
    hidden = pl.ds(pl.multiple_of(step * HIDDEN_BLOCK, HIDDEN_BLOCK), HIDDEN_BLOCK)
    wide, narrow = wide_ref[share, hidden], narrow_ref[share, hidden]
    activated, slope = gelu_and_slope(dot_nt(normed, wide))
    activated = activated.astype(BF16)
    acc_ref[...] += dot_nn(activated, narrow)
    store_share(share, half, give_ref, keep_ref, 1, dot_tn(activated, cotangent))
    grad_widened = (dot_nt(cotangent, narrow) * slope).astype(BF16)
    back_ref[...] += dot_nn(grad_widened, wide)
    store_share(share, half, give_ref, keep_ref, 0, dot_tn(grad_widened, normed))

    @pl.when((share == shares - 1) & (step == pl.num_programs(1) - 1))
    def _():
        layer_ref[...] = acc_ref[...].astype(BF16)
        norm_back_into(
            out_ref, low_ref, gain_grad_ref, rows_ref, gain_ref, back_ref, cotangent_ref
        )


def params():
    return pltpu.CompilerParams(vmem_limit_bytes=VMEM_BYTES)


def cost():
    return pl.CostEstimate(flops=1 << 20, bytes_accessed=1 << 16, transcendentals=0)


def shape(dims, dtype):
    return jax.ShapeDtypeStruct(dims, dtype)


def whole(array):
    return pl.BlockSpec(array.shape, lambda *_: (0,) * len(array.shape))


def anywhere(arrays):
    return [pl.BlockSpec(memory_space=pl.ANY) for _ in arrays]


def pack_kernel(flipped, *refs):
    out_ref, start = refs[-1], 0
    for source, turn in zip(refs[:-1], flipped):
        rows = source.shape[1] if turn else source.shape[0]
        span = slice(start, start + rows)
        out_ref[span] = flip(source[...]) if turn else source[...]
        start += rows


def pack(*parts):
    arrays, flipped = zip(*parts)
    rows = sum(a.shape[1] if turn else a.shape[0] for a, turn in parts)
    features = arrays[0].shape[0] if flipped[0] else arrays[0].shape[1]
    return pl.pallas_call(
        functools.partial(pack_kernel, flipped),
        out_shape=shape((rows, features), BF16),
        compiler_params=params(),
        cost_estimate=cost(),
        name="pack",
    )(*arrays)


def self_forward(heads, buckets, rows, gain, weights, ids):
    doc, features = rows.shape
    width, shares = heads * HEAD_DIM, len(weights)
    out_shape = (
        shape((shares, doc, 3 * width), BF16),
        shape((shares, doc, width), BF16),
        shape((shares, 8, doc), F32),
        shape((doc, features), F32),
    )
    return pl.pallas_call(
        functools.partial(self_forward_kernel, heads, buckets, shares),
        grid=(shares,),
        in_specs=[whole(rows), whole(gain), whole(ids), *anywhere(weights)],
        out_specs=(
            *[pl.BlockSpec((1, *o.shape[1:]), lambda i: (i, 0, 0)) for o in out_shape[:3]],
            whole(out_shape[3]),
        ),
        out_shape=out_shape,
        scratch_shapes=[
            pltpu.VMEM((shares, *weights[0].shape), BF16),
            pltpu.VMEM((doc, features), BF16),
            pltpu.SemaphoreType.DMA((shares,)),
        ],
        compiler_params=params(),
        cost_estimate=cost(),
        name="self_forward",
    )(rows, gain, ids, *weights)


def self_backward(heads, buckets, rows, gain, ids, branch, add, saved, weights):
    doc, features = rows.shape
    width, shares = heads * HEAD_DIM, len(weights)
    half = shares // 2
    packed = shape((half, 4 * width, features), BF16)
    out_shape = (
        packed,
        packed,
        shape((shares, heads, doc, doc), BF16),
        shape((doc, features), F32),
        shape((8, features), F32),
    )
    return pl.pallas_call(
        functools.partial(self_backward_kernel, heads, buckets, shares),
        grid=(shares,),
        in_specs=[
            whole(rows),
            whole(gain),
            whole(ids),
            whole(branch),
            whole(add),
            *[pl.BlockSpec((1, *s.shape[1:]), lambda i: (i, 0, 0)) for s in saved],
            *anywhere(weights),
        ],
        out_specs=(
            pl.BlockSpec((1, *packed.shape[1:]), lambda i: (jnp.minimum(i, half - 1), 0, 0)),
            pl.BlockSpec((1, *packed.shape[1:]), lambda i: (jnp.maximum(i - half, 0), 0, 0)),
            pl.BlockSpec((1, heads, doc, doc), lambda i: (i, 0, 0, 0)),
            whole(out_shape[3]),
            whole(out_shape[4]),
        ),
        out_shape=out_shape,
        scratch_shapes=[
            pltpu.VMEM((shares, *weights[0].shape), BF16),
            pltpu.VMEM((doc, features), BF16),
            pltpu.VMEM((doc, features), F32),
            pltpu.VMEM((doc, width), BF16),
            pltpu.VMEM((doc, 3 * width), BF16),
            pltpu.SemaphoreType.DMA((shares,)),
        ],
        compiler_params=params(),
        cost_estimate=cost(),
        name="self_backward",
    )(rows, gain, ids, branch, add, *saved, *weights)


def bucket_sums(ids, ds, buckets):
    shares, heads, doc, _ = ds.shape
    sums = pl.pallas_call(
        functools.partial(bucket_sum_kernel, heads, buckets),
        grid=(shares,),
        in_specs=[whole(ids), pl.BlockSpec((1, heads, doc, doc), lambda i: (i, 0, 0, 0))],
        out_specs=pl.BlockSpec((1, heads, buckets, LANES), lambda i: (i, 0, 0, 0)),
        out_shape=shape((shares, heads, buckets, LANES), F32),
        scratch_shapes=[pltpu.VMEM(ds.shape[1:], F32)],
        compiler_params=params(),
        cost_estimate=cost(),
        name="bucket_sums",
    )(ids, ds)
    return jnp.sum(sums, axis=3)


def cross_forward(heads, rows, gain, memory, mask, weights):
    (doc, features), slots = rows.shape, memory.shape[0]
    width, shares = heads * HEAD_DIM, len(weights)
    out_shape = (
        shape((shares, doc, width), BF16),
        shape((shares, slots, width), BF16),
        shape((shares, slots, width), BF16),
        shape((shares, doc, width), BF16),
        shape((shares, 8, doc), F32),
        shape((doc, features), F32),
    )
    key = pl.BlockSpec((1, K_BLOCK, width), lambda i, j: (i, j, 0))
    query = pl.BlockSpec((1, doc, width), lambda i, j: (i, 0, 0))
    return pl.pallas_call(
        functools.partial(cross_forward_kernel, heads, shares),
        grid=(shares, slots // K_BLOCK),
        in_specs=[
            whole(rows),
            whole(gain),
            pl.BlockSpec((K_BLOCK, features), lambda i, j: (j, 0)),
            pl.BlockSpec((K_BLOCK, Q_BLOCK), lambda i, j: (j, 0)),
            *anywhere(weights),
        ],
        out_specs=(
            query,
            key,
            key,
            query,
            pl.BlockSpec((1, 8, doc), lambda i, j: (i, 0, 0)),
            whole(out_shape[5]),
        ),
        out_shape=out_shape,
        scratch_shapes=[
            pltpu.VMEM((shares, *weights[0].shape), BF16),
            pltpu.VMEM((doc, features), BF16),
            pltpu.VMEM((width, doc), BF16),
            pltpu.VMEM((8, doc), F32),
            pltpu.VMEM((8, doc), F32),
            pltpu.VMEM((width, doc), F32),
            pltpu.SemaphoreType.DMA((shares,)),
        ],
        compiler_params=params(),
        cost_estimate=cost(),
        name="cross_forward",
    )(rows, gain, memory, mask, *weights)


def cross_backward(heads, rows, gain, memory, mask, branch, add, saved, weights):
    (doc, features), slots = rows.shape, memory.shape[0]
    width, shares = heads * HEAD_DIM, len(weights)
    half, steps = shares // 2, slots // K_BLOCK
    packed = shape((half, 4 * width, features), BF16)
    out_shape = (
        packed,
        packed,
        shape((slots, features), BF16),
        shape((doc, features), F32),
        shape((doc, features), BF16),
        shape((8, features), F32),
    )
    key = pl.BlockSpec((1, K_BLOCK, width), lambda i, j: (j, i, 0))
    block = pl.BlockSpec((K_BLOCK, features), lambda i, j: (i, 0))

    def give_index(i, j):
        return (jnp.where(i == steps - 1, jnp.minimum(j, half - 1), 0), 0, 0)

    def keep_index(i, j):
        return (jnp.where(i == steps - 1, jnp.maximum(j - half, 0), 0), 0, 0)

    query, _, _, mixed, lse = saved
    return pl.pallas_call(
        functools.partial(cross_backward_kernel, heads, shares),
        grid=(steps, shares),
        in_specs=[
            whole(rows),
            whole(gain),
            block,
            pl.BlockSpec((K_BLOCK, Q_BLOCK), lambda i, j: (i, 0)),
            whole(branch),
            whole(add),
            whole(query),
            key,
            key,
            whole(mixed),
            whole(lse),
            *anywhere(weights),
        ],
        out_specs=(
            pl.BlockSpec((1, *packed.shape[1:]), give_index),
            pl.BlockSpec((1, *packed.shape[1:]), keep_index),
            block,
            *[whole(o) for o in out_shape[3:]],
        ),
        out_shape=out_shape,
        scratch_shapes=[
            pltpu.VMEM((shares, *weights[0].shape), BF16),
            pltpu.VMEM((doc, features), BF16),
            pltpu.VMEM((doc, features), F32),
            pltpu.VMEM((K_BLOCK, features), F32),
            pltpu.VMEM((shares, doc, width), BF16),
            pltpu.VMEM((shares, width, doc), BF16),
            pltpu.VMEM((shares, width, doc), BF16),
            pltpu.VMEM((shares, 8, doc), F32),
            pltpu.VMEM((shares, width, doc), F32),
            pltpu.VMEM((doc, width), BF16),
            pltpu.VMEM((K_BLOCK, width), BF16),
            pltpu.VMEM((K_BLOCK, width), BF16),
            pltpu.VMEM((shares, width, features), F32),
            pltpu.VMEM((shares, width, features), F32),
            pltpu.SemaphoreType.DMA((shares,)),
        ],
        compiler_params=params(),
        cost_estimate=cost(),
        name="cross_backward",
    )(rows, gain, memory, mask, branch, add, *saved, *weights)


def feed_forward(rows, gain, cotangent, wide, narrow):
    (doc, features), hidden = rows.shape, wide[0].shape[0]
    shares = len(wide)
    half, steps = shares // 2, hidden // HIDDEN_BLOCK
    packed = shape((half, 2, hidden, features), BF16)
    out_shape = (
        packed,
        packed,
        shape((doc, features), BF16),
        shape((doc, features), F32),
        shape((doc, features), BF16),
        shape((8, features), F32),
    )

    def give_index(i, j):
        late = i >= half
        return (jnp.minimum(i, half - 1), 0, jnp.where(late, steps - 1, j), 0)

    def keep_index(i, j):
        return (jnp.maximum(i - half, 0), 0, jnp.where(i < half, 0, j), 0)

    return pl.pallas_call(
        functools.partial(feed_forward_kernel, shares),
        grid=(shares, steps),
        in_specs=[
            whole(rows),
            whole(gain),
            whole(cotangent),
            *anywhere(wide),
            *anywhere(narrow),
        ],
        out_specs=(
            pl.BlockSpec((1, 2, HIDDEN_BLOCK, features), give_index),
            pl.BlockSpec((1, 2, HIDDEN_BLOCK, features), keep_index),
            *[whole(o) for o in out_shape[2:]],
        ),
        out_shape=out_shape,
        scratch_shapes=[
            pltpu.VMEM((shares, hidden, features), BF16),
            pltpu.VMEM((shares, hidden, features), BF16),
            pltpu.VMEM((doc, features), BF16),
            pltpu.VMEM((doc, features), F32),
            pltpu.VMEM((doc, features), F32),
            pltpu.SemaphoreType.DMA((shares,)),
            pltpu.SemaphoreType.DMA((shares,)),
        ],
        compiler_params=params(),
        cost_estimate=cost(),
        name="feed_forward",
    )(rows, gain, cotangent, *wide, *narrow)


def swap(array, bit, size):
    return lax.ppermute(array, "mp", [(i, i ^ bit) for i in range(size)])


def add_low(a, b):
    return (a.astype(F32) + b.astype(F32)).astype(BF16)


def fold_rest(stack, size):
    shares, bit = {2 * i: stack[i] for i in range(stack.shape[0])}, 2
    while bit < size:
        shares = {
            j: add_low(shares[j], swap(shares[j | bit], bit, size)) for j in shares if not j & bit
        }
        bit *= 2
    return shares[0]


def shards(
    decoder_rows,
    memory_rows,
    decoder_token_length,
    memory_length,
    bucket_ids,
    relative_bucket_bias,
    self_gain,
    self_query,
    self_key,
    self_value,
    self_out,
    cross_gain,
    cross_query,
    cross_key,
    cross_value,
    cross_out,
    hidden_gain,
    widen_weight,
    narrow_weight,
    layer_cotangent,
):
    dp_size = lax.axis_size("dp")
    mp_size = lax.axis_size("mp")
    me = lax.axis_index("mp")
    doc, features = decoder_rows.shape
    slots = memory_rows.shape[0]
    cols = self_query.shape[1]
    heads = cols // HEAD_DIM
    buckets = relative_bucket_bias.shape[0]
    order = [*range(1, mp_size, 2), *range(0, mp_size, 2)]

    bias_rows = jnp.zeros((TABLE_ROWS, features), BF16)
    bias_rows = bias_rows.at[:heads, :buckets].set(relative_bucket_bias.T)
    own_self = pack(
        (self_query.T, False), (self_key.T, False), (self_value.T, False), (self_out, False), (bias_rows, False)
    )
    own_self, memory_rows = lax.optimization_barrier((own_self, memory_rows))
    own_cross = pack(
        (cross_query.T, False), (cross_key.T, False), (cross_value.T, False), (cross_out, False)
    )
    own_wide = pack((widen_weight, True))

    def first_hops(own):
        shares, bit = {0: own}, mp_size // 2
        while bit > 1:
            for j in list(shares):
                shares[j | bit] = swap(shares[j], bit, mp_size)
            bit //= 2
        return shares

    def last_hop(shares):
        for j in list(shares):
            shares[j | 1] = swap(shares[j], 1, mp_size)
        return [shares[j] for j in order]

    near_self = first_hops(own_self)
    w_self = last_hop(near_self)
    near_cross = first_hops(own_cross)
    near_wide = first_hops(own_wide)
    near_narrow = first_hops(narrow_weight)
    memory_seen = lax.all_to_all(
        memory_rows.reshape(dp_size, slots // dp_size, features), "dp", 0, 0
    ).reshape(slots, features)

    doc_length = lax.dynamic_index_in_dim(decoder_token_length, me, keepdims=False)
    doc_memory = lax.dynamic_index_in_dim(memory_length, me, keepdims=False)
    position = jnp.arange(doc, dtype=jnp.int32)
    allowed = (position[:, None] <= position[None, :]) & (position[:, None] < doc_length)
    ids = jnp.where(allowed, bucket_ids.T, buckets)
    mask = jnp.where(jnp.arange(slots, dtype=jnp.int32) < doc_memory, 0.0, MASKED)
    mask = jnp.broadcast_to(mask[:, None].astype(F32), (slots, Q_BLOCK))

    gain_self = self_gain.astype(F32)[None]
    gain_cross = cross_gain.astype(F32)[None]
    gain_hidden = hidden_gain.astype(F32)[None]

    *saved_self, after_self = self_forward(heads, buckets, decoder_rows, gain_self, w_self, ids)
    near_cross, after_self = lax.optimization_barrier((near_cross, after_self))
    w_cross = last_hop(near_cross)
    *saved_cross, after_cross = cross_forward(
        heads, after_self, gain_cross, memory_seen, mask, w_cross
    )

    near_wide, near_narrow, after_cross = lax.optimization_barrier(
        (near_wide, near_narrow, after_cross)
    )
    w_wide, w_narrow = last_hop(near_wide), last_hop(near_narrow)
    give, keep, layer_output, grad_after_cross, branch, hidden_gain_grad = feed_forward(
        after_cross, gain_hidden, layer_cotangent, w_wide, w_narrow
    )
    part_hidden = add_low(keep, swap(give, 1, mp_size))
    branch, part_hidden = lax.optimization_barrier((branch, part_hidden))

    give, keep, grad_memory, grad_after_self, branch, cross_gain_grad = cross_backward(
        heads,
        after_self,
        gain_cross,
        memory_seen,
        mask,
        branch,
        grad_after_cross,
        saved_cross,
        w_cross,
    )
    memory_grad = lax.all_to_all(
        grad_memory.reshape(dp_size, slots // dp_size, features), "dp", 0, 0
    ).reshape(slots, features)
    part_hidden = fold_rest(part_hidden, mp_size)
    branch, part_hidden = lax.optimization_barrier((branch, part_hidden))
    sum_hidden = lax.psum(part_hidden, "dp")
    part_cross = add_low(keep, swap(give, 1, mp_size))

    give, keep, score_grads, input_grad, self_gain_grad = self_backward(
        heads,
        buckets,
        decoder_rows,
        gain_self,
        ids,
        branch,
        grad_after_self,
        saved_self,
        w_self,
    )
    part_self = add_low(keep, swap(give, 1, mp_size))
    part_cross = fold_rest(part_cross, mp_size)
    part_self = fold_rest(part_self, mp_size)
    part_cross, part_self, sum_hidden = lax.optimization_barrier(
        (part_cross, part_self, sum_hidden)
    )
    sum_cross, sum_self = lax.psum((part_cross, part_self), "dp")

    sums = bucket_sums(ids, score_grads, buckets)
    back_to = [order.index(j) for j in range(mp_size)]
    sums = jnp.stack([sums[i] for i in back_to])
    sums = jnp.take(sums, me ^ jnp.arange(mp_size), axis=0)
    gains = jnp.stack([self_gain_grad, cross_gain_grad, hidden_gain_grad]).sum(axis=1)
    small = lax.psum(jnp.concatenate([gains.reshape(-1), sums.reshape(-1)]), ("dp", "mp"))
    gains = small[: 3 * features].reshape(3, features)
    sums = small[3 * features :].reshape(mp_size, heads, buckets)
    position_grad = lax.dynamic_index_in_dim(sums, me, keepdims=False).T

    sum_self = sum_self.astype(F32)
    sum_cross = sum_cross.astype(F32)
    sum_hidden = sum_hidden.astype(F32)
    return (
        layer_output,
        input_grad,
        memory_grad,
        position_grad,
        gains[0],
        sum_self[:cols].T,
        sum_self[cols : 2 * cols].T,
        sum_self[2 * cols : 3 * cols].T,
        sum_self[3 * cols :],
        gains[1],
        sum_cross[:cols].T,
        sum_cross[cols : 2 * cols].T,
        sum_cross[2 * cols : 3 * cols].T,
        sum_cross[3 * cols :],
        gains[2],
        sum_hidden[0].T,
        sum_hidden[1],
    )


def solution(mesh):
    return jax.shard_map(
        shards,
        mesh=mesh,
        in_specs=(
            P(("dp", "mp"), None),
            P(("dp", "mp"), None),
            P("dp"),
            P("dp"),
            P(),
            P(None, "mp"),
            P(),
            P(None, "mp"),
            P(None, "mp"),
            P(None, "mp"),
            P("mp", None),
            P(),
            P(None, "mp"),
            P(None, "mp"),
            P(None, "mp"),
            P("mp", None),
            P(),
            P(None, "mp"),
            P("mp", None),
            P(("dp", "mp"), None),
        ),
        out_specs=(
            P(("dp", "mp"), None),
            P(("dp", "mp"), None),
            P(("dp", "mp"), None),
            P(None, "mp"),
            P(),
            P(None, "mp"),
            P(None, "mp"),
            P(None, "mp"),
            P("mp", None),
            P(),
            P(None, "mp"),
            P(None, "mp"),
            P(None, "mp"),
            P("mp", None),
            P(),
            P(None, "mp"),
            P("mp", None),
        ),
        check_vma=False,
    )
```

```python
import functools

import jax
import jax.numpy as jnp
from jax import lax
from jax.experimental import pallas as pl
from jax.experimental.pallas import tpu as pltpu
from jax.sharding import PartitionSpec as P

HEAD_DIM = 64
NORM_EPS = 1e-06
MASKED = -1e30
SCALE = HEAD_DIM**-0.5
BF16 = jnp.bfloat16
F32 = jnp.float32
LANES = 128
TABLE_ROWS = 16
Q_BLOCK = 256
K_BLOCK = 512
HIDDEN_BLOCK = 256
ROW_BLOCK = 128
VMEM_BYTES = 56 * 1024 * 1024
GELU_ROOT = 0.7978845608028654
GELU_CUBE = 0.044715


def dot_nn(a, b):
    return lax.dot_general(a, b, (((1,), (0,)), ((), ())), preferred_element_type=F32)


def dot_nt(a, b):
    return lax.dot_general(a, b, (((1,), (1,)), ((), ())), preferred_element_type=F32)


def dot_tn(a, b):
    return lax.dot_general(a, b, (((0,), (0,)), ((), ())), preferred_element_type=F32)


def flip(a):
    return a.astype(F32).T.astype(BF16)


def head(h):
    return slice(h * HEAD_DIM, (h + 1) * HEAD_DIM)


def row_blocks(ref):
    return [slice(i, i + ROW_BLOCK) for i in range(0, ref.shape[0], ROW_BLOCK)]


def norm_scale(rows):
    return lax.rsqrt(jnp.mean(rows * rows, axis=-1, keepdims=True) + NORM_EPS)


def norm_into(normed_ref, rows_ref, gain_ref):
    for span in row_blocks(rows_ref):
        rows = rows_ref[span].astype(F32)
        normed_ref[span] = (rows * norm_scale(rows) * gain_ref[...]).astype(BF16)


def norm_back_into(out_ref, low_ref, gain_grad_ref, rows_ref, gain_ref, grad_ref, add_ref):
    gain_grad_ref[...] = jnp.zeros_like(gain_grad_ref)
    for span in row_blocks(rows_ref):
        rows, grad = rows_ref[span].astype(F32), grad_ref[span]
        scale = norm_scale(rows)
        unit = rows * scale
        grad_unit = grad * gain_ref[...]
        mean = jnp.mean(grad_unit * unit, axis=-1, keepdims=True)
        out = add_ref[span].astype(F32) + scale * (grad_unit - unit * mean)
        out_ref[span] = out
        if low_ref is not None:
            low_ref[span] = out.astype(BF16)
        gain_grad_ref[...] += jnp.sum((grad * unit).reshape(-1, 8, rows.shape[1]), axis=0)


def gelu_and_slope(v):
    square = v * v
    bend = jnp.tanh(GELU_ROOT * (v + GELU_CUBE * v * square))
    half = 0.5 * (1.0 + bend)
    slope = half + 0.5 * v * (1.0 - bend * bend) * GELU_ROOT * (1.0 + 3.0 * GELU_CUBE * square)
    return v * half, slope


def bias_block(table, ids_ref, h, rows, start):
    row = jnp.broadcast_to(table[h : h + 1, :], (rows, LANES))
    return jnp.concatenate(
        [
            jnp.take_along_axis(row, ids_ref[:rows, c : c + LANES], axis=1)
            for c in range(start, start + Q_BLOCK, LANES)
        ],
        axis=1,
    )


def bias_table(weights, buckets):
    table = weights[-TABLE_ROWS:, :LANES].astype(F32)
    lane = lax.broadcasted_iota(jnp.int32, table.shape, 1)
    return jnp.where(lane < buckets, table, MASKED)


def fetch(first, share, sources, stack, sems):
    @pl.when(first & (share == 0))
    def _():
        for p, source in enumerate(sources):
            pltpu.make_async_copy(source, stack.at[p], sems.at[p]).start()

    for p, source in enumerate(sources):

        @pl.when(first & (share == p))
        def _(p=p, source=source):
            pltpu.make_async_copy(source, stack.at[p], sems.at[p]).wait()


def store_share(share, half, give_ref, keep_ref, rows, value):
    value = value.astype(BF16)

    @pl.when(share < half)
    def _():
        give_ref[0, rows] = value

    @pl.when(share >= half)
    def _():
        keep_ref[0, rows] = value


def self_forward_kernel(heads, buckets, shares, rows_ref, gain_ref, ids_ref, *refs):
    sources, (qkv_ref, mixed_ref, lse_ref, out_ref, w_ref, normed_ref, sems) = (
        refs[:shares],
        refs[shares:],
    )
    share = pl.program_id(0)
    width = heads * HEAD_DIM
    doc = rows_ref.shape[0]
    fetch(True, share, sources, w_ref, sems)

    @pl.when(share == 0)
    def _():
        norm_into(normed_ref, rows_ref, gain_ref)
        out_ref[...] = rows_ref[...].astype(F32)

    weights = w_ref.at[share]
    qkv_ref[0] = dot_nt(normed_ref[...], weights[: 3 * width]).astype(BF16)
    table = bias_table(weights, buckets)
    for h in range(heads):
        cols = head(h)
        k = qkv_ref[0, :, width + cols.start : width + cols.stop]
        q_t = flip(qkv_ref[0, :, cols].astype(F32) * SCALE)
        v_t = flip(qkv_ref[0, :, 2 * width + cols.start : 2 * width + cols.stop])
        for start in range(0, doc, Q_BLOCK):
            rows = start + Q_BLOCK
            span = slice(start, rows)
            s = dot_nn(k[:rows], q_t[:, span]) + bias_block(table, ids_ref, h, rows, start)
            top = jnp.max(s, axis=0, keepdims=True)
            p = jnp.exp(s - top)
            total = jnp.sum(p, axis=0, keepdims=True)
            mixed_t = dot_nn(v_t[:, :rows], p.astype(BF16)) / total
            mixed_ref[0, span, cols] = mixed_t.T.astype(BF16)
            lse_ref[0, h : h + 1, span] = top + jnp.log(total)
    out_ref[...] += dot_nn(mixed_ref[0], weights[3 * width : 4 * width])


def self_backward_kernel(heads, buckets, shares, *refs):
    rows_ref, gain_ref, ids_ref, branch_ref, add_ref, qkv_ref, mixed_ref, lse_ref = refs[:8]
    sources = refs[8 : 8 + shares]
    give_ref, keep_ref, ds_ref, out_ref, gain_grad_ref = refs[8 + shares : 13 + shares]
    w_ref, normed_ref, back_ref, g_ref, grad_ref, sems = refs[13 + shares :]
    share, half = pl.program_id(0), shares // 2
    width = heads * HEAD_DIM
    doc = rows_ref.shape[0]
    fetch(True, share, sources, w_ref, sems)

    @pl.when(share == 0)
    def _():
        norm_into(normed_ref, rows_ref, gain_ref)
        back_ref[...] = jnp.zeros_like(back_ref)

    weights = w_ref.at[share]
    w_out = slice(3 * width, 4 * width)
    table = bias_table(weights, buckets)
    g_ref[...] = dot_nt(branch_ref[...], weights[w_out]).astype(BF16)
    for h in range(heads):
        cols = head(h)
        k_cols = slice(width + cols.start, width + cols.stop)
        v_cols = slice(2 * width + cols.start, 2 * width + cols.stop)
        q = qkv_ref[0, :, cols]
        k = qkv_ref[0, :, k_cols]
        v = qkv_ref[0, :, v_cols]
        g = g_ref[:, cols]
        q_t = flip(q.astype(F32) * SCALE)
        k_t = flip(k)
        g_t = g.astype(F32).T
        inner = jnp.sum(g_t * mixed_ref[0, :, cols].astype(F32).T, axis=0, keepdims=True)
        g_t = g_t.astype(BF16)
        grad_k = grad_v = None
        for start in range(0, doc, Q_BLOCK):
            rows = start + Q_BLOCK
            span = slice(start, rows)
            s = dot_nn(k[:rows], q_t[:, span]) + bias_block(table, ids_ref, h, rows, start)
            p = jnp.exp(s - lse_ref[0, h : h + 1, span])
            grad_p = dot_nn(v[:rows], g_t[:, span])
            ds = (p * (grad_p - inner[:, span])).astype(BF16)
            ds_ref[0, h, :rows, span] = ds
            grad_q = dot_nn(k_t[:, :rows], ds) * SCALE
            grad_ref[span, cols] = grad_q.T.astype(BF16)
            part_v = dot_nn(p.astype(BF16), g[span])
            part_k = dot_nn(ds, q[span])
            if grad_v is not None:
                part_v = jnp.concatenate([part_v[:start] + grad_v, part_v[start:]], axis=0)
                part_k = jnp.concatenate([part_k[:start] + grad_k, part_k[start:]], axis=0)
            grad_v, grad_k = part_v, part_k
        grad_ref[:, k_cols] = (grad_k * SCALE).astype(BF16)
        grad_ref[:, v_cols] = grad_v.astype(BF16)
    store_share(
        share,
        half,
        give_ref,
        keep_ref,
        slice(0, 3 * width),
        dot_tn(grad_ref[...], normed_ref[...]),
    )
    store_share(
        share, half, give_ref, keep_ref, w_out, dot_tn(mixed_ref[0], branch_ref[...])
    )
    back_ref[...] += dot_nn(grad_ref[...], weights[: 3 * width])

    @pl.when(share == shares - 1)
    def _():
        norm_back_into(out_ref, None, gain_grad_ref, rows_ref, gain_ref, back_ref, add_ref)


def bucket_sum_kernel(heads, buckets, ids_ref, ds_ref, out_ref, wide_ref):
    doc = ids_ref.shape[0]
    wide_ref[...] = ds_ref[0].astype(F32)

    def one_bucket(b, carry):
        sums = [jnp.zeros((8, LANES), F32) for _ in range(heads)]
        for c in range(0, doc, LANES):
            rows = c + LANES
            hit = ids_ref[:rows, c : c + LANES] == b
            for h in range(heads):
                kept = jnp.where(hit, wide_ref[h, :rows, c : c + LANES], 0.0)
                sums[h] = sums[h] + jnp.sum(kept.reshape(rows // 8, 8, LANES), axis=0)
        for h in range(heads):
            out_ref[0, h, pl.ds(b, 1), :] = jnp.sum(sums[h], axis=0, keepdims=True)
        return carry

    lax.fori_loop(0, buckets, one_bucket, 0)


def cross_forward_kernel(heads, shares, rows_ref, gain_ref, memory_ref, mask_ref, *refs):
    sources = refs[:shares]
    q_ref, k_ref, v_ref, mixed_ref, lse_ref, out_ref = refs[shares : shares + 6]
    w_ref, normed_ref, q_t, top_ref, sum_ref, mix_t, sems = refs[shares + 6 :]
    share, step = pl.program_id(0), pl.program_id(1)
    width = heads * HEAD_DIM
    doc = rows_ref.shape[0]
    fetch(step == 0, share, sources, w_ref, sems)
    weights = w_ref.at[share]

    @pl.when((share == 0) & (step == 0))
    def _():
        norm_into(normed_ref, rows_ref, gain_ref)
        out_ref[...] = rows_ref[...]

    @pl.when(step == 0)
    def _():
        q_ref[0] = dot_nt(normed_ref[...], weights[:width]).astype(BF16)
        for h in range(heads):
            q_t[head(h), :] = flip(q_ref[0, :, head(h)].astype(F32) * SCALE)
        top_ref[...] = jnp.full_like(top_ref, MASKED)
        sum_ref[...] = jnp.zeros_like(sum_ref)
        mix_t[...] = jnp.zeros_like(mix_t)

    k_ref[0] = dot_nt(memory_ref[...], weights[width : 2 * width]).astype(BF16)
    v_ref[0] = dot_nt(memory_ref[...], weights[2 * width : 3 * width]).astype(BF16)
    for h in range(heads):
        k = k_ref[0, :, head(h)]
        v_t = flip(v_ref[0, :, head(h)])
        for start in range(0, doc, Q_BLOCK):
            span = slice(start, start + Q_BLOCK)
            s = dot_nn(k, q_t[head(h), span]) + mask_ref[...]
            old = top_ref[h : h + 1, span]
            top = jnp.maximum(old, jnp.max(s, axis=0, keepdims=True))
            p = jnp.exp(s - top)
            decay = jnp.exp(old - top)
            top_ref[h : h + 1, span] = top
            sum_ref[h : h + 1, span] = sum_ref[h : h + 1, span] * decay + jnp.sum(
                p, axis=0, keepdims=True
            )
            mix_t[head(h), span] = mix_t[head(h), span] * decay + dot_nn(v_t, p.astype(BF16))

    @pl.when(step == pl.num_programs(1) - 1)
    def _():
        for h in range(heads):
            mixed = mix_t[head(h), :] / sum_ref[h : h + 1, :]
            mixed_ref[0, :, head(h)] = mixed.T.astype(BF16)
        lse_ref[0] = top_ref[...] + jnp.log(sum_ref[...])
        out_ref[...] += dot_nn(mixed_ref[0], weights[3 * width : 4 * width])


def cross_backward_kernel(heads, shares, *refs):
    rows_ref, gain_ref, memory_ref, mask_ref, branch_ref, add_ref = refs[:6]
    q_ref, k_ref, v_ref, mixed_ref, lse_ref = refs[6:11]
    sources = refs[11 : 11 + shares]
    give_ref, keep_ref, memory_out_ref, out_ref, low_ref, gain_grad_ref = refs[
        11 + shares : 17 + shares
    ]
    (
        w_ref,
        normed_ref,
        back_ref,
        memory_acc,
        g_ref,
        q_t,
        g_t,
        inner_ref,
        grad_q_t,
        grad_q_ref,
        grad_k_ref,
        grad_v_ref,
        sum_k_ref,
        sum_v_ref,
        sems,
    ) = refs[17 + shares :]
    step, share, half = pl.program_id(0), pl.program_id(1), shares // 2
    last = pl.num_programs(0) - 1
    width = heads * HEAD_DIM
    doc = rows_ref.shape[0]
    w_out = slice(3 * width, 4 * width)
    fetch(step == 0, share, sources, w_ref, sems)
    weights = w_ref.at[share]

    @pl.when((step == 0) & (share == 0))
    def _():
        norm_into(normed_ref, rows_ref, gain_ref)
        back_ref[...] = jnp.zeros_like(back_ref)

    @pl.when(step == 0)
    def _():
        g_ref[share] = dot_nt(branch_ref[...], weights[w_out]).astype(BF16)
        for h in range(heads):
            q_t[share, head(h), :] = flip(q_ref[share, :, head(h)].astype(F32) * SCALE)
            wide = g_ref[share, :, head(h)].astype(F32).T
            g_t[share, head(h), :] = wide.astype(BF16)
            inner_ref[share, h : h + 1, :] = jnp.sum(
                wide * mixed_ref[share, :, head(h)].astype(F32).T, axis=0, keepdims=True
            )
        grad_q_t[share] = jnp.zeros(grad_q_t.shape[1:], F32)
        sum_k_ref[share] = jnp.zeros(sum_k_ref.shape[1:], F32)
        sum_v_ref[share] = jnp.zeros(sum_v_ref.shape[1:], F32)

    @pl.when(share == 0)
    def _():
        memory_acc[...] = jnp.zeros_like(memory_acc)

    for h in range(heads):
        k = k_ref[0, :, head(h)]
        v = v_ref[0, :, head(h)]
        k_t = flip(k)
        grad_k = grad_v = None
        for start in range(0, doc, Q_BLOCK):
            span = slice(start, start + Q_BLOCK)
            s = dot_nn(k, q_t[share, head(h), span]) + mask_ref[...]
            p = jnp.exp(s - lse_ref[share, h : h + 1, span])
            grad_p = dot_nn(v, g_t[share, head(h), span])
            ds = (p * (grad_p - inner_ref[share, h : h + 1, span])).astype(BF16)
            part_v = dot_nn(p.astype(BF16), g_ref[share, span, head(h)])
            part_k = dot_nn(ds, q_ref[share, span, head(h)])
            grad_q_t[share, head(h), span] += dot_nn(k_t, ds)
            grad_v = part_v if grad_v is None else grad_v + part_v
            grad_k = part_k if grad_k is None else grad_k + part_k
        grad_k_ref[:, head(h)] = (grad_k * SCALE).astype(BF16)
        grad_v_ref[:, head(h)] = grad_v.astype(BF16)
    memory = memory_ref[...]
    sum_k_ref[share] += dot_tn(grad_k_ref[...], memory)
    sum_v_ref[share] += dot_tn(grad_v_ref[...], memory)
    memory_acc[...] += dot_nn(grad_k_ref[...], weights[width : 2 * width]) + dot_nn(
        grad_v_ref[...], weights[2 * width : 3 * width]
    )

    @pl.when(share == shares - 1)
    def _():
        memory_out_ref[...] = memory_acc[...].astype(BF16)

    @pl.when(step == last)
    def _():
        for h in range(heads):
            grad_q_ref[:, head(h)] = (grad_q_t[share, head(h), :] * SCALE).T.astype(BF16)
        parts = (
            (slice(0, width), dot_tn(grad_q_ref[...], normed_ref[...])),
            (slice(width, 2 * width), sum_k_ref[share]),
            (slice(2 * width, 3 * width), sum_v_ref[share]),
            (w_out, dot_tn(mixed_ref[share], branch_ref[...])),
        )
        for rows, value in parts:
            store_share(share, half, give_ref, keep_ref, rows, value)
        back_ref[...] += dot_nn(grad_q_ref[...], weights[:width])

    @pl.when((step == last) & (share == shares - 1))
    def _():
        norm_back_into(out_ref, low_ref, gain_grad_ref, rows_ref, gain_ref, back_ref, add_ref)


def feed_forward_kernel(shares, rows_ref, gain_ref, cotangent_ref, *refs):
    wide_sources, narrow_sources = refs[:shares], refs[shares : 2 * shares]
    give_ref, keep_ref, layer_ref, out_ref, low_ref, gain_grad_ref = refs[
        2 * shares : 2 * shares + 6
    ]
    wide_ref, narrow_ref, normed_ref, acc_ref, back_ref, wide_sems, narrow_sems = refs[
        2 * shares + 6 :
    ]
    share, step, half = pl.program_id(0), pl.program_id(1), shares // 2
    fetch(step == 0, share, wide_sources, wide_ref, wide_sems)
    fetch(step == 0, share, narrow_sources, narrow_ref, narrow_sems)

    @pl.when((share == 0) & (step == 0))
    def _():
        norm_into(normed_ref, rows_ref, gain_ref)
        acc_ref[...] = rows_ref[...]
        back_ref[...] = jnp.zeros_like(back_ref)

    normed, cotangent = normed_ref[...], cotangent_ref[...]
    hidden = pl.ds(pl.multiple_of(step * HIDDEN_BLOCK, HIDDEN_BLOCK), HIDDEN_BLOCK)
    wide, narrow = wide_ref[share, hidden], narrow_ref[share, hidden]
    activated, slope = gelu_and_slope(dot_nt(normed, wide))
    activated = activated.astype(BF16)
    acc_ref[...] += dot_nn(activated, narrow)
    store_share(share, half, give_ref, keep_ref, 1, dot_tn(activated, cotangent))
    grad_widened = (dot_nt(cotangent, narrow) * slope).astype(BF16)
    back_ref[...] += dot_nn(grad_widened, wide)
    store_share(share, half, give_ref, keep_ref, 0, dot_tn(grad_widened, normed))

    @pl.when((share == shares - 1) & (step == pl.num_programs(1) - 1))
    def _():
        layer_ref[...] = acc_ref[...].astype(BF16)
        norm_back_into(
            out_ref, low_ref, gain_grad_ref, rows_ref, gain_ref, back_ref, cotangent_ref
        )


def params():
    return pltpu.CompilerParams(vmem_limit_bytes=VMEM_BYTES)


def cost():
    return pl.CostEstimate(flops=1 << 20, bytes_accessed=1 << 16, transcendentals=0)


def shape(dims, dtype):
    return jax.ShapeDtypeStruct(dims, dtype)


def whole(array):
    return pl.BlockSpec(array.shape, lambda *_: (0,) * len(array.shape))


def anywhere(arrays):
    return [pl.BlockSpec(memory_space=pl.ANY) for _ in arrays]


def pack_kernel(flipped, *refs):
    out_ref, start = refs[-1], 0
    for source, turn in zip(refs[:-1], flipped):
        rows = source.shape[1] if turn else source.shape[0]
        span = slice(start, start + rows)
        out_ref[span] = flip(source[...]) if turn else source[...]
        start += rows


def pack(*parts):
    arrays, flipped = zip(*parts)
    rows = sum(a.shape[1] if turn else a.shape[0] for a, turn in parts)
    features = arrays[0].shape[0] if flipped[0] else arrays[0].shape[1]
    return pl.pallas_call(
        functools.partial(pack_kernel, flipped),
        out_shape=shape((rows, features), BF16),
        compiler_params=params(),
        cost_estimate=cost(),
        name="pack",
    )(*arrays)


def self_forward(heads, buckets, rows, gain, weights, ids):
    doc, features = rows.shape
    width, shares = heads * HEAD_DIM, len(weights)
    out_shape = (
        shape((shares, doc, 3 * width), BF16),
        shape((shares, doc, width), BF16),
        shape((shares, 8, doc), F32),
        shape((doc, features), F32),
    )
    return pl.pallas_call(
        functools.partial(self_forward_kernel, heads, buckets, shares),
        grid=(shares,),
        in_specs=[whole(rows), whole(gain), whole(ids), *anywhere(weights)],
        out_specs=(
            *[pl.BlockSpec((1, *o.shape[1:]), lambda i: (i, 0, 0)) for o in out_shape[:3]],
            whole(out_shape[3]),
        ),
        out_shape=out_shape,
        scratch_shapes=[
            pltpu.VMEM((shares, *weights[0].shape), BF16),
            pltpu.VMEM((doc, features), BF16),
            pltpu.SemaphoreType.DMA((shares,)),
        ],
        compiler_params=params(),
        cost_estimate=cost(),
        name="self_forward",
    )(rows, gain, ids, *weights)


def self_backward(heads, buckets, rows, gain, ids, branch, add, saved, weights):
    doc, features = rows.shape
    width, shares = heads * HEAD_DIM, len(weights)
    half = shares // 2
    packed = shape((half, 4 * width, features), BF16)
    out_shape = (
        packed,
        packed,
        shape((shares, heads, doc, doc), BF16),
        shape((doc, features), F32),
        shape((8, features), F32),
    )
    return pl.pallas_call(
        functools.partial(self_backward_kernel, heads, buckets, shares),
        grid=(shares,),
        in_specs=[
            whole(rows),
            whole(gain),
            whole(ids),
            whole(branch),
            whole(add),
            *[pl.BlockSpec((1, *s.shape[1:]), lambda i: (i, 0, 0)) for s in saved],
            *anywhere(weights),
        ],
        out_specs=(
            pl.BlockSpec((1, *packed.shape[1:]), lambda i: (jnp.minimum(i, half - 1), 0, 0)),
            pl.BlockSpec((1, *packed.shape[1:]), lambda i: (jnp.maximum(i - half, 0), 0, 0)),
            pl.BlockSpec((1, heads, doc, doc), lambda i: (i, 0, 0, 0)),
            whole(out_shape[3]),
            whole(out_shape[4]),
        ),
        out_shape=out_shape,
        scratch_shapes=[
            pltpu.VMEM((shares, *weights[0].shape), BF16),
            pltpu.VMEM((doc, features), BF16),
            pltpu.VMEM((doc, features), F32),
            pltpu.VMEM((doc, width), BF16),
            pltpu.VMEM((doc, 3 * width), BF16),
            pltpu.SemaphoreType.DMA((shares,)),
        ],
        compiler_params=params(),
        cost_estimate=cost(),
        name="self_backward",
    )(rows, gain, ids, branch, add, *saved, *weights)


def bucket_sums(ids, ds, buckets):
    shares, heads, doc, _ = ds.shape
    sums = pl.pallas_call(
        functools.partial(bucket_sum_kernel, heads, buckets),
        grid=(shares,),
        in_specs=[whole(ids), pl.BlockSpec((1, heads, doc, doc), lambda i: (i, 0, 0, 0))],
        out_specs=pl.BlockSpec((1, heads, buckets, LANES), lambda i: (i, 0, 0, 0)),
        out_shape=shape((shares, heads, buckets, LANES), F32),
        scratch_shapes=[pltpu.VMEM(ds.shape[1:], F32)],
        compiler_params=params(),
        cost_estimate=cost(),
        name="bucket_sums",
    )(ids, ds)
    return jnp.sum(sums, axis=3)


def cross_forward(heads, rows, gain, memory, mask, weights):
    (doc, features), slots = rows.shape, memory.shape[0]
    width, shares = heads * HEAD_DIM, len(weights)
    out_shape = (
        shape((shares, doc, width), BF16),
        shape((shares, slots, width), BF16),
        shape((shares, slots, width), BF16),
        shape((shares, doc, width), BF16),
        shape((shares, 8, doc), F32),
        shape((doc, features), F32),
    )
    key = pl.BlockSpec((1, K_BLOCK, width), lambda i, j: (i, j, 0))
    query = pl.BlockSpec((1, doc, width), lambda i, j: (i, 0, 0))
    return pl.pallas_call(
        functools.partial(cross_forward_kernel, heads, shares),
        grid=(shares, slots // K_BLOCK),
        in_specs=[
            whole(rows),
            whole(gain),
            pl.BlockSpec((K_BLOCK, features), lambda i, j: (j, 0)),
            pl.BlockSpec((K_BLOCK, Q_BLOCK), lambda i, j: (j, 0)),
            *anywhere(weights),
        ],
        out_specs=(
            query,
            key,
            key,
            query,
            pl.BlockSpec((1, 8, doc), lambda i, j: (i, 0, 0)),
            whole(out_shape[5]),
        ),
        out_shape=out_shape,
        scratch_shapes=[
            pltpu.VMEM((shares, *weights[0].shape), BF16),
            pltpu.VMEM((doc, features), BF16),
            pltpu.VMEM((width, doc), BF16),
            pltpu.VMEM((8, doc), F32),
            pltpu.VMEM((8, doc), F32),
            pltpu.VMEM((width, doc), F32),
            pltpu.SemaphoreType.DMA((shares,)),
        ],
        compiler_params=params(),
        cost_estimate=cost(),
        name="cross_forward",
    )(rows, gain, memory, mask, *weights)


def cross_backward(heads, rows, gain, memory, mask, branch, add, saved, weights):
    (doc, features), slots = rows.shape, memory.shape[0]
    width, shares = heads * HEAD_DIM, len(weights)
    half, steps = shares // 2, slots // K_BLOCK
    packed = shape((half, 4 * width, features), BF16)
    out_shape = (
        packed,
        packed,
        shape((slots, features), BF16),
        shape((doc, features), F32),
        shape((doc, features), BF16),
        shape((8, features), F32),
    )
    key = pl.BlockSpec((1, K_BLOCK, width), lambda i, j: (j, i, 0))
    block = pl.BlockSpec((K_BLOCK, features), lambda i, j: (i, 0))

    def give_index(i, j):
        return (jnp.where(i == steps - 1, jnp.minimum(j, half - 1), 0), 0, 0)

    def keep_index(i, j):
        return (jnp.where(i == steps - 1, jnp.maximum(j - half, 0), 0), 0, 0)

    query, _, _, mixed, lse = saved
    return pl.pallas_call(
        functools.partial(cross_backward_kernel, heads, shares),
        grid=(steps, shares),
        in_specs=[
            whole(rows),
            whole(gain),
            block,
            pl.BlockSpec((K_BLOCK, Q_BLOCK), lambda i, j: (i, 0)),
            whole(branch),
            whole(add),
            whole(query),
            key,
            key,
            whole(mixed),
            whole(lse),
            *anywhere(weights),
        ],
        out_specs=(
            pl.BlockSpec((1, *packed.shape[1:]), give_index),
            pl.BlockSpec((1, *packed.shape[1:]), keep_index),
            block,
            *[whole(o) for o in out_shape[3:]],
        ),
        out_shape=out_shape,
        scratch_shapes=[
            pltpu.VMEM((shares, *weights[0].shape), BF16),
            pltpu.VMEM((doc, features), BF16),
            pltpu.VMEM((doc, features), F32),
            pltpu.VMEM((K_BLOCK, features), F32),
            pltpu.VMEM((shares, doc, width), BF16),
            pltpu.VMEM((shares, width, doc), BF16),
            pltpu.VMEM((shares, width, doc), BF16),
            pltpu.VMEM((shares, 8, doc), F32),
            pltpu.VMEM((shares, width, doc), F32),
            pltpu.VMEM((doc, width), BF16),
            pltpu.VMEM((K_BLOCK, width), BF16),
            pltpu.VMEM((K_BLOCK, width), BF16),
            pltpu.VMEM((shares, width, features), F32),
            pltpu.VMEM((shares, width, features), F32),
            pltpu.SemaphoreType.DMA((shares,)),
        ],
        compiler_params=params(),
        cost_estimate=cost(),
        name="cross_backward",
    )(rows, gain, memory, mask, branch, add, *saved, *weights)


def feed_forward(rows, gain, cotangent, wide, narrow):
    (doc, features), hidden = rows.shape, wide[0].shape[0]
    shares = len(wide)
    half, steps = shares // 2, hidden // HIDDEN_BLOCK
    packed = shape((half, 2, hidden, features), BF16)
    out_shape = (
        packed,
        packed,
        shape((doc, features), BF16),
        shape((doc, features), F32),
        shape((doc, features), BF16),
        shape((8, features), F32),
    )

    def give_index(i, j):
        late = i >= half
        return (jnp.minimum(i, half - 1), 0, jnp.where(late, steps - 1, j), 0)

    def keep_index(i, j):
        return (jnp.maximum(i - half, 0), 0, jnp.where(i < half, 0, j), 0)

    return pl.pallas_call(
        functools.partial(feed_forward_kernel, shares),
        grid=(shares, steps),
        in_specs=[
            whole(rows),
            whole(gain),
            whole(cotangent),
            *anywhere(wide),
            *anywhere(narrow),
        ],
        out_specs=(
            pl.BlockSpec((1, 2, HIDDEN_BLOCK, features), give_index),
            pl.BlockSpec((1, 2, HIDDEN_BLOCK, features), keep_index),
            *[whole(o) for o in out_shape[2:]],
        ),
        out_shape=out_shape,
        scratch_shapes=[
            pltpu.VMEM((shares, hidden, features), BF16),
            pltpu.VMEM((shares, hidden, features), BF16),
            pltpu.VMEM((doc, features), BF16),
            pltpu.VMEM((doc, features), F32),
            pltpu.VMEM((doc, features), F32),
            pltpu.SemaphoreType.DMA((shares,)),
            pltpu.SemaphoreType.DMA((shares,)),
        ],
        compiler_params=params(),
        cost_estimate=cost(),
        name="feed_forward",
    )(rows, gain, cotangent, *wide, *narrow)


def ring_place(me, size):
    return jnp.where(me % 2 == 0, me // 2, size - 1 - me // 2)


def ring_device(place, size):
    return jnp.where(place < size // 2, 2 * place, 2 * (size - 1 - place) + 1)


def ring_kernel(size, peers, count, *refs):
    parts, small_ref = refs[:count], refs[count]
    outs, small_out_ref = refs[count + 1 : 2 * count + 1], refs[2 * count + 1]
    slots = refs[2 * count + 2 : 3 * count + 2]
    near_ref, far_ref, send, came, send_out, came_out, small_sems = refs[3 * count + 2 :]
    me, row = lax.axis_index("dp"), lax.axis_index("mp")
    place = ring_place(me, size)
    ways = (
        (place, ring_device((place + 1) % size, size)),
        (size - 1 - place, ring_device((place + size - 1) % size, size)),
    )

    barrier = pltpu.get_barrier_semaphore()

    def greet(t, carry):
        other = (me + t) % size
        pl.semaphore_signal(
            barrier, inc=1, device_id=(other, row), device_id_type=pl.DeviceIdType.MESH
        )
        return carry

    lax.fori_loop(1, size, greet, 0)
    for t in range(1, peers):
        pl.semaphore_signal(
            barrier,
            inc=1,
            device_id=(me, (row + t) % peers),
            device_id_type=pl.DeviceIdType.MESH,
        )
    pl.semaphore_wait(barrier, size - 1 + peers - 1)

    def remote(src, dst, send_sem, recv_sem, device):
        return pltpu.make_async_remote_copy(
            src_ref=src,
            dst_ref=dst,
            send_sem=send_sem,
            recv_sem=recv_sem,
            device_id=device,
            device_id_type=pl.DeviceIdType.MESH,
        )

    def block(i, way, number):
        rows = parts[i].shape[0] // (2 * size)
        start = way * size * rows + number * rows
        return pl.ds(pl.multiple_of(start, 16), rows)

    def near_copy(t):
        return remote(
            small_ref,
            near_ref.at[row],
            small_sems.at[0, t],
            small_sems.at[1, t],
            (me, (row + t) % peers),
        )

    def far_copy(t):
        return remote(
            far_ref.at[me],
            far_ref.at[me],
            small_sems.at[2, t],
            small_sems.at[3, t],
            ((me + t) % size, row),
        )

    for t in range(1, peers):
        near_copy(t).start()
    near_ref[pl.ds(row, 1)] = small_ref[...][None]

    rings = [(i, way) for i in range(count) for way in range(2)]

    def first_copy(i, way, step):
        return remote(
            slots[i].at[way, step - 1],
            slots[i].at[way, step],
            send.at[i, way, step],
            came.at[i, way, step],
            (ways[way][1], row),
        )

    def start_copy(i, way):
        return remote(
            parts[i].at[block(i, way, ways[way][0])],
            slots[i].at[way, 0],
            send.at[i, way, 0],
            came.at[i, way, 0],
            (ways[way][1], row),
        )

    def out_copy(i, way, step):
        span = block(i, way, (ways[way][0] + 1 - step + size) % size)
        return remote(
            outs[i].at[span],
            outs[i].at[span],
            send_out.at[i, way, step],
            came_out.at[i, way, step],
            (ways[way][1], row),
        )

    for i, way in rings:
        start_copy(i, way).start()

    def add_steps(step, carry):
        for i, way in rings:
            start_copy_like = remote(
                slots[i].at[way, step - 1],
                slots[i].at[way, step - 1],
                send.at[i, way, step - 1],
                came.at[i, way, step - 1],
                (ways[way][1], row),
            )
            start_copy_like.wait_recv()
            span = block(i, way, (ways[way][0] - step + size) % size)
            slots[i][way, step - 1] = (
                slots[i][way, step - 1].astype(F32) + parts[i][span].astype(F32)
            ).astype(BF16)
            first_copy(i, way, step).start()
        return carry

    lax.fori_loop(1, size - 1, add_steps, 0)

    for t in range(1, peers):
        near_copy(t).wait_recv()
    total = near_ref[0]
    for k in range(1, peers):
        total = total + near_ref[k]
    far_ref[pl.ds(me, 1)] = total[None]

    def far_start(t, carry):
        far_copy(t).start()
        return carry

    lax.fori_loop(1, size, far_start, 0)

    for i, way in rings:
        remote(
            slots[i].at[way, size - 2],
            slots[i].at[way, size - 2],
            send.at[i, way, size - 2],
            came.at[i, way, size - 2],
            (ways[way][1], row),
        ).wait_recv()
        span = block(i, way, (ways[way][0] + 1) % size)
        outs[i][span] = (
            slots[i][way, size - 2].astype(F32) + parts[i][span].astype(F32)
        ).astype(BF16)
        out_copy(i, way, 0).start()

    def pass_steps(step, carry):
        for i, way in rings:
            out_copy(i, way, step - 1).wait_recv()
            out_copy(i, way, step).start()
        return carry

    lax.fori_loop(1, size - 1, pass_steps, 0)

    def far_wait(t, carry):
        far_copy(t).wait()
        return carry

    lax.fori_loop(1, size, far_wait, 0)

    def far_add(k, total):
        return total + far_ref[k]

    small_out_ref[...] = lax.fori_loop(1, size, far_add, far_ref[0])
    for i, way in rings:
        out_copy(i, way, size - 2).wait_recv()
    for t in range(1, peers):
        near_copy(t).wait_send()

    for i, way in rings:
        start_copy(i, way).wait_send()

    def sent(step, carry):
        for i, way in rings:
            first_copy(i, way, step).wait_send()
        return carry

    lax.fori_loop(1, size - 1, sent, 0)

    def sent_out(step, carry):
        for i, way in rings:
            out_copy(i, way, step).wait_send()
        return carry

    lax.fori_loop(0, size - 1, sent_out, 0)


def ring_sums(size, peers, parts, small):
    grain = 2 * 16 * size
    rows = [p.shape[0] for p in parts]
    parts = [jnp.pad(p, ((0, -p.shape[0] % grain), (0, 0))) for p in parts]
    count = len(parts)
    vmem = pl.BlockSpec(memory_space=pltpu.VMEM)
    steps = pltpu.SemaphoreType.DMA((count, 2, size - 1))
    *sums, small = pl.pallas_call(
        functools.partial(ring_kernel, size, peers, count),
        in_specs=[vmem] * (count + 1),
        out_specs=[vmem] * (count + 1),
        out_shape=[*[shape(p.shape, BF16) for p in parts], shape(small.shape, F32)],
        scratch_shapes=[
            *[
                pltpu.VMEM((2, size - 1, p.shape[0] // (2 * size), p.shape[1]), BF16)
                for p in parts
            ],
            pltpu.VMEM((peers, *small.shape), F32),
            pltpu.VMEM((size, *small.shape), F32),
            steps,
            steps,
            steps,
            steps,
            pltpu.SemaphoreType.DMA((4, max(size, peers))),
        ],
        compiler_params=pltpu.CompilerParams(
            vmem_limit_bytes=VMEM_BYTES, collective_id=0, has_side_effects=True
        ),
        cost_estimate=cost(),
        name="ring_sums",
    )(*parts, small)
    return [total[:r] for total, r in zip(sums, rows)], small


def swap(array, bit, size):
    return lax.ppermute(array, "mp", [(i, i ^ bit) for i in range(size)])


def add_low(a, b):
    return (a.astype(F32) + b.astype(F32)).astype(BF16)


def fold_rest(stack, size):
    shares, bit = {2 * i: stack[i] for i in range(stack.shape[0])}, 2
    while bit < size:
        shares = {
            j: add_low(shares[j], swap(shares[j | bit], bit, size)) for j in shares if not j & bit
        }
        bit *= 2
    return shares[0]


def shards(
    decoder_rows,
    memory_rows,
    decoder_token_length,
    memory_length,
    bucket_ids,
    relative_bucket_bias,
    self_gain,
    self_query,
    self_key,
    self_value,
    self_out,
    cross_gain,
    cross_query,
    cross_key,
    cross_value,
    cross_out,
    hidden_gain,
    widen_weight,
    narrow_weight,
    layer_cotangent,
):
    dp_size = lax.axis_size("dp")
    mp_size = lax.axis_size("mp")
    me = lax.axis_index("mp")
    doc, features = decoder_rows.shape
    slots = memory_rows.shape[0]
    cols = self_query.shape[1]
    heads = cols // HEAD_DIM
    buckets = relative_bucket_bias.shape[0]
    order = [*range(1, mp_size, 2), *range(0, mp_size, 2)]

    bias_rows = jnp.zeros((TABLE_ROWS, features), BF16)
    bias_rows = bias_rows.at[:heads, :buckets].set(relative_bucket_bias.T)
    own_self = pack(
        (self_query.T, False), (self_key.T, False), (self_value.T, False), (self_out, False), (bias_rows, False)
    )
    own_self, memory_rows = lax.optimization_barrier((own_self, memory_rows))
    own_cross = pack(
        (cross_query.T, False), (cross_key.T, False), (cross_value.T, False), (cross_out, False)
    )
    own_wide = pack((widen_weight, True))

    def first_hops(own):
        shares, bit = {0: own}, mp_size // 2
        while bit > 1:
            for j in list(shares):
                shares[j | bit] = swap(shares[j], bit, mp_size)
            bit //= 2
        return shares

    def last_hop(shares):
        for j in list(shares):
            shares[j | 1] = swap(shares[j], 1, mp_size)
        return [shares[j] for j in order]

    near_self = first_hops(own_self)
    w_self = last_hop(near_self)
    near_cross = first_hops(own_cross)
    near_wide = first_hops(own_wide)
    near_narrow = first_hops(narrow_weight)
    memory_seen = lax.all_to_all(
        memory_rows.reshape(dp_size, slots // dp_size, features), "dp", 0, 0
    ).reshape(slots, features)

    doc_length = lax.dynamic_index_in_dim(decoder_token_length, me, keepdims=False)
    doc_memory = lax.dynamic_index_in_dim(memory_length, me, keepdims=False)
    position = jnp.arange(doc, dtype=jnp.int32)
    allowed = (position[:, None] <= position[None, :]) & (position[:, None] < doc_length)
    ids = jnp.where(allowed, bucket_ids.T, buckets)
    mask = jnp.where(jnp.arange(slots, dtype=jnp.int32) < doc_memory, 0.0, MASKED)
    mask = jnp.broadcast_to(mask[:, None].astype(F32), (slots, Q_BLOCK))

    gain_self = self_gain.astype(F32)[None]
    gain_cross = cross_gain.astype(F32)[None]
    gain_hidden = hidden_gain.astype(F32)[None]

    *saved_self, after_self = self_forward(heads, buckets, decoder_rows, gain_self, w_self, ids)
    near_cross, after_self = lax.optimization_barrier((near_cross, after_self))
    w_cross = last_hop(near_cross)
    *saved_cross, after_cross = cross_forward(
        heads, after_self, gain_cross, memory_seen, mask, w_cross
    )

    near_wide, near_narrow, after_cross = lax.optimization_barrier(
        (near_wide, near_narrow, after_cross)
    )
    w_wide, w_narrow = last_hop(near_wide), last_hop(near_narrow)
    give, keep, layer_output, grad_after_cross, branch, hidden_gain_grad = feed_forward(
        after_cross, gain_hidden, layer_cotangent, w_wide, w_narrow
    )
    part_hidden = add_low(keep, swap(give, 1, mp_size))
    branch, part_hidden = lax.optimization_barrier((branch, part_hidden))

    give, keep, grad_memory, grad_after_self, branch, cross_gain_grad = cross_backward(
        heads,
        after_self,
        gain_cross,
        memory_seen,
        mask,
        branch,
        grad_after_cross,
        saved_cross,
        w_cross,
    )
    memory_grad = lax.all_to_all(
        grad_memory.reshape(dp_size, slots // dp_size, features), "dp", 0, 0
    ).reshape(slots, features)
    part_hidden = fold_rest(part_hidden, mp_size)
    branch, part_hidden = lax.optimization_barrier((branch, part_hidden))
    part_cross = add_low(keep, swap(give, 1, mp_size))
    branch, part_cross = lax.optimization_barrier((branch, part_cross))
    part_cross = fold_rest(part_cross, mp_size)

    give, keep, score_grads, input_grad, self_gain_grad = self_backward(
        heads,
        buckets,
        decoder_rows,
        gain_self,
        ids,
        branch,
        grad_after_self,
        saved_self,
        w_self,
    )
    part_self = add_low(keep, swap(give, 1, mp_size))
    part_self = fold_rest(part_self, mp_size)

    sums = bucket_sums(ids, score_grads, buckets)
    back_to = [order.index(j) for j in range(mp_size)]
    sums = jnp.stack([sums[i] for i in back_to])
    sums = jnp.take(sums, me ^ jnp.arange(mp_size), axis=0)
    gains = jnp.stack([self_gain_grad, cross_gain_grad, hidden_gain_grad]).sum(axis=1)
    small = jnp.concatenate([gains.reshape(-1), sums.reshape(-1)])
    used = small.shape[0]
    small = jnp.pad(small, (0, -used % (8 * LANES))).reshape(-1, LANES)
    (sum_hidden, sum_cross, sum_self), small = ring_sums(
        dp_size, mp_size, [part_hidden.reshape(-1, features), part_cross, part_self], small
    )
    small = small.reshape(-1)[:used]
    gains = small[: 3 * features].reshape(3, features)
    sums = small[3 * features :].reshape(mp_size, heads, buckets)
    position_grad = lax.dynamic_index_in_dim(sums, me, keepdims=False).T

    sum_self = sum_self.astype(F32)
    sum_cross = sum_cross.astype(F32)
    sum_hidden = sum_hidden.astype(F32).reshape(2, -1, features)
    return (
        layer_output,
        input_grad,
        memory_grad,
        position_grad,
        gains[0],
        sum_self[:cols].T,
        sum_self[cols : 2 * cols].T,
        sum_self[2 * cols : 3 * cols].T,
        sum_self[3 * cols :],
        gains[1],
        sum_cross[:cols].T,
        sum_cross[cols : 2 * cols].T,
        sum_cross[2 * cols : 3 * cols].T,
        sum_cross[3 * cols :],
        gains[2],
        sum_hidden[0].T,
        sum_hidden[1],
    )


def solution(mesh):
    return jax.shard_map(
        shards,
        mesh=mesh,
        in_specs=(
            P(("dp", "mp"), None),
            P(("dp", "mp"), None),
            P("dp"),
            P("dp"),
            P(),
            P(None, "mp"),
            P(),
            P(None, "mp"),
            P(None, "mp"),
            P(None, "mp"),
            P("mp", None),
            P(),
            P(None, "mp"),
            P(None, "mp"),
            P(None, "mp"),
            P("mp", None),
            P(),
            P(None, "mp"),
            P("mp", None),
            P(("dp", "mp"), None),
        ),
        out_specs=(
            P(("dp", "mp"), None),
            P(("dp", "mp"), None),
            P(("dp", "mp"), None),
            P(None, "mp"),
            P(),
            P(None, "mp"),
            P(None, "mp"),
            P(None, "mp"),
            P("mp", None),
            P(),
            P(None, "mp"),
            P(None, "mp"),
            P(None, "mp"),
            P("mp", None),
            P(),
            P(None, "mp"),
            P("mp", None),
        ),
        check_vma=False,
    )
```

```python
import functools

import jax
import jax.numpy as jnp
from jax import lax
from jax.experimental import pallas as pl
from jax.experimental.pallas import tpu as pltpu
from jax.sharding import PartitionSpec as P

HEAD_DIM = 64
NORM_EPS = 1e-06
MASKED = -1e30
SCALE = HEAD_DIM**-0.5
BF16 = jnp.bfloat16
F32 = jnp.float32
LANES = 128
TABLE_ROWS = 16
HEAD_BLOCK = 256
BLOCK_HEADS = HEAD_BLOCK // HEAD_DIM
Q_BLOCK = 256
K_BLOCK = 256
HIDDEN_BLOCK = 256
ROW_BLOCK = 128
VMEM_BYTES = 56 * 1024 * 1024
GELU_ROOT = 0.7978845608028654
GELU_CUBE = 0.044715


def dot_nn(a, b):
    return lax.dot_general(a, b, (((1,), (0,)), ((), ())), preferred_element_type=F32)


def dot_nt(a, b):
    return lax.dot_general(a, b, (((1,), (1,)), ((), ())), preferred_element_type=F32)


def dot_tn(a, b):
    return lax.dot_general(a, b, (((0,), (0,)), ((), ())), preferred_element_type=F32)


def flip(a):
    return a.astype(F32).T.astype(BF16)


def spans(size, step):
    return [slice(i, i + step) for i in range(0, size, step)]


def norm_scale(rows):
    return lax.rsqrt(jnp.mean(rows * rows, axis=-1, keepdims=True) + NORM_EPS)


def norm_into(normed_ref, rows_ref, gain_ref):
    for span in spans(rows_ref.shape[0], ROW_BLOCK):
        rows = rows_ref[span].astype(F32)
        normed_ref[span] = (rows * norm_scale(rows) * gain_ref[...]).astype(BF16)


def norm_back_into(span, grad, out_ref, low_ref, gain_grad_ref, rows_ref, gain_ref, add_ref):
    rows = rows_ref[span].astype(F32)
    scale = norm_scale(rows)
    unit = rows * scale
    grad_unit = grad * gain_ref[...]
    mean = jnp.mean(grad_unit * unit, axis=-1, keepdims=True)
    out = add_ref[span].astype(F32) + scale * (grad_unit - unit * mean)
    out_ref[span] = out
    if low_ref is not None:
        low_ref[span] = out.astype(BF16)
    gain_grad_ref[...] += jnp.sum((grad * unit).reshape(-1, 8, rows.shape[1]), axis=0)


def gelu_and_slope(v):
    square = v * v
    bend = jnp.tanh(GELU_ROOT * (v + GELU_CUBE * v * square))
    half = 0.5 * (1.0 + bend)
    slope = half + 0.5 * v * (1.0 - bend * bend) * GELU_ROOT * (1.0 + 3.0 * GELU_CUBE * square)
    return v * half, slope


def lane_block(start):
    return pl.ds(pl.multiple_of(start, LANES), LANES)


def extra_lanes(rows, allowed):
    lane = lax.broadcasted_iota(jnp.int32, (rows, LANES), 1) % HEAD_DIM
    first = MASKED if allowed is None else jnp.where(allowed, 0.0, MASKED)
    return jnp.where(lane == 0, first, jnp.where(lane < 4, 1.0, 0.0)).astype(BF16)


def pick(which, block, other):
    lane = lax.broadcasted_iota(jnp.int32, block.shape, 1)
    return jnp.where((lane < HEAD_DIM) == (which == 0), block, other)


def half_rows(which):
    return slice(which * HEAD_DIM, (which + 1) * HEAD_DIM)


def split(values):
    high = values.astype(BF16).astype(F32)
    rest = values - high
    middle = rest.astype(BF16).astype(F32)
    return high, middle, rest - middle


def with_extra(which, block_t, masked, minus):
    columns = block_t.shape[1]
    row = lax.broadcasted_iota(jnp.int32, (HEAD_DIM, columns), 0)
    extra = jnp.where(row == 0, 1.0 if masked else 0.0, 0.0)
    if minus is not None:
        for i, part in enumerate(split(minus)):
            extra = jnp.where(row == i + 1, -part, extra)
    own = block_t[half_rows(which)]
    return jnp.concatenate([own, extra] if which == 0 else [extra, own], axis=0).astype(BF16)


def bias_block(table_ref, ids_ref, index, rows, start):
    row = jnp.broadcast_to(table_ref[pl.ds(index, 1), :], (rows, LANES))
    return jnp.concatenate(
        [
            jnp.take_along_axis(row, ids_ref[:rows, c : c + LANES], axis=1)
            for c in range(start, start + Q_BLOCK, LANES)
        ],
        axis=1,
    )


class Stack:
    def __init__(self, sources, stack_ref, sems, kinds, rows):
        features = stack_ref.shape[0] // kinds
        self.copies = [
            [
                pltpu.make_async_copy(
                    source.at[pl.ds(kind * rows, rows)],
                    stack_ref.at[pl.ds(kind * features + p * rows, rows)],
                    sems.at[p, kind],
                )
                for p, source in enumerate(sources)
            ]
            for kind in range(kinds)
        ]

    def start(self):
        for copies in self.copies:
            for copy in copies:
                copy.start()

    def wait(self, *kinds):
        for kind in kinds:
            for copy in self.copies[kind]:
                copy.wait()


def table_copies(sources, tables_ref, sems, kinds):
    start = sources[0].shape[0] - TABLE_ROWS
    return [
        pltpu.make_async_copy(
            source.at[pl.ds(start, TABLE_ROWS)], tables_ref.at[p], sems.at[p, kinds]
        )
        for p, source in enumerate(sources)
    ]


def table_into(table_ref, tables_ref, heads, buckets):
    for p in range(tables_ref.shape[0]):
        rows = tables_ref[p, :, :LANES].astype(F32)
        lane = lax.broadcasted_iota(jnp.int32, rows.shape, 1)
        rows = jnp.where(lane < buckets, rows, MASKED)
        for h in range(heads):
            table_ref[p * heads + h : p * heads + h + 1, :] = rows[h : h + 1, :]


def self_forward_kernel(heads, buckets, shares, rows_ref, gain_ref, ids_ref, *refs):
    sources = refs[:shares]
    q_ref, k_ref, v_ref, mixed_ref, lse_ref, out_ref = refs[shares : shares + 6]
    w_ref, tables_ref, table_ref, normed_ref, sems = refs[shares + 6 :]
    step = pl.program_id(0)
    doc, features = rows_ref.shape
    stack = Stack(sources, w_ref, sems, 4, heads * HEAD_DIM)

    @pl.when(step == 0)
    def _():
        stack.start()
        tables = table_copies(sources, tables_ref, sems, 4)
        for copy in tables:
            copy.start()
        norm_into(normed_ref, rows_ref, gain_ref)
        out_ref[...] = rows_ref[...].astype(F32)
        for copy in tables:
            copy.wait()
        table_into(table_ref, tables_ref, heads, buckets)
        stack.wait(0, 1, 2, 3)

    def weights(kind):
        start = pl.multiple_of(kind * features + step * HEAD_BLOCK, HEAD_BLOCK)
        return w_ref[pl.ds(start, HEAD_BLOCK)]

    for kind, ref in enumerate((q_ref, k_ref, v_ref)):
        ref[...] = dot_nt(normed_ref[...], weights(kind)).astype(BF16)
    none = jnp.zeros((doc, LANES), BF16)
    for pair in range(BLOCK_HEADS // 2):
        lanes = slice(pair * LANES, (pair + 1) * LANES)
        k, v_t = k_ref[:, lanes], flip(v_ref[:, lanes])
        q_t = flip(q_ref[:, lanes].astype(F32) * SCALE)
        k_of = [pick(which, k, none) for which in range(2)]
        for span in spans(doc, Q_BLOCK):
            rows, mixed = span.stop, []
            for which in range(2):
                h = 2 * pair + which
                s = dot_nn(k_of[which][:rows], q_t[:, span])
                s = s + bias_block(table_ref, ids_ref, step * BLOCK_HEADS + h, rows, span.start)
                top = jnp.max(s, axis=0, keepdims=True)
                p = jnp.exp(s - top)
                total = jnp.sum(p, axis=0, keepdims=True)
                mixed.append(dot_nn(v_t[half_rows(which), :rows], p.astype(BF16)) / total)
                lse_ref[0, h : h + 1, span] = top + jnp.log(total)
            mixed_ref[span, lanes] = jnp.concatenate(mixed, axis=0).T.astype(BF16)
    out_ref[...] += dot_nn(mixed_ref[...], weights(3))


def self_backward_kernel(heads, buckets, shares, *refs):
    rows_ref, gain_ref, ids_ref, branch_ref, add_ref = refs[:5]
    q_ref, k_ref, v_ref, mixed_ref, lse_ref = refs[5:10]
    sources = refs[10 : 10 + shares]
    give_ref, keep_ref, ds_ref, out_ref, gain_grad_ref = refs[10 + shares : 15 + shares]
    w_ref, tables_ref, table_ref, normed_ref, g_ref, grad_ref, sems = refs[15 + shares :]
    step = pl.program_id(0)
    doc, features = rows_ref.shape
    half = features // 2
    stack = Stack(sources, w_ref, sems, 4, heads * HEAD_DIM)

    @pl.when(step == 0)
    def _():
        stack.start()
        tables = table_copies(sources, tables_ref, sems, 4)
        for copy in tables:
            copy.start()
        norm_into(normed_ref, rows_ref, gain_ref)
        for copy in tables:
            copy.wait()
        table_into(table_ref, tables_ref, heads, buckets)
        stack.wait(3)

    start = pl.multiple_of(3 * features + step * HEAD_BLOCK, HEAD_BLOCK)
    g_ref[...] = dot_nt(branch_ref[...], w_ref[pl.ds(start, HEAD_BLOCK)]).astype(BF16)
    none = jnp.zeros((doc, LANES), BF16)
    ones = extra_lanes(doc, None)
    for pair in range(BLOCK_HEADS // 2):
        lanes = lane_block(step * HEAD_BLOCK + pair * LANES)
        q, k, v = q_ref[:, lanes], k_ref[:, lanes], v_ref[:, lanes]
        g = g_ref[:, pair * LANES : (pair + 1) * LANES]
        q_t, k_t = q.astype(F32).T * SCALE, flip(k)
        g_t = g.astype(F32).T
        inner = g_t * mixed_ref[:, lanes].astype(F32).T
        per_head = []
        for which in range(2):
            h = 2 * pair + which
            minus = jnp.sum(inner[half_rows(which)], axis=0, keepdims=True)
            per_head.append(
                (
                    pick(which, k, ones),
                    pick(which, v, ones),
                    with_extra(which, q_t, False, lse_ref[0, h : h + 1, :]),
                    with_extra(which, g_t, False, minus),
                    pick(which, q, none),
                    pick(which, g, none),
                )
            )
        grad_k = grad_v = None
        for span in spans(doc, Q_BLOCK):
            rows, grad_q, part_k, part_v = span.stop, [], None, None
            for which, (k_of, v_of, q_with, g_with, q_of, g_of) in enumerate(per_head):
                h = 2 * pair + which
                s = dot_nn(k_of[:rows], q_with[:, span])
                s = s + bias_block(table_ref, ids_ref, step * BLOCK_HEADS + h, rows, span.start)
                p = jnp.exp(s)
                ds = (p * dot_nn(v_of[:rows], g_with[:, span])).astype(BF16)
                ds_ref[h, :rows, span] = ds
                grad_q.append(dot_nn(k_t[half_rows(which), :rows], ds))
                to_v = dot_nn(p.astype(BF16), g_of[span])
                to_k = dot_nn(ds, q_of[span])
                part_v = to_v if part_v is None else part_v + to_v
                part_k = to_k if part_k is None else part_k + to_k
            grad_q = (jnp.concatenate(grad_q, axis=0) * SCALE).T
            grad_ref[0, span, lanes] = grad_q.astype(BF16)
            if grad_v is not None:
                part_v = jnp.concatenate(
                    [part_v[: span.start] + grad_v, part_v[span.start :]], axis=0
                )
                part_k = jnp.concatenate(
                    [part_k[: span.start] + grad_k, part_k[span.start :]], axis=0
                )
            grad_v, grad_k = part_v, part_k
        grad_ref[1, :, lanes] = (grad_k * SCALE).astype(BF16)
        grad_ref[2, :, lanes] = grad_v.astype(BF16)

    @pl.when(step == pl.num_programs(0) - 1)
    def _():
        stack.wait(0, 1, 2)
        for ref, columns in ((give_ref, slice(0, half)), (keep_ref, slice(half, features))):
            for kind in range(3):
                ref[kind] = dot_tn(grad_ref[kind, :, columns], normed_ref[...]).astype(BF16)
            ref[3] = dot_tn(mixed_ref[:, columns], branch_ref[...]).astype(BF16)
        gain_grad_ref[...] = jnp.zeros_like(gain_grad_ref)
        for span in spans(doc, ROW_BLOCK):
            back = dot_nn(grad_ref[0, span], w_ref[:features])
            back = back + dot_nn(grad_ref[1, span], w_ref[features : 2 * features])
            back = back + dot_nn(grad_ref[2, span], w_ref[2 * features : 3 * features])
            norm_back_into(
                span, back, out_ref, None, gain_grad_ref, rows_ref, gain_ref, add_ref
            )


def bucket_sum_kernel(heads, buckets, ids_ref, ds_ref, out_ref, wide_ref):
    doc = ids_ref.shape[0]
    wide_ref[...] = ds_ref[...].astype(F32)

    def one_bucket(b, carry):
        sums = [jnp.zeros((8, LANES), F32) for _ in range(heads)]
        for c in range(0, doc, LANES):
            rows = c + LANES
            hit = ids_ref[:rows, c : c + LANES] == b
            for h in range(heads):
                kept = jnp.where(hit, wide_ref[h, :rows, c : c + LANES], 0.0)
                sums[h] = sums[h] + jnp.sum(kept.reshape(rows // 8, 8, LANES), axis=0)
        for h in range(heads):
            out_ref[h, pl.ds(b, 1), :] = jnp.sum(sums[h], axis=0, keepdims=True)
        return carry

    lax.fori_loop(0, buckets, one_bucket, 0)


def cross_forward_kernel(heads, shares, length_ref, rows_ref, gain_ref, memory_ref, *refs):
    sources = refs[:shares]
    q_ref, k_ref, v_ref, mixed_ref, lse_ref, out_ref = refs[shares : shares + 6]
    w_ref, normed_ref, extra_ref, p_ref, sems = refs[shares + 6 :]
    step = pl.program_id(0)
    (doc, features), slots = rows_ref.shape, memory_ref.shape[0]
    stack = Stack(sources, w_ref, sems, 4, heads * HEAD_DIM)

    @pl.when(step == 0)
    def _():
        stack.start()
        norm_into(normed_ref, rows_ref, gain_ref)
        out_ref[...] = rows_ref[...]
        slot = lax.broadcasted_iota(jnp.int32, (slots, LANES), 0)
        extra_ref[...] = extra_lanes(slots, slot < length_ref[0])
        stack.wait(0, 1, 2, 3)

    def weights(kind):
        start = pl.multiple_of(kind * features + step * HEAD_BLOCK, HEAD_BLOCK)
        return w_ref[pl.ds(start, HEAD_BLOCK)]

    q_ref[...] = dot_nt(normed_ref[...], weights(0)).astype(BF16)
    k_ref[...] = dot_nt(memory_ref[...], weights(1)).astype(BF16)
    v_ref[...] = dot_nt(memory_ref[...], weights(2)).astype(BF16)

    units = [
        (pair, which, span)
        for pair in range(BLOCK_HEADS // 2)
        for span in spans(doc, Q_BLOCK)
        for which in range(2)
    ]
    v_t = [flip(v_ref[:, p * LANES : (p + 1) * LANES]) for p in range(BLOCK_HEADS // 2)]
    q_t = [
        q_ref[:, p * LANES : (p + 1) * LANES].astype(F32).T * SCALE
        for p in range(BLOCK_HEADS // 2)
    ]

    def scores(unit):
        pair, which, span = unit
        q_with = with_extra(which, q_t[pair][:, span], True, None)
        k_of = pick(which, k_ref[:, pair * LANES : (pair + 1) * LANES], extra_ref[...])
        return [dot_nn(k_of[rows], q_with) for rows in spans(slots, K_BLOCK)]

    mixed = {}
    ahead = scores(units[0])
    for i, (pair, which, span) in enumerate(units):
        s, slot = ahead, i % 2
        if i + 1 < len(units):
            ahead = scores(units[i + 1])
        top = functools.reduce(jnp.maximum, [jnp.max(c, axis=0, keepdims=True) for c in s])
        total = None
        for rows, chunk in zip(spans(slots, K_BLOCK), s):
            p = jnp.exp(chunk - top)
            part = jnp.sum(p, axis=0, keepdims=True)
            total = part if total is None else total + part
            p_ref[slot, rows] = p.astype(BF16)
        h = 2 * pair + which
        lse_ref[0, h : h + 1, span] = top + jnp.log(total)
        mixed[which] = dot_nn(v_t[pair][half_rows(which)], p_ref[slot]) / total
        if which == 1:
            out = jnp.concatenate([mixed[0], mixed[1]], axis=0).T
            mixed_ref[span, pair * LANES : (pair + 1) * LANES] = out.astype(BF16)
    out_ref[...] += dot_nn(mixed_ref[...], weights(3))


def cross_backward_kernel(heads, shares, length_ref, *refs):
    rows_ref, gain_ref, memory_ref, branch_ref, add_ref = refs[:5]
    q_ref, k_ref, v_ref, mixed_ref, lse_ref = refs[5:10]
    sources = refs[10 : 10 + shares]
    give_ref, keep_ref, memory_out_ref, out_ref, low_ref, gain_grad_ref = refs[
        10 + shares : 16 + shares
    ]
    w_ref, normed_ref, extra_ref, g_ref, grad_q_ref, grad_ref, ds_ref, sems = refs[16 + shares :]
    step = pl.program_id(0)
    (doc, features), slots = rows_ref.shape, memory_ref.shape[0]
    half = features // 2
    stack = Stack(sources, w_ref, sems, 4, heads * HEAD_DIM)

    @pl.when(step == 0)
    def _():
        stack.start()
        norm_into(normed_ref, rows_ref, gain_ref)
        slot = lax.broadcasted_iota(jnp.int32, (slots, LANES), 0)
        extra_ref[...] = extra_lanes(slots, slot < length_ref[0])
        stack.wait(3)

    start = pl.multiple_of(3 * features + step * HEAD_BLOCK, HEAD_BLOCK)
    g_ref[...] = dot_nt(branch_ref[...], w_ref[pl.ds(start, HEAD_BLOCK)]).astype(BF16)
    none = jnp.zeros((doc, LANES), BF16)
    for pair in range(BLOCK_HEADS // 2):
        local = slice(pair * LANES, (pair + 1) * LANES)
        lanes = lane_block(step * HEAD_BLOCK + pair * LANES)
        v_lanes = lane_block(features + step * HEAD_BLOCK + pair * LANES)
        q, g = q_ref[:, lanes], g_ref[:, local]
        q_t, g_t = q.astype(F32).T * SCALE, g.astype(F32).T
        inner = g_t * mixed_ref[:, lanes].astype(F32).T
        per_head = []
        for which in range(2):
            h = 2 * pair + which
            minus = jnp.sum(inner[half_rows(which)], axis=0, keepdims=True)
            per_head.append(
                (
                    with_extra(which, q_t, True, lse_ref[0, h : h + 1, :]),
                    with_extra(which, g_t, False, minus),
                    pick(which, q, none),
                    pick(which, g, none),
                )
            )
        for rows in spans(slots, K_BLOCK):
            k, v, extra = k_ref[rows, local], v_ref[rows, local], extra_ref[rows]
            part_k = part_v = None
            for which, (q_with, g_with, q_of, g_of) in enumerate(per_head):
                p = jnp.exp(dot_nn(pick(which, k, extra), q_with))
                ds = (p * dot_nn(pick(which, v, extra), g_with)).astype(BF16)
                ds_ref[which, rows] = ds
                to_v = dot_nn(p.astype(BF16), g_of)
                to_k = dot_nn(ds, q_of)
                part_v = to_v if part_v is None else part_v + to_v
                part_k = to_k if part_k is None else part_k + to_k
            grad_ref[rows, lanes] = (part_k * SCALE).astype(BF16)
            grad_ref[rows, v_lanes] = part_v.astype(BF16)
        k_t = flip(k_ref[:, local])
        grad_q = [dot_nn(k_t[half_rows(which)], ds_ref[which]) for which in range(2)]
        grad_q_ref[:, lanes] = (jnp.concatenate(grad_q, axis=0) * SCALE).T.astype(BF16)

    @pl.when(step == pl.num_programs(0) - 1)
    def _():
        stack.wait(0, 1, 2)
        for ref, first in ((give_ref, 0), (keep_ref, half)):
            columns = slice(first, first + half)
            v_columns = slice(features + first, features + first + half)
            ref[0] = dot_tn(grad_q_ref[:, columns], normed_ref[...]).astype(BF16)
            ref[1] = dot_tn(grad_ref[:, columns], memory_ref[...]).astype(BF16)
            ref[2] = dot_tn(grad_ref[:, v_columns], memory_ref[...]).astype(BF16)
            ref[3] = dot_tn(mixed_ref[:, columns], branch_ref[...]).astype(BF16)
        gain_grad_ref[...] = jnp.zeros_like(gain_grad_ref)
        for span in spans(doc, ROW_BLOCK):
            back = dot_nn(grad_q_ref[span], w_ref[:features])
            norm_back_into(
                span, back, out_ref, low_ref, gain_grad_ref, rows_ref, gain_ref, add_ref
            )
        for rows in spans(slots, K_BLOCK):
            memory_out_ref[rows] = dot_nn(
                grad_ref[rows], w_ref[features : 3 * features]
            ).astype(BF16)


def feed_forward_kernel(shares, rows_ref, gain_ref, cotangent_ref, *refs):
    wide_sources, narrow_sources = refs[:shares], refs[shares : 2 * shares]
    give_ref, keep_ref, layer_ref, out_ref, low_ref, gain_grad_ref = refs[
        2 * shares : 2 * shares + 6
    ]
    (
        wide_ref,
        narrow_ref,
        normed_ref,
        normed_t,
        cotangent_t,
        active_ref,
        grad_ref,
        sems,
    ) = refs[2 * shares + 6 :]
    step, steps = pl.program_id(0), pl.num_programs(0)
    doc = rows_ref.shape[0]
    hidden = wide_sources[0].shape[0]
    per_share = hidden // HIDDEN_BLOCK
    copies = [
        [
            pltpu.make_async_copy(
                source, stack.at[pl.ds(p * hidden, hidden)], sems.at[p, kind]
            )
            for kind, (source, stack) in enumerate(((w, wide_ref), (n, narrow_ref)))
        ]
        for p, (w, n) in enumerate(zip(wide_sources, narrow_sources))
    ]

    @pl.when(step == 0)
    def _():
        for pair in copies:
            for copy in pair:
                copy.start()
        norm_into(normed_ref, rows_ref, gain_ref)
        for span in spans(doc, ROW_BLOCK):
            normed_t[:, span] = flip(normed_ref[span])
            cotangent_t[:, span] = flip(cotangent_ref[span])

    for p, pair in enumerate(copies):

        @pl.when(step == p * per_share)
        def _(pair=pair):
            for copy in pair:
                copy.wait()

    units = pl.ds(pl.multiple_of(step * HIDDEN_BLOCK, HIDDEN_BLOCK), HIDDEN_BLOCK)
    activated, slope = gelu_and_slope(dot_nn(wide_ref[units], normed_t[...]))
    active_ref[units] = activated.astype(BF16)
    grad_ref[units] = (dot_nn(narrow_ref[units], cotangent_t[...]) * slope).astype(BF16)

    def store(ref):
        ref[0] = dot_nn(grad_ref[units], normed_ref[...]).astype(BF16)
        ref[1] = dot_nn(active_ref[units], cotangent_ref[...]).astype(BF16)

    @pl.when(step < steps // 2)
    def _():
        store(give_ref)

    @pl.when(step >= steps // 2)
    def _():
        store(keep_ref)

    @pl.when(step == steps - 1)
    def _():
        gain_grad_ref[...] = jnp.zeros_like(gain_grad_ref)
        for span in spans(doc, ROW_BLOCK):
            layer = rows_ref[span] + dot_tn(active_ref[:, span], narrow_ref[...])
            layer_ref[span] = layer.astype(BF16)
            back = dot_tn(grad_ref[:, span], wide_ref[...])
            norm_back_into(
                span, back, out_ref, low_ref, gain_grad_ref, rows_ref, gain_ref, cotangent_ref
            )


def pack_kernel(flipped, *refs):
    out_ref, start = refs[-1], 0
    for source, turn in zip(refs[:-1], flipped):
        rows = source.shape[1] if turn else source.shape[0]
        span = slice(start, start + rows)
        out_ref[span] = flip(source[...]) if turn else source[...]
        start += rows


def add_kernel(kept_ref, came_ref, out_ref):
    out_ref[...] = (kept_ref[...].astype(F32) + came_ref[...].astype(F32)).astype(BF16)


def finish_kernel(hidden_ref, cross_ref, self_ref, wide_ref, narrow_ref, *outs):
    hidden = narrow_ref.shape[0]
    for span in spans(hidden, ROW_BLOCK):
        wide_ref[:, span] = hidden_ref[span].astype(F32).T
        narrow_ref[span] = hidden_ref[hidden + span.start : hidden + span.stop].astype(F32)
    rows = outs[0].shape[0]
    for source, refs in ((self_ref, outs[:4]), (cross_ref, outs[4:])):
        for kind, ref in enumerate(refs):
            ref[...] = source[kind * rows : (kind + 1) * rows].astype(F32)


def params():
    return pltpu.CompilerParams(vmem_limit_bytes=VMEM_BYTES)


def cost():
    return pl.CostEstimate(flops=1 << 20, bytes_accessed=1 << 16, transcendentals=0)


def shape(dims, dtype):
    return jax.ShapeDtypeStruct(dims, dtype)


def whole(array):
    return pl.BlockSpec(
        array.shape, lambda *_: (0,) * len(array.shape), pipeline_mode=pl.Buffered(1)
    )


def result(array):
    return pl.BlockSpec(array.shape, lambda *_: (0,) * len(array.shape))


def columns(rows):
    return pl.BlockSpec((rows, HEAD_BLOCK), lambda i: (0, i))


def anywhere(arrays):
    return [pl.BlockSpec(memory_space=pl.ANY) for _ in arrays]


SCALAR = pl.BlockSpec(memory_space=pltpu.SMEM)


def call(kernel, name, grid, in_specs, out_specs, out_shape, scratch, args):
    return pl.pallas_call(
        kernel,
        grid=grid,
        in_specs=in_specs,
        out_specs=out_specs,
        out_shape=out_shape,
        scratch_shapes=scratch,
        compiler_params=params(),
        cost_estimate=cost(),
        name=name,
    )(*args)


def pack(*parts):
    arrays, flipped = zip(*parts)
    rows = sum(a.shape[1] if turn else a.shape[0] for a, turn in parts)
    features = arrays[0].shape[0] if flipped[0] else arrays[0].shape[1]
    return pl.pallas_call(
        functools.partial(pack_kernel, flipped),
        out_shape=shape((rows, features), BF16),
        compiler_params=params(),
        cost_estimate=cost(),
        name="pack",
    )(*arrays)


def add_share(kept, came, index, count):
    kinds, rows, features = kept.shape
    rows //= count
    share = pl.BlockSpec((1, rows, features), lambda i: (i, index, 0))
    out = shape((kinds, rows, features), BF16)
    own = pl.BlockSpec((1, rows, features), lambda i: (i, 0, 0))
    return call(add_kernel, "add_share", (kinds,), [share, share], own, out, [], (kept, came))


def self_forward(heads, buckets, rows, gain, weights, ids):
    doc, features = rows.shape
    shares, steps = len(weights), features // HEAD_BLOCK
    narrow, tall = shape((doc, features), BF16), shape((doc, features), F32)
    out_shape = (*[narrow] * 4, shape((steps, 8, doc), F32), tall)
    return call(
        functools.partial(self_forward_kernel, heads, buckets, shares),
        "self_forward",
        (steps,),
        [whole(rows), whole(gain), whole(ids), *anywhere(weights)],
        (*[columns(doc)] * 4, pl.BlockSpec((1, 8, doc), lambda i: (i, 0, 0)), result(tall)),
        out_shape,
        [
            pltpu.VMEM((4 * features, features), BF16),
            pltpu.VMEM((shares, TABLE_ROWS, features), BF16),
            pltpu.VMEM((TABLE_ROWS, LANES), F32),
            pltpu.VMEM((doc, features), BF16),
            pltpu.SemaphoreType.DMA((shares, 5)),
        ],
        (rows, gain, ids, *weights),
    )


def self_backward(heads, buckets, rows, gain, ids, branch, add, saved, weights):
    doc, features = rows.shape
    shares, steps = len(weights), features // HEAD_BLOCK
    packed = shape((4, features // 2, features), BF16)
    out_shape = (
        packed,
        packed,
        shape((steps * BLOCK_HEADS, doc, doc), BF16),
        shape((doc, features), F32),
        shape((8, features), F32),
    )
    *arrays, lse = saved
    return call(
        functools.partial(self_backward_kernel, heads, buckets, shares),
        "self_backward",
        (steps,),
        [
            *[whole(a) for a in (rows, gain, ids, branch, add, *arrays)],
            pl.BlockSpec((1, 8, doc), lambda i: (i, 0, 0)),
            *anywhere(weights),
        ],
        (
            result(packed),
            result(packed),
            pl.BlockSpec((BLOCK_HEADS, doc, doc), lambda i: (i, 0, 0)),
            result(out_shape[3]),
            result(out_shape[4]),
        ),
        out_shape,
        [
            pltpu.VMEM((4 * features, features), BF16),
            pltpu.VMEM((shares, TABLE_ROWS, features), BF16),
            pltpu.VMEM((TABLE_ROWS, LANES), F32),
            pltpu.VMEM((doc, features), BF16),
            pltpu.VMEM((doc, HEAD_BLOCK), BF16),
            pltpu.VMEM((3, doc, features), BF16),
            pltpu.SemaphoreType.DMA((shares, 5)),
        ],
        (rows, gain, ids, branch, add, *arrays, lse, *weights),
    )


def bucket_sums(ids, ds, buckets):
    heads, doc, _ = ds.shape
    sums = call(
        functools.partial(bucket_sum_kernel, BLOCK_HEADS, buckets),
        "bucket_sums",
        (heads // BLOCK_HEADS,),
        [whole(ids), pl.BlockSpec((BLOCK_HEADS, doc, doc), lambda i: (i, 0, 0))],
        pl.BlockSpec((BLOCK_HEADS, buckets, LANES), lambda i: (i, 0, 0)),
        shape((heads, buckets, LANES), F32),
        [pltpu.VMEM((BLOCK_HEADS, doc, doc), F32)],
        (ids, ds),
    )
    return jnp.sum(sums, axis=2)


def cross_forward(heads, rows, gain, memory, length, weights):
    (doc, features), slots = rows.shape, memory.shape[0]
    shares, steps = len(weights), features // HEAD_BLOCK
    query, key = shape((doc, features), BF16), shape((slots, features), BF16)
    tall = shape((doc, features), F32)
    return call(
        functools.partial(cross_forward_kernel, heads, shares),
        "cross_forward",
        (steps,),
        [SCALAR, whole(rows), whole(gain), whole(memory), *anywhere(weights)],
        (
            columns(doc),
            columns(slots),
            columns(slots),
            columns(doc),
            pl.BlockSpec((1, 8, doc), lambda i: (i, 0, 0)),
            result(tall),
        ),
        (query, key, key, query, shape((steps, 8, doc), F32), tall),
        [
            pltpu.VMEM((4 * features, features), BF16),
            pltpu.VMEM((doc, features), BF16),
            pltpu.VMEM((slots, LANES), BF16),
            pltpu.VMEM((2, slots, Q_BLOCK), BF16),
            pltpu.SemaphoreType.DMA((shares, 4)),
        ],
        (length, rows, gain, memory, *weights),
    )


def cross_backward(heads, rows, gain, memory, length, branch, add, saved, weights):
    (doc, features), slots = rows.shape, memory.shape[0]
    shares, steps = len(weights), features // HEAD_BLOCK
    packed = shape((4, features // 2, features), BF16)
    out_shape = (
        packed,
        packed,
        shape((slots, features), BF16),
        shape((doc, features), F32),
        shape((doc, features), BF16),
        shape((8, features), F32),
    )
    query, key, value, mixed, lse = saved
    return call(
        functools.partial(cross_backward_kernel, heads, shares),
        "cross_backward",
        (steps,),
        [
            SCALAR,
            *[whole(a) for a in (rows, gain, memory, branch, add, query)],
            columns(slots),
            columns(slots),
            whole(mixed),
            pl.BlockSpec((1, 8, doc), lambda i: (i, 0, 0)),
            *anywhere(weights),
        ],
        tuple(result(o) for o in out_shape),
        out_shape,
        [
            pltpu.VMEM((4 * features, features), BF16),
            pltpu.VMEM((doc, features), BF16),
            pltpu.VMEM((slots, LANES), BF16),
            pltpu.VMEM((doc, HEAD_BLOCK), BF16),
            pltpu.VMEM((doc, features), BF16),
            pltpu.VMEM((slots, 2 * features), BF16),
            pltpu.VMEM((2, slots, doc), BF16),
            pltpu.SemaphoreType.DMA((shares, 4)),
        ],
        (length, rows, gain, memory, branch, add, *saved, *weights),
    )


def feed_forward(rows, gain, cotangent, wide, narrow):
    (doc, features), shares = rows.shape, len(wide)
    hidden = wide[0].shape[0] * shares
    steps = hidden // HIDDEN_BLOCK
    half = steps // 2
    packed = shape((2, hidden // 2, features), BF16)
    out_shape = (
        packed,
        packed,
        shape((doc, features), BF16),
        shape((doc, features), F32),
        shape((doc, features), BF16),
        shape((8, features), F32),
    )
    block = (2, HIDDEN_BLOCK, features)
    return call(
        functools.partial(feed_forward_kernel, shares),
        "feed_forward",
        (steps,),
        [whole(rows), whole(gain), whole(cotangent), *anywhere(wide), *anywhere(narrow)],
        (
            pl.BlockSpec(block, lambda i: (0, jnp.minimum(i, half - 1), 0)),
            pl.BlockSpec(block, lambda i: (0, jnp.maximum(i - half, 0), 0)),
            *[result(o) for o in out_shape[2:]],
        ),
        out_shape,
        [
            pltpu.VMEM((hidden, features), BF16),
            pltpu.VMEM((hidden, features), BF16),
            pltpu.VMEM((doc, features), BF16),
            pltpu.VMEM((features, doc), BF16),
            pltpu.VMEM((features, doc), BF16),
            pltpu.VMEM((hidden, doc), BF16),
            pltpu.VMEM((hidden, doc), BF16),
            pltpu.SemaphoreType.DMA((shares, 2)),
        ],
        (rows, gain, cotangent, *wide, *narrow),
    )


def finish(sum_hidden, sum_cross, sum_self):
    rows, features = sum_self.shape
    hidden, part = sum_hidden.shape[0] // 2, shape((rows // 4, features), F32)
    wide, narrow, *parts = pl.pallas_call(
        finish_kernel,
        out_shape=[
            shape((features, hidden), F32),
            shape((hidden, features), F32),
            *[part] * 8,
        ],
        compiler_params=params(),
        cost_estimate=cost(),
        name="finish",
    )(sum_hidden, sum_cross, sum_self)
    return wide, narrow, parts[:4], parts[4:]


def ring_place(me, size):
    return jnp.where(me % 2 == 0, me // 2, size - 1 - me // 2)


def ring_device(place, size):
    return jnp.where(place < size // 2, 2 * place, 2 * (size - 1 - place) + 1)


def ring_kernel(size, peers, count, *refs):
    parts, small_ref = refs[:count], refs[count]
    outs, small_out_ref = refs[count + 1 : 2 * count + 1], refs[2 * count + 1]
    slots = refs[2 * count + 2 : 3 * count + 2]
    near_ref, far_ref, send, came, send_out, came_out, small_sems = refs[3 * count + 2 :]
    me, row = lax.axis_index("dp"), lax.axis_index("mp")
    place = ring_place(me, size)
    ways = (
        (place, ring_device((place + 1) % size, size)),
        (size - 1 - place, ring_device((place + size - 1) % size, size)),
    )

    barrier = pltpu.get_barrier_semaphore()

    def greet(t, carry):
        other = (me + t) % size
        pl.semaphore_signal(
            barrier, inc=1, device_id=(other, row), device_id_type=pl.DeviceIdType.MESH
        )
        return carry

    lax.fori_loop(1, size, greet, 0)
    for t in range(1, peers):
        pl.semaphore_signal(
            barrier,
            inc=1,
            device_id=(me, (row + t) % peers),
            device_id_type=pl.DeviceIdType.MESH,
        )
    pl.semaphore_wait(barrier, size - 1 + peers - 1)

    def remote(src, dst, send_sem, recv_sem, device):
        return pltpu.make_async_remote_copy(
            src_ref=src,
            dst_ref=dst,
            send_sem=send_sem,
            recv_sem=recv_sem,
            device_id=device,
            device_id_type=pl.DeviceIdType.MESH,
        )

    def block(i, way, number):
        rows = parts[i].shape[0] // (2 * size)
        start = way * size * rows + number * rows
        return pl.ds(pl.multiple_of(start, 16), rows)

    def near_copy(t):
        return remote(
            small_ref,
            near_ref.at[row],
            small_sems.at[0, t],
            small_sems.at[1, t],
            (me, (row + t) % peers),
        )

    def far_copy(t):
        return remote(
            far_ref.at[me],
            far_ref.at[me],
            small_sems.at[2, t],
            small_sems.at[3, t],
            ((me + t) % size, row),
        )

    for t in range(1, peers):
        near_copy(t).start()
    near_ref[pl.ds(row, 1)] = small_ref[...][None]

    rings = [(i, way) for i in range(count) for way in range(2)]

    def first_copy(i, way, step):
        return remote(
            slots[i].at[way, step - 1],
            slots[i].at[way, step],
            send.at[i, way, step],
            came.at[i, way, step],
            (ways[way][1], row),
        )

    def start_copy(i, way):
        return remote(
            parts[i].at[block(i, way, ways[way][0])],
            slots[i].at[way, 0],
            send.at[i, way, 0],
            came.at[i, way, 0],
            (ways[way][1], row),
        )

    def out_copy(i, way, step):
        span = block(i, way, (ways[way][0] + 1 - step + size) % size)
        return remote(
            outs[i].at[span],
            outs[i].at[span],
            send_out.at[i, way, step],
            came_out.at[i, way, step],
            (ways[way][1], row),
        )

    for i, way in rings:
        start_copy(i, way).start()

    def add_steps(step, carry):
        for i, way in rings:
            start_copy_like = remote(
                slots[i].at[way, step - 1],
                slots[i].at[way, step - 1],
                send.at[i, way, step - 1],
                came.at[i, way, step - 1],
                (ways[way][1], row),
            )
            start_copy_like.wait_recv()
            span = block(i, way, (ways[way][0] - step + size) % size)
            slots[i][way, step - 1] = (
                slots[i][way, step - 1].astype(F32) + parts[i][span].astype(F32)
            ).astype(BF16)
            first_copy(i, way, step).start()
        return carry

    lax.fori_loop(1, size - 1, add_steps, 0)

    for t in range(1, peers):
        near_copy(t).wait_recv()
    total = near_ref[0]
    for k in range(1, peers):
        total = total + near_ref[k]
    far_ref[pl.ds(me, 1)] = total[None]

    def far_start(t, carry):
        far_copy(t).start()
        return carry

    lax.fori_loop(1, size, far_start, 0)

    for i, way in rings:
        remote(
            slots[i].at[way, size - 2],
            slots[i].at[way, size - 2],
            send.at[i, way, size - 2],
            came.at[i, way, size - 2],
            (ways[way][1], row),
        ).wait_recv()
        span = block(i, way, (ways[way][0] + 1) % size)
        outs[i][span] = (
            slots[i][way, size - 2].astype(F32) + parts[i][span].astype(F32)
        ).astype(BF16)
        out_copy(i, way, 0).start()

    def pass_steps(step, carry):
        for i, way in rings:
            out_copy(i, way, step - 1).wait_recv()
            out_copy(i, way, step).start()
        return carry

    lax.fori_loop(1, size - 1, pass_steps, 0)

    def far_wait(t, carry):
        far_copy(t).wait()
        return carry

    lax.fori_loop(1, size, far_wait, 0)

    def far_add(k, total):
        return total + far_ref[k]

    small_out_ref[...] = lax.fori_loop(1, size, far_add, far_ref[0])
    for i, way in rings:
        out_copy(i, way, size - 2).wait_recv()
    for t in range(1, peers):
        near_copy(t).wait_send()

    for i, way in rings:
        start_copy(i, way).wait_send()

    def sent(step, carry):
        for i, way in rings:
            first_copy(i, way, step).wait_send()
        return carry

    lax.fori_loop(1, size - 1, sent, 0)

    def sent_out(step, carry):
        for i, way in rings:
            out_copy(i, way, step).wait_send()
        return carry

    lax.fori_loop(0, size - 1, sent_out, 0)


def ring_sums(size, peers, parts, small):
    grain = 2 * 16 * size
    rows = [p.shape[0] for p in parts]
    parts = [jnp.pad(p, ((0, -p.shape[0] % grain), (0, 0))) for p in parts]
    count = len(parts)
    vmem = pl.BlockSpec(memory_space=pltpu.VMEM)
    steps = pltpu.SemaphoreType.DMA((count, 2, size - 1))
    *sums, small = pl.pallas_call(
        functools.partial(ring_kernel, size, peers, count),
        in_specs=[vmem] * (count + 1),
        out_specs=[vmem] * (count + 1),
        out_shape=[*[shape(p.shape, BF16) for p in parts], shape(small.shape, F32)],
        scratch_shapes=[
            *[
                pltpu.VMEM((2, size - 1, p.shape[0] // (2 * size), p.shape[1]), BF16)
                for p in parts
            ],
            pltpu.VMEM((peers, *small.shape), F32),
            pltpu.VMEM((size, *small.shape), F32),
            steps,
            steps,
            steps,
            steps,
            pltpu.SemaphoreType.DMA((4, max(size, peers))),
        ],
        compiler_params=pltpu.CompilerParams(
            vmem_limit_bytes=VMEM_BYTES, collective_id=0, has_side_effects=True
        ),
        cost_estimate=cost(),
        name="ring_sums",
    )(*parts, small)
    return [total[:r] for total, r in zip(sums, rows)], small


def swap(array, bit, size):
    return lax.ppermute(array, "mp", [(i, i ^ bit) for i in range(size)])


def after(array, *others):
    return lax.optimization_barrier((array, others))[0]


def sum_shares(kept, came, size, tie):
    count = size // 2
    sent = {j: add_share(kept, came, j // 2, count) for j in range(2, size, 4)}
    tie = after(tie, sent)
    shares = {j: add_share(kept, came, j // 2, count) for j in range(0, size, 4)} | sent
    bit = 2
    while bit < size:
        shares = {
            j: add_share(shares[j], swap(shares[j | bit], bit, size), 0, 1)
            for j in shares
            if not j & bit
        }
        bit *= 2
    return shares[0], tie


def shards(
    decoder_rows,
    memory_rows,
    decoder_token_length,
    memory_length,
    bucket_ids,
    relative_bucket_bias,
    self_gain,
    self_query,
    self_key,
    self_value,
    self_out,
    cross_gain,
    cross_query,
    cross_key,
    cross_value,
    cross_out,
    hidden_gain,
    widen_weight,
    narrow_weight,
    layer_cotangent,
):
    dp_size = lax.axis_size("dp")
    mp_size = lax.axis_size("mp")
    me = lax.axis_index("mp")
    doc, features = decoder_rows.shape
    slots = memory_rows.shape[0]
    cols = self_query.shape[1]
    heads = cols // HEAD_DIM
    buckets = relative_bucket_bias.shape[0]
    order = [*range(1, mp_size, 2), *range(0, mp_size, 2)]

    bias_rows = jnp.zeros((TABLE_ROWS, features), BF16)
    bias_rows = bias_rows.at[:heads, :buckets].set(relative_bucket_bias.T)
    own_self = pack(
        (self_query.T, False), (self_key.T, False), (self_value.T, False), (self_out, False), (bias_rows, False)
    )
    own_cross = pack(
        (cross_query.T, False), (cross_key.T, False), (cross_value.T, False), (cross_out, False)
    )
    own_wide = pack((widen_weight, True))
    memory_rows = after(memory_rows, own_cross, own_wide)

    def first_hops(own):
        shares, bit = {0: own}, mp_size // 2
        while bit > 1:
            for j in list(shares):
                shares[j | bit] = swap(shares[j], bit, mp_size)
            bit //= 2
        return shares

    def last_hop(shares, *others):
        shares[1] = swap(shares[0], 1, mp_size)
        for j in range(2, mp_size, 2):
            shares[j] = after(shares[j], *others)
            shares[j | 1] = swap(shares[j], 1, mp_size)
        return [shares[j] for j in order]

    near_self = first_hops(own_self)
    w_self = last_hop(near_self, own_cross, own_wide)
    near_cross = first_hops(own_cross)
    near_wide = first_hops(own_wide)
    near_narrow = first_hops(narrow_weight)
    memory_seen = lax.all_to_all(
        memory_rows.reshape(dp_size, slots // dp_size, features), "dp", 0, 0
    ).reshape(slots, features)

    doc_length = lax.dynamic_index_in_dim(decoder_token_length, me, keepdims=False)
    doc_memory = lax.dynamic_index_in_dim(memory_length, me)
    position = jnp.arange(doc, dtype=jnp.int32)
    allowed = (position[:, None] <= position[None, :]) & (position[:, None] < doc_length)
    ids = jnp.where(allowed, bucket_ids.T, buckets)
    gain_self = self_gain.astype(F32)[None]
    gain_cross = cross_gain.astype(F32)[None]
    gain_hidden = hidden_gain.astype(F32)[None]

    *saved_self, after_self = self_forward(heads, buckets, decoder_rows, gain_self, w_self, ids)
    w_cross = last_hop(near_cross, after_self)
    *saved_cross, after_cross = cross_forward(
        heads, after_self, gain_cross, memory_seen, doc_memory, w_cross
    )

    w_wide, w_narrow = last_hop(near_wide, after_cross), last_hop(near_narrow, after_cross)
    give, keep, layer_output, grad_after_cross, branch, hidden_gain_grad = feed_forward(
        after_cross, gain_hidden, layer_cotangent, w_wide, w_narrow
    )
    part_hidden, branch = sum_shares(keep, swap(give, 1, mp_size), mp_size, branch)

    give, keep, grad_memory, grad_after_self, branch, cross_gain_grad = cross_backward(
        heads,
        after_self,
        gain_cross,
        memory_seen,
        doc_memory,
        branch,
        grad_after_cross,
        saved_cross,
        w_cross,
    )
    memory_grad = lax.all_to_all(
        grad_memory.reshape(dp_size, slots // dp_size, features), "dp", 0, 0
    ).reshape(slots, features)
    came = after(swap(give, 1, mp_size), part_hidden)
    part_cross, branch = sum_shares(keep, came, mp_size, branch)

    give, keep, score_grads, input_grad, self_gain_grad = self_backward(
        heads,
        buckets,
        decoder_rows,
        gain_self,
        ids,
        branch,
        grad_after_self,
        saved_self,
        w_self,
    )
    came = swap(after(give, part_cross), 1, mp_size)
    part_self, score_grads = sum_shares(keep, came, mp_size, score_grads)

    sums = bucket_sums(ids, score_grads, buckets)
    sums = sums.reshape(mp_size, heads, buckets)
    sums = jnp.stack([sums[order.index(j)] for j in range(mp_size)])
    sums = jnp.take(sums, me ^ jnp.arange(mp_size), axis=0)
    gains = jnp.stack([self_gain_grad, cross_gain_grad, hidden_gain_grad]).sum(axis=1)
    small = jnp.concatenate([gains.reshape(-1), sums.reshape(-1)])
    used = small.shape[0]
    small = jnp.pad(small, (0, -used % (8 * LANES))).reshape(-1, LANES)
    (sum_hidden, sum_cross, sum_self), small = ring_sums(
        dp_size,
        mp_size,
        [part.reshape(-1, features) for part in (part_hidden, part_cross, part_self)],
        small,
    )
    wide_grad, narrow_grad, self_grads, cross_grads = finish(sum_hidden, sum_cross, sum_self)
    small = small.reshape(-1)[:used]
    gains = small[: 3 * features].reshape(3, features)
    sums = small[3 * features :].reshape(mp_size, heads, buckets)
    position_grad = lax.dynamic_index_in_dim(sums, me, keepdims=False).T

    return (
        layer_output,
        input_grad,
        memory_grad,
        position_grad,
        gains[0],
        *[grad.T for grad in self_grads[:3]],
        self_grads[3],
        gains[1],
        *[grad.T for grad in cross_grads[:3]],
        cross_grads[3],
        gains[2],
        wide_grad,
        narrow_grad,
    )


def solution(mesh):
    return jax.shard_map(
        shards,
        mesh=mesh,
        in_specs=(
            P(("dp", "mp"), None),
            P(("dp", "mp"), None),
            P("dp"),
            P("dp"),
            P(),
            P(None, "mp"),
            P(),
            P(None, "mp"),
            P(None, "mp"),
            P(None, "mp"),
            P("mp", None),
            P(),
            P(None, "mp"),
            P(None, "mp"),
            P(None, "mp"),
            P("mp", None),
            P(),
            P(None, "mp"),
            P("mp", None),
            P(("dp", "mp"), None),
        ),
        out_specs=(
            P(("dp", "mp"), None),
            P(("dp", "mp"), None),
            P(("dp", "mp"), None),
            P(None, "mp"),
            P(),
            P(None, "mp"),
            P(None, "mp"),
            P(None, "mp"),
            P("mp", None),
            P(),
            P(None, "mp"),
            P(None, "mp"),
            P(None, "mp"),
            P("mp", None),
            P(),
            P(None, "mp"),
            P("mp", None),
        ),
        check_vma=False,
    )
```

```python
import functools

import jax
import jax.numpy as jnp
from jax import lax
from jax.experimental import pallas as pl
from jax.experimental.pallas import tpu as pltpu
from jax.sharding import PartitionSpec as P

HEAD_DIM = 64
NORM_EPS = 1e-06
MASKED = -1e30
SCALE = HEAD_DIM**-0.5
BF16 = jnp.bfloat16
F32 = jnp.float32
LANES = 128
TABLE_ROWS = 16
HEAD_BLOCK = 256
BLOCK_HEADS = HEAD_BLOCK // HEAD_DIM
Q_BLOCK = 256
K_BLOCK = 256
HIDDEN_BLOCK = 256
ROW_BLOCK = 128
VMEM_BYTES = 56 * 1024 * 1024
GELU_ROOT = 0.7978845608028654
GELU_CUBE = 0.044715


def dot_nn(a, b):
    return lax.dot_general(a, b, (((1,), (0,)), ((), ())), preferred_element_type=F32)


def dot_nt(a, b):
    return lax.dot_general(a, b, (((1,), (1,)), ((), ())), preferred_element_type=F32)


def dot_tn(a, b):
    return lax.dot_general(a, b, (((0,), (0,)), ((), ())), preferred_element_type=F32)


def flip(a):
    return a.astype(F32).T.astype(BF16)


def spans(size, step):
    return [slice(i, i + step) for i in range(0, size, step)]


def norm_scale(rows):
    return lax.rsqrt(jnp.mean(rows * rows, axis=-1, keepdims=True) + NORM_EPS)


def norm_into(normed_ref, rows_ref, gain_ref):
    for span in spans(rows_ref.shape[0], ROW_BLOCK):
        rows = rows_ref[span].astype(F32)
        normed_ref[span] = (rows * norm_scale(rows) * gain_ref[...]).astype(BF16)


def norm_back_into(span, grad, out_ref, low_ref, gain_grad_ref, rows_ref, gain_ref, add_ref):
    rows = rows_ref[span].astype(F32)
    scale = norm_scale(rows)
    unit = rows * scale
    grad_unit = grad * gain_ref[...]
    mean = jnp.mean(grad_unit * unit, axis=-1, keepdims=True)
    out = add_ref[span].astype(F32) + scale * (grad_unit - unit * mean)
    out_ref[span] = out
    if low_ref is not None:
        low_ref[span] = out.astype(BF16)
    gain_grad_ref[...] += jnp.sum((grad * unit).reshape(-1, 8, rows.shape[1]), axis=0)


def gelu_and_slope(v):
    square = v * v
    bend = jnp.tanh(GELU_ROOT * (v + GELU_CUBE * v * square))
    half = 0.5 * (1.0 + bend)
    slope = half + 0.5 * v * (1.0 - bend * bend) * GELU_ROOT * (1.0 + 3.0 * GELU_CUBE * square)
    return v * half, slope


def lane_block(start):
    return pl.ds(pl.multiple_of(start, LANES), LANES)


def extra_lanes(rows, allowed):
    lane = lax.broadcasted_iota(jnp.int32, (rows, LANES), 1) % HEAD_DIM
    first = MASKED if allowed is None else jnp.where(allowed, 0.0, MASKED)
    return jnp.where(lane == 0, first, jnp.where(lane < 4, 1.0, 0.0)).astype(BF16)


def pick(which, block, other):
    lane = lax.broadcasted_iota(jnp.int32, block.shape, 1)
    return jnp.where((lane < HEAD_DIM) == (which == 0), block, other)


def half_rows(which):
    return slice(which * HEAD_DIM, (which + 1) * HEAD_DIM)


def split(values):
    high = values.astype(BF16).astype(F32)
    rest = values - high
    middle = rest.astype(BF16).astype(F32)
    return high, middle, rest - middle


def with_extra(which, block_t, masked, minus):
    columns = block_t.shape[1]
    row = lax.broadcasted_iota(jnp.int32, (HEAD_DIM, columns), 0)
    extra = jnp.where(row == 0, 1.0 if masked else 0.0, 0.0)
    if minus is not None:
        for i, part in enumerate(split(minus)):
            extra = jnp.where(row == i + 1, -part, extra)
    own = block_t[half_rows(which)]
    return jnp.concatenate([own, extra] if which == 0 else [extra, own], axis=0).astype(BF16)


def bias_block(table_ref, ids_ref, index, rows, start):
    row = jnp.broadcast_to(table_ref[pl.ds(index, 1), :], (rows, LANES))
    return jnp.concatenate(
        [
            jnp.take_along_axis(row, ids_ref[:rows, c : c + LANES], axis=1)
            for c in range(start, start + Q_BLOCK, LANES)
        ],
        axis=1,
    )


class Stack:
    def __init__(self, sources, stack_ref, sems, kinds, rows):
        features = stack_ref.shape[0] // kinds
        self.copies = [
            [
                pltpu.make_async_copy(
                    source.at[pl.ds(kind * rows, rows)],
                    stack_ref.at[pl.ds(kind * features + p * rows, rows)],
                    sems.at[p, kind],
                )
                for p, source in enumerate(sources)
            ]
            for kind in range(kinds)
        ]

    def start(self):
        for copies in self.copies:
            for copy in copies:
                copy.start()

    def wait(self, *kinds):
        for kind in kinds:
            for copy in self.copies[kind]:
                copy.wait()


def table_copies(sources, tables_ref, sems, kinds):
    start = sources[0].shape[0] - TABLE_ROWS
    return [
        pltpu.make_async_copy(
            source.at[pl.ds(start, TABLE_ROWS)], tables_ref.at[p], sems.at[p, kinds]
        )
        for p, source in enumerate(sources)
    ]


def table_into(table_ref, tables_ref, heads, buckets):
    for p in range(tables_ref.shape[0]):
        rows = tables_ref[p, :, :LANES].astype(F32)
        lane = lax.broadcasted_iota(jnp.int32, rows.shape, 1)
        rows = jnp.where(lane < buckets, rows, MASKED)
        for h in range(heads):
            table_ref[p * heads + h : p * heads + h + 1, :] = rows[h : h + 1, :]


def self_forward_kernel(heads, buckets, shares, rows_ref, gain_ref, ids_ref, *refs):
    sources = refs[:shares]
    q_ref, k_ref, v_ref, mixed_ref, lse_ref, out_ref = refs[shares : shares + 6]
    w_ref, tables_ref, table_ref, normed_ref, sems = refs[shares + 6 :]
    step = pl.program_id(0)
    doc, features = rows_ref.shape
    stack = Stack(sources, w_ref, sems, 4, heads * HEAD_DIM)

    @pl.when(step == 0)
    def _():
        stack.start()
        tables = table_copies(sources, tables_ref, sems, 4)
        for copy in tables:
            copy.start()
        norm_into(normed_ref, rows_ref, gain_ref)
        out_ref[...] = rows_ref[...].astype(F32)
        for copy in tables:
            copy.wait()
        table_into(table_ref, tables_ref, heads, buckets)
        stack.wait(0, 1, 2, 3)

    def weights(kind):
        start = pl.multiple_of(kind * features + step * HEAD_BLOCK, HEAD_BLOCK)
        return w_ref[pl.ds(start, HEAD_BLOCK)]

    for kind, ref in enumerate((q_ref, k_ref, v_ref)):
        ref[...] = dot_nt(normed_ref[...], weights(kind)).astype(BF16)
    none = jnp.zeros((doc, LANES), BF16)
    for pair in range(BLOCK_HEADS // 2):
        lanes = slice(pair * LANES, (pair + 1) * LANES)
        k, v_t = k_ref[:, lanes], flip(v_ref[:, lanes])
        q_t = flip(q_ref[:, lanes].astype(F32) * SCALE)
        k_of = [pick(which, k, none) for which in range(2)]
        for span in spans(doc, Q_BLOCK):
            rows, mixed = span.stop, []
            for which in range(2):
                h = 2 * pair + which
                s = dot_nn(k_of[which][:rows], q_t[:, span])
                s = s + bias_block(table_ref, ids_ref, step * BLOCK_HEADS + h, rows, span.start)
                top = jnp.max(s, axis=0, keepdims=True)
                p = jnp.exp(s - top)
                total = jnp.sum(p, axis=0, keepdims=True)
                mixed.append(dot_nn(v_t[half_rows(which), :rows], p.astype(BF16)) / total)
                lse_ref[0, h : h + 1, span] = top + jnp.log(total)
            mixed_ref[span, lanes] = jnp.concatenate(mixed, axis=0).T.astype(BF16)
    out_ref[...] += dot_nn(mixed_ref[...], weights(3))


def self_backward_kernel(heads, buckets, shares, *refs):
    rows_ref, gain_ref, ids_ref, branch_ref, add_ref = refs[:5]
    q_ref, k_ref, v_ref, mixed_ref, lse_ref = refs[5:10]
    sources = refs[10 : 10 + shares]
    give_ref, keep_ref, ds_ref, out_ref, gain_grad_ref = refs[10 + shares : 15 + shares]
    w_ref, tables_ref, table_ref, normed_ref, g_ref, grad_ref, sems = refs[15 + shares :]
    step = pl.program_id(0)
    doc, features = rows_ref.shape
    half = features // 2
    stack = Stack(sources, w_ref, sems, 4, heads * HEAD_DIM)

    @pl.when(step == 0)
    def _():
        stack.start()
        tables = table_copies(sources, tables_ref, sems, 4)
        for copy in tables:
            copy.start()
        norm_into(normed_ref, rows_ref, gain_ref)
        for copy in tables:
            copy.wait()
        table_into(table_ref, tables_ref, heads, buckets)
        stack.wait(3)

    start = pl.multiple_of(3 * features + step * HEAD_BLOCK, HEAD_BLOCK)
    g_ref[...] = dot_nt(branch_ref[...], w_ref[pl.ds(start, HEAD_BLOCK)]).astype(BF16)
    none = jnp.zeros((doc, LANES), BF16)
    ones = extra_lanes(doc, None)
    for pair in range(BLOCK_HEADS // 2):
        lanes = lane_block(step * HEAD_BLOCK + pair * LANES)
        q, k, v = q_ref[:, lanes], k_ref[:, lanes], v_ref[:, lanes]
        g = g_ref[:, pair * LANES : (pair + 1) * LANES]
        q_t, k_t = q.astype(F32).T * SCALE, flip(k)
        g_t = g.astype(F32).T
        inner = g_t * mixed_ref[:, lanes].astype(F32).T
        per_head = []
        for which in range(2):
            h = 2 * pair + which
            minus = jnp.sum(inner[half_rows(which)], axis=0, keepdims=True)
            per_head.append(
                (
                    pick(which, k, ones),
                    pick(which, v, ones),
                    with_extra(which, q_t, False, lse_ref[0, h : h + 1, :]),
                    with_extra(which, g_t, False, minus),
                    pick(which, q, none),
                    pick(which, g, none),
                )
            )
        grad_k = grad_v = None
        for span in spans(doc, Q_BLOCK):
            rows, grad_q, part_k, part_v = span.stop, [], None, None
            for which, (k_of, v_of, q_with, g_with, q_of, g_of) in enumerate(per_head):
                h = 2 * pair + which
                s = dot_nn(k_of[:rows], q_with[:, span])
                s = s + bias_block(table_ref, ids_ref, step * BLOCK_HEADS + h, rows, span.start)
                p = jnp.exp(s)
                ds = (p * dot_nn(v_of[:rows], g_with[:, span])).astype(BF16)
                ds_ref[h, :rows, span] = ds
                grad_q.append(dot_nn(k_t[half_rows(which), :rows], ds))
                to_v = dot_nn(p.astype(BF16), g_of[span])
                to_k = dot_nn(ds, q_of[span])
                part_v = to_v if part_v is None else part_v + to_v
                part_k = to_k if part_k is None else part_k + to_k
            grad_q = (jnp.concatenate(grad_q, axis=0) * SCALE).T
            grad_ref[0, span, lanes] = grad_q.astype(BF16)
            if grad_v is not None:
                part_v = jnp.concatenate(
                    [part_v[: span.start] + grad_v, part_v[span.start :]], axis=0
                )
                part_k = jnp.concatenate(
                    [part_k[: span.start] + grad_k, part_k[span.start :]], axis=0
                )
            grad_v, grad_k = part_v, part_k
        grad_ref[1, :, lanes] = (grad_k * SCALE).astype(BF16)
        grad_ref[2, :, lanes] = grad_v.astype(BF16)

    @pl.when(step == pl.num_programs(0) - 1)
    def _():
        stack.wait(0, 1, 2)
        for ref, columns in ((give_ref, slice(0, half)), (keep_ref, slice(half, features))):
            for kind in range(3):
                ref[kind] = dot_tn(grad_ref[kind, :, columns], normed_ref[...]).astype(BF16)
            ref[3] = dot_tn(mixed_ref[:, columns], branch_ref[...]).astype(BF16)
        gain_grad_ref[...] = jnp.zeros_like(gain_grad_ref)
        for span in spans(doc, ROW_BLOCK):
            back = dot_nn(grad_ref[0, span], w_ref[:features])
            back = back + dot_nn(grad_ref[1, span], w_ref[features : 2 * features])
            back = back + dot_nn(grad_ref[2, span], w_ref[2 * features : 3 * features])
            norm_back_into(
                span, back, out_ref, None, gain_grad_ref, rows_ref, gain_ref, add_ref
            )


def cross_forward_kernel(heads, shares, length_ref, rows_ref, gain_ref, memory_ref, *refs):
    sources = refs[:shares]
    q_ref, k_ref, v_ref, mixed_ref, lse_ref, out_ref = refs[shares : shares + 6]
    w_ref, normed_ref, extra_ref, p_ref, sems = refs[shares + 6 :]
    step = pl.program_id(0)
    (doc, features), slots = rows_ref.shape, memory_ref.shape[0]
    stack = Stack(sources, w_ref, sems, 4, heads * HEAD_DIM)

    @pl.when(step == 0)
    def _():
        stack.start()
        norm_into(normed_ref, rows_ref, gain_ref)
        out_ref[...] = rows_ref[...]
        slot = lax.broadcasted_iota(jnp.int32, (slots, LANES), 0)
        extra_ref[...] = extra_lanes(slots, slot < length_ref[0])
        stack.wait(0, 1, 2, 3)

    def weights(kind):
        start = pl.multiple_of(kind * features + step * HEAD_BLOCK, HEAD_BLOCK)
        return w_ref[pl.ds(start, HEAD_BLOCK)]

    q_ref[...] = dot_nt(normed_ref[...], weights(0)).astype(BF16)
    k_ref[...] = dot_nt(memory_ref[...], weights(1)).astype(BF16)
    v_ref[...] = dot_nt(memory_ref[...], weights(2)).astype(BF16)

    units = [
        (pair, which, span)
        for pair in range(BLOCK_HEADS // 2)
        for span in spans(doc, Q_BLOCK)
        for which in range(2)
    ]
    v_t = [flip(v_ref[:, p * LANES : (p + 1) * LANES]) for p in range(BLOCK_HEADS // 2)]
    q_t = [
        q_ref[:, p * LANES : (p + 1) * LANES].astype(F32).T * SCALE
        for p in range(BLOCK_HEADS // 2)
    ]

    def scores(unit):
        pair, which, span = unit
        q_with = with_extra(which, q_t[pair][:, span], True, None)
        k_of = pick(which, k_ref[:, pair * LANES : (pair + 1) * LANES], extra_ref[...])
        return [dot_nn(k_of[rows], q_with) for rows in spans(slots, K_BLOCK)]

    mixed = {}
    ahead = scores(units[0])
    for i, (pair, which, span) in enumerate(units):
        s, slot = ahead, i % 2
        if i + 1 < len(units):
            ahead = scores(units[i + 1])
        top = functools.reduce(jnp.maximum, [jnp.max(c, axis=0, keepdims=True) for c in s])
        total = None
        for rows, chunk in zip(spans(slots, K_BLOCK), s):
            p = jnp.exp(chunk - top)
            part = jnp.sum(p, axis=0, keepdims=True)
            total = part if total is None else total + part
            p_ref[slot, rows] = p.astype(BF16)
        h = 2 * pair + which
        lse_ref[0, h : h + 1, span] = top + jnp.log(total)
        mixed[which] = dot_nn(v_t[pair][half_rows(which)], p_ref[slot]) / total
        if which == 1:
            out = jnp.concatenate([mixed[0], mixed[1]], axis=0).T
            mixed_ref[span, pair * LANES : (pair + 1) * LANES] = out.astype(BF16)
    out_ref[...] += dot_nn(mixed_ref[...], weights(3))


def cross_backward_kernel(heads, shares, length_ref, *refs):
    rows_ref, gain_ref, memory_ref, branch_ref, add_ref = refs[:5]
    q_ref, k_ref, v_ref, mixed_ref, lse_ref = refs[5:10]
    sources = refs[10 : 10 + shares]
    give_ref, keep_ref, memory_out_ref, out_ref, low_ref, gain_grad_ref = refs[
        10 + shares : 16 + shares
    ]
    w_ref, normed_ref, extra_ref, g_ref, grad_q_ref, grad_ref, ds_ref, sems = refs[16 + shares :]
    step = pl.program_id(0)
    (doc, features), slots = rows_ref.shape, memory_ref.shape[0]
    half = features // 2
    stack = Stack(sources, w_ref, sems, 4, heads * HEAD_DIM)

    @pl.when(step == 0)
    def _():
        stack.start()
        norm_into(normed_ref, rows_ref, gain_ref)
        slot = lax.broadcasted_iota(jnp.int32, (slots, LANES), 0)
        extra_ref[...] = extra_lanes(slots, slot < length_ref[0])
        stack.wait(3)

    start = pl.multiple_of(3 * features + step * HEAD_BLOCK, HEAD_BLOCK)
    g_ref[...] = dot_nt(branch_ref[...], w_ref[pl.ds(start, HEAD_BLOCK)]).astype(BF16)
    none = jnp.zeros((doc, LANES), BF16)
    for pair in range(BLOCK_HEADS // 2):
        local = slice(pair * LANES, (pair + 1) * LANES)
        lanes = lane_block(step * HEAD_BLOCK + pair * LANES)
        v_lanes = lane_block(features + step * HEAD_BLOCK + pair * LANES)
        q, g = q_ref[:, lanes], g_ref[:, local]
        q_t, g_t = q.astype(F32).T * SCALE, g.astype(F32).T
        inner = g_t * mixed_ref[:, lanes].astype(F32).T
        per_head = []
        for which in range(2):
            h = 2 * pair + which
            minus = jnp.sum(inner[half_rows(which)], axis=0, keepdims=True)
            per_head.append(
                (
                    with_extra(which, q_t, True, lse_ref[0, h : h + 1, :]),
                    with_extra(which, g_t, False, minus),
                    pick(which, q, none),
                    pick(which, g, none),
                )
            )
        for rows in spans(slots, K_BLOCK):
            k, v, extra = k_ref[rows, local], v_ref[rows, local], extra_ref[rows]
            part_k = part_v = None
            for which, (q_with, g_with, q_of, g_of) in enumerate(per_head):
                p = jnp.exp(dot_nn(pick(which, k, extra), q_with))
                ds = (p * dot_nn(pick(which, v, extra), g_with)).astype(BF16)
                ds_ref[which, rows] = ds
                to_v = dot_nn(p.astype(BF16), g_of)
                to_k = dot_nn(ds, q_of)
                part_v = to_v if part_v is None else part_v + to_v
                part_k = to_k if part_k is None else part_k + to_k
            grad_ref[rows, lanes] = (part_k * SCALE).astype(BF16)
            grad_ref[rows, v_lanes] = part_v.astype(BF16)
        k_t = flip(k_ref[:, local])
        grad_q = [dot_nn(k_t[half_rows(which)], ds_ref[which]) for which in range(2)]
        grad_q_ref[:, lanes] = (jnp.concatenate(grad_q, axis=0) * SCALE).T.astype(BF16)

    @pl.when(step == pl.num_programs(0) - 1)
    def _():
        stack.wait(0, 1, 2)
        for ref, first in ((give_ref, 0), (keep_ref, half)):
            columns = slice(first, first + half)
            v_columns = slice(features + first, features + first + half)
            ref[0] = dot_tn(grad_q_ref[:, columns], normed_ref[...]).astype(BF16)
            ref[1] = dot_tn(grad_ref[:, columns], memory_ref[...]).astype(BF16)
            ref[2] = dot_tn(grad_ref[:, v_columns], memory_ref[...]).astype(BF16)
            ref[3] = dot_tn(mixed_ref[:, columns], branch_ref[...]).astype(BF16)
        gain_grad_ref[...] = jnp.zeros_like(gain_grad_ref)
        for span in spans(doc, ROW_BLOCK):
            back = dot_nn(grad_q_ref[span], w_ref[:features])
            norm_back_into(
                span, back, out_ref, low_ref, gain_grad_ref, rows_ref, gain_ref, add_ref
            )
        for rows in spans(slots, K_BLOCK):
            memory_out_ref[rows] = dot_nn(
                grad_ref[rows], w_ref[features : 3 * features]
            ).astype(BF16)


def feed_forward_kernel(first, last, rows_ref, gain_ref, cotangent_ref, *refs):
    sources, refs = refs[:2], refs[2:]
    if not first:
        (layer_in_ref, back_in_ref), refs = refs[:2], refs[2:]
    give_ref, keep_ref, layer_ref, out_ref = refs[:4]
    if last:
        low_ref, gain_grad_ref = refs[4:6]
        refs = refs[2:]
    (
        wide_ref,
        narrow_ref,
        normed_ref,
        normed_t,
        cotangent_t,
        active_ref,
        grad_ref,
        sems,
    ) = refs[4:]
    step, steps = pl.program_id(0), pl.num_programs(0)
    doc = rows_ref.shape[0]
    hidden = sources[0].shape[0] // 2
    copies = [
        [
            pltpu.make_async_copy(
                source.at[pl.ds(kind * hidden, hidden)],
                stack.at[pl.ds(p * hidden, hidden)],
                sems.at[p, kind],
            )
            for kind, stack in enumerate((wide_ref, narrow_ref))
        ]
        for p, source in enumerate(sources)
    ]

    @pl.when(step == 0)
    def _():
        for pair in copies:
            for copy in pair:
                copy.start()
        norm_into(normed_ref, rows_ref, gain_ref)
        for span in spans(doc, ROW_BLOCK):
            normed_t[:, span] = flip(normed_ref[span])
            cotangent_t[:, span] = flip(cotangent_ref[span])

    for p, pair in enumerate(copies):

        @pl.when(step == p * (hidden // HIDDEN_BLOCK))
        def _(pair=pair):
            for copy in pair:
                copy.wait()

    units = pl.ds(pl.multiple_of(step * HIDDEN_BLOCK, HIDDEN_BLOCK), HIDDEN_BLOCK)
    activated, slope = gelu_and_slope(dot_nn(wide_ref[units], normed_t[...]))
    active_ref[units] = activated.astype(BF16)
    grad_ref[units] = (dot_nn(narrow_ref[units], cotangent_t[...]) * slope).astype(BF16)

    def store(ref):
        ref[0] = dot_nn(grad_ref[units], normed_ref[...]).astype(BF16)
        ref[1] = dot_nn(active_ref[units], cotangent_ref[...]).astype(BF16)

    @pl.when(step < steps // 2)
    def _():
        store(give_ref)

    @pl.when(step >= steps // 2)
    def _():
        store(keep_ref)

    @pl.when(step == steps - 1)
    def _():
        if last:
            gain_grad_ref[...] = jnp.zeros_like(gain_grad_ref)
        for span in spans(doc, ROW_BLOCK):
            layer = rows_ref[span] if first else layer_in_ref[span]
            layer = layer + dot_tn(active_ref[:, span], narrow_ref[...])
            layer_ref[span] = layer.astype(layer_ref.dtype)
            back = dot_tn(grad_ref[:, span], wide_ref[...])
            if not first:
                back = back + back_in_ref[span]
            if last:
                norm_back_into(
                    span, back, out_ref, low_ref, gain_grad_ref, rows_ref, gain_ref, cotangent_ref
                )
            else:
                out_ref[span] = back


def pack_kernel(flipped, *refs):
    out_ref, start = refs[-1], 0
    for source, turn in zip(refs[:-1], flipped):
        rows = source.shape[1] if turn else source.shape[0]
        span = slice(start, start + rows)
        out_ref[span] = flip(source[...]) if turn else source[...]
        start += rows


def finish_kernel(hidden_ref, cross_ref, self_ref, wide_ref, narrow_ref, *outs):
    hidden = narrow_ref.shape[0]
    for span in spans(hidden, ROW_BLOCK):
        wide_ref[:, span] = hidden_ref[span].astype(F32).T
        narrow_ref[span] = hidden_ref[hidden + span.start : hidden + span.stop].astype(F32)
    rows = outs[0].shape[0]
    for source, refs in ((self_ref, outs[:4]), (cross_ref, outs[4:])):
        for kind, ref in enumerate(refs):
            ref[...] = source[kind * rows : (kind + 1) * rows].astype(F32)


def params():
    return pltpu.CompilerParams(vmem_limit_bytes=VMEM_BYTES)


def cost():
    return pl.CostEstimate(flops=1 << 20, bytes_accessed=1 << 16, transcendentals=0)


def shape(dims, dtype):
    return jax.ShapeDtypeStruct(dims, dtype)


def whole(array):
    return pl.BlockSpec(
        array.shape, lambda *_: (0,) * len(array.shape), pipeline_mode=pl.Buffered(1)
    )


def result(array):
    return pl.BlockSpec(array.shape, lambda *_: (0,) * len(array.shape))


def columns(rows):
    return pl.BlockSpec((rows, HEAD_BLOCK), lambda i: (0, i))


def anywhere(arrays):
    return [pl.BlockSpec(memory_space=pl.ANY) for _ in arrays]


SCALAR = pl.BlockSpec(memory_space=pltpu.SMEM)


def call(kernel, name, grid, in_specs, out_specs, out_shape, scratch, args):
    return pl.pallas_call(
        kernel,
        grid=grid,
        in_specs=in_specs,
        out_specs=out_specs,
        out_shape=out_shape,
        scratch_shapes=scratch,
        compiler_params=params(),
        cost_estimate=cost(),
        name=name,
    )(*args)


def pack(*parts):
    arrays, flipped = zip(*parts)
    rows = sum(a.shape[1] if turn else a.shape[0] for a, turn in parts)
    features = arrays[0].shape[0] if flipped[0] else arrays[0].shape[1]
    return pl.pallas_call(
        functools.partial(pack_kernel, flipped),
        out_shape=shape((rows, features), BF16),
        compiler_params=params(),
        cost_estimate=cost(),
        name="pack",
    )(*arrays)


def self_forward(heads, buckets, rows, gain, weights, ids):
    doc, features = rows.shape
    shares, steps = len(weights), features // HEAD_BLOCK
    narrow, tall = shape((doc, features), BF16), shape((doc, features), F32)
    out_shape = (*[narrow] * 4, shape((steps, 8, doc), F32), tall)
    return call(
        functools.partial(self_forward_kernel, heads, buckets, shares),
        "self_forward",
        (steps,),
        [whole(rows), whole(gain), whole(ids), *anywhere(weights)],
        (*[columns(doc)] * 4, pl.BlockSpec((1, 8, doc), lambda i: (i, 0, 0)), result(tall)),
        out_shape,
        [
            pltpu.VMEM((4 * features, features), BF16),
            pltpu.VMEM((shares, TABLE_ROWS, features), BF16),
            pltpu.VMEM((TABLE_ROWS, LANES), F32),
            pltpu.VMEM((doc, features), BF16),
            pltpu.SemaphoreType.DMA((shares, 5)),
        ],
        (rows, gain, ids, *weights),
    )


def self_backward(heads, buckets, rows, gain, ids, branch, add, saved, weights):
    doc, features = rows.shape
    shares, steps = len(weights), features // HEAD_BLOCK
    packed = shape((4, features // 2, features), BF16)
    out_shape = (
        packed,
        packed,
        shape((steps * BLOCK_HEADS, doc, doc), BF16),
        shape((doc, features), F32),
        shape((8, features), F32),
    )
    *arrays, lse = saved
    return call(
        functools.partial(self_backward_kernel, heads, buckets, shares),
        "self_backward",
        (steps,),
        [
            *[whole(a) for a in (rows, gain, ids, branch, add, *arrays)],
            pl.BlockSpec((1, 8, doc), lambda i: (i, 0, 0)),
            *anywhere(weights),
        ],
        (
            result(packed),
            result(packed),
            pl.BlockSpec((BLOCK_HEADS, doc, doc), lambda i: (i, 0, 0)),
            result(out_shape[3]),
            result(out_shape[4]),
        ),
        out_shape,
        [
            pltpu.VMEM((4 * features, features), BF16),
            pltpu.VMEM((shares, TABLE_ROWS, features), BF16),
            pltpu.VMEM((TABLE_ROWS, LANES), F32),
            pltpu.VMEM((doc, features), BF16),
            pltpu.VMEM((doc, HEAD_BLOCK), BF16),
            pltpu.VMEM((3, doc, features), BF16),
            pltpu.SemaphoreType.DMA((shares, 5)),
        ],
        (rows, gain, ids, branch, add, *arrays, lse, *weights),
    )


def cross_forward(heads, rows, gain, memory, length, weights):
    (doc, features), slots = rows.shape, memory.shape[0]
    shares, steps = len(weights), features // HEAD_BLOCK
    query, key = shape((doc, features), BF16), shape((slots, features), BF16)
    tall = shape((doc, features), F32)
    return call(
        functools.partial(cross_forward_kernel, heads, shares),
        "cross_forward",
        (steps,),
        [SCALAR, whole(rows), whole(gain), whole(memory), *anywhere(weights)],
        (
            columns(doc),
            columns(slots),
            columns(slots),
            columns(doc),
            pl.BlockSpec((1, 8, doc), lambda i: (i, 0, 0)),
            result(tall),
        ),
        (query, key, key, query, shape((steps, 8, doc), F32), tall),
        [
            pltpu.VMEM((4 * features, features), BF16),
            pltpu.VMEM((doc, features), BF16),
            pltpu.VMEM((slots, LANES), BF16),
            pltpu.VMEM((2, slots, Q_BLOCK), BF16),
            pltpu.SemaphoreType.DMA((shares, 4)),
        ],
        (length, rows, gain, memory, *weights),
    )


def cross_backward(heads, rows, gain, memory, length, branch, add, saved, weights):
    (doc, features), slots = rows.shape, memory.shape[0]
    shares, steps = len(weights), features // HEAD_BLOCK
    packed = shape((4, features // 2, features), BF16)
    out_shape = (
        packed,
        packed,
        shape((slots, features), BF16),
        shape((doc, features), F32),
        shape((doc, features), BF16),
        shape((8, features), F32),
    )
    query, key, value, mixed, lse = saved
    return call(
        functools.partial(cross_backward_kernel, heads, shares),
        "cross_backward",
        (steps,),
        [
            SCALAR,
            *[whole(a) for a in (rows, gain, memory, branch, add, query)],
            columns(slots),
            columns(slots),
            whole(mixed),
            pl.BlockSpec((1, 8, doc), lambda i: (i, 0, 0)),
            *anywhere(weights),
        ],
        tuple(result(o) for o in out_shape),
        out_shape,
        [
            pltpu.VMEM((4 * features, features), BF16),
            pltpu.VMEM((doc, features), BF16),
            pltpu.VMEM((slots, LANES), BF16),
            pltpu.VMEM((doc, HEAD_BLOCK), BF16),
            pltpu.VMEM((doc, features), BF16),
            pltpu.VMEM((slots, 2 * features), BF16),
            pltpu.VMEM((2, slots, doc), BF16),
            pltpu.SemaphoreType.DMA((shares, 4)),
        ],
        (length, rows, gain, memory, branch, add, *saved, *weights),
    )


def feed_forward(rows, gain, cotangent, weights, before, last):
    (doc, features), shares = rows.shape, len(weights)
    hidden = weights[0].shape[0] // 2 * shares
    steps = hidden // HIDDEN_BLOCK
    half = steps // 2
    packed, tall = shape((2, hidden // 2, features), BF16), shape((doc, features), F32)
    low = shape((doc, features), BF16)
    rest = [low, tall, low, shape((8, features), F32)] if last else [tall, tall]
    block = (2, HIDDEN_BLOCK, features)
    return call(
        functools.partial(feed_forward_kernel, not before, last),
        "feed_forward",
        (steps,),
        [
            whole(rows),
            whole(gain),
            whole(cotangent),
            *anywhere(weights),
            *[whole(b) for b in before],
        ],
        (
            pl.BlockSpec(block, lambda i: (0, jnp.minimum(i, half - 1), 0)),
            pl.BlockSpec(block, lambda i: (0, jnp.maximum(i - half, 0), 0)),
            *[result(o) for o in rest],
        ),
        (packed, packed, *rest),
        [
            pltpu.VMEM((hidden, features), BF16),
            pltpu.VMEM((hidden, features), BF16),
            pltpu.VMEM((doc, features), BF16),
            pltpu.VMEM((features, doc), BF16),
            pltpu.VMEM((features, doc), BF16),
            pltpu.VMEM((hidden, doc), BF16),
            pltpu.VMEM((hidden, doc), BF16),
            pltpu.SemaphoreType.DMA((shares, 2)),
        ],
        (rows, gain, cotangent, *weights, *before),
    )


def finish(sum_hidden, sum_cross, sum_self):
    rows, features = sum_self.shape
    hidden, part = sum_hidden.shape[0] // 2, shape((rows // 4, features), F32)
    wide, narrow, *parts = pl.pallas_call(
        finish_kernel,
        out_shape=[
            shape((features, hidden), F32),
            shape((hidden, features), F32),
            *[part] * 8,
        ],
        compiler_params=params(),
        cost_estimate=cost(),
        name="finish",
    )(sum_hidden, sum_cross, sum_self)
    return wide, narrow, parts[:4], parts[4:]


def ring_place(me, size):
    return jnp.where(me % 2 == 0, me // 2, size - 1 - me // 2)


def ring_device(place, size):
    return jnp.where(place < size // 2, 2 * place, 2 * (size - 1 - place) + 1)


def differing(row, bit):
    return row + bit - 2 * bit * ((row // bit) % 2)


def share_place(row, other, peers):
    j, bit = 0, 1
    while bit < peers:
        j = j + bit * ((row // bit + other // bit) % 2)
        bit *= 2
    return (j % 2) * (j // 2) + (1 - j % 2) * (peers // 2 + j // 2)


def tail_kernel(size, peers, buckets, heads, *refs):
    hidden_ref, cross_ref, give_ref, keep_ref, ids_ref, ds_ref, *gain_refs = refs[:9]
    outs, small_out_ref = refs[9:12], refs[12]
    slots = refs[13:16]
    kept_ref, came_ref, folded_ref, far_came_ref, part_ref, scores_ref, bucket_ref = refs[16:23]
    small_ref, near_ref, far_ref = refs[23:26]
    send, came, send_out, came_out, small_sems, hop_sems, local_sems = refs[26:]
    parts = (hidden_ref, cross_ref, part_ref)
    me, row = lax.axis_index("dp"), lax.axis_index("mp")
    place = ring_place(me, size)
    ways = (
        (place, ring_device((place + 1) % size, size)),
        (size - 1 - place, ring_device((place + size - 1) % size, size)),
    )
    doc = ids_ref.shape[0]
    mesh = pl.DeviceIdType.MESH

    load_scores = pltpu.make_async_copy(ds_ref, scores_ref, local_sems.at[0])
    load_kept = pltpu.make_async_copy(keep_ref, kept_ref, local_sems.at[1])
    load_scores.start()
    load_kept.start()

    barrier = pltpu.get_barrier_semaphore()

    def greet(t, carry):
        pl.semaphore_signal(
            barrier, inc=1, device_id=((me + t) % size, row), device_id_type=mesh
        )
        return carry

    lax.fori_loop(1, size, greet, 0)
    for t in range(1, peers):
        pl.semaphore_signal(
            barrier, inc=1, device_id=(me, (row + t) % peers), device_id_type=mesh
        )
    pl.semaphore_wait(barrier, size - 1 + peers - 1)

    def remote(src, dst, send_sem, recv_sem, device):
        return pltpu.make_async_remote_copy(
            src_ref=src,
            dst_ref=dst,
            send_sem=send_sem,
            recv_sem=recv_sem,
            device_id=device,
            device_id_type=mesh,
        )

    def block(i, way, number):
        rows = parts[i].shape[0] // (2 * size)
        return pl.ds(pl.multiple_of((way * size + number) * rows, 16), rows)

    def first_copy(i, way):
        return remote(
            parts[i].at[block(i, way, ways[way][0])],
            slots[i].at[way, 0],
            send.at[i, way, 0],
            came.at[i, way, 0],
            (ways[way][1], row),
        )

    def next_copy(i, way, step):
        return remote(
            slots[i].at[way, step - 1],
            slots[i].at[way, step],
            send.at[i, way, step],
            came.at[i, way, step],
            (ways[way][1], row),
        )

    def wait_came(i, way, step):
        remote(
            slots[i].at[way, step],
            slots[i].at[way, step],
            send.at[i, way, step],
            came.at[i, way, step],
            (ways[way][1], row),
        ).wait_recv()

    def out_copy(i, way, step):
        span = block(i, way, (ways[way][0] + 1 - step + size) % size)
        return remote(
            outs[i].at[span],
            outs[i].at[span],
            send_out.at[i, way, step],
            came_out.at[i, way, step],
            (ways[way][1], row),
        )

    def begin(rings):
        for i, way in rings:
            first_copy(i, way).start()

    def plus_part(i, way, step):
        span = block(i, way, (ways[way][0] - step - 1 + size) % size)
        total = slots[i][way, step].astype(F32) + parts[i][span].astype(F32)
        return span, total.astype(BF16)

    def advance(rings, step):
        for i, way in rings:
            wait_came(i, way, step - 1)
            slots[i][way, step - 1] = plus_part(i, way, step - 1)[1]
            next_copy(i, way, step).start()

    def turn(rings):
        for i, way in rings:
            wait_came(i, way, size - 2)
            span, total = plus_part(i, way, size - 2)
            outs[i][span] = total
            out_copy(i, way, 0).start()

    def pass_on(rings, step):
        for i, way in rings:
            out_copy(i, way, step - 1).wait_recv()
            out_copy(i, way, step).start()

    early, late = [(i, way) for i in (0, 1) for way in (0, 1)], [(2, 0), (2, 1)]

    other_core = remote(
        give_ref, came_ref, hop_sems.at[0, 0], hop_sems.at[0, 1], (me, differing(row, 1))
    )
    other_core.start()
    begin(early)

    rows_used, per_row = bucket_ref.shape[0], ds_ref.shape[0] // bucket_ref.shape[0]
    units = rows_used * buckets
    per_round = -(-units // max(2 * (size - 2), 1))

    def bucket_unit(u, carry):
        r, b = u // buckets, u % buckets
        sums = [jnp.zeros((8, LANES), F32) for _ in range(per_row)]
        for c in range(0, doc, LANES):
            hit = ids_ref[: c + LANES, c : c + LANES] == b
            for h in range(per_row):
                grads = scores_ref[r * per_row + h, : c + LANES, c : c + LANES].astype(F32)
                kept = jnp.where(hit, grads, 0.0).reshape(-1, 8, LANES)
                sums[h] = sums[h] + jnp.sum(kept, axis=0)
        for h in range(per_row):
            bucket_ref[r, h, pl.ds(b, 1), :] = jnp.sum(sums[h], axis=0, keepdims=True)
        return carry

    def bucket_round(k):
        low = jnp.minimum(k * per_round, units)
        lax.fori_loop(low, jnp.minimum(low + per_round, units), bucket_unit, 0)

    bucket_ref[...] = jnp.zeros_like(bucket_ref)
    part_ref[...] = jnp.zeros_like(part_ref)
    load_scores.wait()

    def early_step(step, carry):
        advance(early, step)
        bucket_round(step - 1)
        return carry

    middle = min(2, size - 1)
    lax.fori_loop(1, middle, early_step, 0)

    load_kept.wait()
    other_core.wait_recv()
    kinds, count = kept_ref.shape[0], folded_ref.shape[0]
    rows = kept_ref.shape[1] // count

    def fold(index, target, span_of):
        span = slice(index * rows, (index + 1) * rows)
        for kind in range(kinds):
            total = kept_ref[kind, span].astype(F32) + came_ref[kind, span].astype(F32)
            target[span_of(kind)] = total.astype(BF16)

    def kind_rows(kind):
        return slice(kind * rows, (kind + 1) * rows)

    other_chip = None
    if count == 2:
        fold(1, folded_ref.at[1], kind_rows)
        other_chip = remote(
            folded_ref.at[1],
            far_came_ref,
            hop_sems.at[1, 0],
            hop_sems.at[1, 1],
            (me, differing(row, 2)),
        )
        other_chip.start()
    fold(0, folded_ref.at[0], kind_rows)

    lax.fori_loop(middle, size - 1, early_step, 0)
    turn(early)
    used = slice(0, kinds * rows)
    if other_chip is None:
        part_ref[used] = folded_ref[0]
    else:
        other_chip.wait_recv()
        total = folded_ref[0].astype(F32) + far_came_ref[...].astype(F32)
        part_ref[used] = total.astype(BF16)
    begin(late)

    def middle_step(step, carry):
        pass_on(early, step)
        advance(late, step)
        bucket_round(size - 2 + step - 1)
        return carry

    lax.fori_loop(1, size - 1, middle_step, 0)
    if size == 2:
        lax.fori_loop(0, units, bucket_unit, 0)
    turn(late)

    features = gain_refs[0].shape[1]
    per_gain = features // LANES
    gain_rows = len(gain_refs) * per_gain
    small_ref[...] = jnp.zeros_like(small_ref)
    for i, ref in enumerate(gain_refs):
        total = jnp.sum(ref[...], axis=0, keepdims=True)
        for c in range(per_gain):
            at = i * per_gain + c
            small_ref[at : at + 1, :] = total[:, c * LANES : (c + 1) * LANES]
    for r in range(rows_used):
        block_sums = bucket_ref[r].reshape(LANES, LANES).T
        at = gain_rows + r
        small_ref[at : at + 1, :] = jnp.sum(block_sums, axis=0, keepdims=True)

    def near_copy(t):
        return remote(
            small_ref,
            near_ref.at[row],
            small_sems.at[0, t],
            small_sems.at[1, t],
            (me, (row + t) % peers),
        )

    def far_copy(t):
        return remote(
            far_ref.at[me],
            far_ref.at[me],
            small_sems.at[2, t],
            small_sems.at[3, t],
            ((me + t) % size, row),
        )

    for t in range(1, peers):
        near_copy(t).start()
    near_ref[pl.ds(row, 1)] = small_ref[...][None]
    for t in range(1, peers):
        near_copy(t).wait_recv()
    own = rows_used // peers
    total, sums = None, None
    for k in range(peers):
        gains = near_ref[k, :gain_rows]
        mine = near_ref[k, pl.ds(gain_rows + own * share_place(row, k, peers), own)]
        total = gains if total is None else total + gains
        sums = mine if sums is None else sums + mine
    small_ref_rows = far_ref.shape[1]
    far_ref[pl.ds(me, 1)] = jnp.concatenate(
        [total, sums, jnp.zeros((small_ref_rows - gain_rows - own, LANES), F32)], axis=0
    )[None]

    def far_start(t, carry):
        far_copy(t).start()
        return carry

    lax.fori_loop(1, size, far_start, 0)

    def late_step(step, carry):
        pass_on(late, step)
        return carry

    lax.fori_loop(1, size - 1, late_step, 0)

    def far_wait(t, carry):
        far_copy(t).wait()
        return carry

    lax.fori_loop(1, size, far_wait, 0)

    def far_add(k, total):
        return total + far_ref[k]

    small_out_ref[...] = lax.fori_loop(1, size, far_add, far_ref[0])
    for i, way in early + late:
        out_copy(i, way, size - 2).wait_recv()

    for t in range(1, peers):
        near_copy(t).wait_send()
    other_core.wait_send()
    if other_chip is not None:
        other_chip.wait_send()
    for i, way in early + late:
        first_copy(i, way).wait_send()

    def sent(step, carry):
        for i, way in early + late:
            next_copy(i, way, step).wait_send()
        return carry

    lax.fori_loop(1, size - 1, sent, 0)

    def sent_out(step, carry):
        for i, way in early + late:
            out_copy(i, way, step).wait_send()
        return carry

    lax.fori_loop(0, size - 1, sent_out, 0)


def tail_sums(size, peers, buckets, heads, hidden, cross, give, keep, ids, ds, gains):
    assert peers in (2, 4)
    grain = 2 * 16 * size
    kinds, half, features = keep.shape
    count = peers // 2
    rows = [hidden.shape[0], cross.shape[0], kinds * half // count]
    padded = [r + -r % grain for r in rows]
    hidden = jnp.pad(hidden, ((0, padded[0] - rows[0]), (0, 0)))
    cross = jnp.pad(cross, ((0, padded[1] - rows[1]), (0, 0)))
    lines = peers * (-(-heads * buckets // LANES))
    small = len(gains) * features // LANES + lines
    small = shape((small + -small % 8, LANES), F32)
    vmem, hbm = pl.BlockSpec(memory_space=pltpu.VMEM), pl.BlockSpec(memory_space=pl.ANY)
    steps = pltpu.SemaphoreType.DMA((3, 2, size - 1))
    *sums, small = pl.pallas_call(
        functools.partial(tail_kernel, size, peers, buckets, heads),
        in_specs=[vmem, vmem, hbm, hbm, vmem, hbm, *[vmem] * len(gains)],
        out_specs=[vmem] * 4,
        out_shape=[*[shape((p, features), BF16) for p in padded], small],
        scratch_shapes=[
            *[pltpu.VMEM((2, size - 1, p // (2 * size), features), BF16) for p in padded],
            pltpu.VMEM(keep.shape, BF16),
            pltpu.VMEM(keep.shape, BF16),
            pltpu.VMEM((count, rows[2], features), BF16),
            pltpu.VMEM((rows[2], features), BF16),
            pltpu.VMEM((padded[2], features), BF16),
            pltpu.VMEM(ds.shape, BF16),
            pltpu.VMEM((lines, LANES // buckets, buckets, LANES), F32),
            pltpu.VMEM(small.shape, F32),
            pltpu.VMEM((peers, *small.shape), F32),
            pltpu.VMEM((size, *small.shape), F32),
            steps,
            steps,
            steps,
            steps,
            pltpu.SemaphoreType.DMA((4, max(size, peers))),
            pltpu.SemaphoreType.DMA((2, 2)),
            pltpu.SemaphoreType.DMA((2,)),
        ],
        compiler_params=pltpu.CompilerParams(
            vmem_limit_bytes=VMEM_BYTES, collective_id=0, has_side_effects=True
        ),
        cost_estimate=cost(),
        name="tail_sums",
    )(hidden, cross, give, keep, ids, ds, *gains)
    return [total[:r] for total, r in zip(sums, rows)], small


def swap(array, bit, size):
    return lax.ppermute(array, "mp", [(i, i ^ bit) for i in range(size)])


def after(array, *others):
    return lax.optimization_barrier((array, others))[0]


def add_low(a, b):
    return (a.astype(F32) + b.astype(F32)).astype(BF16)


def sum_far(shares, size):
    bit = 2
    while bit < size:
        shares = {
            j: add_low(shares[j], swap(shares[j | bit], bit, size)) for j in shares if not j & bit
        }
        bit *= 2
    return shares[0]


def shards(
    decoder_rows,
    memory_rows,
    decoder_token_length,
    memory_length,
    bucket_ids,
    relative_bucket_bias,
    self_gain,
    self_query,
    self_key,
    self_value,
    self_out,
    cross_gain,
    cross_query,
    cross_key,
    cross_value,
    cross_out,
    hidden_gain,
    widen_weight,
    narrow_weight,
    layer_cotangent,
):
    dp_size = lax.axis_size("dp")
    mp_size = lax.axis_size("mp")
    me = lax.axis_index("mp")
    doc, features = decoder_rows.shape
    slots = memory_rows.shape[0]
    cols = self_query.shape[1]
    heads = cols // HEAD_DIM
    buckets = relative_bucket_bias.shape[0]
    order = [*range(1, mp_size, 2), *range(0, mp_size, 2)]

    bias_rows = jnp.zeros((TABLE_ROWS, features), BF16)
    bias_rows = bias_rows.at[:heads, :buckets].set(relative_bucket_bias.T)
    own_self = pack(
        (self_query.T, False), (self_key.T, False), (self_value.T, False), (self_out, False), (bias_rows, False)
    )
    own_cross = pack(
        (cross_query.T, False), (cross_key.T, False), (cross_value.T, False), (cross_out, False)
    )
    own_hidden = pack((widen_weight, True), (narrow_weight, False))

    def first_hops(own):
        shares, bit = {0: own}, mp_size // 2
        while bit > 1:
            for j in list(shares):
                shares[j | bit] = swap(shares[j], bit, mp_size)
            bit //= 2
        return shares

    def last_hop(shares, *others):
        if 1 not in shares:
            shares[1] = swap(shares[0], 1, mp_size)
        for j in range(2, mp_size, 2):
            shares[j] = after(shares[j], *others)
            shares[j | 1] = swap(shares[j], 1, mp_size)
        return shares

    near_self = first_hops(own_self)
    near_self[1] = swap(own_self, 1, mp_size)
    memory_rows = after(memory_rows, near_self[1])
    w_self = last_hop(near_self, own_cross, own_hidden)
    w_self = [w_self[j] for j in order]
    near_cross = first_hops(own_cross)
    near_hidden = first_hops(own_hidden)
    near_hidden[1] = swap(own_hidden, 1, mp_size)
    memory_seen = lax.all_to_all(
        memory_rows.reshape(dp_size, slots // dp_size, features), "dp", 0, 0
    ).reshape(slots, features)

    doc_length = lax.dynamic_index_in_dim(decoder_token_length, me, keepdims=False)
    doc_memory = lax.dynamic_index_in_dim(memory_length, me)
    position = jnp.arange(doc, dtype=jnp.int32)
    allowed = (position[:, None] <= position[None, :]) & (position[:, None] < doc_length)
    ids = jnp.where(allowed, bucket_ids.T, buckets)
    gain_self = self_gain.astype(F32)[None]
    gain_cross = cross_gain.astype(F32)[None]
    gain_hidden = hidden_gain.astype(F32)[None]

    *saved_self, after_self = self_forward(heads, buckets, decoder_rows, gain_self, w_self, ids)
    w_cross = last_hop(near_cross, after_self)
    w_cross = [w_cross[j] for j in order]
    *saved_cross, after_cross = cross_forward(
        heads, after_self, gain_cross, memory_seen, doc_memory, w_cross
    )

    before, shares_hidden = (), {}
    w_hidden = near_hidden
    for j in range(0, mp_size, 2):
        last = j == mp_size - 2
        give, keep, *before = feed_forward(
            after_cross,
            gain_hidden,
            layer_cotangent,
            [w_hidden[j + 1], w_hidden[j]],
            before,
            last,
        )
        shares_hidden[j] = keep, swap(give, 1, mp_size)
        if j == 0:
            w_hidden = last_hop(near_hidden, before[0])
    layer_output, grad_after_cross, branch, hidden_gain_grad = before
    sent = {j: add_low(*shares_hidden[j]) for j in range(2, mp_size, 4)}
    branch = after(branch, sent)
    kept = {j: add_low(*shares_hidden[j]) for j in range(0, mp_size, 4)}
    part_hidden = sum_far(kept | sent, mp_size)

    give, keep, grad_memory, grad_after_self, branch, cross_gain_grad = cross_backward(
        heads,
        after_self,
        gain_cross,
        memory_seen,
        doc_memory,
        branch,
        grad_after_cross,
        saved_cross,
        w_cross,
    )
    memory_grad = lax.all_to_all(
        grad_memory.reshape(dp_size, slots // dp_size, features), "dp", 0, 0
    ).reshape(slots, features)
    came = after(swap(give, 1, mp_size), part_hidden)
    size = cols
    sent = {
        j: add_low(keep[:, j // 2 * size : (j // 2 + 1) * size], came[:, j // 2 * size : (j // 2 + 1) * size])
        for j in range(2, mp_size, 4)
    }
    branch = after(branch, sent)
    kept = {
        j: add_low(keep[:, j // 2 * size : (j // 2 + 1) * size], came[:, j // 2 * size : (j // 2 + 1) * size])
        for j in range(0, mp_size, 4)
    }
    part_cross = sum_far(kept | sent, mp_size)

    give, keep, score_grads, input_grad, self_gain_grad = self_backward(
        heads,
        buckets,
        decoder_rows,
        gain_self,
        ids,
        branch,
        grad_after_self,
        saved_self,
        w_self,
    )
    (sum_hidden, sum_cross, sum_self), small = tail_sums(
        dp_size,
        mp_size,
        buckets,
        heads,
        part_hidden.reshape(-1, features),
        part_cross.reshape(-1, features),
        give,
        keep,
        ids,
        score_grads,
        (self_gain_grad, cross_gain_grad, hidden_gain_grad),
    )
    wide_grad, narrow_grad, self_grads, cross_grads = finish(sum_hidden, sum_cross, sum_self)
    gain_rows = 3 * features // LANES
    gains = small[:gain_rows].reshape(3, features)
    lines = -(-heads * buckets // LANES)
    sums = small[gain_rows : gain_rows + lines, : heads // lines * buckets]
    position_grad = sums.reshape(heads, buckets).T

    return (
        layer_output,
        input_grad,
        memory_grad,
        position_grad,
        gains[0],
        *[grad.T for grad in self_grads[:3]],
        self_grads[3],
        gains[1],
        *[grad.T for grad in cross_grads[:3]],
        cross_grads[3],
        gains[2],
        wide_grad,
        narrow_grad,
    )


def solution(mesh):
    return jax.shard_map(
        shards,
        mesh=mesh,
        in_specs=(
            P(("dp", "mp"), None),
            P(("dp", "mp"), None),
            P("dp"),
            P("dp"),
            P(),
            P(None, "mp"),
            P(),
            P(None, "mp"),
            P(None, "mp"),
            P(None, "mp"),
            P("mp", None),
            P(),
            P(None, "mp"),
            P(None, "mp"),
            P(None, "mp"),
            P("mp", None),
            P(),
            P(None, "mp"),
            P("mp", None),
            P(("dp", "mp"), None),
        ),
        out_specs=(
            P(("dp", "mp"), None),
            P(("dp", "mp"), None),
            P(("dp", "mp"), None),
            P(None, "mp"),
            P(),
            P(None, "mp"),
            P(None, "mp"),
            P(None, "mp"),
            P("mp", None),
            P(),
            P(None, "mp"),
            P(None, "mp"),
            P(None, "mp"),
            P("mp", None),
            P(),
            P(None, "mp"),
            P("mp", None),
        ),
        check_vma=False,
    )
```

```python
import functools

import jax
import jax.numpy as jnp
from jax import lax
from jax.experimental import pallas as pl
from jax.experimental.pallas import tpu as pltpu
from jax.sharding import PartitionSpec as P

HEAD_DIM = 64
NORM_EPS = 1e-06
MASKED = -1e30
SCALE = HEAD_DIM**-0.5
BF16 = jnp.bfloat16
F32 = jnp.float32
LANES = 128
TABLE_ROWS = 16
HEAD_BLOCK = 256
BLOCK_HEADS = HEAD_BLOCK // HEAD_DIM
Q_BLOCK = 256
K_BLOCK = 256
HIDDEN_BLOCK = 256
MEMORY_BLOCK = 256
ROW_BLOCK = 128
VMEM_BYTES = 56 * 1024 * 1024
GELU_ROOT = 0.7978845608028654
GELU_CUBE = 0.044715


def dot_nn(a, b):
    return lax.dot_general(a, b, (((1,), (0,)), ((), ())), preferred_element_type=F32)


def dot_nt(a, b):
    return lax.dot_general(a, b, (((1,), (1,)), ((), ())), preferred_element_type=F32)


def dot_tn(a, b):
    return lax.dot_general(a, b, (((0,), (0,)), ((), ())), preferred_element_type=F32)


def flip(a):
    return a.astype(F32).T.astype(BF16)


def spans(size, step):
    return [slice(i, i + step) for i in range(0, size, step)]


def norm_scale(rows):
    return lax.rsqrt(jnp.mean(rows * rows, axis=-1, keepdims=True) + NORM_EPS)


def norm_into(normed_ref, rows_ref, gain_ref):
    for span in spans(rows_ref.shape[0], ROW_BLOCK):
        rows = rows_ref[span].astype(F32)
        normed_ref[span] = (rows * norm_scale(rows) * gain_ref[...]).astype(BF16)


def norm_back_into(span, grad, out_ref, low_ref, gain_grad_ref, rows_ref, gain_ref, add_ref):
    rows = rows_ref[span].astype(F32)
    scale = norm_scale(rows)
    unit = rows * scale
    grad_unit = grad * gain_ref[...]
    mean = jnp.mean(grad_unit * unit, axis=-1, keepdims=True)
    out = add_ref[span].astype(F32) + scale * (grad_unit - unit * mean)
    out_ref[span] = out
    if low_ref is not None:
        low_ref[span] = out.astype(BF16)
    gain_grad_ref[...] += jnp.sum((grad * unit).reshape(-1, 8, rows.shape[1]), axis=0)


def gelu_and_slope(v):
    square = v * v
    bend = jnp.tanh(GELU_ROOT * (v + GELU_CUBE * v * square))
    half = 0.5 * (1.0 + bend)
    slope = half + 0.5 * v * (1.0 - bend * bend) * GELU_ROOT * (1.0 + 3.0 * GELU_CUBE * square)
    return v * half, slope


def lane_block(start):
    return pl.ds(pl.multiple_of(start, LANES), LANES)


def extra_lanes(rows, allowed):
    lane = lax.broadcasted_iota(jnp.int32, (rows, LANES), 1) % HEAD_DIM
    first = MASKED if allowed is None else jnp.where(allowed, 0.0, MASKED)
    return jnp.where(lane == 0, first, jnp.where(lane < 4, 1.0, 0.0)).astype(BF16)


def pick(which, block, other):
    lane = lax.broadcasted_iota(jnp.int32, block.shape, 1)
    return jnp.where((lane < HEAD_DIM) == (which == 0), block, other)


def half_rows(which):
    return slice(which * HEAD_DIM, (which + 1) * HEAD_DIM)


def split(values):
    high = values.astype(BF16).astype(F32)
    rest = values - high
    middle = rest.astype(BF16).astype(F32)
    return high, middle, rest - middle


def with_extra(which, block_t, masked, minus):
    columns = block_t.shape[1]
    row = lax.broadcasted_iota(jnp.int32, (HEAD_DIM, columns), 0)
    extra = jnp.where(row == 0, 1.0 if masked else 0.0, 0.0)
    if minus is not None:
        for i, part in enumerate(split(minus)):
            extra = jnp.where(row == i + 1, -part, extra)
    own = block_t[half_rows(which)]
    return jnp.concatenate([own, extra] if which == 0 else [extra, own], axis=0).astype(BF16)


def bias_block(table_ref, ids_ref, index, rows, start):
    row = jnp.broadcast_to(table_ref[pl.ds(index, 1), :], (rows, LANES))
    return jnp.concatenate(
        [
            jnp.take_along_axis(row, ids_ref[:rows, c : c + LANES], axis=1)
            for c in range(start, start + Q_BLOCK, LANES)
        ],
        axis=1,
    )


def greet_other_core():
    me, row = lax.axis_index("dp"), lax.axis_index("mp")
    barrier = pltpu.get_barrier_semaphore()
    other = (me, row + 1 - 2 * (row % 2))
    pl.semaphore_signal(barrier, inc=1, device_id=other, device_id_type=pl.DeviceIdType.MESH)
    pl.semaphore_wait(barrier, 1)


def to_other_core(source, target, sems):
    me, row = lax.axis_index("dp"), lax.axis_index("mp")
    return pltpu.make_async_remote_copy(
        src_ref=source,
        dst_ref=target,
        send_sem=sems.at[0],
        recv_sem=sems.at[1],
        device_id=(me, row + 1 - 2 * (row % 2)),
        device_id_type=pl.DeviceIdType.MESH,
    )


def low_sum(a, b):
    return (a.astype(F32) + b.astype(F32)).astype(BF16)


class Stack:
    def __init__(self, sources, stack_ref, sems, kinds, rows):
        features = stack_ref.shape[0] // kinds
        self.copies = [
            [
                pltpu.make_async_copy(
                    source.at[pl.ds(kind * rows, rows)],
                    stack_ref.at[pl.ds(kind * features + p * rows, rows)],
                    sems.at[p, kind],
                )
                for p, source in enumerate(sources)
            ]
            for kind in range(kinds)
        ]

    def start(self):
        for copies in self.copies:
            for copy in copies:
                copy.start()

    def wait(self, *kinds):
        for kind in kinds:
            for copy in self.copies[kind]:
                copy.wait()


def table_copies(sources, tables_ref, sems, kinds):
    start = sources[0].shape[0] - TABLE_ROWS
    return [
        pltpu.make_async_copy(
            source.at[pl.ds(start, TABLE_ROWS)], tables_ref.at[p], sems.at[p, kinds]
        )
        for p, source in enumerate(sources)
    ]


def table_into(table_ref, tables_ref, heads, buckets):
    for p in range(tables_ref.shape[0]):
        rows = tables_ref[p, :, :LANES].astype(F32)
        lane = lax.broadcasted_iota(jnp.int32, rows.shape, 1)
        rows = jnp.where(lane < buckets, rows, MASKED)
        for h in range(heads):
            table_ref[p * heads + h : p * heads + h + 1, :] = rows[h : h + 1, :]


def self_forward_kernel(heads, buckets, shares, rows_ref, gain_ref, ids_ref, *refs):
    sources = refs[:shares]
    q_ref, k_ref, v_ref, mixed_ref, lse_ref, out_ref = refs[shares : shares + 6]
    w_ref, tables_ref, table_ref, normed_ref, sems = refs[shares + 6 :]
    step = pl.program_id(0)
    doc, features = rows_ref.shape
    stack = Stack(sources, w_ref, sems, 4, heads * HEAD_DIM)

    @pl.when(step == 0)
    def _():
        stack.start()
        tables = table_copies(sources, tables_ref, sems, 4)
        for copy in tables:
            copy.start()
        norm_into(normed_ref, rows_ref, gain_ref)
        out_ref[...] = rows_ref[...].astype(F32)
        for copy in tables:
            copy.wait()
        table_into(table_ref, tables_ref, heads, buckets)
        stack.wait(0, 1, 2, 3)

    def weights(kind):
        start = pl.multiple_of(kind * features + step * HEAD_BLOCK, HEAD_BLOCK)
        return w_ref[pl.ds(start, HEAD_BLOCK)]

    for kind, ref in enumerate((q_ref, k_ref, v_ref)):
        ref[...] = dot_nt(normed_ref[...], weights(kind)).astype(BF16)
    none = jnp.zeros((doc, LANES), BF16)
    for pair in range(BLOCK_HEADS // 2):
        lanes = slice(pair * LANES, (pair + 1) * LANES)
        k, v_t = k_ref[:, lanes], flip(v_ref[:, lanes])
        q_t = flip(q_ref[:, lanes].astype(F32) * SCALE)
        k_of = [pick(which, k, none) for which in range(2)]
        for span in spans(doc, Q_BLOCK):
            rows, mixed = span.stop, []
            for which in range(2):
                h = 2 * pair + which
                s = dot_nn(k_of[which][:rows], q_t[:, span])
                s = s + bias_block(table_ref, ids_ref, step * BLOCK_HEADS + h, rows, span.start)
                top = jnp.max(s, axis=0, keepdims=True)
                p = jnp.exp(s - top)
                total = jnp.sum(p, axis=0, keepdims=True)
                mixed.append(dot_nn(v_t[half_rows(which), :rows], p.astype(BF16)) / total)
                lse_ref[0, h : h + 1, span] = top + jnp.log(total)
            mixed_ref[span, lanes] = jnp.concatenate(mixed, axis=0).T.astype(BF16)
    out_ref[...] += dot_nn(mixed_ref[...], weights(3))


def self_backward_kernel(heads, buckets, shares, *refs):
    rows_ref, gain_ref, ids_ref, branch_ref, add_ref = refs[:5]
    q_ref, k_ref, v_ref, mixed_ref, lse_ref = refs[5:10]
    sources = refs[10 : 10 + shares]
    give_ref, keep_ref, ds_ref, out_ref, gain_grad_ref = refs[10 + shares : 15 + shares]
    w_ref, tables_ref, table_ref, normed_ref, g_ref, grad_ref, sems = refs[15 + shares :]
    step = pl.program_id(0)
    doc, features = rows_ref.shape
    half = features // 2
    stack = Stack(sources, w_ref, sems, 4, heads * HEAD_DIM)

    @pl.when(step == 0)
    def _():
        stack.start()
        tables = table_copies(sources, tables_ref, sems, 4)
        for copy in tables:
            copy.start()
        norm_into(normed_ref, rows_ref, gain_ref)
        for copy in tables:
            copy.wait()
        table_into(table_ref, tables_ref, heads, buckets)
        stack.wait(3)

    start = pl.multiple_of(3 * features + step * HEAD_BLOCK, HEAD_BLOCK)
    g_ref[...] = dot_nt(branch_ref[...], w_ref[pl.ds(start, HEAD_BLOCK)]).astype(BF16)
    none = jnp.zeros((doc, LANES), BF16)
    ones = extra_lanes(doc, None)
    for pair in range(BLOCK_HEADS // 2):
        lanes = lane_block(step * HEAD_BLOCK + pair * LANES)
        q, k, v = q_ref[:, lanes], k_ref[:, lanes], v_ref[:, lanes]
        g = g_ref[:, pair * LANES : (pair + 1) * LANES]
        q_t, k_t = q.astype(F32).T * SCALE, flip(k)
        g_t = g.astype(F32).T
        inner = g_t * mixed_ref[:, lanes].astype(F32).T
        per_head = []
        for which in range(2):
            h = 2 * pair + which
            minus = jnp.sum(inner[half_rows(which)], axis=0, keepdims=True)
            per_head.append(
                (
                    pick(which, k, ones),
                    pick(which, v, ones),
                    with_extra(which, q_t, False, lse_ref[0, h : h + 1, :]),
                    with_extra(which, g_t, False, minus),
                    pick(which, q, none),
                    pick(which, g, none),
                )
            )
        grad_k = grad_v = None
        for span in spans(doc, Q_BLOCK):
            rows, grad_q, part_k, part_v = span.stop, [], None, None
            for which, (k_of, v_of, q_with, g_with, q_of, g_of) in enumerate(per_head):
                h = 2 * pair + which
                s = dot_nn(k_of[:rows], q_with[:, span])
                s = s + bias_block(table_ref, ids_ref, step * BLOCK_HEADS + h, rows, span.start)
                p = jnp.exp(s)
                ds = (p * dot_nn(v_of[:rows], g_with[:, span])).astype(BF16)
                ds_ref[h, :rows, span] = ds
                grad_q.append(dot_nn(k_t[half_rows(which), :rows], ds))
                to_v = dot_nn(p.astype(BF16), g_of[span])
                to_k = dot_nn(ds, q_of[span])
                part_v = to_v if part_v is None else part_v + to_v
                part_k = to_k if part_k is None else part_k + to_k
            grad_q = (jnp.concatenate(grad_q, axis=0) * SCALE).T
            grad_ref[0, span, lanes] = grad_q.astype(BF16)
            if grad_v is not None:
                part_v = jnp.concatenate(
                    [part_v[: span.start] + grad_v, part_v[span.start :]], axis=0
                )
                part_k = jnp.concatenate(
                    [part_k[: span.start] + grad_k, part_k[span.start :]], axis=0
                )
            grad_v, grad_k = part_v, part_k
        grad_ref[1, :, lanes] = (grad_k * SCALE).astype(BF16)
        grad_ref[2, :, lanes] = grad_v.astype(BF16)

    @pl.when(step == pl.num_programs(0) - 1)
    def _():
        stack.wait(0, 1, 2)
        for ref, columns in ((give_ref, slice(0, half)), (keep_ref, slice(half, features))):
            for kind in range(3):
                ref[kind] = dot_tn(grad_ref[kind, :, columns], normed_ref[...]).astype(BF16)
            ref[3] = dot_tn(mixed_ref[:, columns], branch_ref[...]).astype(BF16)
        gain_grad_ref[...] = jnp.zeros_like(gain_grad_ref)
        for span in spans(doc, ROW_BLOCK):
            back = dot_nn(grad_ref[0, span], w_ref[:features])
            back = back + dot_nn(grad_ref[1, span], w_ref[features : 2 * features])
            back = back + dot_nn(grad_ref[2, span], w_ref[2 * features : 3 * features])
            norm_back_into(
                span, back, out_ref, None, gain_grad_ref, rows_ref, gain_ref, add_ref
            )


def cross_forward_kernel(heads, shares, length_ref, rows_ref, gain_ref, memory_ref, *refs):
    sources = refs[:shares]
    q_ref, k_ref, v_ref, mixed_ref, lse_ref, out_ref = refs[shares : shares + 6]
    w_ref, normed_ref, extra_ref, p_ref, sems = refs[shares + 6 :]
    step = pl.program_id(0)
    (doc, features), slots = rows_ref.shape, memory_ref.shape[0]
    stack = Stack(sources, w_ref, sems, 4, heads * HEAD_DIM)

    @pl.when(step == 0)
    def _():
        stack.start()
        norm_into(normed_ref, rows_ref, gain_ref)
        out_ref[...] = rows_ref[...]
        slot = lax.broadcasted_iota(jnp.int32, (slots, LANES), 0)
        extra_ref[...] = extra_lanes(slots, slot < length_ref[0])
        stack.wait(0, 1, 2, 3)

    def weights(kind):
        start = pl.multiple_of(kind * features + step * HEAD_BLOCK, HEAD_BLOCK)
        return w_ref[pl.ds(start, HEAD_BLOCK)]

    q_ref[...] = dot_nt(normed_ref[...], weights(0)).astype(BF16)
    k_ref[...] = dot_nt(memory_ref[...], weights(1)).astype(BF16)
    v_ref[...] = dot_nt(memory_ref[...], weights(2)).astype(BF16)

    units = [
        (pair, which, span)
        for pair in range(BLOCK_HEADS // 2)
        for span in spans(doc, Q_BLOCK)
        for which in range(2)
    ]
    v_t = [flip(v_ref[:, p * LANES : (p + 1) * LANES]) for p in range(BLOCK_HEADS // 2)]
    q_t = [
        q_ref[:, p * LANES : (p + 1) * LANES].astype(F32).T * SCALE
        for p in range(BLOCK_HEADS // 2)
    ]

    def scores(unit):
        pair, which, span = unit
        q_with = with_extra(which, q_t[pair][:, span], True, None)
        k_of = pick(which, k_ref[:, pair * LANES : (pair + 1) * LANES], extra_ref[...])
        return [dot_nn(k_of[rows], q_with) for rows in spans(slots, K_BLOCK)]

    mixed = {}
    ahead = scores(units[0])
    for i, (pair, which, span) in enumerate(units):
        s, slot = ahead, i % 2
        if i + 1 < len(units):
            ahead = scores(units[i + 1])
        top = functools.reduce(jnp.maximum, [jnp.max(c, axis=0, keepdims=True) for c in s])
        total = None
        for rows, chunk in zip(spans(slots, K_BLOCK), s):
            p = jnp.exp(chunk - top)
            part = jnp.sum(p, axis=0, keepdims=True)
            total = part if total is None else total + part
            p_ref[slot, rows] = p.astype(BF16)
        h = 2 * pair + which
        lse_ref[0, h : h + 1, span] = top + jnp.log(total)
        mixed[which] = dot_nn(v_t[pair][half_rows(which)], p_ref[slot]) / total
        if which == 1:
            out = jnp.concatenate([mixed[0], mixed[1]], axis=0).T
            mixed_ref[span, pair * LANES : (pair + 1) * LANES] = out.astype(BF16)
    out_ref[...] += dot_nn(mixed_ref[...], weights(3))


def cross_backward_kernel(heads, shares, length_ref, *refs):
    gain_ref, branch_ref, q_ref, mixed_ref, lse_ref = refs[:5]
    rows_in, memory_in, add_in, k_in, v_in = refs[5:10]
    sources = refs[10 : 10 + shares]
    count = shares // 2
    sums, refs = refs[10 + shares : 10 + shares + count], refs[10 + shares + count :]
    memory_out, out_ref, low_ref, gain_grad_ref = refs[:4]
    rows_ref, memory_ref, add_ref, k_ref, v_ref = refs[4:9]
    (
        w_ref,
        normed_ref,
        extra_ref,
        g_ref,
        grad_q_ref,
        grad_ref,
        ds_ref,
        give_ref,
        keep_ref,
        came_ref,
        memory_grad_ref,
        sems,
        load_sems,
        key_sems,
        out_sems,
        swap_sems,
    ) = refs[9:]
    (doc, features), slots = rows_ref.shape, memory_ref.shape[0]
    half, blocks = features // 2, features // HEAD_BLOCK
    stack = Stack(sources, w_ref, sems, 4, heads * HEAD_DIM)
    loads = [
        pltpu.make_async_copy(source, target, load_sems.at[i])
        for i, (source, target) in enumerate(
            ((memory_in, memory_ref), (rows_in, rows_ref), (add_in, add_ref))
        )
    ]

    def key_copies(b):
        lanes = pl.ds(pl.multiple_of(b * HEAD_BLOCK, HEAD_BLOCK), HEAD_BLOCK)
        return [
            pltpu.make_async_copy(source.at[:, lanes], target.at[b], key_sems.at[i, b])
            for i, (source, target) in enumerate(((k_in, k_ref), (v_in, v_ref)))
        ]

    stack.start()
    for b in range(blocks):
        for copy in key_copies(b):
            copy.start()
    for copy in loads:
        copy.start()
    greet_other_core()
    slot = lax.broadcasted_iota(jnp.int32, (slots, LANES), 0)
    extra_ref[...] = extra_lanes(slots, slot < length_ref[0])
    none = jnp.zeros((doc, LANES), BF16)
    stack.wait(3)

    def one_block(step, carry):
        start = pl.multiple_of(3 * features + step * HEAD_BLOCK, HEAD_BLOCK)
        g_ref[...] = dot_nt(branch_ref[...], w_ref[pl.ds(start, HEAD_BLOCK)]).astype(BF16)
        for copy in key_copies(step):
            copy.wait()
        for pair in range(BLOCK_HEADS // 2):
            local = slice(pair * LANES, (pair + 1) * LANES)
            lanes = lane_block(step * HEAD_BLOCK + pair * LANES)
            v_lanes = lane_block(features + step * HEAD_BLOCK + pair * LANES)
            q, g = q_ref[:, lanes], g_ref[:, local]
            q_t, g_t = q.astype(F32).T * SCALE, g.astype(F32).T
            inner = g_t * mixed_ref[:, lanes].astype(F32).T
            per_head = []
            for which in range(2):
                h = 2 * pair + which
                minus = jnp.sum(inner[half_rows(which)], axis=0, keepdims=True)
                per_head.append(
                    (
                        with_extra(which, q_t, True, lse_ref[step, h : h + 1, :]),
                        with_extra(which, g_t, False, minus),
                        pick(which, q, none),
                        pick(which, g, none),
                    )
                )
            for rows in spans(slots, K_BLOCK):
                k, v, extra = k_ref[step, rows, local], v_ref[step, rows, local], extra_ref[rows]
                part_k = part_v = None
                for which, (q_with, g_with, q_of, g_of) in enumerate(per_head):
                    p = jnp.exp(dot_nn(pick(which, k, extra), q_with))
                    ds = (p * dot_nn(pick(which, v, extra), g_with)).astype(BF16)
                    ds_ref[which, rows] = ds
                    to_v = dot_nn(p.astype(BF16), g_of)
                    to_k = dot_nn(ds, q_of)
                    part_v = to_v if part_v is None else part_v + to_v
                    part_k = to_k if part_k is None else part_k + to_k
                grad_ref[rows, lanes] = (part_k * SCALE).astype(BF16)
                grad_ref[rows, v_lanes] = part_v.astype(BF16)
            k_t = flip(k_ref[step, :, local])
            grad_q = [dot_nn(k_t[half_rows(which)], ds_ref[which]) for which in range(2)]
            grad_q_ref[:, lanes] = (jnp.concatenate(grad_q, axis=0) * SCALE).T.astype(BF16)
        return carry

    lax.fori_loop(0, blocks, one_block, 0)

    for copy in loads:
        copy.wait()
    norm_into(normed_ref, rows_ref, gain_ref)

    def weight_grads(ref, first):
        columns = slice(first, first + half)
        v_columns = slice(features + first, features + first + half)
        ref[0] = dot_tn(grad_q_ref[:, columns], normed_ref[...]).astype(BF16)
        ref[1] = dot_tn(grad_ref[:, columns], memory_ref[...]).astype(BF16)
        ref[2] = dot_tn(grad_ref[:, v_columns], memory_ref[...]).astype(BF16)
        ref[3] = dot_tn(mixed_ref[:, columns], branch_ref[...]).astype(BF16)

    weight_grads(give_ref, 0)
    swap = to_other_core(give_ref, came_ref, swap_sems)
    swap.start()
    stack.wait(0, 1, 2)
    writes = []
    for i, rows in enumerate(spans(slots, MEMORY_BLOCK)):
        memory_grad_ref[rows] = dot_nn(
            grad_ref[rows], w_ref[features : 3 * features]
        ).astype(BF16)
        writes.append(
            pltpu.make_async_copy(memory_grad_ref.at[rows], memory_out.at[rows], out_sems.at[i])
        )
        writes[-1].start()
    weight_grads(keep_ref, half)
    gain_grad_ref[...] = jnp.zeros_like(gain_grad_ref)
    for span in spans(doc, ROW_BLOCK):
        back = dot_nn(grad_q_ref[span], w_ref[:features])
        norm_back_into(
            span, back, out_ref, low_ref, gain_grad_ref, rows_ref, gain_ref, add_ref
        )
    swap.wait_recv()
    rows = half // count
    for share, sums_ref in enumerate(sums):
        for kind in range(4):
            span = slice(share * rows, (share + 1) * rows)
            to = slice(kind * rows, (kind + 1) * rows)
            sums_ref[to] = low_sum(keep_ref[kind, span], came_ref[kind, span])
    swap.wait_send()
    for copy in writes:
        copy.wait()


def feed_forward_kernel(first, last, rows_ref, gain_ref, cotangent_ref, *refs):
    sources, refs = refs[:2], refs[2:]
    if not first:
        before_in, refs = refs[:2], refs[2:]
    sums_ref, layer_ref, out_ref = refs[:3]
    if last:
        low_ref, gain_grad_ref = refs[3:5]
        refs = refs[2:]
    (
        wide_ref,
        narrow_ref,
        normed_ref,
        normed_t,
        cotangent_t,
        active_ref,
        grad_ref,
        give_ref,
        keep_ref,
        came_ref,
        layer_in_ref,
        back_in_ref,
        sems,
        before_sems,
        swap_sems,
    ) = refs[3:]
    step, steps = pl.program_id(0), pl.num_programs(0)
    half = steps // 2
    doc = rows_ref.shape[0]
    hidden = sources[0].shape[0] // 2
    copies = [
        [
            pltpu.make_async_copy(
                source.at[pl.ds(kind * hidden, hidden)],
                stack.at[pl.ds(p * hidden, hidden)],
                sems.at[p, kind],
            )
            for kind, stack in enumerate((wide_ref, narrow_ref))
        ]
        for p, source in enumerate(sources)
    ]
    loads = []
    if not first:
        loads = [
            pltpu.make_async_copy(source, target, before_sems.at[i])
            for i, (source, target) in enumerate(zip(before_in, (layer_in_ref, back_in_ref)))
        ]
    swap = to_other_core(give_ref, came_ref, swap_sems)

    @pl.when(step == 0)
    def _():
        for pair in copies:
            for copy in pair:
                copy.start()
        for copy in loads:
            copy.start()
        greet_other_core()
        norm_into(normed_ref, rows_ref, gain_ref)
        for span in spans(doc, ROW_BLOCK):
            normed_t[:, span] = flip(normed_ref[span])
            cotangent_t[:, span] = flip(cotangent_ref[span])

    for p, pair in enumerate(copies):

        @pl.when(step == p * half)
        def _(pair=pair):
            for copy in pair:
                copy.wait()

    units = pl.ds(pl.multiple_of(step * HIDDEN_BLOCK, HIDDEN_BLOCK), HIDDEN_BLOCK)
    activated, slope = gelu_and_slope(dot_nn(wide_ref[units], normed_t[...]))
    active_ref[units] = activated.astype(BF16)
    grad_ref[units] = (dot_nn(narrow_ref[units], cotangent_t[...]) * slope).astype(BF16)

    def store(ref, at):
        rows = pl.ds(pl.multiple_of(at * HIDDEN_BLOCK, HIDDEN_BLOCK), HIDDEN_BLOCK)
        ref[0, rows] = dot_nn(grad_ref[units], normed_ref[...]).astype(BF16)
        ref[1, rows] = dot_nn(active_ref[units], cotangent_ref[...]).astype(BF16)

    @pl.when(step < half)
    def _():
        store(give_ref, step)

    @pl.when(step == half - 1)
    def _():
        swap.start()

    @pl.when(step >= half)
    def _():
        store(keep_ref, step - half)

    @pl.when(step == steps - 1)
    def _():
        for copy in loads:
            copy.wait()
        if last:
            gain_grad_ref[...] = jnp.zeros_like(gain_grad_ref)
        for span in spans(doc, ROW_BLOCK):
            layer = rows_ref[span] if first else layer_in_ref[span]
            layer = layer + dot_tn(active_ref[:, span], narrow_ref[...])
            layer_ref[span] = layer.astype(layer_ref.dtype)
            back = dot_tn(grad_ref[:, span], wide_ref[...])
            if not first:
                back = back + back_in_ref[span]
            if last:
                norm_back_into(
                    span, back, out_ref, low_ref, gain_grad_ref, rows_ref, gain_ref, cotangent_ref
                )
            else:
                out_ref[span] = back
        swap.wait_recv()
        for kind in range(2):
            for span in spans(hidden, HIDDEN_BLOCK):
                sums_ref[kind, span] = low_sum(keep_ref[kind, span], came_ref[kind, span])
        swap.wait_send()


def pack_kernel(flipped, *refs):
    out_ref, start = refs[-1], 0
    for source, turn in zip(refs[:-1], flipped):
        rows = source.shape[1] if turn else source.shape[0]
        span = slice(start, start + rows)
        out_ref[span] = flip(source[...]) if turn else source[...]
        start += rows


def finish_kernel(hidden_ref, cross_ref, self_ref, wide_ref, narrow_ref, *outs):
    hidden = narrow_ref.shape[0]
    for span in spans(hidden, ROW_BLOCK):
        wide_ref[:, span] = hidden_ref[span].astype(F32).T
        narrow_ref[span] = hidden_ref[hidden + span.start : hidden + span.stop].astype(F32)
    rows = outs[0].shape[0]
    for source, refs in ((self_ref, outs[:4]), (cross_ref, outs[4:])):
        for kind, ref in enumerate(refs):
            ref[...] = source[kind * rows : (kind + 1) * rows].astype(F32)


def params():
    return pltpu.CompilerParams(vmem_limit_bytes=VMEM_BYTES)


def cost():
    return pl.CostEstimate(flops=1 << 20, bytes_accessed=1 << 16, transcendentals=0)


def shape(dims, dtype):
    return jax.ShapeDtypeStruct(dims, dtype)


def whole(array):
    return pl.BlockSpec(
        array.shape, lambda *_: (0,) * len(array.shape), pipeline_mode=pl.Buffered(1)
    )


def result(array):
    return pl.BlockSpec(array.shape, lambda *_: (0,) * len(array.shape))


def columns(rows):
    return pl.BlockSpec((rows, HEAD_BLOCK), lambda i: (0, i))


def anywhere(arrays):
    return [pl.BlockSpec(memory_space=pl.ANY) for _ in arrays]


SCALAR = pl.BlockSpec(memory_space=pltpu.SMEM)


def call(kernel, name, grid, in_specs, out_specs, out_shape, scratch, args, channel=None):
    compiler_params = params()
    if channel is not None:
        compiler_params = pltpu.CompilerParams(
            vmem_limit_bytes=VMEM_BYTES, collective_id=channel, has_side_effects=True
        )
    return pl.pallas_call(
        kernel,
        grid=grid,
        in_specs=in_specs,
        out_specs=out_specs,
        out_shape=out_shape,
        scratch_shapes=scratch,
        compiler_params=compiler_params,
        cost_estimate=cost(),
        name=name,
    )(*args)


def pack(*parts):
    arrays, flipped = zip(*parts)
    rows = sum(a.shape[1] if turn else a.shape[0] for a, turn in parts)
    features = arrays[0].shape[0] if flipped[0] else arrays[0].shape[1]
    return pl.pallas_call(
        functools.partial(pack_kernel, flipped),
        out_shape=shape((rows, features), BF16),
        compiler_params=params(),
        cost_estimate=cost(),
        name="pack",
    )(*arrays)


def self_forward(heads, buckets, rows, gain, weights, ids):
    doc, features = rows.shape
    shares, steps = len(weights), features // HEAD_BLOCK
    narrow, tall = shape((doc, features), BF16), shape((doc, features), F32)
    out_shape = (*[narrow] * 4, shape((steps, 8, doc), F32), tall)
    return call(
        functools.partial(self_forward_kernel, heads, buckets, shares),
        "self_forward",
        (steps,),
        [whole(rows), whole(gain), whole(ids), *anywhere(weights)],
        (*[columns(doc)] * 4, pl.BlockSpec((1, 8, doc), lambda i: (i, 0, 0)), result(tall)),
        out_shape,
        [
            pltpu.VMEM((4 * features, features), BF16),
            pltpu.VMEM((shares, TABLE_ROWS, features), BF16),
            pltpu.VMEM((TABLE_ROWS, LANES), F32),
            pltpu.VMEM((doc, features), BF16),
            pltpu.SemaphoreType.DMA((shares, 5)),
        ],
        (rows, gain, ids, *weights),
    )


def self_backward(heads, buckets, rows, gain, ids, branch, add, saved, weights):
    doc, features = rows.shape
    shares, steps = len(weights), features // HEAD_BLOCK
    packed = shape((4, features // 2, features), BF16)
    out_shape = (
        packed,
        packed,
        shape((steps * BLOCK_HEADS, doc, doc), BF16),
        shape((doc, features), F32),
        shape((8, features), F32),
    )
    *arrays, lse = saved
    return call(
        functools.partial(self_backward_kernel, heads, buckets, shares),
        "self_backward",
        (steps,),
        [
            *[whole(a) for a in (rows, gain, ids, branch, add, *arrays)],
            pl.BlockSpec((1, 8, doc), lambda i: (i, 0, 0)),
            *anywhere(weights),
        ],
        (
            result(packed),
            result(packed),
            pl.BlockSpec((BLOCK_HEADS, doc, doc), lambda i: (i, 0, 0)),
            result(out_shape[3]),
            result(out_shape[4]),
        ),
        out_shape,
        [
            pltpu.VMEM((4 * features, features), BF16),
            pltpu.VMEM((shares, TABLE_ROWS, features), BF16),
            pltpu.VMEM((TABLE_ROWS, LANES), F32),
            pltpu.VMEM((doc, features), BF16),
            pltpu.VMEM((doc, HEAD_BLOCK), BF16),
            pltpu.VMEM((3, doc, features), BF16),
            pltpu.SemaphoreType.DMA((shares, 5)),
        ],
        (rows, gain, ids, branch, add, *arrays, lse, *weights),
    )


def cross_forward(heads, rows, gain, memory, length, weights):
    (doc, features), slots = rows.shape, memory.shape[0]
    shares, steps = len(weights), features // HEAD_BLOCK
    query, key = shape((doc, features), BF16), shape((slots, features), BF16)
    tall = shape((doc, features), F32)
    return call(
        functools.partial(cross_forward_kernel, heads, shares),
        "cross_forward",
        (steps,),
        [SCALAR, whole(rows), whole(gain), whole(memory), *anywhere(weights)],
        (
            columns(doc),
            columns(slots),
            columns(slots),
            columns(doc),
            pl.BlockSpec((1, 8, doc), lambda i: (i, 0, 0)),
            result(tall),
        ),
        (query, key, key, query, shape((steps, 8, doc), F32), tall),
        [
            pltpu.VMEM((4 * features, features), BF16),
            pltpu.VMEM((doc, features), BF16),
            pltpu.VMEM((slots, LANES), BF16),
            pltpu.VMEM((2, slots, Q_BLOCK), BF16),
            pltpu.SemaphoreType.DMA((shares, 4)),
        ],
        (length, rows, gain, memory, *weights),
    )


def cross_backward(heads, rows, gain, memory, length, branch, add, saved, weights):
    (doc, features), slots = rows.shape, memory.shape[0]
    shares, blocks = len(weights), features // HEAD_BLOCK
    count = shares // 2
    out_shape = (
        *[shape((4 * heads * HEAD_DIM, features), BF16)] * count,
        shape((slots, features), BF16),
        shape((doc, features), F32),
        shape((doc, features), BF16),
        shape((8, features), F32),
    )
    query, key, value, mixed, lse = saved
    near = (gain, branch, query, mixed, lse)
    far = (rows, memory, add, key, value, *weights)
    vmem, hbm = pl.BlockSpec(memory_space=pltpu.VMEM), pl.BlockSpec(memory_space=pl.ANY)
    packed = pltpu.VMEM((4, features // 2, features), BF16)
    block = pltpu.VMEM((blocks, slots, HEAD_BLOCK), BF16)
    return call(
        functools.partial(cross_backward_kernel, heads, shares),
        "cross_backward",
        (),
        [SCALAR, *[vmem for _ in near], *[hbm for _ in far]],
        (*[vmem] * count, hbm, vmem, vmem, vmem),
        out_shape,
        [
            pltpu.VMEM((doc, features), F32),
            pltpu.VMEM((slots, features), BF16),
            pltpu.VMEM((doc, features), F32),
            block,
            block,
            pltpu.VMEM((4 * features, features), BF16),
            pltpu.VMEM((doc, features), BF16),
            pltpu.VMEM((slots, LANES), BF16),
            pltpu.VMEM((doc, HEAD_BLOCK), BF16),
            pltpu.VMEM((doc, features), BF16),
            pltpu.VMEM((slots, 2 * features), BF16),
            pltpu.VMEM((2, slots, doc), BF16),
            packed,
            packed,
            packed,
            pltpu.VMEM((slots, features), BF16),
            pltpu.SemaphoreType.DMA((shares, 4)),
            pltpu.SemaphoreType.DMA((3,)),
            pltpu.SemaphoreType.DMA((2, blocks)),
            pltpu.SemaphoreType.DMA((slots // MEMORY_BLOCK,)),
            pltpu.SemaphoreType.DMA((2,)),
        ],
        (length, *near, *far),
        channel=1,
    )


def feed_forward(rows, gain, cotangent, weights, before, last):
    (doc, features), shares = rows.shape, len(weights)
    share = weights[0].shape[0] // 2
    hidden = share * shares
    steps = hidden // HIDDEN_BLOCK
    packed, tall = shape((2, share, features), BF16), shape((doc, features), F32)
    low = shape((doc, features), BF16)
    rest = [low, tall, low, shape((8, features), F32)] if last else [tall, tall]
    kept, added = pltpu.VMEM(packed.shape, BF16), pltpu.VMEM(tall.shape, F32)
    return call(
        functools.partial(feed_forward_kernel, not before, last),
        "feed_forward",
        (steps,),
        [whole(rows), whole(gain), whole(cotangent), *anywhere(weights), *anywhere(before)],
        (result(packed), *[result(o) for o in rest]),
        (packed, *rest),
        [
            pltpu.VMEM((hidden, features), BF16),
            pltpu.VMEM((hidden, features), BF16),
            pltpu.VMEM((doc, features), BF16),
            pltpu.VMEM((features, doc), BF16),
            pltpu.VMEM((features, doc), BF16),
            pltpu.VMEM((hidden, doc), BF16),
            pltpu.VMEM((hidden, doc), BF16),
            kept,
            kept,
            kept,
            added,
            added,
            pltpu.SemaphoreType.DMA((shares, 2)),
            pltpu.SemaphoreType.DMA((2,)),
            pltpu.SemaphoreType.DMA((2,)),
        ],
        (rows, gain, cotangent, *weights, *before),
        channel=3 if before else 2,
    )


def finish(sum_hidden, sum_cross, sum_self):
    rows, features = sum_self.shape
    hidden, part = sum_hidden.shape[0] // 2, shape((rows // 4, features), F32)
    wide, narrow, *parts = pl.pallas_call(
        finish_kernel,
        out_shape=[
            shape((features, hidden), F32),
            shape((hidden, features), F32),
            *[part] * 8,
        ],
        compiler_params=params(),
        cost_estimate=cost(),
        name="finish",
    )(sum_hidden, sum_cross, sum_self)
    return wide, narrow, parts[:4], parts[4:]


def ring_place(me, size):
    return jnp.where(me % 2 == 0, me // 2, size - 1 - me // 2)


def ring_device(place, size):
    return jnp.where(place < size // 2, 2 * place, 2 * (size - 1 - place) + 1)


def differing(row, bit):
    return row + bit - 2 * bit * ((row // bit) % 2)


def share_place(row, other, peers):
    j, bit = 0, 1
    while bit < peers:
        j = j + bit * ((row // bit + other // bit) % 2)
        bit *= 2
    return (j % 2) * (j // 2) + (1 - j % 2) * (peers // 2 + j // 2)


def tail_kernel(size, peers, buckets, heads, *refs):
    terms = 1 if peers == 2 else 2
    hidden_refs, cross_refs, refs = refs[:terms], refs[terms : 2 * terms], refs[2 * terms :]
    give_ref, keep_ref, ids_ref, ds_ref, *gain_refs = refs[:7]
    outs, small_out_ref = refs[7:10], refs[10]
    slots, firsts = refs[11:14], refs[14:16]
    kept_ref, came_ref, folded_ref, far_came_ref, part_ref, scores_ref, bucket_ref = refs[16:23]
    small_ref, near_ref, far_ref = refs[23:26]
    send, came, send_out, came_out, small_sems, hop_sems, local_sems = refs[26:]
    parts = (hidden_refs, cross_refs, (part_ref,))
    me, row = lax.axis_index("dp"), lax.axis_index("mp")
    place = ring_place(me, size)
    ways = (
        (place, ring_device((place + 1) % size, size)),
        (size - 1 - place, ring_device((place + size - 1) % size, size)),
    )
    doc = ids_ref.shape[0]
    mesh = pl.DeviceIdType.MESH

    load_scores = pltpu.make_async_copy(ds_ref, scores_ref, local_sems.at[0])
    load_kept = pltpu.make_async_copy(keep_ref, kept_ref, local_sems.at[1])
    load_scores.start()
    load_kept.start()

    barrier = pltpu.get_barrier_semaphore()

    def greet(t, carry):
        pl.semaphore_signal(
            barrier, inc=1, device_id=((me + t) % size, row), device_id_type=mesh
        )
        return carry

    lax.fori_loop(1, size, greet, 0)
    for t in range(1, peers):
        pl.semaphore_signal(
            barrier, inc=1, device_id=(me, (row + t) % peers), device_id_type=mesh
        )
    pl.semaphore_wait(barrier, size - 1 + peers - 1)

    def remote(src, dst, send_sem, recv_sem, device):
        return pltpu.make_async_remote_copy(
            src_ref=src,
            dst_ref=dst,
            send_sem=send_sem,
            recv_sem=recv_sem,
            device_id=device,
            device_id_type=mesh,
        )

    def block(i, way, number):
        rows = outs[i].shape[0] // (2 * size)
        return pl.ds(pl.multiple_of((way * size + number) * rows, 16), rows)

    def part(i, span):
        total = parts[i][0][span].astype(F32)
        for ref in parts[i][1:]:
            total = total + ref[span].astype(F32)
        return total

    def first_copy(i, way):
        return remote(
            firsts[i].at[way] if i < 2 else part_ref.at[block(i, way, ways[way][0])],
            slots[i].at[way, 0],
            send.at[i, way, 0],
            came.at[i, way, 0],
            (ways[way][1], row),
        )

    def next_copy(i, way, step):
        return remote(
            slots[i].at[way, step - 1],
            slots[i].at[way, step],
            send.at[i, way, step],
            came.at[i, way, step],
            (ways[way][1], row),
        )

    def wait_came(i, way, step):
        remote(
            slots[i].at[way, step],
            slots[i].at[way, step],
            send.at[i, way, step],
            came.at[i, way, step],
            (ways[way][1], row),
        ).wait_recv()

    def out_copy(i, way, step):
        span = block(i, way, (ways[way][0] + 1 - step + size) % size)
        return remote(
            outs[i].at[span],
            outs[i].at[span],
            send_out.at[i, way, step],
            came_out.at[i, way, step],
            (ways[way][1], row),
        )

    def begin(rings):
        for i, way in rings:
            if i < 2:
                firsts[i][way] = part(i, block(i, way, ways[way][0])).astype(BF16)
            first_copy(i, way).start()

    def plus_part(i, way, step):
        span = block(i, way, (ways[way][0] - step - 1 + size) % size)
        total = slots[i][way, step].astype(F32) + part(i, span)
        return span, total.astype(BF16)

    def advance(rings, step):
        for i, way in rings:
            wait_came(i, way, step - 1)
            slots[i][way, step - 1] = plus_part(i, way, step - 1)[1]
            next_copy(i, way, step).start()

    def turn(rings):
        for i, way in rings:
            wait_came(i, way, size - 2)
            span, total = plus_part(i, way, size - 2)
            outs[i][span] = total
            out_copy(i, way, 0).start()

    def pass_on(rings, step):
        for i, way in rings:
            out_copy(i, way, step - 1).wait_recv()
            out_copy(i, way, step).start()

    early, late = [(i, way) for i in (0, 1) for way in (0, 1)], [(2, 0), (2, 1)]

    other_core = remote(
        give_ref, came_ref, hop_sems.at[0, 0], hop_sems.at[0, 1], (me, differing(row, 1))
    )
    other_core.start()
    begin(early)

    rows_used, per_row = bucket_ref.shape[0], ds_ref.shape[0] // bucket_ref.shape[0]
    units = rows_used * buckets
    per_round = -(-units // max(2 * (size - 2), 1))

    def bucket_unit(u, carry):
        r, b = u // buckets, u % buckets
        sums = [jnp.zeros((8, LANES), F32) for _ in range(per_row)]
        for c in range(0, doc, LANES):
            hit = ids_ref[: c + LANES, c : c + LANES] == b
            for h in range(per_row):
                grads = scores_ref[r * per_row + h, : c + LANES, c : c + LANES].astype(F32)
                kept = jnp.where(hit, grads, 0.0).reshape(-1, 8, LANES)
                sums[h] = sums[h] + jnp.sum(kept, axis=0)
        for h in range(per_row):
            bucket_ref[r, h, pl.ds(b, 1), :] = jnp.sum(sums[h], axis=0, keepdims=True)
        return carry

    def bucket_round(k):
        low = jnp.minimum(k * per_round, units)
        lax.fori_loop(low, jnp.minimum(low + per_round, units), bucket_unit, 0)

    bucket_ref[...] = jnp.zeros_like(bucket_ref)
    part_ref[...] = jnp.zeros_like(part_ref)
    load_scores.wait()

    def early_step(step, carry):
        advance(early, step)
        bucket_round(step - 1)
        return carry

    middle = min(2, size - 1)
    lax.fori_loop(1, middle, early_step, 0)

    load_kept.wait()
    other_core.wait_recv()
    kinds, count = kept_ref.shape[0], folded_ref.shape[0]
    rows = kept_ref.shape[1] // count

    def fold(index, target, span_of):
        span = slice(index * rows, (index + 1) * rows)
        for kind in range(kinds):
            total = kept_ref[kind, span].astype(F32) + came_ref[kind, span].astype(F32)
            target[span_of(kind)] = total.astype(BF16)

    def kind_rows(kind):
        return slice(kind * rows, (kind + 1) * rows)

    other_chip = None
    if count == 2:
        fold(1, folded_ref.at[1], kind_rows)
        other_chip = remote(
            folded_ref.at[1],
            far_came_ref,
            hop_sems.at[1, 0],
            hop_sems.at[1, 1],
            (me, differing(row, 2)),
        )
        other_chip.start()
    fold(0, folded_ref.at[0], kind_rows)

    lax.fori_loop(middle, size - 1, early_step, 0)
    turn(early)
    used = slice(0, kinds * rows)
    if other_chip is None:
        part_ref[used] = folded_ref[0]
    else:
        other_chip.wait_recv()
        total = folded_ref[0].astype(F32) + far_came_ref[...].astype(F32)
        part_ref[used] = total.astype(BF16)
    begin(late)

    def middle_step(step, carry):
        pass_on(early, step)
        advance(late, step)
        bucket_round(size - 2 + step - 1)
        return carry

    lax.fori_loop(1, size - 1, middle_step, 0)
    if size == 2:
        lax.fori_loop(0, units, bucket_unit, 0)
    turn(late)

    features = gain_refs[0].shape[1]
    per_gain = features // LANES
    gain_rows = len(gain_refs) * per_gain
    small_ref[...] = jnp.zeros_like(small_ref)
    for i, ref in enumerate(gain_refs):
        total = jnp.sum(ref[...], axis=0, keepdims=True)
        for c in range(per_gain):
            at = i * per_gain + c
            small_ref[at : at + 1, :] = total[:, c * LANES : (c + 1) * LANES]
    for r in range(rows_used):
        block_sums = bucket_ref[r].reshape(LANES, LANES).T
        at = gain_rows + r
        small_ref[at : at + 1, :] = jnp.sum(block_sums, axis=0, keepdims=True)

    def near_copy(t):
        return remote(
            small_ref,
            near_ref.at[row],
            small_sems.at[0, t],
            small_sems.at[1, t],
            (me, (row + t) % peers),
        )

    def far_copy(t):
        return remote(
            far_ref.at[me],
            far_ref.at[me],
            small_sems.at[2, t],
            small_sems.at[3, t],
            ((me + t) % size, row),
        )

    for t in range(1, peers):
        near_copy(t).start()
    near_ref[pl.ds(row, 1)] = small_ref[...][None]
    for t in range(1, peers):
        near_copy(t).wait_recv()
    own = rows_used // peers
    total, sums = None, None
    for k in range(peers):
        gains = near_ref[k, :gain_rows]
        mine = near_ref[k, pl.ds(gain_rows + own * share_place(row, k, peers), own)]
        total = gains if total is None else total + gains
        sums = mine if sums is None else sums + mine
    small_ref_rows = far_ref.shape[1]
    far_ref[pl.ds(me, 1)] = jnp.concatenate(
        [total, sums, jnp.zeros((small_ref_rows - gain_rows - own, LANES), F32)], axis=0
    )[None]

    def far_start(t, carry):
        far_copy(t).start()
        return carry

    lax.fori_loop(1, size, far_start, 0)

    def late_step(step, carry):
        pass_on(late, step)
        return carry

    lax.fori_loop(1, size - 1, late_step, 0)

    def far_wait(t, carry):
        far_copy(t).wait()
        return carry

    lax.fori_loop(1, size, far_wait, 0)

    def far_add(k, total):
        return total + far_ref[k]

    small_out_ref[...] = lax.fori_loop(1, size, far_add, far_ref[0])
    for i, way in early + late:
        out_copy(i, way, size - 2).wait_recv()

    for t in range(1, peers):
        near_copy(t).wait_send()
    other_core.wait_send()
    if other_chip is not None:
        other_chip.wait_send()
    for i, way in early + late:
        first_copy(i, way).wait_send()

    def sent(step, carry):
        for i, way in early + late:
            next_copy(i, way, step).wait_send()
        return carry

    lax.fori_loop(1, size - 1, sent, 0)

    def sent_out(step, carry):
        for i, way in early + late:
            out_copy(i, way, step).wait_send()
        return carry

    lax.fori_loop(0, size - 1, sent_out, 0)


def tail_sums(size, peers, buckets, heads, hidden, cross, give, keep, ids, ds, gains):
    assert peers in (2, 4)
    grain = 2 * 16 * size
    kinds, half, features = keep.shape
    count = peers // 2
    rows = [hidden[0].shape[0], cross[0].shape[0], kinds * half // count]
    padded = [r + -r % grain for r in rows]
    hidden = [jnp.pad(h, ((0, padded[0] - rows[0]), (0, 0))) for h in hidden]
    cross = [jnp.pad(c, ((0, padded[1] - rows[1]), (0, 0))) for c in cross]
    lines = peers * (-(-heads * buckets // LANES))
    small = len(gains) * features // LANES + lines
    small = shape((small + -small % 8, LANES), F32)
    vmem, hbm = pl.BlockSpec(memory_space=pltpu.VMEM), pl.BlockSpec(memory_space=pl.ANY)
    steps = pltpu.SemaphoreType.DMA((3, 2, size - 1))
    *sums, small = pl.pallas_call(
        functools.partial(tail_kernel, size, peers, buckets, heads),
        in_specs=[*[vmem] * (2 * len(hidden)), hbm, hbm, vmem, hbm, *[vmem] * len(gains)],
        out_specs=[vmem] * 4,
        out_shape=[*[shape((p, features), BF16) for p in padded], small],
        scratch_shapes=[
            *[pltpu.VMEM((2, size - 1, p // (2 * size), features), BF16) for p in padded],
            *[pltpu.VMEM((2, p // (2 * size), features), BF16) for p in padded[:2]],
            pltpu.VMEM(keep.shape, BF16),
            pltpu.VMEM(keep.shape, BF16),
            pltpu.VMEM((count, rows[2], features), BF16),
            pltpu.VMEM((rows[2], features), BF16),
            pltpu.VMEM((padded[2], features), BF16),
            pltpu.VMEM(ds.shape, BF16),
            pltpu.VMEM((lines, LANES // buckets, buckets, LANES), F32),
            pltpu.VMEM(small.shape, F32),
            pltpu.VMEM((peers, *small.shape), F32),
            pltpu.VMEM((size, *small.shape), F32),
            steps,
            steps,
            steps,
            steps,
            pltpu.SemaphoreType.DMA((4, max(size, peers))),
            pltpu.SemaphoreType.DMA((2, 2)),
            pltpu.SemaphoreType.DMA((2,)),
        ],
        compiler_params=pltpu.CompilerParams(
            vmem_limit_bytes=VMEM_BYTES, collective_id=0, has_side_effects=True
        ),
        cost_estimate=cost(),
        name="tail_sums",
    )(*hidden, *cross, give, keep, ids, ds, *gains)
    return [total[:r] for total, r in zip(sums, rows)], small


def swap(array, bit, size):
    return lax.ppermute(array, "mp", [(i, i ^ bit) for i in range(size)])


def after(array, *others):
    return lax.optimization_barrier((array, others))[0]


def shards(
    decoder_rows,
    memory_rows,
    decoder_token_length,
    memory_length,
    bucket_ids,
    relative_bucket_bias,
    self_gain,
    self_query,
    self_key,
    self_value,
    self_out,
    cross_gain,
    cross_query,
    cross_key,
    cross_value,
    cross_out,
    hidden_gain,
    widen_weight,
    narrow_weight,
    layer_cotangent,
):
    dp_size = lax.axis_size("dp")
    mp_size = lax.axis_size("mp")
    me = lax.axis_index("mp")
    doc, features = decoder_rows.shape
    slots = memory_rows.shape[0]
    cols = self_query.shape[1]
    heads = cols // HEAD_DIM
    buckets = relative_bucket_bias.shape[0]
    order = [*range(1, mp_size, 2), *range(0, mp_size, 2)]

    doc_length = lax.dynamic_index_in_dim(decoder_token_length, me, keepdims=False)
    doc_memory = lax.dynamic_index_in_dim(memory_length, me)
    position = jnp.arange(doc, dtype=jnp.int32)
    allowed = (position[:, None] <= position[None, :]) & (position[:, None] < doc_length)
    ids = jnp.where(allowed, bucket_ids.T, buckets)
    bias_rows = jnp.zeros((TABLE_ROWS, features), BF16)
    bias_rows = bias_rows.at[:heads, :buckets].set(relative_bucket_bias.T)
    own_self = pack(
        (self_query.T, False), (self_key.T, False), (self_value.T, False), (self_out, False), (bias_rows, False)
    )
    own_cross = pack(
        (cross_query.T, False), (cross_key.T, False), (cross_value.T, False), (cross_out, False)
    )
    own_hidden = pack((widen_weight, True), (narrow_weight, False))

    def first_hops(own):
        shares, bit = {0: own}, mp_size // 2
        while bit > 1:
            for j in list(shares):
                shares[j | bit] = swap(shares[j], bit, mp_size)
            bit //= 2
        return shares

    def last_hop(shares, *others):
        if 1 not in shares:
            shares[1] = swap(shares[0], 1, mp_size)
        for j in range(2, mp_size, 2):
            shares[j] = after(shares[j], *others)
            shares[j | 1] = swap(shares[j], 1, mp_size)
        return shares

    near_self = first_hops(own_self)
    near_self[1] = swap(own_self, 1, mp_size)
    memory_rows = after(memory_rows, own_self)
    w_self = last_hop(near_self, own_cross, own_hidden, ids)
    w_self = [w_self[j] for j in order]
    near_cross = first_hops(own_cross)
    near_hidden = first_hops(own_hidden)
    near_hidden[1] = swap(own_hidden, 1, mp_size)
    memory_seen = lax.all_to_all(
        memory_rows.reshape(dp_size, slots // dp_size, features), "dp", 0, 0
    ).reshape(slots, features)

    gain_self = self_gain.astype(F32)[None]
    gain_cross = cross_gain.astype(F32)[None]
    gain_hidden = hidden_gain.astype(F32)[None]

    *saved_self, after_self = self_forward(heads, buckets, decoder_rows, gain_self, w_self, ids)
    w_cross = last_hop(near_cross, after_self)
    w_cross = [w_cross[j] for j in order]
    *saved_cross, after_cross = cross_forward(
        heads, after_self, gain_cross, memory_seen, doc_memory, w_cross
    )

    before, hidden_sums, w_hidden = (), [], near_hidden
    for j in range(0, mp_size, 2):
        summed, *before = feed_forward(
            after_cross,
            gain_hidden,
            layer_cotangent,
            [w_hidden[j + 1], w_hidden[j]],
            before,
            j == mp_size - 2,
        )
        hidden_sums.append(summed.reshape(-1, features))
        if j == 0:
            w_hidden = last_hop(near_hidden, before[0])
    layer_output, grad_after_cross, branch, hidden_gain_grad = before
    hidden_sums[1:] = [swap(summed, 2, mp_size) for summed in hidden_sums[1:]]

    *cross_sums, grad_memory, grad_after_self, branch, cross_gain_grad = cross_backward(
        heads,
        after_self,
        gain_cross,
        memory_seen,
        doc_memory,
        branch,
        grad_after_cross,
        saved_cross,
        w_cross,
    )
    memory_grad = lax.all_to_all(
        grad_memory.reshape(dp_size, slots // dp_size, features), "dp", 0, 0
    ).reshape(slots, features)
    cross_sums[1:] = [
        swap(after(share, hidden_sums[1:]), 2, mp_size) for share in cross_sums[1:]
    ]

    give, keep, score_grads, input_grad, self_gain_grad = self_backward(
        heads,
        buckets,
        decoder_rows,
        gain_self,
        ids,
        branch,
        grad_after_self,
        saved_self,
        w_self,
    )
    (sum_hidden, sum_cross, sum_self), small = tail_sums(
        dp_size,
        mp_size,
        buckets,
        heads,
        hidden_sums,
        cross_sums,
        give,
        keep,
        ids,
        score_grads,
        (self_gain_grad, cross_gain_grad, hidden_gain_grad),
    )
    wide_grad, narrow_grad, self_grads, cross_grads = finish(sum_hidden, sum_cross, sum_self)
    gain_rows = 3 * features // LANES
    gains = small[:gain_rows].reshape(3, features)
    lines = -(-heads * buckets // LANES)
    sums = small[gain_rows : gain_rows + lines, : heads // lines * buckets]
    position_grad = sums.reshape(heads, buckets).T

    return (
        layer_output,
        input_grad,
        memory_grad,
        position_grad,
        gains[0],
        *[grad.T for grad in self_grads[:3]],
        self_grads[3],
        gains[1],
        *[grad.T for grad in cross_grads[:3]],
        cross_grads[3],
        gains[2],
        wide_grad,
        narrow_grad,
    )


def solution(mesh):
    return jax.shard_map(
        shards,
        mesh=mesh,
        in_specs=(
            P(("dp", "mp"), None),
            P(("dp", "mp"), None),
            P("dp"),
            P("dp"),
            P(),
            P(None, "mp"),
            P(),
            P(None, "mp"),
            P(None, "mp"),
            P(None, "mp"),
            P("mp", None),
            P(),
            P(None, "mp"),
            P(None, "mp"),
            P(None, "mp"),
            P("mp", None),
            P(),
            P(None, "mp"),
            P("mp", None),
            P(("dp", "mp"), None),
        ),
        out_specs=(
            P(("dp", "mp"), None),
            P(("dp", "mp"), None),
            P(("dp", "mp"), None),
            P(None, "mp"),
            P(),
            P(None, "mp"),
            P(None, "mp"),
            P(None, "mp"),
            P("mp", None),
            P(),
            P(None, "mp"),
            P(None, "mp"),
            P(None, "mp"),
            P("mp", None),
            P(),
            P(None, "mp"),
            P("mp", None),
        ),
        check_vma=False,
    )
```

```python
import functools

import jax
import jax.numpy as jnp
from jax import lax
from jax.experimental import pallas as pl
from jax.experimental.pallas import tpu as pltpu
from jax.sharding import PartitionSpec as P

HEAD_DIM = 64
NORM_EPS = 1e-06
MASKED = -1e30
SCALE = HEAD_DIM**-0.5
BF16 = jnp.bfloat16
F32 = jnp.float32
LANES = 128
TABLE_ROWS = 16
HEAD_BLOCK = 256
BLOCK_HEADS = HEAD_BLOCK // HEAD_DIM
Q_BLOCK = 256
K_BLOCK = 256
HIDDEN_BLOCK = 256
MEMORY_BLOCK = 256
ROW_BLOCK = 128
VMEM_BYTES = 56 * 1024 * 1024
GELU_ROOT = 0.7978845608028654
GELU_CUBE = 0.044715


def dot_nn(a, b):
    return lax.dot_general(a, b, (((1,), (0,)), ((), ())), preferred_element_type=F32)


def dot_nt(a, b):
    return lax.dot_general(a, b, (((1,), (1,)), ((), ())), preferred_element_type=F32)


def dot_tn(a, b):
    return lax.dot_general(a, b, (((0,), (0,)), ((), ())), preferred_element_type=F32)


def flip(a):
    return a.astype(F32).T.astype(BF16)


def spans(size, step):
    return [slice(i, i + step) for i in range(0, size, step)]


def norm_scale(rows):
    return lax.rsqrt(jnp.mean(rows * rows, axis=-1, keepdims=True) + NORM_EPS)


def norm_into(normed_ref, rows_ref, gain_ref):
    for span in spans(rows_ref.shape[0], ROW_BLOCK):
        rows = rows_ref[span].astype(F32)
        normed_ref[span] = (rows * norm_scale(rows) * gain_ref[...]).astype(BF16)


def norm_back_into(span, grad, out_ref, low_ref, gain_grad_ref, rows_ref, gain_ref, add_ref):
    rows = rows_ref[span].astype(F32)
    scale = norm_scale(rows)
    unit = rows * scale
    grad_unit = grad * gain_ref[...]
    mean = jnp.mean(grad_unit * unit, axis=-1, keepdims=True)
    out = add_ref[span].astype(F32) + scale * (grad_unit - unit * mean)
    out_ref[span] = out
    if low_ref is not None:
        low_ref[span] = out.astype(BF16)
    gain_grad_ref[...] += jnp.sum((grad * unit).reshape(-1, 8, rows.shape[1]), axis=0)


def gelu_and_slope(v):
    square = v * v
    bend = jnp.tanh(GELU_ROOT * (v + GELU_CUBE * v * square))
    half = 0.5 * (1.0 + bend)
    slope = half + 0.5 * v * (1.0 - bend * bend) * GELU_ROOT * (1.0 + 3.0 * GELU_CUBE * square)
    return v * half, slope


def lane_block(start):
    return pl.ds(pl.multiple_of(start, LANES), LANES)


def extra_lanes(rows, allowed):
    lane = lax.broadcasted_iota(jnp.int32, (rows, LANES), 1) % HEAD_DIM
    first = MASKED if allowed is None else jnp.where(allowed, 0.0, MASKED)
    return jnp.where(lane == 0, first, jnp.where(lane < 4, 1.0, 0.0)).astype(BF16)


def pick(which, block, other):
    lane = lax.broadcasted_iota(jnp.int32, block.shape, 1)
    return jnp.where((lane < HEAD_DIM) == (which == 0), block, other)


def half_rows(which):
    return slice(which * HEAD_DIM, (which + 1) * HEAD_DIM)


def split(values):
    high = values.astype(BF16).astype(F32)
    rest = values - high
    middle = rest.astype(BF16).astype(F32)
    return high, middle, rest - middle


def with_extra(which, block_t, masked, minus):
    columns = block_t.shape[1]
    row = lax.broadcasted_iota(jnp.int32, (HEAD_DIM, columns), 0)
    extra = jnp.where(row == 0, 1.0 if masked else 0.0, 0.0)
    if minus is not None:
        for i, part in enumerate(split(minus)):
            extra = jnp.where(row == i + 1, -part, extra)
    own = block_t[half_rows(which)]
    return jnp.concatenate([own, extra] if which == 0 else [extra, own], axis=0).astype(BF16)


def bias_block(table_ref, ids_ref, index, rows, start):
    row = jnp.broadcast_to(table_ref[pl.ds(index, 1), :], (rows, LANES))
    return jnp.concatenate(
        [
            jnp.take_along_axis(row, ids_ref[:rows, c : c + LANES], axis=1)
            for c in range(start, start + Q_BLOCK, LANES)
        ],
        axis=1,
    )


def greet_other_core():
    me, row = lax.axis_index("dp"), lax.axis_index("mp")
    barrier = pltpu.get_barrier_semaphore()
    other = (me, row + 1 - 2 * (row % 2))
    pl.semaphore_signal(barrier, inc=1, device_id=other, device_id_type=pl.DeviceIdType.MESH)
    pl.semaphore_wait(barrier, 1)


def to_other_core(source, target, sems):
    me, row = lax.axis_index("dp"), lax.axis_index("mp")
    return pltpu.make_async_remote_copy(
        src_ref=source,
        dst_ref=target,
        send_sem=sems.at[0],
        recv_sem=sems.at[1],
        device_id=(me, row + 1 - 2 * (row % 2)),
        device_id_type=pl.DeviceIdType.MESH,
    )


def low_sum(a, b):
    return (a.astype(F32) + b.astype(F32)).astype(BF16)


class Stack:
    def __init__(self, sources, stack_ref, sems, kinds, rows):
        features = stack_ref.shape[0] // kinds
        self.copies = [
            [
                pltpu.make_async_copy(
                    source.at[pl.ds(kind * rows, rows)],
                    stack_ref.at[pl.ds(kind * features + p * rows, rows)],
                    sems.at[p, kind],
                )
                for p, source in enumerate(sources)
            ]
            for kind in range(kinds)
        ]

    def start(self):
        for copies in self.copies:
            for copy in copies:
                copy.start()

    def wait(self, *kinds):
        for kind in kinds:
            for copy in self.copies[kind]:
                copy.wait()


def table_copies(sources, tables_ref, sems, kinds):
    start = sources[0].shape[0] - TABLE_ROWS
    return [
        pltpu.make_async_copy(
            source.at[pl.ds(start, TABLE_ROWS)], tables_ref.at[p], sems.at[p, kinds]
        )
        for p, source in enumerate(sources)
    ]


def table_into(table_ref, tables_ref, heads, buckets):
    for p in range(tables_ref.shape[0]):
        rows = tables_ref[p, :, :LANES].astype(F32)
        lane = lax.broadcasted_iota(jnp.int32, rows.shape, 1)
        rows = jnp.where(lane < buckets, rows, MASKED)
        for h in range(heads):
            table_ref[p * heads + h : p * heads + h + 1, :] = rows[h : h + 1, :]


def self_forward_kernel(heads, buckets, shares, rows_ref, gain_ref, ids_ref, *refs):
    sources = refs[:shares]
    q_ref, k_ref, v_ref, mixed_ref, lse_ref, out_ref = refs[shares : shares + 6]
    w_ref, tables_ref, table_ref, normed_ref, sems = refs[shares + 6 :]
    step = pl.program_id(0)
    doc, features = rows_ref.shape
    stack = Stack(sources, w_ref, sems, 4, heads * HEAD_DIM)

    @pl.when(step == 0)
    def _():
        stack.start()
        tables = table_copies(sources, tables_ref, sems, 4)
        for copy in tables:
            copy.start()
        norm_into(normed_ref, rows_ref, gain_ref)
        out_ref[...] = rows_ref[...].astype(F32)
        for copy in tables:
            copy.wait()
        table_into(table_ref, tables_ref, heads, buckets)
        stack.wait(0, 1, 2, 3)

    def weights(kind):
        start = pl.multiple_of(kind * features + step * HEAD_BLOCK, HEAD_BLOCK)
        return w_ref[pl.ds(start, HEAD_BLOCK)]

    for kind, ref in enumerate((q_ref, k_ref, v_ref)):
        ref[...] = dot_nt(normed_ref[...], weights(kind)).astype(BF16)
    none = jnp.zeros((doc, LANES), BF16)
    for pair in range(BLOCK_HEADS // 2):
        lanes = slice(pair * LANES, (pair + 1) * LANES)
        k, v_t = k_ref[:, lanes], flip(v_ref[:, lanes])
        q_t = flip(q_ref[:, lanes].astype(F32) * SCALE)
        k_of = [pick(which, k, none) for which in range(2)]
        for span in spans(doc, Q_BLOCK):
            rows, mixed = span.stop, []
            for which in range(2):
                h = 2 * pair + which
                s = dot_nn(k_of[which][:rows], q_t[:, span])
                s = s + bias_block(table_ref, ids_ref, step * BLOCK_HEADS + h, rows, span.start)
                top = jnp.max(s, axis=0, keepdims=True)
                p = jnp.exp(s - top)
                total = jnp.sum(p, axis=0, keepdims=True)
                mixed.append(dot_nn(v_t[half_rows(which), :rows], p.astype(BF16)) / total)
                lse_ref[0, h : h + 1, span] = top + jnp.log(total)
            mixed_ref[span, lanes] = jnp.concatenate(mixed, axis=0).T.astype(BF16)
    out_ref[...] += dot_nn(mixed_ref[...], weights(3))


def self_backward_kernel(heads, buckets, shares, *refs):
    rows_ref, gain_ref, ids_ref, branch_ref, add_ref = refs[:5]
    q_ref, k_ref, v_ref, mixed_ref, lse_ref = refs[5:10]
    sources = refs[10 : 10 + shares]
    give_ref, keep_ref, ds_ref, out_ref, gain_grad_ref = refs[10 + shares : 15 + shares]
    w_ref, tables_ref, table_ref, normed_ref, g_ref, grad_ref, sems = refs[15 + shares :]
    step = pl.program_id(0)
    doc, features = rows_ref.shape
    half = features // 2
    stack = Stack(sources, w_ref, sems, 4, heads * HEAD_DIM)

    @pl.when(step == 0)
    def _():
        stack.start()
        tables = table_copies(sources, tables_ref, sems, 4)
        for copy in tables:
            copy.start()
        norm_into(normed_ref, rows_ref, gain_ref)
        for copy in tables:
            copy.wait()
        table_into(table_ref, tables_ref, heads, buckets)
        stack.wait(3)

    start = pl.multiple_of(3 * features + step * HEAD_BLOCK, HEAD_BLOCK)
    g_ref[...] = dot_nt(branch_ref[...], w_ref[pl.ds(start, HEAD_BLOCK)]).astype(BF16)
    none = jnp.zeros((doc, LANES), BF16)
    ones = extra_lanes(doc, None)
    for pair in range(BLOCK_HEADS // 2):
        lanes = lane_block(step * HEAD_BLOCK + pair * LANES)
        q, k, v = q_ref[:, lanes], k_ref[:, lanes], v_ref[:, lanes]
        g = g_ref[:, pair * LANES : (pair + 1) * LANES]
        q_t, k_t = q.astype(F32).T * SCALE, flip(k)
        g_t = g.astype(F32).T
        inner = g_t * mixed_ref[:, lanes].astype(F32).T
        per_head = []
        for which in range(2):
            h = 2 * pair + which
            minus = jnp.sum(inner[half_rows(which)], axis=0, keepdims=True)
            per_head.append(
                (
                    pick(which, k, ones),
                    pick(which, v, ones),
                    with_extra(which, q_t, False, lse_ref[0, h : h + 1, :]),
                    with_extra(which, g_t, False, minus),
                    pick(which, q, none),
                    pick(which, g, none),
                )
            )
        grad_k = grad_v = None
        for span in spans(doc, Q_BLOCK):
            rows, grad_q, part_k, part_v = span.stop, [], None, None
            for which, (k_of, v_of, q_with, g_with, q_of, g_of) in enumerate(per_head):
                h = 2 * pair + which
                s = dot_nn(k_of[:rows], q_with[:, span])
                s = s + bias_block(table_ref, ids_ref, step * BLOCK_HEADS + h, rows, span.start)
                p = jnp.exp(s)
                ds = (p * dot_nn(v_of[:rows], g_with[:, span])).astype(BF16)
                ds_ref[h, :rows, span] = ds
                grad_q.append(dot_nn(k_t[half_rows(which), :rows], ds))
                to_v = dot_nn(p.astype(BF16), g_of[span])
                to_k = dot_nn(ds, q_of[span])
                part_v = to_v if part_v is None else part_v + to_v
                part_k = to_k if part_k is None else part_k + to_k
            grad_q = (jnp.concatenate(grad_q, axis=0) * SCALE).T
            grad_ref[0, span, lanes] = grad_q.astype(BF16)
            if grad_v is not None:
                part_v = jnp.concatenate(
                    [part_v[: span.start] + grad_v, part_v[span.start :]], axis=0
                )
                part_k = jnp.concatenate(
                    [part_k[: span.start] + grad_k, part_k[span.start :]], axis=0
                )
            grad_v, grad_k = part_v, part_k
        grad_ref[1, :, lanes] = (grad_k * SCALE).astype(BF16)
        grad_ref[2, :, lanes] = grad_v.astype(BF16)

    @pl.when(step == pl.num_programs(0) - 1)
    def _():
        stack.wait(0, 1, 2)
        for ref, columns in ((give_ref, slice(0, half)), (keep_ref, slice(half, features))):
            for kind in range(3):
                ref[kind] = dot_tn(grad_ref[kind, :, columns], normed_ref[...]).astype(BF16)
            ref[3] = dot_tn(mixed_ref[:, columns], branch_ref[...]).astype(BF16)
        gain_grad_ref[...] = jnp.zeros_like(gain_grad_ref)
        for span in spans(doc, ROW_BLOCK):
            back = dot_nn(grad_ref[0, span], w_ref[:features])
            back = back + dot_nn(grad_ref[1, span], w_ref[features : 2 * features])
            back = back + dot_nn(grad_ref[2, span], w_ref[2 * features : 3 * features])
            norm_back_into(
                span, back, out_ref, None, gain_grad_ref, rows_ref, gain_ref, add_ref
            )


def cross_forward_kernel(heads, shares, length_ref, rows_ref, gain_ref, memory_ref, *refs):
    sources = refs[:shares]
    q_ref, k_ref, v_ref, mixed_ref, lse_ref, out_ref = refs[shares : shares + 6]
    w_ref, normed_ref, extra_ref, p_ref, sems = refs[shares + 6 :]
    step = pl.program_id(0)
    (doc, features), slots = rows_ref.shape, memory_ref.shape[0]
    stack = Stack(sources, w_ref, sems, 4, heads * HEAD_DIM)

    @pl.when(step == 0)
    def _():
        stack.start()
        norm_into(normed_ref, rows_ref, gain_ref)
        out_ref[...] = rows_ref[...]
        slot = lax.broadcasted_iota(jnp.int32, (slots, LANES), 0)
        extra_ref[...] = extra_lanes(slots, slot < length_ref[0])
        stack.wait(0, 1, 2, 3)

    def weights(kind):
        start = pl.multiple_of(kind * features + step * HEAD_BLOCK, HEAD_BLOCK)
        return w_ref[pl.ds(start, HEAD_BLOCK)]

    q_ref[...] = dot_nt(normed_ref[...], weights(0)).astype(BF16)
    k_ref[...] = dot_nt(memory_ref[...], weights(1)).astype(BF16)
    v_ref[...] = dot_nt(memory_ref[...], weights(2)).astype(BF16)

    units = [
        (pair, which, span)
        for pair in range(BLOCK_HEADS // 2)
        for span in spans(doc, Q_BLOCK)
        for which in range(2)
    ]
    v_t = [flip(v_ref[:, p * LANES : (p + 1) * LANES]) for p in range(BLOCK_HEADS // 2)]
    q_t = [
        q_ref[:, p * LANES : (p + 1) * LANES].astype(F32).T * SCALE
        for p in range(BLOCK_HEADS // 2)
    ]

    def scores(unit):
        pair, which, span = unit
        q_with = with_extra(which, q_t[pair][:, span], True, None)
        k_of = pick(which, k_ref[:, pair * LANES : (pair + 1) * LANES], extra_ref[...])
        return [dot_nn(k_of[rows], q_with) for rows in spans(slots, K_BLOCK)]

    mixed = {}
    ahead = scores(units[0])
    for i, (pair, which, span) in enumerate(units):
        s, slot = ahead, i % 2
        if i + 1 < len(units):
            ahead = scores(units[i + 1])
        top = functools.reduce(jnp.maximum, [jnp.max(c, axis=0, keepdims=True) for c in s])
        total = None
        for rows, chunk in zip(spans(slots, K_BLOCK), s):
            p = jnp.exp(chunk - top)
            part = jnp.sum(p, axis=0, keepdims=True)
            total = part if total is None else total + part
            p_ref[slot, rows] = p.astype(BF16)
        h = 2 * pair + which
        lse_ref[0, h : h + 1, span] = top + jnp.log(total)
        mixed[which] = dot_nn(v_t[pair][half_rows(which)], p_ref[slot]) / total
        if which == 1:
            out = jnp.concatenate([mixed[0], mixed[1]], axis=0).T
            mixed_ref[span, pair * LANES : (pair + 1) * LANES] = out.astype(BF16)
    out_ref[...] += dot_nn(mixed_ref[...], weights(3))


def cross_backward_kernel(heads, shares, length_ref, *refs):
    gain_ref, branch_ref, q_ref, mixed_ref, lse_ref = refs[:5]
    rows_in, memory_in, add_in, k_in, v_in = refs[5:10]
    sources = refs[10 : 10 + shares]
    count = shares // 2
    sums, refs = refs[10 + shares : 10 + shares + count], refs[10 + shares + count :]
    memory_out, out_ref, low_ref, gain_grad_ref = refs[:4]
    rows_ref, memory_ref, add_ref, k_ref, v_ref = refs[4:9]
    (
        w_ref,
        normed_ref,
        extra_ref,
        g_ref,
        grad_q_ref,
        grad_ref,
        ds_ref,
        give_ref,
        keep_ref,
        came_ref,
        memory_grad_ref,
        sems,
        load_sems,
        key_sems,
        out_sems,
        swap_sems,
    ) = refs[9:]
    (doc, features), slots = rows_ref.shape, memory_ref.shape[0]
    half, blocks = features // 2, features // HEAD_BLOCK
    stack = Stack(sources, w_ref, sems, 4, heads * HEAD_DIM)
    loads = [
        pltpu.make_async_copy(source, target, load_sems.at[i])
        for i, (source, target) in enumerate(
            ((memory_in, memory_ref), (rows_in, rows_ref), (add_in, add_ref))
        )
    ]

    def key_copies(b):
        lanes = pl.ds(pl.multiple_of(b * HEAD_BLOCK, HEAD_BLOCK), HEAD_BLOCK)
        return [
            pltpu.make_async_copy(source.at[:, lanes], target.at[b], key_sems.at[i, b])
            for i, (source, target) in enumerate(((k_in, k_ref), (v_in, v_ref)))
        ]

    stack.start()
    for b in range(blocks):
        for copy in key_copies(b):
            copy.start()
    for copy in loads:
        copy.start()
    greet_other_core()
    slot = lax.broadcasted_iota(jnp.int32, (slots, LANES), 0)
    extra_ref[...] = extra_lanes(slots, slot < length_ref[0])
    none = jnp.zeros((doc, LANES), BF16)
    stack.wait(3)

    def one_block(step, carry):
        start = pl.multiple_of(3 * features + step * HEAD_BLOCK, HEAD_BLOCK)
        g_ref[...] = dot_nt(branch_ref[...], w_ref[pl.ds(start, HEAD_BLOCK)]).astype(BF16)
        for copy in key_copies(step):
            copy.wait()
        for pair in range(BLOCK_HEADS // 2):
            local = slice(pair * LANES, (pair + 1) * LANES)
            lanes = lane_block(step * HEAD_BLOCK + pair * LANES)
            v_lanes = lane_block(features + step * HEAD_BLOCK + pair * LANES)
            q, g = q_ref[:, lanes], g_ref[:, local]
            q_t, g_t = q.astype(F32).T * SCALE, g.astype(F32).T
            inner = g_t * mixed_ref[:, lanes].astype(F32).T
            per_head = []
            for which in range(2):
                h = 2 * pair + which
                minus = jnp.sum(inner[half_rows(which)], axis=0, keepdims=True)
                per_head.append(
                    (
                        with_extra(which, q_t, True, lse_ref[step, h : h + 1, :]),
                        with_extra(which, g_t, False, minus),
                        pick(which, q, none),
                        pick(which, g, none),
                    )
                )
            for rows in spans(slots, K_BLOCK):
                k, v, extra = k_ref[step, rows, local], v_ref[step, rows, local], extra_ref[rows]
                part_k = part_v = None
                for which, (q_with, g_with, q_of, g_of) in enumerate(per_head):
                    p = jnp.exp(dot_nn(pick(which, k, extra), q_with))
                    ds = (p * dot_nn(pick(which, v, extra), g_with)).astype(BF16)
                    ds_ref[which, rows] = ds
                    to_v = dot_nn(p.astype(BF16), g_of)
                    to_k = dot_nn(ds, q_of)
                    part_v = to_v if part_v is None else part_v + to_v
                    part_k = to_k if part_k is None else part_k + to_k
                grad_ref[rows, lanes] = (part_k * SCALE).astype(BF16)
                grad_ref[rows, v_lanes] = part_v.astype(BF16)
            k_t = flip(k_ref[step, :, local])
            grad_q = [dot_nn(k_t[half_rows(which)], ds_ref[which]) for which in range(2)]
            grad_q_ref[:, lanes] = (jnp.concatenate(grad_q, axis=0) * SCALE).T.astype(BF16)
        return carry

    lax.fori_loop(0, blocks, one_block, 0)

    for copy in loads:
        copy.wait()
    norm_into(normed_ref, rows_ref, gain_ref)

    def weight_grads(ref, first):
        columns = slice(first, first + half)
        v_columns = slice(features + first, features + first + half)
        ref[0] = dot_tn(grad_q_ref[:, columns], normed_ref[...]).astype(BF16)
        ref[1] = dot_tn(grad_ref[:, columns], memory_ref[...]).astype(BF16)
        ref[2] = dot_tn(grad_ref[:, v_columns], memory_ref[...]).astype(BF16)
        ref[3] = dot_tn(mixed_ref[:, columns], branch_ref[...]).astype(BF16)

    weight_grads(give_ref, 0)
    swap = to_other_core(give_ref, came_ref, swap_sems)
    swap.start()
    stack.wait(0, 1, 2)
    writes = []
    for i, rows in enumerate(spans(slots, MEMORY_BLOCK)):
        memory_grad_ref[rows] = dot_nn(
            grad_ref[rows], w_ref[features : 3 * features]
        ).astype(BF16)
        writes.append(
            pltpu.make_async_copy(memory_grad_ref.at[rows], memory_out.at[rows], out_sems.at[i])
        )
        writes[-1].start()
    weight_grads(keep_ref, half)
    gain_grad_ref[...] = jnp.zeros_like(gain_grad_ref)
    for span in spans(doc, ROW_BLOCK):
        back = dot_nn(grad_q_ref[span], w_ref[:features])
        norm_back_into(
            span, back, out_ref, low_ref, gain_grad_ref, rows_ref, gain_ref, add_ref
        )
    swap.wait_recv()
    rows = half // count
    for share, sums_ref in enumerate(sums):
        for kind in range(4):
            span = slice(share * rows, (share + 1) * rows)
            to = slice(kind * rows, (kind + 1) * rows)
            sums_ref[to] = low_sum(keep_ref[kind, span], came_ref[kind, span])
    swap.wait_send()
    for copy in writes:
        copy.wait()


def feed_forward_kernel(first, last, rows_ref, gain_ref, cotangent_ref, *refs):
    sources, refs = refs[:2], refs[2:]
    if not first:
        before_in, refs = refs[:2], refs[2:]
    sums_ref, layer_ref, out_ref = refs[:3]
    if last:
        low_ref, gain_grad_ref = refs[3:5]
        refs = refs[2:]
    (
        wide_ref,
        narrow_ref,
        normed_ref,
        normed_t,
        cotangent_t,
        active_ref,
        grad_ref,
        give_ref,
        keep_ref,
        came_ref,
        layer_in_ref,
        back_in_ref,
        sems,
        before_sems,
        swap_sems,
    ) = refs[3:]
    step, steps = pl.program_id(0), pl.num_programs(0)
    half = steps // 2
    doc = rows_ref.shape[0]
    hidden = sources[0].shape[0] // 2
    copies = [
        [
            pltpu.make_async_copy(
                source.at[pl.ds(kind * hidden, hidden)],
                stack.at[pl.ds(p * hidden, hidden)],
                sems.at[p, kind],
            )
            for kind, stack in enumerate((wide_ref, narrow_ref))
        ]
        for p, source in enumerate(sources)
    ]
    loads = []
    if not first:
        loads = [
            pltpu.make_async_copy(source, target, before_sems.at[i])
            for i, (source, target) in enumerate(zip(before_in, (layer_in_ref, back_in_ref)))
        ]
    swap = to_other_core(give_ref, came_ref, swap_sems)

    @pl.when(step == 0)
    def _():
        for pair in copies:
            for copy in pair:
                copy.start()
        for copy in loads:
            copy.start()
        greet_other_core()
        norm_into(normed_ref, rows_ref, gain_ref)
        for span in spans(doc, ROW_BLOCK):
            normed_t[:, span] = flip(normed_ref[span])
            cotangent_t[:, span] = flip(cotangent_ref[span])

    for p, pair in enumerate(copies):

        @pl.when(step == p * half)
        def _(pair=pair):
            for copy in pair:
                copy.wait()

    units = pl.ds(pl.multiple_of(step * HIDDEN_BLOCK, HIDDEN_BLOCK), HIDDEN_BLOCK)
    activated, slope = gelu_and_slope(dot_nn(wide_ref[units], normed_t[...]))
    active_ref[units] = activated.astype(BF16)
    grad_ref[units] = (dot_nn(narrow_ref[units], cotangent_t[...]) * slope).astype(BF16)

    def store(ref, at):
        rows = pl.ds(pl.multiple_of(at * HIDDEN_BLOCK, HIDDEN_BLOCK), HIDDEN_BLOCK)
        ref[0, rows] = dot_nn(grad_ref[units], normed_ref[...]).astype(BF16)
        ref[1, rows] = dot_nn(active_ref[units], cotangent_ref[...]).astype(BF16)

    @pl.when(step < half)
    def _():
        store(give_ref, step)

    @pl.when(step == half - 1)
    def _():
        swap.start()

    @pl.when(step >= half)
    def _():
        store(keep_ref, step - half)

    @pl.when(step == steps - 1)
    def _():
        for copy in loads:
            copy.wait()
        if last:
            gain_grad_ref[...] = jnp.zeros_like(gain_grad_ref)
        for span in spans(doc, ROW_BLOCK):
            layer = rows_ref[span] if first else layer_in_ref[span]
            layer = layer + dot_tn(active_ref[:, span], narrow_ref[...])
            layer_ref[span] = layer.astype(layer_ref.dtype)
            back = dot_tn(grad_ref[:, span], wide_ref[...])
            if not first:
                back = back + back_in_ref[span]
            if last:
                norm_back_into(
                    span, back, out_ref, low_ref, gain_grad_ref, rows_ref, gain_ref, cotangent_ref
                )
            else:
                out_ref[span] = back
        swap.wait_recv()
        for kind in range(2):
            for span in spans(hidden, HIDDEN_BLOCK):
                sums_ref[kind, span] = low_sum(keep_ref[kind, span], came_ref[kind, span])
        swap.wait_send()


def pack_kernel(flipped, *refs):
    out_ref, start = refs[-1], 0
    for source, turn in zip(refs[:-1], flipped):
        rows = source.shape[1] if turn else source.shape[0]
        span = slice(start, start + rows)
        out_ref[span] = flip(source[...]) if turn else source[...]
        start += rows


def finish_kernel(hidden_ref, cross_ref, self_ref, wide_ref, narrow_ref, *outs):
    hidden = narrow_ref.shape[0]
    for span in spans(hidden, ROW_BLOCK):
        wide_ref[:, span] = hidden_ref[span].astype(F32).T
        narrow_ref[span] = hidden_ref[hidden + span.start : hidden + span.stop].astype(F32)
    rows = outs[0].shape[0]
    for source, refs in ((self_ref, outs[:4]), (cross_ref, outs[4:])):
        for kind, ref in enumerate(refs):
            ref[...] = source[kind * rows : (kind + 1) * rows].astype(F32)


def params():
    return pltpu.CompilerParams(vmem_limit_bytes=VMEM_BYTES)


def cost(flops=1 << 20):
    return pl.CostEstimate(flops=flops, bytes_accessed=1 << 16, transcendentals=0)


def shape(dims, dtype):
    return jax.ShapeDtypeStruct(dims, dtype)


def whole(array):
    return pl.BlockSpec(
        array.shape, lambda *_: (0,) * len(array.shape), pipeline_mode=pl.Buffered(1)
    )


def result(array):
    return pl.BlockSpec(array.shape, lambda *_: (0,) * len(array.shape))


def columns(rows):
    return pl.BlockSpec((rows, HEAD_BLOCK), lambda i: (0, i))


def anywhere(arrays):
    return [pl.BlockSpec(memory_space=pl.ANY) for _ in arrays]


SCALAR = pl.BlockSpec(memory_space=pltpu.SMEM)


def call(
    kernel, name, grid, in_specs, out_specs, out_shape, scratch, args, channel=None, flops=1 << 20
):
    compiler_params = params()
    if channel is not None:
        compiler_params = pltpu.CompilerParams(
            vmem_limit_bytes=VMEM_BYTES, collective_id=channel, has_side_effects=True
        )
    return pl.pallas_call(
        kernel,
        grid=grid,
        in_specs=in_specs,
        out_specs=out_specs,
        out_shape=out_shape,
        scratch_shapes=scratch,
        compiler_params=compiler_params,
        cost_estimate=cost(flops),
        name=name,
    )(*args)


def pack(*parts):
    arrays, flipped = zip(*parts)
    rows = sum(a.shape[1] if turn else a.shape[0] for a, turn in parts)
    features = arrays[0].shape[0] if flipped[0] else arrays[0].shape[1]
    return pl.pallas_call(
        functools.partial(pack_kernel, flipped),
        out_shape=shape((rows, features), BF16),
        compiler_params=params(),
        cost_estimate=cost(),
        name="pack",
    )(*arrays)


def self_forward(heads, buckets, rows, gain, weights, ids):
    doc, features = rows.shape
    shares, steps = len(weights), features // HEAD_BLOCK
    narrow, tall = shape((doc, features), BF16), shape((doc, features), F32)
    out_shape = (*[narrow] * 4, shape((steps, 8, doc), F32), tall)
    return call(
        functools.partial(self_forward_kernel, heads, buckets, shares),
        "self_forward",
        (steps,),
        [whole(rows), whole(gain), whole(ids), *anywhere(weights)],
        (*[columns(doc)] * 4, pl.BlockSpec((1, 8, doc), lambda i: (i, 0, 0)), result(tall)),
        out_shape,
        [
            pltpu.VMEM((4 * features, features), BF16),
            pltpu.VMEM((shares, TABLE_ROWS, features), BF16),
            pltpu.VMEM((TABLE_ROWS, LANES), F32),
            pltpu.VMEM((doc, features), BF16),
            pltpu.SemaphoreType.DMA((shares, 5)),
        ],
        (rows, gain, ids, *weights),
    )


def self_backward(heads, buckets, rows, gain, ids, branch, add, saved, weights):
    doc, features = rows.shape
    shares, steps = len(weights), features // HEAD_BLOCK
    packed = shape((4, features // 2, features), BF16)
    out_shape = (
        packed,
        packed,
        shape((steps * BLOCK_HEADS, doc, doc), BF16),
        shape((doc, features), F32),
        shape((8, features), F32),
    )
    *arrays, lse = saved
    return call(
        functools.partial(self_backward_kernel, heads, buckets, shares),
        "self_backward",
        (steps,),
        [
            *[whole(a) for a in (rows, gain, ids, branch, add, *arrays)],
            pl.BlockSpec((1, 8, doc), lambda i: (i, 0, 0)),
            *anywhere(weights),
        ],
        (
            result(packed),
            result(packed),
            pl.BlockSpec((BLOCK_HEADS, doc, doc), lambda i: (i, 0, 0)),
            result(out_shape[3]),
            result(out_shape[4]),
        ),
        out_shape,
        [
            pltpu.VMEM((4 * features, features), BF16),
            pltpu.VMEM((shares, TABLE_ROWS, features), BF16),
            pltpu.VMEM((TABLE_ROWS, LANES), F32),
            pltpu.VMEM((doc, features), BF16),
            pltpu.VMEM((doc, HEAD_BLOCK), BF16),
            pltpu.VMEM((3, doc, features), BF16),
            pltpu.SemaphoreType.DMA((shares, 5)),
        ],
        (rows, gain, ids, branch, add, *arrays, lse, *weights),
    )


def cross_forward(heads, rows, gain, memory, length, weights):
    (doc, features), slots = rows.shape, memory.shape[0]
    shares, steps = len(weights), features // HEAD_BLOCK
    query, key = shape((doc, features), BF16), shape((slots, features), BF16)
    tall = shape((doc, features), F32)
    return call(
        functools.partial(cross_forward_kernel, heads, shares),
        "cross_forward",
        (steps,),
        [SCALAR, whole(rows), whole(gain), whole(memory), *anywhere(weights)],
        (
            columns(doc),
            columns(slots),
            columns(slots),
            columns(doc),
            pl.BlockSpec((1, 8, doc), lambda i: (i, 0, 0)),
            result(tall),
        ),
        (query, key, key, query, shape((steps, 8, doc), F32), tall),
        [
            pltpu.VMEM((4 * features, features), BF16),
            pltpu.VMEM((doc, features), BF16),
            pltpu.VMEM((slots, LANES), BF16),
            pltpu.VMEM((2, slots, Q_BLOCK), BF16),
            pltpu.SemaphoreType.DMA((shares, 4)),
        ],
        (length, rows, gain, memory, *weights),
    )


def cross_backward(heads, rows, gain, memory, length, branch, add, saved, weights):
    (doc, features), slots = rows.shape, memory.shape[0]
    shares, blocks = len(weights), features // HEAD_BLOCK
    count = shares // 2
    out_shape = (
        *[shape((4 * heads * HEAD_DIM, features), BF16)] * count,
        shape((slots, features), BF16),
        shape((doc, features), F32),
        shape((doc, features), BF16),
        shape((8, features), F32),
    )
    query, key, value, mixed, lse = saved
    near = (gain, branch, query, mixed, lse)
    far = (rows, memory, add, key, value, *weights)
    vmem, hbm = pl.BlockSpec(memory_space=pltpu.VMEM), pl.BlockSpec(memory_space=pl.ANY)
    packed = pltpu.VMEM((4, features // 2, features), BF16)
    block = pltpu.VMEM((blocks, slots, HEAD_BLOCK), BF16)
    return call(
        functools.partial(cross_backward_kernel, heads, shares),
        "cross_backward",
        (),
        [SCALAR, *[vmem for _ in near], *[hbm for _ in far]],
        (*[vmem] * count, hbm, vmem, vmem, vmem),
        out_shape,
        [
            pltpu.VMEM((doc, features), F32),
            pltpu.VMEM((slots, features), BF16),
            pltpu.VMEM((doc, features), F32),
            block,
            block,
            pltpu.VMEM((4 * features, features), BF16),
            pltpu.VMEM((doc, features), BF16),
            pltpu.VMEM((slots, LANES), BF16),
            pltpu.VMEM((doc, HEAD_BLOCK), BF16),
            pltpu.VMEM((doc, features), BF16),
            pltpu.VMEM((slots, 2 * features), BF16),
            pltpu.VMEM((2, slots, doc), BF16),
            packed,
            packed,
            packed,
            pltpu.VMEM((slots, features), BF16),
            pltpu.SemaphoreType.DMA((shares, 4)),
            pltpu.SemaphoreType.DMA((3,)),
            pltpu.SemaphoreType.DMA((2, blocks)),
            pltpu.SemaphoreType.DMA((slots // MEMORY_BLOCK,)),
            pltpu.SemaphoreType.DMA((2,)),
        ],
        (length, *near, *far),
        channel=1,
        flops=48 << 30,
    )


def feed_forward(rows, gain, cotangent, weights, before, last):
    (doc, features), shares = rows.shape, len(weights)
    share = weights[0].shape[0] // 2
    hidden = share * shares
    steps = hidden // HIDDEN_BLOCK
    packed, tall = shape((2, share, features), BF16), shape((doc, features), F32)
    low = shape((doc, features), BF16)
    rest = [low, tall, low, shape((8, features), F32)] if last else [tall, tall]
    kept, added = pltpu.VMEM(packed.shape, BF16), pltpu.VMEM(tall.shape, F32)
    return call(
        functools.partial(feed_forward_kernel, not before, last),
        "feed_forward",
        (steps,),
        [whole(rows), whole(gain), whole(cotangent), *anywhere(weights), *anywhere(before)],
        (result(packed), *[result(o) for o in rest]),
        (packed, *rest),
        [
            pltpu.VMEM((hidden, features), BF16),
            pltpu.VMEM((hidden, features), BF16),
            pltpu.VMEM((doc, features), BF16),
            pltpu.VMEM((features, doc), BF16),
            pltpu.VMEM((features, doc), BF16),
            pltpu.VMEM((hidden, doc), BF16),
            pltpu.VMEM((hidden, doc), BF16),
            kept,
            kept,
            kept,
            added,
            added,
            pltpu.SemaphoreType.DMA((shares, 2)),
            pltpu.SemaphoreType.DMA((2,)),
            pltpu.SemaphoreType.DMA((2,)),
        ],
        (rows, gain, cotangent, *weights, *before),
        channel=3 if before else 2,
    )


def finish(sum_hidden, sum_cross, sum_self):
    rows, features = sum_self.shape
    hidden, part = sum_hidden.shape[0] // 2, shape((rows // 4, features), F32)
    wide, narrow, *parts = pl.pallas_call(
        finish_kernel,
        out_shape=[
            shape((features, hidden), F32),
            shape((hidden, features), F32),
            *[part] * 8,
        ],
        compiler_params=params(),
        cost_estimate=cost(),
        name="finish",
    )(sum_hidden, sum_cross, sum_self)
    return wide, narrow, parts[:4], parts[4:]


def ring_place(me, size):
    return jnp.where(me % 2 == 0, me // 2, size - 1 - me // 2)


def ring_device(place, size):
    return jnp.where(place < size // 2, 2 * place, 2 * (size - 1 - place) + 1)


def differing(row, bit):
    return row + bit - 2 * bit * ((row // bit) % 2)


def share_place(row, other, peers):
    j, bit = 0, 1
    while bit < peers:
        j = j + bit * ((row // bit + other // bit) % 2)
        bit *= 2
    return (j % 2) * (j // 2) + (1 - j % 2) * (peers // 2 + j // 2)


def tail_kernel(size, peers, buckets, heads, *refs):
    terms = 1 if peers == 2 else 2
    hidden_refs, cross_refs, refs = refs[:terms], refs[terms : 2 * terms], refs[2 * terms :]
    give_ref, keep_ref, ids_ref, ds_ref, *gain_refs = refs[:7]
    outs, small_out_ref = refs[7:10], refs[10]
    slots, firsts = refs[11:14], refs[14:16]
    kept_ref, came_ref, folded_ref, far_came_ref, part_ref, scores_ref, bucket_ref = refs[16:23]
    small_ref, near_ref, far_ref = refs[23:26]
    send, came, send_out, came_out, small_sems, hop_sems, local_sems = refs[26:]
    parts = (hidden_refs, cross_refs, (part_ref,))
    me, row = lax.axis_index("dp"), lax.axis_index("mp")
    place = ring_place(me, size)
    ways = (
        (place, ring_device((place + 1) % size, size)),
        (size - 1 - place, ring_device((place + size - 1) % size, size)),
    )
    doc = ids_ref.shape[0]
    mesh = pl.DeviceIdType.MESH

    load_scores = pltpu.make_async_copy(ds_ref, scores_ref, local_sems.at[0])
    load_kept = pltpu.make_async_copy(keep_ref, kept_ref, local_sems.at[1])
    load_scores.start()
    load_kept.start()

    barrier = pltpu.get_barrier_semaphore()

    def greet(t, carry):
        pl.semaphore_signal(
            barrier, inc=1, device_id=((me + t) % size, row), device_id_type=mesh
        )
        return carry

    lax.fori_loop(1, size, greet, 0)
    for t in range(1, peers):
        pl.semaphore_signal(
            barrier, inc=1, device_id=(me, (row + t) % peers), device_id_type=mesh
        )
    pl.semaphore_wait(barrier, size - 1 + peers - 1)

    def remote(src, dst, send_sem, recv_sem, device):
        return pltpu.make_async_remote_copy(
            src_ref=src,
            dst_ref=dst,
            send_sem=send_sem,
            recv_sem=recv_sem,
            device_id=device,
            device_id_type=mesh,
        )

    def block(i, way, number):
        rows = outs[i].shape[0] // (2 * size)
        return pl.ds(pl.multiple_of((way * size + number) * rows, 16), rows)

    def part(i, span):
        total = parts[i][0][span].astype(F32)
        for ref in parts[i][1:]:
            total = total + ref[span].astype(F32)
        return total

    def first_copy(i, way):
        return remote(
            firsts[i].at[way] if i < 2 else part_ref.at[block(i, way, ways[way][0])],
            slots[i].at[way, 0],
            send.at[i, way, 0],
            came.at[i, way, 0],
            (ways[way][1], row),
        )

    def next_copy(i, way, step):
        return remote(
            slots[i].at[way, step - 1],
            slots[i].at[way, step],
            send.at[i, way, step],
            came.at[i, way, step],
            (ways[way][1], row),
        )

    def wait_came(i, way, step):
        remote(
            slots[i].at[way, step],
            slots[i].at[way, step],
            send.at[i, way, step],
            came.at[i, way, step],
            (ways[way][1], row),
        ).wait_recv()

    def out_copy(i, way, step):
        span = block(i, way, (ways[way][0] + 1 - step + size) % size)
        return remote(
            outs[i].at[span],
            outs[i].at[span],
            send_out.at[i, way, step],
            came_out.at[i, way, step],
            (ways[way][1], row),
        )

    def begin(rings):
        for i, way in rings:
            if i < 2:
                firsts[i][way] = part(i, block(i, way, ways[way][0])).astype(BF16)
            first_copy(i, way).start()

    def plus_part(i, way, step):
        span = block(i, way, (ways[way][0] - step - 1 + size) % size)
        total = slots[i][way, step].astype(F32) + part(i, span)
        return span, total.astype(BF16)

    def advance(rings, step):
        for i, way in rings:
            wait_came(i, way, step - 1)
            slots[i][way, step - 1] = plus_part(i, way, step - 1)[1]
            next_copy(i, way, step).start()

    def turn(rings):
        for i, way in rings:
            wait_came(i, way, size - 2)
            span, total = plus_part(i, way, size - 2)
            outs[i][span] = total
            out_copy(i, way, 0).start()

    def pass_on(rings, step):
        for i, way in rings:
            out_copy(i, way, step - 1).wait_recv()
            out_copy(i, way, step).start()

    early, late = [(i, way) for i in (0, 1) for way in (0, 1)], [(2, 0), (2, 1)]

    other_core = remote(
        give_ref, came_ref, hop_sems.at[0, 0], hop_sems.at[0, 1], (me, differing(row, 1))
    )
    other_core.start()
    begin(early)

    rows_used, per_row = bucket_ref.shape[0], ds_ref.shape[0] // bucket_ref.shape[0]
    units = rows_used * buckets
    per_round = -(-units // max(2 * (size - 2), 1))

    def bucket_unit(u, carry):
        r, b = u // buckets, u % buckets
        sums = [jnp.zeros((8, LANES), F32) for _ in range(per_row)]
        for c in range(0, doc, LANES):
            hit = ids_ref[: c + LANES, c : c + LANES] == b
            for h in range(per_row):
                grads = scores_ref[r * per_row + h, : c + LANES, c : c + LANES].astype(F32)
                kept = jnp.where(hit, grads, 0.0).reshape(-1, 8, LANES)
                sums[h] = sums[h] + jnp.sum(kept, axis=0)
        for h in range(per_row):
            bucket_ref[r, h, pl.ds(b, 1), :] = jnp.sum(sums[h], axis=0, keepdims=True)
        return carry

    def bucket_round(k):
        low = jnp.minimum(k * per_round, units)
        lax.fori_loop(low, jnp.minimum(low + per_round, units), bucket_unit, 0)

    bucket_ref[...] = jnp.zeros_like(bucket_ref)
    part_ref[...] = jnp.zeros_like(part_ref)
    load_scores.wait()

    def early_step(step, carry):
        advance(early, step)
        bucket_round(step - 1)
        return carry

    middle = min(2, size - 1)
    lax.fori_loop(1, middle, early_step, 0)

    load_kept.wait()
    other_core.wait_recv()
    kinds, count = kept_ref.shape[0], folded_ref.shape[0]
    rows = kept_ref.shape[1] // count

    def fold(index, target, span_of):
        span = slice(index * rows, (index + 1) * rows)
        for kind in range(kinds):
            total = kept_ref[kind, span].astype(F32) + came_ref[kind, span].astype(F32)
            target[span_of(kind)] = total.astype(BF16)

    def kind_rows(kind):
        return slice(kind * rows, (kind + 1) * rows)

    other_chip = None
    if count == 2:
        fold(1, folded_ref.at[1], kind_rows)
        other_chip = remote(
            folded_ref.at[1],
            far_came_ref,
            hop_sems.at[1, 0],
            hop_sems.at[1, 1],
            (me, differing(row, 2)),
        )
        other_chip.start()
    fold(0, folded_ref.at[0], kind_rows)

    lax.fori_loop(middle, size - 1, early_step, 0)
    turn(early)
    used = slice(0, kinds * rows)
    if other_chip is None:
        part_ref[used] = folded_ref[0]
    else:
        other_chip.wait_recv()
        total = folded_ref[0].astype(F32) + far_came_ref[...].astype(F32)
        part_ref[used] = total.astype(BF16)
    begin(late)

    def middle_step(step, carry):
        pass_on(early, step)
        advance(late, step)
        bucket_round(size - 2 + step - 1)
        return carry

    lax.fori_loop(1, size - 1, middle_step, 0)
    if size == 2:
        lax.fori_loop(0, units, bucket_unit, 0)
    turn(late)

    features = gain_refs[0].shape[1]
    per_gain = features // LANES
    gain_rows = len(gain_refs) * per_gain
    small_ref[...] = jnp.zeros_like(small_ref)
    for i, ref in enumerate(gain_refs):
        total = jnp.sum(ref[...], axis=0, keepdims=True)
        for c in range(per_gain):
            at = i * per_gain + c
            small_ref[at : at + 1, :] = total[:, c * LANES : (c + 1) * LANES]
    for r in range(rows_used):
        block_sums = bucket_ref[r].reshape(LANES, LANES).T
        at = gain_rows + r
        small_ref[at : at + 1, :] = jnp.sum(block_sums, axis=0, keepdims=True)

    def near_copy(t):
        return remote(
            small_ref,
            near_ref.at[row],
            small_sems.at[0, t],
            small_sems.at[1, t],
            (me, (row + t) % peers),
        )

    def far_copy(t):
        return remote(
            far_ref.at[me],
            far_ref.at[me],
            small_sems.at[2, t],
            small_sems.at[3, t],
            ((me + t) % size, row),
        )

    for t in range(1, peers):
        near_copy(t).start()
    near_ref[pl.ds(row, 1)] = small_ref[...][None]
    for t in range(1, peers):
        near_copy(t).wait_recv()
    own = rows_used // peers
    total, sums = None, None
    for k in range(peers):
        gains = near_ref[k, :gain_rows]
        mine = near_ref[k, pl.ds(gain_rows + own * share_place(row, k, peers), own)]
        total = gains if total is None else total + gains
        sums = mine if sums is None else sums + mine
    small_ref_rows = far_ref.shape[1]
    far_ref[pl.ds(me, 1)] = jnp.concatenate(
        [total, sums, jnp.zeros((small_ref_rows - gain_rows - own, LANES), F32)], axis=0
    )[None]

    def far_start(t, carry):
        far_copy(t).start()
        return carry

    lax.fori_loop(1, size, far_start, 0)

    def late_step(step, carry):
        pass_on(late, step)
        return carry

    lax.fori_loop(1, size - 1, late_step, 0)

    def far_wait(t, carry):
        far_copy(t).wait()
        return carry

    lax.fori_loop(1, size, far_wait, 0)

    def far_add(k, total):
        return total + far_ref[k]

    small_out_ref[...] = lax.fori_loop(1, size, far_add, far_ref[0])
    for i, way in early + late:
        out_copy(i, way, size - 2).wait_recv()

    for t in range(1, peers):
        near_copy(t).wait_send()
    other_core.wait_send()
    if other_chip is not None:
        other_chip.wait_send()
    for i, way in early + late:
        first_copy(i, way).wait_send()

    def sent(step, carry):
        for i, way in early + late:
            next_copy(i, way, step).wait_send()
        return carry

    lax.fori_loop(1, size - 1, sent, 0)

    def sent_out(step, carry):
        for i, way in early + late:
            out_copy(i, way, step).wait_send()
        return carry

    lax.fori_loop(0, size - 1, sent_out, 0)


def tail_sums(size, peers, buckets, heads, hidden, cross, give, keep, ids, ds, gains):
    assert peers in (2, 4)
    grain = 2 * 16 * size
    kinds, half, features = keep.shape
    count = peers // 2
    rows = [hidden[0].shape[0], cross[0].shape[0], kinds * half // count]
    padded = [r + -r % grain for r in rows]
    hidden = [jnp.pad(h, ((0, padded[0] - rows[0]), (0, 0))) for h in hidden]
    cross = [jnp.pad(c, ((0, padded[1] - rows[1]), (0, 0))) for c in cross]
    lines = peers * (-(-heads * buckets // LANES))
    small = len(gains) * features // LANES + lines
    small = shape((small + -small % 8, LANES), F32)
    vmem, hbm = pl.BlockSpec(memory_space=pltpu.VMEM), pl.BlockSpec(memory_space=pl.ANY)
    steps = pltpu.SemaphoreType.DMA((3, 2, size - 1))
    *sums, small = pl.pallas_call(
        functools.partial(tail_kernel, size, peers, buckets, heads),
        in_specs=[*[vmem] * (2 * len(hidden)), hbm, hbm, vmem, hbm, *[vmem] * len(gains)],
        out_specs=[vmem] * 4,
        out_shape=[*[shape((p, features), BF16) for p in padded], small],
        scratch_shapes=[
            *[pltpu.VMEM((2, size - 1, p // (2 * size), features), BF16) for p in padded],
            *[pltpu.VMEM((2, p // (2 * size), features), BF16) for p in padded[:2]],
            pltpu.VMEM(keep.shape, BF16),
            pltpu.VMEM(keep.shape, BF16),
            pltpu.VMEM((count, rows[2], features), BF16),
            pltpu.VMEM((rows[2], features), BF16),
            pltpu.VMEM((padded[2], features), BF16),
            pltpu.VMEM(ds.shape, BF16),
            pltpu.VMEM((lines, LANES // buckets, buckets, LANES), F32),
            pltpu.VMEM(small.shape, F32),
            pltpu.VMEM((peers, *small.shape), F32),
            pltpu.VMEM((size, *small.shape), F32),
            steps,
            steps,
            steps,
            steps,
            pltpu.SemaphoreType.DMA((4, max(size, peers))),
            pltpu.SemaphoreType.DMA((2, 2)),
            pltpu.SemaphoreType.DMA((2,)),
        ],
        compiler_params=pltpu.CompilerParams(
            vmem_limit_bytes=VMEM_BYTES, collective_id=0, has_side_effects=True
        ),
        cost_estimate=cost(),
        name="tail_sums",
    )(*hidden, *cross, give, keep, ids, ds, *gains)
    return [total[:r] for total, r in zip(sums, rows)], small


def swap(array, bit, size):
    return lax.ppermute(array, "mp", [(i, i ^ bit) for i in range(size)])


def after(array, *others):
    return lax.optimization_barrier((array, others))[0]


def shards(
    decoder_rows,
    memory_rows,
    decoder_token_length,
    memory_length,
    bucket_ids,
    relative_bucket_bias,
    self_gain,
    self_query,
    self_key,
    self_value,
    self_out,
    cross_gain,
    cross_query,
    cross_key,
    cross_value,
    cross_out,
    hidden_gain,
    widen_weight,
    narrow_weight,
    layer_cotangent,
):
    dp_size = lax.axis_size("dp")
    mp_size = lax.axis_size("mp")
    me = lax.axis_index("mp")
    doc, features = decoder_rows.shape
    slots = memory_rows.shape[0]
    cols = self_query.shape[1]
    heads = cols // HEAD_DIM
    buckets = relative_bucket_bias.shape[0]
    order = [*range(1, mp_size, 2), *range(0, mp_size, 2)]

    doc_length = lax.dynamic_index_in_dim(decoder_token_length, me, keepdims=False)
    doc_memory = lax.dynamic_index_in_dim(memory_length, me)
    position = jnp.arange(doc, dtype=jnp.int32)
    allowed = (position[:, None] <= position[None, :]) & (position[:, None] < doc_length)
    ids = jnp.where(allowed, bucket_ids.T, buckets)
    bias_rows = jnp.zeros((TABLE_ROWS, features), BF16)
    bias_rows = bias_rows.at[:heads, :buckets].set(relative_bucket_bias.T)
    own_self = pack(
        (self_query.T, False), (self_key.T, False), (self_value.T, False), (self_out, False), (bias_rows, False)
    )
    own_cross = pack(
        (cross_query.T, False), (cross_key.T, False), (cross_value.T, False), (cross_out, False)
    )
    own_hidden = pack((widen_weight, True), (narrow_weight, False))

    def first_hops(own):
        shares, bit = {0: own}, mp_size // 2
        while bit > 1:
            for j in list(shares):
                shares[j | bit] = swap(shares[j], bit, mp_size)
            bit //= 2
        return shares

    def last_hop(shares, *others):
        if 1 not in shares:
            shares[1] = swap(shares[0], 1, mp_size)
        for j in range(2, mp_size, 2):
            shares[j] = after(shares[j], *others)
            shares[j | 1] = swap(shares[j], 1, mp_size)
        return shares

    near_self = first_hops(own_self)
    near_self[1] = swap(own_self, 1, mp_size)
    memory_rows = after(memory_rows, own_self)
    w_self = last_hop(near_self, own_cross, own_hidden, ids)
    w_self = [w_self[j] for j in order]
    near_cross = first_hops(own_cross)
    near_hidden = first_hops(own_hidden)
    near_hidden[1] = swap(own_hidden, 1, mp_size)
    memory_seen = lax.all_to_all(
        memory_rows.reshape(dp_size, slots // dp_size, features), "dp", 0, 0
    ).reshape(slots, features)

    gain_self = self_gain.astype(F32)[None]
    gain_cross = cross_gain.astype(F32)[None]
    gain_hidden = hidden_gain.astype(F32)[None]

    *saved_self, after_self = self_forward(heads, buckets, decoder_rows, gain_self, w_self, ids)
    w_cross = last_hop(near_cross, after_self)
    w_cross = [w_cross[j] for j in order]
    *saved_cross, after_cross = cross_forward(
        heads, after_self, gain_cross, memory_seen, doc_memory, w_cross
    )

    before, hidden_sums, w_hidden = (), [], near_hidden
    for j in range(0, mp_size, 2):
        summed, *before = feed_forward(
            after_cross,
            gain_hidden,
            layer_cotangent,
            [w_hidden[j + 1], w_hidden[j]],
            before,
            j == mp_size - 2,
        )
        hidden_sums.append(summed.reshape(-1, features))
        if j == 0:
            w_hidden = last_hop(near_hidden, before[0])
    layer_output, grad_after_cross, branch, hidden_gain_grad = before
    hidden_sums[1:] = [swap(summed, 2, mp_size) for summed in hidden_sums[1:]]

    *cross_sums, grad_memory, grad_after_self, branch, cross_gain_grad = cross_backward(
        heads,
        after_self,
        gain_cross,
        memory_seen,
        doc_memory,
        branch,
        grad_after_cross,
        saved_cross,
        w_cross,
    )
    memory_grad = lax.all_to_all(
        grad_memory.reshape(dp_size, slots // dp_size, features), "dp", 0, 0
    ).reshape(slots, features)
    cross_sums[1:] = [
        swap(after(share, hidden_sums[1:]), 2, mp_size) for share in cross_sums[1:]
    ]

    give, keep, score_grads, input_grad, self_gain_grad = self_backward(
        heads,
        buckets,
        decoder_rows,
        gain_self,
        ids,
        branch,
        grad_after_self,
        saved_self,
        w_self,
    )
    (sum_hidden, sum_cross, sum_self), small = tail_sums(
        dp_size,
        mp_size,
        buckets,
        heads,
        hidden_sums,
        cross_sums,
        give,
        keep,
        ids,
        score_grads,
        (self_gain_grad, cross_gain_grad, hidden_gain_grad),
    )
    wide_grad, narrow_grad, self_grads, cross_grads = finish(sum_hidden, sum_cross, sum_self)
    gain_rows = 3 * features // LANES
    gains = small[:gain_rows].reshape(3, features)
    lines = -(-heads * buckets // LANES)
    sums = small[gain_rows : gain_rows + lines, : heads // lines * buckets]
    position_grad = sums.reshape(heads, buckets).T

    return (
        layer_output,
        input_grad,
        memory_grad,
        position_grad,
        gains[0],
        *[grad.T for grad in self_grads[:3]],
        self_grads[3],
        gains[1],
        *[grad.T for grad in cross_grads[:3]],
        cross_grads[3],
        gains[2],
        wide_grad,
        narrow_grad,
    )


def solution(mesh):
    return jax.shard_map(
        shards,
        mesh=mesh,
        in_specs=(
            P(("dp", "mp"), None),
            P(("dp", "mp"), None),
            P("dp"),
            P("dp"),
            P(),
            P(None, "mp"),
            P(),
            P(None, "mp"),
            P(None, "mp"),
            P(None, "mp"),
            P("mp", None),
            P(),
            P(None, "mp"),
            P(None, "mp"),
            P(None, "mp"),
            P("mp", None),
            P(),
            P(None, "mp"),
            P("mp", None),
            P(("dp", "mp"), None),
        ),
        out_specs=(
            P(("dp", "mp"), None),
            P(("dp", "mp"), None),
            P(("dp", "mp"), None),
            P(None, "mp"),
            P(),
            P(None, "mp"),
            P(None, "mp"),
            P(None, "mp"),
            P("mp", None),
            P(),
            P(None, "mp"),
            P(None, "mp"),
            P(None, "mp"),
            P("mp", None),
            P(),
            P(None, "mp"),
            P("mp", None),
        ),
        check_vma=False,
    )
```

```python
import functools

import jax
import jax.numpy as jnp
from jax import lax
from jax.experimental import pallas as pl
from jax.experimental.pallas import tpu as pltpu
from jax.sharding import PartitionSpec as P

HEAD_DIM = 64
NORM_EPS = 1e-06
MASKED = -1e30
SCALE = HEAD_DIM**-0.5
BF16 = jnp.bfloat16
F32 = jnp.float32
LANES = 128
TABLE_ROWS = 16
TILE_ROWS = 16
LARGEST_SUM = 1e30
HEAD_BLOCK = 256
BLOCK_HEADS = HEAD_BLOCK // HEAD_DIM
Q_BLOCK = 256
K_BLOCK = 256
HIDDEN_BLOCK = 256
MEMORY_BLOCK = 256
FINISH_BLOCK = 384
ROW_BLOCK = 128
VMEM_BYTES = 56 * 1024 * 1024
GELU_ROOT = 0.7978845608028654
GELU_CUBE = 0.044715


def dot_nn(a, b):
    return lax.dot_general(a, b, (((1,), (0,)), ((), ())), preferred_element_type=F32)


def dot_nt(a, b):
    return lax.dot_general(a, b, (((1,), (1,)), ((), ())), preferred_element_type=F32)


def dot_tn(a, b):
    return lax.dot_general(a, b, (((0,), (0,)), ((), ())), preferred_element_type=F32)


def flip(a):
    return a.astype(F32).T.astype(BF16)


def spans(size, step):
    return [slice(i, i + step) for i in range(0, size, step)]


def norm_scale(rows):
    return lax.rsqrt(jnp.mean(rows * rows, axis=-1, keepdims=True) + NORM_EPS)


def norm_into(normed_ref, rows_ref, gain_ref):
    for span in spans(rows_ref.shape[0], ROW_BLOCK):
        rows = rows_ref[span].astype(F32)
        normed_ref[span] = (rows * norm_scale(rows) * gain_ref[...]).astype(BF16)


def norm_back_into(span, grad, out_ref, low_ref, gain_grad_ref, rows_ref, gain_ref, add_ref):
    rows = rows_ref[span].astype(F32)
    scale = norm_scale(rows)
    unit = rows * scale
    grad_unit = grad * gain_ref[...]
    mean = jnp.mean(grad_unit * unit, axis=-1, keepdims=True)
    out = add_ref[span].astype(F32) + scale * (grad_unit - unit * mean)
    out_ref[span] = out
    if low_ref is not None:
        low_ref[span] = out.astype(BF16)
    gain_grad_ref[...] += jnp.sum((grad * unit).reshape(-1, 8, rows.shape[1]), axis=0)


def gelu_and_slope(v):
    square = v * v
    bend = jnp.tanh(GELU_ROOT * (v + GELU_CUBE * v * square))
    half = 0.5 * (1.0 + bend)
    slope = half + 0.5 * v * (1.0 - bend * bend) * GELU_ROOT * (1.0 + 3.0 * GELU_CUBE * square)
    return v * half, slope


def lane_block(start):
    return pl.ds(pl.multiple_of(start, LANES), LANES)


def extra_lanes(rows, allowed):
    lane = lax.broadcasted_iota(jnp.int32, (rows, LANES), 1) % HEAD_DIM
    first = MASKED if allowed is None else jnp.where(allowed, 0.0, MASKED)
    return jnp.where(lane == 0, first, jnp.where(lane < 4, 1.0, 0.0)).astype(BF16)


def pick(which, block, other):
    lane = lax.broadcasted_iota(jnp.int32, block.shape, 1)
    return jnp.where((lane < HEAD_DIM) == (which == 0), block, other)


def half_rows(which):
    return slice(which * HEAD_DIM, (which + 1) * HEAD_DIM)


def split(values):
    high = values.astype(BF16).astype(F32)
    rest = values - high
    middle = rest.astype(BF16).astype(F32)
    return high, middle, rest - middle


def with_extra(which, block_t, masked, minus):
    columns = block_t.shape[1]
    row = lax.broadcasted_iota(jnp.int32, (HEAD_DIM, columns), 0)
    extra = jnp.where(row == 0, 1.0 if masked else 0.0, 0.0)
    if minus is not None:
        for i, part in enumerate(split(minus)):
            extra = jnp.where(row == i + 1, -part, extra)
    own = block_t[half_rows(which)]
    return jnp.concatenate([own, extra] if which == 0 else [extra, own], axis=0).astype(BF16)


def bias_block(table_ref, ids_ref, index, rows, start):
    row = jnp.broadcast_to(table_ref[pl.ds(index, 1), :], (rows, LANES))
    return jnp.concatenate(
        [
            jnp.take_along_axis(row, ids_ref[:rows, c : c + LANES], axis=1)
            for c in range(start, start + Q_BLOCK, LANES)
        ],
        axis=1,
    )


def differing(row, bit):
    return row + bit - 2 * bit * ((row // bit) % 2)


def greet(*bits):
    me, row = lax.axis_index("dp"), lax.axis_index("mp")
    barrier = pltpu.get_barrier_semaphore()
    for bit in bits:
        pl.semaphore_signal(
            barrier,
            inc=1,
            device_id=(me, differing(row, bit)),
            device_id_type=pl.DeviceIdType.MESH,
        )
    pl.semaphore_wait(barrier, len(bits))


def to_differing(bit, source, target, sems):
    me, row = lax.axis_index("dp"), lax.axis_index("mp")
    return pltpu.make_async_remote_copy(
        src_ref=source,
        dst_ref=target,
        send_sem=sems.at[0],
        recv_sem=sems.at[1],
        device_id=(me, differing(row, bit)),
        device_id_type=pl.DeviceIdType.MESH,
    )


def low_sum(a, b):
    return (a.astype(F32) + b.astype(F32)).astype(BF16)


class Stack:
    def __init__(self, sources, stack_ref, sems, kinds, rows):
        features = stack_ref.shape[0] // kinds
        self.copies = [
            [
                pltpu.make_async_copy(
                    source.at[pl.ds(kind * rows, rows)],
                    stack_ref.at[pl.ds(kind * features + p * rows, rows)],
                    sems.at[p, kind],
                )
                for p, source in enumerate(sources)
            ]
            for kind in range(kinds)
        ]

    def start(self):
        for copies in self.copies:
            for copy in copies:
                copy.start()

    def wait(self, *kinds):
        for kind in kinds:
            for copy in self.copies[kind]:
                copy.wait()


def table_copies(sources, tables_ref, sems, kinds):
    start = sources[0].shape[0] - TABLE_ROWS
    return [
        pltpu.make_async_copy(
            source.at[pl.ds(start, TABLE_ROWS)], tables_ref.at[p], sems.at[p, kinds]
        )
        for p, source in enumerate(sources)
    ]


def table_into(table_ref, tables_ref, heads, buckets):
    for p in range(tables_ref.shape[0]):
        rows = tables_ref[p, :, :LANES].astype(F32)
        lane = lax.broadcasted_iota(jnp.int32, rows.shape, 1)
        rows = jnp.where(lane < buckets, rows, MASKED)
        for h in range(heads):
            table_ref[p * heads + h : p * heads + h + 1, :] = rows[h : h + 1, :]


def self_forward_kernel(heads, buckets, shares, rows_ref, gain_ref, ids_ref, *refs):
    sources = refs[:shares]
    q_ref, k_ref, v_ref, mixed_ref, lse_ref, out_ref = refs[shares : shares + 6]
    w_ref, tables_ref, table_ref, normed_ref, sems = refs[shares + 6 :]
    step = pl.program_id(0)
    doc, features = rows_ref.shape
    stack = Stack(sources, w_ref, sems, 4, heads * HEAD_DIM)

    @pl.when(step == 0)
    def _():
        stack.start()
        tables = table_copies(sources, tables_ref, sems, 4)
        for copy in tables:
            copy.start()
        norm_into(normed_ref, rows_ref, gain_ref)
        out_ref[...] = rows_ref[...].astype(F32)
        for copy in tables:
            copy.wait()
        table_into(table_ref, tables_ref, heads, buckets)
        stack.wait(0, 1, 2, 3)

    def weights(kind):
        start = pl.multiple_of(kind * features + step * HEAD_BLOCK, HEAD_BLOCK)
        return w_ref[pl.ds(start, HEAD_BLOCK)]

    for kind, ref in enumerate((q_ref, k_ref, v_ref)):
        ref[...] = dot_nt(normed_ref[...], weights(kind)).astype(BF16)
    none = jnp.zeros((doc, LANES), BF16)
    for pair in range(BLOCK_HEADS // 2):
        lanes = slice(pair * LANES, (pair + 1) * LANES)
        k, v_t = k_ref[:, lanes], flip(v_ref[:, lanes])
        q_t = flip(q_ref[:, lanes].astype(F32) * SCALE)
        k_of = [pick(which, k, none) for which in range(2)]
        for span in spans(doc, Q_BLOCK):
            rows, mixed = span.stop, []
            for which in range(2):
                h = 2 * pair + which
                s = dot_nn(k_of[which][:rows], q_t[:, span])
                s = s + bias_block(table_ref, ids_ref, step * BLOCK_HEADS + h, rows, span.start)
                top = jnp.max(s, axis=0, keepdims=True)
                p = jnp.exp(s - top)
                total = jnp.sum(p, axis=0, keepdims=True)
                mixed.append(dot_nn(v_t[half_rows(which), :rows], p.astype(BF16)) / total)
                lse_ref[0, h : h + 1, span] = top + jnp.log(total)
            mixed_ref[span, lanes] = jnp.concatenate(mixed, axis=0).T.astype(BF16)
    out_ref[...] += dot_nn(mixed_ref[...], weights(3))


def self_backward_kernel(heads, buckets, shares, *refs):
    rows_ref, gain_ref, ids_ref, branch_ref, add_ref = refs[:5]
    q_ref, k_ref, v_ref, mixed_ref, lse_ref = refs[5:10]
    sources = refs[10 : 10 + shares]
    give_ref, keep_ref, ds_ref, out_ref, gain_grad_ref = refs[10 + shares : 15 + shares]
    w_ref, tables_ref, table_ref, normed_ref, g_ref, grad_ref, sems = refs[15 + shares :]
    step = pl.program_id(0)
    doc, features = rows_ref.shape
    half = features // 2
    stack = Stack(sources, w_ref, sems, 4, heads * HEAD_DIM)

    @pl.when(step == 0)
    def _():
        stack.start()
        tables = table_copies(sources, tables_ref, sems, 4)
        for copy in tables:
            copy.start()
        norm_into(normed_ref, rows_ref, gain_ref)
        for copy in tables:
            copy.wait()
        table_into(table_ref, tables_ref, heads, buckets)
        stack.wait(3)

    start = pl.multiple_of(3 * features + step * HEAD_BLOCK, HEAD_BLOCK)
    g_ref[...] = dot_nt(branch_ref[...], w_ref[pl.ds(start, HEAD_BLOCK)]).astype(BF16)
    none = jnp.zeros((doc, LANES), BF16)
    ones = extra_lanes(doc, None)
    for pair in range(BLOCK_HEADS // 2):
        lanes = lane_block(step * HEAD_BLOCK + pair * LANES)
        q, k, v = q_ref[:, lanes], k_ref[:, lanes], v_ref[:, lanes]
        g = g_ref[:, pair * LANES : (pair + 1) * LANES]
        q_t, k_t = q.astype(F32).T * SCALE, flip(k)
        g_t = g.astype(F32).T
        inner = g_t * mixed_ref[:, lanes].astype(F32).T
        per_head = []
        for which in range(2):
            h = 2 * pair + which
            minus = jnp.sum(inner[half_rows(which)], axis=0, keepdims=True)
            per_head.append(
                (
                    pick(which, k, ones),
                    pick(which, v, ones),
                    with_extra(which, q_t, False, lse_ref[0, h : h + 1, :]),
                    with_extra(which, g_t, False, minus),
                    pick(which, q, none),
                    pick(which, g, none),
                )
            )
        grad_k = grad_v = None
        for span in spans(doc, Q_BLOCK):
            rows, grad_q, part_k, part_v = span.stop, [], None, None
            for which, (k_of, v_of, q_with, g_with, q_of, g_of) in enumerate(per_head):
                h = 2 * pair + which
                s = dot_nn(k_of[:rows], q_with[:, span])
                s = s + bias_block(table_ref, ids_ref, step * BLOCK_HEADS + h, rows, span.start)
                p = jnp.exp(s)
                ds = (p * dot_nn(v_of[:rows], g_with[:, span])).astype(BF16)
                ds_ref[h, :rows, span] = ds
                grad_q.append(dot_nn(k_t[half_rows(which), :rows], ds))
                to_v = dot_nn(p.astype(BF16), g_of[span])
                to_k = dot_nn(ds, q_of[span])
                part_v = to_v if part_v is None else part_v + to_v
                part_k = to_k if part_k is None else part_k + to_k
            grad_q = (jnp.concatenate(grad_q, axis=0) * SCALE).T
            grad_ref[0, span, lanes] = grad_q.astype(BF16)
            if grad_v is not None:
                part_v = jnp.concatenate(
                    [part_v[: span.start] + grad_v, part_v[span.start :]], axis=0
                )
                part_k = jnp.concatenate(
                    [part_k[: span.start] + grad_k, part_k[span.start :]], axis=0
                )
            grad_v, grad_k = part_v, part_k
        grad_ref[1, :, lanes] = (grad_k * SCALE).astype(BF16)
        grad_ref[2, :, lanes] = grad_v.astype(BF16)

    @pl.when(step == pl.num_programs(0) - 1)
    def _():
        stack.wait(0, 1, 2)
        for ref, columns in ((give_ref, slice(0, half)), (keep_ref, slice(half, features))):
            for kind in range(3):
                ref[kind] = dot_tn(grad_ref[kind, :, columns], normed_ref[...]).astype(BF16)
            ref[3] = dot_tn(mixed_ref[:, columns], branch_ref[...]).astype(BF16)
        gain_grad_ref[...] = jnp.zeros_like(gain_grad_ref)
        for span in spans(doc, ROW_BLOCK):
            back = dot_nn(grad_ref[0, span], w_ref[:features])
            back = back + dot_nn(grad_ref[1, span], w_ref[features : 2 * features])
            back = back + dot_nn(grad_ref[2, span], w_ref[2 * features : 3 * features])
            norm_back_into(
                span, back, out_ref, None, gain_grad_ref, rows_ref, gain_ref, add_ref
            )


def cross_forward_kernel(heads, shares, length_ref, rows_ref, gain_ref, memory_ref, *refs):
    sources = refs[:shares]
    q_ref, k_ref, v_ref, mixed_ref, lse_ref, out_ref = refs[shares : shares + 6]
    w_ref, normed_ref, extra_ref, p_ref, mix_ref, sems = refs[shares + 6 :]
    step = pl.program_id(0)
    (doc, features), slots = rows_ref.shape, memory_ref.shape[0]
    stack = Stack(sources, w_ref, sems, 4, heads * HEAD_DIM)

    @pl.when(step == 0)
    def _():
        stack.start()
        norm_into(normed_ref, rows_ref, gain_ref)
        out_ref[...] = rows_ref[...]
        slot = lax.broadcasted_iota(jnp.int32, (slots, LANES), 0)
        extra_ref[...] = extra_lanes(slots, slot < length_ref[0])
        stack.wait(0, 1, 2, 3)

    def weights(kind):
        start = pl.multiple_of(kind * features + step * HEAD_BLOCK, HEAD_BLOCK)
        return w_ref[pl.ds(start, HEAD_BLOCK)]

    q_ref[...] = dot_nt(normed_ref[...], weights(0)).astype(BF16)
    k_ref[...] = dot_nt(memory_ref[...], weights(1)).astype(BF16)
    v_ref[...] = dot_nt(memory_ref[...], weights(2)).astype(BF16)

    units = [
        (pair, which, span)
        for pair in range(BLOCK_HEADS // 2)
        for span in spans(doc, Q_BLOCK)
        for which in range(2)
    ]
    ones = jnp.ones((TILE_ROWS, slots), BF16)
    keys = spans(slots, K_BLOCK)

    def lanes_of(pair):
        return slice(pair * LANES, (pair + 1) * LANES)

    def key_side(pair, which):
        return pick(which, k_ref[:, lanes_of(pair)], extra_ref[...])

    def write(pair, which, span, top, total, mixed):
        h = 2 * pair + which
        lse_ref[0, h : h + 1, span] = top + jnp.log(total)
        mix_ref[half_rows(which)] = mixed / total
        if which == 1:
            mixed_ref[span, lanes_of(pair)] = mix_ref[...].T.astype(BF16)

    v_t = [flip(v_ref[:, lanes_of(p)]) for p in range(BLOCK_HEADS // 2)]
    q_t = [q_ref[:, lanes_of(p)].astype(F32).T * SCALE for p in range(BLOCK_HEADS // 2)]

    def begin(unit):
        pair, which, span = unit
        k_of = key_side(pair, which)
        s = dot_nn(k_of[keys[0]], with_extra(which, q_t[pair][:, span], True, None))
        top = jnp.max(s, axis=0, keepdims=True)
        return k_of, s, top, with_extra(which, q_t[pair][:, span], True, top)

    worst = jnp.zeros((1, Q_BLOCK), F32)
    ahead = begin(units[0])
    for i, (pair, which, span) in enumerate(units):
        (k_of, s, top, q_with), slot = ahead, i % 2
        p_ref[slot, keys[0]] = jnp.exp(s - top).astype(BF16)
        for rows in keys[1:]:
            p_ref[slot, rows] = jnp.exp(dot_nn(k_of[rows], q_with)).astype(BF16)
        if i + 1 < len(units):
            ahead = begin(units[i + 1])
        value_side = jnp.concatenate([v_t[pair][half_rows(which)], ones], axis=0)
        mixed = dot_nn(value_side, p_ref[slot])
        total = mixed[HEAD_DIM : HEAD_DIM + 1]
        worst = jnp.maximum(worst, total)
        write(pair, which, span, top, total, mixed[:HEAD_DIM])

    @pl.when(jnp.max(worst) > LARGEST_SUM)
    def _():
        for pair, which, span in units:
            q_with = with_extra(
                which, q_ref[:, lanes_of(pair)].astype(F32).T[:, span] * SCALE, True, None
            )
            k_of = key_side(pair, which)
            s = [dot_nn(k_of[rows], q_with) for rows in keys]
            top = functools.reduce(jnp.maximum, [jnp.max(c, axis=0, keepdims=True) for c in s])
            total = jnp.zeros_like(top)
            for rows, chunk in zip(keys, s):
                p = jnp.exp(chunk - top)
                total = total + jnp.sum(p, axis=0, keepdims=True)
                p_ref[0, rows] = p.astype(BF16)
            mixed = dot_nn(flip(v_ref[:, lanes_of(pair)])[half_rows(which)], p_ref[0])
            write(pair, which, span, top, total, mixed)

    out_ref[...] += dot_nn(mixed_ref[...], weights(3))


def cross_backward_kernel(heads, shares, length_ref, *refs):
    gain_ref, branch_ref, q_ref, mixed_ref, lse_ref = refs[:5]
    rows_in, memory_in, add_in, k_in, v_in = refs[5:10]
    sources = refs[10 : 10 + shares]
    count = shares // 2
    refs = refs[10 + shares :]
    hidden_in, refs = refs[: count - 1], refs[count - 1 :]
    hidden_out, refs = refs[: count - 1], refs[count - 1 :]
    sums, refs = refs[:count], refs[count:]
    memory_out, out_ref, low_ref, gain_grad_ref = refs[:4]
    rows_ref, memory_ref, add_ref, k_ref, v_ref = refs[4:9]
    (
        w_ref,
        normed_ref,
        extra_ref,
        g_ref,
        grad_q_ref,
        grad_ref,
        ds_ref,
        give_ref,
        keep_ref,
        came_ref,
        memory_grad_ref,
        sems,
        load_sems,
        key_sems,
        out_sems,
        swap_sems,
        hop_sems,
    ) = refs[9:]
    (doc, features), slots = rows_ref.shape, memory_ref.shape[0]
    half, blocks = features // 2, features // HEAD_BLOCK
    stack = Stack(sources, w_ref, sems, 4, heads * HEAD_DIM)
    loads = [
        pltpu.make_async_copy(source, target, load_sems.at[i])
        for i, (source, target) in enumerate(
            ((memory_in, memory_ref), (rows_in, rows_ref), (add_in, add_ref))
        )
    ]

    def key_copies(b):
        lanes = pl.ds(pl.multiple_of(b * HEAD_BLOCK, HEAD_BLOCK), HEAD_BLOCK)
        return [
            pltpu.make_async_copy(source.at[:, lanes], target.at[b], key_sems.at[i, b])
            for i, (source, target) in enumerate(((k_in, k_ref), (v_in, v_ref)))
        ]

    stack.start()
    for b in range(blocks):
        for copy in key_copies(b):
            copy.start()
    for copy in loads:
        copy.start()
    greet(*[1, 2][:count])
    hops = [
        to_differing(2, source, target, hop_sems)
        for source, target in zip(hidden_in, hidden_out)
    ]
    for hop in hops:
        hop.start()
    slot = lax.broadcasted_iota(jnp.int32, (slots, LANES), 0)
    extra_ref[...] = extra_lanes(slots, slot < length_ref[0])
    none = jnp.zeros((doc, LANES), BF16)
    stack.wait(3)

    def one_block(step, carry):
        start = pl.multiple_of(3 * features + step * HEAD_BLOCK, HEAD_BLOCK)
        g_ref[...] = dot_nt(branch_ref[...], w_ref[pl.ds(start, HEAD_BLOCK)]).astype(BF16)
        for copy in key_copies(step):
            copy.wait()
        for pair in range(BLOCK_HEADS // 2):
            local = slice(pair * LANES, (pair + 1) * LANES)
            lanes = lane_block(step * HEAD_BLOCK + pair * LANES)
            v_lanes = lane_block(features + step * HEAD_BLOCK + pair * LANES)
            q, g = q_ref[:, lanes], g_ref[:, local]
            q_t, g_t = q.astype(F32).T * SCALE, g.astype(F32).T
            inner = g_t * mixed_ref[:, lanes].astype(F32).T
            per_head = []
            for which in range(2):
                h = 2 * pair + which
                minus = jnp.sum(inner[half_rows(which)], axis=0, keepdims=True)
                per_head.append(
                    (
                        with_extra(which, q_t, True, lse_ref[step, h : h + 1, :]),
                        with_extra(which, g_t, False, minus),
                        pick(which, q, none),
                        pick(which, g, none),
                    )
                )
            for rows in spans(slots, K_BLOCK):
                k, v, extra = k_ref[step, rows, local], v_ref[step, rows, local], extra_ref[rows]
                part_k = part_v = None
                for which, (q_with, g_with, q_of, g_of) in enumerate(per_head):
                    p = jnp.exp(dot_nn(pick(which, k, extra), q_with))
                    ds = (p * dot_nn(pick(which, v, extra), g_with)).astype(BF16)
                    ds_ref[which, rows] = ds
                    to_v = dot_nn(p.astype(BF16), g_of)
                    to_k = dot_nn(ds, q_of)
                    part_v = to_v if part_v is None else part_v + to_v
                    part_k = to_k if part_k is None else part_k + to_k
                grad_ref[rows, lanes] = (part_k * SCALE).astype(BF16)
                grad_ref[rows, v_lanes] = part_v.astype(BF16)
            k_t = flip(k_ref[step, :, local])
            grad_q = [dot_nn(k_t[half_rows(which)], ds_ref[which]) for which in range(2)]
            grad_q_ref[:, lanes] = (jnp.concatenate(grad_q, axis=0) * SCALE).T.astype(BF16)
        return carry

    lax.fori_loop(0, blocks, one_block, 0)

    for copy in loads:
        copy.wait()
    norm_into(normed_ref, rows_ref, gain_ref)

    def weight_grads(ref, first):
        columns = slice(first, first + half)
        v_columns = slice(features + first, features + first + half)
        ref[0] = dot_tn(grad_q_ref[:, columns], normed_ref[...]).astype(BF16)
        ref[1] = dot_tn(grad_ref[:, columns], memory_ref[...]).astype(BF16)
        ref[2] = dot_tn(grad_ref[:, v_columns], memory_ref[...]).astype(BF16)
        ref[3] = dot_tn(mixed_ref[:, columns], branch_ref[...]).astype(BF16)

    weight_grads(give_ref, 0)
    swap = to_differing(1, give_ref, came_ref, swap_sems)
    swap.start()
    stack.wait(0, 1, 2)
    writes = []
    for i, rows in enumerate(spans(slots, MEMORY_BLOCK)):
        memory_grad_ref[rows] = dot_nn(
            grad_ref[rows], w_ref[features : 3 * features]
        ).astype(BF16)
        writes.append(
            pltpu.make_async_copy(memory_grad_ref.at[rows], memory_out.at[rows], out_sems.at[i])
        )
        writes[-1].start()
    weight_grads(keep_ref, half)
    gain_grad_ref[...] = jnp.zeros_like(gain_grad_ref)
    for span in spans(doc, ROW_BLOCK):
        back = dot_nn(grad_q_ref[span], w_ref[:features])
        norm_back_into(
            span, back, out_ref, low_ref, gain_grad_ref, rows_ref, gain_ref, add_ref
        )
    swap.wait_recv()
    rows = half // count
    for share, sums_ref in enumerate(sums):
        for kind in range(4):
            span = slice(share * rows, (share + 1) * rows)
            to = slice(kind * rows, (kind + 1) * rows)
            sums_ref[to] = low_sum(keep_ref[kind, span], came_ref[kind, span])
    swap.wait_send()
    for copy in writes:
        copy.wait()
    for hop in hops:
        hop.wait()


def feed_forward_kernel(first, last, rows_ref, gain_ref, cotangent_ref, *refs):
    sources, refs = refs[:2], refs[2:]
    if not first:
        before_in, refs = refs[:2], refs[2:]
    sums_ref, layer_ref, out_ref = refs[:3]
    if last:
        low_ref, gain_grad_ref = refs[3:5]
        refs = refs[2:]
    (
        wide_ref,
        narrow_ref,
        normed_ref,
        normed_t,
        cotangent_t,
        active_ref,
        grad_ref,
        give_ref,
        keep_ref,
        came_ref,
        layer_in_ref,
        back_in_ref,
        sems,
        before_sems,
        swap_sems,
    ) = refs[3:]
    step, steps = pl.program_id(0), pl.num_programs(0)
    half = steps // 2
    doc = rows_ref.shape[0]
    hidden = sources[0].shape[0] // 2
    copies = [
        [
            pltpu.make_async_copy(
                source.at[pl.ds(kind * hidden, hidden)],
                stack.at[pl.ds(p * hidden, hidden)],
                sems.at[p, kind],
            )
            for kind, stack in enumerate((wide_ref, narrow_ref))
        ]
        for p, source in enumerate(sources)
    ]
    loads = []
    if not first:
        loads = [
            pltpu.make_async_copy(source, target, before_sems.at[i])
            for i, (source, target) in enumerate(zip(before_in, (layer_in_ref, back_in_ref)))
        ]
    swap = to_differing(1, give_ref, came_ref, swap_sems)

    @pl.when(step == 0)
    def _():
        for pair in copies:
            for copy in pair:
                copy.start()
        for copy in loads:
            copy.start()
        greet(1)
        norm_into(normed_ref, rows_ref, gain_ref)
        for span in spans(doc, ROW_BLOCK):
            normed_t[:, span] = flip(normed_ref[span])
            cotangent_t[:, span] = flip(cotangent_ref[span])

    for p, pair in enumerate(copies):

        @pl.when(step == p * half)
        def _(pair=pair):
            for copy in pair:
                copy.wait()

    units = pl.ds(pl.multiple_of(step * HIDDEN_BLOCK, HIDDEN_BLOCK), HIDDEN_BLOCK)
    activated, slope = gelu_and_slope(dot_nn(wide_ref[units], normed_t[...]))
    active_ref[units] = activated.astype(BF16)
    grad_ref[units] = (dot_nn(narrow_ref[units], cotangent_t[...]) * slope).astype(BF16)

    def store(ref, at):
        rows = pl.ds(pl.multiple_of(at * HIDDEN_BLOCK, HIDDEN_BLOCK), HIDDEN_BLOCK)
        ref[0, rows] = dot_nn(grad_ref[units], normed_ref[...]).astype(BF16)
        ref[1, rows] = dot_nn(active_ref[units], cotangent_ref[...]).astype(BF16)

    @pl.when(step < half)
    def _():
        store(give_ref, step)

    @pl.when(step == half - 1)
    def _():
        swap.start()

    @pl.when(step >= half)
    def _():
        store(keep_ref, step - half)

    @pl.when(step == steps - 1)
    def _():
        for copy in loads:
            copy.wait()
        if last:
            gain_grad_ref[...] = jnp.zeros_like(gain_grad_ref)
        for span in spans(doc, ROW_BLOCK):
            layer = rows_ref[span] if first else layer_in_ref[span]
            layer = layer + dot_tn(active_ref[:, span], narrow_ref[...])
            layer_ref[span] = layer.astype(layer_ref.dtype)
            back = dot_tn(grad_ref[:, span], wide_ref[...])
            if not first:
                back = back + back_in_ref[span]
            if last:
                norm_back_into(
                    span, back, out_ref, low_ref, gain_grad_ref, rows_ref, gain_ref, cotangent_ref
                )
            else:
                out_ref[span] = back
        swap.wait_recv()
        for kind in range(2):
            for span in spans(hidden, HIDDEN_BLOCK):
                sums_ref[kind, span] = low_sum(keep_ref[kind, span], came_ref[kind, span])
        swap.wait_send()


def pack_kernel(flipped, *refs):
    out_ref, start = refs[-1], 0
    for source, turn in zip(refs[:-1], flipped):
        rows = source.shape[1] if turn else source.shape[0]
        span = slice(start, start + rows)
        out_ref[span] = flip(source[...]) if turn else source[...]
        start += rows


def finish_kernel(*refs):
    sources, outs, refs = refs[:3], refs[3:13], refs[13:]
    ins, wides, in_sems, out_sems = refs[:3], refs[3:13], refs[13], refs[14]
    loads, writes = [], []
    for i, (source, target) in enumerate(zip(sources, ins)):
        for j, span in enumerate(spans(target.shape[0], FINISH_BLOCK)):
            loads.append(
                pltpu.make_async_copy(source.at[span], target.at[span], in_sems.at[i, j])
            )
            loads[-1].start()

    def write(i, part):
        writes.append(
            pltpu.make_async_copy(wides[i].at[part], outs[i].at[part], out_sems.at[len(writes)])
        )
        writes[-1].start()

    waiting = iter(loads)
    hidden = wides[1].shape[0]
    for span in spans(hidden, FINISH_BLOCK):
        next(waiting).wait()
        for part in spans(FINISH_BLOCK, LANES):
            rows = slice(span.start + part.start, span.start + part.stop)
            wides[0][:, rows] = ins[0][rows].astype(F32).T
        write(0, (slice(None), span))
    for span in spans(hidden, FINISH_BLOCK):
        next(waiting).wait()
        rows = slice(hidden + span.start, hidden + span.stop)
        wides[1][span] = ins[0][rows].astype(F32)
        write(1, span)
    for i in (1, 2):
        for _ in spans(ins[i].shape[0], FINISH_BLOCK):
            next(waiting).wait()
        rows = wides[2].shape[0]
        for kind in range(4):
            at = 2 + 4 * (i - 1) + kind
            wides[at][...] = ins[i][kind * rows : (kind + 1) * rows].astype(F32)
            write(at, slice(None))
    for copy in writes:
        copy.wait()


def params():
    return pltpu.CompilerParams(vmem_limit_bytes=VMEM_BYTES)


def cost(flops=1 << 20):
    return pl.CostEstimate(flops=flops, bytes_accessed=1 << 16, transcendentals=0)


def shape(dims, dtype):
    return jax.ShapeDtypeStruct(dims, dtype)


def whole(array):
    return pl.BlockSpec(
        array.shape, lambda *_: (0,) * len(array.shape), pipeline_mode=pl.Buffered(1)
    )


def result(array):
    return pl.BlockSpec(array.shape, lambda *_: (0,) * len(array.shape))


def columns(rows):
    return pl.BlockSpec((rows, HEAD_BLOCK), lambda i: (0, i))


def anywhere(arrays):
    return [pl.BlockSpec(memory_space=pl.ANY) for _ in arrays]


SCALAR = pl.BlockSpec(memory_space=pltpu.SMEM)


def call(
    kernel, name, grid, in_specs, out_specs, out_shape, scratch, args, channel=None, flops=1 << 20
):
    compiler_params = params()
    if channel is not None:
        compiler_params = pltpu.CompilerParams(
            vmem_limit_bytes=VMEM_BYTES, collective_id=channel, has_side_effects=True
        )
    return pl.pallas_call(
        kernel,
        grid=grid,
        in_specs=in_specs,
        out_specs=out_specs,
        out_shape=out_shape,
        scratch_shapes=scratch,
        compiler_params=compiler_params,
        cost_estimate=cost(flops),
        name=name,
    )(*args)


def pack(*parts):
    arrays, flipped = zip(*parts)
    rows = sum(a.shape[1] if turn else a.shape[0] for a, turn in parts)
    features = arrays[0].shape[0] if flipped[0] else arrays[0].shape[1]
    return pl.pallas_call(
        functools.partial(pack_kernel, flipped),
        out_shape=shape((rows, features), BF16),
        compiler_params=params(),
        cost_estimate=cost(),
        name="pack",
    )(*arrays)


def self_forward(heads, buckets, rows, gain, weights, ids):
    doc, features = rows.shape
    shares, steps = len(weights), features // HEAD_BLOCK
    narrow, tall = shape((doc, features), BF16), shape((doc, features), F32)
    out_shape = (*[narrow] * 4, shape((steps, 8, doc), F32), tall)
    return call(
        functools.partial(self_forward_kernel, heads, buckets, shares),
        "self_forward",
        (steps,),
        [whole(rows), whole(gain), whole(ids), *anywhere(weights)],
        (*[columns(doc)] * 4, pl.BlockSpec((1, 8, doc), lambda i: (i, 0, 0)), result(tall)),
        out_shape,
        [
            pltpu.VMEM((4 * features, features), BF16),
            pltpu.VMEM((shares, TABLE_ROWS, features), BF16),
            pltpu.VMEM((TABLE_ROWS, LANES), F32),
            pltpu.VMEM((doc, features), BF16),
            pltpu.SemaphoreType.DMA((shares, 5)),
        ],
        (rows, gain, ids, *weights),
    )


def self_backward(heads, buckets, rows, gain, ids, branch, add, saved, weights):
    doc, features = rows.shape
    shares, steps = len(weights), features // HEAD_BLOCK
    packed = shape((4, features // 2, features), BF16)
    out_shape = (
        packed,
        packed,
        shape((steps * BLOCK_HEADS, doc, doc), BF16),
        shape((doc, features), F32),
        shape((8, features), F32),
    )
    *arrays, lse = saved
    return call(
        functools.partial(self_backward_kernel, heads, buckets, shares),
        "self_backward",
        (steps,),
        [
            *[whole(a) for a in (rows, gain, ids, branch, add, *arrays)],
            pl.BlockSpec((1, 8, doc), lambda i: (i, 0, 0)),
            *anywhere(weights),
        ],
        (
            result(packed),
            result(packed),
            pl.BlockSpec((BLOCK_HEADS, doc, doc), lambda i: (i, 0, 0)),
            result(out_shape[3]),
            result(out_shape[4]),
        ),
        out_shape,
        [
            pltpu.VMEM((4 * features, features), BF16),
            pltpu.VMEM((shares, TABLE_ROWS, features), BF16),
            pltpu.VMEM((TABLE_ROWS, LANES), F32),
            pltpu.VMEM((doc, features), BF16),
            pltpu.VMEM((doc, HEAD_BLOCK), BF16),
            pltpu.VMEM((3, doc, features), BF16),
            pltpu.SemaphoreType.DMA((shares, 5)),
        ],
        (rows, gain, ids, branch, add, *arrays, lse, *weights),
    )


def cross_forward(heads, rows, gain, memory, length, weights):
    (doc, features), slots = rows.shape, memory.shape[0]
    shares, steps = len(weights), features // HEAD_BLOCK
    query, key = shape((doc, features), BF16), shape((slots, features), BF16)
    tall = shape((doc, features), F32)
    return call(
        functools.partial(cross_forward_kernel, heads, shares),
        "cross_forward",
        (steps,),
        [SCALAR, whole(rows), whole(gain), whole(memory), *anywhere(weights)],
        (
            columns(doc),
            columns(slots),
            columns(slots),
            columns(doc),
            pl.BlockSpec((1, 8, doc), lambda i: (i, 0, 0)),
            result(tall),
        ),
        (query, key, key, query, shape((steps, 8, doc), F32), tall),
        [
            pltpu.VMEM((4 * features, features), BF16),
            pltpu.VMEM((doc, features), BF16),
            pltpu.VMEM((slots, LANES), BF16),
            pltpu.VMEM((2, slots, Q_BLOCK), BF16),
            pltpu.VMEM((LANES, Q_BLOCK), F32),
            pltpu.SemaphoreType.DMA((shares, 4)),
        ],
        (length, rows, gain, memory, *weights),
    )


def cross_backward(heads, rows, gain, memory, length, branch, add, saved, weights, hidden):
    (doc, features), slots = rows.shape, memory.shape[0]
    shares, blocks = len(weights), features // HEAD_BLOCK
    count = shares // 2
    out_shape = (
        *[shape(h.shape, BF16) for h in hidden],
        *[shape((4 * heads * HEAD_DIM, features), BF16)] * count,
        shape((slots, features), BF16),
        shape((doc, features), F32),
        shape((doc, features), BF16),
        shape((8, features), F32),
    )
    query, key, value, mixed, lse = saved
    near = (gain, branch, query, mixed, lse)
    far = (rows, memory, add, key, value, *weights, *hidden)
    vmem, hbm = pl.BlockSpec(memory_space=pltpu.VMEM), pl.BlockSpec(memory_space=pl.ANY)
    packed = pltpu.VMEM((4, features // 2, features), BF16)
    block = pltpu.VMEM((blocks, slots, HEAD_BLOCK), BF16)
    return call(
        functools.partial(cross_backward_kernel, heads, shares),
        "cross_backward",
        (),
        [SCALAR, *[vmem for _ in near], *[hbm for _ in far]],
        (*[hbm] * len(hidden), *[vmem] * count, hbm, vmem, vmem, vmem),
        out_shape,
        [
            pltpu.VMEM((doc, features), F32),
            pltpu.VMEM((slots, features), BF16),
            pltpu.VMEM((doc, features), F32),
            block,
            block,
            pltpu.VMEM((4 * features, features), BF16),
            pltpu.VMEM((doc, features), BF16),
            pltpu.VMEM((slots, LANES), BF16),
            pltpu.VMEM((doc, HEAD_BLOCK), BF16),
            pltpu.VMEM((doc, features), BF16),
            pltpu.VMEM((slots, 2 * features), BF16),
            pltpu.VMEM((2, slots, doc), BF16),
            packed,
            packed,
            packed,
            pltpu.VMEM((slots, features), BF16),
            pltpu.SemaphoreType.DMA((shares, 4)),
            pltpu.SemaphoreType.DMA((3,)),
            pltpu.SemaphoreType.DMA((2, blocks)),
            pltpu.SemaphoreType.DMA((slots // MEMORY_BLOCK,)),
            pltpu.SemaphoreType.DMA((2,)),
            pltpu.SemaphoreType.DMA((2,)),
        ],
        (length, *near, *far),
        channel=1,
    )


def feed_forward(rows, gain, cotangent, weights, before, last):
    (doc, features), shares = rows.shape, len(weights)
    share = weights[0].shape[0] // 2
    hidden = share * shares
    steps = hidden // HIDDEN_BLOCK
    packed, tall = shape((2, share, features), BF16), shape((doc, features), F32)
    low = shape((doc, features), BF16)
    rest = [low, tall, low, shape((8, features), F32)] if last else [tall, tall]
    kept, added = pltpu.VMEM(packed.shape, BF16), pltpu.VMEM(tall.shape, F32)
    return call(
        functools.partial(feed_forward_kernel, not before, last),
        "feed_forward",
        (steps,),
        [whole(rows), whole(gain), whole(cotangent), *anywhere(weights), *anywhere(before)],
        (result(packed), *[result(o) for o in rest]),
        (packed, *rest),
        [
            pltpu.VMEM((hidden, features), BF16),
            pltpu.VMEM((hidden, features), BF16),
            pltpu.VMEM((doc, features), BF16),
            pltpu.VMEM((features, doc), BF16),
            pltpu.VMEM((features, doc), BF16),
            pltpu.VMEM((hidden, doc), BF16),
            pltpu.VMEM((hidden, doc), BF16),
            kept,
            kept,
            kept,
            added,
            added,
            pltpu.SemaphoreType.DMA((shares, 2)),
            pltpu.SemaphoreType.DMA((2,)),
            pltpu.SemaphoreType.DMA((2,)),
        ],
        (rows, gain, cotangent, *weights, *before),
        channel=3 if before else 2,
    )


def finish(sum_hidden, sum_cross, sum_self):
    rows, features = sum_self.shape
    hidden, part = sum_hidden.shape[0] // 2, shape((rows // 4, features), F32)
    out_shape = [shape((features, hidden), F32), shape((hidden, features), F32), *[part] * 8]
    sources = (sum_hidden, sum_cross, sum_self)
    writes = 2 * hidden // FINISH_BLOCK + 8
    wide, narrow, *parts = pl.pallas_call(
        finish_kernel,
        in_specs=anywhere(sources),
        out_specs=anywhere(out_shape),
        out_shape=out_shape,
        scratch_shapes=[
            *[pltpu.VMEM(source.shape, BF16) for source in sources],
            *[pltpu.VMEM(out.shape, F32) for out in out_shape],
            pltpu.SemaphoreType.DMA((3, sum_hidden.shape[0] // FINISH_BLOCK)),
            pltpu.SemaphoreType.DMA((writes,)),
        ],
        compiler_params=params(),
        cost_estimate=cost(),
        name="finish",
    )(*sources)
    return wide, narrow, parts[4:], parts[:4]


def ring_place(me, size):
    return jnp.where(me % 2 == 0, me // 2, size - 1 - me // 2)


def ring_device(place, size):
    return jnp.where(place < size // 2, 2 * place, 2 * (size - 1 - place) + 1)


def share_place(row, other, peers):
    j, bit = 0, 1
    while bit < peers:
        j = j + bit * ((row // bit + other // bit) % 2)
        bit *= 2
    return (j % 2) * (j // 2) + (1 - j % 2) * (peers // 2 + j // 2)


def tail_kernel(size, peers, buckets, heads, *refs):
    terms = 1 if peers == 2 else 2
    hidden_refs, cross_refs, refs = refs[:terms], refs[terms : 2 * terms], refs[2 * terms :]
    give_ref, keep_ref, ids_ref, ds_ref, *gain_refs = refs[:7]
    outs, small_out_ref = refs[7:10], refs[10]
    slots, firsts = refs[11:14], refs[14:16]
    kept_ref, came_ref, folded_ref, far_came_ref, part_ref, scores_ref, bucket_ref = refs[16:23]
    small_ref, near_ref, far_ref = refs[23:26]
    send, came, send_out, came_out, small_sems, hop_sems, local_sems = refs[26:]
    parts = (hidden_refs, cross_refs, (part_ref,))
    me, row = lax.axis_index("dp"), lax.axis_index("mp")
    place = ring_place(me, size)
    ways = (
        (place, ring_device((place + 1) % size, size)),
        (size - 1 - place, ring_device((place + size - 1) % size, size)),
    )
    doc = ids_ref.shape[0]
    mesh = pl.DeviceIdType.MESH

    load_scores = pltpu.make_async_copy(ds_ref, scores_ref, local_sems.at[0])
    load_kept = pltpu.make_async_copy(keep_ref, kept_ref, local_sems.at[1])
    load_scores.start()
    load_kept.start()

    barrier = pltpu.get_barrier_semaphore()

    def greet(t, carry):
        pl.semaphore_signal(
            barrier, inc=1, device_id=((me + t) % size, row), device_id_type=mesh
        )
        return carry

    lax.fori_loop(1, size, greet, 0)
    for t in range(1, peers):
        pl.semaphore_signal(
            barrier, inc=1, device_id=(me, (row + t) % peers), device_id_type=mesh
        )
    pl.semaphore_wait(barrier, size - 1 + peers - 1)

    def remote(src, dst, send_sem, recv_sem, device):
        return pltpu.make_async_remote_copy(
            src_ref=src,
            dst_ref=dst,
            send_sem=send_sem,
            recv_sem=recv_sem,
            device_id=device,
            device_id_type=mesh,
        )

    def block(i, way, number):
        rows = outs[i].shape[0] // (2 * size)
        return pl.ds(pl.multiple_of((way * size + number) * rows, 16), rows)

    def part(i, span):
        total = parts[i][0][span].astype(F32)
        for ref in parts[i][1:]:
            total = total + ref[span].astype(F32)
        return total

    def first_copy(i, way):
        return remote(
            firsts[i].at[way] if i < 2 else part_ref.at[block(i, way, ways[way][0])],
            slots[i].at[way, 0],
            send.at[i, way, 0],
            came.at[i, way, 0],
            (ways[way][1], row),
        )

    def next_copy(i, way, step):
        return remote(
            slots[i].at[way, step - 1],
            slots[i].at[way, step],
            send.at[i, way, step],
            came.at[i, way, step],
            (ways[way][1], row),
        )

    def wait_came(i, way, step):
        remote(
            slots[i].at[way, step],
            slots[i].at[way, step],
            send.at[i, way, step],
            came.at[i, way, step],
            (ways[way][1], row),
        ).wait_recv()

    def out_copy(i, way, step):
        span = block(i, way, (ways[way][0] + 1 - step + size) % size)
        return remote(
            outs[i].at[span],
            outs[i].at[span],
            send_out.at[i, way, step],
            came_out.at[i, way, step],
            (ways[way][1], row),
        )

    def begin(rings):
        for i, way in rings:
            if i < 2:
                firsts[i][way] = part(i, block(i, way, ways[way][0])).astype(BF16)
            first_copy(i, way).start()

    def plus_part(i, way, step):
        span = block(i, way, (ways[way][0] - step - 1 + size) % size)
        total = slots[i][way, step].astype(F32) + part(i, span)
        return span, total.astype(BF16)

    def advance(rings, step):
        for i, way in rings:
            wait_came(i, way, step - 1)
            slots[i][way, step - 1] = plus_part(i, way, step - 1)[1]
            next_copy(i, way, step).start()

    def turn(rings):
        for i, way in rings:
            wait_came(i, way, size - 2)
            span, total = plus_part(i, way, size - 2)
            outs[i][span] = total
            out_copy(i, way, 0).start()

    def pass_on(rings, step):
        for i, way in rings:
            out_copy(i, way, step - 1).wait_recv()
            out_copy(i, way, step).start()

    early, late = [(i, way) for i in (0, 1) for way in (0, 1)], [(2, 0), (2, 1)]

    other_core = remote(
        give_ref, came_ref, hop_sems.at[0, 0], hop_sems.at[0, 1], (me, differing(row, 1))
    )
    other_core.start()
    begin(early)

    rows_used, per_row = bucket_ref.shape[0], ds_ref.shape[0] // bucket_ref.shape[0]
    units = rows_used * buckets
    per_round = -(-units // max(2 * (size - 2), 1))

    def bucket_unit(u, carry):
        r, b = u // buckets, u % buckets
        sums = [jnp.zeros((8, LANES), F32) for _ in range(per_row)]
        for c in range(0, doc, LANES):
            hit = ids_ref[: c + LANES, c : c + LANES] == b
            for h in range(per_row):
                grads = scores_ref[r * per_row + h, : c + LANES, c : c + LANES].astype(F32)
                kept = jnp.where(hit, grads, 0.0).reshape(-1, 8, LANES)
                sums[h] = sums[h] + jnp.sum(kept, axis=0)
        for h in range(per_row):
            bucket_ref[r, h, pl.ds(b, 1), :] = jnp.sum(sums[h], axis=0, keepdims=True)
        return carry

    def bucket_round(k):
        low = jnp.minimum(k * per_round, units)
        lax.fori_loop(low, jnp.minimum(low + per_round, units), bucket_unit, 0)

    bucket_ref[...] = jnp.zeros_like(bucket_ref)
    part_ref[...] = jnp.zeros_like(part_ref)
    load_scores.wait()

    def early_step(step, carry):
        advance(early, step)
        bucket_round(step - 1)
        return carry

    middle = min(2, size - 1)
    lax.fori_loop(1, middle, early_step, 0)

    load_kept.wait()
    other_core.wait_recv()
    kinds, count = kept_ref.shape[0], folded_ref.shape[0]
    rows = kept_ref.shape[1] // count

    def fold(index, target, span_of):
        span = slice(index * rows, (index + 1) * rows)
        for kind in range(kinds):
            total = kept_ref[kind, span].astype(F32) + came_ref[kind, span].astype(F32)
            target[span_of(kind)] = total.astype(BF16)

    def kind_rows(kind):
        return slice(kind * rows, (kind + 1) * rows)

    other_chip = None
    if count == 2:
        fold(1, folded_ref.at[1], kind_rows)
        other_chip = remote(
            folded_ref.at[1],
            far_came_ref,
            hop_sems.at[1, 0],
            hop_sems.at[1, 1],
            (me, differing(row, 2)),
        )
        other_chip.start()
    fold(0, folded_ref.at[0], kind_rows)

    lax.fori_loop(middle, size - 1, early_step, 0)
    turn(early)
    used = slice(0, kinds * rows)
    if other_chip is None:
        part_ref[used] = folded_ref[0]
    else:
        other_chip.wait_recv()
        total = folded_ref[0].astype(F32) + far_came_ref[...].astype(F32)
        part_ref[used] = total.astype(BF16)
    begin(late)

    def middle_step(step, carry):
        pass_on(early, step)
        advance(late, step)
        bucket_round(size - 2 + step - 1)
        return carry

    lax.fori_loop(1, size - 1, middle_step, 0)
    if size == 2:
        lax.fori_loop(0, units, bucket_unit, 0)
    turn(late)

    features = gain_refs[0].shape[1]
    per_gain = features // LANES
    gain_rows = len(gain_refs) * per_gain
    small_ref[...] = jnp.zeros_like(small_ref)
    for i, ref in enumerate(gain_refs):
        total = jnp.sum(ref[...], axis=0, keepdims=True)
        for c in range(per_gain):
            at = i * per_gain + c
            small_ref[at : at + 1, :] = total[:, c * LANES : (c + 1) * LANES]
    for r in range(rows_used):
        block_sums = bucket_ref[r].reshape(LANES, LANES).T
        at = gain_rows + r
        small_ref[at : at + 1, :] = jnp.sum(block_sums, axis=0, keepdims=True)

    def near_copy(t):
        return remote(
            small_ref,
            near_ref.at[row],
            small_sems.at[0, t],
            small_sems.at[1, t],
            (me, (row + t) % peers),
        )

    def far_copy(t):
        return remote(
            far_ref.at[me],
            far_ref.at[me],
            small_sems.at[2, t],
            small_sems.at[3, t],
            ((me + t) % size, row),
        )

    for t in range(1, peers):
        near_copy(t).start()
    near_ref[pl.ds(row, 1)] = small_ref[...][None]
    for t in range(1, peers):
        near_copy(t).wait_recv()
    own = rows_used // peers
    total, sums = None, None
    for k in range(peers):
        gains = near_ref[k, :gain_rows]
        mine = near_ref[k, pl.ds(gain_rows + own * share_place(row, k, peers), own)]
        total = gains if total is None else total + gains
        sums = mine if sums is None else sums + mine
    small_ref_rows = far_ref.shape[1]
    far_ref[pl.ds(me, 1)] = jnp.concatenate(
        [total, sums, jnp.zeros((small_ref_rows - gain_rows - own, LANES), F32)], axis=0
    )[None]

    def far_start(t, carry):
        far_copy(t).start()
        return carry

    lax.fori_loop(1, size, far_start, 0)

    def late_step(step, carry):
        pass_on(late, step)
        return carry

    lax.fori_loop(1, size - 1, late_step, 0)

    def far_wait(t, carry):
        far_copy(t).wait()
        return carry

    lax.fori_loop(1, size, far_wait, 0)

    def far_add(k, total):
        return total + far_ref[k]

    small_out_ref[...] = lax.fori_loop(1, size, far_add, far_ref[0])
    for i, way in early + late:
        out_copy(i, way, size - 2).wait_recv()

    for t in range(1, peers):
        near_copy(t).wait_send()
    other_core.wait_send()
    if other_chip is not None:
        other_chip.wait_send()
    for i, way in early + late:
        first_copy(i, way).wait_send()

    def sent(step, carry):
        for i, way in early + late:
            next_copy(i, way, step).wait_send()
        return carry

    lax.fori_loop(1, size - 1, sent, 0)

    def sent_out(step, carry):
        for i, way in early + late:
            out_copy(i, way, step).wait_send()
        return carry

    lax.fori_loop(0, size - 1, sent_out, 0)


def tail_sums(size, peers, buckets, heads, hidden, cross, give, keep, ids, ds, gains):
    assert peers in (2, 4)
    grain = 2 * 16 * size
    kinds, half, features = keep.shape
    count = peers // 2
    rows = [hidden[0].shape[0], cross[0].shape[0], kinds * half // count]
    padded = [r + -r % grain for r in rows]
    hidden = [jnp.pad(h, ((0, padded[0] - rows[0]), (0, 0))) for h in hidden]
    cross = [jnp.pad(c, ((0, padded[1] - rows[1]), (0, 0))) for c in cross]
    lines = peers * (-(-heads * buckets // LANES))
    small = len(gains) * features // LANES + lines
    small = shape((small + -small % 8, LANES), F32)
    vmem, hbm = pl.BlockSpec(memory_space=pltpu.VMEM), pl.BlockSpec(memory_space=pl.ANY)
    steps = pltpu.SemaphoreType.DMA((3, 2, size - 1))
    *sums, small = pl.pallas_call(
        functools.partial(tail_kernel, size, peers, buckets, heads),
        in_specs=[*[vmem] * (2 * len(hidden)), hbm, hbm, vmem, hbm, *[vmem] * len(gains)],
        out_specs=[vmem] * 4,
        out_shape=[*[shape((p, features), BF16) for p in padded], small],
        scratch_shapes=[
            *[pltpu.VMEM((2, size - 1, p // (2 * size), features), BF16) for p in padded],
            *[pltpu.VMEM((2, p // (2 * size), features), BF16) for p in padded[:2]],
            pltpu.VMEM(keep.shape, BF16),
            pltpu.VMEM(keep.shape, BF16),
            pltpu.VMEM((count, rows[2], features), BF16),
            pltpu.VMEM((rows[2], features), BF16),
            pltpu.VMEM((padded[2], features), BF16),
            pltpu.VMEM(ds.shape, BF16),
            pltpu.VMEM((lines, LANES // buckets, buckets, LANES), F32),
            pltpu.VMEM(small.shape, F32),
            pltpu.VMEM((peers, *small.shape), F32),
            pltpu.VMEM((size, *small.shape), F32),
            steps,
            steps,
            steps,
            steps,
            pltpu.SemaphoreType.DMA((4, max(size, peers))),
            pltpu.SemaphoreType.DMA((2, 2)),
            pltpu.SemaphoreType.DMA((2,)),
        ],
        compiler_params=pltpu.CompilerParams(
            vmem_limit_bytes=VMEM_BYTES, collective_id=0, has_side_effects=True
        ),
        cost_estimate=cost(),
        name="tail_sums",
    )(*hidden, *cross, give, keep, ids, ds, *gains)
    return [total[:r] for total, r in zip(sums, rows)], small


def swap(array, bit, size):
    return lax.ppermute(array, "mp", [(i, i ^ bit) for i in range(size)])


def after(array, *others):
    return lax.optimization_barrier((array, others))[0]


def shards(
    decoder_rows,
    memory_rows,
    decoder_token_length,
    memory_length,
    bucket_ids,
    relative_bucket_bias,
    self_gain,
    self_query,
    self_key,
    self_value,
    self_out,
    cross_gain,
    cross_query,
    cross_key,
    cross_value,
    cross_out,
    hidden_gain,
    widen_weight,
    narrow_weight,
    layer_cotangent,
):
    dp_size = lax.axis_size("dp")
    mp_size = lax.axis_size("mp")
    me = lax.axis_index("mp")
    doc, features = decoder_rows.shape
    slots = memory_rows.shape[0]
    cols = self_query.shape[1]
    heads = cols // HEAD_DIM
    buckets = relative_bucket_bias.shape[0]
    order = [*range(1, mp_size, 2), *range(0, mp_size, 2)]

    doc_length = lax.dynamic_index_in_dim(decoder_token_length, me, keepdims=False)
    doc_memory = lax.dynamic_index_in_dim(memory_length, me)
    position = jnp.arange(doc, dtype=jnp.int32)
    allowed = (position[:, None] <= position[None, :]) & (position[:, None] < doc_length)
    ids = jnp.where(allowed, bucket_ids.T, buckets)
    bias_rows = jnp.zeros((TABLE_ROWS, features), BF16)
    bias_rows = bias_rows.at[:heads, :buckets].set(relative_bucket_bias.T)
    own_self = pack(
        (self_query.T, False), (self_key.T, False), (self_value.T, False), (self_out, False), (bias_rows, False)
    )
    own_cross = pack(
        (cross_query.T, False), (cross_key.T, False), (cross_value.T, False), (cross_out, False)
    )
    own_hidden = pack((widen_weight, True), (narrow_weight, False))

    def first_hops(own):
        shares, bit = {0: own}, mp_size // 2
        while bit > 1:
            for j in list(shares):
                shares[j | bit] = swap(shares[j], bit, mp_size)
            bit //= 2
        return shares

    def last_hop(shares, *others):
        if 1 not in shares:
            shares[1] = swap(shares[0], 1, mp_size)
        for j in range(2, mp_size, 2):
            shares[j] = after(shares[j], *others)
            shares[j | 1] = swap(shares[j], 1, mp_size)
        return shares

    near_self = first_hops(own_self)
    near_self[1] = swap(own_self, 1, mp_size)
    memory_rows = after(memory_rows, own_self)
    w_self = last_hop(near_self, own_cross, own_hidden, ids)
    w_self = [w_self[j] for j in order]
    near_cross = first_hops(own_cross)
    near_hidden = first_hops(own_hidden)
    near_hidden[1] = swap(own_hidden, 1, mp_size)
    memory_seen = lax.all_to_all(
        memory_rows.reshape(dp_size, slots // dp_size, features), "dp", 0, 0
    ).reshape(slots, features)

    gain_self = self_gain.astype(F32)[None]
    gain_cross = cross_gain.astype(F32)[None]
    gain_hidden = hidden_gain.astype(F32)[None]

    *saved_self, after_self = self_forward(heads, buckets, decoder_rows, gain_self, w_self, ids)
    w_cross = last_hop(near_cross, after_self)
    w_cross = [w_cross[j] for j in order]
    *saved_cross, after_cross = cross_forward(
        heads, after_self, gain_cross, memory_seen, doc_memory, w_cross
    )

    before, hidden_sums, w_hidden = (), [], near_hidden
    for j in range(0, mp_size, 2):
        summed, *before = feed_forward(
            after_cross,
            gain_hidden,
            layer_cotangent,
            [w_hidden[j + 1], w_hidden[j]],
            before,
            j == mp_size - 2,
        )
        hidden_sums.append(summed.reshape(-1, features))
        if j == 0:
            w_hidden = last_hop(near_hidden, before[0])
    layer_output, grad_after_cross, branch, hidden_gain_grad = before

    *sums, grad_memory, grad_after_self, branch, cross_gain_grad = cross_backward(
        heads,
        after_self,
        gain_cross,
        memory_seen,
        doc_memory,
        branch,
        grad_after_cross,
        saved_cross,
        w_cross,
        hidden_sums[1:],
    )
    hidden_sums[1:], cross_sums = sums[: mp_size // 2 - 1], sums[mp_size // 2 - 1 :]
    memory_grad = lax.all_to_all(
        grad_memory.reshape(dp_size, slots // dp_size, features), "dp", 0, 0
    ).reshape(slots, features)
    cross_sums[1:] = [swap(share, 2, mp_size) for share in cross_sums[1:]]

    give, keep, score_grads, input_grad, self_gain_grad = self_backward(
        heads,
        buckets,
        decoder_rows,
        gain_self,
        ids,
        branch,
        grad_after_self,
        saved_self,
        w_self,
    )
    (sum_hidden, sum_cross, sum_self), small = tail_sums(
        dp_size,
        mp_size,
        buckets,
        heads,
        hidden_sums,
        cross_sums,
        give,
        keep,
        ids,
        score_grads,
        (self_gain_grad, cross_gain_grad, hidden_gain_grad),
    )
    wide_grad, narrow_grad, self_grads, cross_grads = finish(sum_hidden, sum_cross, sum_self)
    gain_rows = 3 * features // LANES
    gains = small[:gain_rows].reshape(3, features)
    lines = -(-heads * buckets // LANES)
    sums = small[gain_rows : gain_rows + lines, : heads // lines * buckets]
    position_grad = sums.reshape(heads, buckets).T

    return (
        layer_output,
        input_grad,
        memory_grad,
        position_grad,
        gains[0],
        *[grad.T for grad in self_grads[:3]],
        self_grads[3],
        gains[1],
        *[grad.T for grad in cross_grads[:3]],
        cross_grads[3],
        gains[2],
        wide_grad,
        narrow_grad,
    )


def solution(mesh):
    return jax.shard_map(
        shards,
        mesh=mesh,
        in_specs=(
            P(("dp", "mp"), None),
            P(("dp", "mp"), None),
            P("dp"),
            P("dp"),
            P(),
            P(None, "mp"),
            P(),
            P(None, "mp"),
            P(None, "mp"),
            P(None, "mp"),
            P("mp", None),
            P(),
            P(None, "mp"),
            P(None, "mp"),
            P(None, "mp"),
            P("mp", None),
            P(),
            P(None, "mp"),
            P("mp", None),
            P(("dp", "mp"), None),
        ),
        out_specs=(
            P(("dp", "mp"), None),
            P(("dp", "mp"), None),
            P(("dp", "mp"), None),
            P(None, "mp"),
            P(),
            P(None, "mp"),
            P(None, "mp"),
            P(None, "mp"),
            P("mp", None),
            P(),
            P(None, "mp"),
            P(None, "mp"),
            P(None, "mp"),
            P("mp", None),
            P(),
            P(None, "mp"),
            P("mp", None),
        ),
        check_vma=False,
    )
```

```python
import functools

import jax
import jax.numpy as jnp
from jax import lax
from jax.experimental import pallas as pl
from jax.experimental.pallas import tpu as pltpu
from jax.sharding import PartitionSpec as P

HEAD_DIM = 64
NORM_EPS = 1e-06
MASKED = -1e30
SCALE = HEAD_DIM**-0.5
BF16 = jnp.bfloat16
F32 = jnp.float32
LANES = 128
TABLE_ROWS = 16
TILE_ROWS = 16
LARGEST_SUM = 1e30
HEAD_BLOCK = 256
BLOCK_HEADS = HEAD_BLOCK // HEAD_DIM
Q_BLOCK = 256
K_BLOCK = 256
HIDDEN_BLOCK = 256
MEMORY_BLOCK = 256
FINISH_BLOCK = 384
ROW_BLOCK = 128
VMEM_BYTES = 56 * 1024 * 1024
GELU_ROOT = 0.7978845608028654
GELU_CUBE = 0.044715


def dot_nn(a, b):
    return lax.dot_general(a, b, (((1,), (0,)), ((), ())), preferred_element_type=F32)


def dot_nt(a, b):
    return lax.dot_general(a, b, (((1,), (1,)), ((), ())), preferred_element_type=F32)


def dot_tn(a, b):
    return lax.dot_general(a, b, (((0,), (0,)), ((), ())), preferred_element_type=F32)


def flip(a):
    return a.astype(F32).T.astype(BF16)


def spans(size, step):
    return [slice(i, i + step) for i in range(0, size, step)]


def norm_scale(rows):
    return lax.rsqrt(jnp.mean(rows * rows, axis=-1, keepdims=True) + NORM_EPS)


def norm_into(normed_ref, rows_ref, gain_ref):
    for span in spans(rows_ref.shape[0], ROW_BLOCK):
        rows = rows_ref[span].astype(F32)
        normed_ref[span] = (rows * norm_scale(rows) * gain_ref[...]).astype(BF16)


def norm_back_into(span, grad, out_ref, low_ref, gain_grad_ref, rows_ref, gain_ref, add_ref):
    rows = rows_ref[span].astype(F32)
    scale = norm_scale(rows)
    unit = rows * scale
    grad_unit = grad * gain_ref[...]
    mean = jnp.mean(grad_unit * unit, axis=-1, keepdims=True)
    out = add_ref[span].astype(F32) + scale * (grad_unit - unit * mean)
    out_ref[span] = out
    if low_ref is not None:
        low_ref[span] = out.astype(BF16)
    gain_grad_ref[...] += jnp.sum((grad * unit).reshape(-1, 8, rows.shape[1]), axis=0)


def gelu_and_slope(v):
    square = v * v
    bend = jnp.tanh(GELU_ROOT * (v + GELU_CUBE * v * square))
    half = 0.5 * (1.0 + bend)
    slope = half + 0.5 * v * (1.0 - bend * bend) * GELU_ROOT * (1.0 + 3.0 * GELU_CUBE * square)
    return v * half, slope


def lane_block(start):
    return pl.ds(pl.multiple_of(start, LANES), LANES)


def extra_lanes(rows, allowed):
    lane = lax.broadcasted_iota(jnp.int32, (rows, LANES), 1) % HEAD_DIM
    first = MASKED if allowed is None else jnp.where(allowed, 0.0, MASKED)
    return jnp.where(lane == 0, first, jnp.where(lane < 4, 1.0, 0.0)).astype(BF16)


def pick(which, block, other):
    lane = lax.broadcasted_iota(jnp.int32, block.shape, 1)
    return jnp.where((lane < HEAD_DIM) == (which == 0), block, other)


def half_rows(which):
    return slice(which * HEAD_DIM, (which + 1) * HEAD_DIM)


def split(values):
    high = values.astype(BF16).astype(F32)
    rest = values - high
    middle = rest.astype(BF16).astype(F32)
    return high, middle, rest - middle


def with_extra(which, block_t, masked, minus):
    columns = block_t.shape[1]
    row = lax.broadcasted_iota(jnp.int32, (HEAD_DIM, columns), 0)
    extra = jnp.where(row == 0, 1.0 if masked else 0.0, 0.0)
    if minus is not None:
        for i, part in enumerate(split(minus)):
            extra = jnp.where(row == i + 1, -part, extra)
    own = block_t[half_rows(which)]
    return jnp.concatenate([own, extra] if which == 0 else [extra, own], axis=0).astype(BF16)


def bias_block(table_ref, ids_ref, index, rows, start):
    row = jnp.broadcast_to(table_ref[pl.ds(index, 1), :], (rows, LANES))
    return jnp.concatenate(
        [
            jnp.take_along_axis(row, ids_ref[:rows, c : c + LANES], axis=1)
            for c in range(start, start + Q_BLOCK, LANES)
        ],
        axis=1,
    )


def ring_place(me, size):
    return jnp.where(me % 2 == 0, me // 2, size - 1 - me // 2)


def ring_device(place, size):
    return jnp.where(place < size // 2, 2 * place, 2 * (size - 1 - place) + 1)


def ring_ways(size):
    me = lax.axis_index("dp")
    place = ring_place(me, size)
    return (
        (place, ring_device((place + 1) % size, size)),
        (size - 1 - place, ring_device((place + size - 1) % size, size)),
    )


def differing(row, bit):
    return row + bit - 2 * bit * ((row // bit) % 2)


def remote(source, target, send_sem, recv_sem, device):
    return pltpu.make_async_remote_copy(
        src_ref=source,
        dst_ref=target,
        send_sem=send_sem,
        recv_sem=recv_sem,
        device_id=device,
        device_id_type=pl.DeviceIdType.MESH,
    )


def greet(bits, devices=()):
    me, row = lax.axis_index("dp"), lax.axis_index("mp")
    barrier = pltpu.get_barrier_semaphore()
    others = [(me, differing(row, bit)) for bit in bits] + [(device, row) for device in devices]
    for other in others:
        pl.semaphore_signal(
            barrier, inc=1, device_id=other, device_id_type=pl.DeviceIdType.MESH
        )
    pl.semaphore_wait(barrier, len(others))


def to_differing(bit, source, target, sems):
    me, row = lax.axis_index("dp"), lax.axis_index("mp")
    return remote(source, target, sems.at[0], sems.at[1], (me, differing(row, bit)))


class Scatter:
    def __init__(self, size, sources, parts, slots, done, send, came):
        self.size, self.sources, self.parts, self.slots = size, sources, parts, slots
        self.done, self.send, self.came = done, send, came
        self.ways, self.row = ring_ways(size), lax.axis_index("mp")
        self.rings = [(i, way) for i in range(len(parts)) for way in range(2)]

    def block(self, i, way, number):
        rows = self.slots[i].shape[2]
        return pl.ds(pl.multiple_of((way * self.size + number) * rows, 16), rows)

    def copy(self, i, way, step, source):
        return remote(
            source,
            self.slots[i].at[way, step],
            self.send.at[i, way, step],
            self.came.at[i, way, step],
            (self.ways[way][1], self.row),
        )

    def first(self, i, way):
        span = self.block(i, way, self.ways[way][0])
        return self.copy(i, way, 0, self.sources[i].at[span])

    def next(self, i, way, step):
        return self.copy(i, way, step, self.slots[i].at[way, step - 1])

    def begin(self):
        for i, way in self.rings:
            self.first(i, way).start()

    def total(self, i, way, step):
        self.copy(i, way, step, self.slots[i].at[way, step]).wait_recv()
        span = self.block(i, way, (self.ways[way][0] - step - 1 + self.size) % self.size)
        return low_sum(self.slots[i][way, step], self.parts[i][span])

    def advance(self, step):
        for i, way in self.rings:
            self.slots[i][way, step - 1] = self.total(i, way, step - 1)
            self.next(i, way, step).start()

    def turn(self):
        for i, way in self.rings:
            self.done[i][way] = self.total(i, way, self.size - 2)

    def wait_sent(self):
        for i, way in self.rings:
            self.first(i, way).wait_send()

        def sent(step, carry):
            for i, way in self.rings:
                self.next(i, way, step).wait_send()
            return carry

        lax.fori_loop(1, self.size - 1, sent, 0)


def low_sum(a, b):
    return (a.astype(F32) + b.astype(F32)).astype(BF16)


class Stack:
    def __init__(self, sources, stack_ref, sems, kinds, rows):
        features = stack_ref.shape[0] // kinds
        self.copies = [
            [
                pltpu.make_async_copy(
                    source.at[pl.ds(kind * rows, rows)],
                    stack_ref.at[pl.ds(kind * features + p * rows, rows)],
                    sems.at[p, kind],
                )
                for p, source in enumerate(sources)
            ]
            for kind in range(kinds)
        ]

    def start(self):
        for copies in self.copies:
            for copy in copies:
                copy.start()

    def wait(self, *kinds):
        for kind in kinds:
            for copy in self.copies[kind]:
                copy.wait()


def table_copies(sources, tables_ref, sems, kinds):
    start = sources[0].shape[0] - TABLE_ROWS
    return [
        pltpu.make_async_copy(
            source.at[pl.ds(start, TABLE_ROWS)], tables_ref.at[p], sems.at[p, kinds]
        )
        for p, source in enumerate(sources)
    ]


def table_into(table_ref, tables_ref, heads, buckets):
    for p in range(tables_ref.shape[0]):
        rows = tables_ref[p, :, :LANES].astype(F32)
        lane = lax.broadcasted_iota(jnp.int32, rows.shape, 1)
        rows = jnp.where(lane < buckets, rows, MASKED)
        for h in range(heads):
            table_ref[p * heads + h : p * heads + h + 1, :] = rows[h : h + 1, :]


def self_forward_kernel(heads, buckets, shares, rows_ref, gain_ref, ids_ref, *refs):
    sources = refs[:shares]
    q_ref, k_ref, v_ref, mixed_ref, lse_ref, out_ref = refs[shares : shares + 6]
    w_ref, tables_ref, table_ref, normed_ref, sems = refs[shares + 6 :]
    step = pl.program_id(0)
    doc, features = rows_ref.shape
    stack = Stack(sources, w_ref, sems, 4, heads * HEAD_DIM)

    @pl.when(step == 0)
    def _():
        stack.start()
        tables = table_copies(sources, tables_ref, sems, 4)
        for copy in tables:
            copy.start()
        norm_into(normed_ref, rows_ref, gain_ref)
        out_ref[...] = rows_ref[...].astype(F32)
        for copy in tables:
            copy.wait()
        table_into(table_ref, tables_ref, heads, buckets)
        stack.wait(0, 1, 2, 3)

    def weights(kind):
        start = pl.multiple_of(kind * features + step * HEAD_BLOCK, HEAD_BLOCK)
        return w_ref[pl.ds(start, HEAD_BLOCK)]

    for kind, ref in enumerate((q_ref, k_ref, v_ref)):
        ref[...] = dot_nt(normed_ref[...], weights(kind)).astype(BF16)
    none = jnp.zeros((doc, LANES), BF16)
    for pair in range(BLOCK_HEADS // 2):
        lanes = slice(pair * LANES, (pair + 1) * LANES)
        k, v_t = k_ref[:, lanes], flip(v_ref[:, lanes])
        q_t = flip(q_ref[:, lanes].astype(F32) * SCALE)
        k_of = [pick(which, k, none) for which in range(2)]
        for span in spans(doc, Q_BLOCK):
            rows, mixed = span.stop, []
            for which in range(2):
                h = 2 * pair + which
                s = dot_nn(k_of[which][:rows], q_t[:, span])
                s = s + bias_block(table_ref, ids_ref, step * BLOCK_HEADS + h, rows, span.start)
                top = jnp.max(s, axis=0, keepdims=True)
                p = jnp.exp(s - top)
                total = jnp.sum(p, axis=0, keepdims=True)
                mixed.append(dot_nn(v_t[half_rows(which), :rows], p.astype(BF16)) / total)
                lse_ref[0, h : h + 1, span] = top + jnp.log(total)
            mixed_ref[span, lanes] = jnp.concatenate(mixed, axis=0).T.astype(BF16)
    out_ref[...] += dot_nn(mixed_ref[...], weights(3))


def self_backward_kernel(heads, buckets, shares, *refs):
    rows_ref, gain_ref, ids_ref, branch_ref, add_ref = refs[:5]
    q_ref, k_ref, v_ref, mixed_ref, lse_ref = refs[5:10]
    sources = refs[10 : 10 + shares]
    give_ref, keep_ref, ds_ref, out_ref, gain_grad_ref = refs[10 + shares : 15 + shares]
    w_ref, tables_ref, table_ref, normed_ref, g_ref, grad_ref, sems = refs[15 + shares :]
    step = pl.program_id(0)
    doc, features = rows_ref.shape
    half = features // 2
    stack = Stack(sources, w_ref, sems, 4, heads * HEAD_DIM)

    @pl.when(step == 0)
    def _():
        stack.start()
        tables = table_copies(sources, tables_ref, sems, 4)
        for copy in tables:
            copy.start()
        norm_into(normed_ref, rows_ref, gain_ref)
        for copy in tables:
            copy.wait()
        table_into(table_ref, tables_ref, heads, buckets)
        stack.wait(3)

    start = pl.multiple_of(3 * features + step * HEAD_BLOCK, HEAD_BLOCK)
    g_ref[...] = dot_nt(branch_ref[...], w_ref[pl.ds(start, HEAD_BLOCK)]).astype(BF16)
    none = jnp.zeros((doc, LANES), BF16)
    ones = extra_lanes(doc, None)
    for pair in range(BLOCK_HEADS // 2):
        lanes = lane_block(step * HEAD_BLOCK + pair * LANES)
        q, k, v = q_ref[:, lanes], k_ref[:, lanes], v_ref[:, lanes]
        g = g_ref[:, pair * LANES : (pair + 1) * LANES]
        q_t, k_t = q.astype(F32).T * SCALE, flip(k)
        g_t = g.astype(F32).T
        inner = g_t * mixed_ref[:, lanes].astype(F32).T
        per_head = []
        for which in range(2):
            h = 2 * pair + which
            minus = jnp.sum(inner[half_rows(which)], axis=0, keepdims=True)
            per_head.append(
                (
                    pick(which, k, ones),
                    pick(which, v, ones),
                    with_extra(which, q_t, False, lse_ref[0, h : h + 1, :]),
                    with_extra(which, g_t, False, minus),
                    pick(which, q, none),
                    pick(which, g, none),
                )
            )
        grad_k = grad_v = None
        for span in spans(doc, Q_BLOCK):
            rows, grad_q, part_k, part_v = span.stop, [], None, None
            for which, (k_of, v_of, q_with, g_with, q_of, g_of) in enumerate(per_head):
                h = 2 * pair + which
                s = dot_nn(k_of[:rows], q_with[:, span])
                s = s + bias_block(table_ref, ids_ref, step * BLOCK_HEADS + h, rows, span.start)
                p = jnp.exp(s)
                ds = (p * dot_nn(v_of[:rows], g_with[:, span])).astype(BF16)
                ds_ref[h, :rows, span] = ds
                grad_q.append(dot_nn(k_t[half_rows(which), :rows], ds))
                to_v = dot_nn(p.astype(BF16), g_of[span])
                to_k = dot_nn(ds, q_of[span])
                part_v = to_v if part_v is None else part_v + to_v
                part_k = to_k if part_k is None else part_k + to_k
            grad_q = (jnp.concatenate(grad_q, axis=0) * SCALE).T
            grad_ref[0, span, lanes] = grad_q.astype(BF16)
            if grad_v is not None:
                part_v = jnp.concatenate(
                    [part_v[: span.start] + grad_v, part_v[span.start :]], axis=0
                )
                part_k = jnp.concatenate(
                    [part_k[: span.start] + grad_k, part_k[span.start :]], axis=0
                )
            grad_v, grad_k = part_v, part_k
        grad_ref[1, :, lanes] = (grad_k * SCALE).astype(BF16)
        grad_ref[2, :, lanes] = grad_v.astype(BF16)

    @pl.when(step == pl.num_programs(0) - 1)
    def _():
        stack.wait(0, 1, 2)
        for ref, columns in ((give_ref, slice(0, half)), (keep_ref, slice(half, features))):
            for kind in range(3):
                ref[kind] = dot_tn(grad_ref[kind, :, columns], normed_ref[...]).astype(BF16)
            ref[3] = dot_tn(mixed_ref[:, columns], branch_ref[...]).astype(BF16)
        gain_grad_ref[...] = jnp.zeros_like(gain_grad_ref)
        for span in spans(doc, ROW_BLOCK):
            back = dot_nn(grad_ref[0, span], w_ref[:features])
            back = back + dot_nn(grad_ref[1, span], w_ref[features : 2 * features])
            back = back + dot_nn(grad_ref[2, span], w_ref[2 * features : 3 * features])
            norm_back_into(
                span, back, out_ref, None, gain_grad_ref, rows_ref, gain_ref, add_ref
            )


def cross_forward_kernel(heads, shares, length_ref, rows_ref, gain_ref, memory_ref, *refs):
    sources = refs[:shares]
    q_ref, k_ref, v_ref, mixed_ref, lse_ref, out_ref = refs[shares : shares + 6]
    w_ref, normed_ref, extra_ref, p_ref, mix_ref, sems = refs[shares + 6 :]
    step = pl.program_id(0)
    (doc, features), slots = rows_ref.shape, memory_ref.shape[0]
    stack = Stack(sources, w_ref, sems, 4, heads * HEAD_DIM)

    @pl.when(step == 0)
    def _():
        stack.start()
        norm_into(normed_ref, rows_ref, gain_ref)
        out_ref[...] = rows_ref[...]
        slot = lax.broadcasted_iota(jnp.int32, (slots, LANES), 0)
        extra_ref[...] = extra_lanes(slots, slot < length_ref[0])
        stack.wait(0, 1, 2, 3)

    def weights(kind):
        start = pl.multiple_of(kind * features + step * HEAD_BLOCK, HEAD_BLOCK)
        return w_ref[pl.ds(start, HEAD_BLOCK)]

    q_ref[...] = dot_nt(normed_ref[...], weights(0)).astype(BF16)
    k_ref[...] = dot_nt(memory_ref[...], weights(1)).astype(BF16)
    v_ref[...] = dot_nt(memory_ref[...], weights(2)).astype(BF16)

    units = [
        (pair, which, span)
        for pair in range(BLOCK_HEADS // 2)
        for span in spans(doc, Q_BLOCK)
        for which in range(2)
    ]
    ones = jnp.ones((TILE_ROWS, slots), BF16)
    keys = spans(slots, K_BLOCK)

    def lanes_of(pair):
        return slice(pair * LANES, (pair + 1) * LANES)

    def key_side(pair, which):
        return pick(which, k_ref[:, lanes_of(pair)], extra_ref[...])

    def write(pair, which, span, top, total, mixed):
        h = 2 * pair + which
        lse_ref[0, h : h + 1, span] = top + jnp.log(total)
        mix_ref[half_rows(which)] = mixed / total
        if which == 1:
            mixed_ref[span, lanes_of(pair)] = mix_ref[...].T.astype(BF16)

    v_t = [flip(v_ref[:, lanes_of(p)]) for p in range(BLOCK_HEADS // 2)]
    q_t = [q_ref[:, lanes_of(p)].astype(F32).T * SCALE for p in range(BLOCK_HEADS // 2)]

    def begin(unit):
        pair, which, span = unit
        k_of = key_side(pair, which)
        s = dot_nn(k_of[keys[0]], with_extra(which, q_t[pair][:, span], True, None))
        top = jnp.max(s, axis=0, keepdims=True)
        return k_of, s, top, with_extra(which, q_t[pair][:, span], True, top)

    worst = jnp.zeros((1, Q_BLOCK), F32)
    ahead = begin(units[0])
    for i, (pair, which, span) in enumerate(units):
        (k_of, s, top, q_with), slot = ahead, i % 2
        p_ref[slot, keys[0]] = jnp.exp(s - top).astype(BF16)
        for rows in keys[1:]:
            p_ref[slot, rows] = jnp.exp(dot_nn(k_of[rows], q_with)).astype(BF16)
        if i + 1 < len(units):
            ahead = begin(units[i + 1])
        value_side = jnp.concatenate([v_t[pair][half_rows(which)], ones], axis=0)
        mixed = dot_nn(value_side, p_ref[slot])
        total = mixed[HEAD_DIM : HEAD_DIM + 1]
        worst = jnp.maximum(worst, total)
        write(pair, which, span, top, total, mixed[:HEAD_DIM])

    @pl.when(jnp.max(worst) > LARGEST_SUM)
    def _():
        for pair, which, span in units:
            q_with = with_extra(
                which, q_ref[:, lanes_of(pair)].astype(F32).T[:, span] * SCALE, True, None
            )
            k_of = key_side(pair, which)
            s = [dot_nn(k_of[rows], q_with) for rows in keys]
            top = functools.reduce(jnp.maximum, [jnp.max(c, axis=0, keepdims=True) for c in s])
            total = jnp.zeros_like(top)
            for rows, chunk in zip(keys, s):
                p = jnp.exp(chunk - top)
                total = total + jnp.sum(p, axis=0, keepdims=True)
                p_ref[0, rows] = p.astype(BF16)
            mixed = dot_nn(flip(v_ref[:, lanes_of(pair)])[half_rows(which)], p_ref[0])
            write(pair, which, span, top, total, mixed)

    out_ref[...] += dot_nn(mixed_ref[...], weights(3))


def cross_backward_kernel(heads, shares, size, scattered, hops_wanted, length_ref, *refs):
    gain_ref, branch_ref, q_ref, mixed_ref, lse_ref = refs[:5]
    rows_in, memory_in, add_in, k_in, v_in = refs[5:10]
    sources = refs[10 : 10 + shares]
    count = shares // 2
    refs = refs[10 + shares :]
    scatter_in, refs = refs[:scattered], refs[scattered:]
    hidden_in, refs = refs[:hops_wanted], refs[hops_wanted:]
    hidden_out, refs = refs[:hops_wanted], refs[hops_wanted:]
    if scattered:
        scatter_out, refs = refs[0], refs[1:]
        parts, refs = refs[-4 * scattered - 4 :], refs[: -4 * scattered - 4]
        scatter = Scatter(
            size,
            scatter_in,
            parts[:scattered],
            parts[scattered : 2 * scattered],
            parts[2 * scattered : 3 * scattered],
            *parts[4 * scattered : 4 * scattered + 2],
        )
        scatter_came = parts[3 * scattered]
        part_sems, done_sems = parts[4 * scattered + 2 :]
        part_loads = [
            pltpu.make_async_copy(source, target, part_sems.at[i])
            for i, (source, target) in enumerate(zip(scatter_in, parts))
        ]
    sums, refs = refs[:count], refs[count:]
    memory_out, out_ref, low_ref, gain_grad_ref = refs[:4]
    rows_ref, memory_ref, add_ref, k_ref, v_ref = refs[4:9]
    (
        w_ref,
        normed_ref,
        extra_ref,
        g_ref,
        grad_q_ref,
        grad_ref,
        ds_ref,
        give_ref,
        keep_ref,
        came_ref,
        memory_grad_ref,
        sems,
        load_sems,
        key_sems,
        out_sems,
        swap_sems,
        hop_sems,
    ) = refs[9:]
    (doc, features), slots = rows_ref.shape, memory_ref.shape[0]
    half, blocks = features // 2, features // HEAD_BLOCK
    stack = Stack(sources, w_ref, sems, 4, heads * HEAD_DIM)
    loads = [
        pltpu.make_async_copy(source, target, load_sems.at[i])
        for i, (source, target) in enumerate(
            ((memory_in, memory_ref), (rows_in, rows_ref), (add_in, add_ref))
        )
    ]

    def key_copies(b):
        lanes = pl.ds(pl.multiple_of(b * HEAD_BLOCK, HEAD_BLOCK), HEAD_BLOCK)
        return [
            pltpu.make_async_copy(source.at[:, lanes], target.at[b], key_sems.at[i, b])
            for i, (source, target) in enumerate(((k_in, k_ref), (v_in, v_ref)))
        ]

    stack.start()
    for b in range(blocks):
        for copy in key_copies(b):
            copy.start()
    for copy in loads:
        copy.start()
    greet([1, 2][:count], [way[1] for way in ring_ways(size)] if scattered else [])
    hops = [
        to_differing(2, source, target, hop_sems.at[i])
        for i, (source, target) in enumerate(zip(hidden_in, hidden_out))
    ]
    for hop in hops:
        hop.start()
    if scattered:
        scatter.begin()
        for copy in part_loads:
            copy.start()
        for copy in part_loads:
            copy.wait()
    slot = lax.broadcasted_iota(jnp.int32, (slots, LANES), 0)
    extra_ref[...] = extra_lanes(slots, slot < length_ref[0])
    none = jnp.zeros((doc, LANES), BF16)
    stack.wait(3)

    def one_block(step, carry):
        start = pl.multiple_of(3 * features + step * HEAD_BLOCK, HEAD_BLOCK)
        g_ref[...] = dot_nt(branch_ref[...], w_ref[pl.ds(start, HEAD_BLOCK)]).astype(BF16)
        for copy in key_copies(step):
            copy.wait()
        for pair in range(BLOCK_HEADS // 2):
            local = slice(pair * LANES, (pair + 1) * LANES)
            lanes = lane_block(step * HEAD_BLOCK + pair * LANES)
            v_lanes = lane_block(features + step * HEAD_BLOCK + pair * LANES)
            q, g = q_ref[:, lanes], g_ref[:, local]
            q_t, g_t = q.astype(F32).T * SCALE, g.astype(F32).T
            inner = g_t * mixed_ref[:, lanes].astype(F32).T
            per_head = []
            for which in range(2):
                h = 2 * pair + which
                minus = jnp.sum(inner[half_rows(which)], axis=0, keepdims=True)
                per_head.append(
                    (
                        with_extra(which, q_t, True, lse_ref[step, h : h + 1, :]),
                        with_extra(which, g_t, False, minus),
                        pick(which, q, none),
                        pick(which, g, none),
                    )
                )
            for rows in spans(slots, K_BLOCK):
                k, v, extra = k_ref[step, rows, local], v_ref[step, rows, local], extra_ref[rows]
                part_k = part_v = None
                for which, (q_with, g_with, q_of, g_of) in enumerate(per_head):
                    p = jnp.exp(dot_nn(pick(which, k, extra), q_with))
                    ds = (p * dot_nn(pick(which, v, extra), g_with)).astype(BF16)
                    ds_ref[which, rows] = ds
                    to_v = dot_nn(p.astype(BF16), g_of)
                    to_k = dot_nn(ds, q_of)
                    part_v = to_v if part_v is None else part_v + to_v
                    part_k = to_k if part_k is None else part_k + to_k
                grad_ref[rows, lanes] = (part_k * SCALE).astype(BF16)
                grad_ref[rows, v_lanes] = part_v.astype(BF16)
            k_t = flip(k_ref[step, :, local])
            grad_q = [dot_nn(k_t[half_rows(which)], ds_ref[which]) for which in range(2)]
            grad_q_ref[:, lanes] = (jnp.concatenate(grad_q, axis=0) * SCALE).T.astype(BF16)
            if scattered:
                scatter_step(1 + step * (BLOCK_HEADS // 2) + pair)
        return carry

    places = blocks * (BLOCK_HEADS // 2)

    def scatter_step(step):
        if size - 2 >= places:
            scatter.advance(step)
        elif size > 2:

            @pl.when(step <= size - 2)
            def _():
                scatter.advance(step)

    lax.fori_loop(0, blocks, one_block, 0)
    if scattered:

        def rest(step, carry):
            scatter.advance(step)
            return carry

        lax.fori_loop(min(places, size - 2) + 1, size - 1, rest, 0)
        scatter.turn()
        done_hops = [
            to_differing(2, done, scatter_came, done_sems) for done in scatter.done[1:]
        ]
        for hop in done_hops:
            hop.start()

    for copy in loads:
        copy.wait()
    norm_into(normed_ref, rows_ref, gain_ref)

    def weight_grads(ref, first):
        columns = slice(first, first + half)
        v_columns = slice(features + first, features + first + half)
        ref[0] = dot_tn(grad_q_ref[:, columns], normed_ref[...]).astype(BF16)
        ref[1] = dot_tn(grad_ref[:, columns], memory_ref[...]).astype(BF16)
        ref[2] = dot_tn(grad_ref[:, v_columns], memory_ref[...]).astype(BF16)
        ref[3] = dot_tn(mixed_ref[:, columns], branch_ref[...]).astype(BF16)

    weight_grads(give_ref, 0)
    swap = to_differing(1, give_ref, came_ref, swap_sems)
    swap.start()
    stack.wait(0, 1, 2)
    writes = []
    for i, rows in enumerate(spans(slots, MEMORY_BLOCK)):
        memory_grad_ref[rows] = dot_nn(
            grad_ref[rows], w_ref[features : 3 * features]
        ).astype(BF16)
        writes.append(
            pltpu.make_async_copy(memory_grad_ref.at[rows], memory_out.at[rows], out_sems.at[i])
        )
        writes[-1].start()
    weight_grads(keep_ref, half)
    gain_grad_ref[...] = jnp.zeros_like(gain_grad_ref)
    for span in spans(doc, ROW_BLOCK):
        back = dot_nn(grad_q_ref[span], w_ref[:features])
        norm_back_into(
            span, back, out_ref, low_ref, gain_grad_ref, rows_ref, gain_ref, add_ref
        )
    swap.wait_recv()
    rows = half // count
    for share, sums_ref in enumerate(sums):
        for kind in range(4):
            span = slice(share * rows, (share + 1) * rows)
            to = slice(kind * rows, (kind + 1) * rows)
            sums_ref[to] = low_sum(keep_ref[kind, span], came_ref[kind, span])
    swap.wait_send()
    for copy in writes:
        copy.wait()
    for hop in hops:
        hop.wait()
    if scattered:
        for hop in done_hops:
            hop.wait()
        own = scatter.done[0][...]
        scatter_out[...] = low_sum(own, scatter_came[...]) if done_hops else own
        scatter.wait_sent()


def feed_forward_kernel(first, last, rows_ref, gain_ref, cotangent_ref, *refs):
    sources, refs = refs[:2], refs[2:]
    if not first:
        before_in, refs = refs[:2], refs[2:]
    sums, layer_ref, out_ref = refs[:2], refs[2], refs[3]
    if last:
        low_ref, gain_grad_ref = refs[4:6]
        refs = refs[2:]
    (
        wide_ref,
        narrow_ref,
        normed_ref,
        normed_t,
        cotangent_t,
        active_ref,
        grad_ref,
        give_ref,
        keep_ref,
        came_ref,
        layer_in_ref,
        back_in_ref,
        sems,
        before_sems,
        swap_sems,
    ) = refs[4:]
    step, steps = pl.program_id(0), pl.num_programs(0)
    half = steps // 2
    doc = rows_ref.shape[0]
    hidden = sources[0].shape[0] // 2
    copies = [
        [
            pltpu.make_async_copy(
                source.at[pl.ds(kind * hidden, hidden)],
                stack.at[pl.ds(p * hidden, hidden)],
                sems.at[p, kind],
            )
            for kind, stack in enumerate((wide_ref, narrow_ref))
        ]
        for p, source in enumerate(sources)
    ]
    loads = []
    if not first:
        loads = [
            pltpu.make_async_copy(source, target, before_sems.at[i])
            for i, (source, target) in enumerate(zip(before_in, (layer_in_ref, back_in_ref)))
        ]
    swap = to_differing(1, give_ref, came_ref, swap_sems)

    @pl.when(step == 0)
    def _():
        for pair in copies:
            for copy in pair:
                copy.start()
        for copy in loads:
            copy.start()
        greet([1])
        norm_into(normed_ref, rows_ref, gain_ref)
        for span in spans(doc, ROW_BLOCK):
            normed_t[:, span] = flip(normed_ref[span])
            cotangent_t[:, span] = flip(cotangent_ref[span])

    for p, pair in enumerate(copies):

        @pl.when(step == p * half)
        def _(pair=pair):
            for copy in pair:
                copy.wait()

    units = pl.ds(pl.multiple_of(step * HIDDEN_BLOCK, HIDDEN_BLOCK), HIDDEN_BLOCK)
    activated, slope = gelu_and_slope(dot_nn(wide_ref[units], normed_t[...]))
    active_ref[units] = activated.astype(BF16)
    grad_ref[units] = (dot_nn(narrow_ref[units], cotangent_t[...]) * slope).astype(BF16)

    def store(ref, at):
        rows = pl.ds(pl.multiple_of(at * HIDDEN_BLOCK, HIDDEN_BLOCK), HIDDEN_BLOCK)
        ref[0, rows] = dot_nn(grad_ref[units], normed_ref[...]).astype(BF16)
        ref[1, rows] = dot_nn(active_ref[units], cotangent_ref[...]).astype(BF16)

    @pl.when(step < half)
    def _():
        store(give_ref, step)

    @pl.when(step == half - 1)
    def _():
        swap.start()

    @pl.when(step >= half)
    def _():
        store(keep_ref, step - half)

    @pl.when(step == steps - 1)
    def _():
        for copy in loads:
            copy.wait()
        if last:
            gain_grad_ref[...] = jnp.zeros_like(gain_grad_ref)
        for span in spans(doc, ROW_BLOCK):
            layer = rows_ref[span] if first else layer_in_ref[span]
            layer = layer + dot_tn(active_ref[:, span], narrow_ref[...])
            layer_ref[span] = layer.astype(layer_ref.dtype)
            back = dot_tn(grad_ref[:, span], wide_ref[...])
            if not first:
                back = back + back_in_ref[span]
            if last:
                norm_back_into(
                    span, back, out_ref, low_ref, gain_grad_ref, rows_ref, gain_ref, cotangent_ref
                )
            else:
                out_ref[span] = back
        swap.wait_recv()
        for kind, sums_ref in enumerate(sums):
            for span in spans(hidden, HIDDEN_BLOCK):
                sums_ref[span] = low_sum(keep_ref[kind, span], came_ref[kind, span])
        swap.wait_send()


def pack_kernel(flipped, *refs):
    out_ref, start = refs[-1], 0
    for source, turn in zip(refs[:-1], flipped):
        rows = source.shape[1] if turn else source.shape[0]
        span = slice(start, start + rows)
        out_ref[span] = flip(source[...]) if turn else source[...]
        start += rows


def finish_kernel(*refs):
    sources, outs, refs = refs[:4], refs[4:14], refs[14:]
    ins, wides, in_sems, out_sems = refs[:4], refs[4:14], refs[14], refs[15]
    loads, writes = [], []
    for i, (source, target) in enumerate(zip(sources, ins)):
        for j, span in enumerate(spans(target.shape[0], FINISH_BLOCK)):
            loads.append(
                pltpu.make_async_copy(source.at[span], target.at[span], in_sems.at[i, j])
            )
            loads[-1].start()

    def write(i, part):
        writes.append(
            pltpu.make_async_copy(wides[i].at[part], outs[i].at[part], out_sems.at[len(writes)])
        )
        writes[-1].start()

    waiting = iter(loads)
    hidden = wides[1].shape[0]
    for span in spans(hidden, FINISH_BLOCK):
        next(waiting).wait()
        for part in spans(FINISH_BLOCK, LANES):
            rows = slice(span.start + part.start, span.start + part.stop)
            wides[0][:, rows] = ins[0][rows].astype(F32).T
        write(0, (slice(None), span))
    for span in spans(hidden, FINISH_BLOCK):
        next(waiting).wait()
        wides[1][span] = ins[1][span].astype(F32)
        write(1, span)
    for i in (2, 3):
        for _ in spans(ins[i].shape[0], FINISH_BLOCK):
            next(waiting).wait()
        rows = wides[2].shape[0]
        for kind in range(4):
            at = 2 + 4 * (i - 2) + kind
            wides[at][...] = ins[i][kind * rows : (kind + 1) * rows].astype(F32)
            write(at, slice(None))
    for copy in writes:
        copy.wait()


def params():
    return pltpu.CompilerParams(vmem_limit_bytes=VMEM_BYTES)


def cost(flops=1 << 20):
    return pl.CostEstimate(flops=flops, bytes_accessed=1 << 16, transcendentals=0)


def shape(dims, dtype):
    return jax.ShapeDtypeStruct(dims, dtype)


def whole(array):
    return pl.BlockSpec(
        array.shape, lambda *_: (0,) * len(array.shape), pipeline_mode=pl.Buffered(1)
    )


def result(array):
    return pl.BlockSpec(array.shape, lambda *_: (0,) * len(array.shape))


def columns(rows):
    return pl.BlockSpec((rows, HEAD_BLOCK), lambda i: (0, i))


def anywhere(arrays):
    return [pl.BlockSpec(memory_space=pl.ANY) for _ in arrays]


SCALAR = pl.BlockSpec(memory_space=pltpu.SMEM)


def call(
    kernel, name, grid, in_specs, out_specs, out_shape, scratch, args, channel=None, flops=1 << 20
):
    compiler_params = params()
    if channel is not None:
        compiler_params = pltpu.CompilerParams(
            vmem_limit_bytes=VMEM_BYTES, collective_id=channel, has_side_effects=True
        )
    return pl.pallas_call(
        kernel,
        grid=grid,
        in_specs=in_specs,
        out_specs=out_specs,
        out_shape=out_shape,
        scratch_shapes=scratch,
        compiler_params=compiler_params,
        cost_estimate=cost(flops),
        name=name,
    )(*args)


def pack(*parts):
    arrays, flipped = zip(*parts)
    rows = sum(a.shape[1] if turn else a.shape[0] for a, turn in parts)
    features = arrays[0].shape[0] if flipped[0] else arrays[0].shape[1]
    return pl.pallas_call(
        functools.partial(pack_kernel, flipped),
        out_shape=shape((rows, features), BF16),
        compiler_params=params(),
        cost_estimate=cost(),
        name="pack",
    )(*arrays)


def self_forward(heads, buckets, rows, gain, weights, ids):
    doc, features = rows.shape
    shares, steps = len(weights), features // HEAD_BLOCK
    narrow, tall = shape((doc, features), BF16), shape((doc, features), F32)
    out_shape = (*[narrow] * 4, shape((steps, 8, doc), F32), tall)
    return call(
        functools.partial(self_forward_kernel, heads, buckets, shares),
        "self_forward",
        (steps,),
        [whole(rows), whole(gain), whole(ids), *anywhere(weights)],
        (*[columns(doc)] * 4, pl.BlockSpec((1, 8, doc), lambda i: (i, 0, 0)), result(tall)),
        out_shape,
        [
            pltpu.VMEM((4 * features, features), BF16),
            pltpu.VMEM((shares, TABLE_ROWS, features), BF16),
            pltpu.VMEM((TABLE_ROWS, LANES), F32),
            pltpu.VMEM((doc, features), BF16),
            pltpu.SemaphoreType.DMA((shares, 5)),
        ],
        (rows, gain, ids, *weights),
    )


def self_backward(heads, buckets, rows, gain, ids, branch, add, saved, weights):
    doc, features = rows.shape
    shares, steps = len(weights), features // HEAD_BLOCK
    packed = shape((4, features // 2, features), BF16)
    out_shape = (
        packed,
        packed,
        shape((steps * BLOCK_HEADS, doc, doc), BF16),
        shape((doc, features), F32),
        shape((8, features), F32),
    )
    *arrays, lse = saved
    return call(
        functools.partial(self_backward_kernel, heads, buckets, shares),
        "self_backward",
        (steps,),
        [
            *[whole(a) for a in (rows, gain, ids, branch, add, *arrays)],
            pl.BlockSpec((1, 8, doc), lambda i: (i, 0, 0)),
            *anywhere(weights),
        ],
        (
            result(packed),
            result(packed),
            pl.BlockSpec((BLOCK_HEADS, doc, doc), lambda i: (i, 0, 0)),
            result(out_shape[3]),
            result(out_shape[4]),
        ),
        out_shape,
        [
            pltpu.VMEM((4 * features, features), BF16),
            pltpu.VMEM((shares, TABLE_ROWS, features), BF16),
            pltpu.VMEM((TABLE_ROWS, LANES), F32),
            pltpu.VMEM((doc, features), BF16),
            pltpu.VMEM((doc, HEAD_BLOCK), BF16),
            pltpu.VMEM((3, doc, features), BF16),
            pltpu.SemaphoreType.DMA((shares, 5)),
        ],
        (rows, gain, ids, branch, add, *arrays, lse, *weights),
    )


def cross_forward(heads, rows, gain, memory, length, weights):
    (doc, features), slots = rows.shape, memory.shape[0]
    shares, steps = len(weights), features // HEAD_BLOCK
    query, key = shape((doc, features), BF16), shape((slots, features), BF16)
    tall = shape((doc, features), F32)
    return call(
        functools.partial(cross_forward_kernel, heads, shares),
        "cross_forward",
        (steps,),
        [SCALAR, whole(rows), whole(gain), whole(memory), *anywhere(weights)],
        (
            columns(doc),
            columns(slots),
            columns(slots),
            columns(doc),
            pl.BlockSpec((1, 8, doc), lambda i: (i, 0, 0)),
            result(tall),
        ),
        (query, key, key, query, shape((steps, 8, doc), F32), tall),
        [
            pltpu.VMEM((4 * features, features), BF16),
            pltpu.VMEM((doc, features), BF16),
            pltpu.VMEM((slots, LANES), BF16),
            pltpu.VMEM((2, slots, Q_BLOCK), BF16),
            pltpu.VMEM((LANES, Q_BLOCK), F32),
            pltpu.SemaphoreType.DMA((shares, 4)),
        ],
        (length, rows, gain, memory, *weights),
    )


def cross_backward(
    heads, size, rows, gain, memory, length, branch, add, saved, weights, scattered, hops
):
    (doc, features), slots = rows.shape, memory.shape[0]
    shares, blocks = len(weights), features // HEAD_BLOCK
    count = shares // 2
    blocks_out, ring_scratch = [], []
    if scattered:
        number, part = len(scattered), scattered[0].shape
        block = (2, part[0] // (2 * size), features)
        blocks_out = [shape(block, BF16)]
        steps = pltpu.SemaphoreType.DMA((number, 2, size - 1))
        ring_scratch = [
            *[pltpu.VMEM(part, BF16)] * number,
            *[pltpu.VMEM((2, size - 1, *block[1:]), BF16)] * number,
            *[pltpu.VMEM(block, BF16)] * number,
            *[pltpu.VMEM(block, BF16)] * number,
            steps,
            steps,
            pltpu.SemaphoreType.DMA((number,)),
            pltpu.SemaphoreType.DMA((2,)),
        ]
    out_shape = (
        *[shape(h.shape, BF16) for h in hops],
        *blocks_out,
        *[shape((4 * heads * HEAD_DIM, features), BF16)] * count,
        shape((slots, features), BF16),
        shape((doc, features), F32),
        shape((doc, features), BF16),
        shape((8, features), F32),
    )
    query, key, value, mixed, lse = saved
    near = (gain, branch, query, mixed, lse)
    far = (rows, memory, add, key, value, *weights, *scattered, *hops)
    vmem, hbm = pl.BlockSpec(memory_space=pltpu.VMEM), pl.BlockSpec(memory_space=pl.ANY)
    packed = pltpu.VMEM((4, features // 2, features), BF16)
    key_block = pltpu.VMEM((blocks, slots, HEAD_BLOCK), BF16)
    return call(
        functools.partial(
            cross_backward_kernel, heads, shares, size, len(scattered), len(hops)
        ),
        "cross_backward",
        (),
        [SCALAR, *[vmem for _ in near], *[hbm for _ in far]],
        (
            *[hbm] * len(hops),
            *[vmem] * len(blocks_out),
            *[vmem] * count,
            hbm,
            vmem,
            vmem,
            vmem,
        ),
        out_shape,
        [
            pltpu.VMEM((doc, features), F32),
            pltpu.VMEM((slots, features), BF16),
            pltpu.VMEM((doc, features), F32),
            key_block,
            key_block,
            pltpu.VMEM((4 * features, features), BF16),
            pltpu.VMEM((doc, features), BF16),
            pltpu.VMEM((slots, LANES), BF16),
            pltpu.VMEM((doc, HEAD_BLOCK), BF16),
            pltpu.VMEM((doc, features), BF16),
            pltpu.VMEM((slots, 2 * features), BF16),
            pltpu.VMEM((2, slots, doc), BF16),
            packed,
            packed,
            packed,
            pltpu.VMEM((slots, features), BF16),
            pltpu.SemaphoreType.DMA((shares, 4)),
            pltpu.SemaphoreType.DMA((3,)),
            pltpu.SemaphoreType.DMA((2, blocks)),
            pltpu.SemaphoreType.DMA((slots // MEMORY_BLOCK,)),
            pltpu.SemaphoreType.DMA((2,)),
            pltpu.SemaphoreType.DMA((max(len(hops), 1), 2)),
            *ring_scratch,
        ],
        (length, *near, *far),
        channel=1,
    )


def feed_forward(rows, gain, cotangent, weights, before, last):
    (doc, features), shares = rows.shape, len(weights)
    share = weights[0].shape[0] // 2
    hidden = share * shares
    steps = hidden // HIDDEN_BLOCK
    summed, tall = shape((share, features), BF16), shape((doc, features), F32)
    low = shape((doc, features), BF16)
    rest = [low, tall, low, shape((8, features), F32)] if last else [tall, tall]
    kept, added = pltpu.VMEM((2, share, features), BF16), pltpu.VMEM(tall.shape, F32)
    return call(
        functools.partial(feed_forward_kernel, not before, last),
        "feed_forward",
        (steps,),
        [whole(rows), whole(gain), whole(cotangent), *anywhere(weights), *anywhere(before)],
        (result(summed), result(summed), *[result(o) for o in rest]),
        (summed, summed, *rest),
        [
            pltpu.VMEM((hidden, features), BF16),
            pltpu.VMEM((hidden, features), BF16),
            pltpu.VMEM((doc, features), BF16),
            pltpu.VMEM((features, doc), BF16),
            pltpu.VMEM((features, doc), BF16),
            pltpu.VMEM((hidden, doc), BF16),
            pltpu.VMEM((hidden, doc), BF16),
            kept,
            kept,
            kept,
            added,
            added,
            pltpu.SemaphoreType.DMA((shares, 2)),
            pltpu.SemaphoreType.DMA((2,)),
            pltpu.SemaphoreType.DMA((2,)),
        ],
        (rows, gain, cotangent, *weights, *before),
        channel=3 if before else 2,
    )


def finish(sum_wide, sum_narrow, sum_cross, sum_self):
    rows, features = sum_self.shape
    hidden, part = sum_wide.shape[0], shape((rows // 4, features), F32)
    out_shape = [shape((features, hidden), F32), shape((hidden, features), F32), *[part] * 8]
    sources = (sum_wide, sum_narrow, sum_cross, sum_self)
    writes = 2 * hidden // FINISH_BLOCK + 8
    wide, narrow, *parts = pl.pallas_call(
        finish_kernel,
        in_specs=anywhere(sources),
        out_specs=anywhere(out_shape),
        out_shape=out_shape,
        scratch_shapes=[
            *[pltpu.VMEM(source.shape, BF16) for source in sources],
            *[pltpu.VMEM(out.shape, F32) for out in out_shape],
            pltpu.SemaphoreType.DMA((4, hidden // FINISH_BLOCK)),
            pltpu.SemaphoreType.DMA((writes,)),
        ],
        compiler_params=params(),
        cost_estimate=cost(),
        name="finish",
    )(*sources)
    return wide, narrow, parts[4:], parts[:4]


def share_place(row, other, peers):
    j, bit = 0, 1
    while bit < peers:
        j = j + bit * ((row // bit + other // bit) % 2)
        bit *= 2
    return (j % 2) * (j // 2) + (1 - j % 2) * (peers // 2 + j // 2)


def tail_kernel(size, peers, buckets, heads, gathered, counts, *refs):
    parts = []
    for count in counts:
        parts.append(refs[:count])
        refs = refs[count:]
    arrays = len(counts) + 1
    give_ref, keep_ref, ids_ref, ds_ref, *gain_refs = refs[:7]
    outs, small_out_ref, refs = refs[7 : 7 + arrays], refs[7 + arrays], refs[8 + arrays :]
    slots, refs = refs[:arrays], refs[arrays:]
    firsts, refs = refs[:arrays], refs[arrays:]
    kept_ref, came_ref, folded_ref, far_came_ref, part_ref, scores_ref, bucket_ref = refs[:7]
    small_ref, near_ref, far_ref = refs[7:10]
    send, came, send_out, came_out, small_sems, hop_sems, local_sems = refs[10:]
    parts.append((part_ref,))
    me, row = lax.axis_index("dp"), lax.axis_index("mp")
    ways = ring_ways(size)
    doc = ids_ref.shape[0]
    mesh = pl.DeviceIdType.MESH

    load_scores = pltpu.make_async_copy(ds_ref, scores_ref, local_sems.at[0])
    load_kept = pltpu.make_async_copy(keep_ref, kept_ref, local_sems.at[1])
    load_scores.start()
    load_kept.start()

    barrier = pltpu.get_barrier_semaphore()

    def greet(t, carry):
        pl.semaphore_signal(
            barrier, inc=1, device_id=((me + t) % size, row), device_id_type=mesh
        )
        return carry

    lax.fori_loop(1, size, greet, 0)
    for t in range(1, peers):
        pl.semaphore_signal(
            barrier, inc=1, device_id=(me, (row + t) % peers), device_id_type=mesh
        )
    pl.semaphore_wait(barrier, size - 1 + peers - 1)

    def block(i, way, number):
        rows = outs[i].shape[0] // (2 * size)
        return pl.ds(pl.multiple_of((way * size + number) * rows, 16), rows)

    def part(i, span):
        total = parts[i][0][span].astype(F32)
        for ref in parts[i][1:]:
            total = total + ref[span].astype(F32)
        return total

    def first_copy(i, way):
        return remote(
            firsts[i].at[way],
            slots[i].at[way, 0],
            send.at[i, way, 0],
            came.at[i, way, 0],
            (ways[way][1], row),
        )

    def next_copy(i, way, step):
        return remote(
            slots[i].at[way, step - 1],
            slots[i].at[way, step],
            send.at[i, way, step],
            came.at[i, way, step],
            (ways[way][1], row),
        )

    def wait_came(i, way, step):
        remote(
            slots[i].at[way, step],
            slots[i].at[way, step],
            send.at[i, way, step],
            came.at[i, way, step],
            (ways[way][1], row),
        ).wait_recv()

    def out_copy(i, way, step):
        span = block(i, way, (ways[way][0] + 1 - step + size) % size)
        return remote(
            outs[i].at[span],
            outs[i].at[span],
            send_out.at[i, way, step],
            came_out.at[i, way, step],
            (ways[way][1], row),
        )

    def begin(rings):
        for i, way in rings:
            firsts[i][way] = part(i, block(i, way, ways[way][0])).astype(BF16)
            first_copy(i, way).start()

    def plus_part(i, way, step):
        span = block(i, way, (ways[way][0] - step - 1 + size) % size)
        total = slots[i][way, step].astype(F32) + part(i, span)
        return span, total.astype(BF16)

    def advance(rings, step):
        for i, way in rings:
            wait_came(i, way, step - 1)
            slots[i][way, step - 1] = plus_part(i, way, step - 1)[1]
            next_copy(i, way, step).start()

    def turn(rings):
        for i, way in rings:
            wait_came(i, way, size - 2)
            span, total = plus_part(i, way, size - 2)
            outs[i][span] = total
            out_copy(i, way, 0).start()

    def pass_on(rings, step):
        for i, way in rings:
            out_copy(i, way, step - 1).wait_recv()
            out_copy(i, way, step).start()

    ready = [(i, way) for i in range(gathered) for way in range(2)]
    early = [(i, way) for i in range(gathered, arrays - 1) for way in range(2)]
    late = [(arrays - 1, way) for way in range(2)]

    other_core = remote(
        give_ref, came_ref, hop_sems.at[0, 0], hop_sems.at[0, 1], (me, differing(row, 1))
    )
    other_core.start()
    begin(early)
    for i, way in ready:
        outs[i][block(i, way, (ways[way][0] + 1) % size)] = parts[i][0][way]
        out_copy(i, way, 0).start()

    rows_used, per_row = bucket_ref.shape[0], ds_ref.shape[0] // bucket_ref.shape[0]
    units = rows_used * buckets
    per_round = -(-units // max(2 * (size - 2), 1))

    def bucket_unit(u, carry):
        r, b = u // buckets, u % buckets
        sums = [jnp.zeros((8, LANES), F32) for _ in range(per_row)]
        for c in range(0, doc, LANES):
            hit = ids_ref[: c + LANES, c : c + LANES] == b
            for h in range(per_row):
                grads = scores_ref[r * per_row + h, : c + LANES, c : c + LANES].astype(F32)
                kept = jnp.where(hit, grads, 0.0).reshape(-1, 8, LANES)
                sums[h] = sums[h] + jnp.sum(kept, axis=0)
        for h in range(per_row):
            bucket_ref[r, h, pl.ds(b, 1), :] = jnp.sum(sums[h], axis=0, keepdims=True)
        return carry

    def bucket_round(k):
        low = jnp.minimum(k * per_round, units)
        lax.fori_loop(low, jnp.minimum(low + per_round, units), bucket_unit, 0)

    bucket_ref[...] = jnp.zeros_like(bucket_ref)
    part_ref[...] = jnp.zeros_like(part_ref)
    load_scores.wait()

    def early_step(step, carry):
        advance(early, step)
        pass_on(ready, step)
        bucket_round(step - 1)
        return carry

    middle = min(2, size - 1)
    lax.fori_loop(1, middle, early_step, 0)

    load_kept.wait()
    other_core.wait_recv()
    kinds, count = kept_ref.shape[0], folded_ref.shape[0]
    rows = kept_ref.shape[1] // count

    def fold(index, target, span_of):
        span = slice(index * rows, (index + 1) * rows)
        for kind in range(kinds):
            total = kept_ref[kind, span].astype(F32) + came_ref[kind, span].astype(F32)
            target[span_of(kind)] = total.astype(BF16)

    def kind_rows(kind):
        return slice(kind * rows, (kind + 1) * rows)

    other_chip = None
    if count == 2:
        fold(1, folded_ref.at[1], kind_rows)
        other_chip = remote(
            folded_ref.at[1],
            far_came_ref,
            hop_sems.at[1, 0],
            hop_sems.at[1, 1],
            (me, differing(row, 2)),
        )
        other_chip.start()
    fold(0, folded_ref.at[0], kind_rows)

    lax.fori_loop(middle, size - 1, early_step, 0)
    turn(early)
    used = slice(0, kinds * rows)
    if other_chip is None:
        part_ref[used] = folded_ref[0]
    else:
        other_chip.wait_recv()
        total = folded_ref[0].astype(F32) + far_came_ref[...].astype(F32)
        part_ref[used] = total.astype(BF16)
    begin(late)

    def middle_step(step, carry):
        pass_on(early, step)
        advance(late, step)
        bucket_round(size - 2 + step - 1)
        return carry

    lax.fori_loop(1, size - 1, middle_step, 0)
    if size == 2:
        lax.fori_loop(0, units, bucket_unit, 0)
    turn(late)

    features = gain_refs[0].shape[1]
    per_gain = features // LANES
    gain_rows = len(gain_refs) * per_gain
    small_ref[...] = jnp.zeros_like(small_ref)
    for i, ref in enumerate(gain_refs):
        total = jnp.sum(ref[...], axis=0, keepdims=True)
        for c in range(per_gain):
            at = i * per_gain + c
            small_ref[at : at + 1, :] = total[:, c * LANES : (c + 1) * LANES]
    for r in range(rows_used):
        block_sums = bucket_ref[r].reshape(LANES, LANES).T
        at = gain_rows + r
        small_ref[at : at + 1, :] = jnp.sum(block_sums, axis=0, keepdims=True)

    def near_copy(t):
        return remote(
            small_ref,
            near_ref.at[row],
            small_sems.at[0, t],
            small_sems.at[1, t],
            (me, (row + t) % peers),
        )

    def far_copy(t):
        return remote(
            far_ref.at[me],
            far_ref.at[me],
            small_sems.at[2, t],
            small_sems.at[3, t],
            ((me + t) % size, row),
        )

    for t in range(1, peers):
        near_copy(t).start()
    near_ref[pl.ds(row, 1)] = small_ref[...][None]
    for t in range(1, peers):
        near_copy(t).wait_recv()
    own = rows_used // peers
    total, sums = None, None
    for k in range(peers):
        gains = near_ref[k, :gain_rows]
        mine = near_ref[k, pl.ds(gain_rows + own * share_place(row, k, peers), own)]
        total = gains if total is None else total + gains
        sums = mine if sums is None else sums + mine
    small_ref_rows = far_ref.shape[1]
    far_ref[pl.ds(me, 1)] = jnp.concatenate(
        [total, sums, jnp.zeros((small_ref_rows - gain_rows - own, LANES), F32)], axis=0
    )[None]

    def far_start(t, carry):
        far_copy(t).start()
        return carry

    lax.fori_loop(1, size, far_start, 0)

    def late_step(step, carry):
        pass_on(late, step)
        return carry

    lax.fori_loop(1, size - 1, late_step, 0)

    def far_wait(t, carry):
        far_copy(t).wait()
        return carry

    lax.fori_loop(1, size, far_wait, 0)

    def far_add(k, total):
        return total + far_ref[k]

    small_out_ref[...] = lax.fori_loop(1, size, far_add, far_ref[0])
    for i, way in ready + early + late:
        out_copy(i, way, size - 2).wait_recv()

    for t in range(1, peers):
        near_copy(t).wait_send()
    other_core.wait_send()
    if other_chip is not None:
        other_chip.wait_send()
    for i, way in early + late:
        first_copy(i, way).wait_send()

    def sent(step, carry):
        for i, way in early + late:
            next_copy(i, way, step).wait_send()
        return carry

    lax.fori_loop(1, size - 1, sent, 0)

    def sent_out(step, carry):
        for i, way in ready + early + late:
            out_copy(i, way, step).wait_send()
        return carry

    lax.fori_loop(0, size - 1, sent_out, 0)


def tail_sums(size, peers, buckets, heads, blocks, terms, give, keep, ids, ds, gains):
    assert peers in (2, 4)
    grain = 2 * 16 * size
    kinds, half, features = keep.shape
    count = peers // 2
    rows = [size * 2 * b.shape[1] for b in blocks]
    rows += [arrays[0].shape[0] for arrays in terms]
    rows.append(kinds * half // count)
    padded = [r + -r % grain for r in rows]
    parts = [[b] for b in blocks]
    for arrays, r, p in zip(terms, rows[len(blocks) :], padded[len(blocks) :]):
        parts.append([jnp.pad(a, ((0, p - r), (0, 0))) for a in arrays])
    flat = [a for arrays in parts for a in arrays]
    lines = peers * (-(-heads * buckets // LANES))
    small = len(gains) * features // LANES + lines
    small = shape((small + -small % 8, LANES), F32)
    vmem, hbm = pl.BlockSpec(memory_space=pltpu.VMEM), pl.BlockSpec(memory_space=pl.ANY)
    steps = pltpu.SemaphoreType.DMA((len(rows), 2, size - 1))

    def ring_slots(i, steps):
        if i < len(blocks):
            return pltpu.VMEM((2, 1, 16, LANES), BF16)
        return pltpu.VMEM((2, *steps, padded[i] // (2 * size), features), BF16)

    *sums, small = pl.pallas_call(
        functools.partial(
            tail_kernel, size, peers, buckets, heads, len(blocks), [len(a) for a in parts]
        ),
        in_specs=[*[vmem] * len(flat), hbm, hbm, vmem, hbm, *[vmem] * len(gains)],
        out_specs=[vmem] * (len(rows) + 1),
        out_shape=[*[shape((p, features), BF16) for p in padded], small],
        scratch_shapes=[
            *[ring_slots(i, (size - 1,)) for i in range(len(rows))],
            *[ring_slots(i, ()) for i in range(len(rows))],
            pltpu.VMEM(keep.shape, BF16),
            pltpu.VMEM(keep.shape, BF16),
            pltpu.VMEM((count, rows[-1], features), BF16),
            pltpu.VMEM((rows[-1], features), BF16),
            pltpu.VMEM((padded[-1], features), BF16),
            pltpu.VMEM(ds.shape, BF16),
            pltpu.VMEM((lines, LANES // buckets, buckets, LANES), F32),
            pltpu.VMEM(small.shape, F32),
            pltpu.VMEM((peers, *small.shape), F32),
            pltpu.VMEM((size, *small.shape), F32),
            steps,
            steps,
            steps,
            steps,
            pltpu.SemaphoreType.DMA((4, max(size, peers))),
            pltpu.SemaphoreType.DMA((2, 2)),
            pltpu.SemaphoreType.DMA((2,)),
        ],
        compiler_params=pltpu.CompilerParams(
            vmem_limit_bytes=VMEM_BYTES, collective_id=0, has_side_effects=True
        ),
        cost_estimate=cost(),
        name="tail_sums",
    )(*flat, give, keep, ids, ds, *gains)
    return [total[:r] for total, r in zip(sums, rows)], small


def swap(array, bit, size):
    return lax.ppermute(array, "mp", [(i, i ^ bit) for i in range(size)])


def after(array, *others):
    return lax.optimization_barrier((array, others))[0]


def shards(
    decoder_rows,
    memory_rows,
    decoder_token_length,
    memory_length,
    bucket_ids,
    relative_bucket_bias,
    self_gain,
    self_query,
    self_key,
    self_value,
    self_out,
    cross_gain,
    cross_query,
    cross_key,
    cross_value,
    cross_out,
    hidden_gain,
    widen_weight,
    narrow_weight,
    layer_cotangent,
):
    dp_size = lax.axis_size("dp")
    mp_size = lax.axis_size("mp")
    me = lax.axis_index("mp")
    doc, features = decoder_rows.shape
    slots = memory_rows.shape[0]
    cols = self_query.shape[1]
    heads = cols // HEAD_DIM
    buckets = relative_bucket_bias.shape[0]
    order = [*range(1, mp_size, 2), *range(0, mp_size, 2)]

    doc_length = lax.dynamic_index_in_dim(decoder_token_length, me, keepdims=False)
    doc_memory = lax.dynamic_index_in_dim(memory_length, me)
    position = jnp.arange(doc, dtype=jnp.int32)
    allowed = (position[:, None] <= position[None, :]) & (position[:, None] < doc_length)
    ids = jnp.where(allowed, bucket_ids.T, buckets)
    bias_rows = jnp.zeros((TABLE_ROWS, features), BF16)
    bias_rows = bias_rows.at[:heads, :buckets].set(relative_bucket_bias.T)
    own_self = pack(
        (self_query.T, False), (self_key.T, False), (self_value.T, False), (self_out, False), (bias_rows, False)
    )
    own_cross = pack(
        (cross_query.T, False), (cross_key.T, False), (cross_value.T, False), (cross_out, False)
    )
    own_hidden = pack((widen_weight, True), (narrow_weight, False))

    def first_hops(own):
        shares, bit = {0: own}, mp_size // 2
        while bit > 1:
            for j in list(shares):
                shares[j | bit] = swap(shares[j], bit, mp_size)
            bit //= 2
        return shares

    def last_hop(shares, *others):
        if 1 not in shares:
            shares[1] = swap(shares[0], 1, mp_size)
        for j in range(2, mp_size, 2):
            shares[j] = after(shares[j], *others)
            shares[j | 1] = swap(shares[j], 1, mp_size)
        return shares

    near_self = first_hops(own_self)
    near_self[1] = swap(own_self, 1, mp_size)
    memory_rows = after(memory_rows, own_self)
    w_self = last_hop(near_self, own_cross, own_hidden, ids)
    w_self = [w_self[j] for j in order]
    near_cross = first_hops(own_cross)
    near_hidden = first_hops(own_hidden)
    near_hidden[1] = swap(own_hidden, 1, mp_size)
    memory_seen = lax.all_to_all(
        memory_rows.reshape(dp_size, slots // dp_size, features), "dp", 0, 0
    ).reshape(slots, features)

    gain_self = self_gain.astype(F32)[None]
    gain_cross = cross_gain.astype(F32)[None]
    gain_hidden = hidden_gain.astype(F32)[None]

    *saved_self, after_self = self_forward(heads, buckets, decoder_rows, gain_self, w_self, ids)
    w_cross = last_hop(near_cross, after_self)
    w_cross = [w_cross[j] for j in order]
    *saved_cross, after_cross = cross_forward(
        heads, after_self, gain_cross, memory_seen, doc_memory, w_cross
    )

    before, wide_sums, narrow_sums, w_hidden = (), [], [], near_hidden
    for j in range(0, mp_size, 2):
        wide_sum, narrow_sum, *before = feed_forward(
            after_cross,
            gain_hidden,
            layer_cotangent,
            [w_hidden[j + 1], w_hidden[j]],
            before,
            j == mp_size - 2,
        )
        wide_sums.append(wide_sum)
        narrow_sums.append(narrow_sum)
        if j == 0:
            w_hidden = last_hop(near_hidden, before[0])
    layer_output, grad_after_cross, branch, hidden_gain_grad = before

    scattered, hops = wide_sums, narrow_sums[1:]
    if wide_sums[0].shape[0] % (2 * 16 * dp_size):
        scattered, hops = [], wide_sums[1:] + narrow_sums[1:]
    *sums, grad_memory, grad_after_self, branch, cross_gain_grad = cross_backward(
        heads,
        dp_size,
        after_self,
        gain_cross,
        memory_seen,
        doc_memory,
        branch,
        grad_after_cross,
        saved_cross,
        w_cross,
        scattered,
        hops,
    )
    came, sums = sums[: len(hops)], sums[len(hops) :]
    if scattered:
        blocks, terms, cross_sums = sums[:1], [narrow_sums[:1] + came], sums[1:]
    else:
        blocks, cross_sums = [], sums
        hidden = [wide_sums[0], narrow_sums[0]], came
        terms = [[jnp.concatenate(both, axis=0) for both in hidden if both]]
    memory_grad = lax.all_to_all(
        grad_memory.reshape(dp_size, slots // dp_size, features), "dp", 0, 0
    ).reshape(slots, features)
    cross_sums[1:] = [swap(share, 2, mp_size) for share in cross_sums[1:]]

    give, keep, score_grads, input_grad, self_gain_grad = self_backward(
        heads,
        buckets,
        decoder_rows,
        gain_self,
        ids,
        branch,
        grad_after_self,
        saved_self,
        w_self,
    )
    (*hidden, sum_cross, sum_self), small = tail_sums(
        dp_size,
        mp_size,
        buckets,
        heads,
        blocks,
        terms + [cross_sums],
        give,
        keep,
        ids,
        score_grads,
        (self_gain_grad, cross_gain_grad, hidden_gain_grad),
    )
    wide_grad, narrow_grad, self_grads, cross_grads = finish(
        *(hidden if scattered else jnp.split(hidden[0], 2)), sum_cross, sum_self
    )
    gain_rows = 3 * features // LANES
    gains = small[:gain_rows].reshape(3, features)
    lines = -(-heads * buckets // LANES)
    sums = small[gain_rows : gain_rows + lines, : heads // lines * buckets]
    position_grad = sums.reshape(heads, buckets).T

    return (
        layer_output,
        input_grad,
        memory_grad,
        position_grad,
        gains[0],
        *[grad.T for grad in self_grads[:3]],
        self_grads[3],
        gains[1],
        *[grad.T for grad in cross_grads[:3]],
        cross_grads[3],
        gains[2],
        wide_grad,
        narrow_grad,
    )


def solution(mesh):
    return jax.shard_map(
        shards,
        mesh=mesh,
        in_specs=(
            P(("dp", "mp"), None),
            P(("dp", "mp"), None),
            P("dp"),
            P("dp"),
            P(),
            P(None, "mp"),
            P(),
            P(None, "mp"),
            P(None, "mp"),
            P(None, "mp"),
            P("mp", None),
            P(),
            P(None, "mp"),
            P(None, "mp"),
            P(None, "mp"),
            P("mp", None),
            P(),
            P(None, "mp"),
            P("mp", None),
            P(("dp", "mp"), None),
        ),
        out_specs=(
            P(("dp", "mp"), None),
            P(("dp", "mp"), None),
            P(("dp", "mp"), None),
            P(None, "mp"),
            P(),
            P(None, "mp"),
            P(None, "mp"),
            P(None, "mp"),
            P("mp", None),
            P(),
            P(None, "mp"),
            P(None, "mp"),
            P(None, "mp"),
            P("mp", None),
            P(),
            P(None, "mp"),
            P("mp", None),
        ),
        check_vma=False,
    )
```

```python
import functools

import jax
import jax.numpy as jnp
from jax import lax
from jax.experimental import pallas as pl
from jax.experimental.pallas import tpu as pltpu
from jax.sharding import PartitionSpec as P

HEAD_DIM = 64
NORM_EPS = 1e-06
MASKED = -1e30
SCALE = HEAD_DIM**-0.5
BF16 = jnp.bfloat16
F32 = jnp.float32
LANES = 128
TABLE_ROWS = 16
TILE_ROWS = 16
LARGEST_SUM = 1e30
HEAD_BLOCK = 256
BLOCK_HEADS = HEAD_BLOCK // HEAD_DIM
Q_BLOCK = 256
K_BLOCK = 512
HIDDEN_BLOCK = 256
MEMORY_BLOCK = 768
FINISH_BLOCK = 384
ROW_BLOCK = 128
VMEM_BYTES = 56 * 1024 * 1024
GELU_ROOT = 0.7978845608028654
GELU_CUBE = 0.044715


def dot_nn(a, b):
    return lax.dot_general(a, b, (((1,), (0,)), ((), ())), preferred_element_type=F32)


def dot_nt(a, b):
    return lax.dot_general(a, b, (((1,), (1,)), ((), ())), preferred_element_type=F32)


def dot_tn(a, b):
    return lax.dot_general(a, b, (((0,), (0,)), ((), ())), preferred_element_type=F32)


def flip(a):
    return a.astype(F32).T.astype(BF16)


def spans(size, step):
    return [slice(i, i + step) for i in range(0, size, step)]


def norm_scale(rows):
    return lax.rsqrt(jnp.mean(rows * rows, axis=-1, keepdims=True) + NORM_EPS)


def norm_into(normed_ref, rows_ref, gain_ref):
    for span in spans(rows_ref.shape[0], ROW_BLOCK):
        rows = rows_ref[span].astype(F32)
        normed_ref[span] = (rows * norm_scale(rows) * gain_ref[...]).astype(BF16)


def norm_back_into(span, grad, out_ref, low_ref, gain_grad_ref, rows_ref, gain_ref, add_ref):
    rows = rows_ref[span].astype(F32)
    scale = norm_scale(rows)
    unit = rows * scale
    grad_unit = grad * gain_ref[...]
    mean = jnp.mean(grad_unit * unit, axis=-1, keepdims=True)
    out = add_ref[span].astype(F32) + scale * (grad_unit - unit * mean)
    out_ref[span] = out
    if low_ref is not None:
        low_ref[span] = out.astype(BF16)
    gain_grad_ref[...] += jnp.sum((grad * unit).reshape(-1, 8, rows.shape[1]), axis=0)


def gelu_and_slope(v):
    square = v * v
    bend = jnp.tanh(GELU_ROOT * (v + GELU_CUBE * v * square))
    half = 0.5 * (1.0 + bend)
    slope = half + 0.5 * v * (1.0 - bend * bend) * GELU_ROOT * (1.0 + 3.0 * GELU_CUBE * square)
    return v * half, slope


def lane_block(start):
    return pl.ds(pl.multiple_of(start, LANES), LANES)


def extra_lanes(rows, allowed):
    lane = lax.broadcasted_iota(jnp.int32, (rows, LANES), 1) % HEAD_DIM
    first = MASKED if allowed is None else jnp.where(allowed, 0.0, MASKED)
    return jnp.where(lane == 0, first, jnp.where(lane < 4, 1.0, 0.0)).astype(BF16)


def pick(which, block, other):
    lane = lax.broadcasted_iota(jnp.int32, block.shape, 1)
    return jnp.where((lane < HEAD_DIM) == (which == 0), block, other)


def half_rows(which):
    return slice(which * HEAD_DIM, (which + 1) * HEAD_DIM)


def split(values):
    high = values.astype(BF16).astype(F32)
    rest = values - high
    middle = rest.astype(BF16).astype(F32)
    return high, middle, rest - middle


def with_extra(which, block_t, masked, minus):
    columns = block_t.shape[1]
    row = lax.broadcasted_iota(jnp.int32, (HEAD_DIM, columns), 0)
    extra = jnp.where(row == 0, 1.0 if masked else 0.0, 0.0)
    if minus is not None:
        for i, part in enumerate(split(minus)):
            extra = jnp.where(row == i + 1, -part, extra)
    own = block_t[half_rows(which)]
    return jnp.concatenate([own, extra] if which == 0 else [extra, own], axis=0).astype(BF16)


def bias_block(table_ref, ids_ref, index, rows, start):
    row = jnp.broadcast_to(table_ref[pl.ds(index, 1), :], (rows, LANES))
    return jnp.concatenate(
        [
            jnp.take_along_axis(row, ids_ref[:rows, c : c + LANES], axis=1)
            for c in range(start, start + Q_BLOCK, LANES)
        ],
        axis=1,
    )


def ring_place(me, size):
    return jnp.where(me % 2 == 0, me // 2, size - 1 - me // 2)


def ring_device(place, size):
    return jnp.where(place < size // 2, 2 * place, 2 * (size - 1 - place) + 1)


def ring_ways(size):
    me = lax.axis_index("dp")
    place = ring_place(me, size)
    return (
        (place, ring_device((place + 1) % size, size)),
        (size - 1 - place, ring_device((place + size - 1) % size, size)),
    )


def differing(row, bit):
    return row + bit - 2 * bit * ((row // bit) % 2)


def remote(source, target, send_sem, recv_sem, device):
    return pltpu.make_async_remote_copy(
        src_ref=source,
        dst_ref=target,
        send_sem=send_sem,
        recv_sem=recv_sem,
        device_id=device,
        device_id_type=pl.DeviceIdType.MESH,
    )


def greet(bits, devices=()):
    me, row = lax.axis_index("dp"), lax.axis_index("mp")
    barrier = pltpu.get_barrier_semaphore()
    others = [(me, differing(row, bit)) for bit in bits] + [(device, row) for device in devices]
    for other in others:
        pl.semaphore_signal(
            barrier, inc=1, device_id=other, device_id_type=pl.DeviceIdType.MESH
        )
    pl.semaphore_wait(barrier, len(others))


def to_differing(bit, source, target, sems):
    me, row = lax.axis_index("dp"), lax.axis_index("mp")
    return remote(source, target, sems.at[0], sems.at[1], (me, differing(row, bit)))


class Scatter:
    def __init__(self, size, part, slots, done, send, came):
        self.size, self.part, self.slots, self.done = size, part, slots, done
        self.send, self.came = send, came
        self.ways, self.row = ring_ways(size), lax.axis_index("mp")

    def span(self, way, number):
        rows = self.slots.shape[3]
        return pl.ds(pl.multiple_of((way * self.size + number) * rows, 16), rows)

    def copy(self, way, step, source):
        return remote(
            source,
            self.slots.at[way, step],
            self.send.at[way, step],
            self.came.at[way, step],
            (self.ways[way][1], self.row),
        )

    def first(self, way):
        return self.copy(way, 0, self.part.at[:, self.span(way, self.ways[way][0])])

    def next(self, way, step):
        return self.copy(way, step, self.slots.at[way, step - 1])

    def begin(self):
        for way in range(2):
            self.first(way).start()

    def total(self, way, step):
        self.copy(way, step, self.slots.at[way, step]).wait_recv()
        span = self.span(way, (self.ways[way][0] - step - 1 + self.size) % self.size)
        return low_sum(self.slots[way, step], self.part[:, span])

    def advance(self, step):
        for way in range(2):
            self.slots[way, step - 1] = self.total(way, step - 1)
            self.next(way, step).start()

    def turn(self):
        for way in range(2):
            self.done[way] = self.total(way, self.size - 2)

    def wait_sent(self):
        for way in range(2):
            self.first(way).wait_send()

        def sent(step, carry):
            for way in range(2):
                self.next(way, step).wait_send()
            return carry

        lax.fori_loop(1, self.size - 1, sent, 0)


def low_sum(a, b):
    return (a.astype(F32) + b.astype(F32)).astype(BF16)


class Stack:
    def __init__(self, sources, stack_ref, sems, kinds, rows):
        features = stack_ref.shape[0] // kinds
        self.copies = [
            [
                pltpu.make_async_copy(
                    source.at[pl.ds(kind * rows, rows)],
                    stack_ref.at[pl.ds(kind * features + p * rows, rows)],
                    sems.at[p, kind],
                )
                for p, source in enumerate(sources)
            ]
            for kind in range(kinds)
        ]

    def start(self):
        for copies in self.copies:
            for copy in copies:
                copy.start()

    def wait(self, *kinds):
        for kind in kinds:
            for copy in self.copies[kind]:
                copy.wait()


def table_copies(sources, tables_ref, sems, kinds):
    start = sources[0].shape[0] - TABLE_ROWS
    return [
        pltpu.make_async_copy(
            source.at[pl.ds(start, TABLE_ROWS)], tables_ref.at[p], sems.at[p, kinds]
        )
        for p, source in enumerate(sources)
    ]


def table_into(table_ref, tables_ref, heads, buckets):
    for p in range(tables_ref.shape[0]):
        rows = tables_ref[p, :, :LANES].astype(F32)
        lane = lax.broadcasted_iota(jnp.int32, rows.shape, 1)
        rows = jnp.where(lane < buckets, rows, MASKED)
        for h in range(heads):
            table_ref[p * heads + h : p * heads + h + 1, :] = rows[h : h + 1, :]


def self_forward_kernel(heads, buckets, shares, rows_ref, gain_ref, ids_ref, *refs):
    sources = refs[:shares]
    q_ref, k_ref, v_ref, mixed_ref, lse_ref, out_ref = refs[shares : shares + 6]
    w_ref, tables_ref, table_ref, normed_ref, sems = refs[shares + 6 :]
    step = pl.program_id(0)
    doc, features = rows_ref.shape
    stack = Stack(sources, w_ref, sems, 4, heads * HEAD_DIM)

    @pl.when(step == 0)
    def _():
        stack.start()
        tables = table_copies(sources, tables_ref, sems, 4)
        for copy in tables:
            copy.start()
        norm_into(normed_ref, rows_ref, gain_ref)
        out_ref[...] = rows_ref[...].astype(F32)
        for copy in tables:
            copy.wait()
        table_into(table_ref, tables_ref, heads, buckets)
        stack.wait(0, 1, 2, 3)

    def weights(kind):
        start = pl.multiple_of(kind * features + step * HEAD_BLOCK, HEAD_BLOCK)
        return w_ref[pl.ds(start, HEAD_BLOCK)]

    for kind, ref in enumerate((q_ref, k_ref, v_ref)):
        ref[...] = dot_nt(normed_ref[...], weights(kind)).astype(BF16)
    none = jnp.zeros((doc, LANES), BF16)
    for pair in range(BLOCK_HEADS // 2):
        lanes = slice(pair * LANES, (pair + 1) * LANES)
        k, v_t = k_ref[:, lanes], flip(v_ref[:, lanes])
        q_t = flip(q_ref[:, lanes].astype(F32) * SCALE)
        k_of = [pick(which, k, none) for which in range(2)]
        for span in spans(doc, Q_BLOCK):
            rows, mixed = span.stop, []
            for which in range(2):
                h = 2 * pair + which
                s = dot_nn(k_of[which][:rows], q_t[:, span])
                s = s + bias_block(table_ref, ids_ref, step * BLOCK_HEADS + h, rows, span.start)
                top = jnp.max(s, axis=0, keepdims=True)
                p = jnp.exp(s - top)
                total = jnp.sum(p, axis=0, keepdims=True)
                mixed.append(dot_nn(v_t[half_rows(which), :rows], p.astype(BF16)) / total)
                lse_ref[0, h : h + 1, span] = top + jnp.log(total)
            mixed_ref[span, lanes] = jnp.concatenate(mixed, axis=0).T.astype(BF16)
    out_ref[...] += dot_nn(mixed_ref[...], weights(3))


def self_backward_kernel(heads, buckets, shares, *refs):
    rows_ref, gain_ref, ids_ref, branch_ref, add_ref = refs[:5]
    q_ref, k_ref, v_ref, mixed_ref, lse_ref = refs[5:10]
    sources = refs[10 : 10 + shares]
    give_ref, keep_ref, ds_ref, out_ref, gain_grad_ref = refs[10 + shares : 15 + shares]
    w_ref, tables_ref, table_ref, normed_ref, g_ref, grad_ref, back_ref, sems = refs[15 + shares :]
    step = pl.program_id(0)
    doc, features = rows_ref.shape
    half = features // 2
    stack = Stack(sources, w_ref, sems, 4, heads * HEAD_DIM)

    @pl.when(step == 0)
    def _():
        stack.start()
        tables = table_copies(sources, tables_ref, sems, 4)
        for copy in tables:
            copy.start()
        norm_into(normed_ref, rows_ref, gain_ref)
        for copy in tables:
            copy.wait()
        table_into(table_ref, tables_ref, heads, buckets)
        stack.wait(3)

    start = pl.multiple_of(3 * features + step * HEAD_BLOCK, HEAD_BLOCK)
    g_ref[...] = dot_nt(branch_ref[...], w_ref[pl.ds(start, HEAD_BLOCK)]).astype(BF16)
    none = jnp.zeros((doc, LANES), BF16)
    ones = extra_lanes(doc, None)
    for pair in range(BLOCK_HEADS // 2):
        lanes = lane_block(step * HEAD_BLOCK + pair * LANES)
        q, k, v = q_ref[:, lanes], k_ref[:, lanes], v_ref[:, lanes]
        g = g_ref[:, pair * LANES : (pair + 1) * LANES]
        q_t, k_t = q.astype(F32).T * SCALE, flip(k)
        g_t = g.astype(F32).T
        inner = g_t * mixed_ref[:, lanes].astype(F32).T
        per_head = []
        for which in range(2):
            h = 2 * pair + which
            minus = jnp.sum(inner[half_rows(which)], axis=0, keepdims=True)
            per_head.append(
                (
                    pick(which, k, ones),
                    pick(which, v, ones),
                    with_extra(which, q_t, False, lse_ref[0, h : h + 1, :]),
                    with_extra(which, g_t, False, minus),
                    pick(which, q, none),
                    pick(which, g, none),
                )
            )
        grad_k = grad_v = None
        for span in spans(doc, Q_BLOCK):
            rows, grad_q, part_k, part_v = span.stop, [], None, None
            for which, (k_of, v_of, q_with, g_with, q_of, g_of) in enumerate(per_head):
                h = 2 * pair + which
                s = dot_nn(k_of[:rows], q_with[:, span])
                s = s + bias_block(table_ref, ids_ref, step * BLOCK_HEADS + h, rows, span.start)
                p = jnp.exp(s)
                ds = (p * dot_nn(v_of[:rows], g_with[:, span])).astype(BF16)
                ds_ref[h, :rows, span] = ds
                grad_q.append(dot_nn(k_t[half_rows(which), :rows], ds))
                to_v = dot_nn(p.astype(BF16), g_of[span])
                to_k = dot_nn(ds, q_of[span])
                part_v = to_v if part_v is None else part_v + to_v
                part_k = to_k if part_k is None else part_k + to_k
            grad_q = (jnp.concatenate(grad_q, axis=0) * SCALE).T
            grad_ref[span, lanes] = grad_q.astype(BF16)
            if grad_v is not None:
                part_v = jnp.concatenate(
                    [part_v[: span.start] + grad_v, part_v[span.start :]], axis=0
                )
                part_k = jnp.concatenate(
                    [part_k[: span.start] + grad_k, part_k[span.start :]], axis=0
                )
            grad_v, grad_k = part_v, part_k
        k_lanes = lane_block(features + step * HEAD_BLOCK + pair * LANES)
        v_lanes = lane_block(2 * features + step * HEAD_BLOCK + pair * LANES)
        grad_ref[:, k_lanes] = (grad_k * SCALE).astype(BF16)
        grad_ref[:, v_lanes] = grad_v.astype(BF16)

    @pl.when(step == pl.num_programs(0) - 1)
    def _():
        stack.wait(0, 1, 2)
        for ref, columns in ((give_ref, slice(0, half)), (keep_ref, slice(half, features))):
            for kind in range(3):
                kind_columns = slice(kind * features + columns.start, kind * features + columns.stop)
                ref[kind] = dot_tn(grad_ref[:, kind_columns], normed_ref[...]).astype(BF16)
            ref[3] = dot_tn(mixed_ref[:, columns], branch_ref[...]).astype(BF16)
        gain_grad_ref[...] = jnp.zeros_like(gain_grad_ref)
        back_ref[...] = dot_nn(grad_ref[...], w_ref[: 3 * features])
        for span in spans(doc, ROW_BLOCK):
            norm_back_into(
                span, back_ref[span], out_ref, None, gain_grad_ref, rows_ref, gain_ref, add_ref
            )


def cross_forward_kernel(heads, shares, length_ref, rows_ref, gain_ref, memory_ref, *refs):
    sources = refs[:shares]
    q_ref, k_ref, v_ref, mixed_ref, lse_ref, out_ref = refs[shares : shares + 6]
    w_ref, normed_ref, extra_ref, p_ref, mix_ref, sems = refs[shares + 6 :]
    step = pl.program_id(0)
    (doc, features), slots = rows_ref.shape, memory_ref.shape[0]
    stack = Stack(sources, w_ref, sems, 4, heads * HEAD_DIM)

    @pl.when(step == 0)
    def _():
        stack.start()
        norm_into(normed_ref, rows_ref, gain_ref)
        out_ref[...] = rows_ref[...]
        slot = lax.broadcasted_iota(jnp.int32, (slots, LANES), 0)
        extra_ref[...] = extra_lanes(slots, slot < length_ref[0])
        stack.wait(0, 1, 2, 3)

    def weights(kind):
        start = pl.multiple_of(kind * features + step * HEAD_BLOCK, HEAD_BLOCK)
        return w_ref[pl.ds(start, HEAD_BLOCK)]

    q_ref[...] = dot_nt(normed_ref[...], weights(0)).astype(BF16)
    k_ref[...] = dot_nt(memory_ref[...], weights(1)).astype(BF16)
    v_ref[...] = dot_nt(memory_ref[...], weights(2)).astype(BF16)

    units = [
        (pair, which, span)
        for pair in range(BLOCK_HEADS // 2)
        for span in spans(doc, Q_BLOCK)
        for which in range(2)
    ]
    ones = jnp.ones((TILE_ROWS, slots), BF16)
    keys = spans(slots, K_BLOCK)

    def lanes_of(pair):
        return slice(pair * LANES, (pair + 1) * LANES)

    def key_side(pair, which):
        return pick(which, k_ref[:, lanes_of(pair)], extra_ref[...])

    def write(pair, which, span, top, total, mixed):
        h = 2 * pair + which
        lse_ref[0, h : h + 1, span] = top + jnp.log(total)
        mix_ref[half_rows(which)] = mixed / total
        if which == 1:
            mixed_ref[span, lanes_of(pair)] = mix_ref[...].T.astype(BF16)

    v_t = [flip(v_ref[:, lanes_of(p)]) for p in range(BLOCK_HEADS // 2)]
    q_t = [q_ref[:, lanes_of(p)].astype(F32).T * SCALE for p in range(BLOCK_HEADS // 2)]

    def begin(unit):
        pair, which, span = unit
        k_of = key_side(pair, which)
        s = dot_nn(k_of[keys[0]], with_extra(which, q_t[pair][:, span], True, None))
        top = jnp.max(s, axis=0, keepdims=True)
        return k_of, s, top, with_extra(which, q_t[pair][:, span], True, top)

    worst = jnp.zeros((1, Q_BLOCK), F32)
    ahead = begin(units[0])
    for i, (pair, which, span) in enumerate(units):
        (k_of, s, top, q_with), slot = ahead, i % 2
        p_ref[slot, keys[0]] = jnp.exp(s - top).astype(BF16)
        for rows in keys[1:]:
            p_ref[slot, rows] = jnp.exp(dot_nn(k_of[rows], q_with)).astype(BF16)
        if i + 1 < len(units):
            ahead = begin(units[i + 1])
        value_side = jnp.concatenate([v_t[pair][half_rows(which)], ones], axis=0)
        mixed = dot_nn(value_side, p_ref[slot])
        total = mixed[HEAD_DIM : HEAD_DIM + 1]
        worst = jnp.maximum(worst, total)
        write(pair, which, span, top, total, mixed[:HEAD_DIM])

    @pl.when(jnp.max(worst) > LARGEST_SUM)
    def _():
        for pair, which, span in units:
            q_with = with_extra(
                which, q_ref[:, lanes_of(pair)].astype(F32).T[:, span] * SCALE, True, None
            )
            k_of = key_side(pair, which)
            s = [dot_nn(k_of[rows], q_with) for rows in keys]
            top = functools.reduce(jnp.maximum, [jnp.max(c, axis=0, keepdims=True) for c in s])
            total = jnp.zeros_like(top)
            for rows, chunk in zip(keys, s):
                p = jnp.exp(chunk - top)
                total = total + jnp.sum(p, axis=0, keepdims=True)
                p_ref[0, rows] = p.astype(BF16)
            mixed = dot_nn(flip(v_ref[:, lanes_of(pair)])[half_rows(which)], p_ref[0])
            write(pair, which, span, top, total, mixed)

    out_ref[...] += dot_nn(mixed_ref[...], weights(3))


def cross_backward_kernel(heads, shares, size, scattered, hops_wanted, length_ref, *refs):
    gain_ref, branch_ref, q_ref, mixed_ref, lse_ref = refs[:5]
    rows_in, memory_in, add_in, k_in, v_in = refs[5:10]
    sources = refs[10 : 10 + shares]
    count = shares // 2
    refs = refs[10 + shares :]
    scatter_in, refs = refs[:scattered], refs[scattered:]
    hidden_in, refs = refs[:hops_wanted], refs[hops_wanted:]
    hidden_out, refs = refs[:hops_wanted], refs[hops_wanted:]
    if scattered:
        scatter_out, refs = refs[0], refs[1:]
        (part_ref, ring_slots, done_ref, scatter_came), refs = refs[-8:-4], refs[:-8] + refs[-4:]
        (ring_send, ring_came, part_sems, done_sems), refs = refs[-4:], refs[:-4]
        scatter = Scatter(size, part_ref, ring_slots, done_ref, ring_send, ring_came)
        part_loads = [
            pltpu.make_async_copy(source, part_ref.at[i], part_sems.at[i])
            for i, source in enumerate(scatter_in)
        ]
        for copy in part_loads:
            copy.start()
    sums, refs = refs[:count], refs[count:]
    memory_out, out_ref, low_ref, gain_grad_ref = refs[:4]
    rows_ref, memory_ref, add_ref, k_ref, v_ref = refs[4:9]
    (
        w_ref,
        normed_ref,
        extra_ref,
        g_ref,
        grad_q_ref,
        grad_ref,
        ds_ref,
        give_ref,
        keep_ref,
        came_ref,
        memory_grad_ref,
        back_ref,
        sems,
        load_sems,
        key_sems,
        out_sems,
        swap_sems,
        hop_sems,
    ) = refs[9:]
    (doc, features), slots = rows_ref.shape, memory_ref.shape[0]
    half, blocks = features // 2, features // HEAD_BLOCK
    stack = Stack(sources, w_ref, sems, 4, heads * HEAD_DIM)
    loads = [
        pltpu.make_async_copy(source, target, load_sems.at[i])
        for i, (source, target) in enumerate(
            ((memory_in, memory_ref), (rows_in, rows_ref), (add_in, add_ref))
        )
    ]

    def key_copies(b):
        lanes = pl.ds(pl.multiple_of(b * HEAD_BLOCK, HEAD_BLOCK), HEAD_BLOCK)
        return [
            pltpu.make_async_copy(source.at[:, lanes], target.at[b], key_sems.at[i, b])
            for i, (source, target) in enumerate(((k_in, k_ref), (v_in, v_ref)))
        ]

    stack.start()
    for b in range(blocks):
        for copy in key_copies(b):
            copy.start()
    for copy in loads:
        copy.start()
    greet([1, 2][:count], [way[1] for way in ring_ways(size)] if scattered else [])
    hops = [
        to_differing(2, source, target, hop_sems.at[i])
        for i, (source, target) in enumerate(zip(hidden_in, hidden_out))
    ]
    for hop in hops:
        hop.start()
    if scattered:
        for copy in part_loads:
            copy.wait()
        scatter.begin()
    slot = lax.broadcasted_iota(jnp.int32, (slots, LANES), 0)
    extra_ref[...] = extra_lanes(slots, slot < length_ref[0])
    none = jnp.zeros((doc, LANES), BF16)
    stack.wait(3)

    def one_block(step, carry):
        start = pl.multiple_of(3 * features + step * HEAD_BLOCK, HEAD_BLOCK)
        g_ref[...] = dot_nt(branch_ref[...], w_ref[pl.ds(start, HEAD_BLOCK)]).astype(BF16)
        for copy in key_copies(step):
            copy.wait()
        for pair in range(BLOCK_HEADS // 2):
            local = slice(pair * LANES, (pair + 1) * LANES)
            lanes = lane_block(step * HEAD_BLOCK + pair * LANES)
            v_lanes = lane_block(features + step * HEAD_BLOCK + pair * LANES)
            q, g = q_ref[:, lanes], g_ref[:, local]
            q_t, g_t = q.astype(F32).T * SCALE, g.astype(F32).T
            inner = g_t * mixed_ref[:, lanes].astype(F32).T
            per_head = []
            for which in range(2):
                h = 2 * pair + which
                minus = jnp.sum(inner[half_rows(which)], axis=0, keepdims=True)
                per_head.append(
                    (
                        with_extra(which, q_t, True, lse_ref[step, h : h + 1, :]),
                        with_extra(which, g_t, False, minus),
                        pick(which, q, none),
                        pick(which, g, none),
                    )
                )
            for rows in spans(slots, K_BLOCK):
                k, v, extra = k_ref[step, rows, local], v_ref[step, rows, local], extra_ref[rows]
                part_k = part_v = None
                for which, (q_with, g_with, q_of, g_of) in enumerate(per_head):
                    p = jnp.exp(dot_nn(pick(which, k, extra), q_with))
                    ds = (p * dot_nn(pick(which, v, extra), g_with)).astype(BF16)
                    ds_ref[which, rows] = ds
                    to_v = dot_nn(p.astype(BF16), g_of)
                    to_k = dot_nn(ds, q_of)
                    part_v = to_v if part_v is None else part_v + to_v
                    part_k = to_k if part_k is None else part_k + to_k
                grad_ref[rows, lanes] = (part_k * SCALE).astype(BF16)
                grad_ref[rows, v_lanes] = part_v.astype(BF16)
            k_t = flip(k_ref[step, :, local])
            grad_q = [dot_nn(k_t[half_rows(which)], ds_ref[which]) for which in range(2)]
            grad_q_ref[:, lanes] = (jnp.concatenate(grad_q, axis=0) * SCALE).T.astype(BF16)
            if scattered:
                scatter_step(1 + step * (BLOCK_HEADS // 2) + pair)
        return carry

    places = blocks * (BLOCK_HEADS // 2)

    def scatter_step(step):
        if size - 2 >= places:
            scatter.advance(step)
        elif size > 2:

            @pl.when(step <= size - 2)
            def _():
                scatter.advance(step)

    lax.fori_loop(0, blocks, one_block, 0)
    if scattered:

        def rest(step, carry):
            scatter.advance(step)
            return carry

        lax.fori_loop(min(places, size - 2) + 1, size - 1, rest, 0)
        scatter.turn()
        done_hops = [
            to_differing(2, done_ref.at[:, i], scatter_came, done_sems)
            for i in range(1, scattered)
        ]
        for hop in done_hops:
            hop.start()

    for copy in loads:
        copy.wait()
    norm_into(normed_ref, rows_ref, gain_ref)

    def weight_grads(ref, first):
        columns = slice(first, first + half)
        v_columns = slice(features + first, features + first + half)
        ref[0] = dot_tn(grad_q_ref[:, columns], normed_ref[...]).astype(BF16)
        ref[1] = dot_tn(grad_ref[:, columns], memory_ref[...]).astype(BF16)
        ref[2] = dot_tn(grad_ref[:, v_columns], memory_ref[...]).astype(BF16)
        ref[3] = dot_tn(mixed_ref[:, columns], branch_ref[...]).astype(BF16)

    weight_grads(give_ref, 0)
    swap = to_differing(1, give_ref, came_ref, swap_sems)
    swap.start()
    stack.wait(0, 1, 2)
    writes = []
    for i, rows in enumerate(spans(slots, MEMORY_BLOCK)):
        memory_grad_ref[rows] = dot_nn(
            grad_ref[rows], w_ref[features : 3 * features]
        ).astype(BF16)
        writes.append(
            pltpu.make_async_copy(memory_grad_ref.at[rows], memory_out.at[rows], out_sems.at[i])
        )
        writes[-1].start()
    weight_grads(keep_ref, half)
    gain_grad_ref[...] = jnp.zeros_like(gain_grad_ref)
    back_ref[...] = dot_nn(grad_q_ref[...], w_ref[:features])
    for span in spans(doc, ROW_BLOCK):
        norm_back_into(
            span, back_ref[span], out_ref, low_ref, gain_grad_ref, rows_ref, gain_ref, add_ref
        )
    swap.wait_recv()
    rows = half // count
    for share, sums_ref in enumerate(sums):
        for kind in range(4):
            span = slice(share * rows, (share + 1) * rows)
            to = slice(kind * rows, (kind + 1) * rows)
            sums_ref[to] = low_sum(keep_ref[kind, span], came_ref[kind, span])
    swap.wait_send()
    for copy in writes:
        copy.wait()
    for hop in hops:
        hop.wait()
    if scattered:
        for hop in done_hops:
            hop.wait()
        own = done_ref[:, 0]
        scatter_out[...] = low_sum(own, scatter_came[...]) if done_hops else own
        scatter.wait_sent()


def feed_forward_kernel(first, last, rows_ref, gain_ref, cotangent_ref, *refs):
    sources, refs = refs[:2], refs[2:]
    if not first:
        before_in, refs = refs[:2], refs[2:]
    sums, layer_ref, out_ref = refs[:2], refs[2], refs[3]
    if last:
        low_ref, gain_grad_ref = refs[4:6]
        refs = refs[2:]
    (
        wide_ref,
        narrow_ref,
        normed_ref,
        normed_t,
        cotangent_t,
        active_ref,
        grad_ref,
        give_ref,
        keep_ref,
        came_ref,
        layer_in_ref,
        back_in_ref,
        product_ref,
        sems,
        before_sems,
        swap_sems,
    ) = refs[4:]
    step, steps = pl.program_id(0), pl.num_programs(0)
    half = steps // 2
    doc = rows_ref.shape[0]
    hidden = sources[0].shape[0] // 2
    copies = [
        [
            pltpu.make_async_copy(
                source.at[pl.ds(kind * hidden, hidden)],
                stack.at[pl.ds(p * hidden, hidden)],
                sems.at[p, kind],
            )
            for kind, stack in enumerate((wide_ref, narrow_ref))
        ]
        for p, source in enumerate(sources)
    ]
    loads = []
    if not first:
        loads = [
            pltpu.make_async_copy(source, target, before_sems.at[i])
            for i, (source, target) in enumerate(zip(before_in, (layer_in_ref, back_in_ref)))
        ]
    swap = to_differing(1, give_ref, came_ref, swap_sems)

    @pl.when(step == 0)
    def _():
        for pair in copies:
            for copy in pair:
                copy.start()
        for copy in loads:
            copy.start()
        greet([1])
        norm_into(normed_ref, rows_ref, gain_ref)
        for span in spans(doc, ROW_BLOCK):
            normed_t[:, span] = flip(normed_ref[span])
            cotangent_t[:, span] = flip(cotangent_ref[span])

    for p, pair in enumerate(copies):

        @pl.when(step == p * half)
        def _(pair=pair):
            for copy in pair:
                copy.wait()

    units = pl.ds(pl.multiple_of(step * HIDDEN_BLOCK, HIDDEN_BLOCK), HIDDEN_BLOCK)
    activated, slope = gelu_and_slope(dot_nn(wide_ref[units], normed_t[...]))
    active_ref[units] = activated.astype(BF16)
    grad_ref[units] = (dot_nn(narrow_ref[units], cotangent_t[...]) * slope).astype(BF16)

    def store(ref, at):
        rows = pl.ds(pl.multiple_of(at * HIDDEN_BLOCK, HIDDEN_BLOCK), HIDDEN_BLOCK)
        ref[0, rows] = dot_nn(grad_ref[units], normed_ref[...]).astype(BF16)
        ref[1, rows] = dot_nn(active_ref[units], cotangent_ref[...]).astype(BF16)

    @pl.when(step < half)
    def _():
        store(give_ref, step)

    @pl.when(step == half - 1)
    def _():
        swap.start()

    @pl.when(step >= half)
    def _():
        store(keep_ref, step - half)

    @pl.when(step == steps - 1)
    def _():
        for copy in loads:
            copy.wait()
        if last:
            gain_grad_ref[...] = jnp.zeros_like(gain_grad_ref)
        product_ref[...] = dot_tn(active_ref[...], narrow_ref[...])
        for span in spans(doc, ROW_BLOCK):
            layer = rows_ref[span] if first else layer_in_ref[span]
            layer_ref[span] = (layer + product_ref[span]).astype(layer_ref.dtype)
        product_ref[...] = dot_tn(grad_ref[...], wide_ref[...])
        for span in spans(doc, ROW_BLOCK):
            back = product_ref[span]
            if not first:
                back = back + back_in_ref[span]
            if last:
                norm_back_into(
                    span, back, out_ref, low_ref, gain_grad_ref, rows_ref, gain_ref, cotangent_ref
                )
            else:
                out_ref[span] = back
        swap.wait_recv()
        for kind, sums_ref in enumerate(sums):
            for span in spans(hidden, HIDDEN_BLOCK):
                sums_ref[span] = low_sum(keep_ref[kind, span], came_ref[kind, span])
        swap.wait_send()


def pack_kernel(flipped, *refs):
    out_ref, start = refs[-1], 0
    for source, turn in zip(refs[:-1], flipped):
        rows = source.shape[1] if turn else source.shape[0]
        span = slice(start, start + rows)
        out_ref[span] = flip(source[...]) if turn else source[...]
        start += rows


def finish_kernel(*refs):
    sources, outs, refs = refs[:4], refs[4:14], refs[14:]
    ins, wides, in_sems, out_sems = refs[:4], refs[4:14], refs[14], refs[15]
    loads, writes = [], []
    for i, (source, target) in enumerate(zip(sources, ins)):
        for j, span in enumerate(spans(target.shape[0], FINISH_BLOCK)):
            loads.append(
                pltpu.make_async_copy(source.at[span], target.at[span], in_sems.at[i, j])
            )
            loads[-1].start()

    def write(i, part):
        writes.append(
            pltpu.make_async_copy(wides[i].at[part], outs[i].at[part], out_sems.at[len(writes)])
        )
        writes[-1].start()

    waiting = iter(loads)
    hidden = wides[1].shape[0]
    for span in spans(hidden, FINISH_BLOCK):
        next(waiting).wait()
        for part in spans(FINISH_BLOCK, LANES):
            rows = slice(span.start + part.start, span.start + part.stop)
            wides[0][:, rows] = ins[0][rows].astype(F32).T
        write(0, (slice(None), span))
    for span in spans(hidden, FINISH_BLOCK):
        next(waiting).wait()
        wides[1][span] = ins[1][span].astype(F32)
        write(1, span)
    for i in (2, 3):
        for _ in spans(ins[i].shape[0], FINISH_BLOCK):
            next(waiting).wait()
        rows = wides[2].shape[0]
        for kind in range(4):
            at = 2 + 4 * (i - 2) + kind
            wides[at][...] = ins[i][kind * rows : (kind + 1) * rows].astype(F32)
            write(at, slice(None))
    for copy in writes:
        copy.wait()


def params():
    return pltpu.CompilerParams(vmem_limit_bytes=VMEM_BYTES)


def cost(flops=1 << 20):
    return pl.CostEstimate(flops=flops, bytes_accessed=1 << 16, transcendentals=0)


def shape(dims, dtype):
    return jax.ShapeDtypeStruct(dims, dtype)


def whole(array):
    return pl.BlockSpec(
        array.shape, lambda *_: (0,) * len(array.shape), pipeline_mode=pl.Buffered(1)
    )


def result(array):
    return pl.BlockSpec(array.shape, lambda *_: (0,) * len(array.shape))


def columns(rows):
    return pl.BlockSpec((rows, HEAD_BLOCK), lambda i: (0, i))


def anywhere(arrays):
    return [pl.BlockSpec(memory_space=pl.ANY) for _ in arrays]


SCALAR = pl.BlockSpec(memory_space=pltpu.SMEM)


def call(
    kernel, name, grid, in_specs, out_specs, out_shape, scratch, args, channel=None, flops=1 << 20
):
    compiler_params = params()
    if channel is not None:
        compiler_params = pltpu.CompilerParams(
            vmem_limit_bytes=VMEM_BYTES, collective_id=channel, has_side_effects=True
        )
    return pl.pallas_call(
        kernel,
        grid=grid,
        in_specs=in_specs,
        out_specs=out_specs,
        out_shape=out_shape,
        scratch_shapes=scratch,
        compiler_params=compiler_params,
        cost_estimate=cost(flops),
        name=name,
    )(*args)


def pack(*parts):
    arrays, flipped = zip(*parts)
    rows = sum(a.shape[1] if turn else a.shape[0] for a, turn in parts)
    features = arrays[0].shape[0] if flipped[0] else arrays[0].shape[1]
    return pl.pallas_call(
        functools.partial(pack_kernel, flipped),
        out_shape=shape((rows, features), BF16),
        compiler_params=params(),
        cost_estimate=cost(),
        name="pack",
    )(*arrays)


def self_forward(heads, buckets, rows, gain, weights, ids):
    doc, features = rows.shape
    shares, steps = len(weights), features // HEAD_BLOCK
    narrow, tall = shape((doc, features), BF16), shape((doc, features), F32)
    out_shape = (*[narrow] * 4, shape((steps, 8, doc), F32), tall)
    return call(
        functools.partial(self_forward_kernel, heads, buckets, shares),
        "self_forward",
        (steps,),
        [whole(rows), whole(gain), whole(ids), *anywhere(weights)],
        (*[columns(doc)] * 4, pl.BlockSpec((1, 8, doc), lambda i: (i, 0, 0)), result(tall)),
        out_shape,
        [
            pltpu.VMEM((4 * features, features), BF16),
            pltpu.VMEM((shares, TABLE_ROWS, features), BF16),
            pltpu.VMEM((TABLE_ROWS, LANES), F32),
            pltpu.VMEM((doc, features), BF16),
            pltpu.SemaphoreType.DMA((shares, 5)),
        ],
        (rows, gain, ids, *weights),
    )


def self_backward(heads, buckets, rows, gain, ids, branch, add, saved, weights):
    doc, features = rows.shape
    shares, steps = len(weights), features // HEAD_BLOCK
    packed = shape((4, features // 2, features), BF16)
    out_shape = (
        packed,
        packed,
        shape((steps * BLOCK_HEADS, doc, doc), BF16),
        shape((doc, features), F32),
        shape((8, features), F32),
    )
    *arrays, lse = saved
    return call(
        functools.partial(self_backward_kernel, heads, buckets, shares),
        "self_backward",
        (steps,),
        [
            *[whole(a) for a in (rows, gain, ids, branch, add, *arrays)],
            pl.BlockSpec((1, 8, doc), lambda i: (i, 0, 0)),
            *anywhere(weights),
        ],
        (
            result(packed),
            result(packed),
            pl.BlockSpec((BLOCK_HEADS, doc, doc), lambda i: (i, 0, 0)),
            result(out_shape[3]),
            result(out_shape[4]),
        ),
        out_shape,
        [
            pltpu.VMEM((4 * features, features), BF16),
            pltpu.VMEM((shares, TABLE_ROWS, features), BF16),
            pltpu.VMEM((TABLE_ROWS, LANES), F32),
            pltpu.VMEM((doc, features), BF16),
            pltpu.VMEM((doc, HEAD_BLOCK), BF16),
            pltpu.VMEM((doc, 3 * features), BF16),
            pltpu.VMEM((doc, features), F32),
            pltpu.SemaphoreType.DMA((shares, 5)),
        ],
        (rows, gain, ids, branch, add, *arrays, lse, *weights),
    )


def cross_forward(heads, rows, gain, memory, length, weights):
    (doc, features), slots = rows.shape, memory.shape[0]
    shares, steps = len(weights), features // HEAD_BLOCK
    query, key = shape((doc, features), BF16), shape((slots, features), BF16)
    tall = shape((doc, features), F32)
    return call(
        functools.partial(cross_forward_kernel, heads, shares),
        "cross_forward",
        (steps,),
        [SCALAR, whole(rows), whole(gain), whole(memory), *anywhere(weights)],
        (
            columns(doc),
            columns(slots),
            columns(slots),
            columns(doc),
            pl.BlockSpec((1, 8, doc), lambda i: (i, 0, 0)),
            result(tall),
        ),
        (query, key, key, query, shape((steps, 8, doc), F32), tall),
        [
            pltpu.VMEM((4 * features, features), BF16),
            pltpu.VMEM((doc, features), BF16),
            pltpu.VMEM((slots, LANES), BF16),
            pltpu.VMEM((2, slots, Q_BLOCK), BF16),
            pltpu.VMEM((LANES, Q_BLOCK), F32),
            pltpu.SemaphoreType.DMA((shares, 4)),
        ],
        (length, rows, gain, memory, *weights),
    )


def cross_backward(
    heads, size, rows, gain, memory, length, branch, add, saved, weights, scattered, hops
):
    (doc, features), slots = rows.shape, memory.shape[0]
    shares, blocks = len(weights), features // HEAD_BLOCK
    count = shares // 2
    blocks_out, ring_scratch = [], []
    if scattered:
        number, part = len(scattered), scattered[0].shape
        block = (2, part[0] // (2 * size), features)
        blocks_out = [shape(block, BF16)]
        steps = pltpu.SemaphoreType.DMA((2, size - 1))
        ring_scratch = [
            pltpu.VMEM((number, *part), BF16),
            pltpu.VMEM((2, size - 1, number, *block[1:]), BF16),
            pltpu.VMEM((2, number, *block[1:]), BF16),
            pltpu.VMEM(block, BF16),
            steps,
            steps,
            pltpu.SemaphoreType.DMA((number,)),
            pltpu.SemaphoreType.DMA((2,)),
        ]
    out_shape = (
        *[shape(h.shape, BF16) for h in hops],
        *blocks_out,
        *[shape((4 * heads * HEAD_DIM, features), BF16)] * count,
        shape((slots, features), BF16),
        shape((doc, features), F32),
        shape((doc, features), BF16),
        shape((8, features), F32),
    )
    query, key, value, mixed, lse = saved
    near = (gain, branch, query, mixed, lse)
    far = (rows, memory, add, key, value, *weights, *scattered, *hops)
    vmem, hbm = pl.BlockSpec(memory_space=pltpu.VMEM), pl.BlockSpec(memory_space=pl.ANY)
    packed = pltpu.VMEM((4, features // 2, features), BF16)
    key_block = pltpu.VMEM((blocks, slots, HEAD_BLOCK), BF16)
    return call(
        functools.partial(
            cross_backward_kernel, heads, shares, size, len(scattered), len(hops)
        ),
        "cross_backward",
        (),
        [SCALAR, *[vmem for _ in near], *[hbm for _ in far]],
        (
            *[hbm] * len(hops),
            *[vmem] * len(blocks_out),
            *[vmem] * count,
            hbm,
            vmem,
            vmem,
            vmem,
        ),
        out_shape,
        [
            pltpu.VMEM((doc, features), F32),
            pltpu.VMEM((slots, features), BF16),
            pltpu.VMEM((doc, features), F32),
            key_block,
            key_block,
            pltpu.VMEM((4 * features, features), BF16),
            pltpu.VMEM((doc, features), BF16),
            pltpu.VMEM((slots, LANES), BF16),
            pltpu.VMEM((doc, HEAD_BLOCK), BF16),
            pltpu.VMEM((doc, features), BF16),
            pltpu.VMEM((slots, 2 * features), BF16),
            pltpu.VMEM((2, slots, doc), BF16),
            packed,
            packed,
            packed,
            pltpu.VMEM((slots, features), BF16),
            pltpu.VMEM((doc, features), F32),
            pltpu.SemaphoreType.DMA((shares, 4)),
            pltpu.SemaphoreType.DMA((3,)),
            pltpu.SemaphoreType.DMA((2, blocks)),
            pltpu.SemaphoreType.DMA((slots // MEMORY_BLOCK,)),
            pltpu.SemaphoreType.DMA((2,)),
            pltpu.SemaphoreType.DMA((max(len(hops), 1), 2)),
            *ring_scratch,
        ],
        (length, *near, *far),
        channel=1,
    )


def feed_forward(rows, gain, cotangent, weights, before, last):
    (doc, features), shares = rows.shape, len(weights)
    share = weights[0].shape[0] // 2
    hidden = share * shares
    steps = hidden // HIDDEN_BLOCK
    summed, tall = shape((share, features), BF16), shape((doc, features), F32)
    low = shape((doc, features), BF16)
    rest = [low, tall, low, shape((8, features), F32)] if last else [tall, tall]
    kept, added = pltpu.VMEM((2, share, features), BF16), pltpu.VMEM(tall.shape, F32)
    return call(
        functools.partial(feed_forward_kernel, not before, last),
        "feed_forward",
        (steps,),
        [whole(rows), whole(gain), whole(cotangent), *anywhere(weights), *anywhere(before)],
        (result(summed), result(summed), *[result(o) for o in rest]),
        (summed, summed, *rest),
        [
            pltpu.VMEM((hidden, features), BF16),
            pltpu.VMEM((hidden, features), BF16),
            pltpu.VMEM((doc, features), BF16),
            pltpu.VMEM((features, doc), BF16),
            pltpu.VMEM((features, doc), BF16),
            pltpu.VMEM((hidden, doc), BF16),
            pltpu.VMEM((hidden, doc), BF16),
            kept,
            kept,
            kept,
            added,
            added,
            added,
            pltpu.SemaphoreType.DMA((shares, 2)),
            pltpu.SemaphoreType.DMA((2,)),
            pltpu.SemaphoreType.DMA((2,)),
        ],
        (rows, gain, cotangent, *weights, *before),
        channel=3 if before else 2,
    )


def finish(sum_wide, sum_narrow, sum_cross, sum_self):
    rows, features = sum_self.shape
    hidden, part = sum_wide.shape[0], shape((rows // 4, features), F32)
    out_shape = [shape((features, hidden), F32), shape((hidden, features), F32), *[part] * 8]
    sources = (sum_wide, sum_narrow, sum_cross, sum_self)
    writes = 2 * hidden // FINISH_BLOCK + 8
    wide, narrow, *parts = pl.pallas_call(
        finish_kernel,
        in_specs=anywhere(sources),
        out_specs=anywhere(out_shape),
        out_shape=out_shape,
        scratch_shapes=[
            *[pltpu.VMEM(source.shape, BF16) for source in sources],
            *[pltpu.VMEM(out.shape, F32) for out in out_shape],
            pltpu.SemaphoreType.DMA((4, hidden // FINISH_BLOCK)),
            pltpu.SemaphoreType.DMA((writes,)),
        ],
        compiler_params=params(),
        cost_estimate=cost(),
        name="finish",
    )(*sources)
    return wide, narrow, parts[4:], parts[:4]


def share_place(row, other, peers):
    j, bit = 0, 1
    while bit < peers:
        j = j + bit * ((row // bit + other // bit) % 2)
        bit *= 2
    return (j % 2) * (j // 2) + (1 - j % 2) * (peers // 2 + j // 2)


def tail_kernel(size, peers, buckets, heads, gathered, counts, *refs):
    parts = []
    for count in counts:
        parts.append(refs[:count])
        refs = refs[count:]
    arrays = len(counts) + 1
    give_ref, keep_ref, ids_ref, ds_ref, *gain_refs = refs[:7]
    outs, small_out_ref, refs = refs[7 : 7 + arrays], refs[7 + arrays], refs[8 + arrays :]
    slots, refs = refs[:arrays], refs[arrays:]
    firsts, refs = refs[:arrays], refs[arrays:]
    kept_ref, came_ref, folded_ref, far_came_ref, part_ref, scores_ref, bucket_ref = refs[:7]
    small_ref, near_ref, far_ref = refs[7:10]
    send, came, send_out, came_out, small_sems, hop_sems, local_sems = refs[10:]
    parts.append((part_ref,))
    me, row = lax.axis_index("dp"), lax.axis_index("mp")
    ways = ring_ways(size)
    doc = ids_ref.shape[0]
    mesh = pl.DeviceIdType.MESH

    load_scores = pltpu.make_async_copy(ds_ref, scores_ref, local_sems.at[0])
    load_kept = pltpu.make_async_copy(keep_ref, kept_ref, local_sems.at[1])
    load_scores.start()
    load_kept.start()

    barrier = pltpu.get_barrier_semaphore()

    def greet(t, carry):
        pl.semaphore_signal(
            barrier, inc=1, device_id=((me + t) % size, row), device_id_type=mesh
        )
        return carry

    lax.fori_loop(1, size, greet, 0)
    for t in range(1, peers):
        pl.semaphore_signal(
            barrier, inc=1, device_id=(me, (row + t) % peers), device_id_type=mesh
        )
    pl.semaphore_wait(barrier, size - 1 + peers - 1)

    def block(i, way, number):
        rows = outs[i].shape[0] // (2 * size)
        return pl.ds(pl.multiple_of((way * size + number) * rows, 16), rows)

    def part(i, span):
        total = parts[i][0][span].astype(F32)
        for ref in parts[i][1:]:
            total = total + ref[span].astype(F32)
        return total

    def first_copy(i, way):
        return remote(
            firsts[i].at[way],
            slots[i].at[way, 0],
            send.at[i, way, 0],
            came.at[i, way, 0],
            (ways[way][1], row),
        )

    def next_copy(i, way, step):
        return remote(
            slots[i].at[way, step - 1],
            slots[i].at[way, step],
            send.at[i, way, step],
            came.at[i, way, step],
            (ways[way][1], row),
        )

    def wait_came(i, way, step):
        remote(
            slots[i].at[way, step],
            slots[i].at[way, step],
            send.at[i, way, step],
            came.at[i, way, step],
            (ways[way][1], row),
        ).wait_recv()

    def out_copy(i, way, step):
        span = block(i, way, (ways[way][0] + 1 - step + size) % size)
        return remote(
            outs[i].at[span],
            outs[i].at[span],
            send_out.at[i, way, step],
            came_out.at[i, way, step],
            (ways[way][1], row),
        )

    def begin(rings):
        for i, way in rings:
            firsts[i][way] = part(i, block(i, way, ways[way][0])).astype(BF16)
            first_copy(i, way).start()

    def plus_part(i, way, step):
        span = block(i, way, (ways[way][0] - step - 1 + size) % size)
        total = slots[i][way, step].astype(F32) + part(i, span)
        return span, total.astype(BF16)

    def advance(rings, step):
        for i, way in rings:
            wait_came(i, way, step - 1)
            slots[i][way, step - 1] = plus_part(i, way, step - 1)[1]
            next_copy(i, way, step).start()

    def turn(rings):
        for i, way in rings:
            wait_came(i, way, size - 2)
            span, total = plus_part(i, way, size - 2)
            outs[i][span] = total
            out_copy(i, way, 0).start()

    def pass_on(rings, step):
        for i, way in rings:
            out_copy(i, way, step - 1).wait_recv()
            out_copy(i, way, step).start()

    ready = [(i, way) for i in range(gathered) for way in range(2)]
    early = [(i, way) for i in range(gathered, arrays - 1) for way in range(2)]
    late = [(arrays - 1, way) for way in range(2)]

    other_core = remote(
        give_ref, came_ref, hop_sems.at[0, 0], hop_sems.at[0, 1], (me, differing(row, 1))
    )
    other_core.start()
    begin(early)
    for i, way in ready:
        outs[i][block(i, way, (ways[way][0] + 1) % size)] = parts[i][0][way]
        out_copy(i, way, 0).start()

    rows_used, per_row = bucket_ref.shape[0], ds_ref.shape[0] // bucket_ref.shape[0]
    units = rows_used * buckets
    per_round = -(-units // max(2 * (size - 2), 1))

    def bucket_unit(u, carry):
        r, b = u // buckets, u % buckets
        sums = [jnp.zeros((8, LANES), F32) for _ in range(per_row)]
        for c in range(0, doc, LANES):
            hit = ids_ref[: c + LANES, c : c + LANES] == b
            for h in range(per_row):
                grads = scores_ref[r * per_row + h, : c + LANES, c : c + LANES].astype(F32)
                kept = jnp.where(hit, grads, 0.0).reshape(-1, 8, LANES)
                sums[h] = sums[h] + jnp.sum(kept, axis=0)
        for h in range(per_row):
            bucket_ref[r, h, pl.ds(b, 1), :] = jnp.sum(sums[h], axis=0, keepdims=True)
        return carry

    def bucket_round(k):
        low = jnp.minimum(k * per_round, units)
        lax.fori_loop(low, jnp.minimum(low + per_round, units), bucket_unit, 0)

    bucket_ref[...] = jnp.zeros_like(bucket_ref)
    part_ref[...] = jnp.zeros_like(part_ref)
    load_scores.wait()

    def early_step(step, carry):
        advance(early, step)
        pass_on(ready, step)
        bucket_round(step - 1)
        return carry

    middle = min(2, size - 1)
    lax.fori_loop(1, middle, early_step, 0)

    load_kept.wait()
    other_core.wait_recv()
    kinds, count = kept_ref.shape[0], folded_ref.shape[0]
    rows = kept_ref.shape[1] // count

    def fold(index, target, span_of):
        span = slice(index * rows, (index + 1) * rows)
        for kind in range(kinds):
            total = kept_ref[kind, span].astype(F32) + came_ref[kind, span].astype(F32)
            target[span_of(kind)] = total.astype(BF16)

    def kind_rows(kind):
        return slice(kind * rows, (kind + 1) * rows)

    other_chip = None
    if count == 2:
        fold(1, folded_ref.at[1], kind_rows)
        other_chip = remote(
            folded_ref.at[1],
            far_came_ref,
            hop_sems.at[1, 0],
            hop_sems.at[1, 1],
            (me, differing(row, 2)),
        )
        other_chip.start()
    fold(0, folded_ref.at[0], kind_rows)

    lax.fori_loop(middle, size - 1, early_step, 0)
    turn(early)
    used = slice(0, kinds * rows)
    if other_chip is None:
        part_ref[used] = folded_ref[0]
    else:
        other_chip.wait_recv()
        total = folded_ref[0].astype(F32) + far_came_ref[...].astype(F32)
        part_ref[used] = total.astype(BF16)
    begin(late)

    def middle_step(step, carry):
        pass_on(early, step)
        advance(late, step)
        bucket_round(size - 2 + step - 1)
        return carry

    lax.fori_loop(1, size - 1, middle_step, 0)
    if size == 2:
        lax.fori_loop(0, units, bucket_unit, 0)
    turn(late)

    features = gain_refs[0].shape[1]
    per_gain = features // LANES
    gain_rows = len(gain_refs) * per_gain
    small_ref[...] = jnp.zeros_like(small_ref)
    for i, ref in enumerate(gain_refs):
        total = jnp.sum(ref[...], axis=0, keepdims=True)
        for c in range(per_gain):
            at = i * per_gain + c
            small_ref[at : at + 1, :] = total[:, c * LANES : (c + 1) * LANES]
    for r in range(rows_used):
        block_sums = bucket_ref[r].reshape(LANES, LANES).T
        at = gain_rows + r
        small_ref[at : at + 1, :] = jnp.sum(block_sums, axis=0, keepdims=True)

    def near_copy(t):
        return remote(
            small_ref,
            near_ref.at[row],
            small_sems.at[0, t],
            small_sems.at[1, t],
            (me, (row + t) % peers),
        )

    def far_copy(t):
        return remote(
            far_ref.at[me],
            far_ref.at[me],
            small_sems.at[2, t],
            small_sems.at[3, t],
            ((me + t) % size, row),
        )

    for t in range(1, peers):
        near_copy(t).start()
    near_ref[pl.ds(row, 1)] = small_ref[...][None]
    for t in range(1, peers):
        near_copy(t).wait_recv()
    own = rows_used // peers
    total, sums = None, None
    for k in range(peers):
        gains = near_ref[k, :gain_rows]
        mine = near_ref[k, pl.ds(gain_rows + own * share_place(row, k, peers), own)]
        total = gains if total is None else total + gains
        sums = mine if sums is None else sums + mine
    small_ref_rows = far_ref.shape[1]
    far_ref[pl.ds(me, 1)] = jnp.concatenate(
        [total, sums, jnp.zeros((small_ref_rows - gain_rows - own, LANES), F32)], axis=0
    )[None]

    def far_start(t, carry):
        far_copy(t).start()
        return carry

    lax.fori_loop(1, size, far_start, 0)

    def late_step(step, carry):
        pass_on(late, step)
        return carry

    lax.fori_loop(1, size - 1, late_step, 0)

    def far_wait(t, carry):
        far_copy(t).wait()
        return carry

    lax.fori_loop(1, size, far_wait, 0)

    def far_add(k, total):
        return total + far_ref[k]

    small_out_ref[...] = lax.fori_loop(1, size, far_add, far_ref[0])
    for i, way in ready + early + late:
        out_copy(i, way, size - 2).wait_recv()

    for t in range(1, peers):
        near_copy(t).wait_send()
    other_core.wait_send()
    if other_chip is not None:
        other_chip.wait_send()
    for i, way in early + late:
        first_copy(i, way).wait_send()

    def sent(step, carry):
        for i, way in early + late:
            next_copy(i, way, step).wait_send()
        return carry

    lax.fori_loop(1, size - 1, sent, 0)

    def sent_out(step, carry):
        for i, way in ready + early + late:
            out_copy(i, way, step).wait_send()
        return carry

    lax.fori_loop(0, size - 1, sent_out, 0)


def tail_sums(size, peers, buckets, heads, blocks, terms, give, keep, ids, ds, gains):
    assert peers in (2, 4)
    grain = 2 * 16 * size
    kinds, half, features = keep.shape
    count = peers // 2
    rows = [size * 2 * b.shape[1] for b in blocks]
    rows += [arrays[0].shape[0] for arrays in terms]
    rows.append(kinds * half // count)
    padded = [r + -r % grain for r in rows]
    parts = [[b] for b in blocks]
    for arrays, r, p in zip(terms, rows[len(blocks) :], padded[len(blocks) :]):
        parts.append([jnp.pad(a, ((0, p - r), (0, 0))) for a in arrays])
    flat = [a for arrays in parts for a in arrays]
    lines = peers * (-(-heads * buckets // LANES))
    small = len(gains) * features // LANES + lines
    small = shape((small + -small % 8, LANES), F32)
    vmem, hbm = pl.BlockSpec(memory_space=pltpu.VMEM), pl.BlockSpec(memory_space=pl.ANY)
    steps = pltpu.SemaphoreType.DMA((len(rows), 2, size - 1))

    def ring_slots(i, steps):
        if i < len(blocks):
            return pltpu.VMEM((2, 1, 16, LANES), BF16)
        return pltpu.VMEM((2, *steps, padded[i] // (2 * size), features), BF16)

    *sums, small = pl.pallas_call(
        functools.partial(
            tail_kernel, size, peers, buckets, heads, len(blocks), [len(a) for a in parts]
        ),
        in_specs=[*[vmem] * len(flat), hbm, hbm, vmem, hbm, *[vmem] * len(gains)],
        out_specs=[vmem] * (len(rows) + 1),
        out_shape=[*[shape((p, features), BF16) for p in padded], small],
        scratch_shapes=[
            *[ring_slots(i, (size - 1,)) for i in range(len(rows))],
            *[ring_slots(i, ()) for i in range(len(rows))],
            pltpu.VMEM(keep.shape, BF16),
            pltpu.VMEM(keep.shape, BF16),
            pltpu.VMEM((count, rows[-1], features), BF16),
            pltpu.VMEM((rows[-1], features), BF16),
            pltpu.VMEM((padded[-1], features), BF16),
            pltpu.VMEM(ds.shape, BF16),
            pltpu.VMEM((lines, LANES // buckets, buckets, LANES), F32),
            pltpu.VMEM(small.shape, F32),
            pltpu.VMEM((peers, *small.shape), F32),
            pltpu.VMEM((size, *small.shape), F32),
            steps,
            steps,
            steps,
            steps,
            pltpu.SemaphoreType.DMA((4, max(size, peers))),
            pltpu.SemaphoreType.DMA((2, 2)),
            pltpu.SemaphoreType.DMA((2,)),
        ],
        compiler_params=pltpu.CompilerParams(
            vmem_limit_bytes=VMEM_BYTES, collective_id=0, has_side_effects=True
        ),
        cost_estimate=cost(),
        name="tail_sums",
    )(*flat, give, keep, ids, ds, *gains)
    return [total[:r] for total, r in zip(sums, rows)], small


def swap(array, bit, size):
    return lax.ppermute(array, "mp", [(i, i ^ bit) for i in range(size)])


def after(array, *others):
    return lax.optimization_barrier((array, others))[0]


def shards(
    decoder_rows,
    memory_rows,
    decoder_token_length,
    memory_length,
    bucket_ids,
    relative_bucket_bias,
    self_gain,
    self_query,
    self_key,
    self_value,
    self_out,
    cross_gain,
    cross_query,
    cross_key,
    cross_value,
    cross_out,
    hidden_gain,
    widen_weight,
    narrow_weight,
    layer_cotangent,
):
    dp_size = lax.axis_size("dp")
    mp_size = lax.axis_size("mp")
    me = lax.axis_index("mp")
    doc, features = decoder_rows.shape
    slots = memory_rows.shape[0]
    cols = self_query.shape[1]
    heads = cols // HEAD_DIM
    buckets = relative_bucket_bias.shape[0]
    order = [*range(1, mp_size, 2), *range(0, mp_size, 2)]

    doc_length = lax.dynamic_index_in_dim(decoder_token_length, me, keepdims=False)
    doc_memory = lax.dynamic_index_in_dim(memory_length, me)
    position = jnp.arange(doc, dtype=jnp.int32)
    allowed = (position[:, None] <= position[None, :]) & (position[:, None] < doc_length)
    ids = jnp.where(allowed, bucket_ids.T, buckets)
    bias_rows = jnp.zeros((TABLE_ROWS, features), BF16)
    bias_rows = bias_rows.at[:heads, :buckets].set(relative_bucket_bias.T)
    own_self = pack(
        (self_query.T, False), (self_key.T, False), (self_value.T, False), (self_out, False), (bias_rows, False)
    )
    own_cross = pack(
        (cross_query.T, False), (cross_key.T, False), (cross_value.T, False), (cross_out, False)
    )
    own_hidden = pack((widen_weight, True), (narrow_weight, False))

    def first_hops(own):
        shares, bit = {0: own}, mp_size // 2
        while bit > 1:
            for j in list(shares):
                shares[j | bit] = swap(shares[j], bit, mp_size)
            bit //= 2
        return shares

    def last_hop(shares, *others):
        if 1 not in shares:
            shares[1] = swap(shares[0], 1, mp_size)
        for j in range(2, mp_size, 2):
            shares[j] = after(shares[j], *others)
            shares[j | 1] = swap(shares[j], 1, mp_size)
        return shares

    near_self = first_hops(own_self)
    near_self[1] = swap(own_self, 1, mp_size)
    memory_rows = after(memory_rows, own_self)
    w_self = last_hop(near_self, own_cross, own_hidden, ids)
    w_self = [w_self[j] for j in order]
    near_cross = first_hops(own_cross)
    near_hidden = first_hops(own_hidden)
    near_hidden[1] = swap(own_hidden, 1, mp_size)
    memory_seen = lax.all_to_all(
        memory_rows.reshape(dp_size, slots // dp_size, features), "dp", 0, 0
    ).reshape(slots, features)

    gain_self = self_gain.astype(F32)[None]
    gain_cross = cross_gain.astype(F32)[None]
    gain_hidden = hidden_gain.astype(F32)[None]

    *saved_self, after_self = self_forward(heads, buckets, decoder_rows, gain_self, w_self, ids)
    w_cross = last_hop(near_cross, after_self)
    w_cross = [w_cross[j] for j in order]
    *saved_cross, after_cross = cross_forward(
        heads, after_self, gain_cross, memory_seen, doc_memory, w_cross
    )

    before, wide_sums, narrow_sums, w_hidden = (), [], [], near_hidden
    for j in range(0, mp_size, 2):
        wide_sum, narrow_sum, *before = feed_forward(
            after_cross,
            gain_hidden,
            layer_cotangent,
            [w_hidden[j + 1], w_hidden[j]],
            before,
            j == mp_size - 2,
        )
        wide_sums.append(wide_sum)
        narrow_sums.append(narrow_sum)
        if j == 0:
            w_hidden = last_hop(near_hidden, before[0])
    layer_output, grad_after_cross, branch, hidden_gain_grad = before

    scattered, hops = wide_sums, narrow_sums[1:]
    if wide_sums[0].shape[0] % (2 * 16 * dp_size):
        scattered, hops = [], wide_sums[1:] + narrow_sums[1:]
    *sums, grad_memory, grad_after_self, branch, cross_gain_grad = cross_backward(
        heads,
        dp_size,
        after_self,
        gain_cross,
        memory_seen,
        doc_memory,
        branch,
        grad_after_cross,
        saved_cross,
        w_cross,
        scattered,
        hops,
    )
    came, sums = sums[: len(hops)], sums[len(hops) :]
    if scattered:
        blocks, terms, cross_sums = sums[:1], [narrow_sums[:1] + came], sums[1:]
    else:
        blocks, cross_sums = [], sums
        hidden = [wide_sums[0], narrow_sums[0]], came
        terms = [[jnp.concatenate(both, axis=0) for both in hidden if both]]
    memory_grad = lax.all_to_all(
        grad_memory.reshape(dp_size, slots // dp_size, features), "dp", 0, 0
    ).reshape(slots, features)
    cross_sums[1:] = [swap(share, 2, mp_size) for share in cross_sums[1:]]

    give, keep, score_grads, input_grad, self_gain_grad = self_backward(
        heads,
        buckets,
        decoder_rows,
        gain_self,
        ids,
        branch,
        grad_after_self,
        saved_self,
        w_self,
    )
    (*hidden, sum_cross, sum_self), small = tail_sums(
        dp_size,
        mp_size,
        buckets,
        heads,
        blocks,
        terms + [cross_sums],
        give,
        keep,
        ids,
        score_grads,
        (self_gain_grad, cross_gain_grad, hidden_gain_grad),
    )
    wide_grad, narrow_grad, self_grads, cross_grads = finish(
        *(hidden if scattered else jnp.split(hidden[0], 2)), sum_cross, sum_self
    )
    gain_rows = 3 * features // LANES
    gains = small[:gain_rows].reshape(3, features)
    lines = -(-heads * buckets // LANES)
    sums = small[gain_rows : gain_rows + lines, : heads // lines * buckets]
    position_grad = sums.reshape(heads, buckets).T

    return (
        layer_output,
        input_grad,
        memory_grad,
        position_grad,
        gains[0],
        *[grad.T for grad in self_grads[:3]],
        self_grads[3],
        gains[1],
        *[grad.T for grad in cross_grads[:3]],
        cross_grads[3],
        gains[2],
        wide_grad,
        narrow_grad,
    )


def solution(mesh):
    return jax.shard_map(
        shards,
        mesh=mesh,
        in_specs=(
            P(("dp", "mp"), None),
            P(("dp", "mp"), None),
            P("dp"),
            P("dp"),
            P(),
            P(None, "mp"),
            P(),
            P(None, "mp"),
            P(None, "mp"),
            P(None, "mp"),
            P("mp", None),
            P(),
            P(None, "mp"),
            P(None, "mp"),
            P(None, "mp"),
            P("mp", None),
            P(),
            P(None, "mp"),
            P("mp", None),
            P(("dp", "mp"), None),
        ),
        out_specs=(
            P(("dp", "mp"), None),
            P(("dp", "mp"), None),
            P(("dp", "mp"), None),
            P(None, "mp"),
            P(),
            P(None, "mp"),
            P(None, "mp"),
            P(None, "mp"),
            P("mp", None),
            P(),
            P(None, "mp"),
            P(None, "mp"),
            P(None, "mp"),
            P("mp", None),
            P(),
            P(None, "mp"),
            P("mp", None),
        ),
        check_vma=False,
    )
```

```python
import functools

import jax
import jax.numpy as jnp
from jax import lax
from jax.experimental import pallas as pl
from jax.experimental.pallas import tpu as pltpu
from jax.sharding import PartitionSpec as P

HEAD_DIM = 64
NORM_EPS = 1e-06
MASKED = -1e30
SCALE = HEAD_DIM**-0.5
BF16 = jnp.bfloat16
F32 = jnp.float32
LANES = 128
TABLE_ROWS = 16
TILE_ROWS = 16
LARGEST_SUM = 1e30
LATE_STEP = 5
HEAD_BLOCK = 256
BLOCK_HEADS = HEAD_BLOCK // HEAD_DIM
Q_BLOCK = 256
K_BLOCK = 512
FORWARD_K_BLOCK = 256
HIDDEN_BLOCK = 256
MEMORY_BLOCK = 768
FINISH_BLOCK = 384
ROW_BLOCK = 128
VMEM_BYTES = 56 * 1024 * 1024
GELU_ROOT = 0.7978845608028654
GELU_CUBE = 0.044715


def dot_nn(a, b):
    return lax.dot_general(a, b, (((1,), (0,)), ((), ())), preferred_element_type=F32)


def dot_nt(a, b):
    return lax.dot_general(a, b, (((1,), (1,)), ((), ())), preferred_element_type=F32)


def dot_tn(a, b):
    return lax.dot_general(a, b, (((0,), (0,)), ((), ())), preferred_element_type=F32)


def flip(a):
    return a.astype(F32).T.astype(BF16)


def spans(size, step):
    return [slice(i, i + step) for i in range(0, size, step)]


def norm_scale(rows):
    return lax.rsqrt(jnp.mean(rows * rows, axis=-1, keepdims=True) + NORM_EPS)


def norm_into(normed_ref, rows_ref, gain_ref):
    for span in spans(rows_ref.shape[0], ROW_BLOCK):
        rows = rows_ref[span].astype(F32)
        normed_ref[span] = (rows * norm_scale(rows) * gain_ref[...]).astype(BF16)


def norm_back_into(span, grad, out_ref, low_ref, gain_grad_ref, rows_ref, gain_ref, add_ref):
    rows = rows_ref[span].astype(F32)
    scale = norm_scale(rows)
    unit = rows * scale
    grad_unit = grad * gain_ref[...]
    mean = jnp.mean(grad_unit * unit, axis=-1, keepdims=True)
    out = add_ref[span].astype(F32) + scale * (grad_unit - unit * mean)
    out_ref[span] = out
    if low_ref is not None:
        low_ref[span] = out.astype(BF16)
    gain_grad_ref[...] += jnp.sum((grad * unit).reshape(-1, 8, rows.shape[1]), axis=0)


def gelu_and_slope(v):
    square = v * v
    bend = jnp.tanh(GELU_ROOT * (v + GELU_CUBE * v * square))
    half = 0.5 * (1.0 + bend)
    slope = half + 0.5 * v * (1.0 - bend * bend) * GELU_ROOT * (1.0 + 3.0 * GELU_CUBE * square)
    return v * half, slope


def lane_block(start):
    return pl.ds(pl.multiple_of(start, LANES), LANES)


def extra_lanes(rows, allowed):
    lane = lax.broadcasted_iota(jnp.int32, (rows, LANES), 1) % HEAD_DIM
    first = MASKED if allowed is None else jnp.where(allowed, 0.0, MASKED)
    return jnp.where(lane == 0, first, jnp.where(lane < 4, 1.0, 0.0)).astype(BF16)


def pick(which, block, other):
    lane = lax.broadcasted_iota(jnp.int32, block.shape, 1)
    return jnp.where((lane < HEAD_DIM) == (which == 0), block, other)


def half_rows(which):
    return slice(which * HEAD_DIM, (which + 1) * HEAD_DIM)


def split(values):
    high = values.astype(BF16).astype(F32)
    rest = values - high
    middle = rest.astype(BF16).astype(F32)
    return high, middle, rest - middle


def with_extra(which, block_t, masked, minus):
    columns = block_t.shape[1]
    row = lax.broadcasted_iota(jnp.int32, (HEAD_DIM, columns), 0)
    extra = jnp.where(row == 0, 1.0 if masked else 0.0, 0.0)
    if minus is not None:
        for i, part in enumerate(split(minus)):
            extra = jnp.where(row == i + 1, -part, extra)
    own = block_t[half_rows(which)]
    return jnp.concatenate([own, extra] if which == 0 else [extra, own], axis=0).astype(BF16)


def bias_block(table_ref, ids_ref, index, rows, start):
    row = jnp.broadcast_to(table_ref[pl.ds(index, 1), :], (rows, LANES))
    return jnp.concatenate(
        [
            jnp.take_along_axis(row, ids_ref[:rows, c : c + LANES], axis=1)
            for c in range(start, start + Q_BLOCK, LANES)
        ],
        axis=1,
    )


def ring_place(me, size):
    return jnp.where(me % 2 == 0, me // 2, size - 1 - me // 2)


def ring_device(place, size):
    return jnp.where(place < size // 2, 2 * place, 2 * (size - 1 - place) + 1)


def ring_ways(size):
    me = lax.axis_index("dp")
    place = ring_place(me, size)
    return (
        (place, ring_device((place + 1) % size, size)),
        (size - 1 - place, ring_device((place + size - 1) % size, size)),
    )


def differing(row, bit):
    return row + bit - 2 * bit * ((row // bit) % 2)


def remote(source, target, send_sem, recv_sem, device):
    return pltpu.make_async_remote_copy(
        src_ref=source,
        dst_ref=target,
        send_sem=send_sem,
        recv_sem=recv_sem,
        device_id=device,
        device_id_type=pl.DeviceIdType.MESH,
    )


def greet(bits, devices=()):
    me, row = lax.axis_index("dp"), lax.axis_index("mp")
    barrier = pltpu.get_barrier_semaphore()
    others = [(me, differing(row, bit)) for bit in bits] + [(device, row) for device in devices]
    for other in others:
        pl.semaphore_signal(
            barrier, inc=1, device_id=other, device_id_type=pl.DeviceIdType.MESH
        )
    pl.semaphore_wait(barrier, len(others))


def to_differing(bit, source, target, sems):
    me, row = lax.axis_index("dp"), lax.axis_index("mp")
    return remote(source, target, sems.at[0], sems.at[1], (me, differing(row, bit)))


class Scatter:
    def __init__(self, size, part, slots, done, send, came):
        self.size, self.part, self.slots, self.done = size, part, slots, done
        self.send, self.came = send, came
        self.ways, self.row = ring_ways(size), lax.axis_index("mp")

    def span(self, way, number):
        rows = self.slots.shape[3]
        return pl.ds(pl.multiple_of((way * self.size + number) * rows, 16), rows)

    def copy(self, way, step, source):
        return remote(
            source,
            self.slots.at[way, step],
            self.send.at[way, step],
            self.came.at[way, step],
            (self.ways[way][1], self.row),
        )

    def first(self, way):
        return self.copy(way, 0, self.part.at[:, self.span(way, self.ways[way][0])])

    def next(self, way, step):
        return self.copy(way, step, self.slots.at[way, step - 1])

    def begin(self):
        for way in range(2):
            self.first(way).start()

    def total(self, way, step):
        self.copy(way, step, self.slots.at[way, step]).wait_recv()
        span = self.span(way, (self.ways[way][0] - step - 1 + self.size) % self.size)
        return low_sum(self.slots[way, step], self.part[:, span])

    def advance(self, step):
        for way in range(2):
            self.slots[way, step - 1] = self.total(way, step - 1)
            self.next(way, step).start()

    def turn(self):
        for way in range(2):
            self.done[way] = self.total(way, self.size - 2)

    def wait_sent(self):
        for way in range(2):
            self.first(way).wait_send()

        def sent(step, carry):
            for way in range(2):
                self.next(way, step).wait_send()
            return carry

        lax.fori_loop(1, self.size - 1, sent, 0)


def low_sum(a, b):
    return (a.astype(F32) + b.astype(F32)).astype(BF16)


class Stack:
    def __init__(self, sources, stack_ref, sems, kinds, rows):
        features = stack_ref.shape[0] // kinds
        self.copies = [
            [
                pltpu.make_async_copy(
                    source.at[pl.ds(kind * rows, rows)],
                    stack_ref.at[pl.ds(kind * features + p * rows, rows)],
                    sems.at[p, kind],
                )
                for p, source in enumerate(sources)
            ]
            for kind in range(kinds)
        ]

    def start(self):
        for copies in self.copies:
            for copy in copies:
                copy.start()

    def wait(self, *kinds):
        for kind in kinds:
            for copy in self.copies[kind]:
                copy.wait()


def table_copies(sources, tables_ref, sems, kinds):
    start = sources[0].shape[0] - TABLE_ROWS
    return [
        pltpu.make_async_copy(
            source.at[pl.ds(start, TABLE_ROWS)], tables_ref.at[p], sems.at[p, kinds]
        )
        for p, source in enumerate(sources)
    ]


def table_into(table_ref, tables_ref, heads, buckets):
    for p in range(tables_ref.shape[0]):
        rows = tables_ref[p, :, :LANES].astype(F32)
        lane = lax.broadcasted_iota(jnp.int32, rows.shape, 1)
        rows = jnp.where(lane < buckets, rows, MASKED)
        for h in range(heads):
            table_ref[p * heads + h : p * heads + h + 1, :] = rows[h : h + 1, :]


def self_forward_kernel(heads, buckets, shares, rows_ref, gain_ref, ids_ref, *refs):
    sources = refs[:shares]
    q_ref, k_ref, v_ref, mixed_ref, lse_ref, out_ref = refs[shares : shares + 6]
    w_ref, tables_ref, table_ref, normed_ref, sems = refs[shares + 6 :]
    step = pl.program_id(0)
    doc, features = rows_ref.shape
    stack = Stack(sources, w_ref, sems, 4, heads * HEAD_DIM)

    @pl.when(step == 0)
    def _():
        stack.start()
        tables = table_copies(sources, tables_ref, sems, 4)
        for copy in tables:
            copy.start()
        norm_into(normed_ref, rows_ref, gain_ref)
        out_ref[...] = rows_ref[...].astype(F32)
        for copy in tables:
            copy.wait()
        table_into(table_ref, tables_ref, heads, buckets)
        stack.wait(0, 1, 2, 3)

    def weights(kind):
        start = pl.multiple_of(kind * features + step * HEAD_BLOCK, HEAD_BLOCK)
        return w_ref[pl.ds(start, HEAD_BLOCK)]

    for kind, ref in enumerate((q_ref, k_ref, v_ref)):
        ref[...] = dot_nt(normed_ref[...], weights(kind)).astype(BF16)
    none = jnp.zeros((doc, LANES), BF16)
    for pair in range(BLOCK_HEADS // 2):
        lanes = slice(pair * LANES, (pair + 1) * LANES)
        k, v_t = k_ref[:, lanes], flip(v_ref[:, lanes])
        q_t = flip(q_ref[:, lanes].astype(F32) * SCALE)
        k_of = [pick(which, k, none) for which in range(2)]
        for span in spans(doc, Q_BLOCK):
            rows, mixed = span.stop, []
            for which in range(2):
                h = 2 * pair + which
                s = dot_nn(k_of[which][:rows], q_t[:, span])
                s = s + bias_block(table_ref, ids_ref, step * BLOCK_HEADS + h, rows, span.start)
                top = jnp.max(s, axis=0, keepdims=True)
                p = jnp.exp(s - top)
                total = jnp.sum(p, axis=0, keepdims=True)
                mixed.append(dot_nn(v_t[half_rows(which), :rows], p.astype(BF16)) / total)
                lse_ref[0, h : h + 1, span] = top + jnp.log(total)
            mixed_ref[span, lanes] = jnp.concatenate(mixed, axis=0).T.astype(BF16)
    out_ref[...] += dot_nn(mixed_ref[...], weights(3))


def self_backward_kernel(heads, buckets, shares, *refs):
    rows_ref, gain_ref, ids_ref, branch_ref, add_ref = refs[:5]
    q_ref, k_ref, v_ref, mixed_ref, lse_ref = refs[5:10]
    sources = refs[10 : 10 + shares]
    give_ref, keep_ref, ds_ref, out_ref, gain_grad_ref = refs[10 + shares : 15 + shares]
    w_ref, tables_ref, table_ref, normed_ref, g_ref, grad_ref, back_ref, sems = refs[15 + shares :]
    step = pl.program_id(0)
    doc, features = rows_ref.shape
    half = features // 2
    stack = Stack(sources, w_ref, sems, 4, heads * HEAD_DIM)

    @pl.when(step == 0)
    def _():
        stack.start()
        tables = table_copies(sources, tables_ref, sems, 4)
        for copy in tables:
            copy.start()
        norm_into(normed_ref, rows_ref, gain_ref)
        for copy in tables:
            copy.wait()
        table_into(table_ref, tables_ref, heads, buckets)
        stack.wait(3)

    start = pl.multiple_of(3 * features + step * HEAD_BLOCK, HEAD_BLOCK)
    g_ref[...] = dot_nt(branch_ref[...], w_ref[pl.ds(start, HEAD_BLOCK)]).astype(BF16)
    none = jnp.zeros((doc, LANES), BF16)
    ones = extra_lanes(doc, None)
    for pair in range(BLOCK_HEADS // 2):
        lanes = lane_block(step * HEAD_BLOCK + pair * LANES)
        q, k, v = q_ref[:, lanes], k_ref[:, lanes], v_ref[:, lanes]
        g = g_ref[:, pair * LANES : (pair + 1) * LANES]
        q_t, k_t = q.astype(F32).T * SCALE, flip(k)
        g_t = g.astype(F32).T
        inner = g_t * mixed_ref[:, lanes].astype(F32).T
        per_head = []
        for which in range(2):
            h = 2 * pair + which
            minus = jnp.sum(inner[half_rows(which)], axis=0, keepdims=True)
            per_head.append(
                (
                    pick(which, k, ones),
                    pick(which, v, ones),
                    with_extra(which, q_t, False, lse_ref[0, h : h + 1, :]),
                    with_extra(which, g_t, False, minus),
                    pick(which, q, none),
                    pick(which, g, none),
                )
            )
        grad_k = grad_v = None
        for span in spans(doc, Q_BLOCK):
            rows, grad_q, part_k, part_v = span.stop, [], None, None
            for which, (k_of, v_of, q_with, g_with, q_of, g_of) in enumerate(per_head):
                h = 2 * pair + which
                s = dot_nn(k_of[:rows], q_with[:, span])
                s = s + bias_block(table_ref, ids_ref, step * BLOCK_HEADS + h, rows, span.start)
                p = jnp.exp(s)
                ds = (p * dot_nn(v_of[:rows], g_with[:, span])).astype(BF16)
                ds_ref[h, :rows, span] = ds
                grad_q.append(dot_nn(k_t[half_rows(which), :rows], ds))
                to_v = dot_nn(p.astype(BF16), g_of[span])
                to_k = dot_nn(ds, q_of[span])
                part_v = to_v if part_v is None else part_v + to_v
                part_k = to_k if part_k is None else part_k + to_k
            grad_q = (jnp.concatenate(grad_q, axis=0) * SCALE).T
            grad_ref[span, lanes] = grad_q.astype(BF16)
            if grad_v is not None:
                part_v = jnp.concatenate(
                    [part_v[: span.start] + grad_v, part_v[span.start :]], axis=0
                )
                part_k = jnp.concatenate(
                    [part_k[: span.start] + grad_k, part_k[span.start :]], axis=0
                )
            grad_v, grad_k = part_v, part_k
        k_lanes = lane_block(features + step * HEAD_BLOCK + pair * LANES)
        v_lanes = lane_block(2 * features + step * HEAD_BLOCK + pair * LANES)
        grad_ref[:, k_lanes] = (grad_k * SCALE).astype(BF16)
        grad_ref[:, v_lanes] = grad_v.astype(BF16)

    @pl.when(step == pl.num_programs(0) - 1)
    def _():
        stack.wait(0, 1, 2)
        for ref, columns in ((give_ref, slice(0, half)), (keep_ref, slice(half, features))):
            for kind in range(3):
                kind_columns = slice(kind * features + columns.start, kind * features + columns.stop)
                ref[kind] = dot_tn(grad_ref[:, kind_columns], normed_ref[...]).astype(BF16)
            ref[3] = dot_tn(mixed_ref[:, columns], branch_ref[...]).astype(BF16)
        gain_grad_ref[...] = jnp.zeros_like(gain_grad_ref)
        back_ref[...] = dot_nn(grad_ref[...], w_ref[: 3 * features])
        for span in spans(doc, ROW_BLOCK):
            norm_back_into(
                span, back_ref[span], out_ref, None, gain_grad_ref, rows_ref, gain_ref, add_ref
            )


def cross_forward_kernel(heads, shares, length_ref, rows_ref, gain_ref, memory_ref, *refs):
    sources = refs[:shares]
    q_ref, k_ref, v_ref, mixed_ref, lse_ref, out_ref = refs[shares : shares + 6]
    w_ref, normed_ref, extra_ref, p_ref, mix_ref, sems = refs[shares + 6 :]
    step = pl.program_id(0)
    (doc, features), slots = rows_ref.shape, memory_ref.shape[0]
    stack = Stack(sources, w_ref, sems, 4, heads * HEAD_DIM)

    @pl.when(step == 0)
    def _():
        stack.start()
        norm_into(normed_ref, rows_ref, gain_ref)
        out_ref[...] = rows_ref[...]
        slot = lax.broadcasted_iota(jnp.int32, (slots, LANES), 0)
        extra_ref[...] = extra_lanes(slots, slot < length_ref[0])
        stack.wait(0, 1, 2, 3)

    def weights(kind):
        start = pl.multiple_of(kind * features + step * HEAD_BLOCK, HEAD_BLOCK)
        return w_ref[pl.ds(start, HEAD_BLOCK)]

    q_ref[...] = dot_nt(normed_ref[...], weights(0)).astype(BF16)
    k_ref[...] = dot_nt(memory_ref[...], weights(1)).astype(BF16)
    v_ref[...] = dot_nt(memory_ref[...], weights(2)).astype(BF16)

    units = [
        (pair, which, span)
        for pair in range(BLOCK_HEADS // 2)
        for span in spans(doc, Q_BLOCK)
        for which in range(2)
    ]
    ones = jnp.ones((TILE_ROWS, slots), BF16)
    keys = spans(slots, FORWARD_K_BLOCK)

    def lanes_of(pair):
        return slice(pair * LANES, (pair + 1) * LANES)

    def key_side(pair, which):
        return pick(which, k_ref[:, lanes_of(pair)], extra_ref[...])

    def write(pair, which, span, top, total, mixed):
        h = 2 * pair + which
        lse_ref[0, h : h + 1, span] = top + jnp.log(total)
        mix_ref[half_rows(which)] = mixed / total
        if which == 1:
            mixed_ref[span, lanes_of(pair)] = mix_ref[...].T.astype(BF16)

    v_t = [flip(v_ref[:, lanes_of(p)]) for p in range(BLOCK_HEADS // 2)]
    q_t = [q_ref[:, lanes_of(p)].astype(F32).T * SCALE for p in range(BLOCK_HEADS // 2)]

    def begin(unit):
        pair, which, span = unit
        k_of = key_side(pair, which)
        s = dot_nn(k_of[keys[0]], with_extra(which, q_t[pair][:, span], True, None))
        top = jnp.max(s, axis=0, keepdims=True)
        return k_of, s, top, with_extra(which, q_t[pair][:, span], True, top)

    worst = jnp.zeros((1, Q_BLOCK), F32)
    ahead = begin(units[0])
    for i, (pair, which, span) in enumerate(units):
        (k_of, s, top, q_with), slot = ahead, i % 2
        p_ref[slot, keys[0]] = jnp.exp(s - top).astype(BF16)
        for rows in keys[1:]:
            p_ref[slot, rows] = jnp.exp(dot_nn(k_of[rows], q_with)).astype(BF16)
        if i + 1 < len(units):
            ahead = begin(units[i + 1])
        value_side = jnp.concatenate([v_t[pair][half_rows(which)], ones], axis=0)
        mixed = dot_nn(value_side, p_ref[slot])
        total = mixed[HEAD_DIM : HEAD_DIM + 1]
        worst = jnp.maximum(worst, total)
        write(pair, which, span, top, total, mixed[:HEAD_DIM])

    @pl.when(jnp.max(worst) > LARGEST_SUM)
    def _():
        for pair, which, span in units:
            q_with = with_extra(
                which, q_ref[:, lanes_of(pair)].astype(F32).T[:, span] * SCALE, True, None
            )
            k_of = key_side(pair, which)
            s = [dot_nn(k_of[rows], q_with) for rows in keys]
            top = functools.reduce(jnp.maximum, [jnp.max(c, axis=0, keepdims=True) for c in s])
            total = jnp.zeros_like(top)
            for rows, chunk in zip(keys, s):
                p = jnp.exp(chunk - top)
                total = total + jnp.sum(p, axis=0, keepdims=True)
                p_ref[0, rows] = p.astype(BF16)
            mixed = dot_nn(flip(v_ref[:, lanes_of(pair)])[half_rows(which)], p_ref[0])
            write(pair, which, span, top, total, mixed)

    out_ref[...] += dot_nn(mixed_ref[...], weights(3))


def cross_backward_kernel(heads, shares, size, scattered, length_ref, *refs):
    gain_ref, branch_ref, q_ref, mixed_ref, lse_ref = refs[:5]
    rows_in, memory_in, add_in, k_in, v_in = refs[5:10]
    sources = refs[10 : 10 + shares]
    count = shares // 2
    refs = refs[10 + shares :]
    wide_in, narrow_in, refs = refs[:count], refs[count : 2 * count], refs[2 * count :]
    loads_first = []
    if scattered:
        (wide_out, narrow_out), refs = refs[:2], refs[2:]
        (wide_part, wide_slots, wide_done, wide_came), refs = refs[-14:-10], refs[:-14] + refs[-10:]
        (narrow_part, narrow_far, narrow_slots, narrow_done), refs = (
            refs[-10:-6],
            refs[:-10] + refs[-6:],
        )
        (wide_send, wide_recv, narrow_send, narrow_recv, part_sems, done_sems), refs = (
            refs[-6:],
            refs[:-6],
        )
        wide = Scatter(size, wide_part, wide_slots, wide_done, wide_send, wide_recv)
        narrow = Scatter(size, narrow_part, narrow_slots, narrow_done, narrow_send, narrow_recv)
        loads_first = [
            pltpu.make_async_copy(source, target, part_sems.at[i])
            for i, (source, target) in enumerate(
                [*zip(wide_in, [wide_part.at[i] for i in range(count)])]
                + [(narrow_in[0], narrow_part.at[0])]
            )
        ]
        for copy in loads_first:
            copy.start()
        hop_pairs = [(source, narrow_far) for source in narrow_in[1:]]
    else:
        hop_pairs = [*zip((*wide_in[1:], *narrow_in[1:]), refs)]
        refs = refs[len(hop_pairs) :]
    sums, refs = refs[:count], refs[count:]
    memory_out, out_ref, low_ref, gain_grad_ref = refs[:4]
    rows_ref, memory_ref, add_ref, k_ref, v_ref = refs[4:9]
    (
        w_ref,
        normed_ref,
        extra_ref,
        g_ref,
        grad_q_ref,
        grad_ref,
        ds_ref,
        give_ref,
        keep_ref,
        came_ref,
        memory_grad_ref,
        back_ref,
        sems,
        load_sems,
        key_sems,
        out_sems,
        swap_sems,
        hop_sems,
    ) = refs[9:]
    (doc, features), slots = rows_ref.shape, memory_ref.shape[0]
    half, blocks = features // 2, features // HEAD_BLOCK
    stack = Stack(sources, w_ref, sems, 4, heads * HEAD_DIM)
    loads = [
        pltpu.make_async_copy(source, target, load_sems.at[i])
        for i, (source, target) in enumerate(
            ((memory_in, memory_ref), (rows_in, rows_ref), (add_in, add_ref))
        )
    ]

    def key_copies(b):
        lanes = pl.ds(pl.multiple_of(b * HEAD_BLOCK, HEAD_BLOCK), HEAD_BLOCK)
        return [
            pltpu.make_async_copy(source.at[:, lanes], target.at[b], key_sems.at[i, b])
            for i, (source, target) in enumerate(((k_in, k_ref), (v_in, v_ref)))
        ]

    stack.start()
    for b in range(blocks):
        for copy in key_copies(b):
            copy.start()
    for copy in loads:
        copy.start()
    greet([1, 2][:count], [way[1] for way in ring_ways(size)] if scattered else [])
    hops = [
        to_differing(2, source, target, hop_sems.at[i])
        for i, (source, target) in enumerate(hop_pairs)
    ]
    for hop in hops:
        hop.start()
    if scattered:
        for copy in loads_first:
            copy.wait()
        wide.begin()
    slot = lax.broadcasted_iota(jnp.int32, (slots, LANES), 0)
    extra_ref[...] = extra_lanes(slots, slot < length_ref[0])
    none = jnp.zeros((doc, LANES), BF16)
    stack.wait(3)

    def one_block(step, carry):
        start = pl.multiple_of(3 * features + step * HEAD_BLOCK, HEAD_BLOCK)
        g_ref[...] = dot_nt(branch_ref[...], w_ref[pl.ds(start, HEAD_BLOCK)]).astype(BF16)
        for copy in key_copies(step):
            copy.wait()
        for pair in range(BLOCK_HEADS // 2):
            local = slice(pair * LANES, (pair + 1) * LANES)
            lanes = lane_block(step * HEAD_BLOCK + pair * LANES)
            v_lanes = lane_block(features + step * HEAD_BLOCK + pair * LANES)
            q, g = q_ref[:, lanes], g_ref[:, local]
            q_t, g_t = q.astype(F32).T * SCALE, g.astype(F32).T
            inner = g_t * mixed_ref[:, lanes].astype(F32).T
            per_head = []
            for which in range(2):
                h = 2 * pair + which
                minus = jnp.sum(inner[half_rows(which)], axis=0, keepdims=True)
                per_head.append(
                    (
                        with_extra(which, q_t, True, lse_ref[step, h : h + 1, :]),
                        with_extra(which, g_t, False, minus),
                        pick(which, q, none),
                        pick(which, g, none),
                    )
                )
            for rows in spans(slots, K_BLOCK):
                k, v, extra = k_ref[step, rows, local], v_ref[step, rows, local], extra_ref[rows]
                part_k = part_v = None
                for which, (q_with, g_with, q_of, g_of) in enumerate(per_head):
                    p = jnp.exp(dot_nn(pick(which, k, extra), q_with))
                    ds = (p * dot_nn(pick(which, v, extra), g_with)).astype(BF16)
                    ds_ref[which, rows] = ds
                    to_v = dot_nn(p.astype(BF16), g_of)
                    to_k = dot_nn(ds, q_of)
                    part_v = to_v if part_v is None else part_v + to_v
                    part_k = to_k if part_k is None else part_k + to_k
                grad_ref[rows, lanes] = (part_k * SCALE).astype(BF16)
                grad_ref[rows, v_lanes] = part_v.astype(BF16)
            k_t = flip(k_ref[step, :, local])
            grad_q = [dot_nn(k_t[half_rows(which)], ds_ref[which]) for which in range(2)]
            grad_q_ref[:, lanes] = (jnp.concatenate(grad_q, axis=0) * SCALE).T.astype(BF16)
            if scattered:
                ring_step(1 + step * (BLOCK_HEADS // 2) + pair)
        return carry

    places = blocks * (BLOCK_HEADS // 2)

    def ring_step(step):
        if size - 2 >= places:
            wide.advance(step)
        elif size > 2:

            @pl.when(step <= size - 2)
            def _():
                wide.advance(step)

    lax.fori_loop(0, blocks, one_block, 0)
    if scattered:

        def rest(step, carry):
            wide.advance(step)
            return carry

        lax.fori_loop(min(places, size - 2) + 1, size - 1, rest, 0)
        wide.turn()
        done_hops = [
            to_differing(2, wide_done.at[:, i], wide_came, done_sems) for i in range(1, count)
        ]
        for hop in done_hops:
            hop.start()
        for hop in hops:
            hop.wait_recv()
        if hops:
            narrow_part[0] = low_sum(narrow_part[0], narrow_far[...])
        narrow.begin()

    def narrow_step(step):
        if scattered and step <= size - 2:
            narrow.advance(step)

    for copy in loads:
        copy.wait()
    norm_into(normed_ref, rows_ref, gain_ref)

    def weight_grads(ref, first, ring_at):
        columns = slice(first, first + half)
        v_columns = slice(features + first, features + first + half)
        ref[0] = dot_tn(grad_q_ref[:, columns], normed_ref[...]).astype(BF16)
        ref[1] = dot_tn(grad_ref[:, columns], memory_ref[...]).astype(BF16)
        narrow_step(ring_at)
        ref[2] = dot_tn(grad_ref[:, v_columns], memory_ref[...]).astype(BF16)
        ref[3] = dot_tn(mixed_ref[:, columns], branch_ref[...]).astype(BF16)

    weight_grads(give_ref, 0, 1)
    swap = to_differing(1, give_ref, came_ref, swap_sems)
    swap.start()
    stack.wait(0, 1, 2)
    writes = []
    for i, rows in enumerate(spans(slots, MEMORY_BLOCK)):
        memory_grad_ref[rows] = dot_nn(
            grad_ref[rows], w_ref[features : 3 * features]
        ).astype(BF16)
        writes.append(
            pltpu.make_async_copy(memory_grad_ref.at[rows], memory_out.at[rows], out_sems.at[i])
        )
        writes[-1].start()
        narrow_step(2 + i)
    weight_grads(keep_ref, half, 4)
    narrow_step(5)
    gain_grad_ref[...] = jnp.zeros_like(gain_grad_ref)
    back_ref[...] = dot_nn(grad_q_ref[...], w_ref[:features])
    narrow_step(6)
    for span in spans(doc, ROW_BLOCK):
        norm_back_into(
            span, back_ref[span], out_ref, low_ref, gain_grad_ref, rows_ref, gain_ref, add_ref
        )
    swap.wait_recv()
    rows = half // count
    for share, sums_ref in enumerate(sums):
        for kind in range(4):
            span = slice(share * rows, (share + 1) * rows)
            to = slice(kind * rows, (kind + 1) * rows)
            sums_ref[to] = low_sum(keep_ref[kind, span], came_ref[kind, span])
    swap.wait_send()
    for copy in writes:
        copy.wait()
    if not scattered:
        for hop in hops:
            hop.wait()
        return

    def last_steps(step, carry):
        narrow.advance(step)
        return carry

    lax.fori_loop(7, size - 1, last_steps, 0)
    for hop in done_hops:
        hop.wait()
    own = wide_done[:, 0]
    wide_out[...] = low_sum(own, wide_came[...]) if done_hops else own
    narrow.turn()
    narrow_out[...] = narrow_done[:, 0]
    for hop in hops:
        hop.wait_send()
    wide.wait_sent()
    narrow.wait_sent()


def feed_forward_kernel(first, last, rows_ref, gain_ref, cotangent_ref, *refs):
    sources, refs = refs[:2], refs[2:]
    if not first:
        before_in, refs = refs[:2], refs[2:]
    sums, layer_ref, out_ref = refs[:2], refs[2], refs[3]
    if last:
        low_ref, gain_grad_ref = refs[4:6]
        refs = refs[2:]
    (
        wide_ref,
        narrow_ref,
        normed_ref,
        normed_t,
        cotangent_t,
        active_ref,
        grad_ref,
        give_ref,
        keep_ref,
        came_ref,
        layer_in_ref,
        back_in_ref,
        product_ref,
        sems,
        before_sems,
        swap_sems,
    ) = refs[4:]
    step, steps = pl.program_id(0), pl.num_programs(0)
    half = steps // 2
    doc = rows_ref.shape[0]
    hidden = sources[0].shape[0] // 2
    copies = [
        [
            pltpu.make_async_copy(
                source.at[pl.ds(kind * hidden, hidden)],
                stack.at[pl.ds(p * hidden, hidden)],
                sems.at[p, kind],
            )
            for kind, stack in enumerate((wide_ref, narrow_ref))
        ]
        for p, source in enumerate(sources)
    ]
    loads = []
    if not first:
        loads = [
            pltpu.make_async_copy(source, target, before_sems.at[i])
            for i, (source, target) in enumerate(zip(before_in, (layer_in_ref, back_in_ref)))
        ]
    swap = to_differing(1, give_ref, came_ref, swap_sems)

    @pl.when(step == 0)
    def _():
        for pair in copies:
            for copy in pair:
                copy.start()
        for copy in loads:
            copy.start()
        greet([1])
        norm_into(normed_ref, rows_ref, gain_ref)
        for span in spans(doc, ROW_BLOCK):
            normed_t[:, span] = flip(normed_ref[span])
            cotangent_t[:, span] = flip(cotangent_ref[span])

    for p, pair in enumerate(copies):

        @pl.when(step == p * half)
        def _(pair=pair):
            for copy in pair:
                copy.wait()

    units = pl.ds(pl.multiple_of(step * HIDDEN_BLOCK, HIDDEN_BLOCK), HIDDEN_BLOCK)
    activated, slope = gelu_and_slope(dot_nn(wide_ref[units], normed_t[...]))
    active_ref[units] = activated.astype(BF16)
    grad_ref[units] = (dot_nn(narrow_ref[units], cotangent_t[...]) * slope).astype(BF16)

    def store(ref, at):
        rows = pl.ds(pl.multiple_of(at * HIDDEN_BLOCK, HIDDEN_BLOCK), HIDDEN_BLOCK)
        ref[0, rows] = dot_nn(grad_ref[units], normed_ref[...]).astype(BF16)
        ref[1, rows] = dot_nn(active_ref[units], cotangent_ref[...]).astype(BF16)

    @pl.when(step < half)
    def _():
        store(give_ref, step)

    @pl.when(step == half - 1)
    def _():
        swap.start()

    @pl.when(step >= half)
    def _():
        store(keep_ref, step - half)

    @pl.when(step == steps - 1)
    def _():
        for copy in loads:
            copy.wait()
        if last:
            gain_grad_ref[...] = jnp.zeros_like(gain_grad_ref)
        product_ref[...] = dot_tn(active_ref[...], narrow_ref[...])
        for span in spans(doc, ROW_BLOCK):
            layer = rows_ref[span] if first else layer_in_ref[span]
            layer_ref[span] = (layer + product_ref[span]).astype(layer_ref.dtype)
        product_ref[...] = dot_tn(grad_ref[...], wide_ref[...])
        for span in spans(doc, ROW_BLOCK):
            back = product_ref[span]
            if not first:
                back = back + back_in_ref[span]
            if last:
                norm_back_into(
                    span, back, out_ref, low_ref, gain_grad_ref, rows_ref, gain_ref, cotangent_ref
                )
            else:
                out_ref[span] = back
        swap.wait_recv()
        for kind, sums_ref in enumerate(sums):
            for span in spans(hidden, HIDDEN_BLOCK):
                sums_ref[span] = low_sum(keep_ref[kind, span], came_ref[kind, span])
        swap.wait_send()


def pack_kernel(flipped, *refs):
    out_ref, start = refs[-1], 0
    for source, turn in zip(refs[:-1], flipped):
        if source.shape[-1] != out_ref.shape[1] and not turn:
            out_ref[start:] = jnp.zeros((TABLE_ROWS, out_ref.shape[1]), BF16)
            out_ref[start : start + source.shape[0], : source.shape[1]] = source[...]
            continue
        rows = source.shape[1] if turn else source.shape[0]
        span = slice(start, start + rows)
        out_ref[span] = flip(source[...]) if turn else source[...]
        start += rows


def finish_kernel(*refs):
    sources, passed, outs, through, refs = refs[:4], refs[4:6], refs[6:16], refs[16:18], refs[18:]
    ins, wides, in_sems, out_sems, pass_sems = refs[:4], refs[4:14], refs[14], refs[15], refs[16]
    loads, writes = [], []
    passes = [
        pltpu.make_async_copy(source, target, pass_sems.at[i])
        for i, (source, target) in enumerate(zip(passed, through))
    ]
    for i, (source, target) in enumerate(zip(sources, ins)):
        for j, span in enumerate(spans(target.shape[0], FINISH_BLOCK)):
            loads.append(
                pltpu.make_async_copy(source.at[span], target.at[span], in_sems.at[i, j])
            )
            loads[-1].start()

    for copy in passes:
        copy.start()

    def write(i, part):
        writes.append(
            pltpu.make_async_copy(wides[i].at[part], outs[i].at[part], out_sems.at[len(writes)])
        )
        writes[-1].start()

    waiting = iter(loads)
    hidden = wides[1].shape[0]
    for span in spans(hidden, FINISH_BLOCK):
        next(waiting).wait()
        for part in spans(FINISH_BLOCK, LANES):
            rows = slice(span.start + part.start, span.start + part.stop)
            wides[0][:, rows] = ins[0][rows].astype(F32).T
        write(0, (slice(None), span))
    for span in spans(hidden, FINISH_BLOCK):
        next(waiting).wait()
        wides[1][span] = ins[1][span].astype(F32)
        write(1, span)
    for i in (2, 3):
        for _ in spans(ins[i].shape[0], FINISH_BLOCK):
            next(waiting).wait()
        rows = wides[2].shape[0]
        for kind in range(4):
            at = 2 + 4 * (i - 2) + kind
            wides[at][...] = ins[i][kind * rows : (kind + 1) * rows].astype(F32)
            write(at, slice(None))
    for copy in writes + passes:
        copy.wait()


def params():
    return pltpu.CompilerParams(vmem_limit_bytes=VMEM_BYTES)


def cost(flops=1 << 20):
    return pl.CostEstimate(flops=flops, bytes_accessed=1 << 16, transcendentals=0)


def shape(dims, dtype):
    return jax.ShapeDtypeStruct(dims, dtype)


def whole(array):
    return pl.BlockSpec(
        array.shape, lambda *_: (0,) * len(array.shape), pipeline_mode=pl.Buffered(1)
    )


def result(array):
    return pl.BlockSpec(array.shape, lambda *_: (0,) * len(array.shape))


def columns(rows):
    return pl.BlockSpec((rows, HEAD_BLOCK), lambda i: (0, i))


def anywhere(arrays):
    return [pl.BlockSpec(memory_space=pl.ANY) for _ in arrays]


SCALAR = pl.BlockSpec(memory_space=pltpu.SMEM)


def call(
    kernel, name, grid, in_specs, out_specs, out_shape, scratch, args, channel=None, flops=1 << 20
):
    compiler_params = params()
    if channel is not None:
        compiler_params = pltpu.CompilerParams(
            vmem_limit_bytes=VMEM_BYTES, collective_id=channel, has_side_effects=True
        )
    return pl.pallas_call(
        kernel,
        grid=grid,
        in_specs=in_specs,
        out_specs=out_specs,
        out_shape=out_shape,
        scratch_shapes=scratch,
        compiler_params=compiler_params,
        cost_estimate=cost(flops),
        name=name,
    )(*args)


def pack(*parts):
    arrays, flipped = zip(*parts)
    features = arrays[0].shape[0] if flipped[0] else arrays[0].shape[1]
    rows = [a.shape[1] if turn else a.shape[0] for a, turn in parts]
    if arrays[-1].shape[1] < features and not flipped[-1]:
        rows[-1] = TABLE_ROWS
    rows = sum(rows)
    return pl.pallas_call(
        functools.partial(pack_kernel, flipped),
        out_shape=shape((rows, features), BF16),
        compiler_params=params(),
        cost_estimate=cost(),
        name="pack",
    )(*arrays)


def self_forward(heads, buckets, rows, gain, weights, ids):
    doc, features = rows.shape
    shares, steps = len(weights), features // HEAD_BLOCK
    narrow, tall = shape((doc, features), BF16), shape((doc, features), F32)
    out_shape = (*[narrow] * 4, shape((steps, 8, doc), F32), tall)
    return call(
        functools.partial(self_forward_kernel, heads, buckets, shares),
        "self_forward",
        (steps,),
        [whole(rows), whole(gain), whole(ids), *anywhere(weights)],
        (*[columns(doc)] * 4, pl.BlockSpec((1, 8, doc), lambda i: (i, 0, 0)), result(tall)),
        out_shape,
        [
            pltpu.VMEM((4 * features, features), BF16),
            pltpu.VMEM((shares, TABLE_ROWS, features), BF16),
            pltpu.VMEM((TABLE_ROWS, LANES), F32),
            pltpu.VMEM((doc, features), BF16),
            pltpu.SemaphoreType.DMA((shares, 5)),
        ],
        (rows, gain, ids, *weights),
    )


def self_backward(heads, buckets, rows, gain, ids, branch, add, saved, weights):
    doc, features = rows.shape
    shares, steps = len(weights), features // HEAD_BLOCK
    packed = shape((4, features // 2, features), BF16)
    out_shape = (
        packed,
        packed,
        shape((steps * BLOCK_HEADS, doc, doc), BF16),
        shape((doc, features), F32),
        shape((8, features), F32),
    )
    *arrays, lse = saved
    return call(
        functools.partial(self_backward_kernel, heads, buckets, shares),
        "self_backward",
        (steps,),
        [
            *[whole(a) for a in (rows, gain, ids, branch, add, *arrays)],
            pl.BlockSpec((1, 8, doc), lambda i: (i, 0, 0)),
            *anywhere(weights),
        ],
        (
            result(packed),
            result(packed),
            pl.BlockSpec((BLOCK_HEADS, doc, doc), lambda i: (i, 0, 0)),
            result(out_shape[3]),
            result(out_shape[4]),
        ),
        out_shape,
        [
            pltpu.VMEM((4 * features, features), BF16),
            pltpu.VMEM((shares, TABLE_ROWS, features), BF16),
            pltpu.VMEM((TABLE_ROWS, LANES), F32),
            pltpu.VMEM((doc, features), BF16),
            pltpu.VMEM((doc, HEAD_BLOCK), BF16),
            pltpu.VMEM((doc, 3 * features), BF16),
            pltpu.VMEM((doc, features), F32),
            pltpu.SemaphoreType.DMA((shares, 5)),
        ],
        (rows, gain, ids, branch, add, *arrays, lse, *weights),
    )


def cross_forward(heads, rows, gain, memory, length, weights):
    (doc, features), slots = rows.shape, memory.shape[0]
    shares, steps = len(weights), features // HEAD_BLOCK
    query, key = shape((doc, features), BF16), shape((slots, features), BF16)
    tall = shape((doc, features), F32)
    return call(
        functools.partial(cross_forward_kernel, heads, shares),
        "cross_forward",
        (steps,),
        [SCALAR, whole(rows), whole(gain), whole(memory), *anywhere(weights)],
        (
            columns(doc),
            columns(slots),
            columns(slots),
            columns(doc),
            pl.BlockSpec((1, 8, doc), lambda i: (i, 0, 0)),
            result(tall),
        ),
        (query, key, key, query, shape((steps, 8, doc), F32), tall),
        [
            pltpu.VMEM((4 * features, features), BF16),
            pltpu.VMEM((doc, features), BF16),
            pltpu.VMEM((slots, LANES), BF16),
            pltpu.VMEM((2, slots, Q_BLOCK), BF16),
            pltpu.VMEM((LANES, Q_BLOCK), F32),
            pltpu.SemaphoreType.DMA((shares, 4)),
        ],
        (length, rows, gain, memory, *weights),
    )


def cross_backward(
    heads, size, rows, gain, memory, length, branch, add, saved, weights, wide, narrow, scattered
):
    (doc, features), slots = rows.shape, memory.shape[0]
    shares, blocks = len(weights), features // HEAD_BLOCK
    count = shares // 2
    part = wide[0].shape
    far_out, ring_scratch = [shape(part, BF16)] * (2 * (count - 1)), []
    if scattered:
        block = (2, part[0] // (2 * size), features)
        far_out = [shape(block, BF16)] * 2
        steps = pltpu.SemaphoreType.DMA((2, size - 1))
        ring_scratch = [
            pltpu.VMEM((count, *part), BF16),
            pltpu.VMEM((2, size - 1, count, *block[1:]), BF16),
            pltpu.VMEM((2, count, *block[1:]), BF16),
            pltpu.VMEM(block, BF16),
            pltpu.VMEM((1, *part), BF16),
            pltpu.VMEM(part, BF16),
            pltpu.VMEM((2, size - 1, 1, *block[1:]), BF16),
            pltpu.VMEM((2, 1, *block[1:]), BF16),
            *[steps] * 4,
            pltpu.SemaphoreType.DMA((count + 1,)),
            pltpu.SemaphoreType.DMA((2,)),
        ]
    out_shape = (
        *far_out,
        *[shape((4 * heads * HEAD_DIM, features), BF16)] * count,
        shape((slots, features), BF16),
        shape((doc, features), F32),
        shape((doc, features), BF16),
        shape((8, features), F32),
    )
    query, key, value, mixed, lse = saved
    near = (gain, branch, query, mixed, lse)
    far = (rows, memory, add, key, value, *weights, *wide, *narrow)
    vmem, hbm = pl.BlockSpec(memory_space=pltpu.VMEM), pl.BlockSpec(memory_space=pl.ANY)
    packed = pltpu.VMEM((4, features // 2, features), BF16)
    key_block = pltpu.VMEM((blocks, slots, HEAD_BLOCK), BF16)
    return call(
        functools.partial(cross_backward_kernel, heads, shares, size, scattered),
        "cross_backward",
        (),
        [SCALAR, *[vmem for _ in near], *[hbm for _ in far]],
        (
            *[vmem if scattered else hbm for _ in far_out],
            *[vmem] * count,
            hbm,
            vmem,
            vmem,
            vmem,
        ),
        out_shape,
        [
            pltpu.VMEM((doc, features), F32),
            pltpu.VMEM((slots, features), BF16),
            pltpu.VMEM((doc, features), F32),
            key_block,
            key_block,
            pltpu.VMEM((4 * features, features), BF16),
            pltpu.VMEM((doc, features), BF16),
            pltpu.VMEM((slots, LANES), BF16),
            pltpu.VMEM((doc, HEAD_BLOCK), BF16),
            pltpu.VMEM((doc, features), BF16),
            pltpu.VMEM((slots, 2 * features), BF16),
            pltpu.VMEM((2, slots, doc), BF16),
            packed,
            packed,
            packed,
            pltpu.VMEM((slots, features), BF16),
            pltpu.VMEM((doc, features), F32),
            pltpu.SemaphoreType.DMA((shares, 4)),
            pltpu.SemaphoreType.DMA((3,)),
            pltpu.SemaphoreType.DMA((2, blocks)),
            pltpu.SemaphoreType.DMA((slots // MEMORY_BLOCK,)),
            pltpu.SemaphoreType.DMA((2,)),
            pltpu.SemaphoreType.DMA((2, 2)),
            *ring_scratch,
        ],
        (length, *near, *far),
        channel=1,
    )


def feed_forward(rows, gain, cotangent, weights, before, last):
    (doc, features), shares = rows.shape, len(weights)
    share = weights[0].shape[0] // 2
    hidden = share * shares
    steps = hidden // HIDDEN_BLOCK
    summed, tall = shape((share, features), BF16), shape((doc, features), F32)
    low = shape((doc, features), BF16)
    rest = [low, tall, low, shape((8, features), F32)] if last else [tall, tall]
    kept, added = pltpu.VMEM((2, share, features), BF16), pltpu.VMEM(tall.shape, F32)
    return call(
        functools.partial(feed_forward_kernel, not before, last),
        "feed_forward",
        (steps,),
        [whole(rows), whole(gain), whole(cotangent), *anywhere(weights), *anywhere(before)],
        (result(summed), result(summed), *[result(o) for o in rest]),
        (summed, summed, *rest),
        [
            pltpu.VMEM((hidden, features), BF16),
            pltpu.VMEM((hidden, features), BF16),
            pltpu.VMEM((doc, features), BF16),
            pltpu.VMEM((features, doc), BF16),
            pltpu.VMEM((features, doc), BF16),
            pltpu.VMEM((hidden, doc), BF16),
            pltpu.VMEM((hidden, doc), BF16),
            kept,
            kept,
            kept,
            added,
            added,
            added,
            pltpu.SemaphoreType.DMA((shares, 2)),
            pltpu.SemaphoreType.DMA((2,)),
            pltpu.SemaphoreType.DMA((2,)),
        ],
        (rows, gain, cotangent, *weights, *before),
        channel=3 if before else 2,
    )


def finish(sum_wide, sum_narrow, sum_cross, sum_self, *passed):
    rows, features = sum_self.shape
    hidden, part = sum_wide.shape[0], shape((rows // 4, features), F32)
    out_shape = [shape((features, hidden), F32), shape((hidden, features), F32), *[part] * 8]
    sources = (sum_wide, sum_narrow, sum_cross, sum_self)
    writes = 2 * hidden // FINISH_BLOCK + 8
    passed_shape = [shape(a.shape, a.dtype) for a in passed]
    wide, narrow, *parts = pl.pallas_call(
        finish_kernel,
        in_specs=anywhere(sources + passed),
        out_specs=anywhere(out_shape + passed_shape),
        out_shape=out_shape + passed_shape,
        scratch_shapes=[
            *[pltpu.VMEM(source.shape, BF16) for source in sources],
            *[pltpu.VMEM(out.shape, F32) for out in out_shape],
            pltpu.SemaphoreType.DMA((4, hidden // FINISH_BLOCK)),
            pltpu.SemaphoreType.DMA((writes,)),
            pltpu.SemaphoreType.DMA((2,)),
        ],
        compiler_params=params(),
        cost_estimate=cost(),
        name="finish",
    )(*sources, *passed)
    return wide, narrow, parts[4:8], parts[:4], parts[8:]


def share_place(row, other, peers):
    j, bit = 0, 1
    while bit < peers:
        j = j + bit * ((row // bit + other // bit) % 2)
        bit *= 2
    return (j % 2) * (j // 2) + (1 - j % 2) * (peers // 2 + j // 2)


def tail_kernel(size, peers, buckets, heads, gathered, counts, *refs):
    parts = []
    for count in counts:
        parts.append(refs[:count])
        refs = refs[count:]
    arrays = len(counts) + 1
    give_ref, keep_ref, ids_ref, ds_ref, *gain_refs = refs[:7]
    outs, small_out_ref, refs = refs[7 : 7 + arrays], refs[7 + arrays], refs[8 + arrays :]
    slots, refs = refs[:arrays], refs[arrays:]
    firsts, refs = refs[:arrays], refs[arrays:]
    kept_ref, came_ref, folded_ref, far_came_ref, part_ref, scores_ref, bucket_ref = refs[:7]
    small_ref, near_ref, far_ref = refs[7:10]
    send, came, send_out, came_out, small_sems, hop_sems, local_sems = refs[10:]
    parts.append((part_ref,))
    me, row = lax.axis_index("dp"), lax.axis_index("mp")
    ways = ring_ways(size)
    doc = ids_ref.shape[0]
    mesh = pl.DeviceIdType.MESH

    load_scores = pltpu.make_async_copy(ds_ref, scores_ref, local_sems.at[0])
    load_kept = pltpu.make_async_copy(keep_ref, kept_ref, local_sems.at[1])
    load_scores.start()
    load_kept.start()

    barrier = pltpu.get_barrier_semaphore()

    def greet(t, carry):
        pl.semaphore_signal(
            barrier, inc=1, device_id=((me + t) % size, row), device_id_type=mesh
        )
        return carry

    lax.fori_loop(1, size, greet, 0)
    for t in range(1, peers):
        pl.semaphore_signal(
            barrier, inc=1, device_id=(me, (row + t) % peers), device_id_type=mesh
        )
    pl.semaphore_wait(barrier, size - 1 + peers - 1)

    def block(i, way, number):
        rows = outs[i].shape[0] // (2 * size)
        return pl.ds(pl.multiple_of((way * size + number) * rows, 16), rows)

    def part(i, span):
        total = parts[i][0][span].astype(F32)
        for ref in parts[i][1:]:
            total = total + ref[span].astype(F32)
        return total

    def first_copy(i, way):
        return remote(
            firsts[i].at[way],
            slots[i].at[way, 0],
            send.at[i, way, 0],
            came.at[i, way, 0],
            (ways[way][1], row),
        )

    def next_copy(i, way, step):
        return remote(
            slots[i].at[way, step - 1],
            slots[i].at[way, step],
            send.at[i, way, step],
            came.at[i, way, step],
            (ways[way][1], row),
        )

    def wait_came(i, way, step):
        remote(
            slots[i].at[way, step],
            slots[i].at[way, step],
            send.at[i, way, step],
            came.at[i, way, step],
            (ways[way][1], row),
        ).wait_recv()

    def out_copy(i, way, step):
        span = block(i, way, (ways[way][0] + 1 - step + size) % size)
        return remote(
            outs[i].at[span],
            outs[i].at[span],
            send_out.at[i, way, step],
            came_out.at[i, way, step],
            (ways[way][1], row),
        )

    def begin(rings):
        for i, way in rings:
            firsts[i][way] = part(i, block(i, way, ways[way][0])).astype(BF16)
            first_copy(i, way).start()

    def plus_part(i, way, step):
        span = block(i, way, (ways[way][0] - step - 1 + size) % size)
        total = slots[i][way, step].astype(F32) + part(i, span)
        return span, total.astype(BF16)

    def advance(rings, step):
        for i, way in rings:
            wait_came(i, way, step - 1)
            slots[i][way, step - 1] = plus_part(i, way, step - 1)[1]
            next_copy(i, way, step).start()

    def turn(rings):
        for i, way in rings:
            wait_came(i, way, size - 2)
            span, total = plus_part(i, way, size - 2)
            outs[i][span] = total
            out_copy(i, way, 0).start()

    def pass_on(rings, step):
        for i, way in rings:
            out_copy(i, way, step - 1).wait_recv()
            out_copy(i, way, step).start()

    ready = [(i, way) for i in range(gathered) for way in range(2)]
    early = [(i, way) for i in range(gathered, arrays - 1) for way in range(2)]
    late = [(arrays - 1, way) for way in range(2)]

    other_core = remote(
        give_ref, came_ref, hop_sems.at[0, 0], hop_sems.at[0, 1], (me, differing(row, 1))
    )
    other_core.start()
    begin(early)
    for i, way in ready:
        outs[i][block(i, way, (ways[way][0] + 1) % size)] = parts[i][0][way]
        out_copy(i, way, 0).start()

    rows_used, per_row = bucket_ref.shape[0], ds_ref.shape[0] // bucket_ref.shape[0]
    units = rows_used * buckets
    per_round = -(-units // max(2 * (size - 2), 1))

    def bucket_unit(u, carry):
        r, b = u // buckets, u % buckets
        sums = [jnp.zeros((8, LANES), F32) for _ in range(per_row)]
        for c in range(0, doc, LANES):
            hit = ids_ref[: c + LANES, c : c + LANES] == b
            for h in range(per_row):
                grads = scores_ref[r * per_row + h, : c + LANES, c : c + LANES].astype(F32)
                kept = jnp.where(hit, grads, 0.0).reshape(-1, 8, LANES)
                sums[h] = sums[h] + jnp.sum(kept, axis=0)
        for h in range(per_row):
            bucket_ref[r, h, pl.ds(b, 1), :] = jnp.sum(sums[h], axis=0, keepdims=True)
        return carry

    def bucket_round(k):
        low = jnp.minimum(k * per_round, units)
        lax.fori_loop(low, jnp.minimum(low + per_round, units), bucket_unit, 0)

    bucket_ref[...] = jnp.zeros_like(bucket_ref)
    part_ref[...] = jnp.zeros_like(part_ref)
    load_scores.wait()

    def early_step(step, carry):
        advance(early, step)
        pass_on(ready, step)
        bucket_round(step - 1)
        return carry

    middle = min(2, size - 1)
    lax.fori_loop(1, middle, early_step, 0)

    load_kept.wait()
    other_core.wait_recv()
    kinds, count = kept_ref.shape[0], folded_ref.shape[0]
    rows = kept_ref.shape[1] // count

    def fold(index, target, span_of):
        span = slice(index * rows, (index + 1) * rows)
        for kind in range(kinds):
            total = kept_ref[kind, span].astype(F32) + came_ref[kind, span].astype(F32)
            target[span_of(kind)] = total.astype(BF16)

    def kind_rows(kind):
        return slice(kind * rows, (kind + 1) * rows)

    other_chip = None
    if count == 2:
        fold(1, folded_ref.at[1], kind_rows)
        other_chip = remote(
            folded_ref.at[1],
            far_came_ref,
            hop_sems.at[1, 0],
            hop_sems.at[1, 1],
            (me, differing(row, 2)),
        )
        other_chip.start()
    fold(0, folded_ref.at[0], kind_rows)

    begin_late = LATE_STEP if size - 1 > LATE_STEP else size - 1
    lax.fori_loop(middle, min(begin_late + 1, size - 1), early_step, 0)
    if begin_late == size - 1:
        turn(early)
    used = slice(0, kinds * rows)
    if other_chip is None:
        part_ref[used] = folded_ref[0]
    else:
        other_chip.wait_recv()
        total = folded_ref[0].astype(F32) + far_came_ref[...].astype(F32)
        part_ref[used] = total.astype(BF16)
    begin(late)

    def both_step(step, carry):
        early_step(step, carry)
        advance(late, step - begin_late)
        return carry

    def middle_step(step, carry):
        pass_on(early, step)
        advance(late, step + size - 1 - begin_late)
        bucket_round(size - 2 + step - 1)
        return carry

    def end_step(step, carry):
        pass_on(early, step)
        pass_on(late, step - begin_late)
        bucket_round(size - 2 + step - 1)
        return carry

    if begin_late < size - 1:
        lax.fori_loop(begin_late + 1, size - 1, both_step, 0)
        turn(early)
        advance(late, size - 1 - begin_late)
        lax.fori_loop(1, begin_late, middle_step, 0)
        pass_on(early, begin_late)
        turn(late)
        bucket_round(size - 2 + begin_late - 1)
        lax.fori_loop(begin_late + 1, size - 1, end_step, 0)
    else:
        lax.fori_loop(1, size - 1, middle_step, 0)
        turn(late)
    if size == 2:
        lax.fori_loop(0, units, bucket_unit, 0)
    late_passed = size - 2 - begin_late if begin_late < size - 1 else 0

    features = gain_refs[0].shape[1]
    per_gain = features // LANES
    gain_rows = len(gain_refs) * per_gain
    small_ref[...] = jnp.zeros_like(small_ref)
    for i, ref in enumerate(gain_refs):
        total = jnp.sum(ref[...], axis=0, keepdims=True)
        for c in range(per_gain):
            at = i * per_gain + c
            small_ref[at : at + 1, :] = total[:, c * LANES : (c + 1) * LANES]
    for r in range(rows_used):
        block_sums = bucket_ref[r].reshape(LANES, LANES).T
        at = gain_rows + r
        small_ref[at : at + 1, :] = jnp.sum(block_sums, axis=0, keepdims=True)

    def near_copy(t):
        return remote(
            small_ref,
            near_ref.at[row],
            small_sems.at[0, t],
            small_sems.at[1, t],
            (me, (row + t) % peers),
        )

    def far_copy(t):
        return remote(
            far_ref.at[me],
            far_ref.at[me],
            small_sems.at[2, t],
            small_sems.at[3, t],
            ((me + t) % size, row),
        )

    for t in range(1, peers):
        near_copy(t).start()
    near_ref[pl.ds(row, 1)] = small_ref[...][None]
    for t in range(1, peers):
        near_copy(t).wait_recv()
    own = rows_used // peers
    total, sums = None, None
    for k in range(peers):
        gains = near_ref[k, :gain_rows]
        mine = near_ref[k, pl.ds(gain_rows + own * share_place(row, k, peers), own)]
        total = gains if total is None else total + gains
        sums = mine if sums is None else sums + mine
    small_ref_rows = far_ref.shape[1]
    far_ref[pl.ds(me, 1)] = jnp.concatenate(
        [total, sums, jnp.zeros((small_ref_rows - gain_rows - own, LANES), F32)], axis=0
    )[None]

    def far_start(t, carry):
        far_copy(t).start()
        return carry

    lax.fori_loop(1, size, far_start, 0)

    def late_step(step, carry):
        pass_on(late, step)
        return carry

    lax.fori_loop(1 + late_passed, size - 1, late_step, 0)

    def far_wait(t, carry):
        far_copy(t).wait()
        return carry

    lax.fori_loop(1, size, far_wait, 0)

    def far_add(k, total):
        return total + far_ref[k]

    small_out_ref[...] = lax.fori_loop(1, size, far_add, far_ref[0])
    for i, way in ready + early + late:
        out_copy(i, way, size - 2).wait_recv()

    for t in range(1, peers):
        near_copy(t).wait_send()
    other_core.wait_send()
    if other_chip is not None:
        other_chip.wait_send()
    for i, way in early + late:
        first_copy(i, way).wait_send()

    def sent(step, carry):
        for i, way in early + late:
            next_copy(i, way, step).wait_send()
        return carry

    lax.fori_loop(1, size - 1, sent, 0)

    def sent_out(step, carry):
        for i, way in ready + early + late:
            out_copy(i, way, step).wait_send()
        return carry

    lax.fori_loop(0, size - 1, sent_out, 0)


def tail_sums(size, peers, buckets, heads, blocks, terms, give, keep, ids, ds, gains):
    assert peers in (2, 4)
    grain = 2 * 16 * size
    kinds, half, features = keep.shape
    count = peers // 2
    rows = [size * 2 * b.shape[1] for b in blocks]
    rows += [arrays[0].shape[0] for arrays in terms]
    rows.append(kinds * half // count)
    padded = [r + -r % grain for r in rows]
    parts = [[b] for b in blocks]
    for arrays, r, p in zip(terms, rows[len(blocks) :], padded[len(blocks) :]):
        parts.append([jnp.pad(a, ((0, p - r), (0, 0))) for a in arrays])
    flat = [a for arrays in parts for a in arrays]
    lines = peers * (-(-heads * buckets // LANES))
    small = len(gains) * features // LANES + lines
    small = shape((small + -small % 8, LANES), F32)
    vmem, hbm = pl.BlockSpec(memory_space=pltpu.VMEM), pl.BlockSpec(memory_space=pl.ANY)
    steps = pltpu.SemaphoreType.DMA((len(rows), 2, size - 1))

    def ring_slots(i, steps):
        if i < len(blocks):
            return pltpu.VMEM((2, 1, 16, LANES), BF16)
        return pltpu.VMEM((2, *steps, padded[i] // (2 * size), features), BF16)

    *sums, small = pl.pallas_call(
        functools.partial(
            tail_kernel, size, peers, buckets, heads, len(blocks), [len(a) for a in parts]
        ),
        in_specs=[*[vmem] * len(flat), hbm, hbm, vmem, hbm, *[vmem] * len(gains)],
        out_specs=[vmem] * (len(rows) + 1),
        out_shape=[*[shape((p, features), BF16) for p in padded], small],
        scratch_shapes=[
            *[ring_slots(i, (size - 1,)) for i in range(len(rows))],
            *[ring_slots(i, ()) for i in range(len(rows))],
            pltpu.VMEM(keep.shape, BF16),
            pltpu.VMEM(keep.shape, BF16),
            pltpu.VMEM((count, rows[-1], features), BF16),
            pltpu.VMEM((rows[-1], features), BF16),
            pltpu.VMEM((padded[-1], features), BF16),
            pltpu.VMEM(ds.shape, BF16),
            pltpu.VMEM((lines, LANES // buckets, buckets, LANES), F32),
            pltpu.VMEM(small.shape, F32),
            pltpu.VMEM((peers, *small.shape), F32),
            pltpu.VMEM((size, *small.shape), F32),
            steps,
            steps,
            steps,
            steps,
            pltpu.SemaphoreType.DMA((4, max(size, peers))),
            pltpu.SemaphoreType.DMA((2, 2)),
            pltpu.SemaphoreType.DMA((2,)),
        ],
        compiler_params=pltpu.CompilerParams(
            vmem_limit_bytes=VMEM_BYTES, collective_id=0, has_side_effects=True
        ),
        cost_estimate=cost(),
        name="tail_sums",
    )(*flat, give, keep, ids, ds, *gains)
    return [total[:r] for total, r in zip(sums, rows)], small


def swap(array, bit, size):
    return lax.ppermute(array, "mp", [(i, i ^ bit) for i in range(size)])


def after(array, *others):
    return lax.optimization_barrier((array, others))[0]


def shards(
    decoder_rows,
    memory_rows,
    decoder_token_length,
    memory_length,
    bucket_ids,
    relative_bucket_bias,
    self_gain,
    self_query,
    self_key,
    self_value,
    self_out,
    cross_gain,
    cross_query,
    cross_key,
    cross_value,
    cross_out,
    hidden_gain,
    widen_weight,
    narrow_weight,
    layer_cotangent,
):
    dp_size = lax.axis_size("dp")
    mp_size = lax.axis_size("mp")
    me = lax.axis_index("mp")
    doc, features = decoder_rows.shape
    slots = memory_rows.shape[0]
    cols = self_query.shape[1]
    heads = cols // HEAD_DIM
    buckets = relative_bucket_bias.shape[0]
    order = [*range(1, mp_size, 2), *range(0, mp_size, 2)]

    doc_length = lax.dynamic_index_in_dim(decoder_token_length, me, keepdims=False)
    doc_memory = lax.dynamic_index_in_dim(memory_length, me)
    position = jnp.arange(doc, dtype=jnp.int32)
    allowed = (position[:, None] <= position[None, :]) & (position[:, None] < doc_length)
    ids = jnp.where(allowed, bucket_ids.T, buckets)
    own_self = pack(
        (self_query.T, False),
        (self_key.T, False),
        (self_value.T, False),
        (self_out, False),
        (relative_bucket_bias.T, False),
    )
    own_cross = pack(
        (cross_query.T, False), (cross_key.T, False), (cross_value.T, False), (cross_out, False)
    )
    own_hidden = pack((widen_weight, True), (narrow_weight, False))

    def first_hops(own):
        shares, bit = {0: own}, mp_size // 2
        while bit > 1:
            for j in list(shares):
                shares[j | bit] = swap(shares[j], bit, mp_size)
            bit //= 2
        return shares

    def last_hop(shares, *others):
        if 1 not in shares:
            shares[1] = swap(shares[0], 1, mp_size)
        for j in range(2, mp_size, 2):
            shares[j] = after(shares[j], *others)
            shares[j | 1] = swap(shares[j], 1, mp_size)
        return shares

    near_self = first_hops(own_self)
    near_self[1] = swap(own_self, 1, mp_size)
    memory_rows = after(memory_rows, own_self)
    w_self = last_hop(near_self, own_cross, own_hidden, ids)
    w_self = [w_self[j] for j in order]
    near_cross = first_hops(own_cross)
    near_hidden = first_hops(own_hidden)
    near_hidden[1] = swap(own_hidden, 1, mp_size)
    memory_seen = lax.all_to_all(
        memory_rows.reshape(dp_size, slots // dp_size, features), "dp", 0, 0
    ).reshape(slots, features)

    gain_self = self_gain.astype(F32)[None]
    gain_cross = cross_gain.astype(F32)[None]
    gain_hidden = hidden_gain.astype(F32)[None]

    *saved_self, after_self = self_forward(heads, buckets, decoder_rows, gain_self, w_self, ids)
    w_cross = last_hop(near_cross, after_self)
    w_cross = [w_cross[j] for j in order]
    *saved_cross, after_cross = cross_forward(
        heads, after_self, gain_cross, memory_seen, doc_memory, w_cross
    )

    before, wide_sums, narrow_sums, w_hidden = (), [], [], near_hidden
    for j in range(0, mp_size, 2):
        wide_sum, narrow_sum, *before = feed_forward(
            after_cross,
            gain_hidden,
            layer_cotangent,
            [w_hidden[j + 1], w_hidden[j]],
            before,
            j == mp_size - 2,
        )
        wide_sums.append(wide_sum)
        narrow_sums.append(narrow_sum)
        if j == 0:
            w_hidden = last_hop(near_hidden, before[0])
    layer_output, grad_after_cross, branch, hidden_gain_grad = before

    scattered = not wide_sums[0].shape[0] % (2 * 16 * dp_size)
    *sums, grad_memory, grad_after_self, branch, cross_gain_grad = cross_backward(
        heads,
        dp_size,
        after_self,
        gain_cross,
        memory_seen,
        doc_memory,
        branch,
        grad_after_cross,
        saved_cross,
        w_cross,
        wide_sums,
        narrow_sums,
        scattered,
    )
    far = 2 if scattered else mp_size - 2
    came, cross_sums = sums[:far], sums[far:]
    if scattered:
        blocks, terms = came, []
    else:
        hidden = [wide_sums[0], narrow_sums[0]], came
        blocks, terms = [], [[jnp.concatenate(both, axis=0) for both in hidden if both]]
    memory_grad = lax.all_to_all(
        grad_memory.reshape(dp_size, slots // dp_size, features), "dp", 0, 0
    ).reshape(slots, features)
    cross_sums[1:] = [swap(share, 2, mp_size) for share in cross_sums[1:]]

    give, keep, score_grads, input_grad, self_gain_grad = self_backward(
        heads,
        buckets,
        decoder_rows,
        gain_self,
        ids,
        branch,
        grad_after_self,
        saved_self,
        w_self,
    )
    (*hidden, sum_cross, sum_self), small = tail_sums(
        dp_size,
        mp_size,
        buckets,
        heads,
        blocks,
        terms + [cross_sums],
        give,
        keep,
        ids,
        score_grads,
        (self_gain_grad, cross_gain_grad, hidden_gain_grad),
    )
    wide_grad, narrow_grad, self_grads, cross_grads, passed = finish(
        *(hidden if scattered else jnp.split(hidden[0], 2)),
        sum_cross,
        sum_self,
        layer_output,
        memory_grad,
    )
    layer_output, memory_grad = passed
    gain_rows = 3 * features // LANES
    gains = small[:gain_rows].reshape(3, features)
    lines = -(-heads * buckets // LANES)
    sums = small[gain_rows : gain_rows + lines, : heads // lines * buckets]
    position_grad = sums.reshape(heads, buckets).T

    return (
        layer_output,
        input_grad,
        memory_grad,
        position_grad,
        gains[0],
        *[grad.T for grad in self_grads[:3]],
        self_grads[3],
        gains[1],
        *[grad.T for grad in cross_grads[:3]],
        cross_grads[3],
        gains[2],
        wide_grad,
        narrow_grad,
    )


def solution(mesh):
    return jax.shard_map(
        shards,
        mesh=mesh,
        in_specs=(
            P(("dp", "mp"), None),
            P(("dp", "mp"), None),
            P("dp"),
            P("dp"),
            P(),
            P(None, "mp"),
            P(),
            P(None, "mp"),
            P(None, "mp"),
            P(None, "mp"),
            P("mp", None),
            P(),
            P(None, "mp"),
            P(None, "mp"),
            P(None, "mp"),
            P("mp", None),
            P(),
            P(None, "mp"),
            P("mp", None),
            P(("dp", "mp"), None),
        ),
        out_specs=(
            P(("dp", "mp"), None),
            P(("dp", "mp"), None),
            P(("dp", "mp"), None),
            P(None, "mp"),
            P(),
            P(None, "mp"),
            P(None, "mp"),
            P(None, "mp"),
            P("mp", None),
            P(),
            P(None, "mp"),
            P(None, "mp"),
            P(None, "mp"),
            P("mp", None),
            P(),
            P(None, "mp"),
            P("mp", None),
        ),
        check_vma=False,
    )
```

```python
import functools

import jax
import jax.numpy as jnp
from jax import lax
from jax.experimental import pallas as pl
from jax.experimental.pallas import tpu as pltpu
from jax.sharding import PartitionSpec as P

HEAD_DIM = 64
NORM_EPS = 1e-06
MASKED = -1e30
SCALE = HEAD_DIM**-0.5
BF16 = jnp.bfloat16
F32 = jnp.float32
LANES = 128
TABLE_ROWS = 16
TILE_ROWS = 16
LARGEST_SUM = 1e30
LATE_STEP = 4
HEAD_BLOCK = 256
BLOCK_HEADS = HEAD_BLOCK // HEAD_DIM
Q_BLOCK = 256
K_BLOCK = 512
FORWARD_K_BLOCK = 256
HIDDEN_BLOCK = 256
MEMORY_BLOCK = 768
FINISH_BLOCK = 384
ROW_BLOCK = 128
VMEM_BYTES = 56 * 1024 * 1024
GELU_ROOT = 0.7978845608028654
GELU_CUBE = 0.044715


def dot_nn(a, b):
    return lax.dot_general(a, b, (((1,), (0,)), ((), ())), preferred_element_type=F32)


def dot_nt(a, b):
    return lax.dot_general(a, b, (((1,), (1,)), ((), ())), preferred_element_type=F32)


def dot_tn(a, b):
    return lax.dot_general(a, b, (((0,), (0,)), ((), ())), preferred_element_type=F32)


def flip(a):
    return a.astype(F32).T.astype(BF16)


def spans(size, step):
    return [slice(i, i + step) for i in range(0, size, step)]


def norm_scale(rows):
    return lax.rsqrt(jnp.mean(rows * rows, axis=-1, keepdims=True) + NORM_EPS)


def norm_into(normed_ref, rows_ref, gain_ref):
    for span in spans(rows_ref.shape[0], ROW_BLOCK):
        rows = rows_ref[span].astype(F32)
        normed_ref[span] = (rows * norm_scale(rows) * gain_ref[...]).astype(BF16)


def norm_back_into(span, grad, out_ref, low_ref, gain_grad_ref, rows_ref, gain_ref, add_ref):
    rows = rows_ref[span].astype(F32)
    scale = norm_scale(rows)
    unit = rows * scale
    grad_unit = grad * gain_ref[...]
    mean = jnp.mean(grad_unit * unit, axis=-1, keepdims=True)
    out = add_ref[span].astype(F32) + scale * (grad_unit - unit * mean)
    out_ref[span] = out
    if low_ref is not None:
        low_ref[span] = out.astype(BF16)
    gain_grad_ref[...] += jnp.sum((grad * unit).reshape(-1, 8, rows.shape[1]), axis=0)


def gelu_and_slope(v):
    square = v * v
    bend = jnp.tanh(GELU_ROOT * (v + GELU_CUBE * v * square))
    half = 0.5 * (1.0 + bend)
    slope = half + 0.5 * v * (1.0 - bend * bend) * GELU_ROOT * (1.0 + 3.0 * GELU_CUBE * square)
    return v * half, slope


def lane_block(start):
    return pl.ds(pl.multiple_of(start, LANES), LANES)


def extra_lanes(rows, allowed):
    lane = lax.broadcasted_iota(jnp.int32, (rows, LANES), 1) % HEAD_DIM
    first = MASKED if allowed is None else jnp.where(allowed, 0.0, MASKED)
    return jnp.where(lane == 0, first, jnp.where(lane < 4, 1.0, 0.0)).astype(BF16)


def pick(which, block, other):
    lane = lax.broadcasted_iota(jnp.int32, block.shape, 1)
    return jnp.where((lane < HEAD_DIM) == (which == 0), block, other)


def half_rows(which):
    return slice(which * HEAD_DIM, (which + 1) * HEAD_DIM)


def split(values):
    high = values.astype(BF16).astype(F32)
    rest = values - high
    middle = rest.astype(BF16).astype(F32)
    return high, middle, rest - middle


def with_extra(which, block_t, masked, minus):
    columns = block_t.shape[1]
    row = lax.broadcasted_iota(jnp.int32, (HEAD_DIM, columns), 0)
    extra = jnp.where(row == 0, 1.0 if masked else 0.0, 0.0)
    if minus is not None:
        for i, part in enumerate(split(minus)):
            extra = jnp.where(row == i + 1, -part, extra)
    own = block_t[half_rows(which)]
    return jnp.concatenate([own, extra] if which == 0 else [extra, own], axis=0).astype(BF16)


def bias_block(table_ref, ids_ref, index, rows, start):
    row = jnp.broadcast_to(table_ref[pl.ds(index, 1), :], (rows, LANES))
    return jnp.concatenate(
        [
            jnp.take_along_axis(row, ids_ref[:rows, c : c + LANES], axis=1)
            for c in range(start, start + Q_BLOCK, LANES)
        ],
        axis=1,
    )


def ring_place(me, size):
    return jnp.where(me % 2 == 0, me // 2, size - 1 - me // 2)


def ring_device(place, size):
    return jnp.where(place < size // 2, 2 * place, 2 * (size - 1 - place) + 1)


def ring_ways(size):
    me = lax.axis_index("dp")
    place = ring_place(me, size)
    return (
        (place, ring_device((place + 1) % size, size)),
        (size - 1 - place, ring_device((place + size - 1) % size, size)),
    )


def differing(row, bit):
    return row + bit - 2 * bit * ((row // bit) % 2)


def remote(source, target, send_sem, recv_sem, device):
    return pltpu.make_async_remote_copy(
        src_ref=source,
        dst_ref=target,
        send_sem=send_sem,
        recv_sem=recv_sem,
        device_id=device,
        device_id_type=pl.DeviceIdType.MESH,
    )


def greet(bits, devices=()):
    me, row = lax.axis_index("dp"), lax.axis_index("mp")
    barrier = pltpu.get_barrier_semaphore()
    others = [(me, differing(row, bit)) for bit in bits] + [(device, row) for device in devices]
    for other in others:
        pl.semaphore_signal(
            barrier, inc=1, device_id=other, device_id_type=pl.DeviceIdType.MESH
        )
    pl.semaphore_wait(barrier, len(others))


def to_differing(bit, source, target, sems):
    me, row = lax.axis_index("dp"), lax.axis_index("mp")
    return remote(source, target, sems.at[0], sems.at[1], (me, differing(row, bit)))


class Scatter:
    def __init__(self, size, part, slots, done, send, came):
        self.size, self.part, self.slots, self.done = size, part, slots, done
        self.send, self.came = send, came
        self.ways, self.row = ring_ways(size), lax.axis_index("mp")

    def span(self, way, number):
        rows = self.slots.shape[3]
        return pl.ds(pl.multiple_of((way * self.size + number) * rows, 16), rows)

    def copy(self, way, step, source):
        return remote(
            source,
            self.slots.at[way, step],
            self.send.at[way, step],
            self.came.at[way, step],
            (self.ways[way][1], self.row),
        )

    def first(self, way):
        return self.copy(way, 0, self.part.at[:, self.span(way, self.ways[way][0])])

    def next(self, way, step):
        return self.copy(way, step, self.slots.at[way, step - 1])

    def begin(self):
        for way in range(2):
            self.first(way).start()

    def total(self, way, step):
        self.copy(way, step, self.slots.at[way, step]).wait_recv()
        span = self.span(way, (self.ways[way][0] - step - 1 + self.size) % self.size)
        return low_sum(self.slots[way, step], self.part[:, span])

    def advance(self, step):
        for way in range(2):
            self.slots[way, step - 1] = self.total(way, step - 1)
            self.next(way, step).start()

    def turn(self):
        for way in range(2):
            self.done[way] = self.total(way, self.size - 2)

    def wait_sent(self):
        for way in range(2):
            self.first(way).wait_send()

        def sent(step, carry):
            for way in range(2):
                self.next(way, step).wait_send()
            return carry

        lax.fori_loop(1, self.size - 1, sent, 0)


def low_sum(a, b):
    return (a.astype(F32) + b.astype(F32)).astype(BF16)


class Stack:
    def __init__(self, sources, stack_ref, sems, kinds, rows):
        features = stack_ref.shape[0] // kinds
        self.copies = [
            [
                pltpu.make_async_copy(
                    source.at[pl.ds(kind * rows, rows)],
                    stack_ref.at[pl.ds(kind * features + p * rows, rows)],
                    sems.at[p, kind],
                )
                for p, source in enumerate(sources)
            ]
            for kind in range(kinds)
        ]

    def start(self):
        for copies in self.copies:
            for copy in copies:
                copy.start()

    def wait(self, *kinds):
        for kind in kinds:
            for copy in self.copies[kind]:
                copy.wait()


def table_copies(sources, tables_ref, sems, kinds):
    start = sources[0].shape[0] - TABLE_ROWS
    return [
        pltpu.make_async_copy(
            source.at[pl.ds(start, TABLE_ROWS)], tables_ref.at[p], sems.at[p, kinds]
        )
        for p, source in enumerate(sources)
    ]


def table_into(table_ref, tables_ref, heads, buckets):
    for p in range(tables_ref.shape[0]):
        rows = tables_ref[p, :, :LANES].astype(F32)
        lane = lax.broadcasted_iota(jnp.int32, rows.shape, 1)
        rows = jnp.where(lane < buckets, rows, MASKED)
        for h in range(heads):
            table_ref[p * heads + h : p * heads + h + 1, :] = rows[h : h + 1, :]


def self_forward_kernel(heads, buckets, shares, rows_ref, gain_ref, ids_ref, *refs):
    sources = refs[:shares]
    q_ref, k_ref, v_ref, mixed_ref, lse_ref, bias_ref, out_ref = refs[shares : shares + 7]
    w_ref, tables_ref, table_ref, normed_ref, sems = refs[shares + 7 :]
    step = pl.program_id(0)
    doc, features = rows_ref.shape
    stack = Stack(sources, w_ref, sems, 4, heads * HEAD_DIM)

    @pl.when(step == 0)
    def _():
        stack.start()
        tables = table_copies(sources, tables_ref, sems, 4)
        for copy in tables:
            copy.start()
        norm_into(normed_ref, rows_ref, gain_ref)
        out_ref[...] = rows_ref[...].astype(F32)
        for copy in tables:
            copy.wait()
        table_into(table_ref, tables_ref, heads, buckets)
        stack.wait(0, 1, 2, 3)

    def weights(kind):
        start = pl.multiple_of(kind * features + step * HEAD_BLOCK, HEAD_BLOCK)
        return w_ref[pl.ds(start, HEAD_BLOCK)]

    for kind, ref in enumerate((q_ref, k_ref, v_ref)):
        ref[...] = dot_nt(normed_ref[...], weights(kind)).astype(BF16)
    none = jnp.zeros((doc, LANES), BF16)
    for pair in range(BLOCK_HEADS // 2):
        lanes = slice(pair * LANES, (pair + 1) * LANES)
        k, v_t = k_ref[:, lanes], flip(v_ref[:, lanes])
        q_t = flip(q_ref[:, lanes].astype(F32) * SCALE)
        k_of = [pick(which, k, none) for which in range(2)]
        for span in spans(doc, Q_BLOCK):
            rows, mixed = span.stop, []
            for which in range(2):
                h = 2 * pair + which
                bias = bias_block(table_ref, ids_ref, step * BLOCK_HEADS + h, rows, span.start)
                bias_ref[h, :rows, span] = bias.astype(BF16)
                s = dot_nn(k_of[which][:rows], q_t[:, span]) + bias
                top = jnp.max(s, axis=0, keepdims=True)
                p = jnp.exp(s - top)
                total = jnp.sum(p, axis=0, keepdims=True)
                mixed.append(dot_nn(v_t[half_rows(which), :rows], p.astype(BF16)) / total)
                lse_ref[0, h : h + 1, span] = top + jnp.log(total)
            mixed_ref[span, lanes] = jnp.concatenate(mixed, axis=0).T.astype(BF16)
    out_ref[...] += dot_nn(mixed_ref[...], weights(3))


def self_backward_kernel(heads, shares, *refs):
    count = shares // 2
    rows_ref, gain_ref, branch_ref, add_ref = refs[:4]
    q_ref, k_ref, v_ref, mixed_ref, lse_ref, bias_ref = refs[4:10]
    sources, refs = refs[10 : 10 + shares], refs[10 + shares :]
    hop_in, hop_out, refs = refs[: count - 1], refs[count - 1 : 2 * count - 2], refs[2 * count - 2 :]
    sums, refs = refs[:count], refs[count:]
    ds_ref, out_ref, gain_grad_ref = refs[:3]
    w_ref, normed_ref, g_ref, grad_ref, back_ref, give_ref, keep_ref, came_ref = refs[3:11]
    sems, swap_sems, hop_sems = refs[11:]
    step = pl.program_id(0)
    doc, features = rows_ref.shape
    half = features // 2
    stack = Stack(sources, w_ref, sems, 4, heads * HEAD_DIM)
    swap = to_differing(1, give_ref, came_ref, swap_sems)
    hops = [
        to_differing(2, source, target, hop_sems) for source, target in zip(hop_in, hop_out)
    ]

    @pl.when(step == 0)
    def _():
        stack.start()
        greet([1, 2][:count])
        for hop in hops:
            hop.start()
        norm_into(normed_ref, rows_ref, gain_ref)
        stack.wait(3)

    start = pl.multiple_of(3 * features + step * HEAD_BLOCK, HEAD_BLOCK)
    g_ref[...] = dot_nt(branch_ref[...], w_ref[pl.ds(start, HEAD_BLOCK)]).astype(BF16)
    none = jnp.zeros((doc, LANES), BF16)
    ones = extra_lanes(doc, None)
    for pair in range(BLOCK_HEADS // 2):
        lanes = lane_block(step * HEAD_BLOCK + pair * LANES)
        q, k, v = q_ref[:, lanes], k_ref[:, lanes], v_ref[:, lanes]
        g = g_ref[:, pair * LANES : (pair + 1) * LANES]
        q_t, k_t = q.astype(F32).T * SCALE, flip(k)
        g_t = g.astype(F32).T
        inner = g_t * mixed_ref[:, lanes].astype(F32).T
        per_head = []
        for which in range(2):
            h = 2 * pair + which
            minus = jnp.sum(inner[half_rows(which)], axis=0, keepdims=True)
            per_head.append(
                (
                    pick(which, k, ones),
                    pick(which, v, ones),
                    with_extra(which, q_t, False, lse_ref[0, h : h + 1, :]),
                    with_extra(which, g_t, False, minus),
                    pick(which, q, none),
                    pick(which, g, none),
                )
            )
        grad_k = grad_v = None
        for span in spans(doc, Q_BLOCK):
            rows, grad_q, part_k, part_v = span.stop, [], None, None
            for which, (k_of, v_of, q_with, g_with, q_of, g_of) in enumerate(per_head):
                h = 2 * pair + which
                s = dot_nn(k_of[:rows], q_with[:, span])
                p = jnp.exp(s + bias_ref[h, :rows, span].astype(F32))
                ds = (p * dot_nn(v_of[:rows], g_with[:, span])).astype(BF16)
                ds_ref[h, :rows, span] = ds
                grad_q.append(dot_nn(k_t[half_rows(which), :rows], ds))
                to_v = dot_nn(p.astype(BF16), g_of[span])
                to_k = dot_nn(ds, q_of[span])
                part_v = to_v if part_v is None else part_v + to_v
                part_k = to_k if part_k is None else part_k + to_k
            grad_q = (jnp.concatenate(grad_q, axis=0) * SCALE).T
            grad_ref[span, lanes] = grad_q.astype(BF16)
            if grad_v is not None:
                part_v = jnp.concatenate(
                    [part_v[: span.start] + grad_v, part_v[span.start :]], axis=0
                )
                part_k = jnp.concatenate(
                    [part_k[: span.start] + grad_k, part_k[span.start :]], axis=0
                )
            grad_v, grad_k = part_v, part_k
        k_lanes = lane_block(features + step * HEAD_BLOCK + pair * LANES)
        v_lanes = lane_block(2 * features + step * HEAD_BLOCK + pair * LANES)
        grad_ref[:, k_lanes] = (grad_k * SCALE).astype(BF16)
        grad_ref[:, v_lanes] = grad_v.astype(BF16)

    @pl.when(step == pl.num_programs(0) - 1)
    def _():
        stack.wait(0, 1, 2)
        def weight_grads(ref, columns):
            for kind in range(3):
                kind_columns = slice(kind * features + columns.start, kind * features + columns.stop)
                ref[kind] = dot_tn(grad_ref[:, kind_columns], normed_ref[...]).astype(BF16)
            ref[3] = dot_tn(mixed_ref[:, columns], branch_ref[...]).astype(BF16)

        weight_grads(give_ref, slice(0, half))
        swap.start()
        weight_grads(keep_ref, slice(half, features))
        gain_grad_ref[...] = jnp.zeros_like(gain_grad_ref)
        back_ref[...] = dot_nn(grad_ref[...], w_ref[: 3 * features])
        for span in spans(doc, ROW_BLOCK):
            norm_back_into(
                span, back_ref[span], out_ref, None, gain_grad_ref, rows_ref, gain_ref, add_ref
            )
        swap.wait_recv()
        rows = half // count
        for share, sums_ref in enumerate(sums):
            for kind in range(4):
                span = slice(share * rows, (share + 1) * rows)
                to = slice(kind * rows, (kind + 1) * rows)
                sums_ref[to] = low_sum(keep_ref[kind, span], came_ref[kind, span])
        swap.wait_send()
        for hop in hops:
            hop.wait()


def cross_forward_kernel(heads, shares, length_ref, rows_ref, gain_ref, memory_ref, *refs):
    sources = refs[:shares]
    q_ref, k_ref, v_ref, mixed_ref, lse_ref, out_ref = refs[shares : shares + 6]
    w_ref, normed_ref, extra_ref, p_ref, mix_ref, sems = refs[shares + 6 :]
    step = pl.program_id(0)
    (doc, features), slots = rows_ref.shape, memory_ref.shape[0]
    stack = Stack(sources, w_ref, sems, 4, heads * HEAD_DIM)

    @pl.when(step == 0)
    def _():
        stack.start()
        norm_into(normed_ref, rows_ref, gain_ref)
        out_ref[...] = rows_ref[...]
        slot = lax.broadcasted_iota(jnp.int32, (slots, LANES), 0)
        extra_ref[...] = extra_lanes(slots, slot < length_ref[0])
        stack.wait(0, 1, 2, 3)

    def weights(kind):
        start = pl.multiple_of(kind * features + step * HEAD_BLOCK, HEAD_BLOCK)
        return w_ref[pl.ds(start, HEAD_BLOCK)]

    q_ref[...] = dot_nt(normed_ref[...], weights(0)).astype(BF16)
    k_ref[...] = dot_nt(memory_ref[...], weights(1)).astype(BF16)
    v_ref[...] = dot_nt(memory_ref[...], weights(2)).astype(BF16)

    units = [
        (pair, which, span)
        for pair in range(BLOCK_HEADS // 2)
        for span in spans(doc, Q_BLOCK)
        for which in range(2)
    ]
    ones = jnp.ones((TILE_ROWS, slots), BF16)
    keys = spans(slots, FORWARD_K_BLOCK)

    def lanes_of(pair):
        return slice(pair * LANES, (pair + 1) * LANES)

    def key_side(pair, which):
        return pick(which, k_ref[:, lanes_of(pair)], extra_ref[...])

    def write(pair, which, span, top, total, mixed):
        h = 2 * pair + which
        lse_ref[0, h : h + 1, span] = top + jnp.log(total)
        mix_ref[half_rows(which)] = mixed / total
        if which == 1:
            mixed_ref[span, lanes_of(pair)] = mix_ref[...].T.astype(BF16)

    v_t = [flip(v_ref[:, lanes_of(p)]) for p in range(BLOCK_HEADS // 2)]
    q_t = [q_ref[:, lanes_of(p)].astype(F32).T * SCALE for p in range(BLOCK_HEADS // 2)]

    def begin(unit):
        pair, which, span = unit
        k_of = key_side(pair, which)
        s = dot_nn(k_of[keys[0]], with_extra(which, q_t[pair][:, span], True, None))
        top = jnp.max(s, axis=0, keepdims=True)
        return k_of, s, top, with_extra(which, q_t[pair][:, span], True, top)

    worst = jnp.zeros((1, Q_BLOCK), F32)
    ahead = begin(units[0])
    for i, (pair, which, span) in enumerate(units):
        (k_of, s, top, q_with), slot = ahead, i % 2
        p_ref[slot, keys[0]] = jnp.exp(s - top).astype(BF16)
        for rows in keys[1:]:
            p_ref[slot, rows] = jnp.exp(dot_nn(k_of[rows], q_with)).astype(BF16)
        if i + 1 < len(units):
            ahead = begin(units[i + 1])
        value_side = jnp.concatenate([v_t[pair][half_rows(which)], ones], axis=0)
        mixed = dot_nn(value_side, p_ref[slot])
        total = mixed[HEAD_DIM : HEAD_DIM + 1]
        worst = jnp.maximum(worst, total)
        write(pair, which, span, top, total, mixed[:HEAD_DIM])

    @pl.when(jnp.max(worst) > LARGEST_SUM)
    def _():
        for pair, which, span in units:
            q_with = with_extra(
                which, q_ref[:, lanes_of(pair)].astype(F32).T[:, span] * SCALE, True, None
            )
            k_of = key_side(pair, which)
            s = [dot_nn(k_of[rows], q_with) for rows in keys]
            top = functools.reduce(jnp.maximum, [jnp.max(c, axis=0, keepdims=True) for c in s])
            total = jnp.zeros_like(top)
            for rows, chunk in zip(keys, s):
                p = jnp.exp(chunk - top)
                total = total + jnp.sum(p, axis=0, keepdims=True)
                p_ref[0, rows] = p.astype(BF16)
            mixed = dot_nn(flip(v_ref[:, lanes_of(pair)])[half_rows(which)], p_ref[0])
            write(pair, which, span, top, total, mixed)

    out_ref[...] += dot_nn(mixed_ref[...], weights(3))


def cross_backward_kernel(heads, shares, size, scattered, hops_wanted, length_ref, *refs):
    gain_ref, branch_ref, q_ref, mixed_ref, lse_ref = refs[:5]
    rows_in, memory_in, add_in, k_in, v_in = refs[5:10]
    sources = refs[10 : 10 + shares]
    count = shares // 2
    refs = refs[10 + shares :]
    scatter_in, refs = refs[:scattered], refs[scattered:]
    hidden_in, refs = refs[:hops_wanted], refs[hops_wanted:]
    hidden_out, refs = refs[:hops_wanted], refs[hops_wanted:]
    if scattered:
        scatter_out, refs = refs[0], refs[1:]
        (part_ref, ring_slots, done_ref, scatter_came), refs = refs[-8:-4], refs[:-8] + refs[-4:]
        (ring_send, ring_came, part_sems, done_sems), refs = refs[-4:], refs[:-4]
        scatter = Scatter(size, part_ref, ring_slots, done_ref, ring_send, ring_came)
        part_loads = [
            pltpu.make_async_copy(source, part_ref.at[i], part_sems.at[i])
            for i, source in enumerate(scatter_in)
        ]
        for copy in part_loads:
            copy.start()
    sums, refs = refs[:count], refs[count:]
    memory_out, out_ref, low_ref, gain_grad_ref = refs[:4]
    rows_ref, memory_ref, add_ref, k_ref, v_ref = refs[4:9]
    (
        w_ref,
        normed_ref,
        extra_ref,
        g_ref,
        grad_q_ref,
        grad_ref,
        ds_ref,
        give_ref,
        keep_ref,
        came_ref,
        memory_grad_ref,
        back_ref,
        sems,
        load_sems,
        key_sems,
        out_sems,
        swap_sems,
        hop_sems,
    ) = refs[9:]
    (doc, features), slots = rows_ref.shape, memory_ref.shape[0]
    half, blocks = features // 2, features // HEAD_BLOCK
    stack = Stack(sources, w_ref, sems, 4, heads * HEAD_DIM)
    loads = [
        pltpu.make_async_copy(source, target, load_sems.at[i])
        for i, (source, target) in enumerate(
            ((memory_in, memory_ref), (rows_in, rows_ref), (add_in, add_ref))
        )
    ]

    def key_copies(b):
        lanes = pl.ds(pl.multiple_of(b * HEAD_BLOCK, HEAD_BLOCK), HEAD_BLOCK)
        return [
            pltpu.make_async_copy(source.at[:, lanes], target.at[b], key_sems.at[i, b])
            for i, (source, target) in enumerate(((k_in, k_ref), (v_in, v_ref)))
        ]

    stack.start()
    for b in range(blocks):
        for copy in key_copies(b):
            copy.start()
    for copy in loads:
        copy.start()
    greet([1, 2][:count], [way[1] for way in ring_ways(size)] if scattered else [])
    hops = [
        to_differing(2, source, target, hop_sems.at[i])
        for i, (source, target) in enumerate(zip(hidden_in, hidden_out))
    ]
    for hop in hops:
        hop.start()
    if scattered:
        for copy in part_loads:
            copy.wait()
        scatter.begin()
    slot = lax.broadcasted_iota(jnp.int32, (slots, LANES), 0)
    extra_ref[...] = extra_lanes(slots, slot < length_ref[0])
    none = jnp.zeros((doc, LANES), BF16)
    stack.wait(3)

    def one_block(step, carry):
        start = pl.multiple_of(3 * features + step * HEAD_BLOCK, HEAD_BLOCK)
        g_ref[...] = dot_nt(branch_ref[...], w_ref[pl.ds(start, HEAD_BLOCK)]).astype(BF16)
        for copy in key_copies(step):
            copy.wait()
        for pair in range(BLOCK_HEADS // 2):
            local = slice(pair * LANES, (pair + 1) * LANES)
            lanes = lane_block(step * HEAD_BLOCK + pair * LANES)
            v_lanes = lane_block(features + step * HEAD_BLOCK + pair * LANES)
            q, g = q_ref[:, lanes], g_ref[:, local]
            q_t, g_t = q.astype(F32).T * SCALE, g.astype(F32).T
            inner = g_t * mixed_ref[:, lanes].astype(F32).T
            per_head = []
            for which in range(2):
                h = 2 * pair + which
                minus = jnp.sum(inner[half_rows(which)], axis=0, keepdims=True)
                per_head.append(
                    (
                        with_extra(which, q_t, True, lse_ref[step, h : h + 1, :]),
                        with_extra(which, g_t, False, minus),
                        pick(which, q, none),
                        pick(which, g, none),
                    )
                )
            for rows in spans(slots, K_BLOCK):
                k, v, extra = k_ref[step, rows, local], v_ref[step, rows, local], extra_ref[rows]
                part_k = part_v = None
                for which, (q_with, g_with, q_of, g_of) in enumerate(per_head):
                    p = jnp.exp(dot_nn(pick(which, k, extra), q_with))
                    ds = (p * dot_nn(pick(which, v, extra), g_with)).astype(BF16)
                    ds_ref[which, rows] = ds
                    to_v = dot_nn(p.astype(BF16), g_of)
                    to_k = dot_nn(ds, q_of)
                    part_v = to_v if part_v is None else part_v + to_v
                    part_k = to_k if part_k is None else part_k + to_k
                grad_ref[rows, lanes] = (part_k * SCALE).astype(BF16)
                grad_ref[rows, v_lanes] = part_v.astype(BF16)
            k_t = flip(k_ref[step, :, local])
            grad_q = [dot_nn(k_t[half_rows(which)], ds_ref[which]) for which in range(2)]
            grad_q_ref[:, lanes] = (jnp.concatenate(grad_q, axis=0) * SCALE).T.astype(BF16)
            if scattered:
                scatter_step(1 + step * (BLOCK_HEADS // 2) + pair)
        return carry

    places = blocks * (BLOCK_HEADS // 2)

    def scatter_step(step):
        if size - 2 >= places:
            scatter.advance(step)
        elif size > 2:

            @pl.when(step <= size - 2)
            def _():
                scatter.advance(step)

    lax.fori_loop(0, blocks, one_block, 0)
    if scattered:

        def rest(step, carry):
            scatter.advance(step)
            return carry

        lax.fori_loop(min(places, size - 2) + 1, size - 1, rest, 0)
        scatter.turn()
        done_hops = [
            to_differing(2, done_ref.at[:, i], scatter_came, done_sems)
            for i in range(1, scattered)
        ]
        for hop in done_hops:
            hop.start()

    for copy in loads:
        copy.wait()
    norm_into(normed_ref, rows_ref, gain_ref)

    def weight_grads(ref, first):
        columns = slice(first, first + half)
        v_columns = slice(features + first, features + first + half)
        ref[0] = dot_tn(grad_q_ref[:, columns], normed_ref[...]).astype(BF16)
        ref[1] = dot_tn(grad_ref[:, columns], memory_ref[...]).astype(BF16)
        ref[2] = dot_tn(grad_ref[:, v_columns], memory_ref[...]).astype(BF16)
        ref[3] = dot_tn(mixed_ref[:, columns], branch_ref[...]).astype(BF16)

    weight_grads(give_ref, 0)
    swap = to_differing(1, give_ref, came_ref, swap_sems)
    swap.start()
    stack.wait(0, 1, 2)
    writes = []
    for i, rows in enumerate(spans(slots, MEMORY_BLOCK)):
        memory_grad_ref[rows] = dot_nn(
            grad_ref[rows], w_ref[features : 3 * features]
        ).astype(BF16)
        writes.append(
            pltpu.make_async_copy(memory_grad_ref.at[rows], memory_out.at[rows], out_sems.at[i])
        )
        writes[-1].start()
    weight_grads(keep_ref, half)
    gain_grad_ref[...] = jnp.zeros_like(gain_grad_ref)
    back_ref[...] = dot_nn(grad_q_ref[...], w_ref[:features])
    for span in spans(doc, ROW_BLOCK):
        norm_back_into(
            span, back_ref[span], out_ref, low_ref, gain_grad_ref, rows_ref, gain_ref, add_ref
        )
    swap.wait_recv()
    rows = half // count
    for share, sums_ref in enumerate(sums):
        for kind in range(4):
            span = slice(share * rows, (share + 1) * rows)
            to = slice(kind * rows, (kind + 1) * rows)
            sums_ref[to] = low_sum(keep_ref[kind, span], came_ref[kind, span])
    swap.wait_send()
    for copy in writes:
        copy.wait()
    for hop in hops:
        hop.wait()
    if scattered:
        for hop in done_hops:
            hop.wait()
        own = done_ref[:, 0]
        scatter_out[...] = low_sum(own, scatter_came[...]) if done_hops else own
        scatter.wait_sent()


def feed_forward_kernel(first, last, rows_ref, gain_ref, cotangent_ref, *refs):
    sources, refs = refs[:2], refs[2:]
    if not first:
        before_in, refs = refs[:2], refs[2:]
    sums, layer_ref, out_ref = refs[:2], refs[2], refs[3]
    if last:
        low_ref, gain_grad_ref = refs[4:6]
        refs = refs[2:]
    (
        wide_ref,
        narrow_ref,
        normed_ref,
        normed_t,
        cotangent_t,
        active_ref,
        grad_ref,
        give_ref,
        keep_ref,
        came_ref,
        layer_in_ref,
        back_in_ref,
        product_ref,
        sems,
        before_sems,
        swap_sems,
    ) = refs[4:]
    step, steps = pl.program_id(0), pl.num_programs(0)
    half = steps // 2
    doc = rows_ref.shape[0]
    hidden = sources[0].shape[0] // 2
    copies = [
        [
            pltpu.make_async_copy(
                source.at[pl.ds(kind * hidden, hidden)],
                stack.at[pl.ds(p * hidden, hidden)],
                sems.at[p, kind],
            )
            for kind, stack in enumerate((wide_ref, narrow_ref))
        ]
        for p, source in enumerate(sources)
    ]
    loads = []
    if not first:
        loads = [
            pltpu.make_async_copy(source, target, before_sems.at[i])
            for i, (source, target) in enumerate(zip(before_in, (layer_in_ref, back_in_ref)))
        ]
    swap = to_differing(1, give_ref, came_ref, swap_sems)

    @pl.when(step == 0)
    def _():
        for pair in copies:
            for copy in pair:
                copy.start()
        for copy in loads:
            copy.start()
        greet([1])
        norm_into(normed_ref, rows_ref, gain_ref)
        for span in spans(doc, ROW_BLOCK):
            normed_t[:, span] = flip(normed_ref[span])
            cotangent_t[:, span] = flip(cotangent_ref[span])

    for p, pair in enumerate(copies):

        @pl.when(step == p * half)
        def _(pair=pair):
            for copy in pair:
                copy.wait()

    units = pl.ds(pl.multiple_of(step * HIDDEN_BLOCK, HIDDEN_BLOCK), HIDDEN_BLOCK)
    activated, slope = gelu_and_slope(dot_nn(wide_ref[units], normed_t[...]))
    active_ref[units] = activated.astype(BF16)
    grad_ref[units] = (dot_nn(narrow_ref[units], cotangent_t[...]) * slope).astype(BF16)

    def store(ref, at):
        rows = pl.ds(pl.multiple_of(at * HIDDEN_BLOCK, HIDDEN_BLOCK), HIDDEN_BLOCK)
        ref[0, rows] = dot_nn(grad_ref[units], normed_ref[...]).astype(BF16)
        ref[1, rows] = dot_nn(active_ref[units], cotangent_ref[...]).astype(BF16)

    @pl.when(step < half)
    def _():
        store(give_ref, step)

    @pl.when(step == half - 1)
    def _():
        swap.start()

    @pl.when(step >= half)
    def _():
        store(keep_ref, step - half)

    @pl.when(step == steps - 1)
    def _():
        for copy in loads:
            copy.wait()
        if last:
            gain_grad_ref[...] = jnp.zeros_like(gain_grad_ref)
        product_ref[...] = dot_tn(active_ref[...], narrow_ref[...])
        for span in spans(doc, ROW_BLOCK):
            layer = rows_ref[span] if first else layer_in_ref[span]
            layer_ref[span] = (layer + product_ref[span]).astype(layer_ref.dtype)
        product_ref[...] = dot_tn(grad_ref[...], wide_ref[...])
        for span in spans(doc, ROW_BLOCK):
            back = product_ref[span]
            if not first:
                back = back + back_in_ref[span]
            if last:
                norm_back_into(
                    span, back, out_ref, low_ref, gain_grad_ref, rows_ref, gain_ref, cotangent_ref
                )
            else:
                out_ref[span] = back
        swap.wait_recv()
        for kind, sums_ref in enumerate(sums):
            for span in spans(hidden, HIDDEN_BLOCK):
                sums_ref[span] = low_sum(keep_ref[kind, span], came_ref[kind, span])
        swap.wait_send()


def pack_kernel(flipped, *refs):
    out_ref, start = refs[-1], 0
    for source, turn in zip(refs[:-1], flipped):
        if source.shape[-1] != out_ref.shape[1] and not turn:
            out_ref[start:] = jnp.zeros((TABLE_ROWS, out_ref.shape[1]), BF16)
            out_ref[start : start + source.shape[0], : source.shape[1]] = source[...]
            continue
        rows = source.shape[1] if turn else source.shape[0]
        span = slice(start, start + rows)
        out_ref[span] = flip(source[...]) if turn else source[...]
        start += rows


def finish_kernel(*refs):
    sources, outs, refs = refs[:4], refs[4:14], refs[14:]
    ins, wides, in_sems, out_sems = refs[:4], refs[4:14], refs[14], refs[15]
    loads, writes = [], []
    for i, (source, target) in enumerate(zip(sources, ins)):
        for j, span in enumerate(spans(target.shape[0], FINISH_BLOCK)):
            loads.append(
                pltpu.make_async_copy(source.at[span], target.at[span], in_sems.at[i, j])
            )
            loads[-1].start()

    def write(i, part):
        writes.append(
            pltpu.make_async_copy(wides[i].at[part], outs[i].at[part], out_sems.at[len(writes)])
        )
        writes[-1].start()

    waiting = iter(loads)
    hidden = wides[1].shape[0]
    for span in spans(hidden, FINISH_BLOCK):
        next(waiting).wait()
        for part in spans(FINISH_BLOCK, LANES):
            rows = slice(span.start + part.start, span.start + part.stop)
            wides[0][:, rows] = ins[0][rows].astype(F32).T
        write(0, (slice(None), span))
    for span in spans(hidden, FINISH_BLOCK):
        next(waiting).wait()
        wides[1][span] = ins[1][span].astype(F32)
        write(1, span)
    for i in (2, 3):
        for _ in spans(ins[i].shape[0], FINISH_BLOCK):
            next(waiting).wait()
        rows = wides[2].shape[0]
        for kind in range(4):
            at = 2 + 4 * (i - 2) + kind
            wides[at][...] = ins[i][kind * rows : (kind + 1) * rows].astype(F32)
            write(at, slice(None))
    for copy in writes:
        copy.wait()


def params():
    return pltpu.CompilerParams(vmem_limit_bytes=VMEM_BYTES)


def cost(flops=1 << 20):
    return pl.CostEstimate(flops=flops, bytes_accessed=1 << 16, transcendentals=0)


def shape(dims, dtype):
    return jax.ShapeDtypeStruct(dims, dtype)


def whole(array):
    return pl.BlockSpec(
        array.shape, lambda *_: (0,) * len(array.shape), pipeline_mode=pl.Buffered(1)
    )


def result(array):
    return pl.BlockSpec(array.shape, lambda *_: (0,) * len(array.shape))


def columns(rows):
    return pl.BlockSpec((rows, HEAD_BLOCK), lambda i: (0, i))


def anywhere(arrays):
    return [pl.BlockSpec(memory_space=pl.ANY) for _ in arrays]


SCALAR = pl.BlockSpec(memory_space=pltpu.SMEM)


def call(
    kernel, name, grid, in_specs, out_specs, out_shape, scratch, args, channel=None, flops=1 << 20
):
    compiler_params = params()
    if channel is not None:
        compiler_params = pltpu.CompilerParams(
            vmem_limit_bytes=VMEM_BYTES, collective_id=channel, has_side_effects=True
        )
    return pl.pallas_call(
        kernel,
        grid=grid,
        in_specs=in_specs,
        out_specs=out_specs,
        out_shape=out_shape,
        scratch_shapes=scratch,
        compiler_params=compiler_params,
        cost_estimate=cost(flops),
        name=name,
    )(*args)


def pack(*parts):
    arrays, flipped = zip(*parts)
    features = arrays[0].shape[0] if flipped[0] else arrays[0].shape[1]
    rows = [a.shape[1] if turn else a.shape[0] for a, turn in parts]
    if arrays[-1].shape[1] < features and not flipped[-1]:
        rows[-1] = TABLE_ROWS
    rows = sum(rows)
    return pl.pallas_call(
        functools.partial(pack_kernel, flipped),
        out_shape=shape((rows, features), BF16),
        compiler_params=params(),
        cost_estimate=cost(),
        name="pack",
    )(*arrays)


def self_forward(heads, buckets, rows, gain, weights, ids):
    doc, features = rows.shape
    shares, steps = len(weights), features // HEAD_BLOCK
    narrow, tall = shape((doc, features), BF16), shape((doc, features), F32)
    scores = shape((steps * BLOCK_HEADS, doc, doc), BF16)
    out_shape = (*[narrow] * 4, shape((steps, 8, doc), F32), scores, tall)
    return call(
        functools.partial(self_forward_kernel, heads, buckets, shares),
        "self_forward",
        (steps,),
        [whole(rows), whole(gain), whole(ids), *anywhere(weights)],
        (
            *[columns(doc)] * 4,
            pl.BlockSpec((1, 8, doc), lambda i: (i, 0, 0)),
            pl.BlockSpec((BLOCK_HEADS, doc, doc), lambda i: (i, 0, 0)),
            result(tall),
        ),
        out_shape,
        [
            pltpu.VMEM((4 * features, features), BF16),
            pltpu.VMEM((shares, TABLE_ROWS, features), BF16),
            pltpu.VMEM((TABLE_ROWS, LANES), F32),
            pltpu.VMEM((doc, features), BF16),
            pltpu.SemaphoreType.DMA((shares, 5)),
        ],
        (rows, gain, ids, *weights),
    )


def self_backward(heads, rows, gain, branch, add, saved, weights, hops):
    doc, features = rows.shape
    shares, steps = len(weights), features // HEAD_BLOCK
    count = shares // 2
    *arrays, lse, bias = saved
    packed = pltpu.VMEM((4, features // 2, features), BF16)
    scores = pl.BlockSpec((BLOCK_HEADS, doc, doc), lambda i: (i, 0, 0))
    out_shape = (
        *[shape(h.shape, BF16) for h in hops],
        *[shape((4 * heads * HEAD_DIM, features), BF16)] * count,
        shape((steps * BLOCK_HEADS, doc, doc), BF16),
        shape((doc, features), F32),
        shape((8, features), F32),
    )
    return call(
        functools.partial(self_backward_kernel, heads, shares),
        "self_backward",
        (steps,),
        [
            *[whole(a) for a in (rows, gain, branch, add, *arrays)],
            pl.BlockSpec((1, 8, doc), lambda i: (i, 0, 0)),
            scores,
            *anywhere(weights),
            *anywhere(hops),
        ],
        (
            *anywhere(hops),
            *[result(o) for o in out_shape[len(hops) : len(hops) + count]],
            scores,
            result(out_shape[-2]),
            result(out_shape[-1]),
        ),
        out_shape,
        [
            pltpu.VMEM((4 * features, features), BF16),
            pltpu.VMEM((doc, features), BF16),
            pltpu.VMEM((doc, HEAD_BLOCK), BF16),
            pltpu.VMEM((doc, 3 * features), BF16),
            pltpu.VMEM((doc, features), F32),
            packed,
            packed,
            packed,
            pltpu.SemaphoreType.DMA((shares, 4)),
            pltpu.SemaphoreType.DMA((2,)),
            pltpu.SemaphoreType.DMA((2,)),
        ],
        (rows, gain, branch, add, *arrays, lse, bias, *weights, *hops),
        channel=4,
    )


def cross_forward(heads, rows, gain, memory, length, weights):
    (doc, features), slots = rows.shape, memory.shape[0]
    shares, steps = len(weights), features // HEAD_BLOCK
    query, key = shape((doc, features), BF16), shape((slots, features), BF16)
    tall = shape((doc, features), F32)
    return call(
        functools.partial(cross_forward_kernel, heads, shares),
        "cross_forward",
        (steps,),
        [SCALAR, whole(rows), whole(gain), whole(memory), *anywhere(weights)],
        (
            columns(doc),
            columns(slots),
            columns(slots),
            columns(doc),
            pl.BlockSpec((1, 8, doc), lambda i: (i, 0, 0)),
            result(tall),
        ),
        (query, key, key, query, shape((steps, 8, doc), F32), tall),
        [
            pltpu.VMEM((4 * features, features), BF16),
            pltpu.VMEM((doc, features), BF16),
            pltpu.VMEM((slots, LANES), BF16),
            pltpu.VMEM((2, slots, Q_BLOCK), BF16),
            pltpu.VMEM((LANES, Q_BLOCK), F32),
            pltpu.SemaphoreType.DMA((shares, 4)),
        ],
        (length, rows, gain, memory, *weights),
    )


def cross_backward(
    heads, size, rows, gain, memory, length, branch, add, saved, weights, scattered, hops
):
    (doc, features), slots = rows.shape, memory.shape[0]
    shares, blocks = len(weights), features // HEAD_BLOCK
    count = shares // 2
    blocks_out, ring_scratch = [], []
    if scattered:
        number, part = len(scattered), scattered[0].shape
        block = (2, part[0] // (2 * size), features)
        blocks_out = [shape(block, BF16)]
        steps = pltpu.SemaphoreType.DMA((2, size - 1))
        ring_scratch = [
            pltpu.VMEM((number, *part), BF16),
            pltpu.VMEM((2, size - 1, number, *block[1:]), BF16),
            pltpu.VMEM((2, number, *block[1:]), BF16),
            pltpu.VMEM(block, BF16),
            steps,
            steps,
            pltpu.SemaphoreType.DMA((number,)),
            pltpu.SemaphoreType.DMA((2,)),
        ]
    out_shape = (
        *[shape(h.shape, BF16) for h in hops],
        *blocks_out,
        *[shape((4 * heads * HEAD_DIM, features), BF16)] * count,
        shape((slots, features), BF16),
        shape((doc, features), F32),
        shape((doc, features), BF16),
        shape((8, features), F32),
    )
    query, key, value, mixed, lse = saved
    near = (gain, branch, query, mixed, lse)
    far = (rows, memory, add, key, value, *weights, *scattered, *hops)
    vmem, hbm = pl.BlockSpec(memory_space=pltpu.VMEM), pl.BlockSpec(memory_space=pl.ANY)
    packed = pltpu.VMEM((4, features // 2, features), BF16)
    key_block = pltpu.VMEM((blocks, slots, HEAD_BLOCK), BF16)
    return call(
        functools.partial(
            cross_backward_kernel, heads, shares, size, len(scattered), len(hops)
        ),
        "cross_backward",
        (),
        [SCALAR, *[vmem for _ in near], *[hbm for _ in far]],
        (
            *[hbm] * len(hops),
            *[vmem] * len(blocks_out),
            *[vmem] * count,
            hbm,
            vmem,
            vmem,
            vmem,
        ),
        out_shape,
        [
            pltpu.VMEM((doc, features), F32),
            pltpu.VMEM((slots, features), BF16),
            pltpu.VMEM((doc, features), F32),
            key_block,
            key_block,
            pltpu.VMEM((4 * features, features), BF16),
            pltpu.VMEM((doc, features), BF16),
            pltpu.VMEM((slots, LANES), BF16),
            pltpu.VMEM((doc, HEAD_BLOCK), BF16),
            pltpu.VMEM((doc, features), BF16),
            pltpu.VMEM((slots, 2 * features), BF16),
            pltpu.VMEM((2, slots, doc), BF16),
            packed,
            packed,
            packed,
            pltpu.VMEM((slots, features), BF16),
            pltpu.VMEM((doc, features), F32),
            pltpu.SemaphoreType.DMA((shares, 4)),
            pltpu.SemaphoreType.DMA((3,)),
            pltpu.SemaphoreType.DMA((2, blocks)),
            pltpu.SemaphoreType.DMA((slots // MEMORY_BLOCK,)),
            pltpu.SemaphoreType.DMA((2,)),
            pltpu.SemaphoreType.DMA((max(len(hops), 1), 2)),
            *ring_scratch,
        ],
        (length, *near, *far),
        channel=1,
    )


def feed_forward(rows, gain, cotangent, weights, before, last):
    (doc, features), shares = rows.shape, len(weights)
    share = weights[0].shape[0] // 2
    hidden = share * shares
    steps = hidden // HIDDEN_BLOCK
    summed, tall = shape((share, features), BF16), shape((doc, features), F32)
    low = shape((doc, features), BF16)
    rest = [low, tall, low, shape((8, features), F32)] if last else [tall, tall]
    kept, added = pltpu.VMEM((2, share, features), BF16), pltpu.VMEM(tall.shape, F32)
    return call(
        functools.partial(feed_forward_kernel, not before, last),
        "feed_forward",
        (steps,),
        [whole(rows), whole(gain), whole(cotangent), *anywhere(weights), *anywhere(before)],
        (result(summed), result(summed), *[result(o) for o in rest]),
        (summed, summed, *rest),
        [
            pltpu.VMEM((hidden, features), BF16),
            pltpu.VMEM((hidden, features), BF16),
            pltpu.VMEM((doc, features), BF16),
            pltpu.VMEM((features, doc), BF16),
            pltpu.VMEM((features, doc), BF16),
            pltpu.VMEM((hidden, doc), BF16),
            pltpu.VMEM((hidden, doc), BF16),
            kept,
            kept,
            kept,
            added,
            added,
            added,
            pltpu.SemaphoreType.DMA((shares, 2)),
            pltpu.SemaphoreType.DMA((2,)),
            pltpu.SemaphoreType.DMA((2,)),
        ],
        (rows, gain, cotangent, *weights, *before),
        channel=3 if before else 2,
    )


def finish(sum_wide, sum_narrow, sum_cross, sum_self):
    rows, features = sum_self.shape
    hidden, part = sum_wide.shape[0], shape((rows // 4, features), F32)
    out_shape = [shape((features, hidden), F32), shape((hidden, features), F32), *[part] * 8]
    sources = (sum_wide, sum_narrow, sum_cross, sum_self)
    writes = 2 * hidden // FINISH_BLOCK + 8
    wide, narrow, *parts = pl.pallas_call(
        finish_kernel,
        in_specs=anywhere(sources),
        out_specs=anywhere(out_shape),
        out_shape=out_shape,
        scratch_shapes=[
            *[pltpu.VMEM(source.shape, BF16) for source in sources],
            *[pltpu.VMEM(out.shape, F32) for out in out_shape],
            pltpu.SemaphoreType.DMA((4, hidden // FINISH_BLOCK)),
            pltpu.SemaphoreType.DMA((writes,)),
        ],
        compiler_params=params(),
        cost_estimate=cost(),
        name="finish",
    )(*sources)
    return wide, narrow, parts[4:], parts[:4]


def share_place(row, other, peers):
    j, bit = 0, 1
    while bit < peers:
        j = j + bit * ((row // bit + other // bit) % 2)
        bit *= 2
    return (j % 2) * (j // 2) + (1 - j % 2) * (peers // 2 + j // 2)


def tail_kernel(size, peers, buckets, heads, gathered, counts, *refs):
    parts = []
    for count in counts:
        parts.append(refs[:count])
        refs = refs[count:]
    arrays, shares = len(counts) + 1, peers // 2
    last_refs, refs = refs[:shares], refs[shares:]
    ids_ref, ds_ref, *gain_refs = refs[:5]
    outs, small_out_ref, refs = refs[5 : 5 + arrays], refs[5 + arrays], refs[6 + arrays :]
    slots, refs = refs[:arrays], refs[arrays:]
    firsts, refs = refs[:arrays], refs[arrays:]
    far_came_ref, part_ref, scores_ref, bucket_ref = refs[:4]
    small_ref, near_ref, far_ref = refs[4:7]
    send, came, send_out, came_out, small_sems, hop_sems, local_sems = refs[7:]
    parts.append((part_ref,))
    me, row = lax.axis_index("dp"), lax.axis_index("mp")
    ways = ring_ways(size)
    doc = ids_ref.shape[0]
    mesh = pl.DeviceIdType.MESH

    load_scores = pltpu.make_async_copy(ds_ref, scores_ref, local_sems.at[0])
    load_scores.start()

    barrier = pltpu.get_barrier_semaphore()

    def greet(t, carry):
        pl.semaphore_signal(
            barrier, inc=1, device_id=((me + t) % size, row), device_id_type=mesh
        )
        return carry

    lax.fori_loop(1, size, greet, 0)
    for t in range(1, peers):
        pl.semaphore_signal(
            barrier, inc=1, device_id=(me, (row + t) % peers), device_id_type=mesh
        )
    pl.semaphore_wait(barrier, size - 1 + peers - 1)

    def block(i, way, number):
        rows = outs[i].shape[0] // (2 * size)
        return pl.ds(pl.multiple_of((way * size + number) * rows, 16), rows)

    def part(i, span):
        total = parts[i][0][span].astype(F32)
        for ref in parts[i][1:]:
            total = total + ref[span].astype(F32)
        return total

    def first_copy(i, way):
        return remote(
            firsts[i].at[way],
            slots[i].at[way, 0],
            send.at[i, way, 0],
            came.at[i, way, 0],
            (ways[way][1], row),
        )

    def next_copy(i, way, step):
        return remote(
            slots[i].at[way, step - 1],
            slots[i].at[way, step],
            send.at[i, way, step],
            came.at[i, way, step],
            (ways[way][1], row),
        )

    def wait_came(i, way, step):
        remote(
            slots[i].at[way, step],
            slots[i].at[way, step],
            send.at[i, way, step],
            came.at[i, way, step],
            (ways[way][1], row),
        ).wait_recv()

    def out_copy(i, way, step):
        span = block(i, way, (ways[way][0] + 1 - step + size) % size)
        return remote(
            outs[i].at[span],
            outs[i].at[span],
            send_out.at[i, way, step],
            came_out.at[i, way, step],
            (ways[way][1], row),
        )

    def begin(rings):
        for i, way in rings:
            firsts[i][way] = part(i, block(i, way, ways[way][0])).astype(BF16)
            first_copy(i, way).start()

    def plus_part(i, way, step):
        span = block(i, way, (ways[way][0] - step - 1 + size) % size)
        total = slots[i][way, step].astype(F32) + part(i, span)
        return span, total.astype(BF16)

    def advance(rings, step):
        for i, way in rings:
            wait_came(i, way, step - 1)
            slots[i][way, step - 1] = plus_part(i, way, step - 1)[1]
            next_copy(i, way, step).start()

    def turn(rings):
        for i, way in rings:
            wait_came(i, way, size - 2)
            span, total = plus_part(i, way, size - 2)
            outs[i][span] = total
            out_copy(i, way, 0).start()

    def pass_on(rings, step):
        for i, way in rings:
            out_copy(i, way, step - 1).wait_recv()
            out_copy(i, way, step).start()

    ready = [(i, way) for i in range(gathered) for way in range(2)]
    early = [(i, way) for i in range(gathered, arrays - 1) for way in range(2)]
    late = [(arrays - 1, way) for way in range(2)]

    other_chip = None
    if shares == 2:
        other_chip = to_differing(2, last_refs[1], far_came_ref, hop_sems)
        other_chip.start()
    begin(early)
    for i, way in ready:
        outs[i][block(i, way, (ways[way][0] + 1) % size)] = parts[i][0][way]
        out_copy(i, way, 0).start()

    rows_used, per_row = bucket_ref.shape[0], ds_ref.shape[0] // bucket_ref.shape[0]
    units = rows_used * buckets
    per_round = -(-units // max(2 * (size - 2), 1))

    def bucket_unit(u, carry):
        r, b = u // buckets, u % buckets
        sums = [jnp.zeros((8, LANES), F32) for _ in range(per_row)]
        for c in range(0, doc, LANES):
            hit = ids_ref[: c + LANES, c : c + LANES] == b
            for h in range(per_row):
                grads = scores_ref[r * per_row + h, : c + LANES, c : c + LANES].astype(F32)
                kept = jnp.where(hit, grads, 0.0).reshape(-1, 8, LANES)
                sums[h] = sums[h] + jnp.sum(kept, axis=0)
        for h in range(per_row):
            bucket_ref[r, h, pl.ds(b, 1), :] = jnp.sum(sums[h], axis=0, keepdims=True)
        return carry

    def bucket_round(k):
        low = jnp.minimum(k * per_round, units)
        lax.fori_loop(low, jnp.minimum(low + per_round, units), bucket_unit, 0)

    bucket_ref[...] = jnp.zeros_like(bucket_ref)
    part_ref[...] = jnp.zeros_like(part_ref)
    load_scores.wait()

    def early_step(step, carry):
        advance(early, step)
        pass_on(ready, step)
        bucket_round(step - 1)
        return carry

    begin_late = LATE_STEP if size - 1 > LATE_STEP else size - 1
    lax.fori_loop(1, min(begin_late + 1, size - 1), early_step, 0)
    if begin_late == size - 1:
        turn(early)
    used = slice(0, last_refs[0].shape[0])
    if other_chip is None:
        part_ref[used] = last_refs[0][...]
    else:
        other_chip.wait_recv()
        part_ref[used] = low_sum(last_refs[0][...], far_came_ref[...])
    begin(late)

    def both_step(step, carry):
        early_step(step, carry)
        advance(late, step - begin_late)
        return carry

    def middle_step(step, carry):
        pass_on(early, step)
        advance(late, step + size - 1 - begin_late)
        bucket_round(size - 2 + step - 1)
        return carry

    def end_step(step, carry):
        pass_on(early, step)
        pass_on(late, step - begin_late)
        bucket_round(size - 2 + step - 1)
        return carry

    late_passed = 0
    if begin_late < size - 1:
        lax.fori_loop(begin_late + 1, size - 1, both_step, 0)
        turn(early)
        advance(late, size - 1 - begin_late)
        lax.fori_loop(1, begin_late, middle_step, 0)
        pass_on(early, begin_late)
        turn(late)
        bucket_round(size - 2 + begin_late - 1)
        lax.fori_loop(begin_late + 1, size - 1, end_step, 0)
        late_passed = size - 2 - begin_late
    else:
        lax.fori_loop(1, size - 1, middle_step, 0)
        turn(late)
    if size == 2:
        lax.fori_loop(0, units, bucket_unit, 0)

    features = gain_refs[0].shape[1]
    per_gain = features // LANES
    gain_rows = len(gain_refs) * per_gain
    small_ref[...] = jnp.zeros_like(small_ref)
    for i, ref in enumerate(gain_refs):
        total = jnp.sum(ref[...], axis=0, keepdims=True)
        for c in range(per_gain):
            at = i * per_gain + c
            small_ref[at : at + 1, :] = total[:, c * LANES : (c + 1) * LANES]
    for r in range(rows_used):
        block_sums = bucket_ref[r].reshape(LANES, LANES).T
        at = gain_rows + r
        small_ref[at : at + 1, :] = jnp.sum(block_sums, axis=0, keepdims=True)

    def near_copy(t):
        return remote(
            small_ref,
            near_ref.at[row],
            small_sems.at[0, t],
            small_sems.at[1, t],
            (me, (row + t) % peers),
        )

    def far_copy(t):
        return remote(
            far_ref.at[me],
            far_ref.at[me],
            small_sems.at[2, t],
            small_sems.at[3, t],
            ((me + t) % size, row),
        )

    for t in range(1, peers):
        near_copy(t).start()
    near_ref[pl.ds(row, 1)] = small_ref[...][None]
    for t in range(1, peers):
        near_copy(t).wait_recv()
    own = rows_used // peers
    total, sums = None, None
    for k in range(peers):
        gains = near_ref[k, :gain_rows]
        mine = near_ref[k, pl.ds(gain_rows + own * share_place(row, k, peers), own)]
        total = gains if total is None else total + gains
        sums = mine if sums is None else sums + mine
    small_ref_rows = far_ref.shape[1]
    far_ref[pl.ds(me, 1)] = jnp.concatenate(
        [total, sums, jnp.zeros((small_ref_rows - gain_rows - own, LANES), F32)], axis=0
    )[None]

    def far_start(t, carry):
        far_copy(t).start()
        return carry

    lax.fori_loop(1, size, far_start, 0)

    def late_step(step, carry):
        pass_on(late, step)
        return carry

    lax.fori_loop(1 + late_passed, size - 1, late_step, 0)

    def far_wait(t, carry):
        far_copy(t).wait()
        return carry

    lax.fori_loop(1, size, far_wait, 0)

    def far_add(k, total):
        return total + far_ref[k]

    small_out_ref[...] = lax.fori_loop(1, size, far_add, far_ref[0])
    for i, way in ready + early + late:
        out_copy(i, way, size - 2).wait_recv()

    for t in range(1, peers):
        near_copy(t).wait_send()
    if other_chip is not None:
        other_chip.wait_send()
    for i, way in early + late:
        first_copy(i, way).wait_send()

    def sent(step, carry):
        for i, way in early + late:
            next_copy(i, way, step).wait_send()
        return carry

    lax.fori_loop(1, size - 1, sent, 0)

    def sent_out(step, carry):
        for i, way in ready + early + late:
            out_copy(i, way, step).wait_send()
        return carry

    lax.fori_loop(0, size - 1, sent_out, 0)


def tail_sums(size, peers, buckets, heads, blocks, terms, last, ids, ds, gains):
    assert peers in (2, 4)
    grain = 2 * 16 * size
    features = last[0].shape[1]
    rows = [size * 2 * b.shape[1] for b in blocks]
    rows += [arrays[0].shape[0] for arrays in terms]
    rows.append(last[0].shape[0])
    padded = [r + -r % grain for r in rows]
    parts = [[b] for b in blocks]
    for arrays, r, p in zip(terms, rows[len(blocks) :], padded[len(blocks) :]):
        parts.append([jnp.pad(a, ((0, p - r), (0, 0))) for a in arrays])
    flat = [a for arrays in parts for a in arrays]
    lines = peers * (-(-heads * buckets // LANES))
    small = len(gains) * features // LANES + lines
    small = shape((small + -small % 8, LANES), F32)
    vmem, hbm = pl.BlockSpec(memory_space=pltpu.VMEM), pl.BlockSpec(memory_space=pl.ANY)
    steps = pltpu.SemaphoreType.DMA((len(rows), 2, size - 1))

    def ring_slots(i, steps):
        if i < len(blocks):
            return pltpu.VMEM((2, 1, 16, LANES), BF16)
        return pltpu.VMEM((2, *steps, padded[i] // (2 * size), features), BF16)

    *sums, small = pl.pallas_call(
        functools.partial(
            tail_kernel, size, peers, buckets, heads, len(blocks), [len(a) for a in parts]
        ),
        in_specs=[
            *[vmem] * (len(flat) + 1),
            *[hbm] * (len(last) - 1),
            vmem,
            hbm,
            *[vmem] * len(gains),
        ],
        out_specs=[vmem] * (len(rows) + 1),
        out_shape=[*[shape((p, features), BF16) for p in padded], small],
        scratch_shapes=[
            *[ring_slots(i, (size - 1,)) for i in range(len(rows))],
            *[ring_slots(i, ()) for i in range(len(rows))],
            pltpu.VMEM((rows[-1], features), BF16),
            pltpu.VMEM((padded[-1], features), BF16),
            pltpu.VMEM(ds.shape, BF16),
            pltpu.VMEM((lines, LANES // buckets, buckets, LANES), F32),
            pltpu.VMEM(small.shape, F32),
            pltpu.VMEM((peers, *small.shape), F32),
            pltpu.VMEM((size, *small.shape), F32),
            steps,
            steps,
            steps,
            steps,
            pltpu.SemaphoreType.DMA((4, max(size, peers))),
            pltpu.SemaphoreType.DMA((2,)),
            pltpu.SemaphoreType.DMA((1,)),
        ],
        compiler_params=pltpu.CompilerParams(
            vmem_limit_bytes=VMEM_BYTES, collective_id=0, has_side_effects=True
        ),
        cost_estimate=cost(),
        name="tail_sums",
    )(*flat, *last, ids, ds, *gains)
    return [total[:r] for total, r in zip(sums, rows)], small


def swap(array, bit, size):
    return lax.ppermute(array, "mp", [(i, i ^ bit) for i in range(size)])


def after(array, *others):
    return lax.optimization_barrier((array, others))[0]


def shards(
    decoder_rows,
    memory_rows,
    decoder_token_length,
    memory_length,
    bucket_ids,
    relative_bucket_bias,
    self_gain,
    self_query,
    self_key,
    self_value,
    self_out,
    cross_gain,
    cross_query,
    cross_key,
    cross_value,
    cross_out,
    hidden_gain,
    widen_weight,
    narrow_weight,
    layer_cotangent,
):
    dp_size = lax.axis_size("dp")
    mp_size = lax.axis_size("mp")
    me = lax.axis_index("mp")
    doc, features = decoder_rows.shape
    slots = memory_rows.shape[0]
    cols = self_query.shape[1]
    heads = cols // HEAD_DIM
    buckets = relative_bucket_bias.shape[0]
    order = [*range(1, mp_size, 2), *range(0, mp_size, 2)]

    doc_length = lax.dynamic_index_in_dim(decoder_token_length, me, keepdims=False)
    doc_memory = lax.dynamic_index_in_dim(memory_length, me)
    position = jnp.arange(doc, dtype=jnp.int32)
    allowed = (position[:, None] <= position[None, :]) & (position[:, None] < doc_length)
    ids = jnp.where(allowed, bucket_ids.T, buckets)
    own_self = pack(
        (self_query.T, False),
        (self_key.T, False),
        (self_value.T, False),
        (self_out, False),
        (relative_bucket_bias.T, False),
    )
    own_cross = pack(
        (cross_query.T, False), (cross_key.T, False), (cross_value.T, False), (cross_out, False)
    )
    own_hidden = pack((widen_weight, True), (narrow_weight, False))

    def first_hops(own):
        shares, bit = {0: own}, mp_size // 2
        while bit > 1:
            for j in list(shares):
                shares[j | bit] = swap(shares[j], bit, mp_size)
            bit //= 2
        return shares

    def last_hop(shares, *others):
        if 1 not in shares:
            shares[1] = swap(shares[0], 1, mp_size)
        for j in range(2, mp_size, 2):
            shares[j] = after(shares[j], *others)
            shares[j | 1] = swap(shares[j], 1, mp_size)
        return shares

    near_self = first_hops(own_self)
    near_self[1] = swap(own_self, 1, mp_size)
    memory_rows = after(memory_rows, own_self)
    w_self = last_hop(near_self, own_cross, own_hidden, ids)
    w_self = [w_self[j] for j in order]
    near_cross = first_hops(own_cross)
    near_hidden = first_hops(own_hidden)
    near_hidden[1] = swap(own_hidden, 1, mp_size)
    memory_seen = lax.all_to_all(
        memory_rows.reshape(dp_size, slots // dp_size, features), "dp", 0, 0
    ).reshape(slots, features)

    gain_self = self_gain.astype(F32)[None]
    gain_cross = cross_gain.astype(F32)[None]
    gain_hidden = hidden_gain.astype(F32)[None]

    *saved_self, after_self = self_forward(heads, buckets, decoder_rows, gain_self, w_self, ids)
    w_cross = last_hop(near_cross, after_self)
    w_cross = [w_cross[j] for j in order]
    *saved_cross, after_cross = cross_forward(
        heads, after_self, gain_cross, memory_seen, doc_memory, w_cross
    )

    before, wide_sums, narrow_sums, w_hidden = (), [], [], near_hidden
    for j in range(0, mp_size, 2):
        wide_sum, narrow_sum, *before = feed_forward(
            after_cross,
            gain_hidden,
            layer_cotangent,
            [w_hidden[j + 1], w_hidden[j]],
            before,
            j == mp_size - 2,
        )
        wide_sums.append(wide_sum)
        narrow_sums.append(narrow_sum)
        if j == 0:
            w_hidden = last_hop(near_hidden, before[0])
    layer_output, grad_after_cross, branch, hidden_gain_grad = before

    scattered, hops = wide_sums, narrow_sums[1:]
    if wide_sums[0].shape[0] % (2 * 16 * dp_size):
        scattered, hops = [], wide_sums[1:] + narrow_sums[1:]
    *sums, grad_memory, grad_after_self, branch, cross_gain_grad = cross_backward(
        heads,
        dp_size,
        after_self,
        gain_cross,
        memory_seen,
        doc_memory,
        branch,
        grad_after_cross,
        saved_cross,
        w_cross,
        scattered,
        hops,
    )
    came, sums = sums[: len(hops)], sums[len(hops) :]
    if scattered:
        blocks, terms, cross_sums = sums[:1], [narrow_sums[:1] + came], sums[1:]
    else:
        blocks, cross_sums = [], sums
        hidden = [wide_sums[0], narrow_sums[0]], came
        terms = [[jnp.concatenate(both, axis=0) for both in hidden if both]]
    memory_grad = lax.all_to_all(
        grad_memory.reshape(dp_size, slots // dp_size, features), "dp", 0, 0
    ).reshape(slots, features)

    *sums, score_grads, input_grad, self_gain_grad = self_backward(
        heads,
        decoder_rows,
        gain_self,
        branch,
        grad_after_self,
        saved_self,
        w_self,
        cross_sums[1:],
    )
    cross_sums[1:], last = sums[: len(cross_sums) - 1], sums[len(cross_sums) - 1 :]
    (*hidden, sum_cross, sum_self), small = tail_sums(
        dp_size,
        mp_size,
        buckets,
        heads,
        blocks,
        terms + [cross_sums],
        last,
        ids,
        score_grads,
        (self_gain_grad, cross_gain_grad, hidden_gain_grad),
    )
    wide_grad, narrow_grad, self_grads, cross_grads = finish(
        *(hidden if scattered else jnp.split(hidden[0], 2)), sum_cross, sum_self
    )
    gain_rows = 3 * features // LANES
    gains = small[:gain_rows].reshape(3, features)
    lines = -(-heads * buckets // LANES)
    sums = small[gain_rows : gain_rows + lines, : heads // lines * buckets]
    position_grad = sums.reshape(heads, buckets).T

    return (
        layer_output,
        input_grad,
        memory_grad,
        position_grad,
        gains[0],
        *[grad.T for grad in self_grads[:3]],
        self_grads[3],
        gains[1],
        *[grad.T for grad in cross_grads[:3]],
        cross_grads[3],
        gains[2],
        wide_grad,
        narrow_grad,
    )


def solution(mesh):
    return jax.shard_map(
        shards,
        mesh=mesh,
        in_specs=(
            P(("dp", "mp"), None),
            P(("dp", "mp"), None),
            P("dp"),
            P("dp"),
            P(),
            P(None, "mp"),
            P(),
            P(None, "mp"),
            P(None, "mp"),
            P(None, "mp"),
            P("mp", None),
            P(),
            P(None, "mp"),
            P(None, "mp"),
            P(None, "mp"),
            P("mp", None),
            P(),
            P(None, "mp"),
            P("mp", None),
            P(("dp", "mp"), None),
        ),
        out_specs=(
            P(("dp", "mp"), None),
            P(("dp", "mp"), None),
            P(("dp", "mp"), None),
            P(None, "mp"),
            P(),
            P(None, "mp"),
            P(None, "mp"),
            P(None, "mp"),
            P("mp", None),
            P(),
            P(None, "mp"),
            P(None, "mp"),
            P(None, "mp"),
            P("mp", None),
            P(),
            P(None, "mp"),
            P("mp", None),
        ),
        check_vma=False,
    )
```

```python
import functools

import jax
import jax.numpy as jnp
from jax import lax
from jax.experimental import pallas as pl
from jax.experimental.pallas import tpu as pltpu
from jax.sharding import PartitionSpec as P

HEAD_DIM = 64
NORM_EPS = 1e-06
MASKED = -1e30
SCALE = HEAD_DIM**-0.5
BF16 = jnp.bfloat16
F32 = jnp.float32
LANES = 128
TABLE_ROWS = 16
TILE_ROWS = 16
LARGEST_SUM = 1e30
LATE_STEP = 4
HEAD_BLOCK = 256
BLOCK_HEADS = HEAD_BLOCK // HEAD_DIM
Q_BLOCK = 256
K_BLOCK = 512
FORWARD_K_BLOCK = 256
HIDDEN_BLOCK = 256
MEMORY_BLOCK = 768
FINISH_BLOCK = 384
ROW_BLOCK = 128
VMEM_BYTES = 56 * 1024 * 1024
GELU_ROOT = 0.7978845608028654
GELU_CUBE = 0.044715


def dot_nn(a, b):
    return lax.dot_general(a, b, (((1,), (0,)), ((), ())), preferred_element_type=F32)


def dot_nt(a, b):
    return lax.dot_general(a, b, (((1,), (1,)), ((), ())), preferred_element_type=F32)


def dot_tn(a, b):
    return lax.dot_general(a, b, (((0,), (0,)), ((), ())), preferred_element_type=F32)


def flip(a):
    return a.astype(F32).T.astype(BF16)


def spans(size, step):
    return [slice(i, i + step) for i in range(0, size, step)]


def norm_scale(rows):
    return lax.rsqrt(jnp.mean(rows * rows, axis=-1, keepdims=True) + NORM_EPS)


def norm_into(normed_ref, rows_ref, gain_ref):
    for span in spans(rows_ref.shape[0], ROW_BLOCK):
        rows = rows_ref[span].astype(F32)
        normed_ref[span] = (rows * norm_scale(rows) * gain_ref[...]).astype(BF16)


def norm_back_into(span, grad, out_ref, low_ref, gain_grad_ref, rows_ref, gain_ref, add_ref):
    rows = rows_ref[span].astype(F32)
    scale = norm_scale(rows)
    unit = rows * scale
    grad_unit = grad * gain_ref[...]
    mean = jnp.mean(grad_unit * unit, axis=-1, keepdims=True)
    out = add_ref[span].astype(F32) + scale * (grad_unit - unit * mean)
    out_ref[span] = out
    if low_ref is not None:
        low_ref[span] = out.astype(BF16)
    gain_grad_ref[...] += jnp.sum((grad * unit).reshape(-1, 8, rows.shape[1]), axis=0)


def gelu_and_slope(v):
    square = v * v
    bend = jnp.tanh(GELU_ROOT * (v + GELU_CUBE * v * square))
    half = 0.5 * (1.0 + bend)
    slope = half + 0.5 * v * (1.0 - bend * bend) * GELU_ROOT * (1.0 + 3.0 * GELU_CUBE * square)
    return v * half, slope


def lane_block(start):
    return pl.ds(pl.multiple_of(start, LANES), LANES)


def extra_lanes(rows, allowed):
    lane = lax.broadcasted_iota(jnp.int32, (rows, LANES), 1) % HEAD_DIM
    first = MASKED if allowed is None else jnp.where(allowed, 0.0, MASKED)
    return jnp.where(lane == 0, first, jnp.where(lane < 4, 1.0, 0.0)).astype(BF16)


def pick(which, block, other):
    lane = lax.broadcasted_iota(jnp.int32, block.shape, 1)
    return jnp.where((lane < HEAD_DIM) == (which == 0), block, other)


def half_rows(which):
    return slice(which * HEAD_DIM, (which + 1) * HEAD_DIM)


def split(values):
    high = values.astype(BF16).astype(F32)
    rest = values - high
    middle = rest.astype(BF16).astype(F32)
    return high, middle, rest - middle


def with_extra(which, block_t, masked, minus):
    columns = block_t.shape[1]
    row = lax.broadcasted_iota(jnp.int32, (HEAD_DIM, columns), 0)
    extra = jnp.where(row == 0, 1.0 if masked else 0.0, 0.0)
    if minus is not None:
        for i, part in enumerate(split(minus)):
            extra = jnp.where(row == i + 1, -part, extra)
    own = block_t[half_rows(which)]
    return jnp.concatenate([own, extra] if which == 0 else [extra, own], axis=0).astype(BF16)


def bias_block(table_ref, ids_ref, index, rows, start):
    row = jnp.broadcast_to(table_ref[pl.ds(index, 1), :], (rows, LANES))
    return jnp.concatenate(
        [
            jnp.take_along_axis(row, ids_ref[:rows, c : c + LANES], axis=1)
            for c in range(start, start + Q_BLOCK, LANES)
        ],
        axis=1,
    )


def ring_place(me, size):
    return jnp.where(me % 2 == 0, me // 2, size - 1 - me // 2)


def ring_device(place, size):
    return jnp.where(place < size // 2, 2 * place, 2 * (size - 1 - place) + 1)


def ring_ways(size):
    me = lax.axis_index("dp")
    place = ring_place(me, size)
    return (
        (place, ring_device((place + 1) % size, size)),
        (size - 1 - place, ring_device((place + size - 1) % size, size)),
    )


def differing(row, bit):
    return row + bit - 2 * bit * ((row // bit) % 2)


def remote(source, target, send_sem, recv_sem, device):
    return pltpu.make_async_remote_copy(
        src_ref=source,
        dst_ref=target,
        send_sem=send_sem,
        recv_sem=recv_sem,
        device_id=device,
        device_id_type=pl.DeviceIdType.MESH,
    )


def greet(bits, devices=()):
    me, row = lax.axis_index("dp"), lax.axis_index("mp")
    barrier = pltpu.get_barrier_semaphore()
    others = [(me, differing(row, bit)) for bit in bits] + [(device, row) for device in devices]
    for other in others:
        pl.semaphore_signal(
            barrier, inc=1, device_id=other, device_id_type=pl.DeviceIdType.MESH
        )
    pl.semaphore_wait(barrier, len(others))


def to_differing(bit, source, target, sems):
    me, row = lax.axis_index("dp"), lax.axis_index("mp")
    return remote(source, target, sems.at[0], sems.at[1], (me, differing(row, bit)))


class Scatter:
    def __init__(self, size, part, slots, done, send, came):
        self.size, self.part, self.slots, self.done = size, part, slots, done
        self.send, self.came = send, came
        self.ways, self.row = ring_ways(size), lax.axis_index("mp")

    def span(self, way, number):
        rows = self.slots.shape[3]
        return pl.ds(pl.multiple_of((way * self.size + number) * rows, 16), rows)

    def copy(self, way, step, source):
        return remote(
            source,
            self.slots.at[way, step],
            self.send.at[way, step],
            self.came.at[way, step],
            (self.ways[way][1], self.row),
        )

    def first(self, way):
        return self.copy(way, 0, self.part.at[:, self.span(way, self.ways[way][0])])

    def next(self, way, step):
        return self.copy(way, step, self.slots.at[way, step - 1])

    def begin(self):
        for way in range(2):
            self.first(way).start()

    def total(self, way, step):
        self.copy(way, step, self.slots.at[way, step]).wait_recv()
        span = self.span(way, (self.ways[way][0] - step - 1 + self.size) % self.size)
        return low_sum(self.slots[way, step], self.part[:, span])

    def advance(self, step):
        for way in range(2):
            self.slots[way, step - 1] = self.total(way, step - 1)
            self.next(way, step).start()

    def turn(self):
        for way in range(2):
            self.done[way] = self.total(way, self.size - 2)

    def wait_sent(self):
        for way in range(2):
            self.first(way).wait_send()

        def sent(step, carry):
            for way in range(2):
                self.next(way, step).wait_send()
            return carry

        lax.fori_loop(1, self.size - 1, sent, 0)


def low_sum(a, b):
    return (a.astype(F32) + b.astype(F32)).astype(BF16)


class Stack:
    def __init__(self, sources, stack_ref, sems, kinds, rows):
        features = stack_ref.shape[0] // kinds
        self.copies = [
            [
                pltpu.make_async_copy(
                    source.at[pl.ds(kind * rows, rows)],
                    stack_ref.at[pl.ds(kind * features + p * rows, rows)],
                    sems.at[p, kind],
                )
                for p, source in enumerate(sources)
            ]
            for kind in range(kinds)
        ]

    def start(self):
        for copies in self.copies:
            for copy in copies:
                copy.start()

    def wait(self, *kinds):
        for kind in kinds:
            for copy in self.copies[kind]:
                copy.wait()


def table_copies(sources, tables_ref, sems, kinds):
    start = sources[0].shape[0] - TABLE_ROWS
    return [
        pltpu.make_async_copy(
            source.at[pl.ds(start, TABLE_ROWS)], tables_ref.at[p], sems.at[p, kinds]
        )
        for p, source in enumerate(sources)
    ]


def table_into(table_ref, tables_ref, heads, buckets):
    for p in range(tables_ref.shape[0]):
        rows = tables_ref[p, :, :LANES].astype(F32)
        lane = lax.broadcasted_iota(jnp.int32, rows.shape, 1)
        rows = jnp.where(lane < buckets, rows, MASKED)
        for h in range(heads):
            table_ref[p * heads + h : p * heads + h + 1, :] = rows[h : h + 1, :]


def self_forward_kernel(heads, buckets, shares, rows_ref, gain_ref, ids_ref, *refs):
    sources = refs[:shares]
    q_ref, k_ref, v_ref, mixed_ref, lse_ref, bias_ref, out_ref = refs[shares : shares + 7]
    w_ref, tables_ref, table_ref, normed_ref, sems = refs[shares + 7 :]
    step = pl.program_id(0)
    doc, features = rows_ref.shape
    stack = Stack(sources, w_ref, sems, 4, heads * HEAD_DIM)

    @pl.when(step == 0)
    def _():
        stack.start()
        tables = table_copies(sources, tables_ref, sems, 4)
        for copy in tables:
            copy.start()
        norm_into(normed_ref, rows_ref, gain_ref)
        out_ref[...] = rows_ref[...].astype(F32)
        for copy in tables:
            copy.wait()
        table_into(table_ref, tables_ref, heads, buckets)
        stack.wait(0, 1, 2, 3)

    def weights(kind):
        start = pl.multiple_of(kind * features + step * HEAD_BLOCK, HEAD_BLOCK)
        return w_ref[pl.ds(start, HEAD_BLOCK)]

    for kind, ref in enumerate((q_ref, k_ref, v_ref)):
        ref[...] = dot_nt(normed_ref[...], weights(kind)).astype(BF16)
    none = jnp.zeros((doc, LANES), BF16)
    for pair in range(BLOCK_HEADS // 2):
        lanes = slice(pair * LANES, (pair + 1) * LANES)
        k, v_t = k_ref[:, lanes], flip(v_ref[:, lanes])
        q_t = flip(q_ref[:, lanes].astype(F32) * SCALE)
        k_of = [pick(which, k, none) for which in range(2)]
        for span in spans(doc, Q_BLOCK):
            rows, mixed = span.stop, []
            for which in range(2):
                h = 2 * pair + which
                bias = bias_block(table_ref, ids_ref, step * BLOCK_HEADS + h, rows, span.start)
                bias_ref[h, :rows, span] = bias.astype(BF16)
                s = dot_nn(k_of[which][:rows], q_t[:, span]) + bias
                top = jnp.max(s, axis=0, keepdims=True)
                p = jnp.exp(s - top)
                total = jnp.sum(p, axis=0, keepdims=True)
                mixed.append(dot_nn(v_t[half_rows(which), :rows], p.astype(BF16)) / total)
                lse_ref[0, h : h + 1, span] = top + jnp.log(total)
            mixed_ref[span, lanes] = jnp.concatenate(mixed, axis=0).T.astype(BF16)
    out_ref[...] += dot_nn(mixed_ref[...], weights(3))


def self_backward_kernel(heads, shares, *refs):
    count = shares // 2
    rows_ref, gain_ref, branch_ref, add_ref = refs[:4]
    q_ref, k_ref, v_ref, mixed_ref, lse_ref, bias_ref = refs[4:10]
    sources, refs = refs[10 : 10 + shares], refs[10 + shares :]
    hop_in, hop_out, refs = refs[: count - 1], refs[count - 1 : 2 * count - 2], refs[2 * count - 2 :]
    sums, refs = refs[:count], refs[count:]
    ds_ref, out_ref, gain_grad_ref = refs[:3]
    w_ref, normed_ref, g_ref, grad_ref, back_ref, give_ref, keep_ref, came_ref = refs[3:11]
    sems, swap_sems, hop_sems = refs[11:]
    step = pl.program_id(0)
    doc, features = rows_ref.shape
    half = features // 2
    stack = Stack(sources, w_ref, sems, 4, heads * HEAD_DIM)
    swap = to_differing(1, give_ref, came_ref, swap_sems)
    hops = [
        to_differing(2, source, target, hop_sems) for source, target in zip(hop_in, hop_out)
    ]

    @pl.when(step == 0)
    def _():
        stack.start()
        greet([1, 2][:count])
        for hop in hops:
            hop.start()
        norm_into(normed_ref, rows_ref, gain_ref)
        stack.wait(3)

    start = pl.multiple_of(3 * features + step * HEAD_BLOCK, HEAD_BLOCK)
    g_ref[...] = dot_nt(branch_ref[...], w_ref[pl.ds(start, HEAD_BLOCK)]).astype(BF16)
    none = jnp.zeros((doc, LANES), BF16)
    ones = extra_lanes(doc, None)
    for pair in range(BLOCK_HEADS // 2):
        lanes = lane_block(step * HEAD_BLOCK + pair * LANES)
        q, k, v = q_ref[:, lanes], k_ref[:, lanes], v_ref[:, lanes]
        g = g_ref[:, pair * LANES : (pair + 1) * LANES]
        q_t, k_t = q.astype(F32).T * SCALE, flip(k)
        g_t = g.astype(F32).T
        inner = g_t * mixed_ref[:, lanes].astype(F32).T
        per_head = []
        for which in range(2):
            h = 2 * pair + which
            minus = jnp.sum(inner[half_rows(which)], axis=0, keepdims=True)
            per_head.append(
                (
                    pick(which, k, ones),
                    pick(which, v, ones),
                    with_extra(which, q_t, False, lse_ref[0, h : h + 1, :]),
                    with_extra(which, g_t, False, minus),
                    pick(which, q, none),
                    pick(which, g, none),
                )
            )
        grad_k = grad_v = None
        for span in spans(doc, Q_BLOCK):
            rows, grad_q, part_k, part_v = span.stop, [], None, None
            for which, (k_of, v_of, q_with, g_with, q_of, g_of) in enumerate(per_head):
                h = 2 * pair + which
                s = dot_nn(k_of[:rows], q_with[:, span])
                p = jnp.exp(s + bias_ref[h, :rows, span].astype(F32))
                ds = (p * dot_nn(v_of[:rows], g_with[:, span])).astype(BF16)
                ds_ref[h, :rows, span] = ds
                grad_q.append(dot_nn(k_t[half_rows(which), :rows], ds))
                to_v = dot_nn(p.astype(BF16), g_of[span])
                to_k = dot_nn(ds, q_of[span])
                part_v = to_v if part_v is None else part_v + to_v
                part_k = to_k if part_k is None else part_k + to_k
            grad_q = (jnp.concatenate(grad_q, axis=0) * SCALE).T
            grad_ref[span, lanes] = grad_q.astype(BF16)
            if grad_v is not None:
                part_v = jnp.concatenate(
                    [part_v[: span.start] + grad_v, part_v[span.start :]], axis=0
                )
                part_k = jnp.concatenate(
                    [part_k[: span.start] + grad_k, part_k[span.start :]], axis=0
                )
            grad_v, grad_k = part_v, part_k
        k_lanes = lane_block(features + step * HEAD_BLOCK + pair * LANES)
        v_lanes = lane_block(2 * features + step * HEAD_BLOCK + pair * LANES)
        grad_ref[:, k_lanes] = (grad_k * SCALE).astype(BF16)
        grad_ref[:, v_lanes] = grad_v.astype(BF16)

    @pl.when(step == pl.num_programs(0) - 1)
    def _():
        stack.wait(0, 1, 2)
        def weight_grads(ref, columns):
            for kind in range(3):
                kind_columns = slice(kind * features + columns.start, kind * features + columns.stop)
                ref[kind] = dot_tn(grad_ref[:, kind_columns], normed_ref[...]).astype(BF16)
            ref[3] = dot_tn(mixed_ref[:, columns], branch_ref[...]).astype(BF16)

        weight_grads(give_ref, slice(0, half))
        swap.start()
        weight_grads(keep_ref, slice(half, features))
        gain_grad_ref[...] = jnp.zeros_like(gain_grad_ref)
        back_ref[...] = dot_nn(grad_ref[...], w_ref[: 3 * features])
        for span in spans(doc, ROW_BLOCK):
            norm_back_into(
                span, back_ref[span], out_ref, None, gain_grad_ref, rows_ref, gain_ref, add_ref
            )
        swap.wait_recv()
        rows = half // count
        for share, sums_ref in enumerate(sums):
            for kind in range(4):
                span = slice(share * rows, (share + 1) * rows)
                to = slice(kind * rows, (kind + 1) * rows)
                sums_ref[to] = low_sum(keep_ref[kind, span], came_ref[kind, span])
        swap.wait_send()
        for hop in hops:
            hop.wait()


def cross_forward_kernel(heads, shares, length_ref, rows_ref, gain_ref, memory_ref, *refs):
    sources = refs[:shares]
    q_ref, k_ref, v_ref, mixed_ref, lse_ref, out_ref = refs[shares : shares + 6]
    w_ref, normed_ref, extra_ref, p_ref, mix_ref, sems = refs[shares + 6 :]
    step = pl.program_id(0)
    (doc, features), slots = rows_ref.shape, memory_ref.shape[0]
    stack = Stack(sources, w_ref, sems, 4, heads * HEAD_DIM)

    @pl.when(step == 0)
    def _():
        stack.start()
        norm_into(normed_ref, rows_ref, gain_ref)
        out_ref[...] = rows_ref[...]
        slot = lax.broadcasted_iota(jnp.int32, (slots, LANES), 0)
        extra_ref[...] = extra_lanes(slots, slot < length_ref[0])
        stack.wait(0, 1, 2, 3)

    def weights(kind):
        start = pl.multiple_of(kind * features + step * HEAD_BLOCK, HEAD_BLOCK)
        return w_ref[pl.ds(start, HEAD_BLOCK)]

    q_ref[...] = dot_nt(normed_ref[...], weights(0)).astype(BF16)
    k_ref[...] = dot_nt(memory_ref[...], weights(1)).astype(BF16)
    v_ref[...] = dot_nt(memory_ref[...], weights(2)).astype(BF16)

    units = [
        (pair, which, span)
        for pair in range(BLOCK_HEADS // 2)
        for span in spans(doc, Q_BLOCK)
        for which in range(2)
    ]
    ones = jnp.ones((TILE_ROWS, slots), BF16)
    keys = spans(slots, FORWARD_K_BLOCK)

    def lanes_of(pair):
        return slice(pair * LANES, (pair + 1) * LANES)

    def key_side(pair, which):
        return pick(which, k_ref[:, lanes_of(pair)], extra_ref[...])

    def write(pair, which, span, top, total, mixed):
        h = 2 * pair + which
        lse_ref[0, h : h + 1, span] = top + jnp.log(total)
        mix_ref[half_rows(which)] = mixed / total
        if which == 1:
            mixed_ref[span, lanes_of(pair)] = mix_ref[...].T.astype(BF16)

    v_t = [flip(v_ref[:, lanes_of(p)]) for p in range(BLOCK_HEADS // 2)]
    q_t = [q_ref[:, lanes_of(p)].astype(F32).T * SCALE for p in range(BLOCK_HEADS // 2)]

    def begin(unit):
        pair, which, span = unit
        k_of = key_side(pair, which)
        s = dot_nn(k_of[keys[0]], with_extra(which, q_t[pair][:, span], True, None))
        top = jnp.max(s, axis=0, keepdims=True)
        return k_of, s, top, with_extra(which, q_t[pair][:, span], True, top)

    worst = jnp.zeros((1, Q_BLOCK), F32)
    ahead = begin(units[0])
    for i, (pair, which, span) in enumerate(units):
        (k_of, s, top, q_with), slot = ahead, i % 2
        p_ref[slot, keys[0]] = jnp.exp(s - top).astype(BF16)
        for rows in keys[1:]:
            p_ref[slot, rows] = jnp.exp(dot_nn(k_of[rows], q_with)).astype(BF16)
        if i + 1 < len(units):
            ahead = begin(units[i + 1])
        value_side = jnp.concatenate([v_t[pair][half_rows(which)], ones], axis=0)
        mixed = dot_nn(value_side, p_ref[slot])
        total = mixed[HEAD_DIM : HEAD_DIM + 1]
        worst = jnp.maximum(worst, total)
        write(pair, which, span, top, total, mixed[:HEAD_DIM])

    @pl.when(jnp.max(worst) > LARGEST_SUM)
    def _():
        for pair, which, span in units:
            q_with = with_extra(
                which, q_ref[:, lanes_of(pair)].astype(F32).T[:, span] * SCALE, True, None
            )
            k_of = key_side(pair, which)
            s = [dot_nn(k_of[rows], q_with) for rows in keys]
            top = functools.reduce(jnp.maximum, [jnp.max(c, axis=0, keepdims=True) for c in s])
            total = jnp.zeros_like(top)
            for rows, chunk in zip(keys, s):
                p = jnp.exp(chunk - top)
                total = total + jnp.sum(p, axis=0, keepdims=True)
                p_ref[0, rows] = p.astype(BF16)
            mixed = dot_nn(flip(v_ref[:, lanes_of(pair)])[half_rows(which)], p_ref[0])
            write(pair, which, span, top, total, mixed)

    out_ref[...] += dot_nn(mixed_ref[...], weights(3))


def cross_backward_kernel(heads, shares, size, scattered, hops_wanted, length_ref, *refs):
    gain_ref, branch_ref, q_ref, mixed_ref, lse_ref = refs[:5]
    rows_in, memory_in, add_in, k_in, v_in = refs[5:10]
    sources = refs[10 : 10 + shares]
    count = shares // 2
    refs = refs[10 + shares :]
    scatter_in, refs = refs[:scattered], refs[scattered:]
    hidden_in, refs = refs[:hops_wanted], refs[hops_wanted:]
    hidden_out, refs = refs[:hops_wanted], refs[hops_wanted:]
    if scattered:
        scatter_out, refs = refs[0], refs[1:]
        (part_ref, ring_slots, done_ref, scatter_came), refs = refs[-8:-4], refs[:-8] + refs[-4:]
        (ring_send, ring_came, part_sems, done_sems), refs = refs[-4:], refs[:-4]
        scatter = Scatter(size, part_ref, ring_slots, done_ref, ring_send, ring_came)
        part_loads = [
            pltpu.make_async_copy(source, part_ref.at[i], part_sems.at[i])
            for i, source in enumerate(scatter_in)
        ]
        for copy in part_loads:
            copy.start()
    sums, refs = refs[:count], refs[count:]
    memory_out, out_ref, low_ref, gain_grad_ref = refs[:4]
    rows_ref, memory_ref, add_ref, k_ref, v_ref = refs[4:9]
    (
        w_ref,
        normed_ref,
        extra_ref,
        g_ref,
        grad_q_ref,
        grad_ref,
        ds_ref,
        give_ref,
        keep_ref,
        came_ref,
        memory_grad_ref,
        back_ref,
        sems,
        load_sems,
        key_sems,
        out_sems,
        swap_sems,
        hop_sems,
    ) = refs[9:]
    (doc, features), slots = rows_ref.shape, memory_ref.shape[0]
    half, blocks = features // 2, features // HEAD_BLOCK
    stack = Stack(sources, w_ref, sems, 4, heads * HEAD_DIM)
    loads = [
        pltpu.make_async_copy(source, target, load_sems.at[i])
        for i, (source, target) in enumerate(
            ((memory_in, memory_ref), (rows_in, rows_ref), (add_in, add_ref))
        )
    ]

    def key_copies(b):
        lanes = pl.ds(pl.multiple_of(b * HEAD_BLOCK, HEAD_BLOCK), HEAD_BLOCK)
        return [
            pltpu.make_async_copy(source.at[:, lanes], target.at[b], key_sems.at[i, b])
            for i, (source, target) in enumerate(((k_in, k_ref), (v_in, v_ref)))
        ]

    stack.start()
    for b in range(blocks):
        for copy in key_copies(b):
            copy.start()
    for copy in loads:
        copy.start()
    greet([1, 2][:count], [way[1] for way in ring_ways(size)] if scattered else [])
    hops = [
        to_differing(2, source, target, hop_sems.at[i])
        for i, (source, target) in enumerate(zip(hidden_in, hidden_out))
    ]
    for hop in hops:
        hop.start()
    if scattered:
        for copy in part_loads:
            copy.wait()
        scatter.begin()
    slot = lax.broadcasted_iota(jnp.int32, (slots, LANES), 0)
    extra_ref[...] = extra_lanes(slots, slot < length_ref[0])
    none = jnp.zeros((doc, LANES), BF16)
    stack.wait(3)

    def one_block(step, carry):
        start = pl.multiple_of(3 * features + step * HEAD_BLOCK, HEAD_BLOCK)
        g_ref[...] = dot_nt(branch_ref[...], w_ref[pl.ds(start, HEAD_BLOCK)]).astype(BF16)
        for copy in key_copies(step):
            copy.wait()
        for pair in range(BLOCK_HEADS // 2):
            local = slice(pair * LANES, (pair + 1) * LANES)
            lanes = lane_block(step * HEAD_BLOCK + pair * LANES)
            v_lanes = lane_block(features + step * HEAD_BLOCK + pair * LANES)
            q, g = q_ref[:, lanes], g_ref[:, local]
            q_t, g_t = q.astype(F32).T * SCALE, g.astype(F32).T
            inner = g_t * mixed_ref[:, lanes].astype(F32).T
            per_head = []
            for which in range(2):
                h = 2 * pair + which
                minus = jnp.sum(inner[half_rows(which)], axis=0, keepdims=True)
                per_head.append(
                    (
                        with_extra(which, q_t, True, lse_ref[step, h : h + 1, :]),
                        with_extra(which, g_t, False, minus),
                        pick(which, q, none),
                        pick(which, g, none),
                    )
                )
            for rows in spans(slots, K_BLOCK):
                k, v, extra = k_ref[step, rows, local], v_ref[step, rows, local], extra_ref[rows]
                part_k = part_v = None
                for which, (q_with, g_with, q_of, g_of) in enumerate(per_head):
                    p = jnp.exp(dot_nn(pick(which, k, extra), q_with))
                    ds = (p * dot_nn(pick(which, v, extra), g_with)).astype(BF16)
                    ds_ref[which, rows] = ds
                    to_v = dot_nn(p.astype(BF16), g_of)
                    to_k = dot_nn(ds, q_of)
                    part_v = to_v if part_v is None else part_v + to_v
                    part_k = to_k if part_k is None else part_k + to_k
                grad_ref[rows, lanes] = (part_k * SCALE).astype(BF16)
                grad_ref[rows, v_lanes] = part_v.astype(BF16)
            k_t = flip(k_ref[step, :, local])
            grad_q = [dot_nn(k_t[half_rows(which)], ds_ref[which]) for which in range(2)]
            grad_q_ref[:, lanes] = (jnp.concatenate(grad_q, axis=0) * SCALE).T.astype(BF16)
            if scattered:
                scatter_step(1 + step * (BLOCK_HEADS // 2) + pair)
        return carry

    places = blocks * (BLOCK_HEADS // 2)

    def scatter_step(step):
        if size - 2 >= places:
            scatter.advance(step)
        elif size > 2:

            @pl.when(step <= size - 2)
            def _():
                scatter.advance(step)

    lax.fori_loop(0, blocks, one_block, 0)
    if scattered:

        def rest(step, carry):
            scatter.advance(step)
            return carry

        lax.fori_loop(min(places, size - 2) + 1, size - 1, rest, 0)
        scatter.turn()
        done_hops = [
            to_differing(2, done_ref.at[:, i], scatter_came, done_sems)
            for i in range(1, scattered)
        ]
        for hop in done_hops:
            hop.start()

    for copy in loads:
        copy.wait()
    norm_into(normed_ref, rows_ref, gain_ref)

    def weight_grads(ref, first):
        columns = slice(first, first + half)
        v_columns = slice(features + first, features + first + half)
        ref[0] = dot_tn(grad_q_ref[:, columns], normed_ref[...]).astype(BF16)
        ref[1] = dot_tn(grad_ref[:, columns], memory_ref[...]).astype(BF16)
        ref[2] = dot_tn(grad_ref[:, v_columns], memory_ref[...]).astype(BF16)
        ref[3] = dot_tn(mixed_ref[:, columns], branch_ref[...]).astype(BF16)

    weight_grads(give_ref, 0)
    swap = to_differing(1, give_ref, came_ref, swap_sems)
    swap.start()
    stack.wait(0, 1, 2)
    writes = []
    for i, rows in enumerate(spans(slots, MEMORY_BLOCK)):
        memory_grad_ref[rows] = dot_nn(
            grad_ref[rows], w_ref[features : 3 * features]
        ).astype(BF16)
        writes.append(
            pltpu.make_async_copy(memory_grad_ref.at[rows], memory_out.at[rows], out_sems.at[i])
        )
        writes[-1].start()
    weight_grads(keep_ref, half)
    gain_grad_ref[...] = jnp.zeros_like(gain_grad_ref)
    back_ref[...] = dot_nn(grad_q_ref[...], w_ref[:features])
    for span in spans(doc, ROW_BLOCK):
        norm_back_into(
            span, back_ref[span], out_ref, low_ref, gain_grad_ref, rows_ref, gain_ref, add_ref
        )
    swap.wait_recv()
    rows = half // count
    for share, sums_ref in enumerate(sums):
        for kind in range(4):
            span = slice(share * rows, (share + 1) * rows)
            to = slice(kind * rows, (kind + 1) * rows)
            sums_ref[to] = low_sum(keep_ref[kind, span], came_ref[kind, span])
    swap.wait_send()
    for copy in writes:
        copy.wait()
    for hop in hops:
        hop.wait()
    if scattered:
        for hop in done_hops:
            hop.wait()
        own = done_ref[:, 0]
        scatter_out[...] = low_sum(own, scatter_came[...]) if done_hops else own
        scatter.wait_sent()


def feed_forward_kernel(first, last, rows_ref, gain_ref, cotangent_ref, *refs):
    sources, refs = refs[:2], refs[2:]
    if not first:
        before_in, refs = refs[:2], refs[2:]
    sums, layer_ref, out_ref = refs[:2], refs[2], refs[3]
    if last:
        low_ref, gain_grad_ref = refs[4:6]
        refs = refs[2:]
    (
        wide_ref,
        narrow_ref,
        normed_ref,
        normed_t,
        cotangent_t,
        active_ref,
        grad_ref,
        give_ref,
        keep_ref,
        came_ref,
        layer_in_ref,
        back_in_ref,
        product_ref,
        even_ref,
        odd_ref,
        sems,
        before_sems,
        swap_sems,
    ) = refs[4:]
    step, steps = pl.program_id(0), pl.num_programs(0)
    half = steps // 2
    doc = rows_ref.shape[0]
    hidden = sources[0].shape[0] // 2
    copies = [
        [
            pltpu.make_async_copy(
                source.at[pl.ds(kind * hidden, hidden)],
                stack.at[pl.ds(p * hidden, hidden)],
                sems.at[p, kind],
            )
            for kind, stack in enumerate((wide_ref, narrow_ref))
        ]
        for p, source in enumerate(sources)
    ]
    loads = []
    if not first:
        loads = [
            pltpu.make_async_copy(source, target, before_sems.at[i])
            for i, (source, target) in enumerate(zip(before_in, (layer_in_ref, back_in_ref)))
        ]
    swap = to_differing(1, give_ref, came_ref, swap_sems)

    @pl.when(step == 0)
    def _():
        for pair in copies:
            for copy in pair:
                copy.start()
        for copy in loads:
            copy.start()
        greet([1])
        norm_into(normed_ref, rows_ref, gain_ref)
        for span in spans(doc, ROW_BLOCK):
            normed_t[:, span] = flip(normed_ref[span])
            cotangent_t[:, span] = flip(cotangent_ref[span])

    for p, pair in enumerate(copies):

        @pl.when(step == max(p * half - 1, 0))
        def _(pair=pair):
            for copy in pair:
                copy.wait()

    def hidden_rows(block):
        return pl.ds(pl.multiple_of(block * HIDDEN_BLOCK, HIDDEN_BLOCK), HIDDEN_BLOCK)

    def products(block, target):
        units = hidden_rows(block)
        target[0] = dot_nn(wide_ref[units], normed_t[...])
        target[1] = dot_nn(narrow_ref[units], cotangent_t[...])

    def work(now, later, kept_in, at):
        units = hidden_rows(step)
        activated, slope = gelu_and_slope(now[0])
        activated = activated.astype(BF16)
        grad = (now[1] * slope).astype(BF16)
        active_ref[units] = activated
        grad_ref[units] = grad
        products(jnp.minimum(step + 1, steps - 1), later)
        rows = hidden_rows(at)
        kept_in[0, rows] = dot_nn(grad, normed_ref[...]).astype(BF16)
        kept_in[1, rows] = dot_nn(activated, cotangent_ref[...]).astype(BF16)

    @pl.when(step == 0)
    def _():
        products(0, even_ref)

    for odd, (now, later) in enumerate(((even_ref, odd_ref), (odd_ref, even_ref))):

        @pl.when((step % 2 == odd) & (step < half))
        def _(now=now, later=later):
            work(now, later, give_ref, step)

        @pl.when((step % 2 == odd) & (step >= half))
        def _(now=now, later=later):
            work(now, later, keep_ref, step - half)

    @pl.when(step == half - 1)
    def _():
        swap.start()

    @pl.when(step == steps - 1)
    def _():
        for copy in loads:
            copy.wait()
        if last:
            gain_grad_ref[...] = jnp.zeros_like(gain_grad_ref)
        product_ref[...] = dot_tn(active_ref[...], narrow_ref[...])
        for span in spans(doc, ROW_BLOCK):
            layer = rows_ref[span] if first else layer_in_ref[span]
            layer_ref[span] = (layer + product_ref[span]).astype(layer_ref.dtype)
        product_ref[...] = dot_tn(grad_ref[...], wide_ref[...])
        for span in spans(doc, ROW_BLOCK):
            back = product_ref[span]
            if not first:
                back = back + back_in_ref[span]
            if last:
                norm_back_into(
                    span, back, out_ref, low_ref, gain_grad_ref, rows_ref, gain_ref, cotangent_ref
                )
            else:
                out_ref[span] = back
        swap.wait_recv()
        for kind, sums_ref in enumerate(sums):
            for span in spans(hidden, HIDDEN_BLOCK):
                sums_ref[span] = low_sum(keep_ref[kind, span], came_ref[kind, span])
        swap.wait_send()


def pack_kernel(flipped, *refs):
    out_ref, start = refs[-1], 0
    for source, turn in zip(refs[:-1], flipped):
        if source.shape[-1] != out_ref.shape[1] and not turn:
            out_ref[start:] = jnp.zeros((TABLE_ROWS, out_ref.shape[1]), BF16)
            out_ref[start : start + source.shape[0], : source.shape[1]] = source[...]
            continue
        rows = source.shape[1] if turn else source.shape[0]
        span = slice(start, start + rows)
        out_ref[span] = flip(source[...]) if turn else source[...]
        start += rows


def finish_kernel(*refs):
    sources, outs, refs = refs[:4], refs[4:14], refs[14:]
    ins, wides, in_sems, out_sems = refs[:4], refs[4:14], refs[14], refs[15]
    loads, writes = [], []
    for i, (source, target) in enumerate(zip(sources, ins)):
        for j, span in enumerate(spans(target.shape[0], FINISH_BLOCK)):
            loads.append(
                pltpu.make_async_copy(source.at[span], target.at[span], in_sems.at[i, j])
            )
            loads[-1].start()

    def write(i, part):
        writes.append(
            pltpu.make_async_copy(wides[i].at[part], outs[i].at[part], out_sems.at[len(writes)])
        )
        writes[-1].start()

    waiting = iter(loads)
    hidden = wides[1].shape[0]
    for span in spans(hidden, FINISH_BLOCK):
        next(waiting).wait()
        for part in spans(FINISH_BLOCK, LANES):
            rows = slice(span.start + part.start, span.start + part.stop)
            wides[0][:, rows] = ins[0][rows].astype(F32).T
        write(0, (slice(None), span))
    for span in spans(hidden, FINISH_BLOCK):
        next(waiting).wait()
        wides[1][span] = ins[1][span].astype(F32)
        write(1, span)
    for i in (2, 3):
        for _ in spans(ins[i].shape[0], FINISH_BLOCK):
            next(waiting).wait()
        rows = wides[2].shape[0]
        for kind in range(4):
            at = 2 + 4 * (i - 2) + kind
            wides[at][...] = ins[i][kind * rows : (kind + 1) * rows].astype(F32)
            write(at, slice(None))
    for copy in writes:
        copy.wait()


def params():
    return pltpu.CompilerParams(vmem_limit_bytes=VMEM_BYTES)


def cost(flops=1 << 20):
    return pl.CostEstimate(flops=flops, bytes_accessed=1 << 16, transcendentals=0)


def shape(dims, dtype):
    return jax.ShapeDtypeStruct(dims, dtype)


def whole(array):
    return pl.BlockSpec(
        array.shape, lambda *_: (0,) * len(array.shape), pipeline_mode=pl.Buffered(1)
    )


def result(array):
    return pl.BlockSpec(array.shape, lambda *_: (0,) * len(array.shape))


def columns(rows):
    return pl.BlockSpec((rows, HEAD_BLOCK), lambda i: (0, i))


def anywhere(arrays):
    return [pl.BlockSpec(memory_space=pl.ANY) for _ in arrays]


SCALAR = pl.BlockSpec(memory_space=pltpu.SMEM)


def call(
    kernel, name, grid, in_specs, out_specs, out_shape, scratch, args, channel=None, flops=1 << 20
):
    compiler_params = params()
    if channel is not None:
        compiler_params = pltpu.CompilerParams(
            vmem_limit_bytes=VMEM_BYTES, collective_id=channel, has_side_effects=True
        )
    return pl.pallas_call(
        kernel,
        grid=grid,
        in_specs=in_specs,
        out_specs=out_specs,
        out_shape=out_shape,
        scratch_shapes=scratch,
        compiler_params=compiler_params,
        cost_estimate=cost(flops),
        name=name,
    )(*args)


def pack(*parts):
    arrays, flipped = zip(*parts)
    features = arrays[0].shape[0] if flipped[0] else arrays[0].shape[1]
    rows = [a.shape[1] if turn else a.shape[0] for a, turn in parts]
    if arrays[-1].shape[1] < features and not flipped[-1]:
        rows[-1] = TABLE_ROWS
    rows = sum(rows)
    return pl.pallas_call(
        functools.partial(pack_kernel, flipped),
        out_shape=shape((rows, features), BF16),
        compiler_params=params(),
        cost_estimate=cost(),
        name="pack",
    )(*arrays)


def self_forward(heads, buckets, rows, gain, weights, ids):
    doc, features = rows.shape
    shares, steps = len(weights), features // HEAD_BLOCK
    narrow, tall = shape((doc, features), BF16), shape((doc, features), F32)
    scores = shape((steps * BLOCK_HEADS, doc, doc), BF16)
    out_shape = (*[narrow] * 4, shape((steps, 8, doc), F32), scores, tall)
    return call(
        functools.partial(self_forward_kernel, heads, buckets, shares),
        "self_forward",
        (steps,),
        [whole(rows), whole(gain), whole(ids), *anywhere(weights)],
        (
            *[columns(doc)] * 4,
            pl.BlockSpec((1, 8, doc), lambda i: (i, 0, 0)),
            pl.BlockSpec((BLOCK_HEADS, doc, doc), lambda i: (i, 0, 0)),
            result(tall),
        ),
        out_shape,
        [
            pltpu.VMEM((4 * features, features), BF16),
            pltpu.VMEM((shares, TABLE_ROWS, features), BF16),
            pltpu.VMEM((TABLE_ROWS, LANES), F32),
            pltpu.VMEM((doc, features), BF16),
            pltpu.SemaphoreType.DMA((shares, 5)),
        ],
        (rows, gain, ids, *weights),
    )


def self_backward(heads, rows, gain, branch, add, saved, weights, hops):
    doc, features = rows.shape
    shares, steps = len(weights), features // HEAD_BLOCK
    count = shares // 2
    *arrays, lse, bias = saved
    packed = pltpu.VMEM((4, features // 2, features), BF16)
    scores = pl.BlockSpec((BLOCK_HEADS, doc, doc), lambda i: (i, 0, 0))
    out_shape = (
        *[shape(h.shape, BF16) for h in hops],
        *[shape((4 * heads * HEAD_DIM, features), BF16)] * count,
        shape((steps * BLOCK_HEADS, doc, doc), BF16),
        shape((doc, features), F32),
        shape((8, features), F32),
    )
    return call(
        functools.partial(self_backward_kernel, heads, shares),
        "self_backward",
        (steps,),
        [
            *[whole(a) for a in (rows, gain, branch, add, *arrays)],
            pl.BlockSpec((1, 8, doc), lambda i: (i, 0, 0)),
            scores,
            *anywhere(weights),
            *anywhere(hops),
        ],
        (
            *anywhere(hops),
            *[result(o) for o in out_shape[len(hops) : len(hops) + count]],
            scores,
            result(out_shape[-2]),
            result(out_shape[-1]),
        ),
        out_shape,
        [
            pltpu.VMEM((4 * features, features), BF16),
            pltpu.VMEM((doc, features), BF16),
            pltpu.VMEM((doc, HEAD_BLOCK), BF16),
            pltpu.VMEM((doc, 3 * features), BF16),
            pltpu.VMEM((doc, features), F32),
            packed,
            packed,
            packed,
            pltpu.SemaphoreType.DMA((shares, 4)),
            pltpu.SemaphoreType.DMA((2,)),
            pltpu.SemaphoreType.DMA((2,)),
        ],
        (rows, gain, branch, add, *arrays, lse, bias, *weights, *hops),
        channel=4,
    )


def cross_forward(heads, rows, gain, memory, length, weights):
    (doc, features), slots = rows.shape, memory.shape[0]
    shares, steps = len(weights), features // HEAD_BLOCK
    query, key = shape((doc, features), BF16), shape((slots, features), BF16)
    tall = shape((doc, features), F32)
    return call(
        functools.partial(cross_forward_kernel, heads, shares),
        "cross_forward",
        (steps,),
        [SCALAR, whole(rows), whole(gain), whole(memory), *anywhere(weights)],
        (
            columns(doc),
            columns(slots),
            columns(slots),
            columns(doc),
            pl.BlockSpec((1, 8, doc), lambda i: (i, 0, 0)),
            result(tall),
        ),
        (query, key, key, query, shape((steps, 8, doc), F32), tall),
        [
            pltpu.VMEM((4 * features, features), BF16),
            pltpu.VMEM((doc, features), BF16),
            pltpu.VMEM((slots, LANES), BF16),
            pltpu.VMEM((2, slots, Q_BLOCK), BF16),
            pltpu.VMEM((LANES, Q_BLOCK), F32),
            pltpu.SemaphoreType.DMA((shares, 4)),
        ],
        (length, rows, gain, memory, *weights),
    )


def cross_backward(
    heads, size, rows, gain, memory, length, branch, add, saved, weights, scattered, hops
):
    (doc, features), slots = rows.shape, memory.shape[0]
    shares, blocks = len(weights), features // HEAD_BLOCK
    count = shares // 2
    blocks_out, ring_scratch = [], []
    if scattered:
        number, part = len(scattered), scattered[0].shape
        block = (2, part[0] // (2 * size), features)
        blocks_out = [shape(block, BF16)]
        steps = pltpu.SemaphoreType.DMA((2, size - 1))
        ring_scratch = [
            pltpu.VMEM((number, *part), BF16),
            pltpu.VMEM((2, size - 1, number, *block[1:]), BF16),
            pltpu.VMEM((2, number, *block[1:]), BF16),
            pltpu.VMEM(block, BF16),
            steps,
            steps,
            pltpu.SemaphoreType.DMA((number,)),
            pltpu.SemaphoreType.DMA((2,)),
        ]
    out_shape = (
        *[shape(h.shape, BF16) for h in hops],
        *blocks_out,
        *[shape((4 * heads * HEAD_DIM, features), BF16)] * count,
        shape((slots, features), BF16),
        shape((doc, features), F32),
        shape((doc, features), BF16),
        shape((8, features), F32),
    )
    query, key, value, mixed, lse = saved
    near = (gain, branch, query, mixed, lse)
    far = (rows, memory, add, key, value, *weights, *scattered, *hops)
    vmem, hbm = pl.BlockSpec(memory_space=pltpu.VMEM), pl.BlockSpec(memory_space=pl.ANY)
    packed = pltpu.VMEM((4, features // 2, features), BF16)
    key_block = pltpu.VMEM((blocks, slots, HEAD_BLOCK), BF16)
    return call(
        functools.partial(
            cross_backward_kernel, heads, shares, size, len(scattered), len(hops)
        ),
        "cross_backward",
        (),
        [SCALAR, *[vmem for _ in near], *[hbm for _ in far]],
        (
            *[hbm] * len(hops),
            *[vmem] * len(blocks_out),
            *[vmem] * count,
            hbm,
            vmem,
            vmem,
            vmem,
        ),
        out_shape,
        [
            pltpu.VMEM((doc, features), F32),
            pltpu.VMEM((slots, features), BF16),
            pltpu.VMEM((doc, features), F32),
            key_block,
            key_block,
            pltpu.VMEM((4 * features, features), BF16),
            pltpu.VMEM((doc, features), BF16),
            pltpu.VMEM((slots, LANES), BF16),
            pltpu.VMEM((doc, HEAD_BLOCK), BF16),
            pltpu.VMEM((doc, features), BF16),
            pltpu.VMEM((slots, 2 * features), BF16),
            pltpu.VMEM((2, slots, doc), BF16),
            packed,
            packed,
            packed,
            pltpu.VMEM((slots, features), BF16),
            pltpu.VMEM((doc, features), F32),
            pltpu.SemaphoreType.DMA((shares, 4)),
            pltpu.SemaphoreType.DMA((3,)),
            pltpu.SemaphoreType.DMA((2, blocks)),
            pltpu.SemaphoreType.DMA((slots // MEMORY_BLOCK,)),
            pltpu.SemaphoreType.DMA((2,)),
            pltpu.SemaphoreType.DMA((max(len(hops), 1), 2)),
            *ring_scratch,
        ],
        (length, *near, *far),
        channel=1,
    )


def feed_forward(rows, gain, cotangent, weights, before, last):
    (doc, features), shares = rows.shape, len(weights)
    share = weights[0].shape[0] // 2
    hidden = share * shares
    steps = hidden // HIDDEN_BLOCK
    summed, tall = shape((share, features), BF16), shape((doc, features), F32)
    low = shape((doc, features), BF16)
    rest = [low, tall, low, shape((8, features), F32)] if last else [tall, tall]
    kept, added = pltpu.VMEM((2, share, features), BF16), pltpu.VMEM(tall.shape, F32)
    return call(
        functools.partial(feed_forward_kernel, not before, last),
        "feed_forward",
        (steps,),
        [whole(rows), whole(gain), whole(cotangent), *anywhere(weights), *anywhere(before)],
        (result(summed), result(summed), *[result(o) for o in rest]),
        (summed, summed, *rest),
        [
            pltpu.VMEM((hidden, features), BF16),
            pltpu.VMEM((hidden, features), BF16),
            pltpu.VMEM((doc, features), BF16),
            pltpu.VMEM((features, doc), BF16),
            pltpu.VMEM((features, doc), BF16),
            pltpu.VMEM((hidden, doc), BF16),
            pltpu.VMEM((hidden, doc), BF16),
            kept,
            kept,
            kept,
            added,
            added,
            added,
            pltpu.VMEM((2, HIDDEN_BLOCK, doc), F32),
            pltpu.VMEM((2, HIDDEN_BLOCK, doc), F32),
            pltpu.SemaphoreType.DMA((shares, 2)),
            pltpu.SemaphoreType.DMA((2,)),
            pltpu.SemaphoreType.DMA((2,)),
        ],
        (rows, gain, cotangent, *weights, *before),
        channel=3 if before else 2,
    )


def finish(sum_wide, sum_narrow, sum_cross, sum_self):
    rows, features = sum_self.shape
    hidden, part = sum_wide.shape[0], shape((rows // 4, features), F32)
    out_shape = [shape((features, hidden), F32), shape((hidden, features), F32), *[part] * 8]
    sources = (sum_wide, sum_narrow, sum_cross, sum_self)
    writes = 2 * hidden // FINISH_BLOCK + 8
    wide, narrow, *parts = pl.pallas_call(
        finish_kernel,
        in_specs=anywhere(sources),
        out_specs=anywhere(out_shape),
        out_shape=out_shape,
        scratch_shapes=[
            *[pltpu.VMEM(source.shape, BF16) for source in sources],
            *[pltpu.VMEM(out.shape, F32) for out in out_shape],
            pltpu.SemaphoreType.DMA((4, hidden // FINISH_BLOCK)),
            pltpu.SemaphoreType.DMA((writes,)),
        ],
        compiler_params=params(),
        cost_estimate=cost(),
        name="finish",
    )(*sources)
    return wide, narrow, parts[4:], parts[:4]


def share_place(row, other, peers):
    j, bit = 0, 1
    while bit < peers:
        j = j + bit * ((row // bit + other // bit) % 2)
        bit *= 2
    return (j % 2) * (j // 2) + (1 - j % 2) * (peers // 2 + j // 2)


def tail_kernel(size, peers, buckets, heads, gathered, counts, *refs):
    parts = []
    for count in counts:
        parts.append(refs[:count])
        refs = refs[count:]
    arrays, shares = len(counts) + 1, peers // 2
    last_refs, refs = refs[:shares], refs[shares:]
    ids_ref, ds_ref, *gain_refs = refs[:5]
    outs, small_out_ref, refs = refs[5 : 5 + arrays], refs[5 + arrays], refs[6 + arrays :]
    slots, refs = refs[:arrays], refs[arrays:]
    firsts, refs = refs[:arrays], refs[arrays:]
    far_came_ref, part_ref, scores_ref, bucket_ref = refs[:4]
    small_ref, near_ref, far_ref = refs[4:7]
    send, came, send_out, came_out, small_sems, hop_sems, local_sems = refs[7:]
    parts.append((part_ref,))
    me, row = lax.axis_index("dp"), lax.axis_index("mp")
    ways = ring_ways(size)
    doc = ids_ref.shape[0]
    mesh = pl.DeviceIdType.MESH

    load_scores = pltpu.make_async_copy(ds_ref, scores_ref, local_sems.at[0])
    load_scores.start()

    barrier = pltpu.get_barrier_semaphore()

    def greet(t, carry):
        pl.semaphore_signal(
            barrier, inc=1, device_id=((me + t) % size, row), device_id_type=mesh
        )
        return carry

    lax.fori_loop(1, size, greet, 0)
    for t in range(1, peers):
        pl.semaphore_signal(
            barrier, inc=1, device_id=(me, (row + t) % peers), device_id_type=mesh
        )
    pl.semaphore_wait(barrier, size - 1 + peers - 1)

    def block(i, way, number):
        rows = outs[i].shape[0] // (2 * size)
        return pl.ds(pl.multiple_of((way * size + number) * rows, 16), rows)

    def part(i, span):
        total = parts[i][0][span].astype(F32)
        for ref in parts[i][1:]:
            total = total + ref[span].astype(F32)
        return total

    def first_copy(i, way):
        return remote(
            firsts[i].at[way],
            slots[i].at[way, 0],
            send.at[i, way, 0],
            came.at[i, way, 0],
            (ways[way][1], row),
        )

    def next_copy(i, way, step):
        return remote(
            slots[i].at[way, step - 1],
            slots[i].at[way, step],
            send.at[i, way, step],
            came.at[i, way, step],
            (ways[way][1], row),
        )

    def wait_came(i, way, step):
        remote(
            slots[i].at[way, step],
            slots[i].at[way, step],
            send.at[i, way, step],
            came.at[i, way, step],
            (ways[way][1], row),
        ).wait_recv()

    def out_copy(i, way, step):
        span = block(i, way, (ways[way][0] + 1 - step + size) % size)
        return remote(
            outs[i].at[span],
            outs[i].at[span],
            send_out.at[i, way, step],
            came_out.at[i, way, step],
            (ways[way][1], row),
        )

    def begin(rings):
        for i, way in rings:
            firsts[i][way] = part(i, block(i, way, ways[way][0])).astype(BF16)
            first_copy(i, way).start()

    def plus_part(i, way, step):
        span = block(i, way, (ways[way][0] - step - 1 + size) % size)
        total = slots[i][way, step].astype(F32) + part(i, span)
        return span, total.astype(BF16)

    def advance(rings, step):
        for i, way in rings:
            wait_came(i, way, step - 1)
            slots[i][way, step - 1] = plus_part(i, way, step - 1)[1]
            next_copy(i, way, step).start()

    def turn(rings):
        for i, way in rings:
            wait_came(i, way, size - 2)
            span, total = plus_part(i, way, size - 2)
            outs[i][span] = total
            out_copy(i, way, 0).start()

    def pass_on(rings, step):
        for i, way in rings:
            out_copy(i, way, step - 1).wait_recv()
            out_copy(i, way, step).start()

    ready = [(i, way) for i in range(gathered) for way in range(2)]
    early = [(i, way) for i in range(gathered, arrays - 1) for way in range(2)]
    late = [(arrays - 1, way) for way in range(2)]

    other_chip = None
    if shares == 2:
        other_chip = to_differing(2, last_refs[1], far_came_ref, hop_sems)
        other_chip.start()
    begin(early)
    for i, way in ready:
        outs[i][block(i, way, (ways[way][0] + 1) % size)] = parts[i][0][way]
        out_copy(i, way, 0).start()

    rows_used, per_row = bucket_ref.shape[0], ds_ref.shape[0] // bucket_ref.shape[0]
    units = rows_used * buckets
    per_round = -(-units // max(2 * (size - 2), 1))

    def bucket_unit(u, carry):
        r, b = u // buckets, u % buckets
        sums = [jnp.zeros((8, LANES), F32) for _ in range(per_row)]
        for c in range(0, doc, LANES):
            hit = ids_ref[: c + LANES, c : c + LANES] == b
            for h in range(per_row):
                grads = scores_ref[r * per_row + h, : c + LANES, c : c + LANES].astype(F32)
                kept = jnp.where(hit, grads, 0.0).reshape(-1, 8, LANES)
                sums[h] = sums[h] + jnp.sum(kept, axis=0)
        for h in range(per_row):
            bucket_ref[r, h, pl.ds(b, 1), :] = jnp.sum(sums[h], axis=0, keepdims=True)
        return carry

    def bucket_round(k):
        low = jnp.minimum(k * per_round, units)
        lax.fori_loop(low, jnp.minimum(low + per_round, units), bucket_unit, 0)

    bucket_ref[...] = jnp.zeros_like(bucket_ref)
    part_ref[...] = jnp.zeros_like(part_ref)
    load_scores.wait()

    def early_step(step, carry):
        advance(early, step)
        pass_on(ready, step)
        bucket_round(step - 1)
        return carry

    begin_late = LATE_STEP if size - 1 > LATE_STEP else size - 1
    lax.fori_loop(1, min(begin_late + 1, size - 1), early_step, 0)
    if begin_late == size - 1:
        turn(early)
    used = slice(0, last_refs[0].shape[0])
    if other_chip is None:
        part_ref[used] = last_refs[0][...]
    else:
        other_chip.wait_recv()
        part_ref[used] = low_sum(last_refs[0][...], far_came_ref[...])
    begin(late)

    def both_step(step, carry):
        early_step(step, carry)
        advance(late, step - begin_late)
        return carry

    def middle_step(step, carry):
        pass_on(early, step)
        advance(late, step + size - 1 - begin_late)
        bucket_round(size - 2 + step - 1)
        return carry

    def end_step(step, carry):
        pass_on(early, step)
        pass_on(late, step - begin_late)
        bucket_round(size - 2 + step - 1)
        return carry

    late_passed = 0
    if begin_late < size - 1:
        lax.fori_loop(begin_late + 1, size - 1, both_step, 0)
        turn(early)
        advance(late, size - 1 - begin_late)
        lax.fori_loop(1, begin_late, middle_step, 0)
        pass_on(early, begin_late)
        turn(late)
        bucket_round(size - 2 + begin_late - 1)
        lax.fori_loop(begin_late + 1, size - 1, end_step, 0)
        late_passed = size - 2 - begin_late
    else:
        lax.fori_loop(1, size - 1, middle_step, 0)
        turn(late)
    if size == 2:
        lax.fori_loop(0, units, bucket_unit, 0)

    features = gain_refs[0].shape[1]
    per_gain = features // LANES
    gain_rows = len(gain_refs) * per_gain
    small_ref[...] = jnp.zeros_like(small_ref)
    for i, ref in enumerate(gain_refs):
        total = jnp.sum(ref[...], axis=0, keepdims=True)
        for c in range(per_gain):
            at = i * per_gain + c
            small_ref[at : at + 1, :] = total[:, c * LANES : (c + 1) * LANES]
    for r in range(rows_used):
        block_sums = bucket_ref[r].reshape(LANES, LANES).T
        at = gain_rows + r
        small_ref[at : at + 1, :] = jnp.sum(block_sums, axis=0, keepdims=True)

    def near_copy(t):
        return remote(
            small_ref,
            near_ref.at[row],
            small_sems.at[0, t],
            small_sems.at[1, t],
            (me, (row + t) % peers),
        )

    def far_copy(t):
        return remote(
            far_ref.at[me],
            far_ref.at[me],
            small_sems.at[2, t],
            small_sems.at[3, t],
            ((me + t) % size, row),
        )

    for t in range(1, peers):
        near_copy(t).start()
    near_ref[pl.ds(row, 1)] = small_ref[...][None]
    for t in range(1, peers):
        near_copy(t).wait_recv()
    own = rows_used // peers
    total, sums = None, None
    for k in range(peers):
        gains = near_ref[k, :gain_rows]
        mine = near_ref[k, pl.ds(gain_rows + own * share_place(row, k, peers), own)]
        total = gains if total is None else total + gains
        sums = mine if sums is None else sums + mine
    small_ref_rows = far_ref.shape[1]
    far_ref[pl.ds(me, 1)] = jnp.concatenate(
        [total, sums, jnp.zeros((small_ref_rows - gain_rows - own, LANES), F32)], axis=0
    )[None]

    def far_start(t, carry):
        far_copy(t).start()
        return carry

    lax.fori_loop(1, size, far_start, 0)

    def late_step(step, carry):
        pass_on(late, step)
        return carry

    lax.fori_loop(1 + late_passed, size - 1, late_step, 0)

    def far_wait(t, carry):
        far_copy(t).wait()
        return carry

    lax.fori_loop(1, size, far_wait, 0)

    def far_add(k, total):
        return total + far_ref[k]

    small_out_ref[...] = lax.fori_loop(1, size, far_add, far_ref[0])
    for i, way in ready + early + late:
        out_copy(i, way, size - 2).wait_recv()

    for t in range(1, peers):
        near_copy(t).wait_send()
    if other_chip is not None:
        other_chip.wait_send()
    for i, way in early + late:
        first_copy(i, way).wait_send()

    def sent(step, carry):
        for i, way in early + late:
            next_copy(i, way, step).wait_send()
        return carry

    lax.fori_loop(1, size - 1, sent, 0)

    def sent_out(step, carry):
        for i, way in ready + early + late:
            out_copy(i, way, step).wait_send()
        return carry

    lax.fori_loop(0, size - 1, sent_out, 0)


def tail_sums(size, peers, buckets, heads, blocks, terms, last, ids, ds, gains):
    assert peers in (2, 4)
    grain = 2 * 16 * size
    features = last[0].shape[1]
    rows = [size * 2 * b.shape[1] for b in blocks]
    rows += [arrays[0].shape[0] for arrays in terms]
    rows.append(last[0].shape[0])
    padded = [r + -r % grain for r in rows]
    parts = [[b] for b in blocks]
    for arrays, r, p in zip(terms, rows[len(blocks) :], padded[len(blocks) :]):
        parts.append([jnp.pad(a, ((0, p - r), (0, 0))) for a in arrays])
    flat = [a for arrays in parts for a in arrays]
    lines = peers * (-(-heads * buckets // LANES))
    small = len(gains) * features // LANES + lines
    small = shape((small + -small % 8, LANES), F32)
    vmem, hbm = pl.BlockSpec(memory_space=pltpu.VMEM), pl.BlockSpec(memory_space=pl.ANY)
    steps = pltpu.SemaphoreType.DMA((len(rows), 2, size - 1))

    def ring_slots(i, steps):
        if i < len(blocks):
            return pltpu.VMEM((2, 1, 16, LANES), BF16)
        return pltpu.VMEM((2, *steps, padded[i] // (2 * size), features), BF16)

    *sums, small = pl.pallas_call(
        functools.partial(
            tail_kernel, size, peers, buckets, heads, len(blocks), [len(a) for a in parts]
        ),
        in_specs=[
            *[vmem] * (len(flat) + 1),
            *[hbm] * (len(last) - 1),
            vmem,
            hbm,
            *[vmem] * len(gains),
        ],
        out_specs=[vmem] * (len(rows) + 1),
        out_shape=[*[shape((p, features), BF16) for p in padded], small],
        scratch_shapes=[
            *[ring_slots(i, (size - 1,)) for i in range(len(rows))],
            *[ring_slots(i, ()) for i in range(len(rows))],
            pltpu.VMEM((rows[-1], features), BF16),
            pltpu.VMEM((padded[-1], features), BF16),
            pltpu.VMEM(ds.shape, BF16),
            pltpu.VMEM((lines, LANES // buckets, buckets, LANES), F32),
            pltpu.VMEM(small.shape, F32),
            pltpu.VMEM((peers, *small.shape), F32),
            pltpu.VMEM((size, *small.shape), F32),
            steps,
            steps,
            steps,
            steps,
            pltpu.SemaphoreType.DMA((4, max(size, peers))),
            pltpu.SemaphoreType.DMA((2,)),
            pltpu.SemaphoreType.DMA((1,)),
        ],
        compiler_params=pltpu.CompilerParams(
            vmem_limit_bytes=VMEM_BYTES, collective_id=0, has_side_effects=True
        ),
        cost_estimate=cost(),
        name="tail_sums",
    )(*flat, *last, ids, ds, *gains)
    return [total[:r] for total, r in zip(sums, rows)], small


def swap(array, bit, size):
    return lax.ppermute(array, "mp", [(i, i ^ bit) for i in range(size)])


def after(array, *others):
    return lax.optimization_barrier((array, others))[0]


def shards(
    decoder_rows,
    memory_rows,
    decoder_token_length,
    memory_length,
    bucket_ids,
    relative_bucket_bias,
    self_gain,
    self_query,
    self_key,
    self_value,
    self_out,
    cross_gain,
    cross_query,
    cross_key,
    cross_value,
    cross_out,
    hidden_gain,
    widen_weight,
    narrow_weight,
    layer_cotangent,
):
    dp_size = lax.axis_size("dp")
    mp_size = lax.axis_size("mp")
    me = lax.axis_index("mp")
    doc, features = decoder_rows.shape
    slots = memory_rows.shape[0]
    cols = self_query.shape[1]
    heads = cols // HEAD_DIM
    buckets = relative_bucket_bias.shape[0]
    order = [*range(1, mp_size, 2), *range(0, mp_size, 2)]

    doc_length = lax.dynamic_index_in_dim(decoder_token_length, me, keepdims=False)
    doc_memory = lax.dynamic_index_in_dim(memory_length, me)
    position = jnp.arange(doc, dtype=jnp.int32)
    allowed = (position[:, None] <= position[None, :]) & (position[:, None] < doc_length)
    ids = jnp.where(allowed, bucket_ids.T, buckets)
    own_self = pack(
        (self_query.T, False),
        (self_key.T, False),
        (self_value.T, False),
        (self_out, False),
        (relative_bucket_bias.T, False),
    )
    own_cross = pack(
        (cross_query.T, False), (cross_key.T, False), (cross_value.T, False), (cross_out, False)
    )
    own_hidden = pack((widen_weight, True), (narrow_weight, False))

    def first_hops(own):
        shares, bit = {0: own}, mp_size // 2
        while bit > 1:
            for j in list(shares):
                shares[j | bit] = swap(shares[j], bit, mp_size)
            bit //= 2
        return shares

    def last_hop(shares, *others):
        if 1 not in shares:
            shares[1] = swap(shares[0], 1, mp_size)
        for j in range(2, mp_size, 2):
            shares[j] = after(shares[j], *others)
            shares[j | 1] = swap(shares[j], 1, mp_size)
        return shares

    near_self = first_hops(own_self)
    near_self[1] = swap(own_self, 1, mp_size)
    memory_rows = after(memory_rows, own_self)
    w_self = last_hop(near_self, own_cross, own_hidden, ids)
    w_self = [w_self[j] for j in order]
    near_cross = first_hops(own_cross)
    near_hidden = first_hops(own_hidden)
    near_hidden[1] = swap(own_hidden, 1, mp_size)
    memory_seen = lax.all_to_all(
        memory_rows.reshape(dp_size, slots // dp_size, features), "dp", 0, 0
    ).reshape(slots, features)

    gain_self = self_gain.astype(F32)[None]
    gain_cross = cross_gain.astype(F32)[None]
    gain_hidden = hidden_gain.astype(F32)[None]

    *saved_self, after_self = self_forward(heads, buckets, decoder_rows, gain_self, w_self, ids)
    w_cross = last_hop(near_cross, after_self)
    w_cross = [w_cross[j] for j in order]
    *saved_cross, after_cross = cross_forward(
        heads, after_self, gain_cross, memory_seen, doc_memory, w_cross
    )

    before, wide_sums, narrow_sums, w_hidden = (), [], [], near_hidden
    for j in range(0, mp_size, 2):
        wide_sum, narrow_sum, *before = feed_forward(
            after_cross,
            gain_hidden,
            layer_cotangent,
            [w_hidden[j + 1], w_hidden[j]],
            before,
            j == mp_size - 2,
        )
        wide_sums.append(wide_sum)
        narrow_sums.append(narrow_sum)
        if j == 0:
            w_hidden = last_hop(near_hidden, before[0])
    layer_output, grad_after_cross, branch, hidden_gain_grad = before

    scattered, hops = wide_sums, narrow_sums[1:]
    if wide_sums[0].shape[0] % (2 * 16 * dp_size):
        scattered, hops = [], wide_sums[1:] + narrow_sums[1:]
    *sums, grad_memory, grad_after_self, branch, cross_gain_grad = cross_backward(
        heads,
        dp_size,
        after_self,
        gain_cross,
        memory_seen,
        doc_memory,
        branch,
        grad_after_cross,
        saved_cross,
        w_cross,
        scattered,
        hops,
    )
    came, sums = sums[: len(hops)], sums[len(hops) :]
    if scattered:
        blocks, terms, cross_sums = sums[:1], [narrow_sums[:1] + came], sums[1:]
    else:
        blocks, cross_sums = [], sums
        hidden = [wide_sums[0], narrow_sums[0]], came
        terms = [[jnp.concatenate(both, axis=0) for both in hidden if both]]
    memory_grad = lax.all_to_all(
        grad_memory.reshape(dp_size, slots // dp_size, features), "dp", 0, 0
    ).reshape(slots, features)

    *sums, score_grads, input_grad, self_gain_grad = self_backward(
        heads,
        decoder_rows,
        gain_self,
        branch,
        grad_after_self,
        saved_self,
        w_self,
        cross_sums[1:],
    )
    cross_sums[1:], last = sums[: len(cross_sums) - 1], sums[len(cross_sums) - 1 :]
    (*hidden, sum_cross, sum_self), small = tail_sums(
        dp_size,
        mp_size,
        buckets,
        heads,
        blocks,
        terms + [cross_sums],
        last,
        ids,
        score_grads,
        (self_gain_grad, cross_gain_grad, hidden_gain_grad),
    )
    wide_grad, narrow_grad, self_grads, cross_grads = finish(
        *(hidden if scattered else jnp.split(hidden[0], 2)), sum_cross, sum_self
    )
    gain_rows = 3 * features // LANES
    gains = small[:gain_rows].reshape(3, features)
    lines = -(-heads * buckets // LANES)
    sums = small[gain_rows : gain_rows + lines, : heads // lines * buckets]
    position_grad = sums.reshape(heads, buckets).T

    return (
        layer_output,
        input_grad,
        memory_grad,
        position_grad,
        gains[0],
        *[grad.T for grad in self_grads[:3]],
        self_grads[3],
        gains[1],
        *[grad.T for grad in cross_grads[:3]],
        cross_grads[3],
        gains[2],
        wide_grad,
        narrow_grad,
    )


def solution(mesh):
    return jax.shard_map(
        shards,
        mesh=mesh,
        in_specs=(
            P(("dp", "mp"), None),
            P(("dp", "mp"), None),
            P("dp"),
            P("dp"),
            P(),
            P(None, "mp"),
            P(),
            P(None, "mp"),
            P(None, "mp"),
            P(None, "mp"),
            P("mp", None),
            P(),
            P(None, "mp"),
            P(None, "mp"),
            P(None, "mp"),
            P("mp", None),
            P(),
            P(None, "mp"),
            P("mp", None),
            P(("dp", "mp"), None),
        ),
        out_specs=(
            P(("dp", "mp"), None),
            P(("dp", "mp"), None),
            P(("dp", "mp"), None),
            P(None, "mp"),
            P(),
            P(None, "mp"),
            P(None, "mp"),
            P(None, "mp"),
            P("mp", None),
            P(),
            P(None, "mp"),
            P(None, "mp"),
            P(None, "mp"),
            P("mp", None),
            P(),
            P(None, "mp"),
            P("mp", None),
        ),
        check_vma=False,
    )
```

```python
import functools

import jax
import jax.numpy as jnp
from jax import lax
from jax.experimental import pallas as pl
from jax.experimental.pallas import tpu as pltpu
from jax.sharding import PartitionSpec as P

HEAD_DIM = 64
NORM_EPS = 1e-06
MASKED = -1e30
SCALE = HEAD_DIM**-0.5
BF16 = jnp.bfloat16
F32 = jnp.float32
LANES = 128
TABLE_ROWS = 16
TILE_ROWS = 16
LARGEST_SUM = 1e30
LATE_STEP = 4
HEAD_BLOCK = 256
BLOCK_HEADS = HEAD_BLOCK // HEAD_DIM
Q_BLOCK = 256
K_BLOCK = 512
FORWARD_K_BLOCK = 256
HIDDEN_BLOCK = 256
MEMORY_BLOCK = 768
FINISH_BLOCK = 384
ROW_BLOCK = 128
VMEM_BYTES = 56 * 1024 * 1024
VMEM_OF = {
    "self_forward": 28 * 1024 * 1024,
    "cross_forward": 40 * 1024 * 1024,
    "feed_forward": 44 * 1024 * 1024,
    "cross_backward": 56 * 1024 * 1024,
    "self_backward": 44 * 1024 * 1024,
}
GELU_ROOT = 0.7978845608028654
GELU_CUBE = 0.044715


def dot_nn(a, b):
    return lax.dot_general(a, b, (((1,), (0,)), ((), ())), preferred_element_type=F32)


def dot_nt(a, b):
    return lax.dot_general(a, b, (((1,), (1,)), ((), ())), preferred_element_type=F32)


def dot_tn(a, b):
    return lax.dot_general(a, b, (((0,), (0,)), ((), ())), preferred_element_type=F32)


def flip(a):
    return a.astype(F32).T.astype(BF16)


def spans(size, step):
    return [slice(i, i + step) for i in range(0, size, step)]


def norm_scale(rows):
    return lax.rsqrt(jnp.mean(rows * rows, axis=-1, keepdims=True) + NORM_EPS)


def norm_into(normed_ref, rows_ref, gain_ref):
    for span in spans(rows_ref.shape[0], ROW_BLOCK):
        rows = rows_ref[span].astype(F32)
        normed_ref[span] = (rows * norm_scale(rows) * gain_ref[...]).astype(BF16)


def norm_back_into(span, grad, out_ref, low_ref, gain_grad_ref, rows_ref, gain_ref, add_ref):
    rows = rows_ref[span].astype(F32)
    scale = norm_scale(rows)
    unit = rows * scale
    grad_unit = grad * gain_ref[...]
    mean = jnp.mean(grad_unit * unit, axis=-1, keepdims=True)
    out = add_ref[span].astype(F32) + scale * (grad_unit - unit * mean)
    out_ref[span] = out
    if low_ref is not None:
        low_ref[span] = out.astype(BF16)
    gain_grad_ref[...] += jnp.sum((grad * unit).reshape(-1, 8, rows.shape[1]), axis=0)


def gelu_and_slope(v):
    square = v * v
    bend = jnp.tanh(GELU_ROOT * (v + GELU_CUBE * v * square))
    half = 0.5 * (1.0 + bend)
    slope = half + 0.5 * v * (1.0 - bend * bend) * GELU_ROOT * (1.0 + 3.0 * GELU_CUBE * square)
    return v * half, slope


def lane_block(start):
    return pl.ds(pl.multiple_of(start, LANES), LANES)


def extra_lanes(rows, allowed):
    lane = lax.broadcasted_iota(jnp.int32, (rows, LANES), 1) % HEAD_DIM
    first = MASKED if allowed is None else jnp.where(allowed, 0.0, MASKED)
    return jnp.where(lane == 0, first, jnp.where(lane < 4, 1.0, 0.0)).astype(BF16)


def pick(which, block, other):
    lane = lax.broadcasted_iota(jnp.int32, block.shape, 1)
    return jnp.where((lane < HEAD_DIM) == (which == 0), block, other)


def half_rows(which):
    return slice(which * HEAD_DIM, (which + 1) * HEAD_DIM)


def split(values):
    high = values.astype(BF16).astype(F32)
    rest = values - high
    middle = rest.astype(BF16).astype(F32)
    return high, middle, rest - middle


def with_extra(which, block_t, masked, minus):
    columns = block_t.shape[1]
    row = lax.broadcasted_iota(jnp.int32, (HEAD_DIM, columns), 0)
    extra = jnp.where(row == 0, 1.0 if masked else 0.0, 0.0)
    if minus is not None:
        for i, part in enumerate(split(minus)):
            extra = jnp.where(row == i + 1, -part, extra)
    own = block_t[half_rows(which)]
    return jnp.concatenate([own, extra] if which == 0 else [extra, own], axis=0).astype(BF16)


def bias_block(table_ref, ids_ref, index, rows, start):
    row = jnp.broadcast_to(table_ref[pl.ds(index, 1), :], (rows, LANES))
    return jnp.concatenate(
        [
            jnp.take_along_axis(row, ids_ref[:rows, c : c + LANES], axis=1)
            for c in range(start, start + Q_BLOCK, LANES)
        ],
        axis=1,
    )


def ring_place(me, size):
    return jnp.where(me % 2 == 0, me // 2, size - 1 - me // 2)


def ring_device(place, size):
    return jnp.where(place < size // 2, 2 * place, 2 * (size - 1 - place) + 1)


def ring_ways(size):
    me = lax.axis_index("dp")
    place = ring_place(me, size)
    return (
        (place, ring_device((place + 1) % size, size)),
        (size - 1 - place, ring_device((place + size - 1) % size, size)),
    )


def differing(row, bit):
    return row + bit - 2 * bit * ((row // bit) % 2)


def remote(source, target, send_sem, recv_sem, device):
    return pltpu.make_async_remote_copy(
        src_ref=source,
        dst_ref=target,
        send_sem=send_sem,
        recv_sem=recv_sem,
        device_id=device,
        device_id_type=pl.DeviceIdType.MESH,
    )


def greet(bits, devices=()):
    me, row = lax.axis_index("dp"), lax.axis_index("mp")
    barrier = pltpu.get_barrier_semaphore()
    others = [(me, differing(row, bit)) for bit in bits] + [(device, row) for device in devices]
    for other in others:
        pl.semaphore_signal(
            barrier, inc=1, device_id=other, device_id_type=pl.DeviceIdType.MESH
        )
    pl.semaphore_wait(barrier, len(others))


def to_differing(bit, source, target, sems):
    me, row = lax.axis_index("dp"), lax.axis_index("mp")
    return remote(source, target, sems.at[0], sems.at[1], (me, differing(row, bit)))


class Scatter:
    def __init__(self, size, part, slots, done, send, came):
        self.size, self.part, self.slots, self.done = size, part, slots, done
        self.send, self.came = send, came
        self.ways, self.row = ring_ways(size), lax.axis_index("mp")

    def span(self, way, number):
        rows = self.slots.shape[3]
        return pl.ds(pl.multiple_of((way * self.size + number) * rows, 16), rows)

    def copy(self, way, step, source):
        return remote(
            source,
            self.slots.at[way, step],
            self.send.at[way, step],
            self.came.at[way, step],
            (self.ways[way][1], self.row),
        )

    def first(self, way):
        return self.copy(way, 0, self.part.at[:, self.span(way, self.ways[way][0])])

    def next(self, way, step):
        return self.copy(way, step, self.slots.at[way, step - 1])

    def begin(self):
        for way in range(2):
            self.first(way).start()

    def total(self, way, step):
        self.copy(way, step, self.slots.at[way, step]).wait_recv()
        span = self.span(way, (self.ways[way][0] - step - 1 + self.size) % self.size)
        return low_sum(self.slots[way, step], self.part[:, span])

    def advance(self, step):
        for way in range(2):
            self.slots[way, step - 1] = self.total(way, step - 1)
            self.next(way, step).start()

    def turn(self):
        for way in range(2):
            self.done[way] = self.total(way, self.size - 2)

    def wait_sent(self):
        for way in range(2):
            self.first(way).wait_send()

        def sent(step, carry):
            for way in range(2):
                self.next(way, step).wait_send()
            return carry

        lax.fori_loop(1, self.size - 1, sent, 0)


def low_sum(a, b):
    return (a.astype(F32) + b.astype(F32)).astype(BF16)


class Stack:
    def __init__(self, sources, stack_ref, sems, kinds, rows):
        features = stack_ref.shape[0] // kinds
        self.copies = [
            [
                pltpu.make_async_copy(
                    source.at[pl.ds(kind * rows, rows)],
                    stack_ref.at[pl.ds(kind * features + p * rows, rows)],
                    sems.at[p, kind],
                )
                for p, source in enumerate(sources)
            ]
            for kind in range(kinds)
        ]

    def start(self, *kinds):
        for kind in kinds:
            for copy in self.copies[kind]:
                copy.start()

    def wait(self, *kinds):
        for kind in kinds:
            for copy in self.copies[kind]:
                copy.wait()

    def wait_at(self, condition, *kinds):
        @pl.when(condition)
        def _():
            self.wait(*kinds)


def table_copies(sources, tables_ref, sems, kinds):
    start = sources[0].shape[0] - TABLE_ROWS
    return [
        pltpu.make_async_copy(
            source.at[pl.ds(start, TABLE_ROWS)], tables_ref.at[p], sems.at[p, kinds]
        )
        for p, source in enumerate(sources)
    ]


def table_into(table_ref, tables_ref, heads, buckets):
    for p in range(tables_ref.shape[0]):
        rows = tables_ref[p, :, :LANES].astype(F32)
        lane = lax.broadcasted_iota(jnp.int32, rows.shape, 1)
        rows = jnp.where(lane < buckets, rows, MASKED)
        for h in range(heads):
            table_ref[p * heads + h : p * heads + h + 1, :] = rows[h : h + 1, :]


def self_forward_kernel(heads, buckets, shares, rows_ref, gain_ref, ids_ref, *refs):
    sources = refs[:shares]
    q_ref, k_ref, v_ref, mixed_ref, lse_ref, bias_ref, out_ref = refs[shares : shares + 7]
    w_ref, tables_ref, table_ref, normed_ref, sems = refs[shares + 7 :]
    step = pl.program_id(0)
    doc, features = rows_ref.shape
    stack = Stack(sources, w_ref, sems, 4, heads * HEAD_DIM)

    @pl.when(step == 0)
    def _():
        stack.start(0)
        tables = table_copies(sources, tables_ref, sems, 4)
        for copy in tables:
            copy.start()
        stack.start(1, 2, 3)
        norm_into(normed_ref, rows_ref, gain_ref)
        out_ref[...] = rows_ref[...].astype(F32)
        for copy in tables:
            copy.wait()
        table_into(table_ref, tables_ref, heads, buckets)

    def weights(kind):
        start = pl.multiple_of(kind * features + step * HEAD_BLOCK, HEAD_BLOCK)
        return w_ref[pl.ds(start, HEAD_BLOCK)]

    for kind, ref in enumerate((q_ref, k_ref, v_ref)):
        stack.wait_at(step == 0, kind)
        ref[...] = dot_nt(normed_ref[...], weights(kind)).astype(BF16)
    none = jnp.zeros((doc, LANES), BF16)
    for pair in range(BLOCK_HEADS // 2):
        lanes = slice(pair * LANES, (pair + 1) * LANES)
        k, v_t = k_ref[:, lanes], flip(v_ref[:, lanes])
        q_t = flip(q_ref[:, lanes].astype(F32) * SCALE)
        k_of = [pick(which, k, none) for which in range(2)]
        for span in spans(doc, Q_BLOCK):
            rows, mixed = span.stop, []
            for which in range(2):
                h = 2 * pair + which
                bias = bias_block(table_ref, ids_ref, step * BLOCK_HEADS + h, rows, span.start)
                bias_ref[h, :rows, span] = bias.astype(BF16)
                s = dot_nn(k_of[which][:rows], q_t[:, span]) + bias
                top = jnp.max(s, axis=0, keepdims=True)
                p = jnp.exp(s - top)
                total = jnp.sum(p, axis=0, keepdims=True)
                mixed.append(dot_nn(v_t[half_rows(which), :rows], p.astype(BF16)) / total)
                lse_ref[0, h : h + 1, span] = top + jnp.log(total)
            mixed_ref[span, lanes] = jnp.concatenate(mixed, axis=0).T.astype(BF16)
    stack.wait_at(step == 0, 3)
    out_ref[...] += dot_nn(mixed_ref[...], weights(3))


def self_backward_kernel(heads, shares, *refs):
    count = shares // 2
    rows_ref, gain_ref, branch_ref, add_ref = refs[:4]
    q_ref, k_ref, v_ref, mixed_ref, lse_ref, bias_ref = refs[4:10]
    sources, refs = refs[10 : 10 + shares], refs[10 + shares :]
    hop_in, hop_out, refs = refs[: count - 1], refs[count - 1 : 2 * count - 2], refs[2 * count - 2 :]
    sums, refs = refs[:count], refs[count:]
    ds_ref, out_ref, gain_grad_ref = refs[:3]
    w_ref, normed_ref, g_ref, grad_ref, back_ref, give_ref, keep_ref, came_ref = refs[3:11]
    sems, swap_sems, hop_sems = refs[11:]
    step = pl.program_id(0)
    doc, features = rows_ref.shape
    half = features // 2
    stack = Stack(sources, w_ref, sems, 4, heads * HEAD_DIM)
    swap = to_differing(1, give_ref, came_ref, swap_sems)
    hops = [
        to_differing(2, source, target, hop_sems) for source, target in zip(hop_in, hop_out)
    ]

    @pl.when(step == 0)
    def _():
        stack.start(3, 0, 1, 2)
        greet([1, 2][:count])
        for hop in hops:
            hop.start()
        norm_into(normed_ref, rows_ref, gain_ref)
        stack.wait(3)

    start = pl.multiple_of(3 * features + step * HEAD_BLOCK, HEAD_BLOCK)
    g_ref[...] = dot_nt(branch_ref[...], w_ref[pl.ds(start, HEAD_BLOCK)]).astype(BF16)
    none = jnp.zeros((doc, LANES), BF16)
    ones = extra_lanes(doc, None)
    for pair in range(BLOCK_HEADS // 2):
        lanes = lane_block(step * HEAD_BLOCK + pair * LANES)
        q, k, v = q_ref[:, lanes], k_ref[:, lanes], v_ref[:, lanes]
        g = g_ref[:, pair * LANES : (pair + 1) * LANES]
        q_t, k_t = q.astype(F32).T * SCALE, flip(k)
        g_t = g.astype(F32).T
        inner = g_t * mixed_ref[:, lanes].astype(F32).T
        per_head = []
        for which in range(2):
            h = 2 * pair + which
            minus = jnp.sum(inner[half_rows(which)], axis=0, keepdims=True)
            per_head.append(
                (
                    pick(which, k, ones),
                    pick(which, v, ones),
                    with_extra(which, q_t, False, lse_ref[0, h : h + 1, :]),
                    with_extra(which, g_t, False, minus),
                    pick(which, q, none),
                    pick(which, g, none),
                )
            )
        grad_k = grad_v = None
        for span in spans(doc, Q_BLOCK):
            rows, grad_q, part_k, part_v = span.stop, [], None, None
            for which, (k_of, v_of, q_with, g_with, q_of, g_of) in enumerate(per_head):
                h = 2 * pair + which
                s = dot_nn(k_of[:rows], q_with[:, span])
                p = jnp.exp(s + bias_ref[h, :rows, span].astype(F32))
                ds = (p * dot_nn(v_of[:rows], g_with[:, span])).astype(BF16)
                ds_ref[h, :rows, span] = ds
                grad_q.append(dot_nn(k_t[half_rows(which), :rows], ds))
                to_v = dot_nn(p.astype(BF16), g_of[span])
                to_k = dot_nn(ds, q_of[span])
                part_v = to_v if part_v is None else part_v + to_v
                part_k = to_k if part_k is None else part_k + to_k
            grad_q = (jnp.concatenate(grad_q, axis=0) * SCALE).T
            grad_ref[span, lanes] = grad_q.astype(BF16)
            if grad_v is not None:
                part_v = jnp.concatenate(
                    [part_v[: span.start] + grad_v, part_v[span.start :]], axis=0
                )
                part_k = jnp.concatenate(
                    [part_k[: span.start] + grad_k, part_k[span.start :]], axis=0
                )
            grad_v, grad_k = part_v, part_k
        k_lanes = lane_block(features + step * HEAD_BLOCK + pair * LANES)
        v_lanes = lane_block(2 * features + step * HEAD_BLOCK + pair * LANES)
        grad_ref[:, k_lanes] = (grad_k * SCALE).astype(BF16)
        grad_ref[:, v_lanes] = grad_v.astype(BF16)

    @pl.when(step == pl.num_programs(0) - 1)
    def _():
        stack.wait(0, 1, 2)
        def weight_grads(ref, columns):
            for kind in range(3):
                kind_columns = slice(kind * features + columns.start, kind * features + columns.stop)
                ref[kind] = dot_tn(grad_ref[:, kind_columns], normed_ref[...]).astype(BF16)
            ref[3] = dot_tn(mixed_ref[:, columns], branch_ref[...]).astype(BF16)

        weight_grads(give_ref, slice(0, half))
        swap.start()
        weight_grads(keep_ref, slice(half, features))
        gain_grad_ref[...] = jnp.zeros_like(gain_grad_ref)
        back_ref[...] = dot_nn(grad_ref[...], w_ref[: 3 * features])
        for span in spans(doc, ROW_BLOCK):
            norm_back_into(
                span, back_ref[span], out_ref, None, gain_grad_ref, rows_ref, gain_ref, add_ref
            )
        swap.wait_recv()
        rows = half // count
        for share, sums_ref in enumerate(sums):
            for kind in range(4):
                span = slice(share * rows, (share + 1) * rows)
                to = slice(kind * rows, (kind + 1) * rows)
                sums_ref[to] = low_sum(keep_ref[kind, span], came_ref[kind, span])
        swap.wait_send()
        for hop in hops:
            hop.wait()


def cross_forward_kernel(heads, shares, length_ref, rows_ref, gain_ref, memory_ref, *refs):
    sources = refs[:shares]
    q_ref, k_ref, v_ref, mixed_ref, lse_ref, out_ref = refs[shares : shares + 6]
    w_ref, normed_ref, extra_ref, p_ref, mix_ref, sems = refs[shares + 6 :]
    step = pl.program_id(0)
    (doc, features), slots = rows_ref.shape, memory_ref.shape[0]
    stack = Stack(sources, w_ref, sems, 4, heads * HEAD_DIM)

    @pl.when(step == 0)
    def _():
        stack.start(0, 1, 2, 3)
        norm_into(normed_ref, rows_ref, gain_ref)
        out_ref[...] = rows_ref[...]
        slot = lax.broadcasted_iota(jnp.int32, (slots, LANES), 0)
        extra_ref[...] = extra_lanes(slots, slot < length_ref[0])

    def weights(kind):
        start = pl.multiple_of(kind * features + step * HEAD_BLOCK, HEAD_BLOCK)
        return w_ref[pl.ds(start, HEAD_BLOCK)]

    for kind, (ref, source) in enumerate(
        ((q_ref, normed_ref), (k_ref, memory_ref), (v_ref, memory_ref))
    ):
        stack.wait_at(step == 0, kind)
        ref[...] = dot_nt(source[...], weights(kind)).astype(BF16)

    units = [
        (pair, which, span)
        for pair in range(BLOCK_HEADS // 2)
        for span in spans(doc, Q_BLOCK)
        for which in range(2)
    ]
    ones = jnp.ones((TILE_ROWS, slots), BF16)
    keys = spans(slots, FORWARD_K_BLOCK)

    def lanes_of(pair):
        return slice(pair * LANES, (pair + 1) * LANES)

    def key_side(pair, which):
        return pick(which, k_ref[:, lanes_of(pair)], extra_ref[...])

    def write(pair, which, span, top, total, mixed):
        h = 2 * pair + which
        lse_ref[0, h : h + 1, span] = top + jnp.log(total)
        mix_ref[half_rows(which)] = mixed / total
        if which == 1:
            mixed_ref[span, lanes_of(pair)] = mix_ref[...].T.astype(BF16)

    v_t = [flip(v_ref[:, lanes_of(p)]) for p in range(BLOCK_HEADS // 2)]
    q_t = [q_ref[:, lanes_of(p)].astype(F32).T * SCALE for p in range(BLOCK_HEADS // 2)]

    def begin(unit):
        pair, which, span = unit
        k_of = key_side(pair, which)
        s = dot_nn(k_of[keys[0]], with_extra(which, q_t[pair][:, span], True, None))
        top = jnp.max(s, axis=0, keepdims=True)
        return k_of, s, top, with_extra(which, q_t[pair][:, span], True, top)

    worst = jnp.zeros((1, Q_BLOCK), F32)
    ahead = begin(units[0])
    for i, (pair, which, span) in enumerate(units):
        (k_of, s, top, q_with), slot = ahead, i % 2
        p_ref[slot, keys[0]] = jnp.exp(s - top).astype(BF16)
        for rows in keys[1:]:
            p_ref[slot, rows] = jnp.exp(dot_nn(k_of[rows], q_with)).astype(BF16)
        if i + 1 < len(units):
            ahead = begin(units[i + 1])
        value_side = jnp.concatenate([v_t[pair][half_rows(which)], ones], axis=0)
        mixed = dot_nn(value_side, p_ref[slot])
        total = mixed[HEAD_DIM : HEAD_DIM + 1]
        worst = jnp.maximum(worst, total)
        write(pair, which, span, top, total, mixed[:HEAD_DIM])

    @pl.when(jnp.max(worst) > LARGEST_SUM)
    def _():
        for pair, which, span in units:
            q_with = with_extra(
                which, q_ref[:, lanes_of(pair)].astype(F32).T[:, span] * SCALE, True, None
            )
            k_of = key_side(pair, which)
            s = [dot_nn(k_of[rows], q_with) for rows in keys]
            top = functools.reduce(jnp.maximum, [jnp.max(c, axis=0, keepdims=True) for c in s])
            total = jnp.zeros_like(top)
            for rows, chunk in zip(keys, s):
                p = jnp.exp(chunk - top)
                total = total + jnp.sum(p, axis=0, keepdims=True)
                p_ref[0, rows] = p.astype(BF16)
            mixed = dot_nn(flip(v_ref[:, lanes_of(pair)])[half_rows(which)], p_ref[0])
            write(pair, which, span, top, total, mixed)

    stack.wait_at(step == 0, 3)
    out_ref[...] += dot_nn(mixed_ref[...], weights(3))


def cross_backward_kernel(heads, shares, size, scattered, hops_wanted, length_ref, *refs):
    gain_ref, branch_ref, q_ref, mixed_ref, lse_ref = refs[:5]
    rows_in, memory_in, add_in, k_in, v_in = refs[5:10]
    sources = refs[10 : 10 + shares]
    count = shares // 2
    refs = refs[10 + shares :]
    scatter_in, refs = refs[:scattered], refs[scattered:]
    hidden_in, refs = refs[:hops_wanted], refs[hops_wanted:]
    hidden_out, refs = refs[:hops_wanted], refs[hops_wanted:]
    if scattered:
        scatter_out, refs = refs[0], refs[1:]
        (part_ref, ring_slots, done_ref, scatter_came), refs = refs[-8:-4], refs[:-8] + refs[-4:]
        (ring_send, ring_came, part_sems, done_sems), refs = refs[-4:], refs[:-4]
        scatter = Scatter(size, part_ref, ring_slots, done_ref, ring_send, ring_came)
        part_loads = [
            pltpu.make_async_copy(source, part_ref.at[i], part_sems.at[i])
            for i, source in enumerate(scatter_in)
        ]
    sums, refs = refs[:count], refs[count:]
    memory_out, out_ref, low_ref, gain_grad_ref = refs[:4]
    rows_ref, memory_ref, add_ref, k_ref, v_ref = refs[4:9]
    (
        w_ref,
        normed_ref,
        extra_ref,
        g_ref,
        grad_q_ref,
        grad_ref,
        ds_ref,
        give_ref,
        keep_ref,
        came_ref,
        memory_grad_ref,
        back_ref,
        sems,
        load_sems,
        key_sems,
        out_sems,
        swap_sems,
        hop_sems,
    ) = refs[9:]
    (doc, features), slots = rows_ref.shape, memory_ref.shape[0]
    half, blocks = features // 2, features // HEAD_BLOCK
    stack = Stack(sources, w_ref, sems, 4, heads * HEAD_DIM)
    loads = [
        pltpu.make_async_copy(source, target, load_sems.at[i])
        for i, (source, target) in enumerate(
            ((memory_in, memory_ref), (rows_in, rows_ref), (add_in, add_ref))
        )
    ]

    def key_copies(b):
        lanes = pl.ds(pl.multiple_of(b * HEAD_BLOCK, HEAD_BLOCK), HEAD_BLOCK)
        return [
            pltpu.make_async_copy(source.at[:, lanes], target.at[b], key_sems.at[i, b])
            for i, (source, target) in enumerate(((k_in, k_ref), (v_in, v_ref)))
        ]

    stack.start(3)
    for copy in key_copies(0):
        copy.start()
    if scattered:
        for copy in part_loads:
            copy.start()
    for b in range(1, blocks):
        for copy in key_copies(b):
            copy.start()
    for copy in loads:
        copy.start()
    stack.start(0, 1, 2)
    greet([1, 2][:count], [way[1] for way in ring_ways(size)] if scattered else [])
    hops = [
        to_differing(2, source, target, hop_sems.at[i])
        for i, (source, target) in enumerate(zip(hidden_in, hidden_out))
    ]
    for hop in hops:
        hop.start()
    if scattered:
        for copy in part_loads:
            copy.wait()
        scatter.begin()
    slot = lax.broadcasted_iota(jnp.int32, (slots, LANES), 0)
    extra_ref[...] = extra_lanes(slots, slot < length_ref[0])
    none = jnp.zeros((doc, LANES), BF16)
    stack.wait(3)

    def one_block(step, carry):
        start = pl.multiple_of(3 * features + step * HEAD_BLOCK, HEAD_BLOCK)
        g_ref[...] = dot_nt(branch_ref[...], w_ref[pl.ds(start, HEAD_BLOCK)]).astype(BF16)
        for copy in key_copies(step):
            copy.wait()
        for pair in range(BLOCK_HEADS // 2):
            local = slice(pair * LANES, (pair + 1) * LANES)
            lanes = lane_block(step * HEAD_BLOCK + pair * LANES)
            v_lanes = lane_block(features + step * HEAD_BLOCK + pair * LANES)
            q, g = q_ref[:, lanes], g_ref[:, local]
            q_t, g_t = q.astype(F32).T * SCALE, g.astype(F32).T
            inner = g_t * mixed_ref[:, lanes].astype(F32).T
            per_head = []
            for which in range(2):
                h = 2 * pair + which
                minus = jnp.sum(inner[half_rows(which)], axis=0, keepdims=True)
                per_head.append(
                    (
                        with_extra(which, q_t, True, lse_ref[step, h : h + 1, :]),
                        with_extra(which, g_t, False, minus),
                        pick(which, q, none),
                        pick(which, g, none),
                    )
                )
            for rows in spans(slots, K_BLOCK):
                k, v, extra = k_ref[step, rows, local], v_ref[step, rows, local], extra_ref[rows]
                part_k = part_v = None
                for which, (q_with, g_with, q_of, g_of) in enumerate(per_head):
                    p = jnp.exp(dot_nn(pick(which, k, extra), q_with))
                    ds = (p * dot_nn(pick(which, v, extra), g_with)).astype(BF16)
                    ds_ref[which, rows] = ds
                    to_v = dot_nn(p.astype(BF16), g_of)
                    to_k = dot_nn(ds, q_of)
                    part_v = to_v if part_v is None else part_v + to_v
                    part_k = to_k if part_k is None else part_k + to_k
                grad_ref[rows, lanes] = (part_k * SCALE).astype(BF16)
                grad_ref[rows, v_lanes] = part_v.astype(BF16)
            k_t = flip(k_ref[step, :, local])
            grad_q = [dot_nn(k_t[half_rows(which)], ds_ref[which]) for which in range(2)]
            grad_q_ref[:, lanes] = (jnp.concatenate(grad_q, axis=0) * SCALE).T.astype(BF16)
            if scattered:
                scatter_step(1 + step * (BLOCK_HEADS // 2) + pair)
        return carry

    places = blocks * (BLOCK_HEADS // 2)

    def scatter_step(step):
        if size - 2 >= places:
            scatter.advance(step)
        elif size > 2:

            @pl.when(step <= size - 2)
            def _():
                scatter.advance(step)

    lax.fori_loop(0, blocks, one_block, 0)
    if scattered:

        def rest(step, carry):
            scatter.advance(step)
            return carry

        lax.fori_loop(min(places, size - 2) + 1, size - 1, rest, 0)
        scatter.turn()
        done_hops = [
            to_differing(2, done_ref.at[:, i], scatter_came, done_sems)
            for i in range(1, scattered)
        ]
        for hop in done_hops:
            hop.start()

    for copy in loads:
        copy.wait()
    norm_into(normed_ref, rows_ref, gain_ref)

    def weight_grads(ref, first):
        columns = slice(first, first + half)
        v_columns = slice(features + first, features + first + half)
        ref[0] = dot_tn(grad_q_ref[:, columns], normed_ref[...]).astype(BF16)
        ref[1] = dot_tn(grad_ref[:, columns], memory_ref[...]).astype(BF16)
        ref[2] = dot_tn(grad_ref[:, v_columns], memory_ref[...]).astype(BF16)
        ref[3] = dot_tn(mixed_ref[:, columns], branch_ref[...]).astype(BF16)

    weight_grads(give_ref, 0)
    swap = to_differing(1, give_ref, came_ref, swap_sems)
    swap.start()
    stack.wait(0, 1, 2)
    writes = []
    for i, rows in enumerate(spans(slots, MEMORY_BLOCK)):
        memory_grad_ref[rows] = dot_nn(
            grad_ref[rows], w_ref[features : 3 * features]
        ).astype(BF16)
        writes.append(
            pltpu.make_async_copy(memory_grad_ref.at[rows], memory_out.at[rows], out_sems.at[i])
        )
        writes[-1].start()
    weight_grads(keep_ref, half)
    gain_grad_ref[...] = jnp.zeros_like(gain_grad_ref)
    back_ref[...] = dot_nn(grad_q_ref[...], w_ref[:features])
    for span in spans(doc, ROW_BLOCK):
        norm_back_into(
            span, back_ref[span], out_ref, low_ref, gain_grad_ref, rows_ref, gain_ref, add_ref
        )
    swap.wait_recv()
    rows = half // count
    for share, sums_ref in enumerate(sums):
        for kind in range(4):
            span = slice(share * rows, (share + 1) * rows)
            to = slice(kind * rows, (kind + 1) * rows)
            sums_ref[to] = low_sum(keep_ref[kind, span], came_ref[kind, span])
    swap.wait_send()
    for copy in writes:
        copy.wait()
    for hop in hops:
        hop.wait()
    if scattered:
        for hop in done_hops:
            hop.wait()
        own = done_ref[:, 0]
        scatter_out[...] = low_sum(own, scatter_came[...]) if done_hops else own
        scatter.wait_sent()


def feed_forward_kernel(first, last, rows_ref, gain_ref, cotangent_ref, *refs):
    sources, refs = refs[:2], refs[2:]
    if not first:
        before_in, refs = refs[:2], refs[2:]
    sums, layer_ref, out_ref = refs[:2], refs[2], refs[3]
    if last:
        low_ref, gain_grad_ref = refs[4:6]
        refs = refs[2:]
    (
        wide_ref,
        narrow_ref,
        normed_ref,
        normed_t,
        cotangent_t,
        active_ref,
        grad_ref,
        give_ref,
        keep_ref,
        came_ref,
        layer_in_ref,
        back_in_ref,
        product_ref,
        sems,
        before_sems,
        swap_sems,
    ) = refs[4:]
    step, steps = pl.program_id(0), pl.num_programs(0)
    half = steps // 2
    doc = rows_ref.shape[0]
    hidden = sources[0].shape[0] // 2
    copies = [
        [
            pltpu.make_async_copy(
                source.at[pl.ds(kind * hidden, hidden)],
                stack.at[pl.ds(p * hidden, hidden)],
                sems.at[p, kind],
            )
            for kind, stack in enumerate((wide_ref, narrow_ref))
        ]
        for p, source in enumerate(sources)
    ]
    loads = []
    if not first:
        loads = [
            pltpu.make_async_copy(source, target, before_sems.at[i])
            for i, (source, target) in enumerate(zip(before_in, (layer_in_ref, back_in_ref)))
        ]
    swap = to_differing(1, give_ref, came_ref, swap_sems)

    @pl.when(step == 0)
    def _():
        for pair in copies:
            for copy in pair:
                copy.start()
        for copy in loads:
            copy.start()
        greet([1])
        norm_into(normed_ref, rows_ref, gain_ref)
        for span in spans(doc, ROW_BLOCK):
            normed_t[:, span] = flip(normed_ref[span])
            cotangent_t[:, span] = flip(cotangent_ref[span])

    for p, pair in enumerate(copies):

        @pl.when(step == p * half)
        def _(pair=pair):
            for copy in pair:
                copy.wait()

    units = pl.ds(pl.multiple_of(step * HIDDEN_BLOCK, HIDDEN_BLOCK), HIDDEN_BLOCK)
    activated, slope = gelu_and_slope(dot_nn(wide_ref[units], normed_t[...]))
    active_ref[units] = activated.astype(BF16)
    grad_ref[units] = (dot_nn(narrow_ref[units], cotangent_t[...]) * slope).astype(BF16)

    def store(ref, at):
        rows = pl.ds(pl.multiple_of(at * HIDDEN_BLOCK, HIDDEN_BLOCK), HIDDEN_BLOCK)
        ref[0, rows] = dot_nn(grad_ref[units], normed_ref[...]).astype(BF16)
        ref[1, rows] = dot_nn(active_ref[units], cotangent_ref[...]).astype(BF16)

    @pl.when(step < half)
    def _():
        store(give_ref, step)

    @pl.when(step == half - 1)
    def _():
        swap.start()

    @pl.when(step >= half)
    def _():
        store(keep_ref, step - half)

    @pl.when(step == steps - 1)
    def _():
        for copy in loads:
            copy.wait()
        if last:
            gain_grad_ref[...] = jnp.zeros_like(gain_grad_ref)
        product_ref[...] = dot_tn(active_ref[...], narrow_ref[...])
        for span in spans(doc, ROW_BLOCK):
            layer = rows_ref[span] if first else layer_in_ref[span]
            layer_ref[span] = (layer + product_ref[span]).astype(layer_ref.dtype)
        product_ref[...] = dot_tn(grad_ref[...], wide_ref[...])
        for span in spans(doc, ROW_BLOCK):
            back = product_ref[span]
            if not first:
                back = back + back_in_ref[span]
            if last:
                norm_back_into(
                    span, back, out_ref, low_ref, gain_grad_ref, rows_ref, gain_ref, cotangent_ref
                )
            else:
                out_ref[span] = back
        swap.wait_recv()
        for kind, sums_ref in enumerate(sums):
            for span in spans(hidden, HIDDEN_BLOCK):
                sums_ref[span] = low_sum(keep_ref[kind, span], came_ref[kind, span])
        swap.wait_send()


def pack_kernel(flipped, *refs):
    out_ref, start = refs[-1], 0
    for source, turn in zip(refs[:-1], flipped):
        if source.shape[-1] != out_ref.shape[1] and not turn:
            out_ref[start:] = jnp.zeros((TABLE_ROWS, out_ref.shape[1]), BF16)
            out_ref[start : start + source.shape[0], : source.shape[1]] = source[...]
            continue
        rows = source.shape[1] if turn else source.shape[0]
        span = slice(start, start + rows)
        out_ref[span] = flip(source[...]) if turn else source[...]
        start += rows


def finish_kernel(*refs):
    sources, outs, refs = refs[:4], refs[4:14], refs[14:]
    ins, wides, in_sems, out_sems = refs[:4], refs[4:14], refs[14], refs[15]
    loads, writes = [], []
    for i, (source, target) in enumerate(zip(sources, ins)):
        for j, span in enumerate(spans(target.shape[0], FINISH_BLOCK)):
            loads.append(
                pltpu.make_async_copy(source.at[span], target.at[span], in_sems.at[i, j])
            )
            loads[-1].start()

    def write(i, part):
        writes.append(
            pltpu.make_async_copy(wides[i].at[part], outs[i].at[part], out_sems.at[len(writes)])
        )
        writes[-1].start()

    waiting = iter(loads)
    hidden = wides[1].shape[0]
    for span in spans(hidden, FINISH_BLOCK):
        next(waiting).wait()
        for part in spans(FINISH_BLOCK, LANES):
            rows = slice(span.start + part.start, span.start + part.stop)
            wides[0][:, rows] = ins[0][rows].astype(F32).T
        write(0, (slice(None), span))
    for span in spans(hidden, FINISH_BLOCK):
        next(waiting).wait()
        wides[1][span] = ins[1][span].astype(F32)
        write(1, span)
    for i in (2, 3):
        for _ in spans(ins[i].shape[0], FINISH_BLOCK):
            next(waiting).wait()
        rows = wides[2].shape[0]
        for kind in range(4):
            at = 2 + 4 * (i - 2) + kind
            wides[at][...] = ins[i][kind * rows : (kind + 1) * rows].astype(F32)
            write(at, slice(None))
    for copy in writes:
        copy.wait()


def params(size=VMEM_BYTES):
    return pltpu.CompilerParams(vmem_limit_bytes=size)


def cost():
    return pl.CostEstimate(flops=1 << 20, bytes_accessed=1 << 16, transcendentals=0)


def shape(dims, dtype):
    return jax.ShapeDtypeStruct(dims, dtype)


def whole(array):
    return pl.BlockSpec(
        array.shape, lambda *_: (0,) * len(array.shape), pipeline_mode=pl.Buffered(1)
    )


def result(array):
    return pl.BlockSpec(array.shape, lambda *_: (0,) * len(array.shape))


def columns(rows):
    return pl.BlockSpec((rows, HEAD_BLOCK), lambda i: (0, i))


def anywhere(arrays):
    return [pl.BlockSpec(memory_space=pl.ANY) for _ in arrays]


SCALAR = pl.BlockSpec(memory_space=pltpu.SMEM)


def call(
    kernel, name, grid, in_specs, out_specs, out_shape, scratch, args, channel=None
):
    size = VMEM_OF[name]
    compiler_params = params(size)
    if channel is not None:
        compiler_params = pltpu.CompilerParams(
            vmem_limit_bytes=size, collective_id=channel, has_side_effects=True
        )
    return pl.pallas_call(
        kernel,
        grid=grid,
        in_specs=in_specs,
        out_specs=out_specs,
        out_shape=out_shape,
        scratch_shapes=scratch,
        compiler_params=compiler_params,
        cost_estimate=cost(),
        name=name,
    )(*args)


def pack(*parts):
    arrays, flipped = zip(*parts)
    features = arrays[0].shape[0] if flipped[0] else arrays[0].shape[1]
    rows = [a.shape[1] if turn else a.shape[0] for a, turn in parts]
    if arrays[-1].shape[1] < features and not flipped[-1]:
        rows[-1] = TABLE_ROWS
    rows = sum(rows)
    return pl.pallas_call(
        functools.partial(pack_kernel, flipped),
        out_shape=shape((rows, features), BF16),
        compiler_params=params(),
        cost_estimate=cost(),
        name="pack",
    )(*arrays)


def self_forward(heads, buckets, rows, gain, weights, ids):
    doc, features = rows.shape
    shares, steps = len(weights), features // HEAD_BLOCK
    narrow, tall = shape((doc, features), BF16), shape((doc, features), F32)
    scores = shape((steps * BLOCK_HEADS, doc, doc), BF16)
    out_shape = (*[narrow] * 4, shape((steps, 8, doc), F32), scores, tall)
    return call(
        functools.partial(self_forward_kernel, heads, buckets, shares),
        "self_forward",
        (steps,),
        [whole(rows), whole(gain), whole(ids), *anywhere(weights)],
        (
            *[columns(doc)] * 4,
            pl.BlockSpec((1, 8, doc), lambda i: (i, 0, 0)),
            pl.BlockSpec((BLOCK_HEADS, doc, doc), lambda i: (i, 0, 0)),
            result(tall),
        ),
        out_shape,
        [
            pltpu.VMEM((4 * features, features), BF16),
            pltpu.VMEM((shares, TABLE_ROWS, features), BF16),
            pltpu.VMEM((TABLE_ROWS, LANES), F32),
            pltpu.VMEM((doc, features), BF16),
            pltpu.SemaphoreType.DMA((shares, 5)),
        ],
        (rows, gain, ids, *weights),
    )


def self_backward(heads, rows, gain, branch, add, saved, weights, hops):
    doc, features = rows.shape
    shares, steps = len(weights), features // HEAD_BLOCK
    count = shares // 2
    *arrays, lse, bias = saved
    packed = pltpu.VMEM((4, features // 2, features), BF16)
    scores = pl.BlockSpec((BLOCK_HEADS, doc, doc), lambda i: (i, 0, 0))
    out_shape = (
        *[shape(h.shape, BF16) for h in hops],
        *[shape((4 * heads * HEAD_DIM, features), BF16)] * count,
        shape((steps * BLOCK_HEADS, doc, doc), BF16),
        shape((doc, features), F32),
        shape((8, features), F32),
    )
    return call(
        functools.partial(self_backward_kernel, heads, shares),
        "self_backward",
        (steps,),
        [
            *[whole(a) for a in (rows, gain, branch, add, *arrays)],
            pl.BlockSpec((1, 8, doc), lambda i: (i, 0, 0)),
            scores,
            *anywhere(weights),
            *anywhere(hops),
        ],
        (
            *anywhere(hops),
            *[result(o) for o in out_shape[len(hops) : len(hops) + count]],
            scores,
            result(out_shape[-2]),
            result(out_shape[-1]),
        ),
        out_shape,
        [
            pltpu.VMEM((4 * features, features), BF16),
            pltpu.VMEM((doc, features), BF16),
            pltpu.VMEM((doc, HEAD_BLOCK), BF16),
            pltpu.VMEM((doc, 3 * features), BF16),
            pltpu.VMEM((doc, features), F32),
            packed,
            packed,
            packed,
            pltpu.SemaphoreType.DMA((shares, 4)),
            pltpu.SemaphoreType.DMA((2,)),
            pltpu.SemaphoreType.DMA((2,)),
        ],
        (rows, gain, branch, add, *arrays, lse, bias, *weights, *hops),
        channel=4,
    )


def cross_forward(heads, rows, gain, memory, length, weights):
    (doc, features), slots = rows.shape, memory.shape[0]
    shares, steps = len(weights), features // HEAD_BLOCK
    query, key = shape((doc, features), BF16), shape((slots, features), BF16)
    tall = shape((doc, features), F32)
    return call(
        functools.partial(cross_forward_kernel, heads, shares),
        "cross_forward",
        (steps,),
        [SCALAR, whole(rows), whole(gain), whole(memory), *anywhere(weights)],
        (
            columns(doc),
            columns(slots),
            columns(slots),
            columns(doc),
            pl.BlockSpec((1, 8, doc), lambda i: (i, 0, 0)),
            result(tall),
        ),
        (query, key, key, query, shape((steps, 8, doc), F32), tall),
        [
            pltpu.VMEM((4 * features, features), BF16),
            pltpu.VMEM((doc, features), BF16),
            pltpu.VMEM((slots, LANES), BF16),
            pltpu.VMEM((2, slots, Q_BLOCK), BF16),
            pltpu.VMEM((LANES, Q_BLOCK), F32),
            pltpu.SemaphoreType.DMA((shares, 4)),
        ],
        (length, rows, gain, memory, *weights),
    )


def cross_backward(
    heads, size, rows, gain, memory, length, branch, add, saved, weights, scattered, hops
):
    (doc, features), slots = rows.shape, memory.shape[0]
    shares, blocks = len(weights), features // HEAD_BLOCK
    count = shares // 2
    blocks_out, ring_scratch = [], []
    if scattered:
        number, part = len(scattered), scattered[0].shape
        block = (2, part[0] // (2 * size), features)
        blocks_out = [shape(block, BF16)]
        steps = pltpu.SemaphoreType.DMA((2, size - 1))
        ring_scratch = [
            pltpu.VMEM((number, *part), BF16),
            pltpu.VMEM((2, size - 1, number, *block[1:]), BF16),
            pltpu.VMEM((2, number, *block[1:]), BF16),
            pltpu.VMEM(block, BF16),
            steps,
            steps,
            pltpu.SemaphoreType.DMA((number,)),
            pltpu.SemaphoreType.DMA((2,)),
        ]
    out_shape = (
        *[shape(h.shape, BF16) for h in hops],
        *blocks_out,
        *[shape((4 * heads * HEAD_DIM, features), BF16)] * count,
        shape((slots, features), BF16),
        shape((doc, features), F32),
        shape((doc, features), BF16),
        shape((8, features), F32),
    )
    query, key, value, mixed, lse = saved
    near = (gain, branch, query, mixed, lse)
    far = (rows, memory, add, key, value, *weights, *scattered, *hops)
    vmem, hbm = pl.BlockSpec(memory_space=pltpu.VMEM), pl.BlockSpec(memory_space=pl.ANY)
    packed = pltpu.VMEM((4, features // 2, features), BF16)
    key_block = pltpu.VMEM((blocks, slots, HEAD_BLOCK), BF16)
    return call(
        functools.partial(
            cross_backward_kernel, heads, shares, size, len(scattered), len(hops)
        ),
        "cross_backward",
        (),
        [SCALAR, *[vmem for _ in near], *[hbm for _ in far]],
        (
            *[hbm] * len(hops),
            *[vmem] * len(blocks_out),
            *[vmem] * count,
            hbm,
            vmem,
            vmem,
            vmem,
        ),
        out_shape,
        [
            pltpu.VMEM((doc, features), F32),
            pltpu.VMEM((slots, features), BF16),
            pltpu.VMEM((doc, features), F32),
            key_block,
            key_block,
            pltpu.VMEM((4 * features, features), BF16),
            pltpu.VMEM((doc, features), BF16),
            pltpu.VMEM((slots, LANES), BF16),
            pltpu.VMEM((doc, HEAD_BLOCK), BF16),
            pltpu.VMEM((doc, features), BF16),
            pltpu.VMEM((slots, 2 * features), BF16),
            pltpu.VMEM((2, slots, doc), BF16),
            packed,
            packed,
            packed,
            pltpu.VMEM((slots, features), BF16),
            pltpu.VMEM((doc, features), F32),
            pltpu.SemaphoreType.DMA((shares, 4)),
            pltpu.SemaphoreType.DMA((3,)),
            pltpu.SemaphoreType.DMA((2, blocks)),
            pltpu.SemaphoreType.DMA((slots // MEMORY_BLOCK,)),
            pltpu.SemaphoreType.DMA((2,)),
            pltpu.SemaphoreType.DMA((max(len(hops), 1), 2)),
            *ring_scratch,
        ],
        (length, *near, *far),
        channel=1,
    )


def feed_forward(rows, gain, cotangent, weights, before, last):
    (doc, features), shares = rows.shape, len(weights)
    share = weights[0].shape[0] // 2
    hidden = share * shares
    steps = hidden // HIDDEN_BLOCK
    summed, tall = shape((share, features), BF16), shape((doc, features), F32)
    low = shape((doc, features), BF16)
    rest = [low, tall, low, shape((8, features), F32)] if last else [tall, tall]
    kept, added = pltpu.VMEM((2, share, features), BF16), pltpu.VMEM(tall.shape, F32)
    return call(
        functools.partial(feed_forward_kernel, not before, last),
        "feed_forward",
        (steps,),
        [whole(rows), whole(gain), whole(cotangent), *anywhere(weights), *anywhere(before)],
        (result(summed), result(summed), *[result(o) for o in rest]),
        (summed, summed, *rest),
        [
            pltpu.VMEM((hidden, features), BF16),
            pltpu.VMEM((hidden, features), BF16),
            pltpu.VMEM((doc, features), BF16),
            pltpu.VMEM((features, doc), BF16),
            pltpu.VMEM((features, doc), BF16),
            pltpu.VMEM((hidden, doc), BF16),
            pltpu.VMEM((hidden, doc), BF16),
            kept,
            kept,
            kept,
            added,
            added,
            added,
            pltpu.SemaphoreType.DMA((shares, 2)),
            pltpu.SemaphoreType.DMA((2,)),
            pltpu.SemaphoreType.DMA((2,)),
        ],
        (rows, gain, cotangent, *weights, *before),
        channel=3 if before else 2,
    )


def finish(sum_wide, sum_narrow, sum_cross, sum_self):
    rows, features = sum_self.shape
    hidden, part = sum_wide.shape[0], shape((rows // 4, features), F32)
    out_shape = [shape((features, hidden), F32), shape((hidden, features), F32), *[part] * 8]
    sources = (sum_wide, sum_narrow, sum_cross, sum_self)
    writes = 2 * hidden // FINISH_BLOCK + 8
    wide, narrow, *parts = pl.pallas_call(
        finish_kernel,
        in_specs=anywhere(sources),
        out_specs=anywhere(out_shape),
        out_shape=out_shape,
        scratch_shapes=[
            *[pltpu.VMEM(source.shape, BF16) for source in sources],
            *[pltpu.VMEM(out.shape, F32) for out in out_shape],
            pltpu.SemaphoreType.DMA((4, hidden // FINISH_BLOCK)),
            pltpu.SemaphoreType.DMA((writes,)),
        ],
        compiler_params=params(),
        cost_estimate=cost(),
        name="finish",
    )(*sources)
    return wide, narrow, parts[4:], parts[:4]


def share_place(row, other, peers):
    j, bit = 0, 1
    while bit < peers:
        j = j + bit * ((row // bit + other // bit) % 2)
        bit *= 2
    return (j % 2) * (j // 2) + (1 - j % 2) * (peers // 2 + j // 2)


def tail_kernel(size, peers, buckets, heads, gathered, counts, *refs):
    parts = []
    for count in counts:
        parts.append(refs[:count])
        refs = refs[count:]
    arrays, shares = len(counts) + 1, peers // 2
    last_refs, refs = refs[:shares], refs[shares:]
    ids_ref, ds_ref, *gain_refs = refs[:5]
    outs, small_out_ref, refs = refs[5 : 5 + arrays], refs[5 + arrays], refs[6 + arrays :]
    slots, refs = refs[:arrays], refs[arrays:]
    firsts, refs = refs[:arrays], refs[arrays:]
    far_came_ref, part_ref, scores_ref, bucket_ref = refs[:4]
    small_ref, near_ref, far_ref = refs[4:7]
    send, came, send_out, came_out, small_sems, hop_sems, local_sems = refs[7:]
    parts.append((part_ref,))
    me, row = lax.axis_index("dp"), lax.axis_index("mp")
    ways = ring_ways(size)
    doc = ids_ref.shape[0]
    mesh = pl.DeviceIdType.MESH

    load_scores = pltpu.make_async_copy(ds_ref, scores_ref, local_sems.at[0])
    load_scores.start()

    barrier = pltpu.get_barrier_semaphore()

    def greet(t, carry):
        pl.semaphore_signal(
            barrier, inc=1, device_id=((me + t) % size, row), device_id_type=mesh
        )
        return carry

    lax.fori_loop(1, size, greet, 0)
    for t in range(1, peers):
        pl.semaphore_signal(
            barrier, inc=1, device_id=(me, (row + t) % peers), device_id_type=mesh
        )
    pl.semaphore_wait(barrier, size - 1 + peers - 1)

    def block(i, way, number):
        rows = outs[i].shape[0] // (2 * size)
        return pl.ds(pl.multiple_of((way * size + number) * rows, 16), rows)

    def part(i, span):
        total = parts[i][0][span].astype(F32)
        for ref in parts[i][1:]:
            total = total + ref[span].astype(F32)
        return total

    def first_copy(i, way):
        return remote(
            firsts[i].at[way],
            slots[i].at[way, 0],
            send.at[i, way, 0],
            came.at[i, way, 0],
            (ways[way][1], row),
        )

    def next_copy(i, way, step):
        return remote(
            slots[i].at[way, step - 1],
            slots[i].at[way, step],
            send.at[i, way, step],
            came.at[i, way, step],
            (ways[way][1], row),
        )

    def wait_came(i, way, step):
        remote(
            slots[i].at[way, step],
            slots[i].at[way, step],
            send.at[i, way, step],
            came.at[i, way, step],
            (ways[way][1], row),
        ).wait_recv()

    def out_copy(i, way, step):
        span = block(i, way, (ways[way][0] + 1 - step + size) % size)
        return remote(
            outs[i].at[span],
            outs[i].at[span],
            send_out.at[i, way, step],
            came_out.at[i, way, step],
            (ways[way][1], row),
        )

    def begin(rings):
        for i, way in rings:
            firsts[i][way] = part(i, block(i, way, ways[way][0])).astype(BF16)
            first_copy(i, way).start()

    def plus_part(i, way, step):
        span = block(i, way, (ways[way][0] - step - 1 + size) % size)
        total = slots[i][way, step].astype(F32) + part(i, span)
        return span, total.astype(BF16)

    def advance(rings, step):
        for i, way in rings:
            wait_came(i, way, step - 1)
            slots[i][way, step - 1] = plus_part(i, way, step - 1)[1]
            next_copy(i, way, step).start()

    def turn(rings):
        for i, way in rings:
            wait_came(i, way, size - 2)
            span, total = plus_part(i, way, size - 2)
            outs[i][span] = total
            out_copy(i, way, 0).start()

    def pass_on(rings, step):
        for i, way in rings:
            out_copy(i, way, step - 1).wait_recv()
            out_copy(i, way, step).start()

    ready = [(i, way) for i in range(gathered) for way in range(2)]
    early = [(i, way) for i in range(gathered, arrays - 1) for way in range(2)]
    late = [(arrays - 1, way) for way in range(2)]

    other_chip = None
    if shares == 2:
        other_chip = to_differing(2, last_refs[1], far_came_ref, hop_sems)
        other_chip.start()
    begin(early)
    for i, way in ready:
        outs[i][block(i, way, (ways[way][0] + 1) % size)] = parts[i][0][way]
        out_copy(i, way, 0).start()

    rows_used, per_row = bucket_ref.shape[0], ds_ref.shape[0] // bucket_ref.shape[0]
    units = rows_used * buckets
    per_round = -(-units // max(2 * (size - 2), 1))

    def bucket_unit(u, carry):
        r, b = u // buckets, u % buckets
        sums = [jnp.zeros((8, LANES), F32) for _ in range(per_row)]
        for c in range(0, doc, LANES):
            hit = ids_ref[: c + LANES, c : c + LANES] == b
            for h in range(per_row):
                grads = scores_ref[r * per_row + h, : c + LANES, c : c + LANES].astype(F32)
                kept = jnp.where(hit, grads, 0.0).reshape(-1, 8, LANES)
                sums[h] = sums[h] + jnp.sum(kept, axis=0)
        for h in range(per_row):
            bucket_ref[r, h, pl.ds(b, 1), :] = jnp.sum(sums[h], axis=0, keepdims=True)
        return carry

    def bucket_round(k):
        low = jnp.minimum(k * per_round, units)
        lax.fori_loop(low, jnp.minimum(low + per_round, units), bucket_unit, 0)

    bucket_ref[...] = jnp.zeros_like(bucket_ref)
    part_ref[...] = jnp.zeros_like(part_ref)
    load_scores.wait()

    def early_step(step, carry):
        advance(early, step)
        pass_on(ready, step)
        bucket_round(step - 1)
        return carry

    begin_late = LATE_STEP if size - 1 > LATE_STEP else size - 1
    lax.fori_loop(1, min(begin_late + 1, size - 1), early_step, 0)
    if begin_late == size - 1:
        turn(early)
    used = slice(0, last_refs[0].shape[0])
    if other_chip is None:
        part_ref[used] = last_refs[0][...]
    else:
        other_chip.wait_recv()
        part_ref[used] = low_sum(last_refs[0][...], far_came_ref[...])
    begin(late)

    def both_step(step, carry):
        early_step(step, carry)
        advance(late, step - begin_late)
        return carry

    def middle_step(step, carry):
        pass_on(early, step)
        advance(late, step + size - 1 - begin_late)
        bucket_round(size - 2 + step - 1)
        return carry

    def end_step(step, carry):
        pass_on(early, step)
        pass_on(late, step - begin_late)
        bucket_round(size - 2 + step - 1)
        return carry

    late_passed = 0
    if begin_late < size - 1:
        lax.fori_loop(begin_late + 1, size - 1, both_step, 0)
        turn(early)
        advance(late, size - 1 - begin_late)
        lax.fori_loop(1, begin_late, middle_step, 0)
        pass_on(early, begin_late)
        turn(late)
        bucket_round(size - 2 + begin_late - 1)
        lax.fori_loop(begin_late + 1, size - 1, end_step, 0)
        late_passed = size - 2 - begin_late
    else:
        lax.fori_loop(1, size - 1, middle_step, 0)
        turn(late)
    if size == 2:
        lax.fori_loop(0, units, bucket_unit, 0)

    features = gain_refs[0].shape[1]
    per_gain = features // LANES
    gain_rows = len(gain_refs) * per_gain
    small_ref[...] = jnp.zeros_like(small_ref)
    for i, ref in enumerate(gain_refs):
        total = jnp.sum(ref[...], axis=0, keepdims=True)
        for c in range(per_gain):
            at = i * per_gain + c
            small_ref[at : at + 1, :] = total[:, c * LANES : (c + 1) * LANES]
    for r in range(rows_used):
        block_sums = bucket_ref[r].reshape(LANES, LANES).T
        at = gain_rows + r
        small_ref[at : at + 1, :] = jnp.sum(block_sums, axis=0, keepdims=True)

    def near_copy(t):
        return remote(
            small_ref,
            near_ref.at[row],
            small_sems.at[0, t],
            small_sems.at[1, t],
            (me, (row + t) % peers),
        )

    def far_copy(t):
        return remote(
            far_ref.at[me],
            far_ref.at[me],
            small_sems.at[2, t],
            small_sems.at[3, t],
            ((me + t) % size, row),
        )

    for t in range(1, peers):
        near_copy(t).start()
    near_ref[pl.ds(row, 1)] = small_ref[...][None]
    for t in range(1, peers):
        near_copy(t).wait_recv()
    own = rows_used // peers
    total, sums = None, None
    for k in range(peers):
        gains = near_ref[k, :gain_rows]
        mine = near_ref[k, pl.ds(gain_rows + own * share_place(row, k, peers), own)]
        total = gains if total is None else total + gains
        sums = mine if sums is None else sums + mine
    small_ref_rows = far_ref.shape[1]
    far_ref[pl.ds(me, 1)] = jnp.concatenate(
        [total, sums, jnp.zeros((small_ref_rows - gain_rows - own, LANES), F32)], axis=0
    )[None]

    def far_start(t, carry):
        far_copy(t).start()
        return carry

    lax.fori_loop(1, size, far_start, 0)

    def late_step(step, carry):
        pass_on(late, step)
        return carry

    lax.fori_loop(1 + late_passed, size - 1, late_step, 0)

    def far_wait(t, carry):
        far_copy(t).wait()
        return carry

    lax.fori_loop(1, size, far_wait, 0)

    def far_add(k, total):
        return total + far_ref[k]

    small_out_ref[...] = lax.fori_loop(1, size, far_add, far_ref[0])
    for i, way in ready + early + late:
        out_copy(i, way, size - 2).wait_recv()

    for t in range(1, peers):
        near_copy(t).wait_send()
    if other_chip is not None:
        other_chip.wait_send()
    for i, way in early + late:
        first_copy(i, way).wait_send()

    def sent(step, carry):
        for i, way in early + late:
            next_copy(i, way, step).wait_send()
        return carry

    lax.fori_loop(1, size - 1, sent, 0)

    def sent_out(step, carry):
        for i, way in ready + early + late:
            out_copy(i, way, step).wait_send()
        return carry

    lax.fori_loop(0, size - 1, sent_out, 0)


def tail_sums(size, peers, buckets, heads, blocks, terms, last, ids, ds, gains):
    assert peers in (2, 4)
    grain = 2 * 16 * size
    features = last[0].shape[1]
    rows = [size * 2 * b.shape[1] for b in blocks]
    rows += [arrays[0].shape[0] for arrays in terms]
    rows.append(last[0].shape[0])
    padded = [r + -r % grain for r in rows]
    parts = [[b] for b in blocks]
    for arrays, r, p in zip(terms, rows[len(blocks) :], padded[len(blocks) :]):
        parts.append([jnp.pad(a, ((0, p - r), (0, 0))) for a in arrays])
    flat = [a for arrays in parts for a in arrays]
    lines = peers * (-(-heads * buckets // LANES))
    small = len(gains) * features // LANES + lines
    small = shape((small + -small % 8, LANES), F32)
    vmem, hbm = pl.BlockSpec(memory_space=pltpu.VMEM), pl.BlockSpec(memory_space=pl.ANY)
    steps = pltpu.SemaphoreType.DMA((len(rows), 2, size - 1))

    def ring_slots(i, steps):
        if i < len(blocks):
            return pltpu.VMEM((2, 1, 16, LANES), BF16)
        return pltpu.VMEM((2, *steps, padded[i] // (2 * size), features), BF16)

    *sums, small = pl.pallas_call(
        functools.partial(
            tail_kernel, size, peers, buckets, heads, len(blocks), [len(a) for a in parts]
        ),
        in_specs=[
            *[vmem] * (len(flat) + 1),
            *[hbm] * (len(last) - 1),
            vmem,
            hbm,
            *[vmem] * len(gains),
        ],
        out_specs=[vmem] * (len(rows) + 1),
        out_shape=[*[shape((p, features), BF16) for p in padded], small],
        scratch_shapes=[
            *[ring_slots(i, (size - 1,)) for i in range(len(rows))],
            *[ring_slots(i, ()) for i in range(len(rows))],
            pltpu.VMEM((rows[-1], features), BF16),
            pltpu.VMEM((padded[-1], features), BF16),
            pltpu.VMEM(ds.shape, BF16),
            pltpu.VMEM((lines, LANES // buckets, buckets, LANES), F32),
            pltpu.VMEM(small.shape, F32),
            pltpu.VMEM((peers, *small.shape), F32),
            pltpu.VMEM((size, *small.shape), F32),
            steps,
            steps,
            steps,
            steps,
            pltpu.SemaphoreType.DMA((4, max(size, peers))),
            pltpu.SemaphoreType.DMA((2,)),
            pltpu.SemaphoreType.DMA((1,)),
        ],
        compiler_params=pltpu.CompilerParams(
            vmem_limit_bytes=VMEM_BYTES, collective_id=0, has_side_effects=True
        ),
        cost_estimate=cost(),
        name="tail_sums",
    )(*flat, *last, ids, ds, *gains)
    return [total[:r] for total, r in zip(sums, rows)], small


def swap(array, bit, size):
    return lax.ppermute(array, "mp", [(i, i ^ bit) for i in range(size)])


def after(array, *others):
    return lax.optimization_barrier((array, others))[0]


def shards(
    decoder_rows,
    memory_rows,
    decoder_token_length,
    memory_length,
    bucket_ids,
    relative_bucket_bias,
    self_gain,
    self_query,
    self_key,
    self_value,
    self_out,
    cross_gain,
    cross_query,
    cross_key,
    cross_value,
    cross_out,
    hidden_gain,
    widen_weight,
    narrow_weight,
    layer_cotangent,
):
    dp_size = lax.axis_size("dp")
    mp_size = lax.axis_size("mp")
    me = lax.axis_index("mp")
    doc, features = decoder_rows.shape
    slots = memory_rows.shape[0]
    cols = self_query.shape[1]
    heads = cols // HEAD_DIM
    buckets = relative_bucket_bias.shape[0]
    order = [*range(1, mp_size, 2), *range(0, mp_size, 2)]

    doc_length = lax.dynamic_index_in_dim(decoder_token_length, me, keepdims=False)
    doc_memory = lax.dynamic_index_in_dim(memory_length, me)
    position = jnp.arange(doc, dtype=jnp.int32)
    allowed = (position[:, None] <= position[None, :]) & (position[:, None] < doc_length)
    ids = jnp.where(allowed, bucket_ids.T, buckets)
    own_self = pack(
        (self_query.T, False),
        (self_key.T, False),
        (self_value.T, False),
        (self_out, False),
        (relative_bucket_bias.T, False),
    )
    own_cross = pack(
        (cross_query.T, False), (cross_key.T, False), (cross_value.T, False), (cross_out, False)
    )
    own_hidden = pack((widen_weight, True), (narrow_weight, False))

    def first_hops(own):
        shares, bit = {0: own}, mp_size // 2
        while bit > 1:
            for j in list(shares):
                shares[j | bit] = swap(shares[j], bit, mp_size)
            bit //= 2
        return shares

    def last_hop(shares, *others):
        if 1 not in shares:
            shares[1] = swap(shares[0], 1, mp_size)
        for j in range(2, mp_size, 2):
            shares[j] = after(shares[j], *others)
            shares[j | 1] = swap(shares[j], 1, mp_size)
        return shares

    near_self = first_hops(own_self)
    near_self[1] = swap(own_self, 1, mp_size)
    memory_rows = after(memory_rows, own_self)
    w_self = last_hop(near_self, own_cross, own_hidden, ids)
    w_self = [w_self[j] for j in order]
    near_cross = first_hops(own_cross)
    near_hidden = first_hops(own_hidden)
    near_hidden[1] = swap(own_hidden, 1, mp_size)
    memory_seen = lax.all_to_all(
        memory_rows.reshape(dp_size, slots // dp_size, features), "dp", 0, 0
    ).reshape(slots, features)

    gain_self = self_gain.astype(F32)[None]
    gain_cross = cross_gain.astype(F32)[None]
    gain_hidden = hidden_gain.astype(F32)[None]

    *saved_self, after_self = self_forward(heads, buckets, decoder_rows, gain_self, w_self, ids)
    w_cross = last_hop(near_cross, after_self)
    w_cross = [w_cross[j] for j in order]
    *saved_cross, after_cross = cross_forward(
        heads, after_self, gain_cross, memory_seen, doc_memory, w_cross
    )

    before, wide_sums, narrow_sums, w_hidden = (), [], [], near_hidden
    for j in range(0, mp_size, 2):
        wide_sum, narrow_sum, *before = feed_forward(
            after_cross,
            gain_hidden,
            layer_cotangent,
            [w_hidden[j + 1], w_hidden[j]],
            before,
            j == mp_size - 2,
        )
        wide_sums.append(wide_sum)
        narrow_sums.append(narrow_sum)
        if j == 0:
            w_hidden = last_hop(near_hidden, before[0])
    layer_output, grad_after_cross, branch, hidden_gain_grad = before

    scattered, hops = wide_sums, narrow_sums[1:]
    if wide_sums[0].shape[0] % (2 * 16 * dp_size):
        scattered, hops = [], wide_sums[1:] + narrow_sums[1:]
    *sums, grad_memory, grad_after_self, branch, cross_gain_grad = cross_backward(
        heads,
        dp_size,
        after_self,
        gain_cross,
        memory_seen,
        doc_memory,
        branch,
        grad_after_cross,
        saved_cross,
        w_cross,
        scattered,
        hops,
    )
    came, sums = sums[: len(hops)], sums[len(hops) :]
    if scattered:
        blocks, terms, cross_sums = sums[:1], [narrow_sums[:1] + came], sums[1:]
    else:
        blocks, cross_sums = [], sums
        hidden = [wide_sums[0], narrow_sums[0]], came
        terms = [[jnp.concatenate(both, axis=0) for both in hidden if both]]
    memory_grad = lax.all_to_all(
        grad_memory.reshape(dp_size, slots // dp_size, features), "dp", 0, 0
    ).reshape(slots, features)

    *sums, score_grads, input_grad, self_gain_grad = self_backward(
        heads,
        decoder_rows,
        gain_self,
        branch,
        grad_after_self,
        saved_self,
        w_self,
        cross_sums[1:],
    )
    cross_sums[1:], last = sums[: len(cross_sums) - 1], sums[len(cross_sums) - 1 :]
    (*hidden, sum_cross, sum_self), small = tail_sums(
        dp_size,
        mp_size,
        buckets,
        heads,
        blocks,
        terms + [cross_sums],
        last,
        ids,
        score_grads,
        (self_gain_grad, cross_gain_grad, hidden_gain_grad),
    )
    wide_grad, narrow_grad, self_grads, cross_grads = finish(
        *(hidden if scattered else jnp.split(hidden[0], 2)), sum_cross, sum_self
    )
    gain_rows = 3 * features // LANES
    gains = small[:gain_rows].reshape(3, features)
    lines = -(-heads * buckets // LANES)
    sums = small[gain_rows : gain_rows + lines, : heads // lines * buckets]
    position_grad = sums.reshape(heads, buckets).T

    return (
        layer_output,
        input_grad,
        memory_grad,
        position_grad,
        gains[0],
        *[grad.T for grad in self_grads[:3]],
        self_grads[3],
        gains[1],
        *[grad.T for grad in cross_grads[:3]],
        cross_grads[3],
        gains[2],
        wide_grad,
        narrow_grad,
    )


def solution(mesh):
    return jax.shard_map(
        shards,
        mesh=mesh,
        in_specs=(
            P(("dp", "mp"), None),
            P(("dp", "mp"), None),
            P("dp"),
            P("dp"),
            P(),
            P(None, "mp"),
            P(),
            P(None, "mp"),
            P(None, "mp"),
            P(None, "mp"),
            P("mp", None),
            P(),
            P(None, "mp"),
            P(None, "mp"),
            P(None, "mp"),
            P("mp", None),
            P(),
            P(None, "mp"),
            P("mp", None),
            P(("dp", "mp"), None),
        ),
        out_specs=(
            P(("dp", "mp"), None),
            P(("dp", "mp"), None),
            P(("dp", "mp"), None),
            P(None, "mp"),
            P(),
            P(None, "mp"),
            P(None, "mp"),
            P(None, "mp"),
            P("mp", None),
            P(),
            P(None, "mp"),
            P(None, "mp"),
            P(None, "mp"),
            P("mp", None),
            P(),
            P(None, "mp"),
            P("mp", None),
        ),
        check_vma=False,
    )
```

```python
import functools

import jax
import jax.numpy as jnp
from jax import lax
from jax.experimental import pallas as pl
from jax.experimental.pallas import tpu as pltpu
from jax.sharding import PartitionSpec as P

HEAD_DIM = 64
NORM_EPS = 1e-06
MASKED = -1e30
SCALE = HEAD_DIM**-0.5
BF16 = jnp.bfloat16
F32 = jnp.float32
LANES = 128
TABLE_ROWS = 16
TILE_ROWS = 16
LARGEST_SUM = 1e30
LATE_STEP = 4
HEAD_BLOCK = 256
BLOCK_HEADS = HEAD_BLOCK // HEAD_DIM
Q_BLOCK = 256
K_BLOCK = 512
FORWARD_K_BLOCK = 256
HIDDEN_BLOCK = 256
MEMORY_BLOCK = 768
FINISH_BLOCK = 384
ROW_BLOCK = 128
VMEM_BYTES = 56 * 1024 * 1024
GELU_ROOT = 0.7978845608028654
GELU_CUBE = 0.044715


def dot_nn(a, b):
    return lax.dot_general(a, b, (((1,), (0,)), ((), ())), preferred_element_type=F32)


def dot_nt(a, b):
    return lax.dot_general(a, b, (((1,), (1,)), ((), ())), preferred_element_type=F32)


def dot_tn(a, b):
    return lax.dot_general(a, b, (((0,), (0,)), ((), ())), preferred_element_type=F32)


def flip(a):
    return a.astype(F32).T.astype(BF16)


def spans(size, step):
    return [slice(i, i + step) for i in range(0, size, step)]


def norm_scale(rows):
    return lax.rsqrt(jnp.mean(rows * rows, axis=-1, keepdims=True) + NORM_EPS)


def norm_into(normed_ref, rows_ref, gain_ref):
    for span in spans(rows_ref.shape[0], ROW_BLOCK):
        rows = rows_ref[span].astype(F32)
        normed_ref[span] = (rows * norm_scale(rows) * gain_ref[...]).astype(BF16)


def norm_back_into(span, grad, out_ref, low_ref, gain_grad_ref, rows_ref, gain_ref, add_ref):
    rows = rows_ref[span].astype(F32)
    scale = norm_scale(rows)
    unit = rows * scale
    grad_unit = grad * gain_ref[...]
    mean = jnp.mean(grad_unit * unit, axis=-1, keepdims=True)
    out = add_ref[span].astype(F32) + scale * (grad_unit - unit * mean)
    out_ref[span] = out
    if low_ref is not None:
        low_ref[span] = out.astype(BF16)
    gain_grad_ref[...] += jnp.sum((grad * unit).reshape(-1, 8, rows.shape[1]), axis=0)


def gelu_and_slope(v):
    square = v * v
    bend = jnp.tanh(GELU_ROOT * (v + GELU_CUBE * v * square))
    half = 0.5 * (1.0 + bend)
    slope = half + 0.5 * v * (1.0 - bend * bend) * GELU_ROOT * (1.0 + 3.0 * GELU_CUBE * square)
    return v * half, slope


def lane_block(start):
    return pl.ds(pl.multiple_of(start, LANES), LANES)


def extra_lanes(rows, allowed):
    lane = lax.broadcasted_iota(jnp.int32, (rows, LANES), 1) % HEAD_DIM
    first = MASKED if allowed is None else jnp.where(allowed, 0.0, MASKED)
    return jnp.where(lane == 0, first, jnp.where(lane < 4, 1.0, 0.0)).astype(BF16)


def pick(which, block, other):
    lane = lax.broadcasted_iota(jnp.int32, block.shape, 1)
    return jnp.where((lane < HEAD_DIM) == (which == 0), block, other)


def half_rows(which):
    return slice(which * HEAD_DIM, (which + 1) * HEAD_DIM)


def split(values):
    high = values.astype(BF16).astype(F32)
    rest = values - high
    middle = rest.astype(BF16).astype(F32)
    return high, middle, rest - middle


def with_extra(which, block_t, masked, minus):
    columns = block_t.shape[1]
    row = lax.broadcasted_iota(jnp.int32, (HEAD_DIM, columns), 0)
    extra = jnp.where(row == 0, 1.0 if masked else 0.0, 0.0)
    if minus is not None:
        for i, part in enumerate(split(minus)):
            extra = jnp.where(row == i + 1, -part, extra)
    own = block_t[half_rows(which)]
    return jnp.concatenate([own, extra] if which == 0 else [extra, own], axis=0).astype(BF16)


def bias_block(table_ref, ids_ref, index, rows, start):
    row = jnp.broadcast_to(table_ref[pl.ds(index, 1), :], (rows, LANES))
    return jnp.concatenate(
        [
            jnp.take_along_axis(row, ids_ref[:rows, c : c + LANES], axis=1)
            for c in range(start, start + Q_BLOCK, LANES)
        ],
        axis=1,
    )


def ring_place(me, size):
    return jnp.where(me % 2 == 0, me // 2, size - 1 - me // 2)


def ring_device(place, size):
    return jnp.where(place < size // 2, 2 * place, 2 * (size - 1 - place) + 1)


def ring_ways(size):
    me = lax.axis_index("dp")
    place = ring_place(me, size)
    return (
        (place, ring_device((place + 1) % size, size)),
        (size - 1 - place, ring_device((place + size - 1) % size, size)),
    )


def differing(row, bit):
    return row + bit - 2 * bit * ((row // bit) % 2)


def remote(source, target, send_sem, recv_sem, device):
    return pltpu.make_async_remote_copy(
        src_ref=source,
        dst_ref=target,
        send_sem=send_sem,
        recv_sem=recv_sem,
        device_id=device,
        device_id_type=pl.DeviceIdType.MESH,
    )


def greet(bits, devices=()):
    me, row = lax.axis_index("dp"), lax.axis_index("mp")
    barrier = pltpu.get_barrier_semaphore()
    others = [(me, differing(row, bit)) for bit in bits] + [(device, row) for device in devices]
    for other in others:
        pl.semaphore_signal(
            barrier, inc=1, device_id=other, device_id_type=pl.DeviceIdType.MESH
        )
    pl.semaphore_wait(barrier, len(others))


def to_differing(bit, source, target, sems):
    me, row = lax.axis_index("dp"), lax.axis_index("mp")
    return remote(source, target, sems.at[0], sems.at[1], (me, differing(row, bit)))


class Scatter:
    def __init__(self, size, part, slots, done, send, came):
        self.size, self.part, self.slots, self.done = size, part, slots, done
        self.send, self.came = send, came
        self.ways, self.row = ring_ways(size), lax.axis_index("mp")

    def span(self, way, number):
        rows = self.slots.shape[3]
        return pl.ds(pl.multiple_of((way * self.size + number) * rows, 16), rows)

    def copy(self, way, step, source):
        return remote(
            source,
            self.slots.at[way, step],
            self.send.at[way, step],
            self.came.at[way, step],
            (self.ways[way][1], self.row),
        )

    def first(self, way):
        return self.copy(way, 0, self.part.at[:, self.span(way, self.ways[way][0])])

    def next(self, way, step):
        return self.copy(way, step, self.slots.at[way, step - 1])

    def begin(self):
        for way in range(2):
            self.first(way).start()

    def total(self, way, step):
        self.copy(way, step, self.slots.at[way, step]).wait_recv()
        span = self.span(way, (self.ways[way][0] - step - 1 + self.size) % self.size)
        return low_sum(self.slots[way, step], self.part[:, span])

    def advance(self, step):
        for way in range(2):
            self.slots[way, step - 1] = self.total(way, step - 1)
            self.next(way, step).start()

    def turn(self):
        for way in range(2):
            self.done[way] = self.total(way, self.size - 2)

    def wait_sent(self):
        for way in range(2):
            self.first(way).wait_send()

        def sent(step, carry):
            for way in range(2):
                self.next(way, step).wait_send()
            return carry

        lax.fori_loop(1, self.size - 1, sent, 0)


def low_sum(a, b):
    return (a.astype(F32) + b.astype(F32)).astype(BF16)


class Stack:
    def __init__(self, sources, stack_ref, sems, kinds, rows):
        features = stack_ref.shape[0] // kinds
        self.copies = [
            [
                pltpu.make_async_copy(
                    source.at[pl.ds(kind * rows, rows)],
                    stack_ref.at[pl.ds(kind * features + p * rows, rows)],
                    sems.at[p, kind],
                )
                for p, source in enumerate(sources)
            ]
            for kind in range(kinds)
        ]

    def start(self, *kinds):
        for kind in kinds:
            for copy in self.copies[kind]:
                copy.start()

    def wait(self, *kinds):
        for kind in kinds:
            for copy in self.copies[kind]:
                copy.wait()

    def wait_at(self, condition, *kinds):
        @pl.when(condition)
        def _():
            self.wait(*kinds)


def table_copies(sources, tables_ref, sems, kinds):
    start = sources[0].shape[0] - TABLE_ROWS
    return [
        pltpu.make_async_copy(
            source.at[pl.ds(start, TABLE_ROWS)], tables_ref.at[p], sems.at[p, kinds]
        )
        for p, source in enumerate(sources)
    ]


def table_into(table_ref, tables_ref, heads, buckets):
    for p in range(tables_ref.shape[0]):
        rows = tables_ref[p, :, :LANES].astype(F32)
        lane = lax.broadcasted_iota(jnp.int32, rows.shape, 1)
        rows = jnp.where(lane < buckets, rows, MASKED)
        for h in range(heads):
            table_ref[p * heads + h : p * heads + h + 1, :] = rows[h : h + 1, :]


def self_forward_kernel(heads, buckets, shares, rows_ref, gain_ref, ids_ref, *refs):
    sources = refs[:shares]
    q_ref, k_ref, v_ref, mixed_ref, lse_ref, bias_ref, out_ref = refs[shares : shares + 7]
    w_ref, tables_ref, table_ref, normed_ref, sems = refs[shares + 7 :]
    step = pl.program_id(0)
    doc, features = rows_ref.shape
    stack = Stack(sources, w_ref, sems, 4, heads * HEAD_DIM)

    @pl.when(step == 0)
    def _():
        stack.start(0)
        tables = table_copies(sources, tables_ref, sems, 4)
        for copy in tables:
            copy.start()
        stack.start(1, 2, 3)
        norm_into(normed_ref, rows_ref, gain_ref)
        out_ref[...] = rows_ref[...].astype(F32)
        for copy in tables:
            copy.wait()
        table_into(table_ref, tables_ref, heads, buckets)

    def weights(kind):
        start = pl.multiple_of(kind * features + step * HEAD_BLOCK, HEAD_BLOCK)
        return w_ref[pl.ds(start, HEAD_BLOCK)]

    for kind, ref in enumerate((q_ref, k_ref, v_ref)):
        stack.wait_at(step == 0, kind)
        ref[...] = dot_nt(normed_ref[...], weights(kind)).astype(BF16)
    none = jnp.zeros((doc, LANES), BF16)
    for pair in range(BLOCK_HEADS // 2):
        lanes = slice(pair * LANES, (pair + 1) * LANES)
        k, v_t = k_ref[:, lanes], flip(v_ref[:, lanes])
        q_t = flip(q_ref[:, lanes].astype(F32) * SCALE)
        k_of = [pick(which, k, none) for which in range(2)]
        for span in spans(doc, Q_BLOCK):
            rows, mixed = span.stop, []
            for which in range(2):
                h = 2 * pair + which
                bias = bias_block(table_ref, ids_ref, step * BLOCK_HEADS + h, rows, span.start)
                bias_ref[h, :rows, span] = bias.astype(BF16)
                s = dot_nn(k_of[which][:rows], q_t[:, span]) + bias
                top = jnp.max(s, axis=0, keepdims=True)
                p = jnp.exp(s - top)
                total = jnp.sum(p, axis=0, keepdims=True)
                mixed.append(dot_nn(v_t[half_rows(which), :rows], p.astype(BF16)) / total)
                lse_ref[0, h : h + 1, span] = top + jnp.log(total)
            mixed_ref[span, lanes] = jnp.concatenate(mixed, axis=0).T.astype(BF16)
    stack.wait_at(step == 0, 3)
    out_ref[...] += dot_nn(mixed_ref[...], weights(3))


def self_backward_kernel(heads, shares, *refs):
    count = shares // 2
    rows_ref, gain_ref, branch_ref, add_ref = refs[:4]
    q_ref, k_ref, v_ref, mixed_ref, lse_ref, bias_ref = refs[4:10]
    sources, refs = refs[10 : 10 + shares], refs[10 + shares :]
    hop_in, hop_out, refs = refs[: count - 1], refs[count - 1 : 2 * count - 2], refs[2 * count - 2 :]
    sums, refs = refs[:count], refs[count:]
    ds_ref, out_ref, gain_grad_ref = refs[:3]
    w_ref, normed_ref, g_ref, grad_ref, back_ref, give_ref, keep_ref, came_ref = refs[3:11]
    sems, swap_sems, hop_sems = refs[11:]
    step = pl.program_id(0)
    doc, features = rows_ref.shape
    half = features // 2
    stack = Stack(sources, w_ref, sems, 4, heads * HEAD_DIM)
    swap = to_differing(1, give_ref, came_ref, swap_sems)
    hops = [
        to_differing(2, source, target, hop_sems) for source, target in zip(hop_in, hop_out)
    ]

    @pl.when(step == 0)
    def _():
        stack.start(3, 0, 1, 2)
        greet([1, 2][:count])
        for hop in hops:
            hop.start()
        norm_into(normed_ref, rows_ref, gain_ref)
        stack.wait(3)

    start = pl.multiple_of(3 * features + step * HEAD_BLOCK, HEAD_BLOCK)
    g_ref[...] = dot_nt(branch_ref[...], w_ref[pl.ds(start, HEAD_BLOCK)]).astype(BF16)
    none = jnp.zeros((doc, LANES), BF16)
    ones = extra_lanes(doc, None)
    for pair in range(BLOCK_HEADS // 2):
        lanes = lane_block(step * HEAD_BLOCK + pair * LANES)
        q, k, v = q_ref[:, lanes], k_ref[:, lanes], v_ref[:, lanes]
        g = g_ref[:, pair * LANES : (pair + 1) * LANES]
        q_t, k_t = q.astype(F32).T * SCALE, flip(k)
        g_t = g.astype(F32).T
        inner = g_t * mixed_ref[:, lanes].astype(F32).T
        per_head = []
        for which in range(2):
            h = 2 * pair + which
            minus = jnp.sum(inner[half_rows(which)], axis=0, keepdims=True)
            per_head.append(
                (
                    pick(which, k, ones),
                    pick(which, v, ones),
                    with_extra(which, q_t, False, lse_ref[0, h : h + 1, :]),
                    with_extra(which, g_t, False, minus),
                    pick(which, q, none),
                    pick(which, g, none),
                )
            )
        grad_k = grad_v = None
        for span in spans(doc, Q_BLOCK):
            rows, grad_q, part_k, part_v = span.stop, [], None, None
            for which, (k_of, v_of, q_with, g_with, q_of, g_of) in enumerate(per_head):
                h = 2 * pair + which
                s = dot_nn(k_of[:rows], q_with[:, span])
                p = jnp.exp(s + bias_ref[h, :rows, span].astype(F32))
                ds = (p * dot_nn(v_of[:rows], g_with[:, span])).astype(BF16)
                ds_ref[h, :rows, span] = ds
                grad_q.append(dot_nn(k_t[half_rows(which), :rows], ds))
                to_v = dot_nn(p.astype(BF16), g_of[span])
                to_k = dot_nn(ds, q_of[span])
                part_v = to_v if part_v is None else part_v + to_v
                part_k = to_k if part_k is None else part_k + to_k
            grad_q = (jnp.concatenate(grad_q, axis=0) * SCALE).T
            grad_ref[span, lanes] = grad_q.astype(BF16)
            if grad_v is not None:
                part_v = jnp.concatenate(
                    [part_v[: span.start] + grad_v, part_v[span.start :]], axis=0
                )
                part_k = jnp.concatenate(
                    [part_k[: span.start] + grad_k, part_k[span.start :]], axis=0
                )
            grad_v, grad_k = part_v, part_k
        k_lanes = lane_block(features + step * HEAD_BLOCK + pair * LANES)
        v_lanes = lane_block(2 * features + step * HEAD_BLOCK + pair * LANES)
        grad_ref[:, k_lanes] = (grad_k * SCALE).astype(BF16)
        grad_ref[:, v_lanes] = grad_v.astype(BF16)

    @pl.when(step == pl.num_programs(0) - 1)
    def _():
        stack.wait(0, 1, 2)
        def weight_grads(ref, columns):
            for kind in range(3):
                kind_columns = slice(kind * features + columns.start, kind * features + columns.stop)
                ref[kind] = dot_tn(grad_ref[:, kind_columns], normed_ref[...]).astype(BF16)
            ref[3] = dot_tn(mixed_ref[:, columns], branch_ref[...]).astype(BF16)

        weight_grads(give_ref, slice(0, half))
        swap.start()
        weight_grads(keep_ref, slice(half, features))
        gain_grad_ref[...] = jnp.zeros_like(gain_grad_ref)
        back_ref[...] = dot_nn(grad_ref[...], w_ref[: 3 * features])
        for span in spans(doc, ROW_BLOCK):
            norm_back_into(
                span, back_ref[span], out_ref, None, gain_grad_ref, rows_ref, gain_ref, add_ref
            )
        swap.wait_recv()
        rows = half // count
        for share, sums_ref in enumerate(sums):
            for kind in range(4):
                span = slice(share * rows, (share + 1) * rows)
                to = slice(kind * rows, (kind + 1) * rows)
                sums_ref[to] = low_sum(keep_ref[kind, span], came_ref[kind, span])
        swap.wait_send()
        for hop in hops:
            hop.wait()


def cross_forward_kernel(heads, shares, length_ref, rows_ref, gain_ref, memory_ref, *refs):
    sources = refs[:shares]
    q_ref, k_ref, v_ref, mixed_ref, lse_ref, out_ref = refs[shares : shares + 6]
    w_ref, normed_ref, extra_ref, p_ref, mix_ref, sems = refs[shares + 6 :]
    step = pl.program_id(0)
    (doc, features), slots = rows_ref.shape, memory_ref.shape[0]
    stack = Stack(sources, w_ref, sems, 4, heads * HEAD_DIM)

    @pl.when(step == 0)
    def _():
        stack.start(0, 1, 2, 3)
        norm_into(normed_ref, rows_ref, gain_ref)
        out_ref[...] = rows_ref[...]
        slot = lax.broadcasted_iota(jnp.int32, (slots, LANES), 0)
        extra_ref[...] = extra_lanes(slots, slot < length_ref[0])
        stack.wait(0, 1, 2, 3)

    def weights(kind):
        start = pl.multiple_of(kind * features + step * HEAD_BLOCK, HEAD_BLOCK)
        return w_ref[pl.ds(start, HEAD_BLOCK)]

    q_ref[...] = dot_nt(normed_ref[...], weights(0)).astype(BF16)
    k_ref[...] = dot_nt(memory_ref[...], weights(1)).astype(BF16)
    v_ref[...] = dot_nt(memory_ref[...], weights(2)).astype(BF16)

    units = [
        (pair, which, span)
        for pair in range(BLOCK_HEADS // 2)
        for span in spans(doc, Q_BLOCK)
        for which in range(2)
    ]
    ones = jnp.ones((TILE_ROWS, slots), BF16)
    keys = spans(slots, FORWARD_K_BLOCK)

    def lanes_of(pair):
        return slice(pair * LANES, (pair + 1) * LANES)

    def key_side(pair, which):
        return pick(which, k_ref[:, lanes_of(pair)], extra_ref[...])

    def write(pair, which, span, top, total, mixed):
        h = 2 * pair + which
        lse_ref[0, h : h + 1, span] = top + jnp.log(total)
        mix_ref[half_rows(which)] = mixed / total
        if which == 1:
            mixed_ref[span, lanes_of(pair)] = mix_ref[...].T.astype(BF16)

    v_t = [flip(v_ref[:, lanes_of(p)]) for p in range(BLOCK_HEADS // 2)]
    q_t = [q_ref[:, lanes_of(p)].astype(F32).T * SCALE for p in range(BLOCK_HEADS // 2)]

    def begin(unit):
        pair, which, span = unit
        k_of = key_side(pair, which)
        s = dot_nn(k_of[keys[0]], with_extra(which, q_t[pair][:, span], True, None))
        top = jnp.max(s, axis=0, keepdims=True)
        return k_of, s, top, with_extra(which, q_t[pair][:, span], True, top)

    worst = jnp.zeros((1, Q_BLOCK), F32)
    ahead = begin(units[0])
    for i, (pair, which, span) in enumerate(units):
        (k_of, s, top, q_with), slot = ahead, i % 2
        p_ref[slot, keys[0]] = jnp.exp(s - top).astype(BF16)
        for rows in keys[1:]:
            p_ref[slot, rows] = jnp.exp(dot_nn(k_of[rows], q_with)).astype(BF16)
        if i + 1 < len(units):
            ahead = begin(units[i + 1])
        value_side = jnp.concatenate([v_t[pair][half_rows(which)], ones], axis=0)
        mixed = dot_nn(value_side, p_ref[slot])
        total = mixed[HEAD_DIM : HEAD_DIM + 1]
        worst = jnp.maximum(worst, total)
        write(pair, which, span, top, total, mixed[:HEAD_DIM])

    @pl.when(jnp.max(worst) > LARGEST_SUM)
    def _():
        for pair, which, span in units:
            q_with = with_extra(
                which, q_ref[:, lanes_of(pair)].astype(F32).T[:, span] * SCALE, True, None
            )
            k_of = key_side(pair, which)
            s = [dot_nn(k_of[rows], q_with) for rows in keys]
            top = functools.reduce(jnp.maximum, [jnp.max(c, axis=0, keepdims=True) for c in s])
            total = jnp.zeros_like(top)
            for rows, chunk in zip(keys, s):
                p = jnp.exp(chunk - top)
                total = total + jnp.sum(p, axis=0, keepdims=True)
                p_ref[0, rows] = p.astype(BF16)
            mixed = dot_nn(flip(v_ref[:, lanes_of(pair)])[half_rows(which)], p_ref[0])
            write(pair, which, span, top, total, mixed)

    out_ref[...] += dot_nn(mixed_ref[...], weights(3))


def cross_backward_kernel(heads, shares, size, scattered, hops_wanted, length_ref, *refs):
    gain_ref, branch_ref, q_ref, mixed_ref, lse_ref = refs[:5]
    rows_in, memory_in, add_in, k_in, v_in = refs[5:10]
    sources = refs[10 : 10 + shares]
    count = shares // 2
    refs = refs[10 + shares :]
    scatter_in, refs = refs[:scattered], refs[scattered:]
    hidden_in, refs = refs[:hops_wanted], refs[hops_wanted:]
    hidden_out, refs = refs[:hops_wanted], refs[hops_wanted:]
    if scattered:
        scatter_out, refs = refs[0], refs[1:]
        (part_ref, ring_slots, done_ref, scatter_came), refs = refs[-8:-4], refs[:-8] + refs[-4:]
        (ring_send, ring_came, part_sems, done_sems), refs = refs[-4:], refs[:-4]
        scatter = Scatter(size, part_ref, ring_slots, done_ref, ring_send, ring_came)
        part_loads = [
            pltpu.make_async_copy(source, part_ref.at[i], part_sems.at[i])
            for i, source in enumerate(scatter_in)
        ]
    sums, refs = refs[:count], refs[count:]
    memory_out, out_ref, low_ref, gain_grad_ref = refs[:4]
    rows_ref, memory_ref, add_ref, k_ref, v_ref = refs[4:9]
    (
        w_ref,
        normed_ref,
        extra_ref,
        g_ref,
        grad_q_ref,
        grad_ref,
        ds_ref,
        give_ref,
        keep_ref,
        came_ref,
        memory_grad_ref,
        back_ref,
        sems,
        load_sems,
        key_sems,
        out_sems,
        swap_sems,
        hop_sems,
    ) = refs[9:]
    (doc, features), slots = rows_ref.shape, memory_ref.shape[0]
    half, blocks = features // 2, features // HEAD_BLOCK
    stack = Stack(sources, w_ref, sems, 4, heads * HEAD_DIM)
    loads = [
        pltpu.make_async_copy(source, target, load_sems.at[i])
        for i, (source, target) in enumerate(
            ((memory_in, memory_ref), (rows_in, rows_ref), (add_in, add_ref))
        )
    ]

    def key_copies(b):
        lanes = pl.ds(pl.multiple_of(b * HEAD_BLOCK, HEAD_BLOCK), HEAD_BLOCK)
        return [
            pltpu.make_async_copy(source.at[:, lanes], target.at[b], key_sems.at[i, b])
            for i, (source, target) in enumerate(((k_in, k_ref), (v_in, v_ref)))
        ]

    stack.start(3)
    for copy in key_copies(0):
        copy.start()
    if scattered:
        for copy in part_loads:
            copy.start()
    for b in range(1, blocks):
        for copy in key_copies(b):
            copy.start()
    for copy in loads:
        copy.start()
    stack.start(0, 1, 2)
    greet([1, 2][:count], [way[1] for way in ring_ways(size)] if scattered else [])
    hops = [
        to_differing(2, source, target, hop_sems.at[i])
        for i, (source, target) in enumerate(zip(hidden_in, hidden_out))
    ]
    for hop in hops:
        hop.start()
    if scattered:
        for copy in part_loads:
            copy.wait()
        scatter.begin()
    slot = lax.broadcasted_iota(jnp.int32, (slots, LANES), 0)
    extra_ref[...] = extra_lanes(slots, slot < length_ref[0])
    none = jnp.zeros((doc, LANES), BF16)
    stack.wait(3)

    def one_block(step, carry):
        start = pl.multiple_of(3 * features + step * HEAD_BLOCK, HEAD_BLOCK)
        g_ref[...] = dot_nt(branch_ref[...], w_ref[pl.ds(start, HEAD_BLOCK)]).astype(BF16)
        for copy in key_copies(step):
            copy.wait()
        for pair in range(BLOCK_HEADS // 2):
            local = slice(pair * LANES, (pair + 1) * LANES)
            lanes = lane_block(step * HEAD_BLOCK + pair * LANES)
            v_lanes = lane_block(features + step * HEAD_BLOCK + pair * LANES)
            q, g = q_ref[:, lanes], g_ref[:, local]
            q_t, g_t = q.astype(F32).T * SCALE, g.astype(F32).T
            inner = g_t * mixed_ref[:, lanes].astype(F32).T
            per_head = []
            for which in range(2):
                h = 2 * pair + which
                minus = jnp.sum(inner[half_rows(which)], axis=0, keepdims=True)
                per_head.append(
                    (
                        with_extra(which, q_t, True, lse_ref[step, h : h + 1, :]),
                        with_extra(which, g_t, False, minus),
                        pick(which, q, none),
                        pick(which, g, none),
                    )
                )
            for rows in spans(slots, K_BLOCK):
                k, v, extra = k_ref[step, rows, local], v_ref[step, rows, local], extra_ref[rows]
                part_k = part_v = None
                for which, (q_with, g_with, q_of, g_of) in enumerate(per_head):
                    p = jnp.exp(dot_nn(pick(which, k, extra), q_with))
                    ds = (p * dot_nn(pick(which, v, extra), g_with)).astype(BF16)
                    ds_ref[which, rows] = ds
                    to_v = dot_nn(p.astype(BF16), g_of)
                    to_k = dot_nn(ds, q_of)
                    part_v = to_v if part_v is None else part_v + to_v
                    part_k = to_k if part_k is None else part_k + to_k
                grad_ref[rows, lanes] = (part_k * SCALE).astype(BF16)
                grad_ref[rows, v_lanes] = part_v.astype(BF16)
            k_t = flip(k_ref[step, :, local])
            grad_q = [dot_nn(k_t[half_rows(which)], ds_ref[which]) for which in range(2)]
            grad_q_ref[:, lanes] = (jnp.concatenate(grad_q, axis=0) * SCALE).T.astype(BF16)
            if scattered:
                scatter_step(1 + step * (BLOCK_HEADS // 2) + pair)
        return carry

    places = blocks * (BLOCK_HEADS // 2)

    def scatter_step(step):
        if size - 2 >= places:
            scatter.advance(step)
        elif size > 2:

            @pl.when(step <= size - 2)
            def _():
                scatter.advance(step)

    lax.fori_loop(0, blocks, one_block, 0)
    if scattered:

        def rest(step, carry):
            scatter.advance(step)
            return carry

        lax.fori_loop(min(places, size - 2) + 1, size - 1, rest, 0)
        scatter.turn()
        done_hops = [
            to_differing(2, done_ref.at[:, i], scatter_came, done_sems)
            for i in range(1, scattered)
        ]
        for hop in done_hops:
            hop.start()

    for copy in loads:
        copy.wait()
    norm_into(normed_ref, rows_ref, gain_ref)

    def weight_grads(ref, first):
        columns = slice(first, first + half)
        v_columns = slice(features + first, features + first + half)
        ref[0] = dot_tn(grad_q_ref[:, columns], normed_ref[...]).astype(BF16)
        ref[1] = dot_tn(grad_ref[:, columns], memory_ref[...]).astype(BF16)
        ref[2] = dot_tn(grad_ref[:, v_columns], memory_ref[...]).astype(BF16)
        ref[3] = dot_tn(mixed_ref[:, columns], branch_ref[...]).astype(BF16)

    weight_grads(give_ref, 0)
    swap = to_differing(1, give_ref, came_ref, swap_sems)
    swap.start()
    stack.wait(0, 1, 2)
    writes = []
    for i, rows in enumerate(spans(slots, MEMORY_BLOCK)):
        memory_grad_ref[rows] = dot_nn(
            grad_ref[rows], w_ref[features : 3 * features]
        ).astype(BF16)
        writes.append(
            pltpu.make_async_copy(memory_grad_ref.at[rows], memory_out.at[rows], out_sems.at[i])
        )
        writes[-1].start()
    weight_grads(keep_ref, half)
    gain_grad_ref[...] = jnp.zeros_like(gain_grad_ref)
    back_ref[...] = dot_nn(grad_q_ref[...], w_ref[:features])
    for span in spans(doc, ROW_BLOCK):
        norm_back_into(
            span, back_ref[span], out_ref, low_ref, gain_grad_ref, rows_ref, gain_ref, add_ref
        )
    swap.wait_recv()
    rows = half // count
    for share, sums_ref in enumerate(sums):
        for kind in range(4):
            span = slice(share * rows, (share + 1) * rows)
            to = slice(kind * rows, (kind + 1) * rows)
            sums_ref[to] = low_sum(keep_ref[kind, span], came_ref[kind, span])
    swap.wait_send()
    for copy in writes:
        copy.wait()
    for hop in hops:
        hop.wait()
    if scattered:
        for hop in done_hops:
            hop.wait()
        own = done_ref[:, 0]
        scatter_out[...] = low_sum(own, scatter_came[...]) if done_hops else own
        scatter.wait_sent()


def feed_forward_kernel(first, last, rows_ref, gain_ref, cotangent_ref, *refs):
    sources, refs = refs[:2], refs[2:]
    if not first:
        before_in, refs = refs[:2], refs[2:]
    outs, refs = refs[:4], refs[4:]
    low_ref = None
    if last:
        outs, gain_grad_ref, refs = (*outs, refs[0]), refs[1], refs[2:]
    (
        wide_ref,
        narrow_ref,
        normed_ref,
        normed_t,
        cotangent_t,
        active_ref,
        grad_ref,
        give_ref,
        keep_ref,
        came_ref,
        layer_in_ref,
        back_in_ref,
        product_ref,
        sems,
        before_sems,
        swap_sems,
        out_sems,
        *results,
    ) = refs
    sums, (layer_ref, out_ref) = results[:2], results[2:4]
    if last:
        low_ref = results[4]
    writes = [
        pltpu.make_async_copy(source, target, out_sems.at[i])
        for i, (source, target) in enumerate(zip(results, outs))
    ]
    step, steps = pl.program_id(0), pl.num_programs(0)
    half = steps // 2
    doc = rows_ref.shape[0]
    hidden = sources[0].shape[0] // 2
    copies = [
        [
            pltpu.make_async_copy(
                source.at[pl.ds(kind * hidden, hidden)],
                stack.at[pl.ds(p * hidden, hidden)],
                sems.at[p, kind],
            )
            for kind, stack in enumerate((wide_ref, narrow_ref))
        ]
        for p, source in enumerate(sources)
    ]
    loads = []
    if not first:
        loads = [
            pltpu.make_async_copy(source, target, before_sems.at[i])
            for i, (source, target) in enumerate(zip(before_in, (layer_in_ref, back_in_ref)))
        ]
    swap = to_differing(1, give_ref, came_ref, swap_sems)

    @pl.when(step == 0)
    def _():
        for pair in copies:
            for copy in pair:
                copy.start()
        for copy in loads:
            copy.start()
        greet([1])
        norm_into(normed_ref, rows_ref, gain_ref)
        for span in spans(doc, ROW_BLOCK):
            normed_t[:, span] = flip(normed_ref[span])
            cotangent_t[:, span] = flip(cotangent_ref[span])

    for p, pair in enumerate(copies):

        @pl.when(step == p * half)
        def _(pair=pair):
            for copy in pair:
                copy.wait()

    units = pl.ds(pl.multiple_of(step * HIDDEN_BLOCK, HIDDEN_BLOCK), HIDDEN_BLOCK)
    activated, slope = gelu_and_slope(dot_nn(wide_ref[units], normed_t[...]))
    active_ref[units] = activated.astype(BF16)
    grad_ref[units] = (dot_nn(narrow_ref[units], cotangent_t[...]) * slope).astype(BF16)

    def store(ref, at):
        rows = pl.ds(pl.multiple_of(at * HIDDEN_BLOCK, HIDDEN_BLOCK), HIDDEN_BLOCK)
        ref[0, rows] = dot_nn(grad_ref[units], normed_ref[...]).astype(BF16)
        ref[1, rows] = dot_nn(active_ref[units], cotangent_ref[...]).astype(BF16)

    @pl.when(step < half)
    def _():
        store(give_ref, step)

    @pl.when(step == half - 1)
    def _():
        swap.start()

    @pl.when(step >= half)
    def _():
        store(keep_ref, step - half)

    @pl.when(step == steps - 1)
    def _():
        for copy in loads:
            copy.wait()
        if last:
            gain_grad_ref[...] = jnp.zeros_like(gain_grad_ref)
        product_ref[...] = dot_tn(active_ref[...], narrow_ref[...])
        for span in spans(doc, ROW_BLOCK):
            layer = rows_ref[span] if first else layer_in_ref[span]
            layer_ref[span] = (layer + product_ref[span]).astype(layer_ref.dtype)
        writes[2].start()
        product_ref[...] = dot_tn(grad_ref[...], wide_ref[...])
        for span in spans(doc, ROW_BLOCK):
            back = product_ref[span]
            if not first:
                back = back + back_in_ref[span]
            if last:
                norm_back_into(
                    span, back, out_ref, low_ref, gain_grad_ref, rows_ref, gain_ref, cotangent_ref
                )
            else:
                out_ref[span] = back
        for copy in writes[3:]:
            copy.start()
        swap.wait_recv()
        for kind, sums_ref in enumerate(sums):
            for span in spans(hidden, HIDDEN_BLOCK):
                sums_ref[span] = low_sum(keep_ref[kind, span], came_ref[kind, span])
            writes[kind].start()
        swap.wait_send()
        for copy in writes:
            copy.wait()


def pack_kernel(flipped, *refs):
    out_ref, start = refs[-1], 0
    for source, turn in zip(refs[:-1], flipped):
        if source.shape[-1] != out_ref.shape[1] and not turn:
            out_ref[start:] = jnp.zeros((TABLE_ROWS, out_ref.shape[1]), BF16)
            out_ref[start : start + source.shape[0], : source.shape[1]] = source[...]
            continue
        rows = source.shape[1] if turn else source.shape[0]
        span = slice(start, start + rows)
        out_ref[span] = flip(source[...]) if turn else source[...]
        start += rows


def finish_kernel(*refs):
    sources, outs, refs = refs[:4], refs[4:14], refs[14:]
    ins, wides, in_sems, out_sems = refs[:4], refs[4:14], refs[14], refs[15]
    loads, writes = [], []
    for i, (source, target) in enumerate(zip(sources, ins)):
        for j, span in enumerate(spans(target.shape[0], FINISH_BLOCK)):
            loads.append(
                pltpu.make_async_copy(source.at[span], target.at[span], in_sems.at[i, j])
            )
            loads[-1].start()

    def write(i, part):
        writes.append(
            pltpu.make_async_copy(wides[i].at[part], outs[i].at[part], out_sems.at[len(writes)])
        )
        writes[-1].start()

    waiting = iter(loads)
    hidden = wides[1].shape[0]
    for span in spans(hidden, FINISH_BLOCK):
        next(waiting).wait()
        for part in spans(FINISH_BLOCK, LANES):
            rows = slice(span.start + part.start, span.start + part.stop)
            wides[0][:, rows] = ins[0][rows].astype(F32).T
        write(0, (slice(None), span))
    for span in spans(hidden, FINISH_BLOCK):
        next(waiting).wait()
        wides[1][span] = ins[1][span].astype(F32)
        write(1, span)
    for i in (2, 3):
        for _ in spans(ins[i].shape[0], FINISH_BLOCK):
            next(waiting).wait()
        rows = wides[2].shape[0]
        for kind in range(4):
            at = 2 + 4 * (i - 2) + kind
            wides[at][...] = ins[i][kind * rows : (kind + 1) * rows].astype(F32)
            write(at, slice(None))
    for copy in writes:
        copy.wait()


def params():
    return pltpu.CompilerParams(vmem_limit_bytes=VMEM_BYTES)


def cost(flops=1 << 20):
    return pl.CostEstimate(flops=flops, bytes_accessed=1 << 16, transcendentals=0)


def shape(dims, dtype):
    return jax.ShapeDtypeStruct(dims, dtype)


def whole(array):
    return pl.BlockSpec(
        array.shape, lambda *_: (0,) * len(array.shape), pipeline_mode=pl.Buffered(1)
    )


def result(array):
    return pl.BlockSpec(array.shape, lambda *_: (0,) * len(array.shape))


def columns(rows):
    return pl.BlockSpec((rows, HEAD_BLOCK), lambda i: (0, i))


def anywhere(arrays):
    return [pl.BlockSpec(memory_space=pl.ANY) for _ in arrays]


SCALAR = pl.BlockSpec(memory_space=pltpu.SMEM)


def call(
    kernel, name, grid, in_specs, out_specs, out_shape, scratch, args, channel=None, flops=1 << 20
):
    compiler_params = params()
    if channel is not None:
        compiler_params = pltpu.CompilerParams(
            vmem_limit_bytes=VMEM_BYTES, collective_id=channel, has_side_effects=True
        )
    return pl.pallas_call(
        kernel,
        grid=grid,
        in_specs=in_specs,
        out_specs=out_specs,
        out_shape=out_shape,
        scratch_shapes=scratch,
        compiler_params=compiler_params,
        cost_estimate=cost(flops),
        name=name,
    )(*args)


def pack(*parts):
    arrays, flipped = zip(*parts)
    features = arrays[0].shape[0] if flipped[0] else arrays[0].shape[1]
    rows = [a.shape[1] if turn else a.shape[0] for a, turn in parts]
    if arrays[-1].shape[1] < features and not flipped[-1]:
        rows[-1] = TABLE_ROWS
    rows = sum(rows)
    return pl.pallas_call(
        functools.partial(pack_kernel, flipped),
        out_shape=shape((rows, features), BF16),
        compiler_params=params(),
        cost_estimate=cost(),
        name="pack",
    )(*arrays)


def self_forward(heads, buckets, rows, gain, weights, ids):
    doc, features = rows.shape
    shares, steps = len(weights), features // HEAD_BLOCK
    narrow, tall = shape((doc, features), BF16), shape((doc, features), F32)
    scores = shape((steps * BLOCK_HEADS, doc, doc), BF16)
    out_shape = (*[narrow] * 4, shape((steps, 8, doc), F32), scores, tall)
    return call(
        functools.partial(self_forward_kernel, heads, buckets, shares),
        "self_forward",
        (steps,),
        [whole(rows), whole(gain), whole(ids), *anywhere(weights)],
        (
            *[columns(doc)] * 4,
            pl.BlockSpec((1, 8, doc), lambda i: (i, 0, 0)),
            pl.BlockSpec((BLOCK_HEADS, doc, doc), lambda i: (i, 0, 0)),
            result(tall),
        ),
        out_shape,
        [
            pltpu.VMEM((4 * features, features), BF16),
            pltpu.VMEM((shares, TABLE_ROWS, features), BF16),
            pltpu.VMEM((TABLE_ROWS, LANES), F32),
            pltpu.VMEM((doc, features), BF16),
            pltpu.SemaphoreType.DMA((shares, 5)),
        ],
        (rows, gain, ids, *weights),
    )


def self_backward(heads, rows, gain, branch, add, saved, weights, hops):
    doc, features = rows.shape
    shares, steps = len(weights), features // HEAD_BLOCK
    count = shares // 2
    *arrays, lse, bias = saved
    packed = pltpu.VMEM((4, features // 2, features), BF16)
    scores = pl.BlockSpec((BLOCK_HEADS, doc, doc), lambda i: (i, 0, 0))
    out_shape = (
        *[shape(h.shape, BF16) for h in hops],
        *[shape((4 * heads * HEAD_DIM, features), BF16)] * count,
        shape((steps * BLOCK_HEADS, doc, doc), BF16),
        shape((doc, features), F32),
        shape((8, features), F32),
    )
    return call(
        functools.partial(self_backward_kernel, heads, shares),
        "self_backward",
        (steps,),
        [
            *[whole(a) for a in (rows, gain, branch, add, *arrays)],
            pl.BlockSpec((1, 8, doc), lambda i: (i, 0, 0)),
            scores,
            *anywhere(weights),
            *anywhere(hops),
        ],
        (
            *anywhere(hops),
            *[result(o) for o in out_shape[len(hops) : len(hops) + count]],
            scores,
            result(out_shape[-2]),
            result(out_shape[-1]),
        ),
        out_shape,
        [
            pltpu.VMEM((4 * features, features), BF16),
            pltpu.VMEM((doc, features), BF16),
            pltpu.VMEM((doc, HEAD_BLOCK), BF16),
            pltpu.VMEM((doc, 3 * features), BF16),
            pltpu.VMEM((doc, features), F32),
            packed,
            packed,
            packed,
            pltpu.SemaphoreType.DMA((shares, 4)),
            pltpu.SemaphoreType.DMA((2,)),
            pltpu.SemaphoreType.DMA((2,)),
        ],
        (rows, gain, branch, add, *arrays, lse, bias, *weights, *hops),
        channel=4,
    )


def cross_forward(heads, rows, gain, memory, length, weights):
    (doc, features), slots = rows.shape, memory.shape[0]
    shares, steps = len(weights), features // HEAD_BLOCK
    query, key = shape((doc, features), BF16), shape((slots, features), BF16)
    tall = shape((doc, features), F32)
    return call(
        functools.partial(cross_forward_kernel, heads, shares),
        "cross_forward",
        (steps,),
        [SCALAR, whole(rows), whole(gain), whole(memory), *anywhere(weights)],
        (
            columns(doc),
            columns(slots),
            columns(slots),
            columns(doc),
            pl.BlockSpec((1, 8, doc), lambda i: (i, 0, 0)),
            result(tall),
        ),
        (query, key, key, query, shape((steps, 8, doc), F32), tall),
        [
            pltpu.VMEM((4 * features, features), BF16),
            pltpu.VMEM((doc, features), BF16),
            pltpu.VMEM((slots, LANES), BF16),
            pltpu.VMEM((2, slots, Q_BLOCK), BF16),
            pltpu.VMEM((LANES, Q_BLOCK), F32),
            pltpu.SemaphoreType.DMA((shares, 4)),
        ],
        (length, rows, gain, memory, *weights),
    )


def cross_backward(
    heads, size, rows, gain, memory, length, branch, add, saved, weights, scattered, hops
):
    (doc, features), slots = rows.shape, memory.shape[0]
    shares, blocks = len(weights), features // HEAD_BLOCK
    count = shares // 2
    blocks_out, ring_scratch = [], []
    if scattered:
        number, part = len(scattered), scattered[0].shape
        block = (2, part[0] // (2 * size), features)
        blocks_out = [shape(block, BF16)]
        steps = pltpu.SemaphoreType.DMA((2, size - 1))
        ring_scratch = [
            pltpu.VMEM((number, *part), BF16),
            pltpu.VMEM((2, size - 1, number, *block[1:]), BF16),
            pltpu.VMEM((2, number, *block[1:]), BF16),
            pltpu.VMEM(block, BF16),
            steps,
            steps,
            pltpu.SemaphoreType.DMA((number,)),
            pltpu.SemaphoreType.DMA((2,)),
        ]
    out_shape = (
        *[shape(h.shape, BF16) for h in hops],
        *blocks_out,
        *[shape((4 * heads * HEAD_DIM, features), BF16)] * count,
        shape((slots, features), BF16),
        shape((doc, features), F32),
        shape((doc, features), BF16),
        shape((8, features), F32),
    )
    query, key, value, mixed, lse = saved
    near = (gain, branch, query, mixed, lse)
    far = (rows, memory, add, key, value, *weights, *scattered, *hops)
    vmem, hbm = pl.BlockSpec(memory_space=pltpu.VMEM), pl.BlockSpec(memory_space=pl.ANY)
    packed = pltpu.VMEM((4, features // 2, features), BF16)
    key_block = pltpu.VMEM((blocks, slots, HEAD_BLOCK), BF16)
    return call(
        functools.partial(
            cross_backward_kernel, heads, shares, size, len(scattered), len(hops)
        ),
        "cross_backward",
        (),
        [SCALAR, *[vmem for _ in near], *[hbm for _ in far]],
        (
            *[hbm] * len(hops),
            *[vmem] * len(blocks_out),
            *[vmem] * count,
            hbm,
            vmem,
            vmem,
            vmem,
        ),
        out_shape,
        [
            pltpu.VMEM((doc, features), F32),
            pltpu.VMEM((slots, features), BF16),
            pltpu.VMEM((doc, features), F32),
            key_block,
            key_block,
            pltpu.VMEM((4 * features, features), BF16),
            pltpu.VMEM((doc, features), BF16),
            pltpu.VMEM((slots, LANES), BF16),
            pltpu.VMEM((doc, HEAD_BLOCK), BF16),
            pltpu.VMEM((doc, features), BF16),
            pltpu.VMEM((slots, 2 * features), BF16),
            pltpu.VMEM((2, slots, doc), BF16),
            packed,
            packed,
            packed,
            pltpu.VMEM((slots, features), BF16),
            pltpu.VMEM((doc, features), F32),
            pltpu.SemaphoreType.DMA((shares, 4)),
            pltpu.SemaphoreType.DMA((3,)),
            pltpu.SemaphoreType.DMA((2, blocks)),
            pltpu.SemaphoreType.DMA((slots // MEMORY_BLOCK,)),
            pltpu.SemaphoreType.DMA((2,)),
            pltpu.SemaphoreType.DMA((max(len(hops), 1), 2)),
            *ring_scratch,
        ],
        (length, *near, *far),
        channel=1,
    )


def feed_forward(rows, gain, cotangent, weights, before, last):
    (doc, features), shares = rows.shape, len(weights)
    share = weights[0].shape[0] // 2
    hidden = share * shares
    steps = hidden // HIDDEN_BLOCK
    summed, tall = shape((share, features), BF16), shape((doc, features), F32)
    low = shape((doc, features), BF16)
    rest = [low, tall, low, shape((8, features), F32)] if last else [tall, tall]
    by_copy = [summed, summed, *rest[:3]]
    kept, added = pltpu.VMEM((2, share, features), BF16), pltpu.VMEM(tall.shape, F32)
    return call(
        functools.partial(feed_forward_kernel, not before, last),
        "feed_forward",
        (steps,),
        [whole(rows), whole(gain), whole(cotangent), *anywhere(weights), *anywhere(before)],
        (*anywhere(by_copy), *[result(o) for o in rest[3:]]),
        (summed, summed, *rest),
        [
            pltpu.VMEM((hidden, features), BF16),
            pltpu.VMEM((hidden, features), BF16),
            pltpu.VMEM((doc, features), BF16),
            pltpu.VMEM((features, doc), BF16),
            pltpu.VMEM((features, doc), BF16),
            pltpu.VMEM((hidden, doc), BF16),
            pltpu.VMEM((hidden, doc), BF16),
            kept,
            kept,
            kept,
            added,
            added,
            added,
            pltpu.SemaphoreType.DMA((shares, 2)),
            pltpu.SemaphoreType.DMA((2,)),
            pltpu.SemaphoreType.DMA((2,)),
            pltpu.SemaphoreType.DMA((len(by_copy),)),
            *[pltpu.VMEM(o.shape, o.dtype) for o in by_copy],
        ],
        (rows, gain, cotangent, *weights, *before),
        channel=3 if before else 2,
    )


def finish(sum_wide, sum_narrow, sum_cross, sum_self):
    rows, features = sum_self.shape
    hidden, part = sum_wide.shape[0], shape((rows // 4, features), F32)
    out_shape = [shape((features, hidden), F32), shape((hidden, features), F32), *[part] * 8]
    sources = (sum_wide, sum_narrow, sum_cross, sum_self)
    writes = 2 * hidden // FINISH_BLOCK + 8
    wide, narrow, *parts = pl.pallas_call(
        finish_kernel,
        in_specs=anywhere(sources),
        out_specs=anywhere(out_shape),
        out_shape=out_shape,
        scratch_shapes=[
            *[pltpu.VMEM(source.shape, BF16) for source in sources],
            *[pltpu.VMEM(out.shape, F32) for out in out_shape],
            pltpu.SemaphoreType.DMA((4, hidden // FINISH_BLOCK)),
            pltpu.SemaphoreType.DMA((writes,)),
        ],
        compiler_params=params(),
        cost_estimate=cost(),
        name="finish",
    )(*sources)
    return wide, narrow, parts[4:], parts[:4]


def share_place(row, other, peers):
    j, bit = 0, 1
    while bit < peers:
        j = j + bit * ((row // bit + other // bit) % 2)
        bit *= 2
    return (j % 2) * (j // 2) + (1 - j % 2) * (peers // 2 + j // 2)


def tail_kernel(size, peers, buckets, heads, gathered, counts, *refs):
    flat, refs = refs[: sum(counts)], refs[sum(counts) :]
    arrays, shares = len(counts) + 1, peers // 2
    last_refs, refs = refs[:shares], refs[shares:]
    ids_in, ds_ref, *gain_refs = refs[:5]
    results, small_out_ref, refs = refs[5 : 5 + arrays], refs[5 + arrays], refs[6 + arrays :]
    outs, refs = refs[:arrays], refs[arrays:]
    operands, refs = refs[: len(flat) + 2], refs[len(flat) + 2 :]
    operand_sems, out_sems, refs = refs[0], refs[1], refs[2:]
    loads = [
        pltpu.make_async_copy(source, target, operand_sems.at[i])
        for i, (source, target) in enumerate(zip((*flat, last_refs[0], ids_in), operands))
    ]
    for copy in loads:
        copy.start()
    last_ref, ids_ref = operands[len(flat) :]
    parts = []
    for count in counts:
        parts.append(operands[:count])
        operands = operands[count:]
    writes = [
        pltpu.make_async_copy(source, target, out_sems.at[i])
        for i, (source, target) in enumerate(zip(outs, results))
    ]
    slots, refs = refs[:arrays], refs[arrays:]
    firsts, refs = refs[:arrays], refs[arrays:]
    far_came_ref, part_ref, scores_ref, bucket_ref = refs[:4]
    small_ref, near_ref, far_ref = refs[4:7]
    send, came, send_out, came_out, small_sems, hop_sems, local_sems = refs[7:]
    parts.append((part_ref,))
    me, row = lax.axis_index("dp"), lax.axis_index("mp")
    ways = ring_ways(size)
    doc = ids_ref.shape[0]
    mesh = pl.DeviceIdType.MESH

    load_scores = pltpu.make_async_copy(ds_ref, scores_ref, local_sems.at[0])
    load_scores.start()

    barrier = pltpu.get_barrier_semaphore()

    def greet(t, carry):
        pl.semaphore_signal(
            barrier, inc=1, device_id=((me + t) % size, row), device_id_type=mesh
        )
        return carry

    lax.fori_loop(1, size, greet, 0)
    for t in range(1, peers):
        pl.semaphore_signal(
            barrier, inc=1, device_id=(me, (row + t) % peers), device_id_type=mesh
        )
    pl.semaphore_wait(barrier, size - 1 + peers - 1)

    def block(i, way, number):
        rows = outs[i].shape[0] // (2 * size)
        return pl.ds(pl.multiple_of((way * size + number) * rows, 16), rows)

    def part(i, span):
        total = parts[i][0][span].astype(F32)
        for ref in parts[i][1:]:
            total = total + ref[span].astype(F32)
        return total

    def first_copy(i, way):
        return remote(
            firsts[i].at[way],
            slots[i].at[way, 0],
            send.at[i, way, 0],
            came.at[i, way, 0],
            (ways[way][1], row),
        )

    def next_copy(i, way, step):
        return remote(
            slots[i].at[way, step - 1],
            slots[i].at[way, step],
            send.at[i, way, step],
            came.at[i, way, step],
            (ways[way][1], row),
        )

    def wait_came(i, way, step):
        remote(
            slots[i].at[way, step],
            slots[i].at[way, step],
            send.at[i, way, step],
            came.at[i, way, step],
            (ways[way][1], row),
        ).wait_recv()

    def out_copy(i, way, step):
        span = block(i, way, (ways[way][0] + 1 - step + size) % size)
        return remote(
            outs[i].at[span],
            outs[i].at[span],
            send_out.at[i, way, step],
            came_out.at[i, way, step],
            (ways[way][1], row),
        )

    def begin(rings):
        for i, way in rings:
            firsts[i][way] = part(i, block(i, way, ways[way][0])).astype(BF16)
            first_copy(i, way).start()

    def plus_part(i, way, step):
        span = block(i, way, (ways[way][0] - step - 1 + size) % size)
        total = slots[i][way, step].astype(F32) + part(i, span)
        return span, total.astype(BF16)

    def advance(rings, step):
        for i, way in rings:
            wait_came(i, way, step - 1)
            slots[i][way, step - 1] = plus_part(i, way, step - 1)[1]
            next_copy(i, way, step).start()

    def turn(rings):
        for i, way in rings:
            wait_came(i, way, size - 2)
            span, total = plus_part(i, way, size - 2)
            outs[i][span] = total
            out_copy(i, way, 0).start()

    def pass_on(rings, step):
        for i, way in rings:
            out_copy(i, way, step - 1).wait_recv()
            out_copy(i, way, step).start()

    ready = [(i, way) for i in range(gathered) for way in range(2)]
    early = [(i, way) for i in range(gathered, arrays - 1) for way in range(2)]
    late = [(arrays - 1, way) for way in range(2)]

    other_chip = None
    if shares == 2:
        other_chip = to_differing(2, last_refs[1], far_came_ref, hop_sems)
        other_chip.start()
    for copy in loads[: len(flat)]:
        copy.wait()
    begin(early)
    for i, way in ready:
        outs[i][block(i, way, (ways[way][0] + 1) % size)] = parts[i][0][way]
        out_copy(i, way, 0).start()

    rows_used, per_row = bucket_ref.shape[0], ds_ref.shape[0] // bucket_ref.shape[0]
    units = rows_used * buckets
    per_round = -(-units // max(2 * (size - 2), 1))

    def bucket_unit(u, carry):
        r, b = u // buckets, u % buckets
        sums = [jnp.zeros((8, LANES), F32) for _ in range(per_row)]
        for c in range(0, doc, LANES):
            hit = ids_ref[: c + LANES, c : c + LANES] == b
            for h in range(per_row):
                grads = scores_ref[r * per_row + h, : c + LANES, c : c + LANES].astype(F32)
                kept = jnp.where(hit, grads, 0.0).reshape(-1, 8, LANES)
                sums[h] = sums[h] + jnp.sum(kept, axis=0)
        for h in range(per_row):
            bucket_ref[r, h, pl.ds(b, 1), :] = jnp.sum(sums[h], axis=0, keepdims=True)
        return carry

    def bucket_round(k):
        low = jnp.minimum(k * per_round, units)
        lax.fori_loop(low, jnp.minimum(low + per_round, units), bucket_unit, 0)

    bucket_ref[...] = jnp.zeros_like(bucket_ref)
    part_ref[...] = jnp.zeros_like(part_ref)
    load_scores.wait()
    for copy in loads[len(flat) :]:
        copy.wait()

    def early_step(step, carry):
        advance(early, step)
        pass_on(ready, step)
        bucket_round(step - 1)
        return carry

    begin_late = LATE_STEP if size - 1 > LATE_STEP else size - 1
    lax.fori_loop(1, min(begin_late + 1, size - 1), early_step, 0)
    if begin_late == size - 1:
        turn(early)
    used = slice(0, last_refs[0].shape[0])
    if other_chip is None:
        part_ref[used] = last_ref[...]
    else:
        other_chip.wait_recv()
        part_ref[used] = low_sum(last_ref[...], far_came_ref[...])
    begin(late)

    def both_step(step, carry):
        early_step(step, carry)
        advance(late, step - begin_late)
        return carry

    def middle_step(step, carry):
        pass_on(early, step)
        advance(late, step + size - 1 - begin_late)
        bucket_round(size - 2 + step - 1)
        return carry

    def end_step(step, carry):
        pass_on(early, step)
        pass_on(late, step - begin_late)
        bucket_round(size - 2 + step - 1)
        return carry

    late_passed = 0
    if begin_late < size - 1:
        lax.fori_loop(begin_late + 1, size - 1, both_step, 0)
        turn(early)
        advance(late, size - 1 - begin_late)
        lax.fori_loop(1, begin_late, middle_step, 0)
        pass_on(early, begin_late)
        turn(late)
        bucket_round(size - 2 + begin_late - 1)
        lax.fori_loop(begin_late + 1, size - 1, end_step, 0)
        late_passed = size - 2 - begin_late
    else:
        lax.fori_loop(1, size - 1, middle_step, 0)
        turn(late)
    if size == 2:
        lax.fori_loop(0, units, bucket_unit, 0)

    for i, way in ready + early:
        out_copy(i, way, size - 2).wait_recv()
        if way == 1:
            writes[i].start()

    features = gain_refs[0].shape[1]
    per_gain = features // LANES
    gain_rows = len(gain_refs) * per_gain
    small_ref[...] = jnp.zeros_like(small_ref)
    for i, ref in enumerate(gain_refs):
        total = jnp.sum(ref[...], axis=0, keepdims=True)
        for c in range(per_gain):
            at = i * per_gain + c
            small_ref[at : at + 1, :] = total[:, c * LANES : (c + 1) * LANES]
    for r in range(rows_used):
        block_sums = bucket_ref[r].reshape(LANES, LANES).T
        at = gain_rows + r
        small_ref[at : at + 1, :] = jnp.sum(block_sums, axis=0, keepdims=True)

    def near_copy(t):
        return remote(
            small_ref,
            near_ref.at[row],
            small_sems.at[0, t],
            small_sems.at[1, t],
            (me, (row + t) % peers),
        )

    def far_copy(t):
        return remote(
            far_ref.at[me],
            far_ref.at[me],
            small_sems.at[2, t],
            small_sems.at[3, t],
            ((me + t) % size, row),
        )

    for t in range(1, peers):
        near_copy(t).start()
    near_ref[pl.ds(row, 1)] = small_ref[...][None]
    for t in range(1, peers):
        near_copy(t).wait_recv()
    own = rows_used // peers
    total, sums = None, None
    for k in range(peers):
        gains = near_ref[k, :gain_rows]
        mine = near_ref[k, pl.ds(gain_rows + own * share_place(row, k, peers), own)]
        total = gains if total is None else total + gains
        sums = mine if sums is None else sums + mine
    small_ref_rows = far_ref.shape[1]
    far_ref[pl.ds(me, 1)] = jnp.concatenate(
        [total, sums, jnp.zeros((small_ref_rows - gain_rows - own, LANES), F32)], axis=0
    )[None]

    def far_start(t, carry):
        far_copy(t).start()
        return carry

    lax.fori_loop(1, size, far_start, 0)

    def late_step(step, carry):
        pass_on(late, step)
        return carry

    lax.fori_loop(1 + late_passed, size - 1, late_step, 0)

    def far_wait(t, carry):
        far_copy(t).wait()
        return carry

    lax.fori_loop(1, size, far_wait, 0)

    def far_add(k, total):
        return total + far_ref[k]

    small_out_ref[...] = lax.fori_loop(1, size, far_add, far_ref[0])
    for i, way in late:
        out_copy(i, way, size - 2).wait_recv()
    writes[-1].start()

    for t in range(1, peers):
        near_copy(t).wait_send()
    if other_chip is not None:
        other_chip.wait_send()
    for i, way in early + late:
        first_copy(i, way).wait_send()

    def sent(step, carry):
        for i, way in early + late:
            next_copy(i, way, step).wait_send()
        return carry

    lax.fori_loop(1, size - 1, sent, 0)

    for copy in writes:
        copy.wait()

    def sent_out(step, carry):
        for i, way in ready + early + late:
            out_copy(i, way, step).wait_send()
        return carry

    lax.fori_loop(0, size - 1, sent_out, 0)


def tail_sums(size, peers, buckets, heads, blocks, terms, last, ids, ds, gains):
    assert peers in (2, 4)
    grain = 2 * 16 * size
    features = last[0].shape[1]
    rows = [size * 2 * b.shape[1] for b in blocks]
    rows += [arrays[0].shape[0] for arrays in terms]
    rows.append(last[0].shape[0])
    padded = [r + -r % grain for r in rows]
    parts = [[b] for b in blocks]
    for arrays, r, p in zip(terms, rows[len(blocks) :], padded[len(blocks) :]):
        parts.append([jnp.pad(a, ((0, p - r), (0, 0))) for a in arrays])
    flat = [a for arrays in parts for a in arrays]
    lines = peers * (-(-heads * buckets // LANES))
    small = len(gains) * features // LANES + lines
    small = shape((small + -small % 8, LANES), F32)
    vmem, hbm = pl.BlockSpec(memory_space=pltpu.VMEM), pl.BlockSpec(memory_space=pl.ANY)
    steps = pltpu.SemaphoreType.DMA((len(rows), 2, size - 1))

    def ring_slots(i, steps):
        if i < len(blocks):
            return pltpu.VMEM((2, 1, 16, LANES), BF16)
        return pltpu.VMEM((2, *steps, padded[i] // (2 * size), features), BF16)

    *sums, small = pl.pallas_call(
        functools.partial(
            tail_kernel, size, peers, buckets, heads, len(blocks), [len(a) for a in parts]
        ),
        in_specs=[
            *[hbm] * (len(flat) + len(last) + 2),
            *[vmem] * len(gains),
        ],
        out_specs=[*[hbm] * len(rows), vmem],
        out_shape=[*[shape((p, features), BF16) for p in padded], small],
        scratch_shapes=[
            *[pltpu.VMEM((p, features), BF16) for p in padded],
            *[pltpu.VMEM(a.shape, a.dtype) for a in (*flat, last[0], ids)],
            pltpu.SemaphoreType.DMA((len(flat) + 2,)),
            pltpu.SemaphoreType.DMA((len(rows),)),
            *[ring_slots(i, (size - 1,)) for i in range(len(rows))],
            *[ring_slots(i, ()) for i in range(len(rows))],
            pltpu.VMEM((rows[-1], features), BF16),
            pltpu.VMEM((padded[-1], features), BF16),
            pltpu.VMEM(ds.shape, BF16),
            pltpu.VMEM((lines, LANES // buckets, buckets, LANES), F32),
            pltpu.VMEM(small.shape, F32),
            pltpu.VMEM((peers, *small.shape), F32),
            pltpu.VMEM((size, *small.shape), F32),
            steps,
            steps,
            steps,
            steps,
            pltpu.SemaphoreType.DMA((4, max(size, peers))),
            pltpu.SemaphoreType.DMA((2,)),
            pltpu.SemaphoreType.DMA((1,)),
        ],
        compiler_params=pltpu.CompilerParams(
            vmem_limit_bytes=VMEM_BYTES, collective_id=0, has_side_effects=True
        ),
        cost_estimate=cost(),
        name="tail_sums",
    )(*flat, *last, ids, ds, *gains)
    return [total[:r] for total, r in zip(sums, rows)], small


def swap(array, bit, size):
    return lax.ppermute(array, "mp", [(i, i ^ bit) for i in range(size)])


def after(array, *others):
    return lax.optimization_barrier((array, others))[0]


def shards(
    decoder_rows,
    memory_rows,
    decoder_token_length,
    memory_length,
    bucket_ids,
    relative_bucket_bias,
    self_gain,
    self_query,
    self_key,
    self_value,
    self_out,
    cross_gain,
    cross_query,
    cross_key,
    cross_value,
    cross_out,
    hidden_gain,
    widen_weight,
    narrow_weight,
    layer_cotangent,
):
    dp_size = lax.axis_size("dp")
    mp_size = lax.axis_size("mp")
    me = lax.axis_index("mp")
    doc, features = decoder_rows.shape
    slots = memory_rows.shape[0]
    cols = self_query.shape[1]
    heads = cols // HEAD_DIM
    buckets = relative_bucket_bias.shape[0]
    order = [*range(1, mp_size, 2), *range(0, mp_size, 2)]

    doc_length = lax.dynamic_index_in_dim(decoder_token_length, me, keepdims=False)
    doc_memory = lax.dynamic_index_in_dim(memory_length, me)
    position = jnp.arange(doc, dtype=jnp.int32)
    allowed = (position[:, None] <= position[None, :]) & (position[:, None] < doc_length)
    ids = jnp.where(allowed, bucket_ids.T, buckets)
    own_self = pack(
        (self_query.T, False),
        (self_key.T, False),
        (self_value.T, False),
        (self_out, False),
        (relative_bucket_bias.T, False),
    )
    own_cross = pack(
        (cross_query.T, False), (cross_key.T, False), (cross_value.T, False), (cross_out, False)
    )
    own_hidden = pack((widen_weight, True), (narrow_weight, False))

    def first_hops(own):
        shares, bit = {0: own}, mp_size // 2
        while bit > 1:
            for j in list(shares):
                shares[j | bit] = swap(shares[j], bit, mp_size)
            bit //= 2
        return shares

    def last_hop(shares, *others):
        if 1 not in shares:
            shares[1] = swap(shares[0], 1, mp_size)
        for j in range(2, mp_size, 2):
            shares[j] = after(shares[j], *others)
            shares[j | 1] = swap(shares[j], 1, mp_size)
        return shares

    near_self = first_hops(own_self)
    near_self[1] = swap(own_self, 1, mp_size)
    memory_rows = after(memory_rows, own_self)
    w_self = last_hop(near_self, own_cross, own_hidden, ids)
    w_self = [w_self[j] for j in order]
    near_cross = first_hops(own_cross)
    near_hidden = first_hops(own_hidden)
    near_hidden[1] = swap(own_hidden, 1, mp_size)
    memory_seen = lax.all_to_all(
        memory_rows.reshape(dp_size, slots // dp_size, features), "dp", 0, 0
    ).reshape(slots, features)

    gain_self = self_gain.astype(F32)[None]
    gain_cross = cross_gain.astype(F32)[None]
    gain_hidden = hidden_gain.astype(F32)[None]

    *saved_self, after_self = self_forward(heads, buckets, decoder_rows, gain_self, w_self, ids)
    w_cross = last_hop(near_cross, after_self)
    w_cross = [w_cross[j] for j in order]
    *saved_cross, after_cross = cross_forward(
        heads, after_self, gain_cross, memory_seen, doc_memory, w_cross
    )

    before, wide_sums, narrow_sums, w_hidden = (), [], [], near_hidden
    for j in range(0, mp_size, 2):
        wide_sum, narrow_sum, *before = feed_forward(
            after_cross,
            gain_hidden,
            layer_cotangent,
            [w_hidden[j + 1], w_hidden[j]],
            before,
            j == mp_size - 2,
        )
        wide_sums.append(wide_sum)
        narrow_sums.append(narrow_sum)
        if j == 0:
            w_hidden = last_hop(near_hidden, before[0])
    layer_output, grad_after_cross, branch, hidden_gain_grad = before

    scattered, hops = wide_sums, narrow_sums[1:]
    if wide_sums[0].shape[0] % (2 * 16 * dp_size):
        scattered, hops = [], wide_sums[1:] + narrow_sums[1:]
    *sums, grad_memory, grad_after_self, branch, cross_gain_grad = cross_backward(
        heads,
        dp_size,
        after_self,
        gain_cross,
        memory_seen,
        doc_memory,
        branch,
        grad_after_cross,
        saved_cross,
        w_cross,
        scattered,
        hops,
    )
    came, sums = sums[: len(hops)], sums[len(hops) :]
    if scattered:
        blocks, terms, cross_sums = sums[:1], [narrow_sums[:1] + came], sums[1:]
    else:
        blocks, cross_sums = [], sums
        hidden = [wide_sums[0], narrow_sums[0]], came
        terms = [[jnp.concatenate(both, axis=0) for both in hidden if both]]
    memory_grad = lax.all_to_all(
        grad_memory.reshape(dp_size, slots // dp_size, features), "dp", 0, 0
    ).reshape(slots, features)

    *sums, score_grads, input_grad, self_gain_grad = self_backward(
        heads,
        decoder_rows,
        gain_self,
        branch,
        grad_after_self,
        saved_self,
        w_self,
        cross_sums[1:],
    )
    cross_sums[1:], last = sums[: len(cross_sums) - 1], sums[len(cross_sums) - 1 :]
    (*hidden, sum_cross, sum_self), small = tail_sums(
        dp_size,
        mp_size,
        buckets,
        heads,
        blocks,
        terms + [cross_sums],
        last,
        ids,
        score_grads,
        (self_gain_grad, cross_gain_grad, hidden_gain_grad),
    )
    wide_grad, narrow_grad, self_grads, cross_grads = finish(
        *(hidden if scattered else jnp.split(hidden[0], 2)), sum_cross, sum_self
    )
    gain_rows = 3 * features // LANES
    gains = small[:gain_rows].reshape(3, features)
    lines = -(-heads * buckets // LANES)
    sums = small[gain_rows : gain_rows + lines, : heads // lines * buckets]
    position_grad = sums.reshape(heads, buckets).T

    return (
        layer_output,
        input_grad,
        memory_grad,
        position_grad,
        gains[0],
        *[grad.T for grad in self_grads[:3]],
        self_grads[3],
        gains[1],
        *[grad.T for grad in cross_grads[:3]],
        cross_grads[3],
        gains[2],
        wide_grad,
        narrow_grad,
    )


def solution(mesh):
    return jax.shard_map(
        shards,
        mesh=mesh,
        in_specs=(
            P(("dp", "mp"), None),
            P(("dp", "mp"), None),
            P("dp"),
            P("dp"),
            P(),
            P(None, "mp"),
            P(),
            P(None, "mp"),
            P(None, "mp"),
            P(None, "mp"),
            P("mp", None),
            P(),
            P(None, "mp"),
            P(None, "mp"),
            P(None, "mp"),
            P("mp", None),
            P(),
            P(None, "mp"),
            P("mp", None),
            P(("dp", "mp"), None),
        ),
        out_specs=(
            P(("dp", "mp"), None),
            P(("dp", "mp"), None),
            P(("dp", "mp"), None),
            P(None, "mp"),
            P(),
            P(None, "mp"),
            P(None, "mp"),
            P(None, "mp"),
            P("mp", None),
            P(),
            P(None, "mp"),
            P(None, "mp"),
            P(None, "mp"),
            P("mp", None),
            P(),
            P(None, "mp"),
            P("mp", None),
        ),
        check_vma=False,
    )
```

```python
import functools

import jax
import jax.numpy as jnp
from jax import lax
from jax.experimental import pallas as pl
from jax.experimental.pallas import tpu as pltpu
from jax.sharding import PartitionSpec as P

HEAD_DIM = 64
NORM_EPS = 1e-06
MASKED = -1e30
SCALE = HEAD_DIM**-0.5
BF16 = jnp.bfloat16
F32 = jnp.float32
LANES = 128
TABLE_ROWS = 16
TILE_ROWS = 16
LARGEST_SUM = 1e30
LATE_STEP = 4
UNIT_BUCKETS = 4
UNIT_ROWS = 64
HEAD_BLOCK = 256
BLOCK_HEADS = HEAD_BLOCK // HEAD_DIM
Q_BLOCK = 256
K_BLOCK = 512
FORWARD_K_BLOCK = 256
HIDDEN_BLOCK = 256
MEMORY_BLOCK = 768
FINISH_BLOCK = 384
ROW_BLOCK = 128
VMEM_BYTES = 56 * 1024 * 1024
GELU_ROOT = 0.7978845608028654
GELU_CUBE = 0.044715


def dot_nn(a, b):
    return lax.dot_general(a, b, (((1,), (0,)), ((), ())), preferred_element_type=F32)


def dot_nt(a, b):
    return lax.dot_general(a, b, (((1,), (1,)), ((), ())), preferred_element_type=F32)


def dot_tn(a, b):
    return lax.dot_general(a, b, (((0,), (0,)), ((), ())), preferred_element_type=F32)


def flip(a):
    return a.astype(F32).T.astype(BF16)


def spans(size, step):
    return [slice(i, i + step) for i in range(0, size, step)]


def norm_scale(rows):
    return lax.rsqrt(jnp.mean(rows * rows, axis=-1, keepdims=True) + NORM_EPS)


def norm_into(normed_ref, rows_ref, gain_ref):
    for span in spans(rows_ref.shape[0], ROW_BLOCK):
        rows = rows_ref[span].astype(F32)
        normed_ref[span] = (rows * norm_scale(rows) * gain_ref[...]).astype(BF16)


def norm_back_into(span, grad, out_ref, low_ref, gain_grad_ref, rows_ref, gain_ref, add_ref):
    rows = rows_ref[span].astype(F32)
    scale = norm_scale(rows)
    unit = rows * scale
    grad_unit = grad * gain_ref[...]
    mean = jnp.mean(grad_unit * unit, axis=-1, keepdims=True)
    out = add_ref[span].astype(F32) + scale * (grad_unit - unit * mean)
    out_ref[span] = out
    if low_ref is not None:
        low_ref[span] = out.astype(BF16)
    gain_grad_ref[...] += jnp.sum((grad * unit).reshape(-1, 8, rows.shape[1]), axis=0)


def gelu_and_slope(v):
    square = v * v
    bend = jnp.tanh(GELU_ROOT * (v + GELU_CUBE * v * square))
    half = 0.5 * (1.0 + bend)
    slope = half + 0.5 * v * (1.0 - bend * bend) * GELU_ROOT * (1.0 + 3.0 * GELU_CUBE * square)
    return v * half, slope


def lane_block(start):
    return pl.ds(pl.multiple_of(start, LANES), LANES)


def extra_lanes(rows, allowed):
    lane = lax.broadcasted_iota(jnp.int32, (rows, LANES), 1) % HEAD_DIM
    first = MASKED if allowed is None else jnp.where(allowed, 0.0, MASKED)
    return jnp.where(lane == 0, first, jnp.where(lane < 4, 1.0, 0.0)).astype(BF16)


def pick(which, block, other):
    lane = lax.broadcasted_iota(jnp.int32, block.shape, 1)
    return jnp.where((lane < HEAD_DIM) == (which == 0), block, other)


def half_rows(which):
    return slice(which * HEAD_DIM, (which + 1) * HEAD_DIM)


def split(values):
    high = values.astype(BF16).astype(F32)
    rest = values - high
    middle = rest.astype(BF16).astype(F32)
    return high, middle, rest - middle


def with_extra(which, block_t, masked, minus):
    columns = block_t.shape[1]
    row = lax.broadcasted_iota(jnp.int32, (HEAD_DIM, columns), 0)
    extra = jnp.where(row == 0, 1.0 if masked else 0.0, 0.0)
    if minus is not None:
        for i, part in enumerate(split(minus)):
            extra = jnp.where(row == i + 1, -part, extra)
    own = block_t[half_rows(which)]
    return jnp.concatenate([own, extra] if which == 0 else [extra, own], axis=0).astype(BF16)


def bias_block(table_ref, ids_ref, index, rows, start):
    row = jnp.broadcast_to(table_ref[pl.ds(index, 1), :], (rows, LANES))
    return jnp.concatenate(
        [
            jnp.take_along_axis(row, ids_ref[:rows, c : c + LANES], axis=1)
            for c in range(start, start + Q_BLOCK, LANES)
        ],
        axis=1,
    )


def ring_place(me, size):
    return jnp.where(me % 2 == 0, me // 2, size - 1 - me // 2)


def ring_device(place, size):
    return jnp.where(place < size // 2, 2 * place, 2 * (size - 1 - place) + 1)


def ring_ways(size):
    me = lax.axis_index("dp")
    place = ring_place(me, size)
    return (
        (place, ring_device((place + 1) % size, size)),
        (size - 1 - place, ring_device((place + size - 1) % size, size)),
    )


def differing(row, bit):
    return row + bit - 2 * bit * ((row // bit) % 2)


def remote(source, target, send_sem, recv_sem, device):
    return pltpu.make_async_remote_copy(
        src_ref=source,
        dst_ref=target,
        send_sem=send_sem,
        recv_sem=recv_sem,
        device_id=device,
        device_id_type=pl.DeviceIdType.MESH,
    )


def greet(bits, devices=()):
    me, row = lax.axis_index("dp"), lax.axis_index("mp")
    barrier = pltpu.get_barrier_semaphore()
    others = [(me, differing(row, bit)) for bit in bits] + [(device, row) for device in devices]
    for other in others:
        pl.semaphore_signal(
            barrier, inc=1, device_id=other, device_id_type=pl.DeviceIdType.MESH
        )
    pl.semaphore_wait(barrier, len(others))


def to_differing(bit, source, target, sems):
    me, row = lax.axis_index("dp"), lax.axis_index("mp")
    return remote(source, target, sems.at[0], sems.at[1], (me, differing(row, bit)))


class Scatter:
    def __init__(self, size, part, slots, done, send, came):
        self.size, self.part, self.slots, self.done = size, part, slots, done
        self.send, self.came = send, came
        self.ways, self.row = ring_ways(size), lax.axis_index("mp")

    def span(self, way, number):
        rows = self.slots.shape[3]
        return pl.ds(pl.multiple_of((way * self.size + number) * rows, 16), rows)

    def copy(self, way, step, source):
        return remote(
            source,
            self.slots.at[way, step],
            self.send.at[way, step],
            self.came.at[way, step],
            (self.ways[way][1], self.row),
        )

    def first(self, way):
        return self.copy(way, 0, self.part.at[:, self.span(way, self.ways[way][0])])

    def next(self, way, step):
        return self.copy(way, step, self.slots.at[way, step - 1])

    def begin(self):
        for way in range(2):
            self.first(way).start()

    def total(self, way, step):
        self.copy(way, step, self.slots.at[way, step]).wait_recv()
        span = self.span(way, (self.ways[way][0] - step - 1 + self.size) % self.size)
        return low_sum(self.slots[way, step], self.part[:, span])

    def advance(self, step):
        for way in range(2):
            self.slots[way, step - 1] = self.total(way, step - 1)
            self.next(way, step).start()

    def turn(self):
        for way in range(2):
            self.done[way] = self.total(way, self.size - 2)

    def wait_sent(self):
        for way in range(2):
            self.first(way).wait_send()

        def sent(step, carry):
            for way in range(2):
                self.next(way, step).wait_send()
            return carry

        lax.fori_loop(1, self.size - 1, sent, 0)


def low_sum(a, b):
    return (a.astype(F32) + b.astype(F32)).astype(BF16)


class Stack:
    def __init__(self, sources, stack_ref, sems, kinds, rows):
        features = stack_ref.shape[0] // kinds
        self.copies = [
            [
                pltpu.make_async_copy(
                    source.at[pl.ds(kind * rows, rows)],
                    stack_ref.at[pl.ds(kind * features + p * rows, rows)],
                    sems.at[p, kind],
                )
                for p, source in enumerate(sources)
            ]
            for kind in range(kinds)
        ]

    def start(self):
        for copies in self.copies:
            for copy in copies:
                copy.start()

    def wait(self, *kinds):
        for kind in kinds:
            for copy in self.copies[kind]:
                copy.wait()


def table_copies(sources, tables_ref, sems, kinds):
    start = sources[0].shape[0] - TABLE_ROWS
    return [
        pltpu.make_async_copy(
            source.at[pl.ds(start, TABLE_ROWS)], tables_ref.at[p], sems.at[p, kinds]
        )
        for p, source in enumerate(sources)
    ]


def table_into(table_ref, tables_ref, heads, buckets):
    for p in range(tables_ref.shape[0]):
        rows = tables_ref[p, :, :LANES].astype(F32)
        lane = lax.broadcasted_iota(jnp.int32, rows.shape, 1)
        rows = jnp.where(lane < buckets, rows, MASKED)
        for h in range(heads):
            table_ref[p * heads + h : p * heads + h + 1, :] = rows[h : h + 1, :]


def self_forward_kernel(heads, buckets, shares, rows_ref, gain_ref, ids_ref, *refs):
    sources = refs[:shares]
    q_ref, k_ref, v_ref, mixed_ref, lse_ref, bias_ref, out_ref = refs[shares : shares + 7]
    w_ref, tables_ref, table_ref, normed_ref, sems = refs[shares + 7 :]
    step = pl.program_id(0)
    doc, features = rows_ref.shape
    stack = Stack(sources, w_ref, sems, 4, heads * HEAD_DIM)

    @pl.when(step == 0)
    def _():
        stack.start()
        tables = table_copies(sources, tables_ref, sems, 4)
        for copy in tables:
            copy.start()
        norm_into(normed_ref, rows_ref, gain_ref)
        out_ref[...] = rows_ref[...].astype(F32)
        for copy in tables:
            copy.wait()
        table_into(table_ref, tables_ref, heads, buckets)
        stack.wait(0, 1, 2, 3)

    def weights(kind):
        start = pl.multiple_of(kind * features + step * HEAD_BLOCK, HEAD_BLOCK)
        return w_ref[pl.ds(start, HEAD_BLOCK)]

    for kind, ref in enumerate((q_ref, k_ref, v_ref)):
        ref[...] = dot_nt(normed_ref[...], weights(kind)).astype(BF16)
    none = jnp.zeros((doc, LANES), BF16)
    for pair in range(BLOCK_HEADS // 2):
        lanes = slice(pair * LANES, (pair + 1) * LANES)
        k, v_t = k_ref[:, lanes], flip(v_ref[:, lanes])
        q_t = flip(q_ref[:, lanes].astype(F32) * SCALE)
        k_of = [pick(which, k, none) for which in range(2)]
        for span in spans(doc, Q_BLOCK):
            rows, mixed = span.stop, []
            for which in range(2):
                h = 2 * pair + which
                bias = bias_block(table_ref, ids_ref, step * BLOCK_HEADS + h, rows, span.start)
                bias_ref[h, :rows, span] = bias.astype(BF16)
                s = dot_nn(k_of[which][:rows], q_t[:, span]) + bias
                top = jnp.max(s, axis=0, keepdims=True)
                p = jnp.exp(s - top)
                total = jnp.sum(p, axis=0, keepdims=True)
                mixed.append(dot_nn(v_t[half_rows(which), :rows], p.astype(BF16)) / total)
                lse_ref[0, h : h + 1, span] = top + jnp.log(total)
            mixed_ref[span, lanes] = jnp.concatenate(mixed, axis=0).T.astype(BF16)
    out_ref[...] += dot_nn(mixed_ref[...], weights(3))


def self_backward_kernel(heads, shares, *refs):
    count = shares // 2
    rows_ref, gain_ref, branch_ref, add_ref = refs[:4]
    q_ref, k_ref, v_ref, mixed_ref, lse_ref, bias_ref = refs[4:10]
    sources, refs = refs[10 : 10 + shares], refs[10 + shares :]
    hop_in, hop_out, refs = refs[: count - 1], refs[count - 1 : 2 * count - 2], refs[2 * count - 2 :]
    sums, refs = refs[:count], refs[count:]
    ds_ref, out_ref, gain_grad_ref = refs[:3]
    w_ref, normed_ref, g_ref, grad_ref, back_ref, give_ref, keep_ref, came_ref = refs[3:11]
    sems, swap_sems, hop_sems = refs[11:]
    step = pl.program_id(0)
    doc, features = rows_ref.shape
    half = features // 2
    stack = Stack(sources, w_ref, sems, 4, heads * HEAD_DIM)
    swap = to_differing(1, give_ref, came_ref, swap_sems)
    hops = [
        to_differing(2, source, target, hop_sems) for source, target in zip(hop_in, hop_out)
    ]

    @pl.when(step == 0)
    def _():
        stack.start()
        greet([1, 2][:count])
        for hop in hops:
            hop.start()
        norm_into(normed_ref, rows_ref, gain_ref)
        stack.wait(3)

    start = pl.multiple_of(3 * features + step * HEAD_BLOCK, HEAD_BLOCK)
    g_ref[...] = dot_nt(branch_ref[...], w_ref[pl.ds(start, HEAD_BLOCK)]).astype(BF16)
    none = jnp.zeros((doc, LANES), BF16)
    ones = extra_lanes(doc, None)
    for pair in range(BLOCK_HEADS // 2):
        lanes = lane_block(step * HEAD_BLOCK + pair * LANES)
        q, k, v = q_ref[:, lanes], k_ref[:, lanes], v_ref[:, lanes]
        g = g_ref[:, pair * LANES : (pair + 1) * LANES]
        q_t, k_t = q.astype(F32).T * SCALE, flip(k)
        g_t = g.astype(F32).T
        inner = g_t * mixed_ref[:, lanes].astype(F32).T
        per_head = []
        for which in range(2):
            h = 2 * pair + which
            minus = jnp.sum(inner[half_rows(which)], axis=0, keepdims=True)
            per_head.append(
                (
                    pick(which, k, ones),
                    pick(which, v, ones),
                    with_extra(which, q_t, False, lse_ref[0, h : h + 1, :]),
                    with_extra(which, g_t, False, minus),
                    pick(which, q, none),
                    pick(which, g, none),
                )
            )
        grad_k = grad_v = None
        for span in spans(doc, Q_BLOCK):
            rows, grad_q, part_k, part_v = span.stop, [], None, None
            for which, (k_of, v_of, q_with, g_with, q_of, g_of) in enumerate(per_head):
                h = 2 * pair + which
                s = dot_nn(k_of[:rows], q_with[:, span])
                p = jnp.exp(s + bias_ref[h, :rows, span].astype(F32))
                ds = (p * dot_nn(v_of[:rows], g_with[:, span])).astype(BF16)
                ds_ref[h, :rows, span] = ds
                grad_q.append(dot_nn(k_t[half_rows(which), :rows], ds))
                to_v = dot_nn(p.astype(BF16), g_of[span])
                to_k = dot_nn(ds, q_of[span])
                part_v = to_v if part_v is None else part_v + to_v
                part_k = to_k if part_k is None else part_k + to_k
            grad_q = (jnp.concatenate(grad_q, axis=0) * SCALE).T
            grad_ref[span, lanes] = grad_q.astype(BF16)
            if grad_v is not None:
                part_v = jnp.concatenate(
                    [part_v[: span.start] + grad_v, part_v[span.start :]], axis=0
                )
                part_k = jnp.concatenate(
                    [part_k[: span.start] + grad_k, part_k[span.start :]], axis=0
                )
            grad_v, grad_k = part_v, part_k
        k_lanes = lane_block(features + step * HEAD_BLOCK + pair * LANES)
        v_lanes = lane_block(2 * features + step * HEAD_BLOCK + pair * LANES)
        grad_ref[:, k_lanes] = (grad_k * SCALE).astype(BF16)
        grad_ref[:, v_lanes] = grad_v.astype(BF16)

    @pl.when(step == pl.num_programs(0) - 1)
    def _():
        stack.wait(0, 1, 2)
        def weight_grads(ref, columns):
            for kind in range(3):
                kind_columns = slice(kind * features + columns.start, kind * features + columns.stop)
                ref[kind] = dot_tn(grad_ref[:, kind_columns], normed_ref[...]).astype(BF16)
            ref[3] = dot_tn(mixed_ref[:, columns], branch_ref[...]).astype(BF16)

        weight_grads(give_ref, slice(0, half))
        swap.start()
        weight_grads(keep_ref, slice(half, features))
        gain_grad_ref[...] = jnp.zeros_like(gain_grad_ref)
        back_ref[...] = dot_nn(grad_ref[...], w_ref[: 3 * features])
        for span in spans(doc, ROW_BLOCK):
            norm_back_into(
                span, back_ref[span], out_ref, None, gain_grad_ref, rows_ref, gain_ref, add_ref
            )
        swap.wait_recv()
        rows = half // count
        for share, sums_ref in enumerate(sums):
            for kind in range(4):
                span = slice(share * rows, (share + 1) * rows)
                to = slice(kind * rows, (kind + 1) * rows)
                sums_ref[to] = low_sum(keep_ref[kind, span], came_ref[kind, span])
        swap.wait_send()
        for hop in hops:
            hop.wait()


def cross_forward_kernel(heads, shares, length_ref, rows_ref, gain_ref, memory_ref, *refs):
    sources = refs[:shares]
    q_ref, k_ref, v_ref, mixed_ref, lse_ref, out_ref = refs[shares : shares + 6]
    w_ref, normed_ref, extra_ref, p_ref, mix_ref, sems = refs[shares + 6 :]
    step = pl.program_id(0)
    (doc, features), slots = rows_ref.shape, memory_ref.shape[0]
    stack = Stack(sources, w_ref, sems, 4, heads * HEAD_DIM)

    @pl.when(step == 0)
    def _():
        stack.start()
        norm_into(normed_ref, rows_ref, gain_ref)
        out_ref[...] = rows_ref[...]
        slot = lax.broadcasted_iota(jnp.int32, (slots, LANES), 0)
        extra_ref[...] = extra_lanes(slots, slot < length_ref[0])
        stack.wait(0, 1, 2, 3)

    def weights(kind):
        start = pl.multiple_of(kind * features + step * HEAD_BLOCK, HEAD_BLOCK)
        return w_ref[pl.ds(start, HEAD_BLOCK)]

    q_ref[...] = dot_nt(normed_ref[...], weights(0)).astype(BF16)
    k_ref[...] = dot_nt(memory_ref[...], weights(1)).astype(BF16)
    v_ref[...] = dot_nt(memory_ref[...], weights(2)).astype(BF16)

    units = [
        (pair, which, span)
        for pair in range(BLOCK_HEADS // 2)
        for span in spans(doc, Q_BLOCK)
        for which in range(2)
    ]
    ones = jnp.ones((TILE_ROWS, slots), BF16)
    keys = spans(slots, FORWARD_K_BLOCK)

    def lanes_of(pair):
        return slice(pair * LANES, (pair + 1) * LANES)

    def key_side(pair, which):
        return pick(which, k_ref[:, lanes_of(pair)], extra_ref[...])

    def write(pair, which, span, top, total, mixed):
        h = 2 * pair + which
        lse_ref[0, h : h + 1, span] = top + jnp.log(total)
        mix_ref[half_rows(which)] = mixed / total
        if which == 1:
            mixed_ref[span, lanes_of(pair)] = mix_ref[...].T.astype(BF16)

    v_t = [flip(v_ref[:, lanes_of(p)]) for p in range(BLOCK_HEADS // 2)]
    q_t = [q_ref[:, lanes_of(p)].astype(F32).T * SCALE for p in range(BLOCK_HEADS // 2)]

    def begin(unit):
        pair, which, span = unit
        k_of = key_side(pair, which)
        s = dot_nn(k_of[keys[0]], with_extra(which, q_t[pair][:, span], True, None))
        top = jnp.max(s, axis=0, keepdims=True)
        return k_of, s, top, with_extra(which, q_t[pair][:, span], True, top)

    worst = jnp.zeros((1, Q_BLOCK), F32)
    ahead = begin(units[0])
    for i, (pair, which, span) in enumerate(units):
        (k_of, s, top, q_with), slot = ahead, i % 2
        p_ref[slot, keys[0]] = jnp.exp(s - top).astype(BF16)
        for rows in keys[1:]:
            p_ref[slot, rows] = jnp.exp(dot_nn(k_of[rows], q_with)).astype(BF16)
        if i + 1 < len(units):
            ahead = begin(units[i + 1])
        value_side = jnp.concatenate([v_t[pair][half_rows(which)], ones], axis=0)
        mixed = dot_nn(value_side, p_ref[slot])
        total = mixed[HEAD_DIM : HEAD_DIM + 1]
        worst = jnp.maximum(worst, total)
        write(pair, which, span, top, total, mixed[:HEAD_DIM])

    @pl.when(jnp.max(worst) > LARGEST_SUM)
    def _():
        for pair, which, span in units:
            q_with = with_extra(
                which, q_ref[:, lanes_of(pair)].astype(F32).T[:, span] * SCALE, True, None
            )
            k_of = key_side(pair, which)
            s = [dot_nn(k_of[rows], q_with) for rows in keys]
            top = functools.reduce(jnp.maximum, [jnp.max(c, axis=0, keepdims=True) for c in s])
            total = jnp.zeros_like(top)
            for rows, chunk in zip(keys, s):
                p = jnp.exp(chunk - top)
                total = total + jnp.sum(p, axis=0, keepdims=True)
                p_ref[0, rows] = p.astype(BF16)
            mixed = dot_nn(flip(v_ref[:, lanes_of(pair)])[half_rows(which)], p_ref[0])
            write(pair, which, span, top, total, mixed)

    out_ref[...] += dot_nn(mixed_ref[...], weights(3))


def cross_backward_kernel(heads, shares, size, scattered, hops_wanted, length_ref, *refs):
    gain_ref, branch_ref, q_ref, mixed_ref, lse_ref = refs[:5]
    rows_in, memory_in, add_in, k_in, v_in = refs[5:10]
    sources = refs[10 : 10 + shares]
    count = shares // 2
    refs = refs[10 + shares :]
    scatter_in, refs = refs[:scattered], refs[scattered:]
    hidden_in, refs = refs[:hops_wanted], refs[hops_wanted:]
    hidden_out, refs = refs[:hops_wanted], refs[hops_wanted:]
    if scattered:
        scatter_out, refs = refs[0], refs[1:]
        (part_ref, ring_slots, done_ref, scatter_came), refs = refs[-8:-4], refs[:-8] + refs[-4:]
        (ring_send, ring_came, part_sems, done_sems), refs = refs[-4:], refs[:-4]
        scatter = Scatter(size, part_ref, ring_slots, done_ref, ring_send, ring_came)
        part_loads = [
            pltpu.make_async_copy(source, part_ref.at[i], part_sems.at[i])
            for i, source in enumerate(scatter_in)
        ]
        for copy in part_loads:
            copy.start()
    sums, refs = refs[:count], refs[count:]
    memory_out, out_ref, low_ref, gain_grad_ref = refs[:4]
    rows_ref, memory_ref, add_ref, k_ref, v_ref = refs[4:9]
    (
        w_ref,
        normed_ref,
        extra_ref,
        g_ref,
        grad_q_ref,
        grad_ref,
        ds_ref,
        give_ref,
        keep_ref,
        came_ref,
        memory_grad_ref,
        back_ref,
        sems,
        load_sems,
        key_sems,
        out_sems,
        swap_sems,
        hop_sems,
    ) = refs[9:]
    (doc, features), slots = rows_ref.shape, memory_ref.shape[0]
    half, blocks = features // 2, features // HEAD_BLOCK
    stack = Stack(sources, w_ref, sems, 4, heads * HEAD_DIM)
    loads = [
        pltpu.make_async_copy(source, target, load_sems.at[i])
        for i, (source, target) in enumerate(
            ((memory_in, memory_ref), (rows_in, rows_ref), (add_in, add_ref))
        )
    ]

    def key_copies(b):
        lanes = pl.ds(pl.multiple_of(b * HEAD_BLOCK, HEAD_BLOCK), HEAD_BLOCK)
        return [
            pltpu.make_async_copy(source.at[:, lanes], target.at[b], key_sems.at[i, b])
            for i, (source, target) in enumerate(((k_in, k_ref), (v_in, v_ref)))
        ]

    stack.start()
    for b in range(blocks):
        for copy in key_copies(b):
            copy.start()
    for copy in loads:
        copy.start()
    greet([1, 2][:count], [way[1] for way in ring_ways(size)] if scattered else [])
    hops = [
        to_differing(2, source, target, hop_sems.at[i])
        for i, (source, target) in enumerate(zip(hidden_in, hidden_out))
    ]
    for hop in hops:
        hop.start()
    if scattered:
        for copy in part_loads:
            copy.wait()
        scatter.begin()
    slot = lax.broadcasted_iota(jnp.int32, (slots, LANES), 0)
    extra_ref[...] = extra_lanes(slots, slot < length_ref[0])
    none = jnp.zeros((doc, LANES), BF16)
    stack.wait(3)

    def one_block(step, carry):
        start = pl.multiple_of(3 * features + step * HEAD_BLOCK, HEAD_BLOCK)
        g_ref[...] = dot_nt(branch_ref[...], w_ref[pl.ds(start, HEAD_BLOCK)]).astype(BF16)
        for copy in key_copies(step):
            copy.wait()
        for pair in range(BLOCK_HEADS // 2):
            local = slice(pair * LANES, (pair + 1) * LANES)
            lanes = lane_block(step * HEAD_BLOCK + pair * LANES)
            v_lanes = lane_block(features + step * HEAD_BLOCK + pair * LANES)
            q, g = q_ref[:, lanes], g_ref[:, local]
            q_t, g_t = q.astype(F32).T * SCALE, g.astype(F32).T
            inner = g_t * mixed_ref[:, lanes].astype(F32).T
            per_head = []
            for which in range(2):
                h = 2 * pair + which
                minus = jnp.sum(inner[half_rows(which)], axis=0, keepdims=True)
                per_head.append(
                    (
                        with_extra(which, q_t, True, lse_ref[step, h : h + 1, :]),
                        with_extra(which, g_t, False, minus),
                        pick(which, q, none),
                        pick(which, g, none),
                    )
                )
            for rows in spans(slots, K_BLOCK):
                k, v, extra = k_ref[step, rows, local], v_ref[step, rows, local], extra_ref[rows]
                part_k = part_v = None
                for which, (q_with, g_with, q_of, g_of) in enumerate(per_head):
                    p = jnp.exp(dot_nn(pick(which, k, extra), q_with))
                    ds = (p * dot_nn(pick(which, v, extra), g_with)).astype(BF16)
                    ds_ref[which, rows] = ds
                    to_v = dot_nn(p.astype(BF16), g_of)
                    to_k = dot_nn(ds, q_of)
                    part_v = to_v if part_v is None else part_v + to_v
                    part_k = to_k if part_k is None else part_k + to_k
                grad_ref[rows, lanes] = (part_k * SCALE).astype(BF16)
                grad_ref[rows, v_lanes] = part_v.astype(BF16)
            k_t = flip(k_ref[step, :, local])
            grad_q = [dot_nn(k_t[half_rows(which)], ds_ref[which]) for which in range(2)]
            grad_q_ref[:, lanes] = (jnp.concatenate(grad_q, axis=0) * SCALE).T.astype(BF16)
            if scattered:
                scatter_step(1 + step * (BLOCK_HEADS // 2) + pair)
        return carry

    places = blocks * (BLOCK_HEADS // 2)

    def scatter_step(step):
        if size - 2 >= places:
            scatter.advance(step)
        elif size > 2:

            @pl.when(step <= size - 2)
            def _():
                scatter.advance(step)

    lax.fori_loop(0, blocks, one_block, 0)
    if scattered:

        def rest(step, carry):
            scatter.advance(step)
            return carry

        lax.fori_loop(min(places, size - 2) + 1, size - 1, rest, 0)
        scatter.turn()
        done_hops = [
            to_differing(2, done_ref.at[:, i], scatter_came, done_sems)
            for i in range(1, scattered)
        ]
        for hop in done_hops:
            hop.start()

    for copy in loads:
        copy.wait()
    norm_into(normed_ref, rows_ref, gain_ref)

    def weight_grads(ref, first):
        columns = slice(first, first + half)
        v_columns = slice(features + first, features + first + half)
        ref[0] = dot_tn(grad_q_ref[:, columns], normed_ref[...]).astype(BF16)
        ref[1] = dot_tn(grad_ref[:, columns], memory_ref[...]).astype(BF16)
        ref[2] = dot_tn(grad_ref[:, v_columns], memory_ref[...]).astype(BF16)
        ref[3] = dot_tn(mixed_ref[:, columns], branch_ref[...]).astype(BF16)

    weight_grads(give_ref, 0)
    swap = to_differing(1, give_ref, came_ref, swap_sems)
    swap.start()
    stack.wait(0, 1, 2)
    writes = []
    for i, rows in enumerate(spans(slots, MEMORY_BLOCK)):
        memory_grad_ref[rows] = dot_nn(
            grad_ref[rows], w_ref[features : 3 * features]
        ).astype(BF16)
        writes.append(
            pltpu.make_async_copy(memory_grad_ref.at[rows], memory_out.at[rows], out_sems.at[i])
        )
        writes[-1].start()
    weight_grads(keep_ref, half)
    gain_grad_ref[...] = jnp.zeros_like(gain_grad_ref)
    back_ref[...] = dot_nn(grad_q_ref[...], w_ref[:features])
    for span in spans(doc, ROW_BLOCK):
        norm_back_into(
            span, back_ref[span], out_ref, low_ref, gain_grad_ref, rows_ref, gain_ref, add_ref
        )
    swap.wait_recv()
    rows = half // count
    for share, sums_ref in enumerate(sums):
        for kind in range(4):
            span = slice(share * rows, (share + 1) * rows)
            to = slice(kind * rows, (kind + 1) * rows)
            sums_ref[to] = low_sum(keep_ref[kind, span], came_ref[kind, span])
    swap.wait_send()
    for copy in writes:
        copy.wait()
    for hop in hops:
        hop.wait()
    if scattered:
        for hop in done_hops:
            hop.wait()
        own = done_ref[:, 0]
        scatter_out[...] = low_sum(own, scatter_came[...]) if done_hops else own
        scatter.wait_sent()


def feed_forward_kernel(first, last, rows_ref, gain_ref, cotangent_ref, *refs):
    sources, refs = refs[:2], refs[2:]
    if not first:
        before_in, refs = refs[:2], refs[2:]
    sums, layer_ref, out_ref = refs[:2], refs[2], refs[3]
    if last:
        low_ref, gain_grad_ref = refs[4:6]
        refs = refs[2:]
    (
        wide_ref,
        narrow_ref,
        normed_ref,
        normed_t,
        cotangent_t,
        active_ref,
        grad_ref,
        give_ref,
        keep_ref,
        came_ref,
        layer_in_ref,
        back_in_ref,
        product_ref,
        sems,
        before_sems,
        swap_sems,
    ) = refs[4:]
    step, steps = pl.program_id(0), pl.num_programs(0)
    half = steps // 2
    doc = rows_ref.shape[0]
    hidden = sources[0].shape[0] // 2
    copies = [
        [
            pltpu.make_async_copy(
                source.at[pl.ds(kind * hidden, hidden)],
                stack.at[pl.ds(p * hidden, hidden)],
                sems.at[p, kind],
            )
            for kind, stack in enumerate((wide_ref, narrow_ref))
        ]
        for p, source in enumerate(sources)
    ]
    loads = []
    if not first:
        loads = [
            pltpu.make_async_copy(source, target, before_sems.at[i])
            for i, (source, target) in enumerate(zip(before_in, (layer_in_ref, back_in_ref)))
        ]
    swap = to_differing(1, give_ref, came_ref, swap_sems)

    @pl.when(step == 0)
    def _():
        for pair in copies:
            for copy in pair:
                copy.start()
        for copy in loads:
            copy.start()
        greet([1])
        norm_into(normed_ref, rows_ref, gain_ref)
        for span in spans(doc, ROW_BLOCK):
            normed_t[:, span] = flip(normed_ref[span])
            cotangent_t[:, span] = flip(cotangent_ref[span])

    for p, pair in enumerate(copies):

        @pl.when(step == p * half)
        def _(pair=pair):
            for copy in pair:
                copy.wait()

    units = pl.ds(pl.multiple_of(step * HIDDEN_BLOCK, HIDDEN_BLOCK), HIDDEN_BLOCK)
    activated, slope = gelu_and_slope(dot_nn(wide_ref[units], normed_t[...]))
    active_ref[units] = activated.astype(BF16)
    grad_ref[units] = (dot_nn(narrow_ref[units], cotangent_t[...]) * slope).astype(BF16)

    def store(ref, at):
        rows = pl.ds(pl.multiple_of(at * HIDDEN_BLOCK, HIDDEN_BLOCK), HIDDEN_BLOCK)
        ref[0, rows] = dot_nn(grad_ref[units], normed_ref[...]).astype(BF16)
        ref[1, rows] = dot_nn(active_ref[units], cotangent_ref[...]).astype(BF16)

    @pl.when(step < half)
    def _():
        store(give_ref, step)

    @pl.when(step == half - 1)
    def _():
        swap.start()

    @pl.when(step >= half)
    def _():
        store(keep_ref, step - half)

    @pl.when(step == steps - 1)
    def _():
        for copy in loads:
            copy.wait()
        if last:
            gain_grad_ref[...] = jnp.zeros_like(gain_grad_ref)
        product_ref[...] = dot_tn(active_ref[...], narrow_ref[...])
        for span in spans(doc, ROW_BLOCK):
            layer = rows_ref[span] if first else layer_in_ref[span]
            layer_ref[span] = (layer + product_ref[span]).astype(layer_ref.dtype)
        product_ref[...] = dot_tn(grad_ref[...], wide_ref[...])
        for span in spans(doc, ROW_BLOCK):
            back = product_ref[span]
            if not first:
                back = back + back_in_ref[span]
            if last:
                norm_back_into(
                    span, back, out_ref, low_ref, gain_grad_ref, rows_ref, gain_ref, cotangent_ref
                )
            else:
                out_ref[span] = back
        swap.wait_recv()
        for kind, sums_ref in enumerate(sums):
            for span in spans(hidden, HIDDEN_BLOCK):
                sums_ref[span] = low_sum(keep_ref[kind, span], came_ref[kind, span])
        swap.wait_send()


def pack_kernel(flipped, *refs):
    out_ref, start = refs[-1], 0
    for source, turn in zip(refs[:-1], flipped):
        if source.shape[-1] != out_ref.shape[1] and not turn:
            out_ref[start:] = jnp.zeros((TABLE_ROWS, out_ref.shape[1]), BF16)
            out_ref[start : start + source.shape[0], : source.shape[1]] = source[...]
            continue
        rows = source.shape[1] if turn else source.shape[0]
        span = slice(start, start + rows)
        out_ref[span] = flip(source[...]) if turn else source[...]
        start += rows


def finish_kernel(*refs):
    sources, outs, refs = refs[:4], refs[4:14], refs[14:]
    ins, wides, in_sems, out_sems = refs[:4], refs[4:14], refs[14], refs[15]
    loads, writes = [], []
    for i, (source, target) in enumerate(zip(sources, ins)):
        for j, span in enumerate(spans(target.shape[0], FINISH_BLOCK)):
            loads.append(
                pltpu.make_async_copy(source.at[span], target.at[span], in_sems.at[i, j])
            )
            loads[-1].start()

    def write(i, part):
        writes.append(
            pltpu.make_async_copy(wides[i].at[part], outs[i].at[part], out_sems.at[len(writes)])
        )
        writes[-1].start()

    waiting = iter(loads)
    hidden = wides[1].shape[0]
    for span in spans(hidden, FINISH_BLOCK):
        next(waiting).wait()
        for part in spans(FINISH_BLOCK, LANES):
            rows = slice(span.start + part.start, span.start + part.stop)
            wides[0][:, rows] = ins[0][rows].astype(F32).T
        write(0, (slice(None), span))
    for span in spans(hidden, FINISH_BLOCK):
        next(waiting).wait()
        wides[1][span] = ins[1][span].astype(F32)
        write(1, span)
    for i in (2, 3):
        for _ in spans(ins[i].shape[0], FINISH_BLOCK):
            next(waiting).wait()
        rows = wides[2].shape[0]
        for kind in range(4):
            at = 2 + 4 * (i - 2) + kind
            wides[at][...] = ins[i][kind * rows : (kind + 1) * rows].astype(F32)
            write(at, slice(None))
    for copy in writes:
        copy.wait()


def params():
    return pltpu.CompilerParams(vmem_limit_bytes=VMEM_BYTES)


def cost(flops=1 << 20):
    return pl.CostEstimate(flops=flops, bytes_accessed=1 << 16, transcendentals=0)


def shape(dims, dtype):
    return jax.ShapeDtypeStruct(dims, dtype)


def whole(array):
    return pl.BlockSpec(
        array.shape, lambda *_: (0,) * len(array.shape), pipeline_mode=pl.Buffered(1)
    )


def result(array):
    return pl.BlockSpec(array.shape, lambda *_: (0,) * len(array.shape))


def columns(rows):
    return pl.BlockSpec((rows, HEAD_BLOCK), lambda i: (0, i))


def anywhere(arrays):
    return [pl.BlockSpec(memory_space=pl.ANY) for _ in arrays]


SCALAR = pl.BlockSpec(memory_space=pltpu.SMEM)


def call(
    kernel, name, grid, in_specs, out_specs, out_shape, scratch, args, channel=None, flops=1 << 20
):
    compiler_params = params()
    if channel is not None:
        compiler_params = pltpu.CompilerParams(
            vmem_limit_bytes=VMEM_BYTES, collective_id=channel, has_side_effects=True
        )
    return pl.pallas_call(
        kernel,
        grid=grid,
        in_specs=in_specs,
        out_specs=out_specs,
        out_shape=out_shape,
        scratch_shapes=scratch,
        compiler_params=compiler_params,
        cost_estimate=cost(flops),
        name=name,
    )(*args)


def pack(*parts):
    arrays, flipped = zip(*parts)
    features = arrays[0].shape[0] if flipped[0] else arrays[0].shape[1]
    rows = [a.shape[1] if turn else a.shape[0] for a, turn in parts]
    if arrays[-1].shape[1] < features and not flipped[-1]:
        rows[-1] = TABLE_ROWS
    rows = sum(rows)
    return pl.pallas_call(
        functools.partial(pack_kernel, flipped),
        out_shape=shape((rows, features), BF16),
        compiler_params=params(),
        cost_estimate=cost(),
        name="pack",
    )(*arrays)


def self_forward(heads, buckets, rows, gain, weights, ids):
    doc, features = rows.shape
    shares, steps = len(weights), features // HEAD_BLOCK
    narrow, tall = shape((doc, features), BF16), shape((doc, features), F32)
    scores = shape((steps * BLOCK_HEADS, doc, doc), BF16)
    out_shape = (*[narrow] * 4, shape((steps, 8, doc), F32), scores, tall)
    return call(
        functools.partial(self_forward_kernel, heads, buckets, shares),
        "self_forward",
        (steps,),
        [whole(rows), whole(gain), whole(ids), *anywhere(weights)],
        (
            *[columns(doc)] * 4,
            pl.BlockSpec((1, 8, doc), lambda i: (i, 0, 0)),
            pl.BlockSpec((BLOCK_HEADS, doc, doc), lambda i: (i, 0, 0)),
            result(tall),
        ),
        out_shape,
        [
            pltpu.VMEM((4 * features, features), BF16),
            pltpu.VMEM((shares, TABLE_ROWS, features), BF16),
            pltpu.VMEM((TABLE_ROWS, LANES), F32),
            pltpu.VMEM((doc, features), BF16),
            pltpu.SemaphoreType.DMA((shares, 5)),
        ],
        (rows, gain, ids, *weights),
    )


def self_backward(heads, rows, gain, branch, add, saved, weights, hops):
    doc, features = rows.shape
    shares, steps = len(weights), features // HEAD_BLOCK
    count = shares // 2
    *arrays, lse, bias = saved
    packed = pltpu.VMEM((4, features // 2, features), BF16)
    scores = pl.BlockSpec((BLOCK_HEADS, doc, doc), lambda i: (i, 0, 0))
    out_shape = (
        *[shape(h.shape, BF16) for h in hops],
        *[shape((4 * heads * HEAD_DIM, features), BF16)] * count,
        shape((steps * BLOCK_HEADS, doc, doc), BF16),
        shape((doc, features), F32),
        shape((8, features), F32),
    )
    return call(
        functools.partial(self_backward_kernel, heads, shares),
        "self_backward",
        (steps,),
        [
            *[whole(a) for a in (rows, gain, branch, add, *arrays)],
            pl.BlockSpec((1, 8, doc), lambda i: (i, 0, 0)),
            scores,
            *anywhere(weights),
            *anywhere(hops),
        ],
        (
            *anywhere(hops),
            *[result(o) for o in out_shape[len(hops) : len(hops) + count]],
            scores,
            result(out_shape[-2]),
            result(out_shape[-1]),
        ),
        out_shape,
        [
            pltpu.VMEM((4 * features, features), BF16),
            pltpu.VMEM((doc, features), BF16),
            pltpu.VMEM((doc, HEAD_BLOCK), BF16),
            pltpu.VMEM((doc, 3 * features), BF16),
            pltpu.VMEM((doc, features), F32),
            packed,
            packed,
            packed,
            pltpu.SemaphoreType.DMA((shares, 4)),
            pltpu.SemaphoreType.DMA((2,)),
            pltpu.SemaphoreType.DMA((2,)),
        ],
        (rows, gain, branch, add, *arrays, lse, bias, *weights, *hops),
        channel=4,
    )


def cross_forward(heads, rows, gain, memory, length, weights):
    (doc, features), slots = rows.shape, memory.shape[0]
    shares, steps = len(weights), features // HEAD_BLOCK
    query, key = shape((doc, features), BF16), shape((slots, features), BF16)
    tall = shape((doc, features), F32)
    return call(
        functools.partial(cross_forward_kernel, heads, shares),
        "cross_forward",
        (steps,),
        [SCALAR, whole(rows), whole(gain), whole(memory), *anywhere(weights)],
        (
            columns(doc),
            columns(slots),
            columns(slots),
            columns(doc),
            pl.BlockSpec((1, 8, doc), lambda i: (i, 0, 0)),
            result(tall),
        ),
        (query, key, key, query, shape((steps, 8, doc), F32), tall),
        [
            pltpu.VMEM((4 * features, features), BF16),
            pltpu.VMEM((doc, features), BF16),
            pltpu.VMEM((slots, LANES), BF16),
            pltpu.VMEM((2, slots, Q_BLOCK), BF16),
            pltpu.VMEM((LANES, Q_BLOCK), F32),
            pltpu.SemaphoreType.DMA((shares, 4)),
        ],
        (length, rows, gain, memory, *weights),
    )


def cross_backward(
    heads, size, rows, gain, memory, length, branch, add, saved, weights, scattered, hops
):
    (doc, features), slots = rows.shape, memory.shape[0]
    shares, blocks = len(weights), features // HEAD_BLOCK
    count = shares // 2
    blocks_out, ring_scratch = [], []
    if scattered:
        number, part = len(scattered), scattered[0].shape
        block = (2, part[0] // (2 * size), features)
        blocks_out = [shape(block, BF16)]
        steps = pltpu.SemaphoreType.DMA((2, size - 1))
        ring_scratch = [
            pltpu.VMEM((number, *part), BF16),
            pltpu.VMEM((2, size - 1, number, *block[1:]), BF16),
            pltpu.VMEM((2, number, *block[1:]), BF16),
            pltpu.VMEM(block, BF16),
            steps,
            steps,
            pltpu.SemaphoreType.DMA((number,)),
            pltpu.SemaphoreType.DMA((2,)),
        ]
    out_shape = (
        *[shape(h.shape, BF16) for h in hops],
        *blocks_out,
        *[shape((4 * heads * HEAD_DIM, features), BF16)] * count,
        shape((slots, features), BF16),
        shape((doc, features), F32),
        shape((doc, features), BF16),
        shape((8, features), F32),
    )
    query, key, value, mixed, lse = saved
    near = (gain, branch, query, mixed, lse)
    far = (rows, memory, add, key, value, *weights, *scattered, *hops)
    vmem, hbm = pl.BlockSpec(memory_space=pltpu.VMEM), pl.BlockSpec(memory_space=pl.ANY)
    packed = pltpu.VMEM((4, features // 2, features), BF16)
    key_block = pltpu.VMEM((blocks, slots, HEAD_BLOCK), BF16)
    return call(
        functools.partial(
            cross_backward_kernel, heads, shares, size, len(scattered), len(hops)
        ),
        "cross_backward",
        (),
        [SCALAR, *[vmem for _ in near], *[hbm for _ in far]],
        (
            *[hbm] * len(hops),
            *[vmem] * len(blocks_out),
            *[vmem] * count,
            hbm,
            vmem,
            vmem,
            vmem,
        ),
        out_shape,
        [
            pltpu.VMEM((doc, features), F32),
            pltpu.VMEM((slots, features), BF16),
            pltpu.VMEM((doc, features), F32),
            key_block,
            key_block,
            pltpu.VMEM((4 * features, features), BF16),
            pltpu.VMEM((doc, features), BF16),
            pltpu.VMEM((slots, LANES), BF16),
            pltpu.VMEM((doc, HEAD_BLOCK), BF16),
            pltpu.VMEM((doc, features), BF16),
            pltpu.VMEM((slots, 2 * features), BF16),
            pltpu.VMEM((2, slots, doc), BF16),
            packed,
            packed,
            packed,
            pltpu.VMEM((slots, features), BF16),
            pltpu.VMEM((doc, features), F32),
            pltpu.SemaphoreType.DMA((shares, 4)),
            pltpu.SemaphoreType.DMA((3,)),
            pltpu.SemaphoreType.DMA((2, blocks)),
            pltpu.SemaphoreType.DMA((slots // MEMORY_BLOCK,)),
            pltpu.SemaphoreType.DMA((2,)),
            pltpu.SemaphoreType.DMA((max(len(hops), 1), 2)),
            *ring_scratch,
        ],
        (length, *near, *far),
        channel=1,
    )


def feed_forward(rows, gain, cotangent, weights, before, last):
    (doc, features), shares = rows.shape, len(weights)
    share = weights[0].shape[0] // 2
    hidden = share * shares
    steps = hidden // HIDDEN_BLOCK
    summed, tall = shape((share, features), BF16), shape((doc, features), F32)
    low = shape((doc, features), BF16)
    rest = [low, tall, low, shape((8, features), F32)] if last else [tall, tall]
    kept, added = pltpu.VMEM((2, share, features), BF16), pltpu.VMEM(tall.shape, F32)
    return call(
        functools.partial(feed_forward_kernel, not before, last),
        "feed_forward",
        (steps,),
        [whole(rows), whole(gain), whole(cotangent), *anywhere(weights), *anywhere(before)],
        (result(summed), result(summed), *[result(o) for o in rest]),
        (summed, summed, *rest),
        [
            pltpu.VMEM((hidden, features), BF16),
            pltpu.VMEM((hidden, features), BF16),
            pltpu.VMEM((doc, features), BF16),
            pltpu.VMEM((features, doc), BF16),
            pltpu.VMEM((features, doc), BF16),
            pltpu.VMEM((hidden, doc), BF16),
            pltpu.VMEM((hidden, doc), BF16),
            kept,
            kept,
            kept,
            added,
            added,
            added,
            pltpu.SemaphoreType.DMA((shares, 2)),
            pltpu.SemaphoreType.DMA((2,)),
            pltpu.SemaphoreType.DMA((2,)),
        ],
        (rows, gain, cotangent, *weights, *before),
        channel=3 if before else 2,
    )


def finish(sum_wide, sum_narrow, sum_cross, sum_self):
    rows, features = sum_self.shape
    hidden, part = sum_wide.shape[0], shape((rows // 4, features), F32)
    out_shape = [shape((features, hidden), F32), shape((hidden, features), F32), *[part] * 8]
    sources = (sum_wide, sum_narrow, sum_cross, sum_self)
    writes = 2 * hidden // FINISH_BLOCK + 8
    wide, narrow, *parts = pl.pallas_call(
        finish_kernel,
        in_specs=anywhere(sources),
        out_specs=anywhere(out_shape),
        out_shape=out_shape,
        scratch_shapes=[
            *[pltpu.VMEM(source.shape, BF16) for source in sources],
            *[pltpu.VMEM(out.shape, F32) for out in out_shape],
            pltpu.SemaphoreType.DMA((4, hidden // FINISH_BLOCK)),
            pltpu.SemaphoreType.DMA((writes,)),
        ],
        compiler_params=params(),
        cost_estimate=cost(),
        name="finish",
    )(*sources)
    return wide, narrow, parts[4:], parts[:4]


def share_place(row, other, peers):
    j, bit = 0, 1
    while bit < peers:
        j = j + bit * ((row // bit + other // bit) % 2)
        bit *= 2
    return (j % 2) * (j // 2) + (1 - j % 2) * (peers // 2 + j // 2)


def tail_kernel(size, peers, buckets, heads, gathered, counts, *refs):
    parts = []
    for count in counts:
        parts.append(refs[:count])
        refs = refs[count:]
    arrays, shares = len(counts) + 1, peers // 2
    last_refs, refs = refs[:shares], refs[shares:]
    ids_ref, ds_ref, *gain_refs = refs[:5]
    outs, small_out_ref, refs = refs[5 : 5 + arrays], refs[5 + arrays], refs[6 + arrays :]
    slots, refs = refs[:arrays], refs[arrays:]
    firsts, refs = refs[:arrays], refs[arrays:]
    far_came_ref, part_ref, scores_ref, bucket_ref = refs[:4]
    small_ref, near_ref, far_ref = refs[4:7]
    send, came, send_out, came_out, small_sems, hop_sems, local_sems = refs[7:]
    parts.append((part_ref,))
    me, row = lax.axis_index("dp"), lax.axis_index("mp")
    ways = ring_ways(size)
    doc = ids_ref.shape[0]
    mesh = pl.DeviceIdType.MESH

    load_scores = pltpu.make_async_copy(ds_ref, scores_ref, local_sems.at[0])
    load_scores.start()

    barrier = pltpu.get_barrier_semaphore()

    def greet(t, carry):
        pl.semaphore_signal(
            barrier, inc=1, device_id=((me + t) % size, row), device_id_type=mesh
        )
        return carry

    lax.fori_loop(1, size, greet, 0)
    for t in range(1, peers):
        pl.semaphore_signal(
            barrier, inc=1, device_id=(me, (row + t) % peers), device_id_type=mesh
        )
    pl.semaphore_wait(barrier, size - 1 + peers - 1)

    def block(i, way, number):
        rows = outs[i].shape[0] // (2 * size)
        return pl.ds(pl.multiple_of((way * size + number) * rows, 16), rows)

    def part(i, span):
        total = parts[i][0][span].astype(F32)
        for ref in parts[i][1:]:
            total = total + ref[span].astype(F32)
        return total

    def first_copy(i, way):
        return remote(
            firsts[i].at[way],
            slots[i].at[way, 0],
            send.at[i, way, 0],
            came.at[i, way, 0],
            (ways[way][1], row),
        )

    def next_copy(i, way, step):
        return remote(
            slots[i].at[way, step - 1],
            slots[i].at[way, step],
            send.at[i, way, step],
            came.at[i, way, step],
            (ways[way][1], row),
        )

    def wait_came(i, way, step):
        remote(
            slots[i].at[way, step],
            slots[i].at[way, step],
            send.at[i, way, step],
            came.at[i, way, step],
            (ways[way][1], row),
        ).wait_recv()

    def out_copy(i, way, step):
        span = block(i, way, (ways[way][0] + 1 - step + size) % size)
        return remote(
            outs[i].at[span],
            outs[i].at[span],
            send_out.at[i, way, step],
            came_out.at[i, way, step],
            (ways[way][1], row),
        )

    def begin(rings):
        for i, way in rings:
            firsts[i][way] = part(i, block(i, way, ways[way][0])).astype(BF16)
            first_copy(i, way).start()

    def plus_part(i, way, step):
        span = block(i, way, (ways[way][0] - step - 1 + size) % size)
        total = slots[i][way, step].astype(F32) + part(i, span)
        return span, total.astype(BF16)

    def advance(rings, step):
        for i, way in rings:
            wait_came(i, way, step - 1)
            slots[i][way, step - 1] = plus_part(i, way, step - 1)[1]
            next_copy(i, way, step).start()

    def turn(rings):
        for i, way in rings:
            wait_came(i, way, size - 2)
            span, total = plus_part(i, way, size - 2)
            outs[i][span] = total
            out_copy(i, way, 0).start()

    def pass_on(rings, step):
        for i, way in rings:
            out_copy(i, way, step - 1).wait_recv()
            out_copy(i, way, step).start()

    ready = [(i, way) for i in range(gathered) for way in range(2)]
    early = [(i, way) for i in range(gathered, arrays - 1) for way in range(2)]
    late = [(arrays - 1, way) for way in range(2)]

    other_chip = None
    if shares == 2:
        other_chip = to_differing(2, last_refs[1], far_came_ref, hop_sems)
        other_chip.start()
    begin(early)
    for i, way in ready:
        outs[i][block(i, way, (ways[way][0] + 1) % size)] = parts[i][0][way]
        out_copy(i, way, 0).start()

    rows_used, per_row = bucket_ref.shape[0], ds_ref.shape[0] // bucket_ref.shape[0]
    per_line = buckets // UNIT_BUCKETS
    units = rows_used * per_line
    per_round = -(-units // max(2 * (size - 2), 1))

    def bucket_unit(u, carry):
        r, first = u // per_line, u % per_line * UNIT_BUCKETS
        sums = [[jnp.zeros((8, LANES), F32)] * UNIT_BUCKETS for _ in range(per_row)]
        for c in range(0, doc, LANES):
            lanes = slice(c, c + LANES)
            for rows in spans(c + LANES, UNIT_ROWS):
                found = ids_ref[rows, lanes] - first
                hits = [found == b for b in range(UNIT_BUCKETS)]
                for h in range(per_row):
                    grads = scores_ref[r * per_row + h, rows, lanes].astype(F32)
                    for b, hit in enumerate(hits):
                        kept = jnp.where(hit, grads, 0.0).reshape(-1, 8, LANES)
                        sums[h][b] = sums[h][b] + jnp.sum(kept, axis=0)
        for h in range(per_row):
            for b in range(UNIT_BUCKETS):
                bucket_ref[r, h, pl.ds(first + b, 1), :] = jnp.sum(
                    sums[h][b], axis=0, keepdims=True
                )
        return carry

    def bucket_round(k):
        low = jnp.minimum(k * per_round, units)
        lax.fori_loop(low, jnp.minimum(low + per_round, units), bucket_unit, 0)

    bucket_ref[...] = jnp.zeros_like(bucket_ref)
    part_ref[...] = jnp.zeros_like(part_ref)
    load_scores.wait()

    def early_step(step, carry):
        advance(early, step)
        pass_on(ready, step)
        bucket_round(step - 1)
        return carry

    begin_late = LATE_STEP if size - 1 > LATE_STEP else size - 1
    lax.fori_loop(1, min(begin_late + 1, size - 1), early_step, 0)
    if begin_late == size - 1:
        turn(early)
    used = slice(0, last_refs[0].shape[0])
    if other_chip is None:
        part_ref[used] = last_refs[0][...]
    else:
        other_chip.wait_recv()
        part_ref[used] = low_sum(last_refs[0][...], far_came_ref[...])
    begin(late)

    def both_step(step, carry):
        early_step(step, carry)
        advance(late, step - begin_late)
        return carry

    def middle_step(step, carry):
        pass_on(early, step)
        advance(late, step + size - 1 - begin_late)
        bucket_round(size - 2 + step - 1)
        return carry

    def end_step(step, carry):
        pass_on(early, step)
        pass_on(late, step - begin_late)
        bucket_round(size - 2 + step - 1)
        return carry

    late_passed = 0
    if begin_late < size - 1:
        lax.fori_loop(begin_late + 1, size - 1, both_step, 0)
        turn(early)
        advance(late, size - 1 - begin_late)
        lax.fori_loop(1, begin_late, middle_step, 0)
        pass_on(early, begin_late)
        turn(late)
        bucket_round(size - 2 + begin_late - 1)
        lax.fori_loop(begin_late + 1, size - 1, end_step, 0)
        late_passed = size - 2 - begin_late
    else:
        lax.fori_loop(1, size - 1, middle_step, 0)
        turn(late)
    if size == 2:
        lax.fori_loop(0, units, bucket_unit, 0)

    features = gain_refs[0].shape[1]
    per_gain = features // LANES
    gain_rows = len(gain_refs) * per_gain
    small_ref[...] = jnp.zeros_like(small_ref)
    for i, ref in enumerate(gain_refs):
        total = jnp.sum(ref[...], axis=0, keepdims=True)
        for c in range(per_gain):
            at = i * per_gain + c
            small_ref[at : at + 1, :] = total[:, c * LANES : (c + 1) * LANES]
    for r in range(rows_used):
        block_sums = bucket_ref[r].reshape(LANES, LANES).T
        at = gain_rows + r
        small_ref[at : at + 1, :] = jnp.sum(block_sums, axis=0, keepdims=True)

    def near_copy(t):
        return remote(
            small_ref,
            near_ref.at[row],
            small_sems.at[0, t],
            small_sems.at[1, t],
            (me, (row + t) % peers),
        )

    def far_copy(t):
        return remote(
            far_ref.at[me],
            far_ref.at[me],
            small_sems.at[2, t],
            small_sems.at[3, t],
            ((me + t) % size, row),
        )

    for t in range(1, peers):
        near_copy(t).start()
    near_ref[pl.ds(row, 1)] = small_ref[...][None]
    for t in range(1, peers):
        near_copy(t).wait_recv()
    own = rows_used // peers
    total, sums = None, None
    for k in range(peers):
        gains = near_ref[k, :gain_rows]
        mine = near_ref[k, pl.ds(gain_rows + own * share_place(row, k, peers), own)]
        total = gains if total is None else total + gains
        sums = mine if sums is None else sums + mine
    small_ref_rows = far_ref.shape[1]
    far_ref[pl.ds(me, 1)] = jnp.concatenate(
        [total, sums, jnp.zeros((small_ref_rows - gain_rows - own, LANES), F32)], axis=0
    )[None]

    def far_start(t, carry):
        far_copy(t).start()
        return carry

    lax.fori_loop(1, size, far_start, 0)

    def late_step(step, carry):
        pass_on(late, step)
        return carry

    lax.fori_loop(1 + late_passed, size - 1, late_step, 0)

    def far_wait(t, carry):
        far_copy(t).wait()
        return carry

    lax.fori_loop(1, size, far_wait, 0)

    def far_add(k, total):
        return total + far_ref[k]

    small_out_ref[...] = lax.fori_loop(1, size, far_add, far_ref[0])
    for i, way in ready + early + late:
        out_copy(i, way, size - 2).wait_recv()

    for t in range(1, peers):
        near_copy(t).wait_send()
    if other_chip is not None:
        other_chip.wait_send()
    for i, way in early + late:
        first_copy(i, way).wait_send()

    def sent(step, carry):
        for i, way in early + late:
            next_copy(i, way, step).wait_send()
        return carry

    lax.fori_loop(1, size - 1, sent, 0)

    def sent_out(step, carry):
        for i, way in ready + early + late:
            out_copy(i, way, step).wait_send()
        return carry

    lax.fori_loop(0, size - 1, sent_out, 0)


def tail_sums(size, peers, buckets, heads, blocks, terms, last, ids, ds, gains):
    assert peers in (2, 4)
    grain = 2 * 16 * size
    features = last[0].shape[1]
    rows = [size * 2 * b.shape[1] for b in blocks]
    rows += [arrays[0].shape[0] for arrays in terms]
    rows.append(last[0].shape[0])
    padded = [r + -r % grain for r in rows]
    parts = [[b] for b in blocks]
    for arrays, r, p in zip(terms, rows[len(blocks) :], padded[len(blocks) :]):
        parts.append([jnp.pad(a, ((0, p - r), (0, 0))) for a in arrays])
    flat = [a for arrays in parts for a in arrays]
    lines = peers * (-(-heads * buckets // LANES))
    small = len(gains) * features // LANES + lines
    small = shape((small + -small % 8, LANES), F32)
    vmem, hbm = pl.BlockSpec(memory_space=pltpu.VMEM), pl.BlockSpec(memory_space=pl.ANY)
    steps = pltpu.SemaphoreType.DMA((len(rows), 2, size - 1))

    def ring_slots(i, steps):
        if i < len(blocks):
            return pltpu.VMEM((2, 1, 16, LANES), BF16)
        return pltpu.VMEM((2, *steps, padded[i] // (2 * size), features), BF16)

    *sums, small = pl.pallas_call(
        functools.partial(
            tail_kernel, size, peers, buckets, heads, len(blocks), [len(a) for a in parts]
        ),
        in_specs=[
            *[vmem] * (len(flat) + 1),
            *[hbm] * (len(last) - 1),
            vmem,
            hbm,
            *[vmem] * len(gains),
        ],
        out_specs=[vmem] * (len(rows) + 1),
        out_shape=[*[shape((p, features), BF16) for p in padded], small],
        scratch_shapes=[
            *[ring_slots(i, (size - 1,)) for i in range(len(rows))],
            *[ring_slots(i, ()) for i in range(len(rows))],
            pltpu.VMEM((rows[-1], features), BF16),
            pltpu.VMEM((padded[-1], features), BF16),
            pltpu.VMEM(ds.shape, BF16),
            pltpu.VMEM((lines, LANES // buckets, buckets, LANES), F32),
            pltpu.VMEM(small.shape, F32),
            pltpu.VMEM((peers, *small.shape), F32),
            pltpu.VMEM((size, *small.shape), F32),
            steps,
            steps,
            steps,
            steps,
            pltpu.SemaphoreType.DMA((4, max(size, peers))),
            pltpu.SemaphoreType.DMA((2,)),
            pltpu.SemaphoreType.DMA((1,)),
        ],
        compiler_params=pltpu.CompilerParams(
            vmem_limit_bytes=VMEM_BYTES, collective_id=0, has_side_effects=True
        ),
        cost_estimate=cost(),
        name="tail_sums",
    )(*flat, *last, ids, ds, *gains)
    return [total[:r] for total, r in zip(sums, rows)], small


def swap(array, bit, size):
    return lax.ppermute(array, "mp", [(i, i ^ bit) for i in range(size)])


def after(array, *others):
    return lax.optimization_barrier((array, others))[0]


def shards(
    decoder_rows,
    memory_rows,
    decoder_token_length,
    memory_length,
    bucket_ids,
    relative_bucket_bias,
    self_gain,
    self_query,
    self_key,
    self_value,
    self_out,
    cross_gain,
    cross_query,
    cross_key,
    cross_value,
    cross_out,
    hidden_gain,
    widen_weight,
    narrow_weight,
    layer_cotangent,
):
    dp_size = lax.axis_size("dp")
    mp_size = lax.axis_size("mp")
    me = lax.axis_index("mp")
    doc, features = decoder_rows.shape
    slots = memory_rows.shape[0]
    cols = self_query.shape[1]
    heads = cols // HEAD_DIM
    buckets = relative_bucket_bias.shape[0]
    order = [*range(1, mp_size, 2), *range(0, mp_size, 2)]

    doc_length = lax.dynamic_index_in_dim(decoder_token_length, me, keepdims=False)
    doc_memory = lax.dynamic_index_in_dim(memory_length, me)
    position = jnp.arange(doc, dtype=jnp.int32)
    allowed = (position[:, None] <= position[None, :]) & (position[:, None] < doc_length)
    ids = jnp.where(allowed, bucket_ids.T, buckets)
    own_self = pack(
        (self_query.T, False),
        (self_key.T, False),
        (self_value.T, False),
        (self_out, False),
        (relative_bucket_bias.T, False),
    )
    own_cross = pack(
        (cross_query.T, False), (cross_key.T, False), (cross_value.T, False), (cross_out, False)
    )
    own_hidden = pack((widen_weight, True), (narrow_weight, False))

    def first_hops(own):
        shares, bit = {0: own}, mp_size // 2
        while bit > 1:
            for j in list(shares):
                shares[j | bit] = swap(shares[j], bit, mp_size)
            bit //= 2
        return shares

    def last_hop(shares, *others):
        if 1 not in shares:
            shares[1] = swap(shares[0], 1, mp_size)
        for j in range(2, mp_size, 2):
            shares[j] = after(shares[j], *others)
            shares[j | 1] = swap(shares[j], 1, mp_size)
        return shares

    near_self = first_hops(own_self)
    near_self[1] = swap(own_self, 1, mp_size)
    memory_rows = after(memory_rows, own_self)
    w_self = last_hop(near_self, own_cross, own_hidden, ids)
    w_self = [w_self[j] for j in order]
    near_cross = first_hops(own_cross)
    near_hidden = first_hops(own_hidden)
    near_hidden[1] = swap(own_hidden, 1, mp_size)
    memory_seen = lax.all_to_all(
        memory_rows.reshape(dp_size, slots // dp_size, features), "dp", 0, 0
    ).reshape(slots, features)

    gain_self = self_gain.astype(F32)[None]
    gain_cross = cross_gain.astype(F32)[None]
    gain_hidden = hidden_gain.astype(F32)[None]

    *saved_self, after_self = self_forward(heads, buckets, decoder_rows, gain_self, w_self, ids)
    w_cross = last_hop(near_cross, after_self)
    w_cross = [w_cross[j] for j in order]
    *saved_cross, after_cross = cross_forward(
        heads, after_self, gain_cross, memory_seen, doc_memory, w_cross
    )

    before, wide_sums, narrow_sums, w_hidden = (), [], [], near_hidden
    for j in range(0, mp_size, 2):
        wide_sum, narrow_sum, *before = feed_forward(
            after_cross,
            gain_hidden,
            layer_cotangent,
            [w_hidden[j + 1], w_hidden[j]],
            before,
            j == mp_size - 2,
        )
        wide_sums.append(wide_sum)
        narrow_sums.append(narrow_sum)
        if j == 0:
            w_hidden = last_hop(near_hidden, before[0])
    layer_output, grad_after_cross, branch, hidden_gain_grad = before

    scattered, hops = wide_sums, narrow_sums[1:]
    if wide_sums[0].shape[0] % (2 * 16 * dp_size):
        scattered, hops = [], wide_sums[1:] + narrow_sums[1:]
    *sums, grad_memory, grad_after_self, branch, cross_gain_grad = cross_backward(
        heads,
        dp_size,
        after_self,
        gain_cross,
        memory_seen,
        doc_memory,
        branch,
        grad_after_cross,
        saved_cross,
        w_cross,
        scattered,
        hops,
    )
    came, sums = sums[: len(hops)], sums[len(hops) :]
    if scattered:
        blocks, terms, cross_sums = sums[:1], [narrow_sums[:1] + came], sums[1:]
    else:
        blocks, cross_sums = [], sums
        hidden = [wide_sums[0], narrow_sums[0]], came
        terms = [[jnp.concatenate(both, axis=0) for both in hidden if both]]
    memory_grad = lax.all_to_all(
        grad_memory.reshape(dp_size, slots // dp_size, features), "dp", 0, 0
    ).reshape(slots, features)

    *sums, score_grads, input_grad, self_gain_grad = self_backward(
        heads,
        decoder_rows,
        gain_self,
        branch,
        grad_after_self,
        saved_self,
        w_self,
        cross_sums[1:],
    )
    cross_sums[1:], last = sums[: len(cross_sums) - 1], sums[len(cross_sums) - 1 :]
    (*hidden, sum_cross, sum_self), small = tail_sums(
        dp_size,
        mp_size,
        buckets,
        heads,
        blocks,
        terms + [cross_sums],
        last,
        ids,
        score_grads,
        (self_gain_grad, cross_gain_grad, hidden_gain_grad),
    )
    wide_grad, narrow_grad, self_grads, cross_grads = finish(
        *(hidden if scattered else jnp.split(hidden[0], 2)), sum_cross, sum_self
    )
    gain_rows = 3 * features // LANES
    gains = small[:gain_rows].reshape(3, features)
    lines = -(-heads * buckets // LANES)
    sums = small[gain_rows : gain_rows + lines, : heads // lines * buckets]
    position_grad = sums.reshape(heads, buckets).T

    return (
        layer_output,
        input_grad,
        memory_grad,
        position_grad,
        gains[0],
        *[grad.T for grad in self_grads[:3]],
        self_grads[3],
        gains[1],
        *[grad.T for grad in cross_grads[:3]],
        cross_grads[3],
        gains[2],
        wide_grad,
        narrow_grad,
    )


def solution(mesh):
    return jax.shard_map(
        shards,
        mesh=mesh,
        in_specs=(
            P(("dp", "mp"), None),
            P(("dp", "mp"), None),
            P("dp"),
            P("dp"),
            P(),
            P(None, "mp"),
            P(),
            P(None, "mp"),
            P(None, "mp"),
            P(None, "mp"),
            P("mp", None),
            P(),
            P(None, "mp"),
            P(None, "mp"),
            P(None, "mp"),
            P("mp", None),
            P(),
            P(None, "mp"),
            P("mp", None),
            P(("dp", "mp"), None),
        ),
        out_specs=(
            P(("dp", "mp"), None),
            P(("dp", "mp"), None),
            P(("dp", "mp"), None),
            P(None, "mp"),
            P(),
            P(None, "mp"),
            P(None, "mp"),
            P(None, "mp"),
            P("mp", None),
            P(),
            P(None, "mp"),
            P(None, "mp"),
            P(None, "mp"),
            P("mp", None),
            P(),
            P(None, "mp"),
            P("mp", None),
        ),
        check_vma=False,
    )
```

```python
import functools

import jax
import jax.numpy as jnp
from jax import lax
from jax.experimental import pallas as pl
from jax.experimental.pallas import tpu as pltpu
from jax.sharding import PartitionSpec as P

HEAD_DIM = 64
NORM_EPS = 1e-06
MASKED = -1e30
SCALE = HEAD_DIM**-0.5
BF16 = jnp.bfloat16
F32 = jnp.float32
LANES = 128
TABLE_ROWS = 16
TILE_ROWS = 16
LARGEST_SUM = 1e30
LATE_STEP = 4
UNIT_BUCKETS = 4
UNIT_ROWS = 64
HEAD_BLOCK = 256
BLOCK_HEADS = HEAD_BLOCK // HEAD_DIM
Q_BLOCK = 256
K_BLOCK = 256
HIDDEN_BLOCK = 256
MEMORY_BLOCK = 768
FINISH_BLOCK = 384
ROW_BLOCK = 128
VMEM_BYTES = 56 * 1024 * 1024
GELU_ROOT = 0.7978845608028654
GELU_CUBE = 0.044715


def dot_nn(a, b):
    return lax.dot_general(a, b, (((1,), (0,)), ((), ())), preferred_element_type=F32)


def dot_nt(a, b):
    return lax.dot_general(a, b, (((1,), (1,)), ((), ())), preferred_element_type=F32)


def dot_tn(a, b):
    return lax.dot_general(a, b, (((0,), (0,)), ((), ())), preferred_element_type=F32)


def flip(a):
    return a.astype(F32).T.astype(BF16)


def spans(size, step):
    return [slice(i, i + step) for i in range(0, size, step)]


def norm_scale(rows):
    return lax.rsqrt(jnp.mean(rows * rows, axis=-1, keepdims=True) + NORM_EPS)


def norm_into(normed_ref, rows_ref, gain_ref):
    for span in spans(rows_ref.shape[0], ROW_BLOCK):
        rows = rows_ref[span].astype(F32)
        normed_ref[span] = (rows * norm_scale(rows) * gain_ref[...]).astype(BF16)


def norm_back_into(span, grad, out_ref, low_ref, gain_grad_ref, rows_ref, gain_ref, add_ref):
    rows = rows_ref[span].astype(F32)
    scale = norm_scale(rows)
    unit = rows * scale
    grad_unit = grad * gain_ref[...]
    mean = jnp.mean(grad_unit * unit, axis=-1, keepdims=True)
    out = add_ref[span].astype(F32) + scale * (grad_unit - unit * mean)
    out_ref[span] = out
    if low_ref is not None:
        low_ref[span] = out.astype(BF16)
    gain_grad_ref[...] += jnp.sum((grad * unit).reshape(-1, 8, rows.shape[1]), axis=0)


def gelu_and_slope(v):
    square = v * v
    bend = jnp.tanh(GELU_ROOT * (v + GELU_CUBE * v * square))
    half = 0.5 * (1.0 + bend)
    slope = half + 0.5 * v * (1.0 - bend * bend) * GELU_ROOT * (1.0 + 3.0 * GELU_CUBE * square)
    return v * half, slope


def lane_block(start):
    return pl.ds(pl.multiple_of(start, LANES), LANES)


def extra_lanes(rows, allowed):
    lane = lax.broadcasted_iota(jnp.int32, (rows, LANES), 1) % HEAD_DIM
    first = MASKED if allowed is None else jnp.where(allowed, 0.0, MASKED)
    return jnp.where(lane == 0, first, jnp.where(lane < 4, 1.0, 0.0)).astype(BF16)


def pick(which, block, other):
    lane = lax.broadcasted_iota(jnp.int32, block.shape, 1)
    return jnp.where((lane < HEAD_DIM) == (which == 0), block, other)


def half_rows(which):
    return slice(which * HEAD_DIM, (which + 1) * HEAD_DIM)


def split(values):
    high = values.astype(BF16).astype(F32)
    rest = values - high
    middle = rest.astype(BF16).astype(F32)
    return high, middle, rest - middle


def with_extra(which, block_t, masked, minus):
    columns = block_t.shape[1]
    row = lax.broadcasted_iota(jnp.int32, (HEAD_DIM, columns), 0)
    extra = jnp.where(row == 0, 1.0 if masked else 0.0, 0.0)
    if minus is not None:
        for i, part in enumerate(split(minus)):
            extra = jnp.where(row == i + 1, -part, extra)
    own = block_t[half_rows(which)]
    return jnp.concatenate([own, extra] if which == 0 else [extra, own], axis=0).astype(BF16)


def bias_block(table_ref, ids_ref, index, rows, start):
    row = jnp.broadcast_to(table_ref[pl.ds(index, 1), :], (rows, LANES))
    return jnp.concatenate(
        [
            jnp.take_along_axis(row, ids_ref[:rows, c : c + LANES], axis=1)
            for c in range(start, start + Q_BLOCK, LANES)
        ],
        axis=1,
    )


def ring_place(me, size):
    return jnp.where(me % 2 == 0, me // 2, size - 1 - me // 2)


def ring_device(place, size):
    return jnp.where(place < size // 2, 2 * place, 2 * (size - 1 - place) + 1)


def ring_ways(size):
    me = lax.axis_index("dp")
    place = ring_place(me, size)
    return (
        (place, ring_device((place + 1) % size, size)),
        (size - 1 - place, ring_device((place + size - 1) % size, size)),
    )


def differing(row, bit):
    return row + bit - 2 * bit * ((row // bit) % 2)


def remote(source, target, send_sem, recv_sem, device):
    return pltpu.make_async_remote_copy(
        src_ref=source,
        dst_ref=target,
        send_sem=send_sem,
        recv_sem=recv_sem,
        device_id=device,
        device_id_type=pl.DeviceIdType.MESH,
    )


def greet(bits, devices=()):
    me, row = lax.axis_index("dp"), lax.axis_index("mp")
    barrier = pltpu.get_barrier_semaphore()
    others = [(me, differing(row, bit)) for bit in bits] + [(device, row) for device in devices]
    for other in others:
        pl.semaphore_signal(
            barrier, inc=1, device_id=other, device_id_type=pl.DeviceIdType.MESH
        )
    pl.semaphore_wait(barrier, len(others))


def to_differing(bit, source, target, sems):
    me, row = lax.axis_index("dp"), lax.axis_index("mp")
    return remote(source, target, sems.at[0], sems.at[1], (me, differing(row, bit)))


class Scatter:
    def __init__(self, size, part, slots, done, send, came):
        self.size, self.part, self.slots, self.done = size, part, slots, done
        self.send, self.came = send, came
        self.ways, self.row = ring_ways(size), lax.axis_index("mp")

    def span(self, way, number):
        rows = self.slots.shape[3]
        return pl.ds(pl.multiple_of((way * self.size + number) * rows, 16), rows)

    def copy(self, way, step, source):
        return remote(
            source,
            self.slots.at[way, step],
            self.send.at[way, step],
            self.came.at[way, step],
            (self.ways[way][1], self.row),
        )

    def first(self, way):
        return self.copy(way, 0, self.part.at[:, self.span(way, self.ways[way][0])])

    def next(self, way, step):
        return self.copy(way, step, self.slots.at[way, step - 1])

    def begin(self):
        for way in range(2):
            self.first(way).start()

    def total(self, way, step):
        self.copy(way, step, self.slots.at[way, step]).wait_recv()
        span = self.span(way, (self.ways[way][0] - step - 1 + self.size) % self.size)
        return low_sum(self.slots[way, step], self.part[:, span])

    def advance(self, step):
        for way in range(2):
            self.slots[way, step - 1] = self.total(way, step - 1)
            self.next(way, step).start()

    def turn(self):
        for way in range(2):
            self.done[way] = self.total(way, self.size - 2)

    def wait_sent(self):
        for way in range(2):
            self.first(way).wait_send()

        def sent(step, carry):
            for way in range(2):
                self.next(way, step).wait_send()
            return carry

        lax.fori_loop(1, self.size - 1, sent, 0)


def low_sum(a, b):
    return (a.astype(F32) + b.astype(F32)).astype(BF16)


class Stack:
    def __init__(self, sources, stack_ref, sems, kinds, rows):
        features = stack_ref.shape[0] // kinds
        self.copies = [
            [
                pltpu.make_async_copy(
                    source.at[pl.ds(kind * rows, rows)],
                    stack_ref.at[pl.ds(kind * features + p * rows, rows)],
                    sems.at[p, kind],
                )
                for p, source in enumerate(sources)
            ]
            for kind in range(kinds)
        ]

    def start(self):
        for copies in self.copies:
            for copy in copies:
                copy.start()

    def wait(self, *kinds):
        for kind in kinds:
            for copy in self.copies[kind]:
                copy.wait()


def table_copies(sources, tables_ref, sems, kinds):
    start = sources[0].shape[0] - TABLE_ROWS
    return [
        pltpu.make_async_copy(
            source.at[pl.ds(start, TABLE_ROWS)], tables_ref.at[p], sems.at[p, kinds]
        )
        for p, source in enumerate(sources)
    ]


def table_into(table_ref, tables_ref, heads, buckets):
    for p in range(tables_ref.shape[0]):
        rows = tables_ref[p, :, :LANES].astype(F32)
        lane = lax.broadcasted_iota(jnp.int32, rows.shape, 1)
        rows = jnp.where(lane < buckets, rows, MASKED)
        for h in range(heads):
            table_ref[p * heads + h : p * heads + h + 1, :] = rows[h : h + 1, :]


def self_forward_kernel(heads, buckets, shares, rows_ref, gain_ref, ids_ref, *refs):
    sources = refs[:shares]
    q_ref, k_ref, v_ref, mixed_ref, lse_ref, bias_ref, out_ref = refs[shares : shares + 7]
    w_ref, tables_ref, table_ref, normed_ref, sems = refs[shares + 7 :]
    step = pl.program_id(0)
    doc, features = rows_ref.shape
    stack = Stack(sources, w_ref, sems, 4, heads * HEAD_DIM)

    @pl.when(step == 0)
    def _():
        stack.start()
        tables = table_copies(sources, tables_ref, sems, 4)
        for copy in tables:
            copy.start()
        norm_into(normed_ref, rows_ref, gain_ref)
        out_ref[...] = rows_ref[...].astype(F32)
        for copy in tables:
            copy.wait()
        table_into(table_ref, tables_ref, heads, buckets)
        stack.wait(0, 1, 2, 3)

    def weights(kind):
        start = pl.multiple_of(kind * features + step * HEAD_BLOCK, HEAD_BLOCK)
        return w_ref[pl.ds(start, HEAD_BLOCK)]

    for kind, ref in enumerate((q_ref, k_ref, v_ref)):
        ref[...] = dot_nt(normed_ref[...], weights(kind)).astype(BF16)
    none = jnp.zeros((doc, LANES), BF16)
    for pair in range(BLOCK_HEADS // 2):
        lanes = slice(pair * LANES, (pair + 1) * LANES)
        k, v_t = k_ref[:, lanes], flip(v_ref[:, lanes])
        q_t = flip(q_ref[:, lanes].astype(F32) * SCALE)
        k_of = [pick(which, k, none) for which in range(2)]
        for span in spans(doc, Q_BLOCK):
            rows, mixed = span.stop, []
            for which in range(2):
                h = 2 * pair + which
                bias = bias_block(table_ref, ids_ref, step * BLOCK_HEADS + h, rows, span.start)
                bias_ref[h, :rows, span] = bias.astype(BF16)
                s = dot_nn(k_of[which][:rows], q_t[:, span]) + bias
                top = jnp.max(s, axis=0, keepdims=True)
                p = jnp.exp(s - top)
                total = jnp.sum(p, axis=0, keepdims=True)
                mixed.append(dot_nn(v_t[half_rows(which), :rows], p.astype(BF16)) / total)
                lse_ref[0, h : h + 1, span] = top + jnp.log(total)
            mixed_ref[span, lanes] = jnp.concatenate(mixed, axis=0).T.astype(BF16)
    out_ref[...] += dot_nn(mixed_ref[...], weights(3))


def self_backward_kernel(heads, shares, *refs):
    count = shares // 2
    rows_ref, gain_ref, branch_ref, add_ref = refs[:4]
    q_ref, k_ref, v_ref, mixed_ref, lse_ref, bias_ref = refs[4:10]
    sources, refs = refs[10 : 10 + shares], refs[10 + shares :]
    hop_in, hop_out, refs = refs[: count - 1], refs[count - 1 : 2 * count - 2], refs[2 * count - 2 :]
    sums, refs = refs[:count], refs[count:]
    ds_ref, out_ref, gain_grad_ref = refs[:3]
    w_ref, normed_ref, g_ref, grad_ref, back_ref, give_ref, keep_ref, came_ref = refs[3:11]
    sems, swap_sems, hop_sems = refs[11:]
    step = pl.program_id(0)
    doc, features = rows_ref.shape
    half = features // 2
    stack = Stack(sources, w_ref, sems, 4, heads * HEAD_DIM)
    swap = to_differing(1, give_ref, came_ref, swap_sems)
    hops = [
        to_differing(2, source, target, hop_sems) for source, target in zip(hop_in, hop_out)
    ]

    @pl.when(step == 0)
    def _():
        stack.start()
        greet([1, 2][:count])
        for hop in hops:
            hop.start()
        norm_into(normed_ref, rows_ref, gain_ref)
        stack.wait(3)

    start = pl.multiple_of(3 * features + step * HEAD_BLOCK, HEAD_BLOCK)
    g_ref[...] = dot_nt(branch_ref[...], w_ref[pl.ds(start, HEAD_BLOCK)]).astype(BF16)
    none = jnp.zeros((doc, LANES), BF16)
    ones = extra_lanes(doc, None)
    for pair in range(BLOCK_HEADS // 2):
        lanes = lane_block(step * HEAD_BLOCK + pair * LANES)
        q, k, v = q_ref[:, lanes], k_ref[:, lanes], v_ref[:, lanes]
        g = g_ref[:, pair * LANES : (pair + 1) * LANES]
        q_t, k_t = q.astype(F32).T * SCALE, flip(k)
        g_t = g.astype(F32).T
        inner = g_t * mixed_ref[:, lanes].astype(F32).T
        per_head = []
        for which in range(2):
            h = 2 * pair + which
            minus = jnp.sum(inner[half_rows(which)], axis=0, keepdims=True)
            per_head.append(
                (
                    pick(which, k, ones),
                    pick(which, v, ones),
                    with_extra(which, q_t, False, lse_ref[0, h : h + 1, :]),
                    with_extra(which, g_t, False, minus),
                    pick(which, q, none),
                    pick(which, g, none),
                )
            )
        grad_k = grad_v = None
        for span in spans(doc, Q_BLOCK):
            rows, grad_q, part_k, part_v = span.stop, [], None, None
            for which, (k_of, v_of, q_with, g_with, q_of, g_of) in enumerate(per_head):
                h = 2 * pair + which
                s = dot_nn(k_of[:rows], q_with[:, span])
                p = jnp.exp(s + bias_ref[h, :rows, span].astype(F32))
                ds = (p * dot_nn(v_of[:rows], g_with[:, span])).astype(BF16)
                ds_ref[h, :rows, span] = ds
                grad_q.append(dot_nn(k_t[half_rows(which), :rows], ds))
                to_v = dot_nn(p.astype(BF16), g_of[span])
                to_k = dot_nn(ds, q_of[span])
                part_v = to_v if part_v is None else part_v + to_v
                part_k = to_k if part_k is None else part_k + to_k
            grad_q = (jnp.concatenate(grad_q, axis=0) * SCALE).T
            grad_ref[span, lanes] = grad_q.astype(BF16)
            if grad_v is not None:
                part_v = jnp.concatenate(
                    [part_v[: span.start] + grad_v, part_v[span.start :]], axis=0
                )
                part_k = jnp.concatenate(
                    [part_k[: span.start] + grad_k, part_k[span.start :]], axis=0
                )
            grad_v, grad_k = part_v, part_k
        k_lanes = lane_block(features + step * HEAD_BLOCK + pair * LANES)
        v_lanes = lane_block(2 * features + step * HEAD_BLOCK + pair * LANES)
        grad_ref[:, k_lanes] = (grad_k * SCALE).astype(BF16)
        grad_ref[:, v_lanes] = grad_v.astype(BF16)

    @pl.when(step == pl.num_programs(0) - 1)
    def _():
        stack.wait(0, 1, 2)
        def weight_grads(ref, columns):
            for kind in range(3):
                kind_columns = slice(kind * features + columns.start, kind * features + columns.stop)
                ref[kind] = dot_tn(grad_ref[:, kind_columns], normed_ref[...]).astype(BF16)
            ref[3] = dot_tn(mixed_ref[:, columns], branch_ref[...]).astype(BF16)

        weight_grads(give_ref, slice(0, half))
        swap.start()
        weight_grads(keep_ref, slice(half, features))
        gain_grad_ref[...] = jnp.zeros_like(gain_grad_ref)
        back_ref[...] = dot_nn(grad_ref[...], w_ref[: 3 * features])
        for span in spans(doc, ROW_BLOCK):
            norm_back_into(
                span, back_ref[span], out_ref, None, gain_grad_ref, rows_ref, gain_ref, add_ref
            )
        swap.wait_recv()
        rows = half // count
        for share, sums_ref in enumerate(sums):
            for kind in range(4):
                span = slice(share * rows, (share + 1) * rows)
                to = slice(kind * rows, (kind + 1) * rows)
                sums_ref[to] = low_sum(keep_ref[kind, span], came_ref[kind, span])
        swap.wait_send()
        for hop in hops:
            hop.wait()


def cross_forward_kernel(heads, shares, length_ref, rows_ref, gain_ref, memory_ref, *refs):
    sources = refs[:shares]
    q_ref, k_ref, v_ref, mixed_ref, lse_ref, out_ref = refs[shares : shares + 6]
    w_ref, normed_ref, extra_ref, p_ref, mix_ref, sems = refs[shares + 6 :]
    step = pl.program_id(0)
    (doc, features), slots = rows_ref.shape, memory_ref.shape[0]
    stack = Stack(sources, w_ref, sems, 4, heads * HEAD_DIM)

    @pl.when(step == 0)
    def _():
        stack.start()
        norm_into(normed_ref, rows_ref, gain_ref)
        out_ref[...] = rows_ref[...]
        slot = lax.broadcasted_iota(jnp.int32, (slots, LANES), 0)
        extra_ref[...] = extra_lanes(slots, slot < length_ref[0])
        stack.wait(0, 1, 2, 3)

    def weights(kind):
        start = pl.multiple_of(kind * features + step * HEAD_BLOCK, HEAD_BLOCK)
        return w_ref[pl.ds(start, HEAD_BLOCK)]

    q_ref[...] = dot_nt(normed_ref[...], weights(0)).astype(BF16)
    k_ref[...] = dot_nt(memory_ref[...], weights(1)).astype(BF16)
    v_ref[...] = dot_nt(memory_ref[...], weights(2)).astype(BF16)

    units = [
        (pair, which, span)
        for pair in range(BLOCK_HEADS // 2)
        for span in spans(doc, Q_BLOCK)
        for which in range(2)
    ]
    ones = jnp.ones((TILE_ROWS, slots), BF16)
    keys = spans(slots, K_BLOCK)

    def lanes_of(pair):
        return slice(pair * LANES, (pair + 1) * LANES)

    def key_side(pair, which):
        return pick(which, k_ref[:, lanes_of(pair)], extra_ref[...])

    def write(pair, which, span, top, total, mixed):
        h = 2 * pair + which
        lse_ref[0, h : h + 1, span] = top + jnp.log(total)
        mix_ref[half_rows(which)] = mixed / total
        if which == 1:
            mixed_ref[span, lanes_of(pair)] = mix_ref[...].T.astype(BF16)

    v_t = [flip(v_ref[:, lanes_of(p)]) for p in range(BLOCK_HEADS // 2)]
    q_t = [q_ref[:, lanes_of(p)].astype(F32).T * SCALE for p in range(BLOCK_HEADS // 2)]

    def begin(unit):
        pair, which, span = unit
        k_of = key_side(pair, which)
        s = dot_nn(k_of[keys[0]], with_extra(which, q_t[pair][:, span], True, None))
        top = jnp.max(s, axis=0, keepdims=True)
        return k_of, s, top, with_extra(which, q_t[pair][:, span], True, top)

    worst = jnp.zeros((1, Q_BLOCK), F32)
    ahead = begin(units[0])
    for i, (pair, which, span) in enumerate(units):
        (k_of, s, top, q_with), slot = ahead, i % 2
        p_ref[slot, keys[0]] = jnp.exp(s - top).astype(BF16)
        for rows in keys[1:]:
            p_ref[slot, rows] = jnp.exp(dot_nn(k_of[rows], q_with)).astype(BF16)
        if i + 1 < len(units):
            ahead = begin(units[i + 1])
        value_side = jnp.concatenate([v_t[pair][half_rows(which)], ones], axis=0)
        mixed = dot_nn(value_side, p_ref[slot])
        total = mixed[HEAD_DIM : HEAD_DIM + 1]
        worst = jnp.maximum(worst, total)
        write(pair, which, span, top, total, mixed[:HEAD_DIM])

    @pl.when(jnp.max(worst) > LARGEST_SUM)
    def _():
        for pair, which, span in units:
            q_with = with_extra(
                which, q_ref[:, lanes_of(pair)].astype(F32).T[:, span] * SCALE, True, None
            )
            k_of = key_side(pair, which)
            s = [dot_nn(k_of[rows], q_with) for rows in keys]
            top = functools.reduce(jnp.maximum, [jnp.max(c, axis=0, keepdims=True) for c in s])
            total = jnp.zeros_like(top)
            for rows, chunk in zip(keys, s):
                p = jnp.exp(chunk - top)
                total = total + jnp.sum(p, axis=0, keepdims=True)
                p_ref[0, rows] = p.astype(BF16)
            mixed = dot_nn(flip(v_ref[:, lanes_of(pair)])[half_rows(which)], p_ref[0])
            write(pair, which, span, top, total, mixed)

    out_ref[...] += dot_nn(mixed_ref[...], weights(3))


def cross_backward_kernel(heads, shares, size, scattered, hops_wanted, length_ref, *refs):
    gain_ref, branch_ref, q_ref, mixed_ref, lse_ref = refs[:5]
    rows_in, memory_in, add_in, k_in, v_in = refs[5:10]
    sources = refs[10 : 10 + shares]
    count = shares // 2
    refs = refs[10 + shares :]
    scatter_in, refs = refs[:scattered], refs[scattered:]
    hidden_in, refs = refs[:hops_wanted], refs[hops_wanted:]
    hidden_out, refs = refs[:hops_wanted], refs[hops_wanted:]
    if scattered:
        scatter_out, refs = refs[0], refs[1:]
        (part_ref, ring_slots, done_ref, scatter_came), refs = refs[-8:-4], refs[:-8] + refs[-4:]
        (ring_send, ring_came, part_sems, done_sems), refs = refs[-4:], refs[:-4]
        scatter = Scatter(size, part_ref, ring_slots, done_ref, ring_send, ring_came)
        part_loads = [
            pltpu.make_async_copy(source, part_ref.at[i], part_sems.at[i])
            for i, source in enumerate(scatter_in)
        ]
        for copy in part_loads:
            copy.start()
    sums, refs = refs[:count], refs[count:]
    memory_out, out_ref, low_ref, gain_grad_ref = refs[:4]
    rows_ref, memory_ref, add_ref, k_ref, v_ref = refs[4:9]
    (
        w_ref,
        normed_ref,
        extra_ref,
        g_ref,
        grad_q_ref,
        grad_ref,
        ds_ref,
        give_ref,
        keep_ref,
        came_ref,
        memory_grad_ref,
        back_ref,
        sems,
        load_sems,
        key_sems,
        out_sems,
        swap_sems,
        hop_sems,
    ) = refs[9:]
    (doc, features), slots = rows_ref.shape, memory_ref.shape[0]
    half, blocks = features // 2, features // HEAD_BLOCK
    stack = Stack(sources, w_ref, sems, 4, heads * HEAD_DIM)
    loads = [
        pltpu.make_async_copy(source, target, load_sems.at[i])
        for i, (source, target) in enumerate(
            ((memory_in, memory_ref), (rows_in, rows_ref), (add_in, add_ref))
        )
    ]

    def key_copies(b):
        lanes = pl.ds(pl.multiple_of(b * HEAD_BLOCK, HEAD_BLOCK), HEAD_BLOCK)
        return [
            pltpu.make_async_copy(source.at[:, lanes], target.at[b], key_sems.at[i, b])
            for i, (source, target) in enumerate(((k_in, k_ref), (v_in, v_ref)))
        ]

    stack.start()
    for b in range(blocks):
        for copy in key_copies(b):
            copy.start()
    for copy in loads:
        copy.start()
    greet([1, 2][:count], [way[1] for way in ring_ways(size)] if scattered else [])
    hops = [
        to_differing(2, source, target, hop_sems.at[i])
        for i, (source, target) in enumerate(zip(hidden_in, hidden_out))
    ]
    for hop in hops:
        hop.start()
    if scattered:
        for copy in part_loads:
            copy.wait()
        scatter.begin()
    slot = lax.broadcasted_iota(jnp.int32, (slots, LANES), 0)
    extra_ref[...] = extra_lanes(slots, slot < length_ref[0])
    none = jnp.zeros((doc, LANES), BF16)
    stack.wait(3)

    def one_block(step, carry):
        start = pl.multiple_of(3 * features + step * HEAD_BLOCK, HEAD_BLOCK)
        g_ref[...] = dot_nt(branch_ref[...], w_ref[pl.ds(start, HEAD_BLOCK)]).astype(BF16)
        for copy in key_copies(step):
            copy.wait()
        for pair in range(BLOCK_HEADS // 2):
            local = slice(pair * LANES, (pair + 1) * LANES)
            lanes = lane_block(step * HEAD_BLOCK + pair * LANES)
            v_lanes = lane_block(features + step * HEAD_BLOCK + pair * LANES)
            q, g = q_ref[:, lanes], g_ref[:, local]
            q_t, g_t = q.astype(F32).T * SCALE, g.astype(F32).T
            inner = g_t * mixed_ref[:, lanes].astype(F32).T
            per_head = []
            for which in range(2):
                h = 2 * pair + which
                minus = jnp.sum(inner[half_rows(which)], axis=0, keepdims=True)
                per_head.append(
                    (
                        with_extra(which, q_t, True, lse_ref[step, h : h + 1, :]),
                        with_extra(which, g_t, False, minus),
                        pick(which, q, none),
                        pick(which, g, none),
                    )
                )
            for rows in spans(slots, K_BLOCK):
                k, v, extra = k_ref[step, rows, local], v_ref[step, rows, local], extra_ref[rows]
                part_k = part_v = None
                for which, (q_with, g_with, q_of, g_of) in enumerate(per_head):
                    p = jnp.exp(dot_nn(pick(which, k, extra), q_with))
                    ds = (p * dot_nn(pick(which, v, extra), g_with)).astype(BF16)
                    ds_ref[which, rows] = ds
                    to_v = dot_nn(p.astype(BF16), g_of)
                    to_k = dot_nn(ds, q_of)
                    part_v = to_v if part_v is None else part_v + to_v
                    part_k = to_k if part_k is None else part_k + to_k
                grad_ref[rows, lanes] = (part_k * SCALE).astype(BF16)
                grad_ref[rows, v_lanes] = part_v.astype(BF16)
            k_t = flip(k_ref[step, :, local])
            grad_q = [dot_nn(k_t[half_rows(which)], ds_ref[which]) for which in range(2)]
            grad_q_ref[:, lanes] = (jnp.concatenate(grad_q, axis=0) * SCALE).T.astype(BF16)
            if scattered:
                scatter_step(1 + step * (BLOCK_HEADS // 2) + pair)
        return carry

    places = blocks * (BLOCK_HEADS // 2)

    def scatter_step(step):
        if size - 2 >= places:
            scatter.advance(step)
        elif size > 2:

            @pl.when(step <= size - 2)
            def _():
                scatter.advance(step)

    lax.fori_loop(0, blocks, one_block, 0)
    if scattered:

        def rest(step, carry):
            scatter.advance(step)
            return carry

        lax.fori_loop(min(places, size - 2) + 1, size - 1, rest, 0)
        scatter.turn()
        done_hops = [
            to_differing(2, done_ref.at[:, i], scatter_came, done_sems)
            for i in range(1, scattered)
        ]
        for hop in done_hops:
            hop.start()

    for copy in loads:
        copy.wait()
    norm_into(normed_ref, rows_ref, gain_ref)

    def weight_grads(ref, first):
        columns = slice(first, first + half)
        v_columns = slice(features + first, features + first + half)
        ref[0] = dot_tn(grad_q_ref[:, columns], normed_ref[...]).astype(BF16)
        ref[1] = dot_tn(grad_ref[:, columns], memory_ref[...]).astype(BF16)
        ref[2] = dot_tn(grad_ref[:, v_columns], memory_ref[...]).astype(BF16)
        ref[3] = dot_tn(mixed_ref[:, columns], branch_ref[...]).astype(BF16)

    weight_grads(give_ref, 0)
    swap = to_differing(1, give_ref, came_ref, swap_sems)
    swap.start()
    stack.wait(0, 1, 2)
    writes = []
    for i, rows in enumerate(spans(slots, MEMORY_BLOCK)):
        memory_grad_ref[rows] = dot_nn(
            grad_ref[rows], w_ref[features : 3 * features]
        ).astype(BF16)
        writes.append(
            pltpu.make_async_copy(memory_grad_ref.at[rows], memory_out.at[rows], out_sems.at[i])
        )
        writes[-1].start()
    weight_grads(keep_ref, half)
    gain_grad_ref[...] = jnp.zeros_like(gain_grad_ref)
    back_ref[...] = dot_nn(grad_q_ref[...], w_ref[:features])
    for span in spans(doc, ROW_BLOCK):
        norm_back_into(
            span, back_ref[span], out_ref, low_ref, gain_grad_ref, rows_ref, gain_ref, add_ref
        )
    swap.wait_recv()
    rows = half // count
    for share, sums_ref in enumerate(sums):
        for kind in range(4):
            span = slice(share * rows, (share + 1) * rows)
            to = slice(kind * rows, (kind + 1) * rows)
            sums_ref[to] = low_sum(keep_ref[kind, span], came_ref[kind, span])
    swap.wait_send()
    for copy in writes:
        copy.wait()
    for hop in hops:
        hop.wait()
    if scattered:
        for hop in done_hops:
            hop.wait()
        own = done_ref[:, 0]
        scatter_out[...] = low_sum(own, scatter_came[...]) if done_hops else own
        scatter.wait_sent()


def feed_forward_kernel(first, last, rows_ref, gain_ref, cotangent_ref, *refs):
    sources, refs = refs[:2], refs[2:]
    if not first:
        before_in, refs = refs[:2], refs[2:]
    sums, layer_ref, out_ref = refs[:2], refs[2], refs[3]
    if last:
        low_ref, gain_grad_ref = refs[4:6]
        refs = refs[2:]
    (
        wide_ref,
        narrow_ref,
        normed_ref,
        normed_t,
        cotangent_t,
        active_ref,
        grad_ref,
        give_ref,
        keep_ref,
        came_ref,
        layer_in_ref,
        back_in_ref,
        product_ref,
        sems,
        before_sems,
        swap_sems,
    ) = refs[4:]
    step, steps = pl.program_id(0), pl.num_programs(0)
    half = steps // 2
    doc = rows_ref.shape[0]
    hidden = sources[0].shape[0] // 2
    copies = [
        [
            pltpu.make_async_copy(
                source.at[pl.ds(kind * hidden, hidden)],
                stack.at[pl.ds(p * hidden, hidden)],
                sems.at[p, kind],
            )
            for kind, stack in enumerate((wide_ref, narrow_ref))
        ]
        for p, source in enumerate(sources)
    ]
    loads = []
    if not first:
        loads = [
            pltpu.make_async_copy(source, target, before_sems.at[i])
            for i, (source, target) in enumerate(zip(before_in, (layer_in_ref, back_in_ref)))
        ]
    swap = to_differing(1, give_ref, came_ref, swap_sems)

    @pl.when(step == 0)
    def _():
        for pair in copies:
            for copy in pair:
                copy.start()
        for copy in loads:
            copy.start()
        greet([1])
        norm_into(normed_ref, rows_ref, gain_ref)
        for span in spans(doc, ROW_BLOCK):
            normed_t[:, span] = flip(normed_ref[span])
            cotangent_t[:, span] = flip(cotangent_ref[span])

    for p, pair in enumerate(copies):

        @pl.when(step == p * half)
        def _(pair=pair):
            for copy in pair:
                copy.wait()

    units = pl.ds(pl.multiple_of(step * HIDDEN_BLOCK, HIDDEN_BLOCK), HIDDEN_BLOCK)
    activated, slope = gelu_and_slope(dot_nn(wide_ref[units], normed_t[...]))
    active_ref[units] = activated.astype(BF16)
    grad_ref[units] = (dot_nn(narrow_ref[units], cotangent_t[...]) * slope).astype(BF16)

    def store(ref, at):
        rows = pl.ds(pl.multiple_of(at * HIDDEN_BLOCK, HIDDEN_BLOCK), HIDDEN_BLOCK)
        ref[0, rows] = dot_nn(grad_ref[units], normed_ref[...]).astype(BF16)
        ref[1, rows] = dot_nn(active_ref[units], cotangent_ref[...]).astype(BF16)

    @pl.when(step < half)
    def _():
        store(give_ref, step)

    @pl.when(step == half - 1)
    def _():
        swap.start()

    @pl.when(step >= half)
    def _():
        store(keep_ref, step - half)

    @pl.when(step == steps - 1)
    def _():
        for copy in loads:
            copy.wait()
        if last:
            gain_grad_ref[...] = jnp.zeros_like(gain_grad_ref)
        product_ref[...] = dot_tn(active_ref[...], narrow_ref[...])
        for span in spans(doc, ROW_BLOCK):
            layer = rows_ref[span] if first else layer_in_ref[span]
            layer_ref[span] = (layer + product_ref[span]).astype(layer_ref.dtype)
        product_ref[...] = dot_tn(grad_ref[...], wide_ref[...])
        for span in spans(doc, ROW_BLOCK):
            back = product_ref[span]
            if not first:
                back = back + back_in_ref[span]
            if last:
                norm_back_into(
                    span, back, out_ref, low_ref, gain_grad_ref, rows_ref, gain_ref, cotangent_ref
                )
            else:
                out_ref[span] = back
        swap.wait_recv()
        for kind, sums_ref in enumerate(sums):
            for span in spans(hidden, HIDDEN_BLOCK):
                sums_ref[span] = low_sum(keep_ref[kind, span], came_ref[kind, span])
        swap.wait_send()


def pack_kernel(flipped, *refs):
    out_ref, start = refs[-1], 0
    for source, turn in zip(refs[:-1], flipped):
        if source.shape[-1] != out_ref.shape[1] and not turn:
            out_ref[start:] = jnp.zeros((TABLE_ROWS, out_ref.shape[1]), BF16)
            out_ref[start : start + source.shape[0], : source.shape[1]] = source[...]
            continue
        rows = source.shape[1] if turn else source.shape[0]
        span = slice(start, start + rows)
        out_ref[span] = flip(source[...]) if turn else source[...]
        start += rows


def finish_kernel(*refs):
    sources, outs, refs = refs[:4], refs[4:14], refs[14:]
    ins, wides, in_sems, out_sems = refs[:4], refs[4:14], refs[14], refs[15]
    loads, writes = [], []
    for i, (source, target) in enumerate(zip(sources, ins)):
        for j, span in enumerate(spans(target.shape[0], FINISH_BLOCK)):
            loads.append(
                pltpu.make_async_copy(source.at[span], target.at[span], in_sems.at[i, j])
            )
            loads[-1].start()

    def write(i, part):
        writes.append(
            pltpu.make_async_copy(wides[i].at[part], outs[i].at[part], out_sems.at[len(writes)])
        )
        writes[-1].start()

    waiting = iter(loads)
    hidden = wides[1].shape[0]
    for span in spans(hidden, FINISH_BLOCK):
        next(waiting).wait()
        for part in spans(FINISH_BLOCK, LANES):
            rows = slice(span.start + part.start, span.start + part.stop)
            wides[0][:, rows] = ins[0][rows].astype(F32).T
        write(0, (slice(None), span))
    for span in spans(hidden, FINISH_BLOCK):
        next(waiting).wait()
        wides[1][span] = ins[1][span].astype(F32)
        write(1, span)
    for i in (2, 3):
        for _ in spans(ins[i].shape[0], FINISH_BLOCK):
            next(waiting).wait()
        rows = wides[2].shape[0]
        for kind in range(4):
            at = 2 + 4 * (i - 2) + kind
            wides[at][...] = ins[i][kind * rows : (kind + 1) * rows].astype(F32)
            write(at, slice(None))
    for copy in writes:
        copy.wait()


def params():
    return pltpu.CompilerParams(vmem_limit_bytes=VMEM_BYTES)


def cost(flops=1 << 20):
    return pl.CostEstimate(flops=flops, bytes_accessed=1 << 16, transcendentals=0)


def shape(dims, dtype):
    return jax.ShapeDtypeStruct(dims, dtype)


def whole(array):
    return pl.BlockSpec(
        array.shape, lambda *_: (0,) * len(array.shape), pipeline_mode=pl.Buffered(1)
    )


def result(array):
    return pl.BlockSpec(array.shape, lambda *_: (0,) * len(array.shape))


def columns(rows):
    return pl.BlockSpec((rows, HEAD_BLOCK), lambda i: (0, i))


def anywhere(arrays):
    return [pl.BlockSpec(memory_space=pl.ANY) for _ in arrays]


SCALAR = pl.BlockSpec(memory_space=pltpu.SMEM)


def call(
    kernel, name, grid, in_specs, out_specs, out_shape, scratch, args, channel=None, flops=1 << 20
):
    compiler_params = params()
    if channel is not None:
        compiler_params = pltpu.CompilerParams(
            vmem_limit_bytes=VMEM_BYTES, collective_id=channel, has_side_effects=True
        )
    return pl.pallas_call(
        kernel,
        grid=grid,
        in_specs=in_specs,
        out_specs=out_specs,
        out_shape=out_shape,
        scratch_shapes=scratch,
        compiler_params=compiler_params,
        cost_estimate=cost(flops),
        name=name,
    )(*args)


def pack(*parts):
    arrays, flipped = zip(*parts)
    features = arrays[0].shape[0] if flipped[0] else arrays[0].shape[1]
    rows = [a.shape[1] if turn else a.shape[0] for a, turn in parts]
    if arrays[-1].shape[1] < features and not flipped[-1]:
        rows[-1] = TABLE_ROWS
    rows = sum(rows)
    return pl.pallas_call(
        functools.partial(pack_kernel, flipped),
        out_shape=shape((rows, features), BF16),
        compiler_params=params(),
        cost_estimate=cost(),
        name="pack",
    )(*arrays)


def self_forward(heads, buckets, rows, gain, weights, ids):
    doc, features = rows.shape
    shares, steps = len(weights), features // HEAD_BLOCK
    narrow, tall = shape((doc, features), BF16), shape((doc, features), F32)
    scores = shape((steps * BLOCK_HEADS, doc, doc), BF16)
    out_shape = (*[narrow] * 4, shape((steps, 8, doc), F32), scores, tall)
    return call(
        functools.partial(self_forward_kernel, heads, buckets, shares),
        "self_forward",
        (steps,),
        [whole(rows), whole(gain), whole(ids), *anywhere(weights)],
        (
            *[columns(doc)] * 4,
            pl.BlockSpec((1, 8, doc), lambda i: (i, 0, 0)),
            pl.BlockSpec((BLOCK_HEADS, doc, doc), lambda i: (i, 0, 0)),
            result(tall),
        ),
        out_shape,
        [
            pltpu.VMEM((4 * features, features), BF16),
            pltpu.VMEM((shares, TABLE_ROWS, features), BF16),
            pltpu.VMEM((TABLE_ROWS, LANES), F32),
            pltpu.VMEM((doc, features), BF16),
            pltpu.SemaphoreType.DMA((shares, 5)),
        ],
        (rows, gain, ids, *weights),
    )


def self_backward(heads, rows, gain, branch, add, saved, weights, hops):
    doc, features = rows.shape
    shares, steps = len(weights), features // HEAD_BLOCK
    count = shares // 2
    *arrays, lse, bias = saved
    packed = pltpu.VMEM((4, features // 2, features), BF16)
    scores = pl.BlockSpec((BLOCK_HEADS, doc, doc), lambda i: (i, 0, 0))
    out_shape = (
        *[shape(h.shape, BF16) for h in hops],
        *[shape((4 * heads * HEAD_DIM, features), BF16)] * count,
        shape((steps * BLOCK_HEADS, doc, doc), BF16),
        shape((doc, features), F32),
        shape((8, features), F32),
    )
    return call(
        functools.partial(self_backward_kernel, heads, shares),
        "self_backward",
        (steps,),
        [
            *[whole(a) for a in (rows, gain, branch, add, *arrays)],
            pl.BlockSpec((1, 8, doc), lambda i: (i, 0, 0)),
            scores,
            *anywhere(weights),
            *anywhere(hops),
        ],
        (
            *anywhere(hops),
            *[result(o) for o in out_shape[len(hops) : len(hops) + count]],
            scores,
            result(out_shape[-2]),
            result(out_shape[-1]),
        ),
        out_shape,
        [
            pltpu.VMEM((4 * features, features), BF16),
            pltpu.VMEM((doc, features), BF16),
            pltpu.VMEM((doc, HEAD_BLOCK), BF16),
            pltpu.VMEM((doc, 3 * features), BF16),
            pltpu.VMEM((doc, features), F32),
            packed,
            packed,
            packed,
            pltpu.SemaphoreType.DMA((shares, 4)),
            pltpu.SemaphoreType.DMA((2,)),
            pltpu.SemaphoreType.DMA((2,)),
        ],
        (rows, gain, branch, add, *arrays, lse, bias, *weights, *hops),
        channel=4,
    )


def cross_forward(heads, rows, gain, memory, length, weights):
    (doc, features), slots = rows.shape, memory.shape[0]
    shares, steps = len(weights), features // HEAD_BLOCK
    query, key = shape((doc, features), BF16), shape((slots, features), BF16)
    tall = shape((doc, features), F32)
    return call(
        functools.partial(cross_forward_kernel, heads, shares),
        "cross_forward",
        (steps,),
        [SCALAR, whole(rows), whole(gain), whole(memory), *anywhere(weights)],
        (
            columns(doc),
            columns(slots),
            columns(slots),
            columns(doc),
            pl.BlockSpec((1, 8, doc), lambda i: (i, 0, 0)),
            result(tall),
        ),
        (query, key, key, query, shape((steps, 8, doc), F32), tall),
        [
            pltpu.VMEM((4 * features, features), BF16),
            pltpu.VMEM((doc, features), BF16),
            pltpu.VMEM((slots, LANES), BF16),
            pltpu.VMEM((2, slots, Q_BLOCK), BF16),
            pltpu.VMEM((LANES, Q_BLOCK), F32),
            pltpu.SemaphoreType.DMA((shares, 4)),
        ],
        (length, rows, gain, memory, *weights),
    )


def cross_backward(
    heads, size, rows, gain, memory, length, branch, add, saved, weights, scattered, hops
):
    (doc, features), slots = rows.shape, memory.shape[0]
    shares, blocks = len(weights), features // HEAD_BLOCK
    count = shares // 2
    blocks_out, ring_scratch = [], []
    if scattered:
        number, part = len(scattered), scattered[0].shape
        block = (2, part[0] // (2 * size), features)
        blocks_out = [shape(block, BF16)]
        steps = pltpu.SemaphoreType.DMA((2, size - 1))
        ring_scratch = [
            pltpu.VMEM((number, *part), BF16),
            pltpu.VMEM((2, size - 1, number, *block[1:]), BF16),
            pltpu.VMEM((2, number, *block[1:]), BF16),
            pltpu.VMEM(block, BF16),
            steps,
            steps,
            pltpu.SemaphoreType.DMA((number,)),
            pltpu.SemaphoreType.DMA((2,)),
        ]
    out_shape = (
        *[shape(h.shape, BF16) for h in hops],
        *blocks_out,
        *[shape((4 * heads * HEAD_DIM, features), BF16)] * count,
        shape((slots, features), BF16),
        shape((doc, features), F32),
        shape((doc, features), BF16),
        shape((8, features), F32),
    )
    query, key, value, mixed, lse = saved
    near = (gain, branch, query, mixed, lse)
    far = (rows, memory, add, key, value, *weights, *scattered, *hops)
    vmem, hbm = pl.BlockSpec(memory_space=pltpu.VMEM), pl.BlockSpec(memory_space=pl.ANY)
    packed = pltpu.VMEM((4, features // 2, features), BF16)
    key_block = pltpu.VMEM((blocks, slots, HEAD_BLOCK), BF16)
    return call(
        functools.partial(
            cross_backward_kernel, heads, shares, size, len(scattered), len(hops)
        ),
        "cross_backward",
        (),
        [SCALAR, *[vmem for _ in near], *[hbm for _ in far]],
        (
            *[hbm] * len(hops),
            *[vmem] * len(blocks_out),
            *[vmem] * count,
            hbm,
            vmem,
            vmem,
            vmem,
        ),
        out_shape,
        [
            pltpu.VMEM((doc, features), F32),
            pltpu.VMEM((slots, features), BF16),
            pltpu.VMEM((doc, features), F32),
            key_block,
            key_block,
            pltpu.VMEM((4 * features, features), BF16),
            pltpu.VMEM((doc, features), BF16),
            pltpu.VMEM((slots, LANES), BF16),
            pltpu.VMEM((doc, HEAD_BLOCK), BF16),
            pltpu.VMEM((doc, features), BF16),
            pltpu.VMEM((slots, 2 * features), BF16),
            pltpu.VMEM((2, slots, doc), BF16),
            packed,
            packed,
            packed,
            pltpu.VMEM((slots, features), BF16),
            pltpu.VMEM((doc, features), F32),
            pltpu.SemaphoreType.DMA((shares, 4)),
            pltpu.SemaphoreType.DMA((3,)),
            pltpu.SemaphoreType.DMA((2, blocks)),
            pltpu.SemaphoreType.DMA((slots // MEMORY_BLOCK,)),
            pltpu.SemaphoreType.DMA((2,)),
            pltpu.SemaphoreType.DMA((max(len(hops), 1), 2)),
            *ring_scratch,
        ],
        (length, *near, *far),
        channel=1,
    )


def feed_forward(rows, gain, cotangent, weights, before, last):
    (doc, features), shares = rows.shape, len(weights)
    share = weights[0].shape[0] // 2
    hidden = share * shares
    steps = hidden // HIDDEN_BLOCK
    summed, tall = shape((share, features), BF16), shape((doc, features), F32)
    low = shape((doc, features), BF16)
    rest = [low, tall, low, shape((8, features), F32)] if last else [tall, tall]
    kept, added = pltpu.VMEM((2, share, features), BF16), pltpu.VMEM(tall.shape, F32)
    return call(
        functools.partial(feed_forward_kernel, not before, last),
        "feed_forward",
        (steps,),
        [whole(rows), whole(gain), whole(cotangent), *anywhere(weights), *anywhere(before)],
        (result(summed), result(summed), *[result(o) for o in rest]),
        (summed, summed, *rest),
        [
            pltpu.VMEM((hidden, features), BF16),
            pltpu.VMEM((hidden, features), BF16),
            pltpu.VMEM((doc, features), BF16),
            pltpu.VMEM((features, doc), BF16),
            pltpu.VMEM((features, doc), BF16),
            pltpu.VMEM((hidden, doc), BF16),
            pltpu.VMEM((hidden, doc), BF16),
            kept,
            kept,
            kept,
            added,
            added,
            added,
            pltpu.SemaphoreType.DMA((shares, 2)),
            pltpu.SemaphoreType.DMA((2,)),
            pltpu.SemaphoreType.DMA((2,)),
        ],
        (rows, gain, cotangent, *weights, *before),
        channel=3 if before else 2,
    )


def finish(sum_wide, sum_narrow, sum_cross, sum_self):
    rows, features = sum_self.shape
    hidden, part = sum_wide.shape[0], shape((rows // 4, features), F32)
    out_shape = [shape((features, hidden), F32), shape((hidden, features), F32), *[part] * 8]
    sources = (sum_wide, sum_narrow, sum_cross, sum_self)
    writes = 2 * hidden // FINISH_BLOCK + 8
    wide, narrow, *parts = pl.pallas_call(
        finish_kernel,
        in_specs=anywhere(sources),
        out_specs=anywhere(out_shape),
        out_shape=out_shape,
        scratch_shapes=[
            *[pltpu.VMEM(source.shape, BF16) for source in sources],
            *[pltpu.VMEM(out.shape, F32) for out in out_shape],
            pltpu.SemaphoreType.DMA((4, hidden // FINISH_BLOCK)),
            pltpu.SemaphoreType.DMA((writes,)),
        ],
        compiler_params=params(),
        cost_estimate=cost(),
        name="finish",
    )(*sources)
    return wide, narrow, parts[4:], parts[:4]


def share_place(row, other, peers):
    j, bit = 0, 1
    while bit < peers:
        j = j + bit * ((row // bit + other // bit) % 2)
        bit *= 2
    return (j % 2) * (j // 2) + (1 - j % 2) * (peers // 2 + j // 2)


def tail_kernel(size, peers, buckets, heads, gathered, counts, *refs):
    parts = []
    for count in counts:
        parts.append(refs[:count])
        refs = refs[count:]
    arrays, shares = len(counts) + 1, peers // 2
    last_refs, refs = refs[:shares], refs[shares:]
    ids_ref, ds_ref, *gain_refs = refs[:5]
    outs, small_out_ref, refs = refs[5 : 5 + arrays], refs[5 + arrays], refs[6 + arrays :]
    slots, refs = refs[:arrays], refs[arrays:]
    firsts, refs = refs[:arrays], refs[arrays:]
    far_came_ref, part_ref, scores_ref, bucket_ref = refs[:4]
    small_ref, near_ref, far_ref = refs[4:7]
    send, came, send_out, came_out, small_sems, hop_sems, local_sems = refs[7:]
    parts.append((part_ref,))
    me, row = lax.axis_index("dp"), lax.axis_index("mp")
    ways = ring_ways(size)
    doc = ids_ref.shape[0]
    mesh = pl.DeviceIdType.MESH

    load_scores = pltpu.make_async_copy(ds_ref, scores_ref, local_sems.at[0])
    load_scores.start()

    barrier = pltpu.get_barrier_semaphore()

    def greet(t, carry):
        pl.semaphore_signal(
            barrier, inc=1, device_id=((me + t) % size, row), device_id_type=mesh
        )
        return carry

    lax.fori_loop(1, size, greet, 0)
    for t in range(1, peers):
        pl.semaphore_signal(
            barrier, inc=1, device_id=(me, (row + t) % peers), device_id_type=mesh
        )
    pl.semaphore_wait(barrier, size - 1 + peers - 1)

    def block(i, way, number):
        rows = outs[i].shape[0] // (2 * size)
        return pl.ds(pl.multiple_of((way * size + number) * rows, 16), rows)

    def part(i, span):
        total = parts[i][0][span].astype(F32)
        for ref in parts[i][1:]:
            total = total + ref[span].astype(F32)
        return total

    def first_copy(i, way):
        return remote(
            firsts[i].at[way],
            slots[i].at[way, 0],
            send.at[i, way, 0],
            came.at[i, way, 0],
            (ways[way][1], row),
        )

    def next_copy(i, way, step):
        return remote(
            slots[i].at[way, step - 1],
            slots[i].at[way, step],
            send.at[i, way, step],
            came.at[i, way, step],
            (ways[way][1], row),
        )

    def wait_came(i, way, step):
        remote(
            slots[i].at[way, step],
            slots[i].at[way, step],
            send.at[i, way, step],
            came.at[i, way, step],
            (ways[way][1], row),
        ).wait_recv()

    def out_copy(i, way, step):
        span = block(i, way, (ways[way][0] + 1 - step + size) % size)
        return remote(
            outs[i].at[span],
            outs[i].at[span],
            send_out.at[i, way, step],
            came_out.at[i, way, step],
            (ways[way][1], row),
        )

    def begin(rings):
        for i, way in rings:
            firsts[i][way] = part(i, block(i, way, ways[way][0])).astype(BF16)
            first_copy(i, way).start()

    def plus_part(i, way, step):
        span = block(i, way, (ways[way][0] - step - 1 + size) % size)
        total = slots[i][way, step].astype(F32) + part(i, span)
        return span, total.astype(BF16)

    def advance(rings, step):
        for i, way in rings:
            wait_came(i, way, step - 1)
            slots[i][way, step - 1] = plus_part(i, way, step - 1)[1]
            next_copy(i, way, step).start()

    def turn(rings):
        for i, way in rings:
            wait_came(i, way, size - 2)
            span, total = plus_part(i, way, size - 2)
            outs[i][span] = total
            out_copy(i, way, 0).start()

    def pass_on(rings, step):
        for i, way in rings:
            out_copy(i, way, step - 1).wait_recv()
            out_copy(i, way, step).start()

    ready = [(i, way) for i in range(gathered) for way in range(2)]
    early = [(i, way) for i in range(gathered, arrays - 1) for way in range(2)]
    late = [(arrays - 1, way) for way in range(2)]

    other_chip = None
    if shares == 2:
        other_chip = to_differing(2, last_refs[1], far_came_ref, hop_sems)
        other_chip.start()
    begin(early)
    for i, way in ready:
        outs[i][block(i, way, (ways[way][0] + 1) % size)] = parts[i][0][way]
        out_copy(i, way, 0).start()

    rows_used, per_row = bucket_ref.shape[0], ds_ref.shape[0] // bucket_ref.shape[0]
    per_line = buckets // UNIT_BUCKETS
    units = rows_used * per_line
    per_round = -(-units // max(2 * (size - 2), 1))

    def bucket_unit(u, carry):
        r, first = u // per_line, u % per_line * UNIT_BUCKETS
        sums = [[jnp.zeros((8, LANES), F32)] * UNIT_BUCKETS for _ in range(per_row)]
        for c in range(0, doc, LANES):
            lanes = slice(c, c + LANES)
            for rows in spans(c + LANES, UNIT_ROWS):
                found = ids_ref[rows, lanes] - first
                hits = [found == b for b in range(UNIT_BUCKETS)]
                for h in range(per_row):
                    grads = scores_ref[r * per_row + h, rows, lanes].astype(F32)
                    for b, hit in enumerate(hits):
                        kept = jnp.where(hit, grads, 0.0).reshape(-1, 8, LANES)
                        sums[h][b] = sums[h][b] + jnp.sum(kept, axis=0)
        for h in range(per_row):
            for b in range(UNIT_BUCKETS):
                bucket_ref[r, h, pl.ds(first + b, 1), :] = jnp.sum(
                    sums[h][b], axis=0, keepdims=True
                )
        return carry

    def bucket_round(k):
        low = jnp.minimum(k * per_round, units)
        lax.fori_loop(low, jnp.minimum(low + per_round, units), bucket_unit, 0)

    bucket_ref[...] = jnp.zeros_like(bucket_ref)
    part_ref[...] = jnp.zeros_like(part_ref)
    load_scores.wait()

    def early_step(step, carry):
        advance(early, step)
        pass_on(ready, step)
        bucket_round(step - 1)
        return carry

    begin_late = LATE_STEP if size - 1 > LATE_STEP else size - 1
    lax.fori_loop(1, min(begin_late + 1, size - 1), early_step, 0)
    if begin_late == size - 1:
        turn(early)
    used = slice(0, last_refs[0].shape[0])
    if other_chip is None:
        part_ref[used] = last_refs[0][...]
    else:
        other_chip.wait_recv()
        part_ref[used] = low_sum(last_refs[0][...], far_came_ref[...])
    begin(late)

    def both_step(step, carry):
        early_step(step, carry)
        advance(late, step - begin_late)
        return carry

    def middle_step(step, carry):
        pass_on(early, step)
        advance(late, step + size - 1 - begin_late)
        bucket_round(size - 2 + step - 1)
        return carry

    def end_step(step, carry):
        pass_on(early, step)
        pass_on(late, step - begin_late)
        bucket_round(size - 2 + step - 1)
        return carry

    late_passed = 0
    if begin_late < size - 1:
        lax.fori_loop(begin_late + 1, size - 1, both_step, 0)
        turn(early)
        advance(late, size - 1 - begin_late)
        lax.fori_loop(1, begin_late, middle_step, 0)
        pass_on(early, begin_late)
        turn(late)
        bucket_round(size - 2 + begin_late - 1)
        lax.fori_loop(begin_late + 1, size - 1, end_step, 0)
        late_passed = size - 2 - begin_late
    else:
        lax.fori_loop(1, size - 1, middle_step, 0)
        turn(late)
    if size == 2:
        lax.fori_loop(0, units, bucket_unit, 0)

    features = gain_refs[0].shape[1]
    per_gain = features // LANES
    gain_rows = len(gain_refs) * per_gain
    small_ref[...] = jnp.zeros_like(small_ref)
    for i, ref in enumerate(gain_refs):
        total = jnp.sum(ref[...], axis=0, keepdims=True)
        for c in range(per_gain):
            at = i * per_gain + c
            small_ref[at : at + 1, :] = total[:, c * LANES : (c + 1) * LANES]
    for r in range(rows_used):
        block_sums = bucket_ref[r].reshape(LANES, LANES).T
        at = gain_rows + r
        small_ref[at : at + 1, :] = jnp.sum(block_sums, axis=0, keepdims=True)

    def near_copy(t):
        return remote(
            small_ref,
            near_ref.at[row],
            small_sems.at[0, t],
            small_sems.at[1, t],
            (me, (row + t) % peers),
        )

    def far_copy(t):
        return remote(
            far_ref.at[me],
            far_ref.at[me],
            small_sems.at[2, t],
            small_sems.at[3, t],
            ((me + t) % size, row),
        )

    for t in range(1, peers):
        near_copy(t).start()
    near_ref[pl.ds(row, 1)] = small_ref[...][None]
    for t in range(1, peers):
        near_copy(t).wait_recv()
    own = rows_used // peers
    total, sums = None, None
    for k in range(peers):
        gains = near_ref[k, :gain_rows]
        mine = near_ref[k, pl.ds(gain_rows + own * share_place(row, k, peers), own)]
        total = gains if total is None else total + gains
        sums = mine if sums is None else sums + mine
    small_ref_rows = far_ref.shape[1]
    far_ref[pl.ds(me, 1)] = jnp.concatenate(
        [total, sums, jnp.zeros((small_ref_rows - gain_rows - own, LANES), F32)], axis=0
    )[None]

    def far_start(t, carry):
        far_copy(t).start()
        return carry

    lax.fori_loop(1, size, far_start, 0)

    def late_step(step, carry):
        pass_on(late, step)
        return carry

    lax.fori_loop(1 + late_passed, size - 1, late_step, 0)

    def far_wait(t, carry):
        far_copy(t).wait()
        return carry

    lax.fori_loop(1, size, far_wait, 0)

    def far_add(k, total):
        return total + far_ref[k]

    small_out_ref[...] = lax.fori_loop(1, size, far_add, far_ref[0])
    for i, way in ready + early + late:
        out_copy(i, way, size - 2).wait_recv()

    for t in range(1, peers):
        near_copy(t).wait_send()
    if other_chip is not None:
        other_chip.wait_send()
    for i, way in early + late:
        first_copy(i, way).wait_send()

    def sent(step, carry):
        for i, way in early + late:
            next_copy(i, way, step).wait_send()
        return carry

    lax.fori_loop(1, size - 1, sent, 0)

    def sent_out(step, carry):
        for i, way in ready + early + late:
            out_copy(i, way, step).wait_send()
        return carry

    lax.fori_loop(0, size - 1, sent_out, 0)


def tail_sums(size, peers, buckets, heads, blocks, terms, last, ids, ds, gains):
    assert peers in (2, 4)
    grain = 2 * 16 * size
    features = last[0].shape[1]
    rows = [size * 2 * b.shape[1] for b in blocks]
    rows += [arrays[0].shape[0] for arrays in terms]
    rows.append(last[0].shape[0])
    padded = [r + -r % grain for r in rows]
    parts = [[b] for b in blocks]
    for arrays, r, p in zip(terms, rows[len(blocks) :], padded[len(blocks) :]):
        parts.append([jnp.pad(a, ((0, p - r), (0, 0))) for a in arrays])
    flat = [a for arrays in parts for a in arrays]
    lines = peers * (-(-heads * buckets // LANES))
    small = len(gains) * features // LANES + lines
    small = shape((small + -small % 8, LANES), F32)
    vmem, hbm = pl.BlockSpec(memory_space=pltpu.VMEM), pl.BlockSpec(memory_space=pl.ANY)
    steps = pltpu.SemaphoreType.DMA((len(rows), 2, size - 1))

    def ring_slots(i, steps):
        if i < len(blocks):
            return pltpu.VMEM((2, 1, 16, LANES), BF16)
        return pltpu.VMEM((2, *steps, padded[i] // (2 * size), features), BF16)

    *sums, small = pl.pallas_call(
        functools.partial(
            tail_kernel, size, peers, buckets, heads, len(blocks), [len(a) for a in parts]
        ),
        in_specs=[
            *[vmem] * (len(flat) + 1),
            *[hbm] * (len(last) - 1),
            vmem,
            hbm,
            *[vmem] * len(gains),
        ],
        out_specs=[vmem] * (len(rows) + 1),
        out_shape=[*[shape((p, features), BF16) for p in padded], small],
        scratch_shapes=[
            *[ring_slots(i, (size - 1,)) for i in range(len(rows))],
            *[ring_slots(i, ()) for i in range(len(rows))],
            pltpu.VMEM((rows[-1], features), BF16),
            pltpu.VMEM((padded[-1], features), BF16),
            pltpu.VMEM(ds.shape, BF16),
            pltpu.VMEM((lines, LANES // buckets, buckets, LANES), F32),
            pltpu.VMEM(small.shape, F32),
            pltpu.VMEM((peers, *small.shape), F32),
            pltpu.VMEM((size, *small.shape), F32),
            steps,
            steps,
            steps,
            steps,
            pltpu.SemaphoreType.DMA((4, max(size, peers))),
            pltpu.SemaphoreType.DMA((2,)),
            pltpu.SemaphoreType.DMA((1,)),
        ],
        compiler_params=pltpu.CompilerParams(
            vmem_limit_bytes=VMEM_BYTES, collective_id=0, has_side_effects=True
        ),
        cost_estimate=cost(),
        name="tail_sums",
    )(*flat, *last, ids, ds, *gains)
    return [total[:r] for total, r in zip(sums, rows)], small


def swap(array, bit, size):
    return lax.ppermute(array, "mp", [(i, i ^ bit) for i in range(size)])


def after(array, *others):
    return lax.optimization_barrier((array, others))[0]


def shards(
    decoder_rows,
    memory_rows,
    decoder_token_length,
    memory_length,
    bucket_ids,
    relative_bucket_bias,
    self_gain,
    self_query,
    self_key,
    self_value,
    self_out,
    cross_gain,
    cross_query,
    cross_key,
    cross_value,
    cross_out,
    hidden_gain,
    widen_weight,
    narrow_weight,
    layer_cotangent,
):
    dp_size = lax.axis_size("dp")
    mp_size = lax.axis_size("mp")
    me = lax.axis_index("mp")
    doc, features = decoder_rows.shape
    slots = memory_rows.shape[0]
    cols = self_query.shape[1]
    heads = cols // HEAD_DIM
    buckets = relative_bucket_bias.shape[0]
    order = [*range(1, mp_size, 2), *range(0, mp_size, 2)]

    doc_length = lax.dynamic_index_in_dim(decoder_token_length, me, keepdims=False)
    doc_memory = lax.dynamic_index_in_dim(memory_length, me)
    position = jnp.arange(doc, dtype=jnp.int32)
    allowed = (position[:, None] <= position[None, :]) & (position[:, None] < doc_length)
    ids = jnp.where(allowed, bucket_ids.T, buckets)
    own_self = pack(
        (self_query.T, False),
        (self_key.T, False),
        (self_value.T, False),
        (self_out, False),
        (relative_bucket_bias.T, False),
    )
    own_cross = pack(
        (cross_query.T, False), (cross_key.T, False), (cross_value.T, False), (cross_out, False)
    )
    own_hidden = pack((widen_weight, True), (narrow_weight, False))

    def first_hops(own):
        shares, bit = {0: own}, mp_size // 2
        while bit > 1:
            for j in list(shares):
                shares[j | bit] = swap(shares[j], bit, mp_size)
            bit //= 2
        return shares

    def last_hop(shares, *others):
        if 1 not in shares:
            shares[1] = swap(shares[0], 1, mp_size)
        for j in range(2, mp_size, 2):
            shares[j] = after(shares[j], *others)
            shares[j | 1] = swap(shares[j], 1, mp_size)
        return shares

    near_self = first_hops(own_self)
    near_self[1] = swap(own_self, 1, mp_size)
    memory_rows = after(memory_rows, own_self)
    w_self = last_hop(near_self, own_cross, own_hidden, ids)
    w_self = [w_self[j] for j in order]
    near_cross = first_hops(own_cross)
    near_hidden = first_hops(own_hidden)
    near_hidden[1] = swap(own_hidden, 1, mp_size)
    memory_seen = lax.all_to_all(
        memory_rows.reshape(dp_size, slots // dp_size, features), "dp", 0, 0
    ).reshape(slots, features)

    gain_self = self_gain.astype(F32)[None]
    gain_cross = cross_gain.astype(F32)[None]
    gain_hidden = hidden_gain.astype(F32)[None]

    *saved_self, after_self = self_forward(heads, buckets, decoder_rows, gain_self, w_self, ids)
    w_cross = last_hop(near_cross, after_self)
    w_cross = [w_cross[j] for j in order]
    *saved_cross, after_cross = cross_forward(
        heads, after_self, gain_cross, memory_seen, doc_memory, w_cross
    )

    before, wide_sums, narrow_sums, w_hidden = (), [], [], near_hidden
    for j in range(0, mp_size, 2):
        wide_sum, narrow_sum, *before = feed_forward(
            after_cross,
            gain_hidden,
            layer_cotangent,
            [w_hidden[j + 1], w_hidden[j]],
            before,
            j == mp_size - 2,
        )
        wide_sums.append(wide_sum)
        narrow_sums.append(narrow_sum)
        if j == 0:
            w_hidden = last_hop(near_hidden, before[0])
    layer_output, grad_after_cross, branch, hidden_gain_grad = before

    scattered, hops = wide_sums, narrow_sums[1:]
    if wide_sums[0].shape[0] % (2 * 16 * dp_size):
        scattered, hops = [], wide_sums[1:] + narrow_sums[1:]
    *sums, grad_memory, grad_after_self, branch, cross_gain_grad = cross_backward(
        heads,
        dp_size,
        after_self,
        gain_cross,
        memory_seen,
        doc_memory,
        branch,
        grad_after_cross,
        saved_cross,
        w_cross,
        scattered,
        hops,
    )
    came, sums = sums[: len(hops)], sums[len(hops) :]
    if scattered:
        blocks, terms, cross_sums = sums[:1], [narrow_sums[:1] + came], sums[1:]
    else:
        blocks, cross_sums = [], sums
        hidden = [wide_sums[0], narrow_sums[0]], came
        terms = [[jnp.concatenate(both, axis=0) for both in hidden if both]]
    memory_grad = lax.all_to_all(
        grad_memory.reshape(dp_size, slots // dp_size, features), "dp", 0, 0
    ).reshape(slots, features)

    *sums, score_grads, input_grad, self_gain_grad = self_backward(
        heads,
        decoder_rows,
        gain_self,
        branch,
        grad_after_self,
        saved_self,
        w_self,
        cross_sums[1:],
    )
    cross_sums[1:], last = sums[: len(cross_sums) - 1], sums[len(cross_sums) - 1 :]
    (*hidden, sum_cross, sum_self), small = tail_sums(
        dp_size,
        mp_size,
        buckets,
        heads,
        blocks,
        terms + [cross_sums],
        last,
        ids,
        score_grads,
        (self_gain_grad, cross_gain_grad, hidden_gain_grad),
    )
    wide_grad, narrow_grad, self_grads, cross_grads = finish(
        *(hidden if scattered else jnp.split(hidden[0], 2)), sum_cross, sum_self
    )
    gain_rows = 3 * features // LANES
    gains = small[:gain_rows].reshape(3, features)
    lines = -(-heads * buckets // LANES)
    sums = small[gain_rows : gain_rows + lines, : heads // lines * buckets]
    position_grad = sums.reshape(heads, buckets).T

    return (
        layer_output,
        input_grad,
        memory_grad,
        position_grad,
        gains[0],
        *[grad.T for grad in self_grads[:3]],
        self_grads[3],
        gains[1],
        *[grad.T for grad in cross_grads[:3]],
        cross_grads[3],
        gains[2],
        wide_grad,
        narrow_grad,
    )


def solution(mesh):
    return jax.shard_map(
        shards,
        mesh=mesh,
        in_specs=(
            P(("dp", "mp"), None),
            P(("dp", "mp"), None),
            P("dp"),
            P("dp"),
            P(),
            P(None, "mp"),
            P(),
            P(None, "mp"),
            P(None, "mp"),
            P(None, "mp"),
            P("mp", None),
            P(),
            P(None, "mp"),
            P(None, "mp"),
            P(None, "mp"),
            P("mp", None),
            P(),
            P(None, "mp"),
            P("mp", None),
            P(("dp", "mp"), None),
        ),
        out_specs=(
            P(("dp", "mp"), None),
            P(("dp", "mp"), None),
            P(("dp", "mp"), None),
            P(None, "mp"),
            P(),
            P(None, "mp"),
            P(None, "mp"),
            P(None, "mp"),
            P("mp", None),
            P(),
            P(None, "mp"),
            P(None, "mp"),
            P(None, "mp"),
            P("mp", None),
            P(),
            P(None, "mp"),
            P("mp", None),
        ),
        check_vma=False,
    )
```
